32 devices in a mesh: ctx: 8 (over z, core), tp: 4 (over y, x).
Axes of the slice: x: 2, y: 2, z: 4, core: 2. Of those that a mesh axis runs over, the one named last changes fastest.
Arguments:
- tokens: bfloat16 [8, 1536, 2048], P('ctx', 'tp'), may hold values from -6 to 6
- counts: int32 [8, 6, 2], replicated, may hold values from 32 to 128, as said below
- norm_gain: bfloat16 [2048], replicated, may hold values from 0.25 to 1.75
- w_query: bfloat16 [2048, 2048], P(None, 'tp'), may hold values from -0.1875 to 0.1875
- w_key: bfloat16 [2048, 2048], P(None, 'tp'), may hold values from -0.1875 to 0.1875
- w_value: bfloat16 [2048, 2048], P(None, 'tp'), may hold values from -0.125 to 0.125
- w_output: bfloat16 [2048, 2048], P('tp'), may hold values from -0.1875 to 0.1875
- mlp_gain: bfloat16 [2048], replicated, may hold values from 0.25 to 1.75
- w_gate: bfloat16 [2048, 8192], P(None, 'tp'), may hold values from -0.125 to 0.125
- w_up: bfloat16 [2048, 8192], P(None, 'tp'), may hold values from -0.125 to 0.125
- w_down: bfloat16 [8192, 2048], P('tp'), may hold values from -0.0625 to 0.0625
- cotangent: bfloat16 [8, 1536, 2048], P('ctx', 'tp'), may hold values from -6 to 6
Outputs:
- output: bfloat16 [8, 1536, 2048], P('ctx', 'tp')
- input_grad: bfloat16 [8, 1536, 2048], P('ctx', 'tp')
- grad_norm_gain: float32 [2048], replicated
- grad_query: float32 [2048, 2048], P(None, 'tp')
- grad_key: float32 [2048, 2048], P(None, 'tp')
- grad_value: float32 [2048, 2048], P(None, 'tp')
- grad_output_w: float32 [2048, 2048], P('tp')
- grad_mlp_gain: float32 [2048], replicated
- grad_gate: float32 [2048, 8192], P(None, 'tp')
- grad_up: float32 [2048, 8192], P(None, 'tp')
- grad_down: float32 [8192, 2048], P('tp')
The draws below stay inside these ranges and needn't reach their ends.
Inputs may be any that keep to these rules, and one draw needn't show every extreme that they name: `counts`: each block's valid tokens are its first ones; every draw has a block with 128 valid tokens and one with 32.
All inputs are finite; a program needn't handle non-finite values.
Results may differ from the reference program's by a relative error of at most 0.015.
Values may be sent and summed in bfloat16 or wider, within the bound.
A program may use at most 448 MiB of HBM per device.

```python
import math
import jax
import jax.numpy as jnp
from jax import lax

D = 2048
HEADS = 16
HD = 128
FF = 8192
SEQS = 6
BLOCK = 128
SEQ_LEN = 2048
TOKC = 1536
N_CTX = 8


def draw_counts(key, part):
    key = jax.random.fold_in(key, 11)
    first_key, second_key, third_key = jax.random.split(key, 3)
    entries = N_CTX * SEQS * 2
    lowest = BLOCK // 4
    drawn = jax.random.randint(first_key, (entries,), lowest, BLOCK + 1)
    full_at = jax.random.randint(second_key, (), 0, entries)
    short_at = (full_at + 1 + jax.random.randint(third_key, (), 0, entries - 1)) % entries
    drawn = drawn.at[full_at].set(BLOCK).at[short_at].set(lowest)
    return drawn.reshape(N_CTX, SEQS, 2).astype(jnp.int32)


def block_scale(key, dims, pieces, low, top_value):
    loudness = 1.0
    for axis_at, blocks in pieces:
        steps = jax.random.uniform(jax.random.fold_in(jax.random.fold_in(key, 6), axis_at), (blocks,), jnp.float32, low / len(pieces), top_value / len(pieces))
        loudness = loudness * jnp.repeat(jnp.exp(steps), dims[axis_at] // blocks).reshape((-1,) + (1,) * (len(dims) - 1 - axis_at))
    return loudness


def bell_draw(rng, shape, spread, reach, shards=(), held_as=jnp.bfloat16):
    loudness = block_scale(rng, shape, shards, -0.22, 0.18) if shards else 1.0
    values = jax.random.normal(rng, shape, jnp.float32) * spread * loudness
    return jnp.minimum(jnp.maximum(values, -reach), reach).astype(held_as)


def setup_inputs(seed: int = 0) -> dict:
    splits = jax.random.split(jax.random.key(seed), 13)
    tokens = bell_draw(splits[0], (N_CTX, TOKC, D), 1.0, 6.0, ((0, 8), (1, 4)))
    counts = draw_counts(jax.random.fold_in(splits[12], 71), 0)
    norm_gain = jnp.clip(1.0 + 0.15 * jax.random.normal(splits[2], (D,), jnp.float32), 0.25, 1.75).astype(jnp.bfloat16)
    w_query = bell_draw(splits[3], (D, D), (D // 2) ** -0.5, 0.1875, ((1, 4),))
    w_key = bell_draw(splits[4], (D, D), (D // 2) ** -0.5, 0.1875, ((1, 4),))
    w_value = bell_draw(splits[5], (D, D), D ** -0.5, 0.125, ((1, 4),))
    w_output = bell_draw(splits[6], (D, D), (D // 2) ** -0.5, 0.1875, ((0, 4),))
    mlp_gain = jnp.clip(1.0 + 0.15 * jax.random.normal(splits[7], (D,), jnp.float32), 0.25, 1.75).astype(jnp.bfloat16)
    w_gate = bell_draw(splits[8], (D, FF), D ** -0.5, 0.125, ((1, 4),))
    w_up = bell_draw(splits[9], (D, FF), D ** -0.5, 0.125, ((1, 4),))
    w_down = bell_draw(splits[10], (FF, D), FF ** -0.5, 0.0625, ((0, 4),))
    cotangent = bell_draw(splits[11], (N_CTX, TOKC, D), 1.0, 6.0, ((0, 8), (1, 4)))
    return {"tokens": tokens, "counts": counts, "norm_gain": norm_gain, "w_query": w_query, "w_key": w_key, "w_value": w_value, "w_output": w_output, "mlp_gain": mlp_gain, "w_gate": w_gate, "w_up": w_up, "w_down": w_down, "cotangent": cotangent}


EPS = 1e-05
THETA = 10000.0
HIGHEST = lax.Precision.HIGHEST

@jax.custom_vjp
def low(v):
    return lax.optimization_barrier(v.astype(jnp.bfloat16)).astype(jnp.float32)

@jax.custom_vjp
def low_back(v):
    return v

def low_keep(v):
    return (low(v), None)

def low_pass(kept, grad):
    return (grad,)

def back_keep(v):
    return (v, None)

def back_low(kept, grad):
    return (low(grad),)
low.defvjp(low_keep, low_pass)
low_back.defvjp(back_keep, back_low)

def norm_rows(values, gain_vec):
    return values * lax.rsqrt(lax.optimization_barrier(jnp.mean(values * values, axis=-1, keepdims=True)) + EPS) * gain_vec

def rotate_pairs(values, cos_tab, sin_tab):
    half_dim = values.shape[-1] // 2
    first_half = values[..., :half_dim]
    second_half = values[..., half_dim:]
    return jnp.concatenate([first_half * cos_tab - second_half * sin_tab, second_half * cos_tab + first_half * sin_tab], axis=-1)

def block_positions(devices):
    offsets = jnp.arange(2 * BLOCK, dtype=jnp.int32)
    inner_pos = offsets % BLOCK
    front_pos = devices[:, None] * BLOCK + inner_pos[None, :]
    back_pos = (2 * N_CTX - 1 - devices[:, None]) * BLOCK + inner_pos[None, :]
    return jnp.where((offsets // BLOCK)[None, :] == 0, front_pos, back_pos)

def to_sequences(flat):
    rest_shape = flat.shape[1:]
    blocks = flat.reshape((N_CTX, SEQS, 2, BLOCK) + rest_shape)
    front_part = jnp.swapaxes(blocks[:, :, 0], 0, 1)
    back_part = jnp.swapaxes(blocks[::-1, :, 1], 0, 1)
    return jnp.concatenate([front_part, back_part], axis=1).reshape((SEQS, SEQ_LEN) + rest_shape)

def from_sequences(whole):
    rest_shape = whole.shape[2:]
    blocks = whole.reshape((SEQS, 2 * N_CTX, BLOCK) + rest_shape)
    front_part = jnp.swapaxes(blocks[:, :N_CTX], 0, 1)
    back_part = jnp.swapaxes(blocks[:, N_CTX:][:, ::-1], 0, 1)
    return jnp.stack([front_part, back_part], axis=2).reshape((N_CTX * SEQS * 2 * BLOCK,) + rest_shape)

def sequence_attention(parts):
    queries, keys, values = parts
    row_block = min(512, SEQ_LEN)
    block_count = SEQ_LEN // row_block
    key_pos = jnp.arange(SEQ_LEN, dtype=jnp.int32)

    def score_block(inputs):
        query_rows, first_row = inputs
        scores = jnp.einsum('qhd,khd->hqk', query_rows, keys, precision=HIGHEST) * HD ** (-0.5) - math.log(SEQ_LEN)
        scores = low_back(scores)
        query_pos = first_row + jnp.arange(row_block, dtype=jnp.int32)
        causal = (query_pos[:, None] >= key_pos[None, :]).astype(jnp.float32)
        attn_prob = low(jax.nn.sigmoid(scores) * causal)
        return jnp.einsum('hqk,khd->qhd', attn_prob, values, precision=HIGHEST)
    starts = jnp.arange(block_count, dtype=jnp.int32) * row_block
    mixed_sum = lax.map(jax.checkpoint(score_block), (queries.reshape(block_count, row_block, HEADS, HD), starts))
    return mixed_sum.reshape(SEQ_LEN, HEADS, HD)

def reference(tokens, counts, norm_gain, w_query, w_key, w_value, w_output, mlp_gain, w_gate, w_up, w_down, cotangent):
    devices = jnp.arange(N_CTX, dtype=jnp.int32)
    positions = jnp.broadcast_to(block_positions(devices)[:, None, :], (N_CTX, SEQS, 2 * BLOCK)).reshape(-1)
    validity = (jnp.arange(BLOCK, dtype=jnp.int32)[None, None, None, :] < counts[:, :, :, None]).astype(jnp.float32).reshape(-1)
    inverse = THETA ** (-(jnp.arange(HD // 2, dtype=jnp.float32) * (2.0 / HD)))
    angles = positions.astype(jnp.float32)[:, None] * inverse[None, :]
    cos_tab = jnp.cos(angles)[:, None, :]
    sin_tab = jnp.sin(angles)[:, None, :]

    def block_forward(x_rows, gain_one, wq_full, wk_full, wv_full, wo_full, gain_two, wg_full, wu_full, wd_full):
        normed = low(norm_rows(x_rows, gain_one))
        queries = low_back(jnp.dot(normed, wq_full, precision=HIGHEST)).reshape(-1, HEADS, HD)
        keys_pre = low_back(jnp.dot(normed, wk_full, precision=HIGHEST)).reshape(-1, HEADS, HD)
        values_pre = low_back(jnp.dot(normed, wv_full, precision=HIGHEST))
        query_rot = low(rotate_pairs(queries, cos_tab, sin_tab))
        key_rot = low(rotate_pairs(keys_pre, cos_tab, sin_tab))
        value_kept = low(values_pre * validity[:, None]).reshape(-1, HEADS, HD)
        attended = lax.map(sequence_attention, (to_sequences(query_rot), to_sequences(key_rot), to_sequences(value_kept)))
        mixed_rows = from_sequences(attended).reshape(-1, D)
        heads_out = low_back(low(mixed_rows * validity[:, None]))
        residual = x_rows + low_back(jnp.dot(heads_out, wo_full, precision=HIGHEST))
        normed_two = low(norm_rows(residual, gain_two))
        gate_pre = low_back(jnp.dot(normed_two, wg_full, precision=HIGHEST))
        up_pre = low_back(jnp.dot(normed_two, wu_full, precision=HIGHEST))
        hidden = low(jax.nn.silu(gate_pre) * up_pre)
        return residual + low_back(jnp.dot(hidden, wd_full, precision=HIGHEST))
    x_rows = tokens.reshape(-1, D).astype(jnp.float32)
    params = [arr.astype(jnp.float32) for arr in (norm_gain, w_query, w_key, w_value, w_output, mlp_gain, w_gate, w_up, w_down)]
    result, pullback = jax.vjp(block_forward, x_rows, *params)
    grads = pullback(cotangent.reshape(-1, D).astype(jnp.float32))
    output = result.astype(jnp.bfloat16).reshape(N_CTX, SEQS * 2 * BLOCK, D)
    input_grad = grads[0].astype(jnp.bfloat16).reshape(N_CTX, SEQS * 2 * BLOCK, D)
    return (output, input_grad, grads[1], grads[2], grads[3], grads[4], grads[5], grads[6], grads[7], grads[8], grads[9])
```

```python
import functools
import math

import jax
import jax.numpy as jnp
from jax import lax
from jax.experimental import pallas as pl
from jax.experimental.pallas import tpu as pltpu
from jax.sharding import PartitionSpec as P

HD = 128
BLOCK = 128
PAIR = 2 * BLOCK
EPS = 1e-05
THETA = 10000.0
LOG2E = 1.4426950408889634
BF = jnp.bfloat16
F32 = jnp.float32
VMEM_LIMIT = 58 * 1024 * 1024

X_SWAP = [(i, i ^ 1) for i in range(4)]
Y_SWAP = [(i, i ^ 2) for i in range(4)]


def dot(left, right):
    return jnp.dot(left, right, preferred_element_type=F32)


def contract_rows(left, right):
    return lax.dot_general(left, right, (((0,), (0,)), ((), ())), preferred_element_type=F32)


def times_transposed(left, right):
    return lax.dot_general(left, right, (((1,), (1,)), ((), ())), preferred_element_type=F32)


def send_x(values):
    return lax.ppermute(values, "tp", X_SWAP)


def send_y(values):
    return lax.ppermute(values, "tp", Y_SWAP)


def gather_rows(own):
    if lax.axis_size("tp") != 4:
        return lax.all_gather(own, "tp", axis=0, tiled=True)
    half = own.shape[0] // 2
    from_x = send_x(own)
    from_y = send_y(own)
    diag_low = send_x(from_y[:half])
    diag_high = send_y(from_x[half:])
    return jnp.concatenate([own, from_x, from_y, diag_low, diag_high])


def scatter_rows(partial):
    if lax.axis_size("tp") != 4:
        return lax.psum_scatter(partial, "tp", scatter_dimension=0, tiled=True).astype(F32)
    rows = partial.shape[0] // 4
    half = rows // 2
    mine = partial[:rows]
    from_x = send_x(jnp.concatenate([partial[rows : rows + half], partial[3 * rows : 3 * rows + half]]))
    from_y = send_y(jnp.concatenate([partial[2 * rows + half : 3 * rows], partial[3 * rows + half :]]))
    for_y = partial[2 * rows : 2 * rows + half].astype(F32) + from_x[half:].astype(F32)
    for_x = partial[rows + half : 2 * rows].astype(F32) + from_y[half:].astype(F32)
    low_rest = send_y(for_y.astype(BF))
    high_rest = send_x(for_x.astype(BF))
    low = mine[:half].astype(F32) + from_x[:half].astype(F32) + low_rest.astype(F32)
    high = mine[half:].astype(F32) + from_y[:half].astype(F32) + high_rest.astype(F32)
    return jnp.concatenate([low, high])


def exchange(pieces, n_ctx):
    got = [pieces[0]]
    for k in range(1, n_ctx):
        got.append(lax.ppermute(pieces[k], "ctx", [(i, i ^ k) for i in range(n_ctx)]))
    return jnp.stack(got)


def qkv_kernel(swap_ref, n_ref, wq_ref, wk_ref, wv_ref, cos_ref, sin_ref, valid_ref, out_ref):
    rows = n_ref[...]
    swap = swap_ref[0]
    first = pl.multiple_of(swap * BLOCK, BLOCK)
    second = pl.multiple_of((1 - swap) * BLOCK, BLOCK)
    cos_tab = cos_ref[...]
    sin_tab = sin_ref[...]
    for which, w_ref in enumerate((wq_ref, wk_ref, wv_ref)):
        product = dot(rows, w_ref[...])
        for head in range(product.shape[1] // HD):
            part = product[:, head * HD : (head + 1) * HD]
            if which < 2:
                part = part * cos_tab + pltpu.roll(part, HD // 2, 1) * sin_tab
            else:
                part = part * valid_ref[...]
            part = part.astype(BF)
            out_ref[head, which, pl.ds(first, BLOCK), :] = part[:BLOCK]
            out_ref[head, which, pl.ds(second, BLOCK), :] = part[BLOCK:]


def project_qkv(swap, normed, wq, wk, wv, cos_tab, sin_tab, valid):
    rows, depth = normed.shape
    width = wq.shape[1]
    heads = width // HD
    steps = rows // PAIR
    row_block = pl.BlockSpec((PAIR, HD), lambda i, s: (i, 0))
    weight = pl.BlockSpec((depth, width), lambda i, s: (0, 0))
    return pl.pallas_call(
        qkv_kernel,
        out_shape=jax.ShapeDtypeStruct((steps * heads, 3, PAIR, HD), BF),
        grid_spec=pltpu.PrefetchScalarGridSpec(
            num_scalar_prefetch=1,
            grid=(steps,),
            in_specs=[
                pl.BlockSpec((PAIR, depth), lambda i, s: (i, 0)),
                weight,
                weight,
                weight,
                row_block,
                row_block,
                row_block,
            ],
            out_specs=pl.BlockSpec((heads, 3, PAIR, HD), lambda i, s: (i, 0, 0, 0)),
        ),
        compiler_params=pltpu.CompilerParams(vmem_limit_bytes=VMEM_LIMIT),
        cost_estimate=pl.CostEstimate(
            flops=6 * rows * depth * width, bytes_accessed=rows * depth * 2 + 6 * depth * width, transcendentals=0
        ),
    )(swap, normed, wq, wk, wv, cos_tab, sin_tab, valid)


def ordered_blocks(n_ctx):
    for block in range(2 * n_ctx):
        if block < n_ctx:
            yield block, block, 0
        else:
            yield block, 2 * n_ctx - 1 - block, 1


def attention_kernel(n_ctx, tile, me_ref, x_ref, o_ref, qs, ks, vs):
    me = me_ref[0]
    length = 2 * n_ctx * BLOCK
    for block, source, half in ordered_blocks(n_ctx):
        place = jnp.bitwise_xor(me, source)
        for which, dest in enumerate((qs, ks, vs)):
            dest[block * BLOCK : (block + 1) * BLOCK, :] = x_ref[place, 0, which, half * BLOCK : (half + 1) * BLOCK, :]
    factor = -(HD ** (-0.5)) * LOG2E
    shift = math.log(length) * LOG2E
    count = length // tile
    per_tile = tile // BLOCK
    row_at = lax.broadcasted_iota(jnp.int32, (tile, tile), 0)
    col_at = lax.broadcasted_iota(jnp.int32, (tile, tile), 1)
    order = list(ordered_blocks(n_ctx))
    for i in range(count):
        query = qs[i * tile : (i + 1) * tile, :]

        def part(j, masked):
            at = pl.ds(pl.multiple_of(j * tile, tile), tile)
            raw = times_transposed(query, ks[at, :])
            prob = 1.0 / (1.0 + jnp.exp2(raw * factor + shift))
            if masked:
                prob = jnp.where(row_at >= col_at, prob, 0.0)
            return dot(prob.astype(BF), vs[at, :])

        total = part(i, True)
        if i > 0:
            total = lax.fori_loop(0, i, lambda j, acc: acc + part(j, False), total)
        low = total.astype(BF)
        for b in range(per_tile):
            _, source, half = order[i * per_tile + b]
            place = jnp.bitwise_xor(me, source)
            o_ref[place, 0, half * BLOCK : (half + 1) * BLOCK, :] = low[b * BLOCK : (b + 1) * BLOCK]


def attention_forward(me, qkv, n_ctx):
    pairs = qkv.shape[1]
    length = 2 * n_ctx * BLOCK
    tile = min(512, length)
    flops = pairs * length * length * HD * 2
    return pl.pallas_call(
        functools.partial(attention_kernel, n_ctx, tile),
        out_shape=jax.ShapeDtypeStruct((n_ctx, pairs, PAIR, HD), BF),
        grid_spec=pltpu.PrefetchScalarGridSpec(
            num_scalar_prefetch=1,
            grid=(pairs,),
            in_specs=[pl.BlockSpec((n_ctx, 1, 3, PAIR, HD), lambda i, s: (0, i, 0, 0, 0))],
            out_specs=pl.BlockSpec((n_ctx, 1, PAIR, HD), lambda i, s: (0, i, 0, 0)),
            scratch_shapes=[pltpu.VMEM((length, HD), BF)] * 3,
        ),
        compiler_params=pltpu.CompilerParams(vmem_limit_bytes=VMEM_LIMIT),
        cost_estimate=pl.CostEstimate(
            flops=flops * 3, bytes_accessed=pairs * length * HD * 8, transcendentals=pairs * length * length
        ),
    )(me, qkv)


def attention_back_kernel(n_ctx, tile, me_ref, x_ref, g_ref, cos_ref, sin_ref, out_ref, qs, ks, vs, gs, dqs):
    me = me_ref[0]
    length = 2 * n_ctx * BLOCK
    for block, source, half in ordered_blocks(n_ctx):
        place = jnp.bitwise_xor(me, source)
        at = slice(block * BLOCK, (block + 1) * BLOCK)
        part_at = slice(half * BLOCK, (half + 1) * BLOCK)
        for which, dest in enumerate((qs, ks, vs)):
            dest[at, :] = x_ref[place, 0, which, part_at, :]
        gs[at, :] = g_ref[place, 0, part_at, :]
    scale = HD ** (-0.5)
    factor = -scale * LOG2E
    shift = math.log(length) * LOG2E
    count = length // tile
    per_tile = tile // BLOCK
    key_at = lax.broadcasted_iota(jnp.int32, (tile, tile), 0)
    query_at = lax.broadcasted_iota(jnp.int32, (tile, tile), 1)
    order = list(ordered_blocks(n_ctx))
    dqs[...] = jnp.zeros_like(dqs)

    def unrotate(values, tile_index):
        at = slice(tile_index * tile, (tile_index + 1) * tile)
        return (values * cos_ref[at, :] - pltpu.roll(values, HD // 2, 1) * sin_ref[at, :]).astype(BF)

    def put(which, tile_index, low):
        for b in range(per_tile):
            _, source, half = order[tile_index * per_tile + b]
            place = jnp.bitwise_xor(me, source)
            out_ref[place, 0, which, half * BLOCK : (half + 1) * BLOCK, :] = low[b * BLOCK : (b + 1) * BLOCK]

    for j in range(count):
        keys = ks[j * tile : (j + 1) * tile, :]
        values = vs[j * tile : (j + 1) * tile, :]

        def part(i, masked):
            at = pl.ds(pl.multiple_of(i * tile, tile), tile)
            query = qs[at, :]
            grad = gs[at, :]
            raw = times_transposed(keys, query)
            prob = 1.0 / (1.0 + jnp.exp2(raw * factor + shift))
            if masked:
                prob = jnp.where(query_at >= key_at, prob, 0.0)
            prob_grad = times_transposed(values, grad)
            score_grad = (prob_grad * prob * (1.0 - prob)).astype(BF)
            dqs[at, :] += contract_rows(score_grad, keys)
            return dot(score_grad, query), dot(prob.astype(BF), grad)

        total = part(j, True)
        if j + 1 < count:

            def step(i, acc):
                more = part(i, False)
                return acc[0] + more[0], acc[1] + more[1]

            total = lax.fori_loop(j + 1, count, step, total)
        put(1, j, unrotate(total[0] * scale, j))
        put(2, j, total[1].astype(BF))
    for i in range(count):
        put(0, i, unrotate(dqs[i * tile : (i + 1) * tile, :] * scale, i))


def attention_backward(me, qkv, grads, cos_tab, sin_tab, n_ctx):
    pairs = qkv.shape[1]
    length = 2 * n_ctx * BLOCK
    tile = min(512, length)
    table = pl.BlockSpec((length, HD), lambda i, s: (0, 0))
    return pl.pallas_call(
        functools.partial(attention_back_kernel, n_ctx, tile),
        out_shape=jax.ShapeDtypeStruct((n_ctx, pairs, 3, PAIR, HD), BF),
        grid_spec=pltpu.PrefetchScalarGridSpec(
            num_scalar_prefetch=1,
            grid=(pairs,),
            in_specs=[
                pl.BlockSpec((n_ctx, 1, 3, PAIR, HD), lambda i, s: (0, i, 0, 0, 0)),
                pl.BlockSpec((n_ctx, 1, PAIR, HD), lambda i, s: (0, i, 0, 0)),
                table,
                table,
            ],
            out_specs=pl.BlockSpec((n_ctx, 1, 3, PAIR, HD), lambda i, s: (0, i, 0, 0, 0)),
            scratch_shapes=[pltpu.VMEM((length, HD), BF)] * 4 + [pltpu.VMEM((length, HD), F32)],
        ),
        compiler_params=pltpu.CompilerParams(vmem_limit_bytes=VMEM_LIMIT),
        cost_estimate=pl.CostEstimate(
            flops=pairs * length * length * HD * 2 * 6,
            bytes_accessed=pairs * length * HD * 14,
            transcendentals=pairs * length * length,
        ),
    )(me, qkv, grads, cos_tab, sin_tab)


def mlp_kernel(n_ref, g_ref, wg_ref, wu_ref, wd_ref, h_ref, dgp_ref, dup_ref):
    rows = n_ref[...]
    gate_pre = dot(rows, wg_ref[...])
    up_pre = dot(rows, wu_ref[...])
    hidden_grad = times_transposed(g_ref[...], wd_ref[...])
    gate_sig = 1.0 / (1.0 + jnp.exp2(gate_pre * (-LOG2E)))
    gate_act = gate_pre * gate_sig
    h_ref[...] = (gate_act * up_pre).astype(BF)
    dup_ref[...] = (hidden_grad * gate_act).astype(BF)
    dgp_ref[...] = (hidden_grad * up_pre * (gate_sig * (1.0 + gate_pre * (1.0 - gate_sig)))).astype(BF)


def mlp_core(normed, grads, wg, wu, wd):
    rows, depth = normed.shape
    hidden = wg.shape[1]
    row_tile, tile = 512, 512
    row_block = pl.BlockSpec((row_tile, depth), lambda j, i: (i, 0))
    out_block = pl.BlockSpec((row_tile, tile), lambda j, i: (i, j))
    out = jax.ShapeDtypeStruct((rows, hidden), BF)
    return pl.pallas_call(
        mlp_kernel,
        out_shape=(out, out, out),
        grid=(hidden // tile, rows // row_tile),
        in_specs=[
            row_block,
            row_block,
            pl.BlockSpec((depth, tile), lambda j, i: (0, j)),
            pl.BlockSpec((depth, tile), lambda j, i: (0, j)),
            pl.BlockSpec((tile, depth), lambda j, i: (j, 0)),
        ],
        out_specs=(out_block, out_block, out_block),
        compiler_params=pltpu.CompilerParams(vmem_limit_bytes=VMEM_LIMIT),
        cost_estimate=pl.CostEstimate(
            flops=6 * rows * depth * hidden,
            bytes_accessed=rows * depth * 4 + 6 * depth * hidden + 6 * rows * hidden,
            transcendentals=rows * hidden,
        ),
    )(normed, grads, wg, wu, wd)


def inverse_rms(values):
    return lax.rsqrt(jnp.mean(values * values, axis=-1, keepdims=True) + EPS)


def norm_back(values, gain, grad):
    inv = inverse_rms(values)
    unit = values * inv
    scaled = grad * gain
    back = (scaled - unit * jnp.mean(scaled * unit, axis=-1, keepdims=True)) * inv
    return back, jnp.sum(grad * unit, axis=0)


def core_swap(values, n_ctx):
    return lax.ppermute(values, "ctx", [(i, i ^ 1) for i in range(n_ctx)])


def chain_pairs(n_ctx):
    chips = n_ctx // 2
    mid = chips // 2
    inward = []
    for hop in range(mid - 1):
        pairs = [(hop, hop + 1), (chips - 1 - hop, chips - 2 - hop)]
        inward.append([(2 * a + core, 2 * b + core) for a, b in pairs for core in range(2)])
    across = [(2 * a + core, 2 * b + core) for a, b in ((mid - 1, mid), (mid, mid - 1)) for core in range(2)]
    outward = [[(b, a) for a, b in hop] for hop in reversed(inward)]
    return inward, across, outward


def chain_sum(parts, n_ctx):
    inward, across, outward = chain_pairs(n_ctx)
    stages = [("add", hop) for hop in inward] + [("across", across)] + [("take", hop) for hop in outward]
    chip = lax.axis_index("ctx") // 2
    total = len(parts)
    state = list(parts)
    for slot in range(total + len(stages) - 1):
        moving = []
        for k, (kind, hop) in enumerate(stages):
            at = slot - k
            if 0 <= at < total:
                moving.append((at, k, kind, hop))
        sent = [lax.ppermute(state[at], "ctx", hop) for at, _, _, hop in moving]
        following = slot + 1 if slot + 1 < total else None
        held = lax.optimization_barrier(tuple(sent) + ((state[following],) if following is not None else ()))
        if following is not None:
            state[following] = held[-1]
        for (at, k, kind, hop), got in zip(moving, held):
            if kind == "take":
                edge = len(outward) - (k - len(inward) - 1)
                chips = n_ctx // 2
                receives = (chip == edge - 1) | (chip == chips - edge)
                state[at] = jnp.where(receives, got, state[at])
            else:
                state[at] = (state[at].astype(F32) + got.astype(F32)).astype(BF)
    return state


def body(
    tokens,
    counts,
    norm_gain,
    w_query,
    w_key,
    w_value,
    w_output,
    mlp_gain,
    w_gate,
    w_up,
    w_down,
    cotangent,
):
    n_ctx = lax.axis_size("ctx")
    me = lax.axis_index("ctx")
    rank = lax.axis_index("tp")
    odd = rank & 1
    core = me & 1
    length = 2 * BLOCK * n_ctx
    heads = w_query.shape[1] // HD
    me_ref = jnp.reshape(me, (1,)).astype(jnp.int32)
    gain_one = norm_gain.astype(F32)
    gain_two = mlp_gain.astype(F32)

    inverse = THETA ** (-(jnp.arange(HD // 2, dtype=F32) * (2.0 / HD)))
    angles = jnp.arange(length, dtype=jnp.int32).astype(F32)[:, None] * inverse[None, :]
    cos_half, sin_half = jnp.cos(angles), jnp.sin(angles)
    cos_full = jnp.concatenate([cos_half, cos_half], axis=1)
    sin_full = jnp.concatenate([-sin_half, sin_half], axis=1)

    def own_blocks(table):
        front = lax.dynamic_slice_in_dim(table, me * BLOCK, BLOCK, 0)
        back = lax.dynamic_slice_in_dim(table, (2 * n_ctx - 1 - me) * BLOCK, BLOCK, 0)
        return front, back

    cos_front, cos_back = own_blocks(cos_full)
    sin_front, sin_back = own_blocks(sin_full)
    own_counts = lax.dynamic_index_in_dim(counts, me, 0, keepdims=False)
    offsets = jnp.arange(BLOCK, dtype=jnp.int32)

    def valid_of(sequence, half):
        return (offsets < own_counts[sequence, half]).astype(F32)

    cos_own = jnp.concatenate([cos_front, cos_back])
    sin_own = jnp.concatenate([sin_front, sin_back])
    sequences = counts.shape[1]
    paired = lax.axis_size("tp") == 4 and sequences == 6
    if paired:
        ranks = [rank ^ k for k in range(4)]
        seq_a = [3 * (r >> 1) + 2 * (r & 1) for r in ranks]
        seq_b = [1 + 3 * (r >> 1) for r in ranks]
        valids = {
            "b": jnp.concatenate([valid_of(s, r & 1) for s, r in zip(seq_b, ranks)]),
            "a": jnp.concatenate([valid_of(s, half) for s in seq_a for half in range(2)]),
        }
        flip_back = lambda own: jnp.where(odd == 1, jnp.roll(own, BLOCK, axis=0), own)
        tables = {
            "b": (jnp.tile(flip_back(cos_own), (2, 1)), jnp.tile(flip_back(sin_own), (2, 1))),
            "a": (jnp.tile(cos_own, (4, 1)), jnp.tile(sin_own, (4, 1))),
        }
        swaps = {"b": jnp.reshape(odd, (1,)).astype(jnp.int32), "a": jnp.zeros((1,), jnp.int32)}
        n_pairs = {"b": 2 * heads, "a": 4 * heads}
    else:
        valids = {"a": jnp.concatenate([valid_of(s, half) for s in range(sequences) for half in range(2)])}
        tables = {"a": (jnp.tile(cos_own, (sequences, 1)), jnp.tile(sin_own, (sequences, 1)))}
        swaps = {"a": jnp.zeros((1,), jnp.int32)}
        n_pairs = {"a": sequences * heads}
    names = tuple(n_pairs)

    def own_rows(array):
        if not paired:
            return {"a": array}
        return {
            "b": lax.dynamic_slice_in_dim(array, (1 - odd) * PAIR, BLOCK, 0),
            "a": lax.dynamic_slice_in_dim(array, odd * BLOCK, PAIR, 0),
        }

    def whole_rows(part):
        if not paired:
            return part["a"]
        return jnp.where(odd == 1, jnp.concatenate([part["b"], part["a"]]), jnp.concatenate([part["a"], part["b"]]))

    x_own = {name: rows.astype(F32) for name, rows in own_rows(tokens[0]).items()}
    g_own = own_rows(cotangent[0])

    def to_dest(array, name):
        per = -(-n_pairs[name] // n_ctx)
        short = per * n_ctx - n_pairs[name]
        if short:
            array = jnp.concatenate([array, jnp.zeros((short,) + array.shape[1:], array.dtype)])
        return [lax.dynamic_slice_in_dim(array, (me ^ k) * per, per, 0) for k in range(n_ctx)]

    def from_dest(array, name):
        places = jnp.arange(n_ctx, dtype=jnp.int32) ^ me
        ordered = jnp.take(array, places, axis=0)
        return ordered.reshape((-1,) + array.shape[2:])[: n_pairs[name]]

    def flip(array, name):
        if name != "b":
            return array
        return jnp.where(odd == 1, array[:, ::-1], array)

    def rows_to_pairs(array, name):
        count = n_pairs[name] // heads
        array = flip(array.reshape(count, 2, BLOCK, heads, HD), name)
        return array.reshape(count, PAIR, heads, HD).transpose(0, 2, 1, 3).reshape(-1, PAIR, HD)

    def pairs_to_rows(array, name):
        count = n_pairs[name] // heads
        array = array.reshape(count, heads, PAIR, HD).transpose(0, 2, 1, 3)
        array = flip(array.reshape(count, 2, BLOCK, heads, HD), name)
        return array.reshape(count * PAIR, heads * HD)

    def forward_attention(name, x_rows):
        normed = (x_rows * inverse_rms(x_rows) * gain_one).astype(BF)
        normed_all = gather_rows(normed)
        cos_tab, sin_tab = tables[name]
        valid = jnp.broadcast_to(valids[name][:, None], cos_tab.shape)
        qkv = project_qkv(swaps[name], normed_all, w_query, w_key, w_value, cos_tab, sin_tab, valid)
        got = exchange(to_dest(qkv, name), n_ctx)
        mixed = attention_forward(me_ref, got, n_ctx)
        back = exchange([mixed[k] for k in range(n_ctx)], n_ctx)
        heads_out = pairs_to_rows(from_dest(back, name), name) * valids[name][:, None].astype(BF)
        attn_rows = scatter_rows(dot(heads_out, w_output).astype(BF))
        residual = x_rows + attn_rows
        normed_two = (residual * inverse_rms(residual) * gain_two).astype(BF)
        return normed_all, got, heads_out, residual, gather_rows(normed_two)

    n1, got, heads_out, residual, n2 = ({} for _ in range(5))
    for name in names:
        n1[name], got[name], heads_out[name], residual[name], n2[name] = forward_attention(name, x_own[name])
    cot = {name: gather_rows(g_own[name]) for name in names}

    h, dgp, dup = ({} for _ in range(3))
    for name in names:
        h[name], dgp[name], dup[name] = mlp_core(n2[name], cot[name], w_gate, w_up, w_down)

    def joined(part):
        return jnp.concatenate([part[name] for name in names]) if len(names) > 1 else part[names[0]]

    def halves(left, right):
        left, right = joined(left), joined(right)
        size = left.shape[1] // 2
        mine = lax.dynamic_slice_in_dim(left, core * size, size, 1)
        other = lax.dynamic_slice_in_dim(left, (1 - core) * size, size, 1)
        sent = core_swap(contract_rows(other, right).astype(BF), n_ctx)
        return (contract_rows(mine, right) + sent.astype(F32)).astype(BF)

    sum_down = halves(h, cot)
    sum_gate = halves(n2, dgp)
    sum_up = halves(n2, dup)

    def feed_back(name, dgp, dup, residual, g_rows):
        partial = (times_transposed(dgp, w_gate) + times_transposed(dup, w_up)).astype(BF)
        normed_grad = scatter_rows(partial)
        back, gain_grad = norm_back(residual, gain_two, normed_grad)
        res_grad = g_rows.astype(F32) + back
        return res_grad, gain_grad, gather_rows(res_grad.astype(BF))

    res_grad, gain_two_grad, da = ({} for _ in range(3))
    for name in names:
        res_grad[name], gain_two_grad[name], da[name] = feed_back(
            name, dgp[name], dup[name], residual[name], g_own[name]
        )

    def attention_back(name, da, got):
        heads_grad = times_transposed(da, w_output).astype(BF) * valids[name][:, None].astype(BF)
        there = exchange(to_dest(rows_to_pairs(heads_grad, name), name), n_ctx)
        grads = attention_backward(me_ref, got, there, cos_full, sin_full, n_ctx)
        back = exchange([grads[k] for k in range(n_ctx)], n_ctx)
        back = from_dest(back, name)
        dq, dk, dv = (pairs_to_rows(back[:, which], name) for which in range(3))
        return dq, dk, dv * valids[name][:, None].astype(BF)

    dq, dk, dv = ({} for _ in range(3))
    for name in names:
        dq[name], dk[name], dv[name] = attention_back(name, da[name], got[name])
    sum_out = halves(heads_out, da)
    sum_q = halves(n1, dq)
    sum_k = halves(n1, dk)
    sum_v = halves(n1, dv)

    def input_back(x_rows, res_grad, dq, dk, dv):
        partial = times_transposed(dq, w_query) + times_transposed(dk, w_key) + times_transposed(dv, w_value)
        back, gain_grad = norm_back(x_rows, gain_one, scatter_rows(partial.astype(BF)))
        return (res_grad + back).astype(BF), gain_grad

    input_grad, gain_one_grad = ({} for _ in range(2))
    for name in names:
        input_grad[name], gain_one_grad[name] = input_back(
            x_own[name], res_grad[name], dq[name], dk[name], dv[name]
        )

    def output_rows(h, residual):
        return (residual + scatter_rows(dot(h, w_down).astype(BF))).astype(BF)

    output = {name: output_rows(h[name], residual[name]) for name in names}

    split = lambda array, count: [
        array[k * (array.shape[0] // count) : (k + 1) * (array.shape[0] // count)] for k in range(count)
    ]
    first = chain_sum(split(sum_down, 2) + split(sum_gate, 2) + split(sum_up, 2), n_ctx)
    second = chain_sum([sum_out, sum_q, sum_k, sum_v], n_ctx)

    def join(parts):
        mine = jnp.concatenate(parts) if len(parts) > 1 else parts[0]
        other = core_swap(mine, n_ctx)
        low = jnp.where(core == 0, mine, other).astype(F32)
        high = jnp.where(core == 0, other, mine).astype(F32)
        return jnp.concatenate([low, high])

    gain_sums = lax.psum(jnp.stack([sum(gain_one_grad.values()), sum(gain_two_grad.values())]), ("ctx", "tp"))
    return (
        whole_rows(output)[None],
        whole_rows(input_grad)[None],
        gain_sums[0],
        join(second[1:2]),
        join(second[2:3]),
        join(second[3:4]),
        join(second[0:1]),
        gain_sums[1],
        join(first[2:4]),
        join(first[4:6]),
        join(first[0:2]),
    )


def solution(mesh):
    placed = (
        P("ctx", "tp", None),
        P(),
        P(),
        P(None, "tp"),
        P(None, "tp"),
        P(None, "tp"),
        P("tp", None),
        P(),
        P(None, "tp"),
        P(None, "tp"),
        P("tp", None),
        P("ctx", "tp", None),
    )
    return jax.shard_map(
        body,
        mesh=mesh,
        in_specs=placed,
        out_specs=(
            P("ctx", "tp", None),
            P("ctx", "tp", None),
            P(),
            P(None, "tp"),
            P(None, "tp"),
            P(None, "tp"),
            P("tp", None),
            P(),
            P(None, "tp"),
            P(None, "tp"),
            P("tp", None),
        ),
        check_vma=False,
    )
```

```python
import functools
import math

import jax
import jax.numpy as jnp
from jax import lax
from jax.experimental import pallas as pl
from jax.experimental.pallas import tpu as pltpu
from jax.sharding import PartitionSpec as P

HD = 128
BLOCK = 128
PAIR = 2 * BLOCK
EPS = 1e-05
THETA = 10000.0
LOG2E = 1.4426950408889634
BF = jnp.bfloat16
F32 = jnp.float32
VMEM_LIMIT = 58 * 1024 * 1024

X_SWAP = [(i, i ^ 1) for i in range(4)]
Y_SWAP = [(i, i ^ 2) for i in range(4)]


def dot(left, right):
    return jnp.dot(left, right, preferred_element_type=F32)


def contract_rows(left, right):
    return lax.dot_general(left, right, (((0,), (0,)), ((), ())), preferred_element_type=F32)


def times_transposed(left, right):
    return lax.dot_general(left, right, (((1,), (1,)), ((), ())), preferred_element_type=F32)


def send_x(values):
    return lax.ppermute(values, "tp", X_SWAP)


def send_y(values):
    return lax.ppermute(values, "tp", Y_SWAP)


def by_four():
    return lax.axis_size("tp") == 4


def gather_first(own):
    if not by_four():
        return (lax.all_gather(own, "tp", axis=0, tiled=True),)
    return own, send_x(own), send_y(own)


def gather_second(held):
    if len(held) == 1:
        return held
    own, from_x, from_y = held
    half = own.shape[0] // 2
    return own, from_x, from_y, send_x(from_y[:half]), send_y(from_x[half:])


def gathered(held):
    return jnp.concatenate(held) if len(held) > 1 else held[0]


def scatter_parts(partial):
    if not by_four():
        return (partial,)
    rows = partial.shape[0] // 4
    half = rows // 2
    at = lambda first: partial[first * half : (first + 1) * half]
    return (
        jnp.concatenate([at(2), at(6)]),
        jnp.concatenate([at(5), at(7)]),
        jnp.concatenate([at(0), at(1), at(4), at(3)]),
    )


def scatter_first(parts):
    if len(parts) == 1:
        return (lax.psum_scatter(parts[0], "tp", scatter_dimension=0, tiled=True),)
    return send_x(parts[0]), send_y(parts[1]), parts[2]


def add_low(left, right):
    return (left.astype(F32) + right.astype(F32)).astype(BF)


def scatter_second(held):
    if len(held) == 1:
        return held
    from_x, from_y, stay = held
    half = from_x.shape[0] // 2
    low_rest = send_y(add_low(stay[2 * half : 3 * half], from_x[half:]))
    high_rest = send_x(add_low(stay[3 * half :], from_y[half:]))
    return from_x, from_y, stay, low_rest, high_rest


def scattered(held):
    if len(held) == 1:
        return held[0].astype(F32)
    from_x, from_y, stay, low_rest, high_rest = (part.astype(F32) for part in held)
    half = low_rest.shape[0]
    low = stay[:half] + from_x[:half] + low_rest
    high = stay[half : 2 * half] + from_y[:half] + high_rest
    return jnp.concatenate([low, high])


def exchange(pieces, places, n_ctx):
    got = {}
    for k in places:
        got[k] = pieces[k] if k == 0 else lax.ppermute(pieces[k], "ctx", [(i, i ^ k) for i in range(n_ctx)])
    return got


def params():
    return pltpu.CompilerParams(vmem_limit_bytes=VMEM_LIMIT)


def whole(shape):
    return pl.BlockSpec(shape, lambda *_: (0,) * len(shape))


def put_partial(refs, first, value, rows):
    if len(refs) == 1:
        refs[0][first : first + value.shape[0], :] = value
        return
    to_x, to_y, stay = refs
    half = rows // 2
    homes = {
        0: (stay, 0), 1: (stay, 1), 2: (to_x, 0), 3: (stay, 3), 4: (stay, 2), 5: (to_y, 0), 6: (to_x, 1), 7: (to_y, 1)
    }
    for part in range(value.shape[0] // half):
        ref, place = homes[first // half + part]
        ref[place * half : (place + 1) * half, :] = value[part * half : (part + 1) * half]


def partial_shapes(rows, width, split):
    if not split:
        return [jax.ShapeDtypeStruct((rows, width), BF)]
    return [jax.ShapeDtypeStruct((rows // 4, width), BF)] * 2 + [jax.ShapeDtypeStruct((rows // 2, width), BF)]


def per_device(pairs, n_ctx):
    return -(-pairs // n_ctx)


def halves_at(swap):
    first = pl.multiple_of(swap * BLOCK, BLOCK)
    second = pl.multiple_of((1 - swap) * BLOCK, BLOCK)
    return pl.ds(first, BLOCK), pl.ds(second, BLOCK)


def qkv_kernel(n_ctx, pairs, scalar_ref, n_ref, wq_ref, wk_ref, wv_ref, cos_ref, sin_ref, valid_ref, *rest):
    out_refs, buffer = rest[:n_ctx], rest[n_ctx]
    rows = n_ref[...]
    first, second = halves_at(scalar_ref[1])
    me = scalar_ref[0]
    cos_tab = cos_ref[...]
    sin_tab = sin_ref[...]
    heads = wq_ref.shape[1] // HD
    step = pl.program_id(0)
    per = out_refs[0].shape[0]
    for pair in range(pairs, per * n_ctx):
        buffer[pair] = jnp.zeros(buffer.shape[1:], BF)
    for which, w_ref in enumerate((wq_ref, wk_ref, wv_ref)):
        product = dot(rows, w_ref[...])
        for head in range(heads):
            part = product[:, head * HD : (head + 1) * HD]
            if which < 2:
                part = part * cos_tab + pltpu.roll(part, HD // 2, 1) * sin_tab
            else:
                part = part * valid_ref[...]
            part = part.astype(BF)
            buffer[step * heads + head, which, first, :] = part[:BLOCK]
            buffer[step * heads + head, which, second, :] = part[BLOCK:]

    @pl.when(step == pl.num_programs(0) - 1)
    def _():
        for k in range(n_ctx):
            source = jnp.bitwise_xor(me, k)
            for p in range(per):
                out_refs[k][p] = buffer[source * per + p]


def project_qkv(scalars, normed, wq, wk, wv, cos_tab, sin_tab, valid, n_ctx):
    rows, depth = normed.shape
    width = wq.shape[1]
    heads = width // HD
    steps = rows // PAIR
    per = per_device(steps * heads, n_ctx)
    row_block = pl.BlockSpec((PAIR, HD), lambda i, s: (i, 0))
    weight = whole((depth, width))
    piece = (per, 3, PAIR, HD)
    return pl.pallas_call(
        functools.partial(qkv_kernel, n_ctx, steps * heads),
        out_shape=[jax.ShapeDtypeStruct(piece, BF)] * n_ctx,
        grid_spec=pltpu.PrefetchScalarGridSpec(
            num_scalar_prefetch=1,
            grid=(steps,),
            in_specs=[
                pl.BlockSpec((PAIR, depth), lambda i, s: (i, 0)),
                weight,
                weight,
                weight,
                row_block,
                row_block,
                row_block,
            ],
            out_specs=[whole(piece)] * n_ctx,
            scratch_shapes=[pltpu.VMEM((per * n_ctx, 3, PAIR, HD), BF)],
        ),
        compiler_params=params(),
        cost_estimate=pl.CostEstimate(
            flops=6 * rows * depth * width, bytes_accessed=rows * depth * 2 + 6 * depth * width, transcendentals=0
        ),
    )(scalars, normed, wq, wk, wv, cos_tab, sin_tab, valid)


def out_kernel(n_ctx, pairs, scalar_ref, *refs):
    piece_refs, (w_ref, valid_ref), (heads_ref, *partial_refs), buffer = (
        refs[:n_ctx],
        refs[n_ctx : n_ctx + 2],
        refs[n_ctx + 2 : -1],
        refs[-1],
    )
    me = scalar_ref[0]
    first, second = halves_at(scalar_ref[1])
    per = piece_refs[0].shape[0]
    heads = w_ref.shape[0] // HD
    for k in range(n_ctx):
        source = jnp.bitwise_xor(me, k)
        for p in range(per):
            buffer[source * per + p] = piece_refs[k][p]
    weight = w_ref[...]
    for sequence in range(pairs // heads):
        at = slice(sequence * PAIR, (sequence + 1) * PAIR)
        rows = jnp.concatenate(
            [
                jnp.concatenate(
                    [buffer[sequence * heads + head, first, :], buffer[sequence * heads + head, second, :]], axis=0
                )
                for head in range(heads)
            ],
            axis=1,
        )
        rows = rows * valid_ref[at, :]
        heads_ref[at, :] = rows
        put_partial(partial_refs, sequence * PAIR, dot(rows, weight).astype(BF), pairs // heads * PAIR // 4)


def project_out(scalars, pieces, weight, valid, pairs, n_ctx, split):
    width, depth = weight.shape
    rows = valid.shape[0]
    per = pieces[0].shape[0]
    shapes = [jax.ShapeDtypeStruct((rows, width), BF)] + partial_shapes(rows, depth, split)
    return pl.pallas_call(
        functools.partial(out_kernel, n_ctx, pairs),
        out_shape=shapes,
        grid_spec=pltpu.PrefetchScalarGridSpec(
            num_scalar_prefetch=1,
            grid=(1,),
            in_specs=[whole(piece.shape) for piece in pieces] + [whole(weight.shape), whole(valid.shape)],
            out_specs=[whole(shape.shape) for shape in shapes],
            scratch_shapes=[pltpu.VMEM((per * n_ctx, PAIR, HD), BF)],
        ),
        compiler_params=params(),
        cost_estimate=pl.CostEstimate(
            flops=2 * rows * depth * width, bytes_accessed=rows * depth * 2 + 2 * depth * width, transcendentals=0
        ),
    )(scalars, *pieces, weight, valid)


def heads_back_kernel(n_ctx, scalar_ref, da_ref, w_ref, valid_ref, *rest):
    out_refs, buffer = rest[:n_ctx], rest[n_ctx]
    me = scalar_ref[0]
    first, second = halves_at(scalar_ref[1])
    per = out_refs[0].shape[0]
    heads = w_ref.shape[0] // HD
    weight = w_ref[...]
    for pair in range(da_ref.shape[0] // PAIR * heads, per * n_ctx):
        buffer[pair] = jnp.zeros(buffer.shape[1:], BF)
    for sequence in range(da_ref.shape[0] // PAIR):
        at = slice(sequence * PAIR, (sequence + 1) * PAIR)
        grad = times_transposed(da_ref[at, :], weight).astype(BF) * valid_ref[at, :]
        for head in range(heads):
            part = grad[:, head * HD : (head + 1) * HD]
            buffer[sequence * heads + head, first, :] = part[:BLOCK]
            buffer[sequence * heads + head, second, :] = part[BLOCK:]
    for k in range(n_ctx):
        source = jnp.bitwise_xor(me, k)
        for p in range(per):
            out_refs[k][p] = buffer[source * per + p]


def heads_back(scalars, da, weight, valid, n_ctx):
    rows, depth = da.shape
    width = weight.shape[0]
    per = per_device(rows // PAIR * (width // HD), n_ctx)
    piece = (per, PAIR, HD)
    return pl.pallas_call(
        functools.partial(heads_back_kernel, n_ctx),
        out_shape=[jax.ShapeDtypeStruct(piece, BF)] * n_ctx,
        grid_spec=pltpu.PrefetchScalarGridSpec(
            num_scalar_prefetch=1,
            grid=(1,),
            in_specs=[whole(da.shape), whole(weight.shape), whole(valid.shape)],
            out_specs=[whole(piece)] * n_ctx,
            scratch_shapes=[pltpu.VMEM((per * n_ctx, PAIR, HD), BF)],
        ),
        compiler_params=params(),
        cost_estimate=pl.CostEstimate(
            flops=2 * rows * depth * width, bytes_accessed=rows * depth * 2 + 2 * depth * width, transcendentals=0
        ),
    )(scalars, da, weight, valid)


def in_kernel(n_ctx, pairs, scalar_ref, *refs):
    piece_refs, weight_refs, valid_ref = refs[:n_ctx], refs[n_ctx : n_ctx + 3], refs[n_ctx + 3]
    grad_refs, partial_refs, buffer = refs[n_ctx + 4 : n_ctx + 7], refs[n_ctx + 7 : -1], refs[-1]
    me = scalar_ref[0]
    first, second = halves_at(scalar_ref[1])
    per = piece_refs[0].shape[0]
    heads = weight_refs[0].shape[1] // HD
    for k in range(n_ctx):
        source = jnp.bitwise_xor(me, k)
        for p in range(per):
            buffer[source * per + p] = piece_refs[k][p]
    for sequence in range(pairs // heads):
        at = slice(sequence * PAIR, (sequence + 1) * PAIR)
        total = None
        for which in range(3):
            rows = jnp.concatenate(
                [
                    jnp.concatenate([buffer[pair, which, first, :], buffer[pair, which, second, :]], axis=0)
                    for pair in range(sequence * heads, (sequence + 1) * heads)
                ],
                axis=1,
            )
            if which == 2:
                rows = rows * valid_ref[at, :]
            grad_refs[which][at, :] = rows
            product = times_transposed(rows, weight_refs[which][...])
            total = product if total is None else total + product
        put_partial(partial_refs, sequence * PAIR, total.astype(BF), pairs // heads * PAIR // 4)


def project_in(scalars, pieces, weights, valid, pairs, n_ctx, split):
    depth, width = weights[0].shape
    rows = valid.shape[0]
    per = pieces[0].shape[0]
    shapes = [jax.ShapeDtypeStruct((rows, width), BF)] * 3 + partial_shapes(rows, depth, split)
    return pl.pallas_call(
        functools.partial(in_kernel, n_ctx, pairs),
        out_shape=shapes,
        grid_spec=pltpu.PrefetchScalarGridSpec(
            num_scalar_prefetch=1,
            grid=(1,),
            in_specs=[whole(piece.shape) for piece in pieces]
            + [whole(weight.shape) for weight in weights]
            + [whole(valid.shape)],
            out_specs=[whole(shape.shape) for shape in shapes],
            scratch_shapes=[pltpu.VMEM((per * n_ctx, 3, PAIR, HD), BF)],
        ),
        compiler_params=params(),
        cost_estimate=pl.CostEstimate(
            flops=6 * rows * depth * width, bytes_accessed=rows * depth * 2 + 6 * depth * width, transcendentals=0
        ),
    )(scalars, *pieces, *weights, valid)


def both_places(me, k, n_ctx):
    source = jnp.bitwise_xor(me, k)
    front = pl.multiple_of(source * BLOCK, BLOCK)
    back = pl.multiple_of((2 * n_ctx - 1 - source) * BLOCK, BLOCK)
    return pl.ds(front, BLOCK), pl.ds(back, BLOCK)


def attention_kernel(n_ctx, tile, scalar_ref, *refs):
    x_refs, o_refs, (qs, ks, vs, os) = refs[:n_ctx], refs[n_ctx : 2 * n_ctx], refs[2 * n_ctx :]
    me = scalar_ref[0]
    length = 2 * n_ctx * BLOCK
    for k in range(n_ctx):
        front, back = both_places(me, k, n_ctx)
        for which, dest in enumerate((qs, ks, vs)):
            dest[front, :] = x_refs[k][0, which, :BLOCK, :]
            dest[back, :] = x_refs[k][0, which, BLOCK:, :]
    factor = -(HD ** (-0.5)) * LOG2E
    shift = math.log(length) * LOG2E
    row_at = lax.broadcasted_iota(jnp.int32, (tile, tile), 0)
    col_at = lax.broadcasted_iota(jnp.int32, (tile, tile), 1)
    for i in range(length // tile):
        query = qs[i * tile : (i + 1) * tile, :]

        def part(j, masked):
            at = pl.ds(pl.multiple_of(j * tile, tile), tile)
            raw = times_transposed(query, ks[at, :])
            prob = 1.0 / (1.0 + jnp.exp2(raw * factor + shift))
            if masked:
                prob = jnp.where(row_at >= col_at, prob, 0.0)
            return dot(prob.astype(BF), vs[at, :])

        total = part(i, True)
        if i > 0:
            total = lax.fori_loop(0, i, lambda j, acc: acc + part(j, False), total)
        os[i * tile : (i + 1) * tile, :] = total.astype(BF)
    for k in range(n_ctx):
        front, back = both_places(me, k, n_ctx)
        o_refs[k][0, :BLOCK, :] = os[front, :]
        o_refs[k][0, BLOCK:, :] = os[back, :]


def attention_forward(scalars, pieces, n_ctx):
    pairs = pieces[0].shape[0]
    length = 2 * n_ctx * BLOCK
    tile = min(512, length)
    return pl.pallas_call(
        functools.partial(attention_kernel, n_ctx, tile),
        out_shape=[jax.ShapeDtypeStruct((pairs, PAIR, HD), BF)] * n_ctx,
        grid_spec=pltpu.PrefetchScalarGridSpec(
            num_scalar_prefetch=1,
            grid=(pairs,),
            in_specs=[pl.BlockSpec((1, 3, PAIR, HD), lambda i, s: (i, 0, 0, 0))] * n_ctx,
            out_specs=[pl.BlockSpec((1, PAIR, HD), lambda i, s: (i, 0, 0))] * n_ctx,
            scratch_shapes=[pltpu.VMEM((length, HD), BF)] * 4,
        ),
        compiler_params=params(),
        cost_estimate=pl.CostEstimate(
            flops=pairs * length * length * HD * 6,
            bytes_accessed=pairs * length * HD * 8,
            transcendentals=pairs * length * length,
        ),
    )(scalars, *pieces)


def attention_back_kernel(n_ctx, tile, scalar_ref, *refs):
    x_refs, g_refs, (cos_ref, sin_ref) = refs[:n_ctx], refs[n_ctx : 2 * n_ctx], refs[2 * n_ctx : 2 * n_ctx + 2]
    out_refs = refs[2 * n_ctx + 2 : 3 * n_ctx + 2]
    qs, ks, vs, gs, os, dqs = refs[3 * n_ctx + 2 :]
    me = scalar_ref[0]
    length = 2 * n_ctx * BLOCK
    for k in range(n_ctx):
        front, back = both_places(me, k, n_ctx)
        for which, dest in enumerate((qs, ks, vs)):
            dest[front, :] = x_refs[k][0, which, :BLOCK, :]
            dest[back, :] = x_refs[k][0, which, BLOCK:, :]
        gs[front, :] = g_refs[k][0, :BLOCK, :]
        gs[back, :] = g_refs[k][0, BLOCK:, :]
    scale = HD ** (-0.5)
    factor = -scale * LOG2E
    shift = math.log(length) * LOG2E
    count = length // tile
    key_at = lax.broadcasted_iota(jnp.int32, (tile, tile), 0)
    query_at = lax.broadcasted_iota(jnp.int32, (tile, tile), 1)
    dqs[...] = jnp.zeros_like(dqs)

    def unrotate(values, at):
        return (values * cos_ref[at, :] - pltpu.roll(values, HD // 2, 1) * sin_ref[at, :]).astype(BF)

    for j in range(count):
        own = slice(j * tile, (j + 1) * tile)
        keys = ks[own, :]
        values = vs[own, :]

        def part(i, masked):
            at = pl.ds(pl.multiple_of(i * tile, tile), tile)
            query = qs[at, :]
            grad = gs[at, :]
            raw = times_transposed(keys, query)
            prob = 1.0 / (1.0 + jnp.exp2(raw * factor + shift))
            if masked:
                prob = jnp.where(query_at >= key_at, prob, 0.0)
            prob_grad = times_transposed(values, grad)
            score_grad = (prob_grad * prob * (1.0 - prob)).astype(BF)
            dqs[at, :] += contract_rows(score_grad, keys)
            return dot(score_grad, query), dot(prob.astype(BF), grad)

        total = part(j, True)
        if j + 1 < count:

            def step(i, acc):
                more = part(i, False)
                return acc[0] + more[0], acc[1] + more[1]

            total = lax.fori_loop(j + 1, count, step, total)
        os[1, own, :] = unrotate(total[0] * scale, own)
        os[2, own, :] = total[1].astype(BF)
    for i in range(count):
        at = slice(i * tile, (i + 1) * tile)
        os[0, at, :] = unrotate(dqs[at, :] * scale, at)
    for k in range(n_ctx):
        front, back = both_places(me, k, n_ctx)
        for which in range(3):
            out_refs[k][0, which, :BLOCK, :] = os[which, front, :]
            out_refs[k][0, which, BLOCK:, :] = os[which, back, :]


def attention_backward(scalars, pieces, grads, cos_tab, sin_tab, n_ctx):
    pairs = pieces[0].shape[0]
    length = 2 * n_ctx * BLOCK
    tile = min(512, length)
    three = pl.BlockSpec((1, 3, PAIR, HD), lambda i, s: (i, 0, 0, 0))
    one = pl.BlockSpec((1, PAIR, HD), lambda i, s: (i, 0, 0))
    return pl.pallas_call(
        functools.partial(attention_back_kernel, n_ctx, tile),
        out_shape=[jax.ShapeDtypeStruct((pairs, 3, PAIR, HD), BF)] * n_ctx,
        grid_spec=pltpu.PrefetchScalarGridSpec(
            num_scalar_prefetch=1,
            grid=(pairs,),
            in_specs=[three] * n_ctx + [one] * n_ctx + [whole((length, HD))] * 2,
            out_specs=[three] * n_ctx,
            scratch_shapes=[pltpu.VMEM((length, HD), BF)] * 4
            + [pltpu.VMEM((3, length, HD), BF), pltpu.VMEM((length, HD), F32)],
        ),
        compiler_params=params(),
        cost_estimate=pl.CostEstimate(
            flops=pairs * length * length * HD * 12,
            bytes_accessed=pairs * length * HD * 14,
            transcendentals=pairs * length * length,
        ),
    )(scalars, *pieces, *grads, cos_tab, sin_tab)


def mlp_kernel(n_ref, g_ref, wg_ref, wu_ref, wd_ref, *rest):
    h_ref, dgp_ref, dup_ref = rest[-3:]
    rows = n_ref[...]
    gate_pre = dot(rows, wg_ref[...])
    up_pre = dot(rows, wu_ref[...])
    hidden_grad = times_transposed(g_ref[...], wd_ref[...])
    gate_sig = 1.0 / (1.0 + jnp.exp2(gate_pre * (-LOG2E)))
    gate_act = gate_pre * gate_sig
    h_ref[...] = (gate_act * up_pre).astype(BF)
    dup_ref[...] = (hidden_grad * gate_act).astype(BF)
    dgp_ref[...] = (hidden_grad * up_pre * (gate_sig * (1.0 + gate_pre * (1.0 - gate_sig)))).astype(BF)


def mlp_core(normed, grads, wg, wu, wd, total, first, held=()):
    rows, depth = normed.shape
    hidden = wg.shape[1]
    row_tile, tile = 512, 512
    skip = first // row_tile
    row_block = pl.BlockSpec((row_tile, depth), lambda j, i: (i, 0))
    out_block = pl.BlockSpec((row_tile, tile), lambda j, i: (i + skip, j))
    out = jax.ShapeDtypeStruct((total, hidden), BF)
    return pl.pallas_call(
        mlp_kernel,
        out_shape=(out, out, out),
        grid=(hidden // tile, rows // row_tile),
        in_specs=[
            row_block,
            row_block,
            pl.BlockSpec((depth, tile), lambda j, i: (0, j)),
            pl.BlockSpec((depth, tile), lambda j, i: (0, j)),
            pl.BlockSpec((tile, depth), lambda j, i: (j, 0)),
        ]
        + [pl.BlockSpec(memory_space=pl.ANY)] * len(held),
        out_specs=(out_block, out_block, out_block),
        input_output_aliases={5 + k: k for k in range(len(held))},
        compiler_params=params(),
        cost_estimate=pl.CostEstimate(
            flops=6 * rows * depth * hidden,
            bytes_accessed=rows * depth * 4 + 6 * depth * hidden + 6 * rows * hidden,
            transcendentals=rows * hidden,
        ),
    )(normed, grads, wg, wu, wd, *held)


def inverse_rms(values):
    return lax.rsqrt(jnp.mean(values * values, axis=-1, keepdims=True) + EPS)


def neighbours():
    index, rank = lax.axis_index("ctx"), lax.axis_index("tp")
    return (index, jnp.bitwise_xor(rank, 1)), (index, jnp.bitwise_xor(rank, 2))


def remote(source, dest, send_sem, recv_sem, device):
    return pltpu.make_async_remote_copy(
        src_ref=source,
        dst_ref=dest,
        send_sem=send_sem,
        recv_sem=recv_sem,
        device_id=device,
        device_id_type=pl.DeviceIdType.MESH,
    )


def signal(sem, device):
    pl.semaphore_signal(sem, inc=1, device_id=device, device_id_type=pl.DeviceIdType.MESH)


class Scatter:
    def __init__(self, partial, groups, bufs, sems):
        self.partial, self.groups = partial, groups
        self.from_x, self.from_y, self.stay, self.stay_y, self.stay_x, self.for_y, self.for_x, self.low, self.high = bufs
        self.first_send, self.first_recv, self.second_send, self.second_recv, self.load_sem = sems
        self.to_x, self.to_y = neighbours()

    @staticmethod
    def scratch(rows, width):
        dma = pltpu.SemaphoreType.DMA
        whole_rows, half_rows = pltpu.VMEM((rows, width), BF), pltpu.VMEM((rows // 2, width), BF)
        return [whole_rows] * 3 + [half_rows] * 6 + [dma((8,)), dma((8,)), dma((4,)), dma((4,)), dma((6,))]

    def first_copies(self, g):
        base, rows, own = self.groups[g]
        half = rows // 2
        part = lambda number: self.partial.at[pl.ds(base + number * half, half)]
        at = lambda buf, number: buf.at[pl.ds(own + number * half, half)]
        plan = [
            (part(2), at(self.from_x, 0), self.to_x),
            (part(6), at(self.from_x, 1), self.to_x),
            (part(5), at(self.from_y, 0), self.to_y),
            (part(7), at(self.from_y, 1), self.to_y),
        ]
        return [
            remote(source, dest, self.first_send.at[4 * g + k], self.first_recv.at[4 * g + k], device)
            for k, (source, dest, device) in enumerate(plan)
        ]

    def loads(self, g):
        base, rows, own = self.groups[g]
        half = rows // 2
        copy = lambda number, count, dest, k: pltpu.make_async_copy(
            self.partial.at[pl.ds(base + number * half, count)], dest, self.load_sem.at[3 * g + k]
        )
        return [
            copy(0, rows, self.stay.at[pl.ds(own, rows)], 0),
            copy(4, half, self.stay_y.at[pl.ds(own // 2, half)], 1),
            copy(3, half, self.stay_x.at[pl.ds(own // 2, half)], 2),
        ]

    def second_copies(self, g):
        _, rows, own = self.groups[g]
        at = pl.ds(own // 2, rows // 2)
        return [
            remote(self.for_y.at[at], self.low.at[at], self.second_send.at[2 * g], self.second_recv.at[2 * g], self.to_y),
            remote(
                self.for_x.at[at], self.high.at[at], self.second_send.at[2 * g + 1], self.second_recv.at[2 * g + 1], self.to_x
            ),
        ]

    def start(self, g):
        copies = self.first_copies(g)
        for k in (1, 3, 0, 2):
            copies[k].start()
        for copy in self.loads(g):
            copy.start()

    def forward(self, g):
        _, rows, own = self.groups[g]
        half = rows // 2
        copies = self.first_copies(g)
        copies[1].wait_recv()
        copies[3].wait_recv()
        for copy in self.loads(g):
            copy.wait()
        at = pl.ds(own // 2, half)
        self.for_y[at, :] = add_low(self.stay_y[at, :], self.from_x[pl.ds(own + half, half), :])
        self.for_x[at, :] = add_low(self.stay_x[at, :], self.from_y[pl.ds(own + half, half), :])
        for copy in self.second_copies(g):
            copy.start()

    def total(self, g, use):
        _, rows, own = self.groups[g]
        half = rows // 2
        copies, seconds = self.first_copies(g), self.second_copies(g)
        copies[0].wait_recv()
        copies[2].wait_recv()
        for copy in copies:
            copy.wait_send()
        for copy in seconds:
            copy.wait()
        first = pl.ds(own, half)
        rest = pl.ds(own // 2, half)
        for side, (got, more) in enumerate(((self.from_x, self.low), (self.from_y, self.high))):
            at = pl.ds(own + side * half, half)
            use(at, self.stay[at, :].astype(F32) + got[first, :].astype(F32) + more[rest, :].astype(F32))


class Gather:
    def __init__(self, own, out, groups, sems):
        self.own, self.out, self.groups = own, out, groups
        self.first_send, self.first_recv, self.second_send, self.second_recv, self.local_sem = sems
        self.to_x, self.to_y = neighbours()

    @staticmethod
    def scratch():
        dma = pltpu.SemaphoreType.DMA
        return [dma((4,)), dma((4,)), dma((4,)), dma((4,)), dma((2,))]

    def first_copies(self, g):
        base, rows, own = self.groups[g]
        source = self.own.at[pl.ds(own, rows)]
        place = lambda k: self.out.at[pl.ds(base + k * rows, rows)]
        return [
            remote(source, place(1), self.first_send.at[2 * g], self.first_recv.at[2 * g], self.to_x),
            remote(source, place(2), self.first_send.at[2 * g + 1], self.first_recv.at[2 * g + 1], self.to_y),
        ]

    def local(self, g):
        base, rows, own = self.groups[g]
        return pltpu.make_async_copy(self.own.at[pl.ds(own, rows)], self.out.at[pl.ds(base, rows)], self.local_sem.at[g])

    def second_copies(self, g):
        base, rows, _ = self.groups[g]
        half = rows // 2
        part = lambda number: self.out.at[pl.ds(base + number * half, half)]
        return [
            remote(part(4), part(6), self.second_send.at[2 * g], self.second_recv.at[2 * g], self.to_x),
            remote(part(3), part(7), self.second_send.at[2 * g + 1], self.second_recv.at[2 * g + 1], self.to_y),
        ]

    def start(self, g):
        for copy in self.first_copies(g):
            copy.start()
        self.local(g).start()

    def forward(self, g):
        for copy in self.first_copies(g):
            copy.wait_recv()
        for copy in self.second_copies(g):
            copy.start()

    def finish(self, g):
        for copy in self.first_copies(g):
            copy.wait_send()
        for copy in self.second_copies(g):
            copy.wait()
        self.local(g).wait()


ROWS = 128
CORE_SLOTS, HOP_SLOTS = 3, 4


class Ring:
    def __init__(self, slots, send_sem, recv_sem, credit, total):
        self.slots, self.send_sem, self.recv_sem, self.credit, self.total = slots, send_sem, recv_sem, credit, total
        self.count = slots.shape[0]

    def copy(self, source, at, send_at, device):
        slot = lax.rem(at, self.count)
        return pltpu.make_async_remote_copy(
            src_ref=source,
            dst_ref=self.slots.at[slot],
            send_sem=self.send_sem.at[send_at],
            recv_sem=self.recv_sem.at[slot],
            device_id=device,
            device_id_type=pl.DeviceIdType.MESH,
        )

    def send(self, source, at, send_at, device):
        @pl.when(at >= self.count)
        def _():
            pl.semaphore_wait(self.credit, 1)

        self.copy(source, at, send_at, device).start()

    def sent(self, source, at, send_at, device):
        self.copy(source, at, send_at, device).wait_send()

    def arrived(self, source, at, send_at, device):
        self.copy(source, at, send_at, device).wait_recv()
        return self.slots.at[lax.rem(at, self.count)]

    def free(self, at, device):
        @pl.when(at + self.count < self.total)
        def _():
            pl.semaphore_signal(self.credit, inc=1, device_id=device, device_id_type=pl.DeviceIdType.MESH)


def sums_kernel(n_ctx, items, n_right, n_extra, tasks, *refs):
    n_left = len(items)
    left_refs, right_refs = refs[:n_left], refs[n_left : n_left + n_right]
    extra_in, refs = refs[n_left + n_right : n_left + n_right + n_extra[0]], refs[n_left + n_right + n_extra[0] :]
    out_refs, extra_out, refs = refs[:n_left], refs[n_left : n_left + n_extra[1]], refs[n_left + n_extra[1] :]
    extra_scratch, refs = refs[: n_extra[2]], refs[n_extra[2] :]
    (
        left_buf, right_buf, other_buf, ring, core_in, hop_in, hop_mid, hop_out, core_out,
        left_sem, right_sem, core_send, core_recv, in_send, in_recv, mid_send, mid_recv, out_send, out_recv,
        fin_send, fin_recv, store_sem, core_credit, in_credit, mid_credit, out_credit, fin_credit,
    ) = refs
    starts = [0]
    for _, _, chunks in items:
        starts.append(starts[-1] + chunks)
    total = starts[-1]
    n_ring = ring.shape[0]
    chips = n_ctx // 2
    mid = chips // 2
    index = lax.axis_index("ctx")
    rank = lax.axis_index("tp")
    core = lax.rem(index, 2)
    chip = index // 2
    low_side = chip < mid
    place = jnp.where(low_side, chip, chips - 1 - chip)
    toward = jnp.where(low_side, 1, -1)
    partner = (chip * 2 + 1 - core, rank)
    after = ((chip + toward) * 2 + core, rank)
    before = ((chip - toward) * 2 + core, rank)
    is_first = place == 0
    is_last = place == mid - 1
    lag_t = mid
    lag_u = lag_t + 2
    lag_o = lag_u + 2 * (mid - 1)
    lag_f = lag_o + 1
    lag_w = lag_f + 1

    barrier = pltpu.get_barrier_semaphore()
    pl.semaphore_signal(barrier, inc=1, device_id=partner, device_id_type=pl.DeviceIdType.MESH)

    @pl.when(chip > 0)
    def _():
        pl.semaphore_signal(
            barrier, inc=1, device_id=((chip - 1) * 2 + core, rank), device_id_type=pl.DeviceIdType.MESH
        )

    @pl.when(chip < chips - 1)
    def _():
        pl.semaphore_signal(
            barrier, inc=1, device_id=((chip + 1) * 2 + core, rank), device_id_type=pl.DeviceIdType.MESH
        )

    greeted = 1
    if tasks is not None:
        for device in neighbours():
            signal(barrier, device)
        greeted = 3
    pl.semaphore_wait(barrier, greeted + jnp.where(chip > 0, 1, 0) + jnp.where(chip < chips - 1, 1, 0))

    to_core = Ring(core_in, core_send, core_recv, core_credit, total)
    to_after = Ring(hop_in, in_send, in_recv, in_credit, total)
    across = Ring(hop_mid, mid_send, mid_recv, mid_credit, total)
    to_before = Ring(hop_out, out_send, out_recv, out_credit, total)
    to_final = Ring(core_out, fin_send, fin_recv, fin_credit, total)

    rights = [pltpu.make_async_copy(right_refs[k], right_buf.at[k], right_sem.at[k]) for k in range(n_right)]
    for copy in rights:
        copy.start()

    def for_item(at, action):
        for number in range(n_left):
            @pl.when((at >= starts[number]) & (at < starts[number + 1]))
            def _(number=number):
                action(number, at - starts[number])

    def rows_at(number, chunk, side):
        half = items[number][2] * ROWS
        return pl.multiple_of(side * half + chunk * ROWS, ROWS)

    def left_copy(number, chunk, slot, which):
        side = core if which == 0 else 1 - core
        return pltpu.make_async_copy(
            left_refs[number].at[:, pl.ds(rows_at(number, chunk, side), ROWS)],
            left_buf.at[slot, which],
            left_sem.at[slot, which],
        )

    def load_left(at):
        def action(number, chunk):
            for which in range(2):
                left_copy(number, chunk, lax.rem(at, 2), which).start()

        for_item(at, action)

    load_left(0)
    planned = tasks(extra_in, extra_out, extra_scratch) if tasks is not None else {}
    if 0 in planned:
        planned.pop(0)()
    for copy in rights:
        copy.wait()

    def step(i, carry):
        def at_lag(lag):
            at = i - lag
            return at, (at >= 0) & (at < total)

        at, now = at_lag(lag_w)

        @pl.when(now)
        def _():
            slot = lax.rem(at, n_ring)
            source = ring.at[slot]

            def action(number, chunk):
                store(number, chunk, at, 0).wait()
                store(number, chunk, at, 1).wait()

            for_item(at, action)
            to_final.sent(source, at, slot, partner)
            to_final.free(at, partner)

            @pl.when(jnp.logical_not(is_first))
            def _():
                to_before.sent(source, at, slot, before)

        at, now = at_lag(lag_o)

        @pl.when(now & jnp.logical_not(is_last))
        def _():
            slot = lax.rem(at, n_ring)
            source = ring.at[slot]
            to_after.sent(source, at, slot, after)
            got = to_before.arrived(source, at, slot, after)
            ring[slot] = got[...]
            to_before.free(at, after)

            @pl.when(jnp.logical_not(is_first))
            def _():
                to_before.send(source, at, slot, before)

        @pl.when(now)
        def _():
            slot = lax.rem(at, n_ring)
            to_final.send(ring.at[slot], at, slot, partner)

        at, now = at_lag(lag_u)

        @pl.when(now & is_last)
        def _():
            slot = lax.rem(at, n_ring)
            source = ring.at[slot]
            across.sent(source, at, slot, after)
            got = across.arrived(source, at, slot, after)
            ring[slot] = add_low(ring[slot], got[...])
            across.free(at, after)

            @pl.when(jnp.logical_not(is_first))
            def _():
                to_before.send(source, at, slot, before)

        at, now = at_lag(lag_t)

        @pl.when(now)
        def _():
            slot = lax.rem(at, n_ring)
            source = ring.at[slot]

            @pl.when(jnp.logical_not(is_first))
            def _():
                got = to_after.arrived(source, at, slot, before)
                ring[slot] = add_low(ring[slot], got[...])
                to_after.free(at, before)

            @pl.when(is_last)
            def _():
                across.send(source, at, slot, after)

            @pl.when(jnp.logical_not(is_first) & jnp.logical_not(is_last))
            def _():
                to_after.send(source, at, slot, after)

        at, now = at_lag(1)

        @pl.when(now)
        def _():
            slot = lax.rem(at, n_ring)
            source = ring.at[slot]
            own = other_buf.at[lax.rem(at, 2)]
            to_core.sent(own, at, lax.rem(at, 2), partner)
            got = to_core.arrived(own, at, lax.rem(at, 2), partner)
            ring[slot] = add_low(ring[slot], got[...])
            to_core.free(at, partner)

            @pl.when(is_first & jnp.logical_not(is_last))
            def _():
                to_after.send(source, at, slot, after)

        at, now = at_lag(lag_f)

        @pl.when(now)
        def _():
            slot = lax.rem(at, n_ring)
            to_final.arrived(ring.at[slot], at, slot, partner)

            def action(number, chunk):
                store(number, chunk, at, 0).start()
                store(number, chunk, at, 1).start()

            for_item(at, action)

        for when, task in planned.items():
            pl.when(i == when)(task)

        @pl.when(i + 1 < total)
        def _():
            load_left(i + 1)

        @pl.when(i < total)
        def _():
            slot = lax.rem(i, 2)

            def action(number, chunk):
                for which in range(2):
                    left_copy(number, chunk, slot, which).wait()
                right = right_buf.at[items[number][1]]
                other_buf[slot] = contract_rows(left_buf[slot, 1], right[...]).astype(BF)
                to_core.send(other_buf.at[slot], i, slot, partner)
                ring[lax.rem(i, n_ring)] = contract_rows(left_buf[slot, 0], right[...]).astype(BF)

            for_item(i, action)

        return carry

    def store(number, chunk, at, which):
        source = ring.at[lax.rem(at, n_ring)] if which == 0 else core_out.at[lax.rem(at, CORE_SLOTS)]
        side = core if which == 0 else 1 - core
        return pltpu.make_async_copy(
            source,
            out_refs[number].at[pl.ds(rows_at(number, chunk, side), ROWS), :],
            store_sem.at[which, lax.rem(at, 2)],
        )

    lax.fori_loop(0, total + lag_w, step, 0)


def weight_sums(items, rights, n_ctx, collective_id, extra=None):
    tokens, width = rights[0].shape
    shapes = [(k, right, left.shape[1] // 2 // ROWS) for k, (left, right) in enumerate(items)]
    mid = n_ctx // 4
    n_ring = mid + 2 + 2 * (mid - 1) + 3
    any_spec = pl.BlockSpec(memory_space=pl.ANY)
    args, arg_specs, outs, out_specs, scratch, tasks = extra if extra is not None else ([], [], [], [], [], None)
    counts = (len(args), len(outs), len(scratch))
    chunk = (ROWS, width)
    dma = pltpu.SemaphoreType.DMA
    return pl.pallas_call(
        functools.partial(sums_kernel, n_ctx, shapes, len(rights), counts, tasks),
        out_shape=[jax.ShapeDtypeStruct((left.shape[1], width), BF) for left, _ in items] + outs,
        in_specs=[any_spec] * (len(items) + len(rights)) + arg_specs,
        out_specs=[any_spec] * len(items) + out_specs,
        scratch_shapes=scratch
        + [
            pltpu.VMEM((2, 2, tokens, ROWS), BF),
            pltpu.VMEM((len(rights), tokens, width), BF),
            pltpu.VMEM((2,) + chunk, BF),
            pltpu.VMEM((n_ring,) + chunk, BF),
            pltpu.VMEM((CORE_SLOTS,) + chunk, BF),
            pltpu.VMEM((HOP_SLOTS,) + chunk, BF),
            pltpu.VMEM((HOP_SLOTS,) + chunk, BF),
            pltpu.VMEM((HOP_SLOTS,) + chunk, BF),
            pltpu.VMEM((CORE_SLOTS,) + chunk, BF),
            dma((2, 2)),
            dma((len(rights),)),
            dma((2,)),
            dma((CORE_SLOTS,)),
            dma((n_ring,)),
            dma((HOP_SLOTS,)),
            dma((n_ring,)),
            dma((HOP_SLOTS,)),
            dma((n_ring,)),
            dma((HOP_SLOTS,)),
            dma((n_ring,)),
            dma((CORE_SLOTS,)),
            dma((2, 2)),
        ]
        + [pltpu.SemaphoreType.REGULAR] * 5,
        compiler_params=pltpu.CompilerParams(
            vmem_limit_bytes=VMEM_LIMIT, collective_id=collective_id, has_side_effects=True
        ),
        cost_estimate=pl.CostEstimate(
            flops=sum(2 * left.shape[1] * tokens * width for left, _ in items),
            bytes_accessed=sum(2 * left.shape[1] * (tokens + width) for left, _ in items),
            transcendentals=0,
        ),
    )(*[left for left, _ in items], *rights, *args)


VMEM_SPEC = pl.BlockSpec(memory_space=pltpu.VMEM)
ANY_SPEC = pl.BlockSpec(memory_space=pl.ANY)


def norm_back_rows(values, gain, grad):
    inv = inverse_rms(values)
    unit = values * inv
    scaled = grad * gain
    back = (scaled - unit * jnp.mean(scaled * unit, axis=-1, keepdims=True)) * inv
    return back, jnp.sum(grad * unit, axis=0, keepdims=True)


def feed_tasks(groups, extra_in, extra_out, scratch):
    d_ref, y_ref, residual, grads, gain = extra_in
    dr, da_all, gain_grad, output = extra_out
    n = len(Scatter.scratch(16, 128))
    bufs, rest = scratch[:n], scratch[n:]
    da_own, free, gather_sems = rest[0], rest[1], rest[2:]
    first = Scatter(d_ref, groups, bufs[:9], bufs[9:])
    last = Scatter(y_ref, groups, bufs[:9], bufs[9:])
    gather = Gather(da_own, da_all, groups, gather_sems)
    order = list(reversed(range(len(groups))))

    def begin():
        gain_grad[...] = jnp.zeros_like(gain_grad)
        for g in order:
            first.start(g)

    def use(at, total):
        back, more = norm_back_rows(residual[at, :], gain[...], total)
        total_grad = grads[at, :].astype(F32) + back
        dr[at, :] = total_grad
        da_own[at, :] = total_grad.astype(BF)
        gain_grad[...] += more

    def spread(g):
        first.total(g, use)
        gather.start(g)

    def use_out(at, total):
        output[at, :] = (residual[at, :] + total).astype(BF)

    def again():
        for device in neighbours():
            signal(free, device)
        for g in order:
            gather.finish(g)

    def begin_out():
        pl.semaphore_wait(free, 2)
        for g in order:
            last.start(g)

    def forward_all():
        for g in order:
            last.forward(g)

    plan = {
        0: begin,
        2: lambda: first.forward(order[0]),
        4: lambda: first.forward(order[-1]),
        5: lambda: spread(order[0]),
        6: lambda: spread(order[-1]),
        8: lambda: gather.forward(order[0]),
        10: lambda: gather.forward(order[-1]),
        12: again,
        13: begin_out,
        16: forward_all,
        18: lambda: [last.total(g, use_out) for g in order] and None,
    }
    return plan


def feed_extra(groups, d_partial, y_partial, residual, grads, gain):
    rows, width = residual.shape
    outs = [
        jax.ShapeDtypeStruct((rows, width), F32),
        jax.ShapeDtypeStruct(d_partial.shape, BF),
        jax.ShapeDtypeStruct((1, width), F32),
        jax.ShapeDtypeStruct((rows, width), BF),
    ]
    scratch = (
        Scatter.scratch(rows, width)
        + [pltpu.VMEM((rows, width), BF), pltpu.SemaphoreType.REGULAR]
        + Gather.scratch()
    )
    return (
        [d_partial, y_partial, residual, grads, gain],
        [ANY_SPEC, ANY_SPEC, VMEM_SPEC, VMEM_SPEC, VMEM_SPEC],
        outs,
        [VMEM_SPEC, ANY_SPEC, VMEM_SPEC, VMEM_SPEC],
        scratch,
        functools.partial(feed_tasks, groups),
    )


def input_tasks(groups, extra_in, extra_out, scratch):
    i_ref, rows_in, dr, gain = extra_in
    input_grad, gain_grad = extra_out
    scatter = Scatter(i_ref, groups, scratch[:9], scratch[9:])
    order = list(reversed(range(len(groups))))

    def begin():
        gain_grad[...] = jnp.zeros_like(gain_grad)
        for g in order:
            scatter.start(g)

    def use(at, total):
        back, more = norm_back_rows(rows_in[at, :], gain[...], total)
        input_grad[at, :] = (dr[at, :] + back).astype(BF)
        gain_grad[...] += more

    return {
        0: begin,
        2: lambda: scatter.forward(order[0]),
        4: lambda: scatter.forward(order[-1]),
        5: lambda: scatter.total(order[0], use),
        6: lambda: scatter.total(order[-1], use),
    }


def input_extra(groups, partial, rows_in, dr, gain):
    rows, width = rows_in.shape
    outs = [jax.ShapeDtypeStruct((rows, width), BF), jax.ShapeDtypeStruct((1, width), F32)]
    return (
        [partial, rows_in, dr, gain],
        [ANY_SPEC, VMEM_SPEC, VMEM_SPEC, VMEM_SPEC],
        outs,
        [VMEM_SPEC, VMEM_SPEC],
        Scatter.scratch(rows, width),
        functools.partial(input_tasks, groups),
    )


def body(
    tokens,
    counts,
    norm_gain,
    w_query,
    w_key,
    w_value,
    w_output,
    mlp_gain,
    w_gate,
    w_up,
    w_down,
    cotangent,
):
    n_ctx = lax.axis_size("ctx")
    me = lax.axis_index("ctx")
    rank = lax.axis_index("tp")
    odd = rank & 1
    core = me & 1
    length = 2 * BLOCK * n_ctx
    heads = w_query.shape[1] // HD
    gain_one = norm_gain.astype(F32)
    gain_two = mlp_gain.astype(F32)

    inverse = THETA ** (-(jnp.arange(HD // 2, dtype=F32) * (2.0 / HD)))
    angles = jnp.arange(length, dtype=jnp.int32).astype(F32)[:, None] * inverse[None, :]
    cos_half, sin_half = jnp.cos(angles), jnp.sin(angles)
    cos_full = jnp.concatenate([cos_half, cos_half], axis=1)
    sin_full = jnp.concatenate([-sin_half, sin_half], axis=1)

    def own_blocks(table):
        front = lax.dynamic_slice_in_dim(table, me * BLOCK, BLOCK, 0)
        back = lax.dynamic_slice_in_dim(table, (2 * n_ctx - 1 - me) * BLOCK, BLOCK, 0)
        return front, back

    cos_front, cos_back = own_blocks(cos_full)
    sin_front, sin_back = own_blocks(sin_full)
    own_counts = lax.dynamic_index_in_dim(counts, me, 0, keepdims=False)
    offsets = jnp.arange(BLOCK, dtype=jnp.int32)

    def valid_of(sequence, half):
        return (offsets < own_counts[sequence, half]).astype(F32)

    cos_own = jnp.concatenate([cos_front, cos_back])
    sin_own = jnp.concatenate([sin_front, sin_back])
    sequences = counts.shape[1]
    paired = lax.axis_size("tp") == 4 and sequences == 6
    if paired:
        ranks = [rank ^ k for k in range(4)]
        seq_a = [3 * (r >> 1) + 2 * (r & 1) for r in ranks]
        seq_b = [1 + 3 * (r >> 1) for r in ranks]
        valids = {
            "b": jnp.concatenate([valid_of(s, r & 1) for s, r in zip(seq_b, ranks)]),
            "a": jnp.concatenate([valid_of(s, half) for s in seq_a for half in range(2)]),
        }
        flip_back = lambda own: jnp.where(odd == 1, jnp.roll(own, BLOCK, axis=0), own)
        tables = {
            "b": (jnp.tile(flip_back(cos_own), (2, 1)), jnp.tile(flip_back(sin_own), (2, 1))),
            "a": (jnp.tile(cos_own, (4, 1)), jnp.tile(sin_own, (4, 1))),
        }
        scalars = {"b": jnp.stack([me, odd]).astype(jnp.int32), "a": jnp.stack([me, 0]).astype(jnp.int32)}
        n_pairs = {"b": 2 * heads, "a": 4 * heads}
    else:
        valids = {"a": jnp.concatenate([valid_of(s, half) for s in range(sequences) for half in range(2)])}
        tables = {"a": (jnp.tile(cos_own, (sequences, 1)), jnp.tile(sin_own, (sequences, 1)))}
        scalars = {"a": jnp.stack([me, 0]).astype(jnp.int32)}
        n_pairs = {"a": sequences * heads}
    names = tuple(n_pairs)

    def own_rows(array):
        if not paired:
            return {"a": array}
        return {
            "b": lax.dynamic_slice_in_dim(array, (1 - odd) * PAIR, BLOCK, 0),
            "a": lax.dynamic_slice_in_dim(array, odd * BLOCK, PAIR, 0),
        }

    def whole_rows(part):
        if not paired:
            return part["a"]
        return jnp.where(odd == 1, jnp.concatenate([part["b"], part["a"]]), jnp.concatenate([part["a"], part["b"]]))

    x_own = {name: rows.astype(F32) for name, rows in own_rows(tokens[0]).items()}
    g_own = own_rows(cotangent[0])

    split = by_four()
    rows_of = {name: valids[name].shape[0] for name in names}
    total_rows = sum(rows_of.values())
    first_row = {"a": 0, "b": rows_of["a"]}
    valid_head = {name: jnp.broadcast_to(valids[name][:, None], (rows_of[name], HD)) for name in names}
    valid_wide = {name: jnp.broadcast_to(valids[name][:, None].astype(BF), (rows_of[name], heads * HD)) for name in names}
    near = [k for k in range(n_ctx) if k < 6]
    far = [k for k in range(n_ctx) if k >= 6]
    state = {}

    def fence():
        names_held = list(state)
        values = lax.optimization_barrier([state[name] for name in names_held])
        state.update(zip(names_held, values))

    def only_b(step):
        if "b" in names:
            step("b")

    def norm_one(n):
        state["n1", n] = (x_own[n] * inverse_rms(x_own[n]) * gain_one).astype(BF)

    def gather_a(key):
        def step(n):
            state[key, n] = gather_first(state[key, n])

        return step

    def gather_b(key):
        def step(n):
            state[key, n] = gather_second(state[key, n])

        return step

    def query(n):
        state["n1", n] = gathered(state["n1", n])
        cos_tab, sin_tab = tables[n]
        state["qkv", n] = project_qkv(
            scalars[n], state["n1", n], w_query, w_key, w_value, cos_tab, sin_tab, valid_head[n], n_ctx
        )

    def swap_part(key, places, to):
        def step(n):
            got = dict(state.get((to, n), {}))
            got.update(exchange(state[key, n], places, n_ctx))
            state[to, n] = got
            if len(got) == n_ctx:
                state[to, n] = [got[k] for k in range(n_ctx)]
                del state[key, n]

        return step

    def attend(n):
        state["mixed", n] = attention_forward(scalars[n], state["got", n], n_ctx)

    def project(n):
        heads_out, *parts = project_out(
            scalars[n], state.pop(("back", n)), w_output, valid_wide[n], n_pairs[n], n_ctx, split
        )
        state["heads", n], state["r", n] = heads_out, tuple(parts)

    def scatter_a(key):
        def step(n):
            state[key, n] = scatter_first(state[key, n])

        return step

    def scatter_b(key):
        def step(n):
            state[key, n] = scatter_second(state[key, n])

        return step

    def norm_two(n):
        residual = x_own[n] + scattered(state.pop(("r", n)))
        state["residual", n] = residual
        state["n2", n] = (residual * inverse_rms(residual) * gain_two).astype(BF)

    def core_mlp(n):
        state["n2", n] = gathered(state["n2", n])
        state["cot", n] = gathered(state["cot", n])
        held = state.get("mlp", ())
        state["mlp"] = mlp_core(
            state["n2", n], state["cot", n], w_gate, w_up, w_down, total_rows, first_row[n], held
        )

    def attend_back(n):
        state["dqkv", n] = attention_backward(
            scalars[n], state.pop(("got", n)), state.pop(("gdo", n)), cos_full, sin_full, n_ctx
        )

    def query_back(n):
        dq, dk, dv, *parts = project_in(
            scalars[n], state.pop(("gdqkv", n)), (w_query, w_key, w_value), valid_wide[n], n_pairs[n], n_ctx, False
        )
        state["dq", n], state["dk", n], state["dv", n], state["i", n] = dq, dk, dv, parts[0]

    def joined(key):
        parts = [state[key, n] for n in ("a", "b") if n in names]
        return jnp.concatenate(parts) if len(parts) > 1 else parts[0]

    only_b(norm_one)
    only_b(gather_a("n1"))
    norm_one("a")
    for n in names:
        state["cot", n] = g_own[n]
    fence()
    only_b(gather_b("n1"))
    fence()
    gather_a("n1")("a")
    only_b(query)
    fence()
    gather_b("n1")("a")
    only_b(swap_part("qkv", near, "got"))
    fence()
    only_b(swap_part("qkv", far, "got"))
    only_b(gather_a("cot"))
    query("a")
    fence()
    swap_part("qkv", near, "got")("a")
    only_b(attend)
    only_b(gather_b("cot"))
    gather_a("cot")("a")
    fence()
    swap_part("qkv", far, "got")("a")
    only_b(swap_part("mixed", range(n_ctx), "back"))
    gather_b("cot")("a")
    fence()
    attend("a")
    only_b(project)
    only_b(scatter_a("r"))
    fence()
    swap_part("mixed", range(n_ctx), "back")("a")
    only_b(scatter_b("r"))
    only_b(norm_two)
    only_b(gather_a("n2"))
    fence()
    project("a")
    only_b(gather_b("n2"))
    fence()
    scatter_a("r")("a")
    only_b(core_mlp)
    fence()
    scatter_b("r")("a")
    fence()
    norm_two("a")
    gather_a("n2")("a")
    fence()
    gather_b("n2")("a")
    fence()
    core_mlp("a")
    fence()
    groups = tuple((first_row[n], rows_of[n] // 4, first_row[n] // 4) for n in ("a", "b") if n in names)
    in_order = [n for n in ("a", "b") if n in names]

    def own_joined(parts):
        return jnp.concatenate([parts[n] for n in in_order]) if len(in_order) > 1 else parts[in_order[0]]

    def by_group(array, scale=1):
        return {n: array[first_row[n] // scale : (first_row[n] + rows_of[n]) // scale] for n in in_order}

    h, dgp, dup = state["mlp"]
    all_n1, all_n2, all_cot, heads_out = (joined(key) for key in ("n1", "n2", "cot", "heads"))
    d_partial = (times_transposed(dgp, w_gate) + times_transposed(dup, w_up)).astype(BF)
    y_partial = dot(h, w_down).astype(BF)
    own_residual, own_grads, own_x = (
        own_joined(part) for part in ({n: state["residual", n] for n in names}, g_own, x_own)
    )
    feed_items, feed_rights = [(h, 0), (dgp, 1), (dup, 1)], [all_cot, all_n2]
    if split:
        extra = feed_extra(groups, d_partial, y_partial, own_residual, own_grads, gain_two[None])
        sum_down, sum_gate, sum_up, dr, da, gain_two_grad, output = weight_sums(feed_items, feed_rights, n_ctx, 1, extra)
    else:
        sum_down, sum_gate, sum_up = weight_sums(feed_items, feed_rights, n_ctx, 1)
        back, gain_two_grad = norm_back_rows(own_residual, gain_two, scattered(scatter_first((d_partial,))))
        dr = own_grads.astype(F32) + back
        da = gathered(gather_first(dr.astype(BF)))
        output = (own_residual + scattered(scatter_first((y_partial,)))).astype(BF)
    for n, rows in by_group(da).items():
        state["da", n] = rows
        state["do", n] = heads_back(scalars[n], rows, w_output, valid_wide[n], n_ctx)
    for n in names:
        swap_part("do", range(n_ctx), "gdo")(n)
    for n in names:
        attend_back(n)
        swap_part("dqkv", range(n_ctx), "gdqkv")(n)
    for n in names:
        query_back(n)
    i_partial = joined("i")
    input_items = [(heads_out, 0), (joined("dq"), 1), (joined("dk"), 1), (joined("dv"), 1)]
    if split:
        extra = input_extra(groups, i_partial, own_x, dr, gain_one[None])
        sum_out, sum_q, sum_k, sum_v, input_grad, gain_one_grad = weight_sums(
            input_items, [da, all_n1], n_ctx, 2, extra
        )
    else:
        sum_out, sum_q, sum_k, sum_v = weight_sums(input_items, [da, all_n1], n_ctx, 2)
        back, gain_one_grad = norm_back_rows(own_x, gain_one, scattered(scatter_first((i_partial,))))
        input_grad = (dr + back).astype(BF)
    gains = jnp.concatenate([gain_one_grad, gain_two_grad])
    for axis in ("tp", "ctx"):
        size = lax.axis_size(axis)
        for bit in range(size.bit_length() - 1):
            gains = gains + lax.ppermute(gains, axis, [(i, i ^ (1 << bit)) for i in range(size)])
    return (
        whole_rows(by_group(output, 4))[None] if split else output[None],
        whole_rows(by_group(input_grad, 4))[None] if split else input_grad[None],
        gains[0],
        sum_q.T.astype(F32),
        sum_k.T.astype(F32),
        sum_v.T.astype(F32),
        sum_out.astype(F32),
        gains[1],
        sum_gate.T.astype(F32),
        sum_up.T.astype(F32),
        sum_down.astype(F32),
    )


def solution(mesh):
    placed = (
        P("ctx", "tp", None),
        P(),
        P(),
        P(None, "tp"),
        P(None, "tp"),
        P(None, "tp"),
        P("tp", None),
        P(),
        P(None, "tp"),
        P(None, "tp"),
        P("tp", None),
        P("ctx", "tp", None),
    )
    return jax.shard_map(
        body,
        mesh=mesh,
        in_specs=placed,
        out_specs=(
            P("ctx", "tp", None),
            P("ctx", "tp", None),
            P(),
            P(None, "tp"),
            P(None, "tp"),
            P(None, "tp"),
            P("tp", None),
            P(),
            P(None, "tp"),
            P(None, "tp"),
            P("tp", None),
        ),
        check_vma=False,
    )
```

```python
import functools
import math

import jax
import jax.numpy as jnp
from jax import lax
from jax.experimental import pallas as pl
from jax.experimental.pallas import tpu as pltpu
from jax.sharding import PartitionSpec as P

HD = 128
BLOCK = 128
PAIR = 2 * BLOCK
EPS = 1e-05
THETA = 10000.0
LOG2E = 1.4426950408889634
BF = jnp.bfloat16
F32 = jnp.float32
VMEM_LIMIT = 58 * 1024 * 1024

X_SWAP = [(i, i ^ 1) for i in range(4)]
Y_SWAP = [(i, i ^ 2) for i in range(4)]


def dot(left, right):
    return jnp.dot(left, right, preferred_element_type=F32)


def contract_rows(left, right):
    return lax.dot_general(left, right, (((0,), (0,)), ((), ())), preferred_element_type=F32)


def times_transposed(left, right):
    return lax.dot_general(left, right, (((1,), (1,)), ((), ())), preferred_element_type=F32)


def send_x(values):
    return lax.ppermute(values, "tp", X_SWAP)


def send_y(values):
    return lax.ppermute(values, "tp", Y_SWAP)


def by_four():
    return lax.axis_size("tp") == 4


def gather_first(own):
    if not by_four():
        return (lax.all_gather(own, "tp", axis=0, tiled=True),)
    return own, send_x(own), send_y(own)


def gather_second(held):
    if len(held) == 1:
        return held
    own, from_x, from_y = held
    half = own.shape[0] // 2
    return own, from_x, from_y, send_x(from_y[:half]), send_y(from_x[half:])


def gathered(held):
    return jnp.concatenate(held) if len(held) > 1 else held[0]


def scatter_parts(partial):
    if not by_four():
        return (partial,)
    rows = partial.shape[0] // 4
    half = rows // 2
    at = lambda first: partial[first * half : (first + 1) * half]
    return (
        jnp.concatenate([at(2), at(6)]),
        jnp.concatenate([at(5), at(7)]),
        jnp.concatenate([at(0), at(1), at(4), at(3)]),
    )


def scatter_first(parts):
    if len(parts) == 1:
        return (lax.psum_scatter(parts[0], "tp", scatter_dimension=0, tiled=True),)
    return send_x(parts[0]), send_y(parts[1]), parts[2]


def add_low(left, right):
    return (left.astype(F32) + right.astype(F32)).astype(BF)


def scatter_second(held):
    if len(held) == 1:
        return held
    from_x, from_y, stay = held
    half = from_x.shape[0] // 2
    low_rest = send_y(add_low(stay[2 * half : 3 * half], from_x[half:]))
    high_rest = send_x(add_low(stay[3 * half :], from_y[half:]))
    return from_x, from_y, stay, low_rest, high_rest


def scattered(held):
    if len(held) == 1:
        return held[0].astype(F32)
    from_x, from_y, stay, low_rest, high_rest = (part.astype(F32) for part in held)
    half = low_rest.shape[0]
    low = stay[:half] + from_x[:half] + low_rest
    high = stay[half : 2 * half] + from_y[:half] + high_rest
    return jnp.concatenate([low, high])


def exchange(pieces, places, n_ctx):
    got = {}
    for k in places:
        got[k] = pieces[k] if k == 0 else lax.ppermute(pieces[k], "ctx", [(i, i ^ k) for i in range(n_ctx)])
    return got


def params():
    return pltpu.CompilerParams(vmem_limit_bytes=VMEM_LIMIT)


def whole(shape):
    return pl.BlockSpec(shape, lambda *_: (0,) * len(shape))


def put_partial(refs, first, value, rows):
    if len(refs) == 1:
        refs[0][first : first + value.shape[0], :] = value
        return
    to_x, to_y, stay = refs
    half = rows // 2
    homes = {
        0: (stay, 0), 1: (stay, 1), 2: (to_x, 0), 3: (stay, 3), 4: (stay, 2), 5: (to_y, 0), 6: (to_x, 1), 7: (to_y, 1)
    }
    for part in range(value.shape[0] // half):
        ref, place = homes[first // half + part]
        ref[place * half : (place + 1) * half, :] = value[part * half : (part + 1) * half]


def partial_shapes(rows, width, split):
    if not split:
        return [jax.ShapeDtypeStruct((rows, width), BF)]
    return [jax.ShapeDtypeStruct((rows // 4, width), BF)] * 2 + [jax.ShapeDtypeStruct((rows // 2, width), BF)]


def per_device(pairs, n_ctx):
    return -(-pairs // n_ctx)


def halves_at(swap):
    first = pl.multiple_of(swap * BLOCK, BLOCK)
    second = pl.multiple_of((1 - swap) * BLOCK, BLOCK)
    return pl.ds(first, BLOCK), pl.ds(second, BLOCK)


def qkv_kernel(n_ctx, pairs, scalar_ref, n_ref, wq_ref, wk_ref, wv_ref, cos_ref, sin_ref, valid_ref, *rest):
    out_refs, buffer = rest[:n_ctx], rest[n_ctx]
    rows = n_ref[...]
    first, second = halves_at(scalar_ref[1])
    me = scalar_ref[0]
    cos_tab = cos_ref[...]
    sin_tab = sin_ref[...]
    heads = wq_ref.shape[1] // HD
    step = pl.program_id(0)
    per = out_refs[0].shape[0]
    for pair in range(pairs, per * n_ctx):
        buffer[pair] = jnp.zeros(buffer.shape[1:], BF)
    for which, w_ref in enumerate((wq_ref, wk_ref, wv_ref)):
        product = dot(rows, w_ref[...])
        for head in range(heads):
            part = product[:, head * HD : (head + 1) * HD]
            if which < 2:
                part = part * cos_tab + pltpu.roll(part, HD // 2, 1) * sin_tab
            else:
                part = part * valid_ref[...]
            part = part.astype(BF)
            buffer[step * heads + head, which, first, :] = part[:BLOCK]
            buffer[step * heads + head, which, second, :] = part[BLOCK:]

    @pl.when(step == pl.num_programs(0) - 1)
    def _():
        for k in range(n_ctx):
            source = jnp.bitwise_xor(me, k)
            for p in range(per):
                out_refs[k][p] = buffer[source * per + p]


def project_qkv(scalars, normed, wq, wk, wv, cos_tab, sin_tab, valid, n_ctx):
    rows, depth = normed.shape
    width = wq.shape[1]
    heads = width // HD
    steps = rows // PAIR
    per = per_device(steps * heads, n_ctx)
    row_block = pl.BlockSpec((PAIR, HD), lambda i, s: (i, 0))
    weight = whole((depth, width))
    piece = (per, 3, PAIR, HD)
    return pl.pallas_call(
        functools.partial(qkv_kernel, n_ctx, steps * heads),
        out_shape=[jax.ShapeDtypeStruct(piece, BF)] * n_ctx,
        grid_spec=pltpu.PrefetchScalarGridSpec(
            num_scalar_prefetch=1,
            grid=(steps,),
            in_specs=[
                pl.BlockSpec((PAIR, depth), lambda i, s: (i, 0)),
                weight,
                weight,
                weight,
                row_block,
                row_block,
                row_block,
            ],
            out_specs=[whole(piece)] * n_ctx,
            scratch_shapes=[pltpu.VMEM((per * n_ctx, 3, PAIR, HD), BF)],
        ),
        compiler_params=params(),
        cost_estimate=pl.CostEstimate(
            flops=6 * rows * depth * width, bytes_accessed=rows * depth * 2 + 6 * depth * width, transcendentals=0
        ),
    )(scalars, normed, wq, wk, wv, cos_tab, sin_tab, valid)


def out_kernel(n_ctx, pairs, scalar_ref, *refs):
    piece_refs, (w_ref, valid_ref), (heads_ref, *partial_refs), buffer = (
        refs[:n_ctx],
        refs[n_ctx : n_ctx + 2],
        refs[n_ctx + 2 : -1],
        refs[-1],
    )
    me = scalar_ref[0]
    first, second = halves_at(scalar_ref[1])
    per = piece_refs[0].shape[0]
    heads = w_ref.shape[0] // HD
    for k in range(n_ctx):
        source = jnp.bitwise_xor(me, k)
        for p in range(per):
            buffer[source * per + p] = piece_refs[k][p]
    weight = w_ref[...]
    for sequence in range(pairs // heads):
        at = slice(sequence * PAIR, (sequence + 1) * PAIR)
        rows = jnp.concatenate(
            [
                jnp.concatenate(
                    [buffer[sequence * heads + head, first, :], buffer[sequence * heads + head, second, :]], axis=0
                )
                for head in range(heads)
            ],
            axis=1,
        )
        rows = rows * valid_ref[at, :]
        heads_ref[at, :] = rows
        put_partial(partial_refs, sequence * PAIR, dot(rows, weight).astype(BF), pairs // heads * PAIR // 4)


def project_out(scalars, pieces, weight, valid, pairs, n_ctx, split):
    width, depth = weight.shape
    rows = valid.shape[0]
    per = pieces[0].shape[0]
    shapes = [jax.ShapeDtypeStruct((rows, width), BF)] + partial_shapes(rows, depth, split)
    return pl.pallas_call(
        functools.partial(out_kernel, n_ctx, pairs),
        out_shape=shapes,
        grid_spec=pltpu.PrefetchScalarGridSpec(
            num_scalar_prefetch=1,
            grid=(1,),
            in_specs=[whole(piece.shape) for piece in pieces] + [whole(weight.shape), whole(valid.shape)],
            out_specs=[whole(shape.shape) for shape in shapes],
            scratch_shapes=[pltpu.VMEM((per * n_ctx, PAIR, HD), BF)],
        ),
        compiler_params=params(),
        cost_estimate=pl.CostEstimate(
            flops=2 * rows * depth * width, bytes_accessed=rows * depth * 2 + 2 * depth * width, transcendentals=0
        ),
    )(scalars, *pieces, weight, valid)


def heads_back_kernel(n_ctx, scalar_ref, da_ref, w_ref, valid_ref, *rest):
    out_refs, buffer = rest[:n_ctx], rest[n_ctx]
    me = scalar_ref[0]
    first, second = halves_at(scalar_ref[1])
    per = out_refs[0].shape[0]
    heads = w_ref.shape[0] // HD
    weight = w_ref[...]
    for pair in range(da_ref.shape[0] // PAIR * heads, per * n_ctx):
        buffer[pair] = jnp.zeros(buffer.shape[1:], BF)
    for sequence in range(da_ref.shape[0] // PAIR):
        at = slice(sequence * PAIR, (sequence + 1) * PAIR)
        grad = times_transposed(da_ref[at, :], weight).astype(BF) * valid_ref[at, :]
        for head in range(heads):
            part = grad[:, head * HD : (head + 1) * HD]
            buffer[sequence * heads + head, first, :] = part[:BLOCK]
            buffer[sequence * heads + head, second, :] = part[BLOCK:]
    for k in range(n_ctx):
        source = jnp.bitwise_xor(me, k)
        for p in range(per):
            out_refs[k][p] = buffer[source * per + p]


def heads_back(scalars, da, weight, valid, n_ctx):
    rows, depth = da.shape
    width = weight.shape[0]
    per = per_device(rows // PAIR * (width // HD), n_ctx)
    piece = (per, PAIR, HD)
    return pl.pallas_call(
        functools.partial(heads_back_kernel, n_ctx),
        out_shape=[jax.ShapeDtypeStruct(piece, BF)] * n_ctx,
        grid_spec=pltpu.PrefetchScalarGridSpec(
            num_scalar_prefetch=1,
            grid=(1,),
            in_specs=[whole(da.shape), whole(weight.shape), whole(valid.shape)],
            out_specs=[whole(piece)] * n_ctx,
            scratch_shapes=[pltpu.VMEM((per * n_ctx, PAIR, HD), BF)],
        ),
        compiler_params=params(),
        cost_estimate=pl.CostEstimate(
            flops=2 * rows * depth * width, bytes_accessed=rows * depth * 2 + 2 * depth * width, transcendentals=0
        ),
    )(scalars, da, weight, valid)


def in_kernel(n_ctx, pairs, scalar_ref, *refs):
    piece_refs, weight_refs, valid_ref = refs[:n_ctx], refs[n_ctx : n_ctx + 3], refs[n_ctx + 3]
    grad_refs, partial_refs, buffer = refs[n_ctx + 4 : n_ctx + 7], refs[n_ctx + 7 : -1], refs[-1]
    me = scalar_ref[0]
    first, second = halves_at(scalar_ref[1])
    per = piece_refs[0].shape[0]
    heads = weight_refs[0].shape[1] // HD
    for k in range(n_ctx):
        source = jnp.bitwise_xor(me, k)
        for p in range(per):
            buffer[source * per + p] = piece_refs[k][p]
    for sequence in range(pairs // heads):
        at = slice(sequence * PAIR, (sequence + 1) * PAIR)
        total = None
        for which in range(3):
            rows = jnp.concatenate(
                [
                    jnp.concatenate([buffer[pair, which, first, :], buffer[pair, which, second, :]], axis=0)
                    for pair in range(sequence * heads, (sequence + 1) * heads)
                ],
                axis=1,
            )
            if which == 2:
                rows = rows * valid_ref[at, :]
            grad_refs[which][at, :] = rows
            product = times_transposed(rows, weight_refs[which][...])
            total = product if total is None else total + product
        put_partial(partial_refs, sequence * PAIR, total.astype(BF), pairs // heads * PAIR // 4)


def project_in(scalars, pieces, weights, valid, pairs, n_ctx, split):
    depth, width = weights[0].shape
    rows = valid.shape[0]
    per = pieces[0].shape[0]
    shapes = [jax.ShapeDtypeStruct((rows, width), BF)] * 3 + partial_shapes(rows, depth, split)
    return pl.pallas_call(
        functools.partial(in_kernel, n_ctx, pairs),
        out_shape=shapes,
        grid_spec=pltpu.PrefetchScalarGridSpec(
            num_scalar_prefetch=1,
            grid=(1,),
            in_specs=[whole(piece.shape) for piece in pieces]
            + [whole(weight.shape) for weight in weights]
            + [whole(valid.shape)],
            out_specs=[whole(shape.shape) for shape in shapes],
            scratch_shapes=[pltpu.VMEM((per * n_ctx, 3, PAIR, HD), BF)],
        ),
        compiler_params=params(),
        cost_estimate=pl.CostEstimate(
            flops=6 * rows * depth * width, bytes_accessed=rows * depth * 2 + 6 * depth * width, transcendentals=0
        ),
    )(scalars, *pieces, *weights, valid)


def both_places(me, k, n_ctx):
    source = jnp.bitwise_xor(me, k)
    front = pl.multiple_of(source * BLOCK, BLOCK)
    back = pl.multiple_of((2 * n_ctx - 1 - source) * BLOCK, BLOCK)
    return pl.ds(front, BLOCK), pl.ds(back, BLOCK)


def attention_kernel(n_ctx, tile, scalar_ref, *refs):
    x_refs, o_refs, (qs, ks, vs, os) = refs[:n_ctx], refs[n_ctx : 2 * n_ctx], refs[2 * n_ctx :]
    me = scalar_ref[0]
    length = 2 * n_ctx * BLOCK
    for k in range(n_ctx):
        front, back = both_places(me, k, n_ctx)
        for which, dest in enumerate((qs, ks, vs)):
            dest[front, :] = x_refs[k][0, which, :BLOCK, :]
            dest[back, :] = x_refs[k][0, which, BLOCK:, :]
    factor = -(HD ** (-0.5)) * LOG2E
    shift = math.log(length) * LOG2E
    row_at = lax.broadcasted_iota(jnp.int32, (tile, tile), 0)
    col_at = lax.broadcasted_iota(jnp.int32, (tile, tile), 1)
    for i in range(length // tile):
        query = qs[i * tile : (i + 1) * tile, :]

        def part(j, masked):
            at = pl.ds(pl.multiple_of(j * tile, tile), tile)
            raw = times_transposed(query, ks[at, :])
            prob = 1.0 / (1.0 + jnp.exp2(raw * factor + shift))
            if masked:
                prob = jnp.where(row_at >= col_at, prob, 0.0)
            return dot(prob.astype(BF), vs[at, :])

        total = part(i, True)
        if i > 0:
            total = lax.fori_loop(0, i, lambda j, acc: acc + part(j, False), total)
        os[i * tile : (i + 1) * tile, :] = total.astype(BF)
    for k in range(n_ctx):
        front, back = both_places(me, k, n_ctx)
        o_refs[k][0, :BLOCK, :] = os[front, :]
        o_refs[k][0, BLOCK:, :] = os[back, :]


def attention_forward(scalars, pieces, n_ctx):
    pairs = pieces[0].shape[0]
    length = 2 * n_ctx * BLOCK
    tile = min(512, length)
    return pl.pallas_call(
        functools.partial(attention_kernel, n_ctx, tile),
        out_shape=[jax.ShapeDtypeStruct((pairs, PAIR, HD), BF)] * n_ctx,
        grid_spec=pltpu.PrefetchScalarGridSpec(
            num_scalar_prefetch=1,
            grid=(pairs,),
            in_specs=[pl.BlockSpec((1, 3, PAIR, HD), lambda i, s: (i, 0, 0, 0))] * n_ctx,
            out_specs=[pl.BlockSpec((1, PAIR, HD), lambda i, s: (i, 0, 0))] * n_ctx,
            scratch_shapes=[pltpu.VMEM((length, HD), BF)] * 4,
        ),
        compiler_params=params(),
        cost_estimate=pl.CostEstimate(
            flops=pairs * length * length * HD * 6,
            bytes_accessed=pairs * length * HD * 8,
            transcendentals=pairs * length * length,
        ),
    )(scalars, *pieces)


def attention_back_kernel(n_ctx, tile, scalar_ref, *refs):
    x_refs, g_refs, (cos_ref, sin_ref) = refs[:n_ctx], refs[n_ctx : 2 * n_ctx], refs[2 * n_ctx : 2 * n_ctx + 2]
    out_refs = refs[2 * n_ctx + 2 : 3 * n_ctx + 2]
    qs, ks, vs, gs, os, dqs = refs[3 * n_ctx + 2 :]
    me = scalar_ref[0]
    length = 2 * n_ctx * BLOCK
    for k in range(n_ctx):
        front, back = both_places(me, k, n_ctx)
        for which, dest in enumerate((qs, ks, vs)):
            dest[front, :] = x_refs[k][0, which, :BLOCK, :]
            dest[back, :] = x_refs[k][0, which, BLOCK:, :]
        gs[front, :] = g_refs[k][0, :BLOCK, :]
        gs[back, :] = g_refs[k][0, BLOCK:, :]
    scale = HD ** (-0.5)
    factor = -scale * LOG2E
    shift = math.log(length) * LOG2E
    count = length // tile
    key_at = lax.broadcasted_iota(jnp.int32, (tile, tile), 0)
    query_at = lax.broadcasted_iota(jnp.int32, (tile, tile), 1)
    dqs[...] = jnp.zeros_like(dqs)

    def unrotate(values, at):
        return (values * cos_ref[at, :] - pltpu.roll(values, HD // 2, 1) * sin_ref[at, :]).astype(BF)

    for j in range(count):
        own = slice(j * tile, (j + 1) * tile)
        keys = ks[own, :]
        values = vs[own, :]

        def part(i, masked):
            at = pl.ds(pl.multiple_of(i * tile, tile), tile)
            query = qs[at, :]
            grad = gs[at, :]
            raw = times_transposed(keys, query)
            prob = 1.0 / (1.0 + jnp.exp2(raw * factor + shift))
            if masked:
                prob = jnp.where(query_at >= key_at, prob, 0.0)
            prob_grad = times_transposed(values, grad)
            score_grad = (prob_grad * prob * (1.0 - prob)).astype(BF)
            dqs[at, :] += contract_rows(score_grad, keys)
            return dot(score_grad, query), dot(prob.astype(BF), grad)

        total = part(j, True)
        if j + 1 < count:

            def step(i, acc):
                more = part(i, False)
                return acc[0] + more[0], acc[1] + more[1]

            total = lax.fori_loop(j + 1, count, step, total)
        os[1, own, :] = unrotate(total[0] * scale, own)
        os[2, own, :] = total[1].astype(BF)
    for i in range(count):
        at = slice(i * tile, (i + 1) * tile)
        os[0, at, :] = unrotate(dqs[at, :] * scale, at)
    for k in range(n_ctx):
        front, back = both_places(me, k, n_ctx)
        for which in range(3):
            out_refs[k][0, which, :BLOCK, :] = os[which, front, :]
            out_refs[k][0, which, BLOCK:, :] = os[which, back, :]


def attention_backward(scalars, pieces, grads, cos_tab, sin_tab, n_ctx):
    pairs = pieces[0].shape[0]
    length = 2 * n_ctx * BLOCK
    tile = min(512, length)
    three = pl.BlockSpec((1, 3, PAIR, HD), lambda i, s: (i, 0, 0, 0))
    one = pl.BlockSpec((1, PAIR, HD), lambda i, s: (i, 0, 0))
    return pl.pallas_call(
        functools.partial(attention_back_kernel, n_ctx, tile),
        out_shape=[jax.ShapeDtypeStruct((pairs, 3, PAIR, HD), BF)] * n_ctx,
        grid_spec=pltpu.PrefetchScalarGridSpec(
            num_scalar_prefetch=1,
            grid=(pairs,),
            in_specs=[three] * n_ctx + [one] * n_ctx + [whole((length, HD))] * 2,
            out_specs=[three] * n_ctx,
            scratch_shapes=[pltpu.VMEM((length, HD), BF)] * 4
            + [pltpu.VMEM((3, length, HD), BF), pltpu.VMEM((length, HD), F32)],
        ),
        compiler_params=params(),
        cost_estimate=pl.CostEstimate(
            flops=pairs * length * length * HD * 12,
            bytes_accessed=pairs * length * HD * 14,
            transcendentals=pairs * length * length,
        ),
    )(scalars, *pieces, *grads, cos_tab, sin_tab)


def mlp_kernel(n_ref, g_ref, wg_ref, wu_ref, wd_ref, *rest):
    h_ref, dgp_ref, dup_ref = rest[-3:]
    rows = n_ref[...]
    gate_pre = dot(rows, wg_ref[...])
    up_pre = dot(rows, wu_ref[...])
    hidden_grad = times_transposed(g_ref[...], wd_ref[...])
    gate_sig = 1.0 / (1.0 + jnp.exp2(gate_pre * (-LOG2E)))
    gate_act = gate_pre * gate_sig
    h_ref[...] = (gate_act * up_pre).astype(BF)
    dup_ref[...] = (hidden_grad * gate_act).astype(BF)
    dgp_ref[...] = (hidden_grad * up_pre * (gate_sig * (1.0 + gate_pre * (1.0 - gate_sig)))).astype(BF)


def mlp_core(normed, grads, wg, wu, wd, total, first, held=()):
    rows, depth = normed.shape
    hidden = wg.shape[1]
    row_tile, tile = 512, 512
    skip = first // row_tile
    row_block = pl.BlockSpec((row_tile, depth), lambda j, i: (i, 0))
    out_block = pl.BlockSpec((row_tile, tile), lambda j, i: (i + skip, j))
    out = jax.ShapeDtypeStruct((total, hidden), BF)
    return pl.pallas_call(
        mlp_kernel,
        out_shape=(out, out, out),
        grid=(hidden // tile, rows // row_tile),
        in_specs=[
            row_block,
            row_block,
            pl.BlockSpec((depth, tile), lambda j, i: (0, j)),
            pl.BlockSpec((depth, tile), lambda j, i: (0, j)),
            pl.BlockSpec((tile, depth), lambda j, i: (j, 0)),
        ]
        + [pl.BlockSpec(memory_space=pl.ANY)] * len(held),
        out_specs=(out_block, out_block, out_block),
        input_output_aliases={5 + k: k for k in range(len(held))},
        compiler_params=params(),
        cost_estimate=pl.CostEstimate(
            flops=6 * rows * depth * hidden,
            bytes_accessed=rows * depth * 4 + 6 * depth * hidden + 6 * rows * hidden,
            transcendentals=rows * hidden,
        ),
    )(normed, grads, wg, wu, wd, *held)


def inverse_rms(values):
    return lax.rsqrt(jnp.mean(values * values, axis=-1, keepdims=True) + EPS)


def neighbours():
    index, rank = lax.axis_index("ctx"), lax.axis_index("tp")
    return (index, jnp.bitwise_xor(rank, 1)), (index, jnp.bitwise_xor(rank, 2))


def remote(source, dest, send_sem, recv_sem, device):
    return pltpu.make_async_remote_copy(
        src_ref=source,
        dst_ref=dest,
        send_sem=send_sem,
        recv_sem=recv_sem,
        device_id=device,
        device_id_type=pl.DeviceIdType.MESH,
    )


def signal(sem, device):
    pl.semaphore_signal(sem, inc=1, device_id=device, device_id_type=pl.DeviceIdType.MESH)


class Scatter:
    def __init__(self, partial, groups, bufs, sems, loaded=True):
        self.partial, self.groups, self.loaded = partial, groups, loaded
        self.from_x, self.from_y, self.for_y, self.for_x, self.low, self.high = bufs[:6]
        if loaded:
            self.stay, self.stay_y, self.stay_x = bufs[6:]
        self.first_send, self.first_recv, self.second_send, self.second_recv, self.load_sem = sems
        self.to_x, self.to_y = neighbours()

    @staticmethod
    def scratch(rows, width, loaded=True):
        dma = pltpu.SemaphoreType.DMA
        whole_rows, half_rows = pltpu.VMEM((rows, width), BF), pltpu.VMEM((rows // 2, width), BF)
        bufs = [whole_rows] * 2 + [half_rows] * 4 + ([whole_rows] + [half_rows] * 2 if loaded else [])
        return bufs + [dma((8,)), dma((8,)), dma((4,)), dma((4,)), dma((6,))]

    def piece(self, g, number):
        base, rows, own = self.groups[g]
        half = rows // 2
        if not self.loaded:
            return self.partial[pl.ds(base + number * half, half), :]
        if number < 2:
            return self.stay[pl.ds(own + number * half, half), :]
        return (self.stay_x if number == 3 else self.stay_y)[pl.ds(own // 2, half), :]

    def first_copies(self, g):
        base, rows, own = self.groups[g]
        half = rows // 2
        part = lambda number: self.partial.at[pl.ds(base + number * half, half)]
        at = lambda buf, number: buf.at[pl.ds(own + number * half, half)]
        plan = [
            (part(2), at(self.from_x, 0), self.to_x),
            (part(6), at(self.from_x, 1), self.to_x),
            (part(5), at(self.from_y, 0), self.to_y),
            (part(7), at(self.from_y, 1), self.to_y),
        ]
        return [
            remote(source, dest, self.first_send.at[4 * g + k], self.first_recv.at[4 * g + k], device)
            for k, (source, dest, device) in enumerate(plan)
        ]

    def loads(self, g):
        base, rows, own = self.groups[g]
        half = rows // 2
        copy = lambda number, count, dest, k: pltpu.make_async_copy(
            self.partial.at[pl.ds(base + number * half, count)], dest, self.load_sem.at[3 * g + k]
        )
        return [
            copy(0, rows, self.stay.at[pl.ds(own, rows)], 0),
            copy(4, half, self.stay_y.at[pl.ds(own // 2, half)], 1),
            copy(3, half, self.stay_x.at[pl.ds(own // 2, half)], 2),
        ]

    def second_copies(self, g):
        _, rows, own = self.groups[g]
        at = pl.ds(own // 2, rows // 2)
        return [
            remote(self.for_y.at[at], self.low.at[at], self.second_send.at[2 * g], self.second_recv.at[2 * g], self.to_y),
            remote(
                self.for_x.at[at], self.high.at[at], self.second_send.at[2 * g + 1], self.second_recv.at[2 * g + 1], self.to_x
            ),
        ]

    def start(self, g, which=(1, 3, 0, 2), loads=True):
        copies = self.first_copies(g)
        for k in which:
            copies[k].start()
        if loads:
            for copy in self.loads(g):
                copy.start()

    def forward(self, g):
        _, rows, own = self.groups[g]
        half = rows // 2
        copies = self.first_copies(g)
        copies[1].wait_recv()
        copies[3].wait_recv()
        if self.loaded:
            for copy in self.loads(g):
                copy.wait()
        at = pl.ds(own // 2, half)
        self.for_y[at, :] = add_low(self.piece(g, 4), self.from_x[pl.ds(own + half, half), :])
        self.for_x[at, :] = add_low(self.piece(g, 3), self.from_y[pl.ds(own + half, half), :])
        for copy in self.second_copies(g):
            copy.start()

    def total(self, g, use):
        _, rows, own = self.groups[g]
        half = rows // 2
        copies, seconds = self.first_copies(g), self.second_copies(g)
        copies[0].wait_recv()
        copies[2].wait_recv()
        for copy in copies:
            copy.wait_send()
        for copy in seconds:
            copy.wait()
        first = pl.ds(own, half)
        rest = pl.ds(own // 2, half)
        for side, (got, more) in enumerate(((self.from_x, self.low), (self.from_y, self.high))):
            at = pl.ds(own + side * half, half)
            use(at, self.piece(g, side).astype(F32) + got[first, :].astype(F32) + more[rest, :].astype(F32))


class Gather:
    def __init__(self, own, out, groups, sems):
        self.own, self.out, self.groups = own, out, groups
        self.first_send, self.first_recv, self.second_send, self.second_recv, self.local_sem = sems
        self.to_x, self.to_y = neighbours()

    @staticmethod
    def scratch():
        dma = pltpu.SemaphoreType.DMA
        return [dma((4,)), dma((4,)), dma((4,)), dma((4,)), dma((2,))]

    def first_copies(self, g):
        base, rows, own = self.groups[g]
        source = self.own.at[pl.ds(own, rows)]
        place = lambda k: self.out.at[pl.ds(base + k * rows, rows)]
        return [
            remote(source, place(1), self.first_send.at[2 * g], self.first_recv.at[2 * g], self.to_x),
            remote(source, place(2), self.first_send.at[2 * g + 1], self.first_recv.at[2 * g + 1], self.to_y),
        ]

    def local(self, g):
        base, rows, own = self.groups[g]
        return pltpu.make_async_copy(self.own.at[pl.ds(own, rows)], self.out.at[pl.ds(base, rows)], self.local_sem.at[g])

    def second_copies(self, g):
        base, rows, _ = self.groups[g]
        half = rows // 2
        part = lambda number: self.out.at[pl.ds(base + number * half, half)]
        return [
            remote(part(4), part(6), self.second_send.at[2 * g], self.second_recv.at[2 * g], self.to_x),
            remote(part(3), part(7), self.second_send.at[2 * g + 1], self.second_recv.at[2 * g + 1], self.to_y),
        ]

    def start(self, g):
        for copy in self.first_copies(g):
            copy.start()
        self.local(g).start()

    def forward(self, g):
        for copy in self.first_copies(g):
            copy.wait_recv()
        for copy in self.second_copies(g):
            copy.start()
        self.local(g).wait()

    def finish(self, g):
        for copy in self.second_copies(g):
            copy.wait_recv()

    def sent(self, g):
        for copy in self.first_copies(g) + self.second_copies(g):
            copy.wait_send()


ROWS = 128
CORE_SLOTS, HOP_SLOTS = 3, 4


class Ring:
    def __init__(self, slots, send_sem, recv_sem, credit, total):
        self.slots, self.send_sem, self.recv_sem, self.credit, self.total = slots, send_sem, recv_sem, credit, total
        self.count = slots.shape[0]

    def copy(self, source, at, send_at, device):
        slot = lax.rem(at, self.count)
        return pltpu.make_async_remote_copy(
            src_ref=source,
            dst_ref=self.slots.at[slot],
            send_sem=self.send_sem.at[send_at],
            recv_sem=self.recv_sem.at[slot],
            device_id=device,
            device_id_type=pl.DeviceIdType.MESH,
        )

    def send(self, source, at, send_at, device):
        @pl.when(at >= self.count)
        def _():
            pl.semaphore_wait(self.credit, 1)

        self.copy(source, at, send_at, device).start()

    def sent(self, source, at, send_at, device):
        self.copy(source, at, send_at, device).wait_send()

    def arrived(self, source, at, send_at, device):
        self.copy(source, at, send_at, device).wait_recv()
        return self.slots.at[lax.rem(at, self.count)]

    def free(self, at, device):
        @pl.when(at + self.count < self.total)
        def _():
            pl.semaphore_signal(self.credit, inc=1, device_id=device, device_id_type=pl.DeviceIdType.MESH)


def sums_kernel(n_ctx, items, n_right, n_extra, tasks, *refs):
    n_left = len(items)
    left_refs, right_refs = refs[:n_left], refs[n_left : n_left + n_right]
    extra_in, refs = refs[n_left + n_right : n_left + n_right + n_extra[0]], refs[n_left + n_right + n_extra[0] :]
    out_refs, extra_out, refs = refs[:n_left], refs[n_left : n_left + n_extra[1]], refs[n_left + n_extra[1] :]
    extra_scratch, refs = refs[: n_extra[2]], refs[n_extra[2] :]
    (
        left_buf, right_buf, other_buf, ring, core_in, hop_in, hop_mid, hop_out, core_out,
        left_sem, right_sem, core_send, core_recv, in_send, in_recv, mid_send, mid_recv, out_send, out_recv,
        fin_send, fin_recv, store_sem, core_credit, in_credit, mid_credit, out_credit, fin_credit,
    ) = refs
    starts = [0]
    for _, _, chunks in items:
        starts.append(starts[-1] + chunks)
    total = starts[-1]
    n_ring = ring.shape[0]
    chips = n_ctx // 2
    mid = chips // 2
    index = lax.axis_index("ctx")
    rank = lax.axis_index("tp")
    core = lax.rem(index, 2)
    chip = index // 2
    low_side = chip < mid
    place = jnp.where(low_side, chip, chips - 1 - chip)
    toward = jnp.where(low_side, 1, -1)
    partner = (chip * 2 + 1 - core, rank)
    after = ((chip + toward) * 2 + core, rank)
    before = ((chip - toward) * 2 + core, rank)
    is_first = place == 0
    is_last = place == mid - 1
    lag_t = mid
    lag_u = lag_t + 2
    lag_o = lag_u + 2 * (mid - 1)
    lag_f = lag_o + 1
    lag_w = lag_f + 1

    barrier = pltpu.get_barrier_semaphore()
    pl.semaphore_signal(barrier, inc=1, device_id=partner, device_id_type=pl.DeviceIdType.MESH)

    @pl.when(chip > 0)
    def _():
        pl.semaphore_signal(
            barrier, inc=1, device_id=((chip - 1) * 2 + core, rank), device_id_type=pl.DeviceIdType.MESH
        )

    @pl.when(chip < chips - 1)
    def _():
        pl.semaphore_signal(
            barrier, inc=1, device_id=((chip + 1) * 2 + core, rank), device_id_type=pl.DeviceIdType.MESH
        )

    greeted = 1
    if tasks is not None:
        for device in neighbours():
            signal(barrier, device)
        greeted = 3
    pl.semaphore_wait(barrier, greeted + jnp.where(chip > 0, 1, 0) + jnp.where(chip < chips - 1, 1, 0))

    to_core = Ring(core_in, core_send, core_recv, core_credit, total)
    to_after = Ring(hop_in, in_send, in_recv, in_credit, total)
    across = Ring(hop_mid, mid_send, mid_recv, mid_credit, total)
    to_before = Ring(hop_out, out_send, out_recv, out_credit, total)
    to_final = Ring(core_out, fin_send, fin_recv, fin_credit, total)

    rights = [pltpu.make_async_copy(right_refs[k], right_buf.at[k], right_sem.at[k]) for k in range(n_right)]
    for copy in rights:
        copy.start()

    def for_item(at, action):
        for number in range(n_left):
            @pl.when((at >= starts[number]) & (at < starts[number + 1]))
            def _(number=number):
                action(number, at - starts[number])

    def rows_at(number, chunk, side):
        half = items[number][2] * ROWS
        return pl.multiple_of(side * half + chunk * ROWS, ROWS)

    def left_copy(number, chunk, slot, which):
        side = core if which == 0 else 1 - core
        return pltpu.make_async_copy(
            left_refs[number].at[:, pl.ds(rows_at(number, chunk, side), ROWS)],
            left_buf.at[slot, which],
            left_sem.at[slot, which],
        )

    def load_left(at):
        def action(number, chunk):
            for which in range(2):
                left_copy(number, chunk, lax.rem(at, 2), which).start()

        for_item(at, action)

    load_left(0)
    planned = tasks(extra_in, extra_out, extra_scratch) if tasks is not None else {}
    if 0 in planned:
        planned.pop(0)()
    for copy in rights:
        copy.wait()

    def step(i, carry):
        def at_lag(lag):
            at = i - lag
            return at, (at >= 0) & (at < total)

        at, now = at_lag(lag_w)

        @pl.when(now)
        def _():
            slot = lax.rem(at, n_ring)
            source = ring.at[slot]

            def action(number, chunk):
                store(number, chunk, at, 0).wait()
                store(number, chunk, at, 1).wait()

            for_item(at, action)
            to_final.sent(source, at, slot, partner)
            to_final.free(at, partner)

            @pl.when(jnp.logical_not(is_first))
            def _():
                to_before.sent(source, at, slot, before)

        at, now = at_lag(lag_o)

        @pl.when(now & jnp.logical_not(is_last))
        def _():
            slot = lax.rem(at, n_ring)
            source = ring.at[slot]
            to_after.sent(source, at, slot, after)
            got = to_before.arrived(source, at, slot, after)
            ring[slot] = got[...]
            to_before.free(at, after)

            @pl.when(jnp.logical_not(is_first))
            def _():
                to_before.send(source, at, slot, before)

        @pl.when(now)
        def _():
            slot = lax.rem(at, n_ring)
            to_final.send(ring.at[slot], at, slot, partner)

        at, now = at_lag(lag_u)

        @pl.when(now & is_last)
        def _():
            slot = lax.rem(at, n_ring)
            source = ring.at[slot]
            across.sent(source, at, slot, after)
            got = across.arrived(source, at, slot, after)
            ring[slot] = add_low(ring[slot], got[...])
            across.free(at, after)

            @pl.when(jnp.logical_not(is_first))
            def _():
                to_before.send(source, at, slot, before)

        at, now = at_lag(lag_t)

        @pl.when(now)
        def _():
            slot = lax.rem(at, n_ring)
            source = ring.at[slot]

            @pl.when(jnp.logical_not(is_first))
            def _():
                got = to_after.arrived(source, at, slot, before)
                ring[slot] = add_low(ring[slot], got[...])
                to_after.free(at, before)

            @pl.when(is_last)
            def _():
                across.send(source, at, slot, after)

            @pl.when(jnp.logical_not(is_first) & jnp.logical_not(is_last))
            def _():
                to_after.send(source, at, slot, after)

        at, now = at_lag(1)

        @pl.when(now)
        def _():
            slot = lax.rem(at, n_ring)
            source = ring.at[slot]
            own = other_buf.at[lax.rem(at, 2)]
            to_core.sent(own, at, lax.rem(at, 2), partner)
            got = to_core.arrived(own, at, lax.rem(at, 2), partner)
            ring[slot] = add_low(ring[slot], got[...])
            to_core.free(at, partner)

            @pl.when(is_first & jnp.logical_not(is_last))
            def _():
                to_after.send(source, at, slot, after)

        at, now = at_lag(lag_f)

        @pl.when(now)
        def _():
            slot = lax.rem(at, n_ring)
            to_final.arrived(ring.at[slot], at, slot, partner)

            def action(number, chunk):
                store(number, chunk, at, 0).start()
                store(number, chunk, at, 1).start()

            for_item(at, action)

        for when, task in planned.items():
            pl.when(i == when)(task)

        @pl.when(i + 1 < total)
        def _():
            load_left(i + 1)

        @pl.when(i < total)
        def _():
            slot = lax.rem(i, 2)

            def action(number, chunk):
                for which in range(2):
                    left_copy(number, chunk, slot, which).wait()
                right = right_buf.at[items[number][1]]
                other_buf[slot] = contract_rows(left_buf[slot, 1], right[...]).astype(BF)
                to_core.send(other_buf.at[slot], i, slot, partner)
                ring[lax.rem(i, n_ring)] = contract_rows(left_buf[slot, 0], right[...]).astype(BF)

            for_item(i, action)

        return carry

    def store(number, chunk, at, which):
        source = ring.at[lax.rem(at, n_ring)] if which == 0 else core_out.at[lax.rem(at, CORE_SLOTS)]
        side = core if which == 0 else 1 - core
        return pltpu.make_async_copy(
            source,
            out_refs[number].at[pl.ds(rows_at(number, chunk, side), ROWS), :],
            store_sem.at[which, lax.rem(at, 2)],
        )

    lax.fori_loop(0, total + lag_w, step, 0)


def weight_sums(items, rights, n_ctx, collective_id, extra=None):
    tokens, width = rights[0].shape
    shapes = [(k, right, left.shape[1] // 2 // ROWS) for k, (left, right) in enumerate(items)]
    mid = n_ctx // 4
    n_ring = mid + 2 + 2 * (mid - 1) + 3
    any_spec = pl.BlockSpec(memory_space=pl.ANY)
    args, arg_specs, outs, out_specs, scratch, tasks = extra if extra is not None else ([], [], [], [], [], None)
    counts = (len(args), len(outs), len(scratch))
    chunk = (ROWS, width)
    dma = pltpu.SemaphoreType.DMA
    return pl.pallas_call(
        functools.partial(sums_kernel, n_ctx, shapes, len(rights), counts, tasks),
        out_shape=[jax.ShapeDtypeStruct((left.shape[1], width), BF) for left, _ in items] + outs,
        in_specs=[any_spec] * (len(items) + len(rights)) + arg_specs,
        out_specs=[any_spec] * len(items) + out_specs,
        scratch_shapes=scratch
        + [
            pltpu.VMEM((2, 2, tokens, ROWS), BF),
            pltpu.VMEM((len(rights), tokens, width), BF),
            pltpu.VMEM((2,) + chunk, BF),
            pltpu.VMEM((n_ring,) + chunk, BF),
            pltpu.VMEM((CORE_SLOTS,) + chunk, BF),
            pltpu.VMEM((HOP_SLOTS,) + chunk, BF),
            pltpu.VMEM((HOP_SLOTS,) + chunk, BF),
            pltpu.VMEM((HOP_SLOTS,) + chunk, BF),
            pltpu.VMEM((CORE_SLOTS,) + chunk, BF),
            dma((2, 2)),
            dma((len(rights),)),
            dma((2,)),
            dma((CORE_SLOTS,)),
            dma((n_ring,)),
            dma((HOP_SLOTS,)),
            dma((n_ring,)),
            dma((HOP_SLOTS,)),
            dma((n_ring,)),
            dma((HOP_SLOTS,)),
            dma((n_ring,)),
            dma((CORE_SLOTS,)),
            dma((2, 2)),
        ]
        + [pltpu.SemaphoreType.REGULAR] * 5,
        compiler_params=pltpu.CompilerParams(
            vmem_limit_bytes=VMEM_LIMIT, collective_id=collective_id, has_side_effects=True
        ),
        cost_estimate=pl.CostEstimate(
            flops=sum(2 * left.shape[1] * tokens * width for left, _ in items),
            bytes_accessed=sum(2 * left.shape[1] * (tokens + width) for left, _ in items),
            transcendentals=0,
        ),
    )(*[left for left, _ in items], *rights, *args)


VMEM_SPEC = pl.BlockSpec(memory_space=pltpu.VMEM)
ANY_SPEC = pl.BlockSpec(memory_space=pl.ANY)


def norm_back_rows(values, gain, grad):
    inv = inverse_rms(values)
    unit = values * inv
    scaled = grad * gain
    back = (scaled - unit * jnp.mean(scaled * unit, axis=-1, keepdims=True)) * inv
    return back, jnp.sum(grad * unit, axis=0, keepdims=True)


def feed_tasks(groups, extra_in, extra_out, scratch):
    d_ref, y_ref, residual, grads, gain = extra_in
    dr, da_all, gain_grad, output = extra_out
    n = len(Scatter.scratch(16, 128))
    bufs, rest = scratch[:n], scratch[n:]
    da_own, free, gather_sems = rest[0], rest[1], rest[2:]
    first = Scatter(d_ref, groups, bufs[:9], bufs[9:])
    last = Scatter(y_ref, groups, bufs[:9], bufs[9:])
    gather = Gather(da_own, da_all, groups, gather_sems)
    order = list(reversed(range(len(groups))))

    def begin():
        gain_grad[...] = jnp.zeros_like(gain_grad)
        for g in order:
            first.start(g)

    def use(at, total):
        back, more = norm_back_rows(residual[at, :], gain[...], total)
        total_grad = grads[at, :].astype(F32) + back
        dr[at, :] = total_grad
        da_own[at, :] = total_grad.astype(BF)
        gain_grad[...] += more

    def spread(g):
        first.total(g, use)
        gather.start(g)

    def use_out(at, total):
        output[at, :] = (residual[at, :] + total).astype(BF)

    def again():
        for device in neighbours():
            signal(free, device)
        for g in order:
            gather.finish(g)
            gather.sent(g)

    def begin_out():
        pl.semaphore_wait(free, 2)
        for g in order:
            last.start(g)

    def forward_all():
        for g in order:
            last.forward(g)

    plan = {
        0: begin,
        2: lambda: first.forward(order[0]),
        4: lambda: first.forward(order[-1]),
        5: lambda: spread(order[0]),
        6: lambda: spread(order[-1]),
        8: lambda: gather.forward(order[0]),
        10: lambda: gather.forward(order[-1]),
        12: again,
        13: begin_out,
        16: forward_all,
        18: lambda: [last.total(g, use_out) for g in order] and None,
    }
    return plan


def feed_extra(groups, d_partial, y_partial, residual, grads, gain):
    rows, width = residual.shape
    outs = [
        jax.ShapeDtypeStruct((rows, width), F32),
        jax.ShapeDtypeStruct(d_partial.shape, BF),
        jax.ShapeDtypeStruct((1, width), F32),
        jax.ShapeDtypeStruct((rows, width), BF),
    ]
    scratch = (
        Scatter.scratch(rows, width)
        + [pltpu.VMEM((rows, width), BF), pltpu.SemaphoreType.REGULAR]
        + Gather.scratch()
    )
    return (
        [d_partial, y_partial, residual, grads, gain],
        [ANY_SPEC, ANY_SPEC, VMEM_SPEC, VMEM_SPEC, VMEM_SPEC],
        outs,
        [VMEM_SPEC, ANY_SPEC, VMEM_SPEC, VMEM_SPEC],
        scratch,
        functools.partial(feed_tasks, groups),
    )


def input_tasks(groups, extra_in, extra_out, scratch):
    i_ref, rows_in, dr, gain = extra_in
    input_grad, gain_grad = extra_out
    scatter = Scatter(i_ref, groups, scratch[:9], scratch[9:])
    order = list(reversed(range(len(groups))))

    def begin():
        gain_grad[...] = jnp.zeros_like(gain_grad)
        for g in order:
            scatter.start(g)

    def use(at, total):
        back, more = norm_back_rows(rows_in[at, :], gain[...], total)
        input_grad[at, :] = (dr[at, :] + back).astype(BF)
        gain_grad[...] += more

    return {
        0: begin,
        2: lambda: scatter.forward(order[0]),
        4: lambda: scatter.forward(order[-1]),
        5: lambda: scatter.total(order[0], use),
        6: lambda: scatter.total(order[-1], use),
    }


def input_extra(groups, partial, rows_in, dr, gain):
    rows, width = rows_in.shape
    outs = [jax.ShapeDtypeStruct((rows, width), BF), jax.ShapeDtypeStruct((1, width), F32)]
    return (
        [partial, rows_in, dr, gain],
        [ANY_SPEC, VMEM_SPEC, VMEM_SPEC, VMEM_SPEC],
        outs,
        [VMEM_SPEC, VMEM_SPEC],
        Scatter.scratch(rows, width),
        functools.partial(input_tasks, groups),
    )


class Exchange:
    def __init__(self, dest, sems, by_device):
        self.dest, self.by_device = dest, by_device
        self.send_sem, self.recv_sem, self.own_sem = sems
        self.n_ctx = dest.shape[1]
        self.me, self.rank = lax.axis_index("ctx"), lax.axis_index("tp")

    @staticmethod
    def scratch(units, n_ctx):
        dma = pltpu.SemaphoreType.DMA
        return [dma((units, n_ctx)), dma((units, n_ctx)), dma((units,))]

    def copy(self, source, unit, k):
        other = jnp.bitwise_xor(self.me, k)
        place = other if self.by_device else k
        return remote(
            source.at[unit, place],
            self.dest.at[unit, k],
            self.send_sem.at[unit, k],
            self.recv_sem.at[unit, k],
            (other, self.rank),
        )

    def own(self, source, unit):
        place = self.me if self.by_device else 0
        return pltpu.make_async_copy(source.at[unit, place], self.dest.at[unit, 0], self.own_sem.at[unit])

    def start(self, source, unit):
        for k in reversed(range(1, self.n_ctx)):
            self.copy(source, unit, k).start()
        self.own(source, unit).start()

    def arrived(self, source, unit):
        for k in range(1, self.n_ctx):
            self.copy(source, unit, k).wait_recv()
        self.own(source, unit).wait()

    def sent(self, source, unit):
        for k in range(1, self.n_ctx):
            self.copy(source, unit, k).wait_send()


def greet(n_ctx, tp_too):
    index, rank = lax.axis_index("ctx"), lax.axis_index("tp")
    barrier = pltpu.get_barrier_semaphore()
    for k in range(1, n_ctx):
        signal(barrier, (jnp.bitwise_xor(index, k), rank))
    if tp_too:
        for device in neighbours():
            signal(barrier, device)
    pl.semaphore_wait(barrier, n_ctx - 1 + (2 if tp_too else 0))


def in_turn(count):
    return [count - 1] + list(range(count - 1))


def attend_rows(qs, ks, vs, os, tile):
    length = qs.shape[0]
    factor = -(HD ** (-0.5)) * LOG2E
    shift = math.log(length) * LOG2E
    row_at = lax.broadcasted_iota(jnp.int32, (tile, tile), 0)
    col_at = lax.broadcasted_iota(jnp.int32, (tile, tile), 1)
    for i in range(length // tile):
        query = qs[i * tile : (i + 1) * tile, :]

        def part(j, masked):
            at = pl.ds(pl.multiple_of(j * tile, tile), tile)
            raw = times_transposed(query, ks[at, :])
            prob = 1.0 / (1.0 + jnp.exp2(raw * factor + shift))
            if masked:
                prob = jnp.where(row_at >= col_at, prob, 0.0)
            return dot(prob.astype(BF), vs[at, :])

        total = part(i, True)
        if i > 0:
            total = lax.fori_loop(0, i, lambda j, acc: acc + part(j, False), total)
        os[i * tile : (i + 1) * tile, :] = total.astype(BF)


def forward_kernel(n_ctx, groups, units, tile, *refs):
    x_ref, cot_ref, gain_one, gain_two, wq_ref, wk_ref, wv_ref, wo_ref, cos_ref, sin_ref, valid_ref = refs[:11]
    n1_out, got_out, heads_out, residual, n2_out, cot_out = refs[11:17]
    rows_buf, own_buf, send, got, o_send, o_got, qs, ks, vs, os = refs[17:27]
    rest = refs[27:]
    n_gather, n_exchange = len(Gather.scratch()), len(Exchange.scratch(1, 2))
    n1_sems, rest = rest[:n_gather], rest[n_gather:]
    n2_sems, rest = rest[:n_gather], rest[n_gather:]
    cot_sems, rest = rest[:n_gather], rest[n_gather:]
    x_sems, rest = rest[:n_exchange], rest[n_exchange:]
    o_sems, rest = rest[:n_exchange], rest[n_exchange:]
    (n1_sem, got_sem), rest = rest[:2], rest[2:]
    me, rank = lax.axis_index("ctx"), lax.axis_index("tp")
    odd = lax.rem(rank, 2)
    heads = wq_ref.shape[1] // HD
    per_unit = n_ctx // heads
    unit_rows = per_unit * PAIR

    greet(n_ctx, True)
    gather_one = Gather(own_buf, rows_buf, groups, n1_sems)
    gather_two = Gather(own_buf, n2_out, groups, n2_sems)
    gather_cot = Gather(cot_ref, cot_out, groups, cot_sems)
    scatter = Scatter(rows_buf, groups, rest[:6], rest[6:], loaded=False)
    trade = Exchange(got, x_sems, True)
    trade_back = Exchange(o_got, o_sems, False)
    order = list(reversed(range(len(groups))))
    last_u, mid_u, end_u = in_turn(len(units))

    def halves_of(u):
        return halves_at(odd if units[u][1] else 0)

    def normed(source, gain, at):
        values = source[at, :].astype(F32)
        return (values * inverse_rms(values) * gain[...]).astype(BF)

    for g in order:
        _, rows, own = groups[g]
        at = pl.ds(own, rows)
        own_buf[at, :] = normed(x_ref, gain_one, at)
        gather_one.start(g)

    def query(u, block):
        base, flipped = units[u]
        first, second = halves_of(u)
        at = pl.ds(base + block * PAIR, PAIR)
        rows = rows_buf[at, :]
        table = 1 if flipped else 0
        for which, w_ref in enumerate((wq_ref, wk_ref, wv_ref)):
            product = dot(rows, w_ref[...])
            for head in range(heads):
                part = product[:, head * HD : (head + 1) * HD]
                if which < 2:
                    part = part * cos_ref[table] + pltpu.roll(part, HD // 2, 1) * sin_ref[table]
                else:
                    part = part * valid_ref[at, :]
                part = part.astype(BF)
                send[u, block * heads + head, which, first, :] = part[:BLOCK]
                send[u, block * heads + head, which, second, :] = part[BLOCK:]

    def query_unit(u):
        for block in range(per_unit):
            query(u, block)
        trade.start(send, u)

    store_n1 = pltpu.make_async_copy(rows_buf, n1_out, n1_sem)
    store_got = [pltpu.make_async_copy(got.at[u], got_out.at[u], got_sem.at[u]) for u in range(len(units))]

    gather_one.forward(order[0])
    gather_one.finish(order[0])
    query_unit(last_u)
    gather_one.forward(order[1])
    query_unit(mid_u)
    gather_one.finish(order[1])
    for g in order:
        gather_cot.start(g)
    query_unit(end_u)
    store_n1.start()

    def attend(u):
        trade.arrived(send, u)
        store_got[u].start()
        for k in range(n_ctx):
            front, back = both_places(me, k, n_ctx)
            for which, dest in enumerate((qs, ks, vs)):
                dest[front, :] = got[u, k, which, :BLOCK, :]
                dest[back, :] = got[u, k, which, BLOCK:, :]
        attend_rows(qs, ks, vs, os, tile)
        for k in range(n_ctx):
            front, back = both_places(me, k, n_ctx)
            o_send[u, k, :BLOCK, :] = os[front, :]
            o_send[u, k, BLOCK:, :] = os[back, :]
        trade_back.start(o_send, u)

    def project(u):
        trade_back.arrived(o_send, u)
        base, _ = units[u]
        first, second = halves_of(u)
        for block in range(per_unit):
            at = pl.ds(base + block * PAIR, PAIR)
            low = valid_ref[at, :].astype(BF)
            for head in range(heads):
                place = jnp.bitwise_xor(me, block * heads + head)
                part = jnp.concatenate([o_got[u, place, first, :], o_got[u, place, second, :]], axis=0)
                heads_out[at, head * HD : (head + 1) * HD] = part * low
            rows_buf[at, :] = dot(heads_out[at, :], wo_ref[...]).astype(BF)

    def use(at, total):
        residual[at, :] = x_ref[at, :].astype(F32) + total
        own_buf[at, :] = normed(residual, gain_two, at)

    def finish_group(g):
        scatter.total(g, use)
        gather_two.start(g)

    attend(last_u)
    for g in order:
        gather_one.sent(g)
    store_n1.wait()
    project(last_u)
    scatter.start(order[0], loads=False)
    for g in order:
        gather_cot.forward(g)
    scatter.forward(order[0])
    finish_group(order[0])
    attend(mid_u)
    gather_two.forward(order[0])
    project(mid_u)
    scatter.start(order[1], (0,), loads=False)
    attend(end_u)
    project(end_u)
    scatter.start(order[1], (1, 3, 2), loads=False)
    scatter.forward(order[1])
    finish_group(order[1])
    gather_two.forward(order[1])
    for u in range(len(units)):
        trade.sent(send, u)
        trade_back.sent(o_send, u)
        store_got[u].wait()
    for g in order:
        gather_cot.finish(g)
        gather_two.finish(g)
        gather_two.sent(g)
        gather_cot.sent(g)


def forward_layer(x_own, cot_own, gain_one, gain_two, wq, wk, wv, wo, cos_tab, sin_tab, valid, n_ctx, groups, units):
    rows, depth = x_own.shape
    width = wq.shape[1]
    tokens = valid.shape[0]
    length = 2 * n_ctx * BLOCK
    n_units = len(units)
    vmem = lambda shape, dtype=BF: pltpu.VMEM(shape, dtype)
    outs = [
        jax.ShapeDtypeStruct((tokens, depth), BF),
        jax.ShapeDtypeStruct((n_units, n_ctx, 3, PAIR, HD), BF),
        jax.ShapeDtypeStruct((tokens, width), BF),
        jax.ShapeDtypeStruct((rows, depth), F32),
        jax.ShapeDtypeStruct((tokens, depth), BF),
        jax.ShapeDtypeStruct((tokens, depth), BF),
    ]
    return pl.pallas_call(
        functools.partial(forward_kernel, n_ctx, groups, units, min(512, length)),
        out_shape=outs,
        in_specs=[VMEM_SPEC, ANY_SPEC] + [VMEM_SPEC] * 9,
        out_specs=[ANY_SPEC, ANY_SPEC, VMEM_SPEC, VMEM_SPEC, ANY_SPEC, ANY_SPEC],
        scratch_shapes=[
            vmem((tokens, depth)),
            vmem((rows, depth)),
            vmem((n_units, n_ctx, 3, PAIR, HD)),
            vmem((n_units, n_ctx, 3, PAIR, HD)),
            vmem((n_units, n_ctx, PAIR, HD)),
            vmem((n_units, n_ctx, PAIR, HD)),
        ]
        + [vmem((length, HD))] * 4
        + Gather.scratch() * 3
        + Exchange.scratch(n_units, n_ctx) * 2
        + [pltpu.SemaphoreType.DMA, pltpu.SemaphoreType.DMA((n_units,))]
        + Scatter.scratch(rows, depth, loaded=False),
        compiler_params=pltpu.CompilerParams(vmem_limit_bytes=VMEM_LIMIT, collective_id=3, has_side_effects=True),
        cost_estimate=pl.CostEstimate(
            flops=8 * tokens * depth * width, bytes_accessed=8 * tokens * depth, transcendentals=0
        ),
    )(x_own, cot_own, gain_one, gain_two, wq, wk, wv, wo, cos_tab, sin_tab, valid)


def attend_rows_back(qs, ks, vs, gs, os, dqs, cos_ref, sin_ref, tile):
    length = qs.shape[0]
    scale = HD ** (-0.5)
    factor = -scale * LOG2E
    shift = math.log(length) * LOG2E
    count = length // tile
    key_at = lax.broadcasted_iota(jnp.int32, (tile, tile), 0)
    query_at = lax.broadcasted_iota(jnp.int32, (tile, tile), 1)
    dqs[...] = jnp.zeros_like(dqs)

    def unrotate(values, at):
        return (values * cos_ref[at, :] - pltpu.roll(values, HD // 2, 1) * sin_ref[at, :]).astype(BF)

    for j in range(count):
        own = slice(j * tile, (j + 1) * tile)
        keys = ks[own, :]
        values = vs[own, :]

        def part(i, masked):
            at = pl.ds(pl.multiple_of(i * tile, tile), tile)
            query = qs[at, :]
            grad = gs[at, :]
            raw = times_transposed(keys, query)
            prob = 1.0 / (1.0 + jnp.exp2(raw * factor + shift))
            if masked:
                prob = jnp.where(query_at >= key_at, prob, 0.0)
            prob_grad = times_transposed(values, grad)
            score_grad = (prob_grad * prob * (1.0 - prob)).astype(BF)
            dqs[at, :] += contract_rows(score_grad, keys)
            return dot(score_grad, query), dot(prob.astype(BF), grad)

        total = part(j, True)
        if j + 1 < count:

            def step(i, acc):
                more = part(i, False)
                return acc[0] + more[0], acc[1] + more[1]

            total = lax.fori_loop(j + 1, count, step, total)
        os[1, own, :] = unrotate(total[0] * scale, own)
        os[2, own, :] = total[1].astype(BF)
    for i in range(count):
        at = slice(i * tile, (i + 1) * tile)
        os[0, at, :] = unrotate(dqs[at, :] * scale, at)


def middle_kernel(n_ctx, units, tile, *refs):
    da_ref, got_ref, wq_ref, wk_ref, wv_ref, wo_ref, cos_ref, sin_ref, valid_ref = refs[:9]
    dq_ref, dk_ref, dv_ref, partial_out = refs[9:13]
    rows_buf, got, do_send, do_got, back_send, back_got, qs, ks, vs, gs, os, dqs = refs[13:25]
    rest = refs[25:]
    n_exchange = len(Exchange.scratch(1, 2))
    do_sems, back_sems, rest = rest[:n_exchange], rest[n_exchange : 2 * n_exchange], rest[2 * n_exchange :]
    da_sem, got_sem, out_sem = rest
    me, rank = lax.axis_index("ctx"), lax.axis_index("tp")
    odd = lax.rem(rank, 2)
    heads = wq_ref.shape[1] // HD
    per_unit = n_ctx // heads
    unit_rows = per_unit * PAIR
    count = len(units)
    order = in_turn(count)

    def rows_of(u):
        return pl.ds(units[u][0], unit_rows)

    load_da = [pltpu.make_async_copy(da_ref.at[rows_of(u)], rows_buf.at[rows_of(u)], da_sem.at[u]) for u in range(count)]
    load_got = [pltpu.make_async_copy(got_ref.at[u], got.at[u], got_sem.at[u]) for u in range(count)]
    store = [
        pltpu.make_async_copy(rows_buf.at[rows_of(u)], partial_out.at[rows_of(u)], out_sem.at[u]) for u in range(count)
    ]
    for u in order:
        load_da[u].start()
    for u in order:
        load_got[u].start()
    greet(n_ctx, False)
    trade = Exchange(do_got, do_sems, True)
    trade_back = Exchange(back_got, back_sems, False)

    for u in order:
        load_da[u].wait()
        base, flipped = units[u]
        first, second = halves_at(odd if flipped else 0)
        for block in range(per_unit):
            at = pl.ds(base + block * PAIR, PAIR)
            grad = times_transposed(rows_buf[at, :], wo_ref[...]).astype(BF)
            low = valid_ref[at, :].astype(BF)
            for head in range(heads):
                part = grad[:, head * HD : (head + 1) * HD] * low
                do_send[u, block * heads + head, first, :] = part[:BLOCK]
                do_send[u, block * heads + head, second, :] = part[BLOCK:]
        trade.start(do_send, u)
    for u in order:
        load_got[u].wait()

    def attend(turn, carry):
        u = lax.rem(turn + count - 1, count)
        trade.arrived(do_send, u)
        for k in range(n_ctx):
            front, back = both_places(me, k, n_ctx)
            for which, dest in enumerate((qs, ks, vs)):
                dest[front, :] = got[u, k, which, :BLOCK, :]
                dest[back, :] = got[u, k, which, BLOCK:, :]
            gs[front, :] = do_got[u, k, :BLOCK, :]
            gs[back, :] = do_got[u, k, BLOCK:, :]
        attend_rows_back(qs, ks, vs, gs, os, dqs, cos_ref, sin_ref, tile)
        for k in range(n_ctx):
            front, back = both_places(me, k, n_ctx)
            for which in range(3):
                back_send[u, k, which, :BLOCK, :] = os[which, front, :]
                back_send[u, k, which, BLOCK:, :] = os[which, back, :]
        trade_back.start(back_send, u)
        return carry

    lax.fori_loop(0, count, attend, 0)

    for u in order:
        trade_back.arrived(back_send, u)
        base, flipped = units[u]
        first, second = halves_at(odd if flipped else 0)
        for block in range(per_unit):
            at = pl.ds(base + block * PAIR, PAIR)
            low = valid_ref[at, :].astype(BF)
            total = None
            for which, (grad_ref, w_ref) in enumerate(((dq_ref, wq_ref), (dk_ref, wk_ref), (dv_ref, wv_ref))):
                for head in range(heads):
                    place = jnp.bitwise_xor(me, block * heads + head)
                    part = jnp.concatenate(
                        [back_got[u, place, which, first, :], back_got[u, place, which, second, :]], axis=0
                    )
                    grad_ref[at, head * HD : (head + 1) * HD] = part * low if which == 2 else part
                product = times_transposed(grad_ref[at, :], w_ref[...])
                total = product if total is None else total + product
            rows_buf[at, :] = total.astype(BF)
        store[u].start()
    for u in order:
        trade.sent(do_send, u)
        trade_back.sent(back_send, u)
        store[u].wait()


def middle_layer(da, got, wq, wk, wv, wo, cos_full, sin_full, valid, n_ctx, units):
    tokens, depth = da.shape
    width = wq.shape[1]
    length = 2 * n_ctx * BLOCK
    count = len(units)
    vmem = lambda shape, dtype=BF: pltpu.VMEM(shape, dtype)
    dma = pltpu.SemaphoreType.DMA
    three, one = (count, n_ctx, 3, PAIR, HD), (count, n_ctx, PAIR, HD)
    return pl.pallas_call(
        functools.partial(middle_kernel, n_ctx, units, min(512, length)),
        out_shape=[jax.ShapeDtypeStruct((tokens, width), BF)] * 3 + [jax.ShapeDtypeStruct((tokens, depth), BF)],
        in_specs=[ANY_SPEC, ANY_SPEC] + [VMEM_SPEC] * 7,
        out_specs=[VMEM_SPEC] * 3 + [ANY_SPEC],
        scratch_shapes=[vmem((tokens, depth)), vmem(three), vmem(one), vmem(one), vmem(three), vmem(three)]
        + [vmem((length, HD))] * 4
        + [vmem((3, length, HD)), vmem((length, HD), F32)]
        + Exchange.scratch(count, n_ctx) * 2
        + [dma((count,))] * 3,
        compiler_params=pltpu.CompilerParams(vmem_limit_bytes=VMEM_LIMIT, collective_id=4, has_side_effects=True),
        cost_estimate=pl.CostEstimate(
            flops=8 * tokens * depth * width, bytes_accessed=8 * tokens * depth, transcendentals=0
        ),
    )(da, got, wq, wk, wv, wo, cos_full, sin_full, valid)


def body(
    tokens,
    counts,
    norm_gain,
    w_query,
    w_key,
    w_value,
    w_output,
    mlp_gain,
    w_gate,
    w_up,
    w_down,
    cotangent,
):
    n_ctx = lax.axis_size("ctx")
    me = lax.axis_index("ctx")
    rank = lax.axis_index("tp")
    odd = rank & 1
    core = me & 1
    length = 2 * BLOCK * n_ctx
    heads = w_query.shape[1] // HD
    gain_one = norm_gain.astype(F32)
    gain_two = mlp_gain.astype(F32)

    inverse = THETA ** (-(jnp.arange(HD // 2, dtype=F32) * (2.0 / HD)))
    angles = jnp.arange(length, dtype=jnp.int32).astype(F32)[:, None] * inverse[None, :]
    cos_half, sin_half = jnp.cos(angles), jnp.sin(angles)
    cos_full = jnp.concatenate([cos_half, cos_half], axis=1)
    sin_full = jnp.concatenate([-sin_half, sin_half], axis=1)

    def own_blocks(table):
        front = lax.dynamic_slice_in_dim(table, me * BLOCK, BLOCK, 0)
        back = lax.dynamic_slice_in_dim(table, (2 * n_ctx - 1 - me) * BLOCK, BLOCK, 0)
        return front, back

    cos_front, cos_back = own_blocks(cos_full)
    sin_front, sin_back = own_blocks(sin_full)
    own_counts = lax.dynamic_index_in_dim(counts, me, 0, keepdims=False)
    offsets = jnp.arange(BLOCK, dtype=jnp.int32)

    def valid_of(sequence, half):
        return (offsets < own_counts[sequence, half]).astype(F32)

    cos_own = jnp.concatenate([cos_front, cos_back])
    sin_own = jnp.concatenate([sin_front, sin_back])
    sequences = counts.shape[1]
    paired = by_four() and sequences == 6 and n_ctx == 2 * heads
    if paired:
        ranks = [rank ^ k for k in range(4)]
        seq_a = [3 * (r >> 1) + 2 * (r & 1) for r in ranks]
        seq_b = [1 + 3 * (r >> 1) for r in ranks]
        valids = {
            "b": jnp.concatenate([valid_of(s, r & 1) for s, r in zip(seq_b, ranks)]),
            "a": jnp.concatenate([valid_of(s, half) for s in seq_a for half in range(2)]),
        }
        flip_back = lambda own: jnp.where(odd == 1, jnp.roll(own, BLOCK, axis=0), own)
        tables = {
            "b": (jnp.tile(flip_back(cos_own), (2, 1)), jnp.tile(flip_back(sin_own), (2, 1))),
            "a": (jnp.tile(cos_own, (4, 1)), jnp.tile(sin_own, (4, 1))),
        }
        scalars = {"b": jnp.stack([me, odd]).astype(jnp.int32), "a": jnp.stack([me, 0]).astype(jnp.int32)}
        n_pairs = {"b": 2 * heads, "a": 4 * heads}
    else:
        valids = {"a": jnp.concatenate([valid_of(s, half) for s in range(sequences) for half in range(2)])}
        tables = {"a": (jnp.tile(cos_own, (sequences, 1)), jnp.tile(sin_own, (sequences, 1)))}
        scalars = {"a": jnp.stack([me, 0]).astype(jnp.int32)}
        n_pairs = {"a": sequences * heads}
    names = tuple(n_pairs)

    def own_rows(array):
        if not paired:
            return {"a": array}
        return {
            "b": lax.dynamic_slice_in_dim(array, (1 - odd) * PAIR, BLOCK, 0),
            "a": lax.dynamic_slice_in_dim(array, odd * BLOCK, PAIR, 0),
        }

    def whole_rows(part):
        if not paired:
            return part["a"]
        return jnp.where(odd == 1, jnp.concatenate([part["b"], part["a"]]), jnp.concatenate([part["a"], part["b"]]))

    x_own = {name: rows.astype(F32) for name, rows in own_rows(tokens[0]).items()}
    g_own = own_rows(cotangent[0])

    split = by_four()
    rows_of = {name: valids[name].shape[0] for name in names}
    total_rows = sum(rows_of.values())
    first_row = {"a": 0, "b": rows_of["a"]}
    valid_head = {name: jnp.broadcast_to(valids[name][:, None], (rows_of[name], HD)) for name in names}
    valid_wide = {name: jnp.broadcast_to(valids[name][:, None].astype(BF), (rows_of[name], heads * HD)) for name in names}
    near = [k for k in range(n_ctx) if k < 6]
    far = [k for k in range(n_ctx) if k >= 6]
    state = {}

    def fence():
        names_held = list(state)
        values = lax.optimization_barrier([state[name] for name in names_held])
        state.update(zip(names_held, values))

    def only_b(step):
        if "b" in names:
            step("b")

    def norm_one(n):
        state["n1", n] = (x_own[n] * inverse_rms(x_own[n]) * gain_one).astype(BF)

    def gather_a(key):
        def step(n):
            state[key, n] = gather_first(state[key, n])

        return step

    def gather_b(key):
        def step(n):
            state[key, n] = gather_second(state[key, n])

        return step

    def query(n):
        state["n1", n] = gathered(state["n1", n])
        cos_tab, sin_tab = tables[n]
        state["qkv", n] = project_qkv(
            scalars[n], state["n1", n], w_query, w_key, w_value, cos_tab, sin_tab, valid_head[n], n_ctx
        )

    def swap_part(key, places, to):
        def step(n):
            got = dict(state.get((to, n), {}))
            got.update(exchange(state[key, n], places, n_ctx))
            state[to, n] = got
            if len(got) == n_ctx:
                state[to, n] = [got[k] for k in range(n_ctx)]
                del state[key, n]

        return step

    def attend(n):
        state["mixed", n] = attention_forward(scalars[n], state["got", n], n_ctx)

    def project(n):
        heads_out, *parts = project_out(
            scalars[n], state.pop(("back", n)), w_output, valid_wide[n], n_pairs[n], n_ctx, split
        )
        state["heads", n], state["r", n] = heads_out, tuple(parts)

    def scatter_a(key):
        def step(n):
            state[key, n] = scatter_first(state[key, n])

        return step

    def scatter_b(key):
        def step(n):
            state[key, n] = scatter_second(state[key, n])

        return step

    def norm_two(n):
        residual = x_own[n] + scattered(state.pop(("r", n)))
        state["residual", n] = residual
        state["n2", n] = (residual * inverse_rms(residual) * gain_two).astype(BF)

    def core_mlp(n):
        state["n2", n] = gathered(state["n2", n])
        state["cot", n] = gathered(state["cot", n])
        held = state.get("mlp", ())
        state["mlp"] = mlp_core(
            state["n2", n], state["cot", n], w_gate, w_up, w_down, total_rows, first_row[n], held
        )

    def attend_back(n):
        state["dqkv", n] = attention_backward(
            scalars[n], state.pop(("got", n)), state.pop(("gdo", n)), cos_full, sin_full, n_ctx
        )

    def query_back(n):
        dq, dk, dv, *parts = project_in(
            scalars[n], state.pop(("gdqkv", n)), (w_query, w_key, w_value), valid_wide[n], n_pairs[n], n_ctx, False
        )
        state["dq", n], state["dk", n], state["dv", n], state["i", n] = dq, dk, dv, parts[0]

    def joined(key):
        parts = [state[key, n] for n in ("a", "b") if n in names]
        return jnp.concatenate(parts) if len(parts) > 1 else parts[0]

    groups = tuple((first_row[n], rows_of[n] // 4, first_row[n] // 4) for n in ("a", "b") if n in names)
    in_order = [n for n in ("a", "b") if n in names]

    def own_joined(parts):
        return jnp.concatenate([parts[n] for n in in_order]) if len(in_order) > 1 else parts[in_order[0]]

    def by_group(array, scale=1):
        return {n: array[first_row[n] // scale : (first_row[n] + rows_of[n]) // scale] for n in in_order}

    own_grads, own_x = own_joined(g_own), own_joined(x_own)
    if paired:
        units = ((0, False), (2 * PAIR, False), (4 * PAIR, True))
        flat_valid = jnp.concatenate([valid_head["a"], valid_head["b"]])
        tabs = [jnp.stack([tab, flip_back(tab)]) for tab in (cos_own, sin_own)]
        all_n1, got, heads_out, own_residual, all_n2, all_cot = forward_layer(
            own_joined(own_rows(tokens[0])), own_grads, gain_one[None], gain_two[None], w_query, w_key, w_value, w_output,
            *tabs, flat_valid, n_ctx, groups, units,
        )
    else:
        norm_one("a")
        state["cot", "a"] = g_own["a"]
        gather_a("n1")("a")
        query("a")
        swap_part("qkv", range(n_ctx), "got")("a")
        attend("a")
        swap_part("mixed", range(n_ctx), "back")("a")
        project("a")
        scatter_a("r")("a")
        norm_two("a")
        gather_a("n2")("a")
        gather_a("cot")("a")
        all_n1, all_n2, all_cot = state["n1", "a"], gathered(state["n2", "a"]), gathered(state["cot", "a"])
        heads_out, own_residual = state["heads", "a"], state["residual", "a"]
    h, dgp, dup = mlp_core(all_n2, all_cot, w_gate, w_up, w_down, total_rows, 0)
    d_partial = (times_transposed(dgp, w_gate) + times_transposed(dup, w_up)).astype(BF)
    y_partial = dot(h, w_down).astype(BF)
    feed_items, feed_rights = [(h, 0), (dgp, 1), (dup, 1)], [all_cot, all_n2]
    if paired:
        extra = feed_extra(groups, d_partial, y_partial, own_residual, own_grads, gain_two[None])
        sum_down, sum_gate, sum_up, dr, da, gain_two_grad, output = weight_sums(feed_items, feed_rights, n_ctx, 1, extra)
    else:
        sum_down, sum_gate, sum_up = weight_sums(feed_items, feed_rights, n_ctx, 1)
        back, gain_two_grad = norm_back_rows(own_residual, gain_two, scattered(scatter_first((d_partial,))))
        dr = own_grads.astype(F32) + back
        da = gathered(gather_first(dr.astype(BF)))
        output = (own_residual + scattered(scatter_first((y_partial,)))).astype(BF)
    if paired:
        dq, dk, dv, i_partial = middle_layer(
            da, got, w_query, w_key, w_value, w_output, cos_full, sin_full, flat_valid, n_ctx, units
        )
    else:
        state["do", "a"] = heads_back(scalars["a"], da, w_output, valid_wide["a"], n_ctx)
        swap_part("do", range(n_ctx), "gdo")("a")
        attend_back("a")
        swap_part("dqkv", range(n_ctx), "gdqkv")("a")
        query_back("a")
        dq, dk, dv, i_partial = (state[key, "a"] for key in ("dq", "dk", "dv", "i"))
    input_items = [(heads_out, 0), (dq, 1), (dk, 1), (dv, 1)]
    if paired:
        extra = input_extra(groups, i_partial, own_x, dr, gain_one[None])
        sum_out, sum_q, sum_k, sum_v, input_grad, gain_one_grad = weight_sums(
            input_items, [da, all_n1], n_ctx, 2, extra
        )
    else:
        sum_out, sum_q, sum_k, sum_v = weight_sums(input_items, [da, all_n1], n_ctx, 2)
        back, gain_one_grad = norm_back_rows(own_x, gain_one, scattered(scatter_first((i_partial,))))
        input_grad = (dr + back).astype(BF)
    gains = jnp.concatenate([gain_one_grad, gain_two_grad])
    for axis in ("tp", "ctx"):
        size = lax.axis_size(axis)
        for bit in range(size.bit_length() - 1):
            gains = gains + lax.ppermute(gains, axis, [(i, i ^ (1 << bit)) for i in range(size)])
    return (
        whole_rows(by_group(output, 4))[None] if paired else output[None],
        whole_rows(by_group(input_grad, 4))[None] if paired else input_grad[None],
        gains[0],
        sum_q.T.astype(F32),
        sum_k.T.astype(F32),
        sum_v.T.astype(F32),
        sum_out.astype(F32),
        gains[1],
        sum_gate.T.astype(F32),
        sum_up.T.astype(F32),
        sum_down.astype(F32),
    )


def solution(mesh):
    placed = (
        P("ctx", "tp", None),
        P(),
        P(),
        P(None, "tp"),
        P(None, "tp"),
        P(None, "tp"),
        P("tp", None),
        P(),
        P(None, "tp"),
        P(None, "tp"),
        P("tp", None),
        P("ctx", "tp", None),
    )
    return jax.shard_map(
        body,
        mesh=mesh,
        in_specs=placed,
        out_specs=(
            P("ctx", "tp", None),
            P("ctx", "tp", None),
            P(),
            P(None, "tp"),
            P(None, "tp"),
            P(None, "tp"),
            P("tp", None),
            P(),
            P(None, "tp"),
            P(None, "tp"),
            P("tp", None),
        ),
        check_vma=False,
    )
```

```python
import functools
import math

import jax
import jax.numpy as jnp
from jax import lax
from jax.experimental import pallas as pl
from jax.experimental.pallas import tpu as pltpu
from jax.sharding import PartitionSpec as P

HD = 128
BLOCK = 128
PAIR = 2 * BLOCK
EPS = 1e-05
THETA = 10000.0
LOG2E = 1.4426950408889634
BF = jnp.bfloat16
F32 = jnp.float32
VMEM_LIMIT = 60 * 1024 * 1024

X_SWAP = [(i, i ^ 1) for i in range(4)]
Y_SWAP = [(i, i ^ 2) for i in range(4)]


def dot(left, right):
    return jnp.dot(left, right, preferred_element_type=F32)


def contract_rows(left, right):
    return lax.dot_general(left, right, (((0,), (0,)), ((), ())), preferred_element_type=F32)


def times_transposed(left, right):
    return lax.dot_general(left, right, (((1,), (1,)), ((), ())), preferred_element_type=F32)


def send_x(values):
    return lax.ppermute(values, "tp", X_SWAP)


def send_y(values):
    return lax.ppermute(values, "tp", Y_SWAP)


def by_four():
    return lax.axis_size("tp") == 4


def gather_first(own):
    if not by_four():
        return (lax.all_gather(own, "tp", axis=0, tiled=True),)
    return own, send_x(own), send_y(own)


def gather_second(held):
    if len(held) == 1:
        return held
    own, from_x, from_y = held
    half = own.shape[0] // 2
    return own, from_x, from_y, send_x(from_y[:half]), send_y(from_x[half:])


def gathered(held):
    return jnp.concatenate(held) if len(held) > 1 else held[0]


def scatter_parts(partial):
    if not by_four():
        return (partial,)
    rows = partial.shape[0] // 4
    half = rows // 2
    at = lambda first: partial[first * half : (first + 1) * half]
    return (
        jnp.concatenate([at(2), at(6)]),
        jnp.concatenate([at(5), at(7)]),
        jnp.concatenate([at(0), at(1), at(4), at(3)]),
    )


def scatter_first(parts):
    if len(parts) == 1:
        return (lax.psum_scatter(parts[0], "tp", scatter_dimension=0, tiled=True),)
    return send_x(parts[0]), send_y(parts[1]), parts[2]


def add_low(left, right):
    return (left.astype(F32) + right.astype(F32)).astype(BF)


def scatter_second(held):
    if len(held) == 1:
        return held
    from_x, from_y, stay = held
    half = from_x.shape[0] // 2
    low_rest = send_y(add_low(stay[2 * half : 3 * half], from_x[half:]))
    high_rest = send_x(add_low(stay[3 * half :], from_y[half:]))
    return from_x, from_y, stay, low_rest, high_rest


def scattered(held):
    if len(held) == 1:
        return held[0].astype(F32)
    from_x, from_y, stay, low_rest, high_rest = (part.astype(F32) for part in held)
    half = low_rest.shape[0]
    low = stay[:half] + from_x[:half] + low_rest
    high = stay[half : 2 * half] + from_y[:half] + high_rest
    return jnp.concatenate([low, high])


def exchange(pieces, places, n_ctx):
    got = {}
    for k in places:
        got[k] = pieces[k] if k == 0 else lax.ppermute(pieces[k], "ctx", [(i, i ^ k) for i in range(n_ctx)])
    return got


def params():
    return pltpu.CompilerParams(vmem_limit_bytes=VMEM_LIMIT)


def whole(shape):
    return pl.BlockSpec(shape, lambda *_: (0,) * len(shape))


def put_partial(refs, first, value, rows):
    if len(refs) == 1:
        refs[0][first : first + value.shape[0], :] = value
        return
    to_x, to_y, stay = refs
    half = rows // 2
    homes = {
        0: (stay, 0), 1: (stay, 1), 2: (to_x, 0), 3: (stay, 3), 4: (stay, 2), 5: (to_y, 0), 6: (to_x, 1), 7: (to_y, 1)
    }
    for part in range(value.shape[0] // half):
        ref, place = homes[first // half + part]
        ref[place * half : (place + 1) * half, :] = value[part * half : (part + 1) * half]


def partial_shapes(rows, width, split):
    if not split:
        return [jax.ShapeDtypeStruct((rows, width), BF)]
    return [jax.ShapeDtypeStruct((rows // 4, width), BF)] * 2 + [jax.ShapeDtypeStruct((rows // 2, width), BF)]


def per_device(pairs, n_ctx):
    return -(-pairs // n_ctx)


def halves_at(swap):
    first = pl.multiple_of(swap * BLOCK, BLOCK)
    second = pl.multiple_of((1 - swap) * BLOCK, BLOCK)
    return pl.ds(first, BLOCK), pl.ds(second, BLOCK)


def qkv_kernel(n_ctx, pairs, scalar_ref, n_ref, wq_ref, wk_ref, wv_ref, cos_ref, sin_ref, valid_ref, *rest):
    out_refs, buffer = rest[:n_ctx], rest[n_ctx]
    rows = n_ref[...]
    first, second = halves_at(scalar_ref[1])
    me = scalar_ref[0]
    cos_tab = cos_ref[...]
    sin_tab = sin_ref[...]
    heads = wq_ref.shape[1] // HD
    step = pl.program_id(0)
    per = out_refs[0].shape[0]
    for pair in range(pairs, per * n_ctx):
        buffer[pair] = jnp.zeros(buffer.shape[1:], BF)
    for which, w_ref in enumerate((wq_ref, wk_ref, wv_ref)):
        product = dot(rows, w_ref[...])
        for head in range(heads):
            part = product[:, head * HD : (head + 1) * HD]
            if which < 2:
                part = part * cos_tab + pltpu.roll(part, HD // 2, 1) * sin_tab
            else:
                part = part * valid_ref[...]
            part = part.astype(BF)
            buffer[step * heads + head, which, first, :] = part[:BLOCK]
            buffer[step * heads + head, which, second, :] = part[BLOCK:]

    @pl.when(step == pl.num_programs(0) - 1)
    def _():
        for k in range(n_ctx):
            source = jnp.bitwise_xor(me, k)
            for p in range(per):
                out_refs[k][p] = buffer[source * per + p]


def project_qkv(scalars, normed, wq, wk, wv, cos_tab, sin_tab, valid, n_ctx):
    rows, depth = normed.shape
    width = wq.shape[1]
    heads = width // HD
    steps = rows // PAIR
    per = per_device(steps * heads, n_ctx)
    row_block = pl.BlockSpec((PAIR, HD), lambda i, s: (i, 0))
    weight = whole((depth, width))
    piece = (per, 3, PAIR, HD)
    return pl.pallas_call(
        functools.partial(qkv_kernel, n_ctx, steps * heads),
        out_shape=[jax.ShapeDtypeStruct(piece, BF)] * n_ctx,
        grid_spec=pltpu.PrefetchScalarGridSpec(
            num_scalar_prefetch=1,
            grid=(steps,),
            in_specs=[
                pl.BlockSpec((PAIR, depth), lambda i, s: (i, 0)),
                weight,
                weight,
                weight,
                row_block,
                row_block,
                row_block,
            ],
            out_specs=[whole(piece)] * n_ctx,
            scratch_shapes=[pltpu.VMEM((per * n_ctx, 3, PAIR, HD), BF)],
        ),
        compiler_params=params(),
        cost_estimate=pl.CostEstimate(
            flops=6 * rows * depth * width, bytes_accessed=rows * depth * 2 + 6 * depth * width, transcendentals=0
        ),
    )(scalars, normed, wq, wk, wv, cos_tab, sin_tab, valid)


def out_kernel(n_ctx, pairs, scalar_ref, *refs):
    piece_refs, (w_ref, valid_ref), (heads_ref, *partial_refs), buffer = (
        refs[:n_ctx],
        refs[n_ctx : n_ctx + 2],
        refs[n_ctx + 2 : -1],
        refs[-1],
    )
    me = scalar_ref[0]
    first, second = halves_at(scalar_ref[1])
    per = piece_refs[0].shape[0]
    heads = w_ref.shape[0] // HD
    for k in range(n_ctx):
        source = jnp.bitwise_xor(me, k)
        for p in range(per):
            buffer[source * per + p] = piece_refs[k][p]
    weight = w_ref[...]
    for sequence in range(pairs // heads):
        at = slice(sequence * PAIR, (sequence + 1) * PAIR)
        rows = jnp.concatenate(
            [
                jnp.concatenate(
                    [buffer[sequence * heads + head, first, :], buffer[sequence * heads + head, second, :]], axis=0
                )
                for head in range(heads)
            ],
            axis=1,
        )
        rows = rows * valid_ref[at, :]
        heads_ref[at, :] = rows
        put_partial(partial_refs, sequence * PAIR, dot(rows, weight).astype(BF), pairs // heads * PAIR // 4)


def project_out(scalars, pieces, weight, valid, pairs, n_ctx, split):
    width, depth = weight.shape
    rows = valid.shape[0]
    per = pieces[0].shape[0]
    shapes = [jax.ShapeDtypeStruct((rows, width), BF)] + partial_shapes(rows, depth, split)
    return pl.pallas_call(
        functools.partial(out_kernel, n_ctx, pairs),
        out_shape=shapes,
        grid_spec=pltpu.PrefetchScalarGridSpec(
            num_scalar_prefetch=1,
            grid=(1,),
            in_specs=[whole(piece.shape) for piece in pieces] + [whole(weight.shape), whole(valid.shape)],
            out_specs=[whole(shape.shape) for shape in shapes],
            scratch_shapes=[pltpu.VMEM((per * n_ctx, PAIR, HD), BF)],
        ),
        compiler_params=params(),
        cost_estimate=pl.CostEstimate(
            flops=2 * rows * depth * width, bytes_accessed=rows * depth * 2 + 2 * depth * width, transcendentals=0
        ),
    )(scalars, *pieces, weight, valid)


def heads_back_kernel(n_ctx, scalar_ref, da_ref, w_ref, valid_ref, *rest):
    out_refs, buffer = rest[:n_ctx], rest[n_ctx]
    me = scalar_ref[0]
    first, second = halves_at(scalar_ref[1])
    per = out_refs[0].shape[0]
    heads = w_ref.shape[0] // HD
    weight = w_ref[...]
    for pair in range(da_ref.shape[0] // PAIR * heads, per * n_ctx):
        buffer[pair] = jnp.zeros(buffer.shape[1:], BF)
    for sequence in range(da_ref.shape[0] // PAIR):
        at = slice(sequence * PAIR, (sequence + 1) * PAIR)
        grad = times_transposed(da_ref[at, :], weight).astype(BF) * valid_ref[at, :]
        for head in range(heads):
            part = grad[:, head * HD : (head + 1) * HD]
            buffer[sequence * heads + head, first, :] = part[:BLOCK]
            buffer[sequence * heads + head, second, :] = part[BLOCK:]
    for k in range(n_ctx):
        source = jnp.bitwise_xor(me, k)
        for p in range(per):
            out_refs[k][p] = buffer[source * per + p]


def heads_back(scalars, da, weight, valid, n_ctx):
    rows, depth = da.shape
    width = weight.shape[0]
    per = per_device(rows // PAIR * (width // HD), n_ctx)
    piece = (per, PAIR, HD)
    return pl.pallas_call(
        functools.partial(heads_back_kernel, n_ctx),
        out_shape=[jax.ShapeDtypeStruct(piece, BF)] * n_ctx,
        grid_spec=pltpu.PrefetchScalarGridSpec(
            num_scalar_prefetch=1,
            grid=(1,),
            in_specs=[whole(da.shape), whole(weight.shape), whole(valid.shape)],
            out_specs=[whole(piece)] * n_ctx,
            scratch_shapes=[pltpu.VMEM((per * n_ctx, PAIR, HD), BF)],
        ),
        compiler_params=params(),
        cost_estimate=pl.CostEstimate(
            flops=2 * rows * depth * width, bytes_accessed=rows * depth * 2 + 2 * depth * width, transcendentals=0
        ),
    )(scalars, da, weight, valid)


def in_kernel(n_ctx, pairs, scalar_ref, *refs):
    piece_refs, weight_refs, valid_ref = refs[:n_ctx], refs[n_ctx : n_ctx + 3], refs[n_ctx + 3]
    grad_refs, partial_refs, buffer = refs[n_ctx + 4 : n_ctx + 7], refs[n_ctx + 7 : -1], refs[-1]
    me = scalar_ref[0]
    first, second = halves_at(scalar_ref[1])
    per = piece_refs[0].shape[0]
    heads = weight_refs[0].shape[1] // HD
    for k in range(n_ctx):
        source = jnp.bitwise_xor(me, k)
        for p in range(per):
            buffer[source * per + p] = piece_refs[k][p]
    for sequence in range(pairs // heads):
        at = slice(sequence * PAIR, (sequence + 1) * PAIR)
        total = None
        for which in range(3):
            rows = jnp.concatenate(
                [
                    jnp.concatenate([buffer[pair, which, first, :], buffer[pair, which, second, :]], axis=0)
                    for pair in range(sequence * heads, (sequence + 1) * heads)
                ],
                axis=1,
            )
            if which == 2:
                rows = rows * valid_ref[at, :]
            grad_refs[which][at, :] = rows
            product = times_transposed(rows, weight_refs[which][...])
            total = product if total is None else total + product
        put_partial(partial_refs, sequence * PAIR, total.astype(BF), pairs // heads * PAIR // 4)


def project_in(scalars, pieces, weights, valid, pairs, n_ctx, split):
    depth, width = weights[0].shape
    rows = valid.shape[0]
    per = pieces[0].shape[0]
    shapes = [jax.ShapeDtypeStruct((rows, width), BF)] * 3 + partial_shapes(rows, depth, split)
    return pl.pallas_call(
        functools.partial(in_kernel, n_ctx, pairs),
        out_shape=shapes,
        grid_spec=pltpu.PrefetchScalarGridSpec(
            num_scalar_prefetch=1,
            grid=(1,),
            in_specs=[whole(piece.shape) for piece in pieces]
            + [whole(weight.shape) for weight in weights]
            + [whole(valid.shape)],
            out_specs=[whole(shape.shape) for shape in shapes],
            scratch_shapes=[pltpu.VMEM((per * n_ctx, 3, PAIR, HD), BF)],
        ),
        compiler_params=params(),
        cost_estimate=pl.CostEstimate(
            flops=6 * rows * depth * width, bytes_accessed=rows * depth * 2 + 6 * depth * width, transcendentals=0
        ),
    )(scalars, *pieces, *weights, valid)


def both_places(me, k, n_ctx):
    source = jnp.bitwise_xor(me, k)
    front = pl.multiple_of(source * BLOCK, BLOCK)
    back = pl.multiple_of((2 * n_ctx - 1 - source) * BLOCK, BLOCK)
    return pl.ds(front, BLOCK), pl.ds(back, BLOCK)


def attention_kernel(n_ctx, tile, scalar_ref, *refs):
    x_refs, o_refs, (qs, ks, vs, os) = refs[:n_ctx], refs[n_ctx : 2 * n_ctx], refs[2 * n_ctx :]
    me = scalar_ref[0]
    length = 2 * n_ctx * BLOCK
    for k in range(n_ctx):
        front, back = both_places(me, k, n_ctx)
        for which, dest in enumerate((qs, ks, vs)):
            dest[front, :] = x_refs[k][0, which, :BLOCK, :]
            dest[back, :] = x_refs[k][0, which, BLOCK:, :]
    factor = -(HD ** (-0.5)) * LOG2E
    shift = math.log(length) * LOG2E
    row_at = lax.broadcasted_iota(jnp.int32, (tile, tile), 0)
    col_at = lax.broadcasted_iota(jnp.int32, (tile, tile), 1)
    for i in range(length // tile):
        query = qs[i * tile : (i + 1) * tile, :]

        def part(j, masked):
            at = pl.ds(pl.multiple_of(j * tile, tile), tile)
            raw = times_transposed(query, ks[at, :])
            prob = 1.0 / (1.0 + jnp.exp2(raw * factor + shift))
            if masked:
                prob = jnp.where(row_at >= col_at, prob, 0.0)
            return dot(prob.astype(BF), vs[at, :])

        total = part(i, True)
        if i > 0:
            total = lax.fori_loop(0, i, lambda j, acc: acc + part(j, False), total)
        os[i * tile : (i + 1) * tile, :] = total.astype(BF)
    for k in range(n_ctx):
        front, back = both_places(me, k, n_ctx)
        o_refs[k][0, :BLOCK, :] = os[front, :]
        o_refs[k][0, BLOCK:, :] = os[back, :]


def attention_forward(scalars, pieces, n_ctx):
    pairs = pieces[0].shape[0]
    length = 2 * n_ctx * BLOCK
    tile = min(512, length)
    return pl.pallas_call(
        functools.partial(attention_kernel, n_ctx, tile),
        out_shape=[jax.ShapeDtypeStruct((pairs, PAIR, HD), BF)] * n_ctx,
        grid_spec=pltpu.PrefetchScalarGridSpec(
            num_scalar_prefetch=1,
            grid=(pairs,),
            in_specs=[pl.BlockSpec((1, 3, PAIR, HD), lambda i, s: (i, 0, 0, 0))] * n_ctx,
            out_specs=[pl.BlockSpec((1, PAIR, HD), lambda i, s: (i, 0, 0))] * n_ctx,
            scratch_shapes=[pltpu.VMEM((length, HD), BF)] * 4,
        ),
        compiler_params=params(),
        cost_estimate=pl.CostEstimate(
            flops=pairs * length * length * HD * 6,
            bytes_accessed=pairs * length * HD * 8,
            transcendentals=pairs * length * length,
        ),
    )(scalars, *pieces)


def attention_back_kernel(n_ctx, tile, scalar_ref, *refs):
    x_refs, g_refs, (cos_ref, sin_ref) = refs[:n_ctx], refs[n_ctx : 2 * n_ctx], refs[2 * n_ctx : 2 * n_ctx + 2]
    out_refs = refs[2 * n_ctx + 2 : 3 * n_ctx + 2]
    qs, ks, vs, gs, os, dqs = refs[3 * n_ctx + 2 :]
    me = scalar_ref[0]
    length = 2 * n_ctx * BLOCK
    for k in range(n_ctx):
        front, back = both_places(me, k, n_ctx)
        for which, dest in enumerate((qs, ks, vs)):
            dest[front, :] = x_refs[k][0, which, :BLOCK, :]
            dest[back, :] = x_refs[k][0, which, BLOCK:, :]
        gs[front, :] = g_refs[k][0, :BLOCK, :]
        gs[back, :] = g_refs[k][0, BLOCK:, :]
    scale = HD ** (-0.5)
    factor = -scale * LOG2E
    shift = math.log(length) * LOG2E
    count = length // tile
    key_at = lax.broadcasted_iota(jnp.int32, (tile, tile), 0)
    query_at = lax.broadcasted_iota(jnp.int32, (tile, tile), 1)
    dqs[...] = jnp.zeros_like(dqs)

    def unrotate(values, at):
        return (values * cos_ref[at, :] - pltpu.roll(values, HD // 2, 1) * sin_ref[at, :]).astype(BF)

    for j in range(count):
        own = slice(j * tile, (j + 1) * tile)
        keys = ks[own, :]
        values = vs[own, :]

        def part(i, masked):
            at = pl.ds(pl.multiple_of(i * tile, tile), tile)
            query = qs[at, :]
            grad = gs[at, :]
            raw = times_transposed(keys, query)
            prob = 1.0 / (1.0 + jnp.exp2(raw * factor + shift))
            if masked:
                prob = jnp.where(query_at >= key_at, prob, 0.0)
            prob_grad = times_transposed(values, grad)
            score_grad = (prob_grad * prob * (1.0 - prob)).astype(BF)
            dqs[at, :] += contract_rows(score_grad, keys)
            return dot(score_grad, query), dot(prob.astype(BF), grad)

        total = part(j, True)
        if j + 1 < count:

            def step(i, acc):
                more = part(i, False)
                return acc[0] + more[0], acc[1] + more[1]

            total = lax.fori_loop(j + 1, count, step, total)
        os[1, own, :] = unrotate(total[0] * scale, own)
        os[2, own, :] = total[1].astype(BF)
    for i in range(count):
        at = slice(i * tile, (i + 1) * tile)
        os[0, at, :] = unrotate(dqs[at, :] * scale, at)
    for k in range(n_ctx):
        front, back = both_places(me, k, n_ctx)
        for which in range(3):
            out_refs[k][0, which, :BLOCK, :] = os[which, front, :]
            out_refs[k][0, which, BLOCK:, :] = os[which, back, :]


def attention_backward(scalars, pieces, grads, cos_tab, sin_tab, n_ctx):
    pairs = pieces[0].shape[0]
    length = 2 * n_ctx * BLOCK
    tile = min(512, length)
    three = pl.BlockSpec((1, 3, PAIR, HD), lambda i, s: (i, 0, 0, 0))
    one = pl.BlockSpec((1, PAIR, HD), lambda i, s: (i, 0, 0))
    return pl.pallas_call(
        functools.partial(attention_back_kernel, n_ctx, tile),
        out_shape=[jax.ShapeDtypeStruct((pairs, 3, PAIR, HD), BF)] * n_ctx,
        grid_spec=pltpu.PrefetchScalarGridSpec(
            num_scalar_prefetch=1,
            grid=(pairs,),
            in_specs=[three] * n_ctx + [one] * n_ctx + [whole((length, HD))] * 2,
            out_specs=[three] * n_ctx,
            scratch_shapes=[pltpu.VMEM((length, HD), BF)] * 4
            + [pltpu.VMEM((3, length, HD), BF), pltpu.VMEM((length, HD), F32)],
        ),
        compiler_params=params(),
        cost_estimate=pl.CostEstimate(
            flops=pairs * length * length * HD * 12,
            bytes_accessed=pairs * length * HD * 14,
            transcendentals=pairs * length * length,
        ),
    )(scalars, *pieces, *grads, cos_tab, sin_tab)


def mlp_kernel(n_ref, g_ref, wg_ref, wu_ref, wd_ref, *rest):
    h_ref, dgp_ref, dup_ref = rest[-3:]
    rows = n_ref[...]
    gate_pre = dot(rows, wg_ref[...])
    up_pre = dot(rows, wu_ref[...])
    hidden_grad = times_transposed(g_ref[...], wd_ref[...])
    gate_sig = 1.0 / (1.0 + jnp.exp2(gate_pre * (-LOG2E)))
    gate_act = gate_pre * gate_sig
    h_ref[...] = (gate_act * up_pre).astype(BF)
    dup_ref[...] = (hidden_grad * gate_act).astype(BF)
    dgp_ref[...] = (hidden_grad * up_pre * (gate_sig * (1.0 + gate_pre * (1.0 - gate_sig)))).astype(BF)


def mlp_core(normed, grads, wg, wu, wd, total, first, held=()):
    rows, depth = normed.shape
    hidden = wg.shape[1]
    row_tile, tile = 512, 512
    skip = first // row_tile
    row_block = pl.BlockSpec((row_tile, depth), lambda j, i: (i, 0))
    out_block = pl.BlockSpec((row_tile, tile), lambda j, i: (i + skip, j))
    out = jax.ShapeDtypeStruct((total, hidden), BF)
    return pl.pallas_call(
        mlp_kernel,
        out_shape=(out, out, out),
        grid=(hidden // tile, rows // row_tile),
        in_specs=[
            row_block,
            row_block,
            pl.BlockSpec((depth, tile), lambda j, i: (0, j)),
            pl.BlockSpec((depth, tile), lambda j, i: (0, j)),
            pl.BlockSpec((tile, depth), lambda j, i: (j, 0)),
        ]
        + [pl.BlockSpec(memory_space=pl.ANY)] * len(held),
        out_specs=(out_block, out_block, out_block),
        input_output_aliases={5 + k: k for k in range(len(held))},
        compiler_params=params(),
        cost_estimate=pl.CostEstimate(
            flops=6 * rows * depth * hidden,
            bytes_accessed=rows * depth * 4 + 6 * depth * hidden + 6 * rows * hidden,
            transcendentals=rows * hidden,
        ),
    )(normed, grads, wg, wu, wd, *held)


def inverse_rms(values):
    return lax.rsqrt(jnp.mean(values * values, axis=-1, keepdims=True) + EPS)


def neighbours():
    index, rank = lax.axis_index("ctx"), lax.axis_index("tp")
    return (index, jnp.bitwise_xor(rank, 1)), (index, jnp.bitwise_xor(rank, 2))


def remote(source, dest, send_sem, recv_sem, device):
    return pltpu.make_async_remote_copy(
        src_ref=source,
        dst_ref=dest,
        send_sem=send_sem,
        recv_sem=recv_sem,
        device_id=device,
        device_id_type=pl.DeviceIdType.MESH,
    )


def signal(sem, device):
    pl.semaphore_signal(sem, inc=1, device_id=device, device_id_type=pl.DeviceIdType.MESH)


class Scatter:
    def __init__(self, partial, groups, bufs, sems, loaded=True):
        self.partial, self.groups, self.loaded = partial, groups, loaded
        self.from_x, self.from_y, self.for_y, self.for_x, self.low, self.high = bufs[:6]
        if loaded:
            self.stay, self.stay_y, self.stay_x = bufs[6:]
        self.first_send, self.first_recv, self.second_send, self.second_recv, self.load_sem = sems
        self.to_x, self.to_y = neighbours()

    @staticmethod
    def scratch(rows, width, loaded=True):
        dma = pltpu.SemaphoreType.DMA
        whole_rows, half_rows = pltpu.VMEM((rows, width), BF), pltpu.VMEM((rows // 2, width), BF)
        bufs = [whole_rows] * 2 + [half_rows] * 4 + ([whole_rows] + [half_rows] * 2 if loaded else [])
        return bufs + [dma((8,)), dma((8,)), dma((4,)), dma((4,)), dma((6,))]

    def piece(self, g, number):
        base, rows, own = self.groups[g]
        half = rows // 2
        if not self.loaded:
            return self.partial[pl.ds(base + number * half, half), :]
        if number < 2:
            return self.stay[pl.ds(own + number * half, half), :]
        return (self.stay_x if number == 3 else self.stay_y)[pl.ds(own // 2, half), :]

    def first_copies(self, g):
        base, rows, own = self.groups[g]
        half = rows // 2
        part = lambda number: self.partial.at[pl.ds(base + number * half, half)]
        at = lambda buf, number: buf.at[pl.ds(own + number * half, half)]
        plan = [
            (part(2), at(self.from_x, 0), self.to_x),
            (part(6), at(self.from_x, 1), self.to_x),
            (part(5), at(self.from_y, 0), self.to_y),
            (part(7), at(self.from_y, 1), self.to_y),
        ]
        return [
            remote(source, dest, self.first_send.at[4 * g + k], self.first_recv.at[4 * g + k], device)
            for k, (source, dest, device) in enumerate(plan)
        ]

    def loads(self, g):
        base, rows, own = self.groups[g]
        half = rows // 2
        copy = lambda number, count, dest, k: pltpu.make_async_copy(
            self.partial.at[pl.ds(base + number * half, count)], dest, self.load_sem.at[3 * g + k]
        )
        return [
            copy(0, rows, self.stay.at[pl.ds(own, rows)], 0),
            copy(4, half, self.stay_y.at[pl.ds(own // 2, half)], 1),
            copy(3, half, self.stay_x.at[pl.ds(own // 2, half)], 2),
        ]

    def second_copies(self, g):
        _, rows, own = self.groups[g]
        at = pl.ds(own // 2, rows // 2)
        return [
            remote(self.for_y.at[at], self.low.at[at], self.second_send.at[2 * g], self.second_recv.at[2 * g], self.to_y),
            remote(
                self.for_x.at[at], self.high.at[at], self.second_send.at[2 * g + 1], self.second_recv.at[2 * g + 1], self.to_x
            ),
        ]

    def start(self, g, which=(1, 3, 0, 2), loads=True):
        copies = self.first_copies(g)
        for k in which:
            copies[k].start()
        if loads:
            for copy in self.loads(g):
                copy.start()

    def forward(self, g):
        _, rows, own = self.groups[g]
        half = rows // 2
        copies = self.first_copies(g)
        copies[1].wait_recv()
        copies[3].wait_recv()
        if self.loaded:
            for copy in self.loads(g):
                copy.wait()
        at = pl.ds(own // 2, half)
        self.for_y[at, :] = add_low(self.piece(g, 4), self.from_x[pl.ds(own + half, half), :])
        self.for_x[at, :] = add_low(self.piece(g, 3), self.from_y[pl.ds(own + half, half), :])
        for copy in self.second_copies(g):
            copy.start()

    def total(self, g, use):
        _, rows, own = self.groups[g]
        half = rows // 2
        copies, seconds = self.first_copies(g), self.second_copies(g)
        copies[0].wait_recv()
        copies[2].wait_recv()
        for copy in copies:
            copy.wait_send()
        for copy in seconds:
            copy.wait()
        first = pl.ds(own, half)
        rest = pl.ds(own // 2, half)
        for side, (got, more) in enumerate(((self.from_x, self.low), (self.from_y, self.high))):
            at = pl.ds(own + side * half, half)
            use(at, self.piece(g, side).astype(F32) + got[first, :].astype(F32) + more[rest, :].astype(F32))


class Gather:
    def __init__(self, own, out, groups, sems):
        self.own, self.out, self.groups = own, out, groups
        self.first_send, self.first_recv, self.second_send, self.second_recv, self.local_sem = sems
        self.to_x, self.to_y = neighbours()

    @staticmethod
    def scratch():
        dma = pltpu.SemaphoreType.DMA
        return [dma((4,)), dma((4,)), dma((4,)), dma((4,)), dma((2,))]

    def first_copies(self, g):
        base, rows, own = self.groups[g]
        source = self.own.at[pl.ds(own, rows)]
        place = lambda k: self.out.at[pl.ds(base + k * rows, rows)]
        return [
            remote(source, place(1), self.first_send.at[2 * g], self.first_recv.at[2 * g], self.to_x),
            remote(source, place(2), self.first_send.at[2 * g + 1], self.first_recv.at[2 * g + 1], self.to_y),
        ]

    def local(self, g):
        base, rows, own = self.groups[g]
        return pltpu.make_async_copy(self.own.at[pl.ds(own, rows)], self.out.at[pl.ds(base, rows)], self.local_sem.at[g])

    def second_copies(self, g):
        base, rows, _ = self.groups[g]
        half = rows // 2
        part = lambda number: self.out.at[pl.ds(base + number * half, half)]
        return [
            remote(part(4), part(6), self.second_send.at[2 * g], self.second_recv.at[2 * g], self.to_x),
            remote(part(3), part(7), self.second_send.at[2 * g + 1], self.second_recv.at[2 * g + 1], self.to_y),
        ]

    def start(self, g):
        for copy in self.first_copies(g):
            copy.start()
        self.local(g).start()

    def forward(self, g):
        for copy in self.first_copies(g):
            copy.wait_recv()
        for copy in self.second_copies(g):
            copy.start()
        self.local(g).wait()

    def finish(self, g):
        for copy in self.second_copies(g):
            copy.wait_recv()

    def sent(self, g):
        for copy in self.first_copies(g) + self.second_copies(g):
            copy.wait_send()


TILE, ROWS = 128, 64
CORE_SLOTS, HOP_SLOTS = 4, 4


class Ring:
    def __init__(self, slots, send_sem, recv_sem, credit, total):
        self.slots, self.send_sem, self.recv_sem, self.credit, self.total = slots, send_sem, recv_sem, credit, total
        self.count = slots.shape[0]

    def copy(self, source, at, send_at, device):
        slot = lax.rem(at, self.count)
        return pltpu.make_async_remote_copy(
            src_ref=source,
            dst_ref=self.slots.at[slot],
            send_sem=self.send_sem.at[send_at],
            recv_sem=self.recv_sem.at[slot],
            device_id=device,
            device_id_type=pl.DeviceIdType.MESH,
        )

    def send(self, source, at, send_at, device):
        @pl.when(at >= self.count)
        def _():
            pl.semaphore_wait(self.credit, 1)

        self.copy(source, at, send_at, device).start()

    def sent(self, source, at, send_at, device):
        self.copy(source, at, send_at, device).wait_send()

    def arrived(self, source, at, send_at, device):
        self.copy(source, at, send_at, device).wait_recv()
        return self.slots.at[lax.rem(at, self.count)]

    def free(self, at, device):
        @pl.when(at + self.count < self.total)
        def _():
            pl.semaphore_signal(self.credit, inc=1, device_id=device, device_id_type=pl.DeviceIdType.MESH)


def sums_kernel(n_ctx, items, n_right, n_extra, tasks, late, *refs):
    n_left = len(items)
    left_refs, right_refs = refs[:n_left], refs[n_left : n_left + n_right]
    extra_in, refs = refs[n_left + n_right : n_left + n_right + n_extra[0]], refs[n_left + n_right + n_extra[0] :]
    out_refs, extra_out, refs = refs[:n_left], refs[n_left : n_left + n_extra[1]], refs[n_left + n_extra[1] :]
    extra_scratch, refs = refs[: n_extra[2]], refs[n_extra[2] :]
    right_refs = list(right_refs) + [extra_out[k] for k in late]
    n_right += len(late)
    (
        left_buf, right_buf, other_buf, ring, core_in, hop_in, hop_mid, hop_out, core_out,
        left_sem, right_sem, core_send, core_recv, in_send, in_recv, mid_send, mid_recv, out_send, out_recv,
        fin_send, fin_recv, store_sem, core_credit, in_credit, mid_credit, out_credit, fin_credit,
    ) = refs
    starts = [0]
    for _, _, chunks in items:
        starts.append(starts[-1] + chunks)
    total = starts[-1]
    n_ring = ring.shape[0]
    chips = n_ctx // 2
    mid = chips // 2
    index = lax.axis_index("ctx")
    rank = lax.axis_index("tp")
    core = lax.rem(index, 2)
    chip = index // 2
    low_side = chip < mid
    place = jnp.where(low_side, chip, chips - 1 - chip)
    toward = jnp.where(low_side, 1, -1)
    partner = (chip * 2 + 1 - core, rank)
    after = ((chip + toward) * 2 + core, rank)
    before = ((chip - toward) * 2 + core, rank)
    is_first = place == 0
    is_last = place == mid - 1
    lag_t = mid
    lag_u = lag_t + 2
    lag_o = lag_u + 2 * (mid - 1)
    lag_f = lag_o + 1
    lag_w = lag_f + 1

    barrier = pltpu.get_barrier_semaphore()
    pl.semaphore_signal(barrier, inc=1, device_id=partner, device_id_type=pl.DeviceIdType.MESH)

    @pl.when(chip > 0)
    def _():
        pl.semaphore_signal(
            barrier, inc=1, device_id=((chip - 1) * 2 + core, rank), device_id_type=pl.DeviceIdType.MESH
        )

    @pl.when(chip < chips - 1)
    def _():
        pl.semaphore_signal(
            barrier, inc=1, device_id=((chip + 1) * 2 + core, rank), device_id_type=pl.DeviceIdType.MESH
        )

    greeted = 1
    if tasks is not None:
        for device in neighbours():
            signal(barrier, device)
        greeted = 3
    pl.semaphore_wait(barrier, greeted + jnp.where(chip > 0, 1, 0) + jnp.where(chip < chips - 1, 1, 0))

    to_core = Ring(core_in, core_send, core_recv, core_credit, total)
    to_after = Ring(hop_in, in_send, in_recv, in_credit, total)
    across = Ring(hop_mid, mid_send, mid_recv, mid_credit, total)
    to_before = Ring(hop_out, out_send, out_recv, out_credit, total)
    to_final = Ring(core_out, fin_send, fin_recv, fin_credit, total)

    def right_copy(k):
        return pltpu.make_async_copy(right_refs[k], right_buf.at[k % 2], right_sem.at[k % 2])

    right_copy(0).start()

    def for_item(at, action):
        for number in range(n_left):
            @pl.when((at >= starts[number]) & (at < starts[number + 1]))
            def _(number=number):
                action(number, at - starts[number])

    def rows_at(number, chunk, side):
        half = items[number][2] * ROWS
        return pl.multiple_of(side * half + chunk * ROWS, ROWS)

    def left_copy(number, chunk, slot, which):
        side = core if which == 0 else 1 - core
        half = items[number][2] * ROWS
        return pltpu.make_async_copy(
            left_refs[number].at[:, pl.ds(pl.multiple_of(side * half + chunk // 2 * TILE, TILE), TILE)],
            left_buf.at[slot, which],
            left_sem.at[slot, which],
        )

    def load_left(at):
        def action(number, chunk):
            for which in range(2):
                left_copy(number, chunk, lax.rem(at // 2, 2), which).start()

        for_item(at, action)

    load_left(0)
    planned, each = tasks(extra_in, extra_out, extra_scratch) if tasks is not None else ({}, None)
    if 0 in planned:
        planned.pop(0)()
    if n_right > 1:
        right_copy(1).start()
    right_copy(0).wait()

    def step(i, carry):
        def at_lag(lag):
            at = i - lag
            return at, (at >= 0) & (at < total)

        at, now = at_lag(lag_w)

        @pl.when(now)
        def _():
            slot = lax.rem(at, n_ring)
            source = ring.at[slot]

            def action(number, chunk):
                store(number, chunk, at, 0).wait()
                store(number, chunk, at, 1).wait()

            for_item(at, action)
            to_final.sent(source, at, slot, partner)
            to_final.free(at, partner)

            @pl.when(jnp.logical_not(is_first))
            def _():
                to_before.sent(source, at, slot, before)

        at, now = at_lag(lag_o)

        @pl.when(now & jnp.logical_not(is_last))
        def _():
            slot = lax.rem(at, n_ring)
            source = ring.at[slot]
            to_after.sent(source, at, slot, after)
            got = to_before.arrived(source, at, slot, after)
            ring[slot] = got[...]
            to_before.free(at, after)

            @pl.when(jnp.logical_not(is_first))
            def _():
                to_before.send(source, at, slot, before)

        @pl.when(now)
        def _():
            slot = lax.rem(at, n_ring)
            to_final.send(ring.at[slot], at, slot, partner)

        at, now = at_lag(lag_u)

        @pl.when(now & is_last)
        def _():
            slot = lax.rem(at, n_ring)
            source = ring.at[slot]
            across.sent(source, at, slot, after)
            got = across.arrived(source, at, slot, after)
            ring[slot] = add_low(ring[slot], got[...])
            across.free(at, after)

            @pl.when(jnp.logical_not(is_first))
            def _():
                to_before.send(source, at, slot, before)

        at, now = at_lag(lag_t)

        @pl.when(now)
        def _():
            slot = lax.rem(at, n_ring)
            source = ring.at[slot]

            @pl.when(jnp.logical_not(is_first))
            def _():
                got = to_after.arrived(source, at, slot, before)
                ring[slot] = add_low(ring[slot], got[...])
                to_after.free(at, before)

            @pl.when(is_last)
            def _():
                across.send(source, at, slot, after)

            @pl.when(jnp.logical_not(is_first) & jnp.logical_not(is_last))
            def _():
                to_after.send(source, at, slot, after)

        at, now = at_lag(1)

        @pl.when(now)
        def _():
            slot = lax.rem(at, n_ring)
            source = ring.at[slot]
            own = other_buf.at[lax.rem(at, 4)]
            to_core.sent(own, at, lax.rem(at, 4), partner)
            got = to_core.arrived(own, at, lax.rem(at, 4), partner)
            ring[slot] = add_low(ring[slot], got[...])
            to_core.free(at, partner)

            @pl.when(is_first & jnp.logical_not(is_last))
            def _():
                to_after.send(source, at, slot, after)

        at, now = at_lag(lag_f)

        @pl.when(now)
        def _():
            slot = lax.rem(at, n_ring)
            to_final.arrived(ring.at[slot], at, slot, partner)

            def action(number, chunk):
                store(number, chunk, at, 0).start()
                store(number, chunk, at, 1).start()

            for_item(at, action)

        for when, task in planned.items():
            pl.when(i == when)(task)

        if each is not None:
            each(i)

        @pl.when((i + 2 < total) & (lax.rem(i, 2) == 0))
        def _():
            load_left(i + 2)

        @pl.when((i < total) & (lax.rem(i, 2) == 0))
        def _():
            slot = lax.rem(i // 2, 2)

            def action(number, chunk):
                which_right = items[number][1]
                if which_right > 0 and items[number - 1][1] != which_right:

                    @pl.when(chunk == 0)
                    def _():
                        right_copy(which_right).wait()

                if which_right > 0 and which_right + 1 < n_right:

                    @pl.when(chunk == items[number][2] // 2)
                    def _():
                        right_copy(which_right + 1).start()

                for which in range(2):
                    left_copy(number, chunk, slot, which).wait()
                right = right_buf.at[which_right % 2]
                product = contract_rows(left_buf[slot, 1], right[...]).astype(BF)
                for part in range(2):
                    place = lax.rem(i + part, 4)
                    other_buf[place] = product[part * ROWS : (part + 1) * ROWS]
                    to_core.send(other_buf.at[place], i + part, place, partner)
                product = contract_rows(left_buf[slot, 0], right[...]).astype(BF)
                for part in range(2):
                    ring[lax.rem(i + part, n_ring)] = product[part * ROWS : (part + 1) * ROWS]

            for_item(i, action)

        return carry

    def store(number, chunk, at, which):
        source = ring.at[lax.rem(at, n_ring)] if which == 0 else core_out.at[lax.rem(at, CORE_SLOTS)]
        side = core if which == 0 else 1 - core
        return pltpu.make_async_copy(
            source,
            out_refs[number].at[pl.ds(rows_at(number, chunk, side), ROWS), :],
            store_sem.at[which, lax.rem(at, 2)],
        )

    lax.fori_loop(0, total + lag_w, step, 0)


def weight_sums(items, rights, n_ctx, collective_id, extra=None, late=()):
    tokens, width = rights[0].shape
    shapes = [(k, right, left.shape[1] // 2 // ROWS) for k, (left, right) in enumerate(items)]
    mid = n_ctx // 4
    n_ring = mid + 2 + 2 * (mid - 1) + 4
    any_spec = pl.BlockSpec(memory_space=pl.ANY)
    args, arg_specs, outs, out_specs, scratch, tasks = extra if extra is not None else ([], [], [], [], [], None)
    counts = (len(args), len(outs), len(scratch))
    chunk = (ROWS, width)
    dma = pltpu.SemaphoreType.DMA
    return pl.pallas_call(
        functools.partial(sums_kernel, n_ctx, shapes, len(rights), counts, tasks, late),
        out_shape=[jax.ShapeDtypeStruct((left.shape[1], width), BF) for left, _ in items] + outs,
        in_specs=[any_spec] * (len(items) + len(rights)) + arg_specs,
        out_specs=[any_spec] * len(items) + out_specs,
        scratch_shapes=scratch
        + [
            pltpu.VMEM((2, 2, tokens, TILE), BF),
            pltpu.VMEM((min(2, len(rights) + len(late)), tokens, width), BF),
            pltpu.VMEM((4,) + chunk, BF),
            pltpu.VMEM((n_ring,) + chunk, BF),
            pltpu.VMEM((CORE_SLOTS,) + chunk, BF),
            pltpu.VMEM((HOP_SLOTS,) + chunk, BF),
            pltpu.VMEM((HOP_SLOTS,) + chunk, BF),
            pltpu.VMEM((HOP_SLOTS,) + chunk, BF),
            pltpu.VMEM((CORE_SLOTS,) + chunk, BF),
            dma((2, 2)),
            dma((2,)),
            dma((4,)),
            dma((CORE_SLOTS,)),
            dma((n_ring,)),
            dma((HOP_SLOTS,)),
            dma((n_ring,)),
            dma((HOP_SLOTS,)),
            dma((n_ring,)),
            dma((HOP_SLOTS,)),
            dma((n_ring,)),
            dma((CORE_SLOTS,)),
            dma((2, 2)),
        ]
        + [pltpu.SemaphoreType.REGULAR] * 5,
        compiler_params=pltpu.CompilerParams(
            vmem_limit_bytes=VMEM_LIMIT, collective_id=collective_id, has_side_effects=True
        ),
        cost_estimate=pl.CostEstimate(
            flops=sum(2 * left.shape[1] * tokens * width for left, _ in items),
            bytes_accessed=sum(2 * left.shape[1] * (tokens + width) for left, _ in items),
            transcendentals=0,
        ),
    )(*[left for left, _ in items], *rights, *args)


VMEM_SPEC = pl.BlockSpec(memory_space=pltpu.VMEM)
ANY_SPEC = pl.BlockSpec(memory_space=pl.ANY)


def norm_back_rows(values, gain, grad):
    inv = inverse_rms(values)
    unit = values * inv
    scaled = grad * gain
    back = (scaled - unit * jnp.mean(scaled * unit, axis=-1, keepdims=True)) * inv
    return back, jnp.sum(grad * unit, axis=0, keepdims=True)


def feed_tasks(groups, extra_in, extra_out, scratch):
    dgp_ref, dup_ref, wg_ref, wu_ref, residual, grads, gain = extra_in
    dr, da_all, gain_grad, d_ref = extra_out
    n = len(Scatter.scratch(16, 128))
    bufs, rest = scratch[:n], scratch[n:]
    weights, lefts, tile_out, weight_sem, left_sem, out_sem = rest[:6]
    da_own = bufs[0]
    scatter = Scatter(d_ref, groups, bufs[:9], bufs[9:])
    gather = Gather(da_own, da_all, groups, rest[6:])
    order = list(reversed(range(len(groups))))
    rows, columns = lefts.shape[2], weights.shape[1]
    row_tiles = dgp_ref.shape[0] // rows
    tiles = row_tiles * (d_ref.shape[1] // columns)

    def weight_copies(part):
        at = pl.ds(pl.multiple_of(part * columns, columns), columns)
        return [
            pltpu.make_async_copy(ref.at[at], weights.at[k], weight_sem.at[k]) for k, ref in enumerate((wg_ref, wu_ref))
        ]

    def left_copies(tile):
        at = pl.ds(pl.multiple_of(lax.rem(tile, row_tiles) * rows, rows), rows)
        slot = lax.rem(tile, 2)
        return [
            pltpu.make_async_copy(ref.at[at], lefts.at[slot, k], left_sem.at[slot, k])
            for k, ref in enumerate((dgp_ref, dup_ref))
        ]

    def out_copy(tile):
        slot = lax.rem(tile, 2)
        return pltpu.make_async_copy(
            tile_out.at[slot],
            d_ref.at[
                pl.ds(pl.multiple_of(lax.rem(tile, row_tiles) * rows, rows), rows),
                pl.ds(pl.multiple_of(tile // row_tiles * columns, columns), columns),
            ],
            out_sem.at[slot],
        )

    def begin():
        gain_grad[...] = jnp.zeros_like(gain_grad)
        for copy in weight_copies(0) + left_copies(0):
            copy.start()

    def each(i):
        @pl.when(i < tiles)
        def _():
            slot = lax.rem(i, 2)

            @pl.when(i + 1 < tiles)
            def _():
                for copy in left_copies(i + 1):
                    copy.start()

            @pl.when(lax.rem(i, row_tiles) == 0)
            def _():
                @pl.when(i > 0)
                def _():
                    for copy in weight_copies(i // row_tiles):
                        copy.start()

                for copy in weight_copies(i // row_tiles):
                    copy.wait()

            for copy in left_copies(i):
                copy.wait()
            total = times_transposed(lefts[slot, 0], weights[0]) + times_transposed(lefts[slot, 1], weights[1])

            @pl.when(i >= 2)
            def _():
                out_copy(i - 2).wait()

            tile_out[slot] = total.astype(BF)
            out_copy(i).start()

    def start():
        out_copy(tiles - 2).wait()
        out_copy(tiles - 1).wait()
        for g in order:
            scatter.start(g)

    def use(at, total):
        back, more = norm_back_rows(residual[at, :], gain[...], total)
        total_grad = grads[at, :].astype(F32) + back
        dr[at, :] = total_grad
        da_own[at, :] = total_grad.astype(BF)
        gain_grad[...] += more

    def spread(g):
        scatter.total(g, use)
        gather.start(g)

    def finish():
        for g in order:
            gather.finish(g)
            gather.sent(g)

    plan = {
        0: begin,
        tiles: start,
        tiles + 4: lambda: scatter.forward(order[0]),
        tiles + 7: lambda: scatter.forward(order[-1]),
        tiles + 8: lambda: spread(order[0]),
        tiles + 10: lambda: spread(order[-1]),
        tiles + 13: lambda: gather.forward(order[0]),
        tiles + 17: lambda: gather.forward(order[-1]),
        tiles + 23: finish,
    }
    return plan, each


def feed_extra(groups, dgp, dup, wg, wu, residual, grads, gain):
    rows, width = residual.shape
    tokens, hidden = dgp.shape
    dma = pltpu.SemaphoreType.DMA
    outs = [
        jax.ShapeDtypeStruct((rows, width), F32),
        jax.ShapeDtypeStruct((tokens, width), BF),
        jax.ShapeDtypeStruct((1, width), F32),
        jax.ShapeDtypeStruct((tokens, width), BF),
    ]
    scratch = (
        Scatter.scratch(rows, width)
        + [
            pltpu.VMEM((2, width // 2, hidden), BF),
            pltpu.VMEM((2, 2, PAIR, hidden), BF),
            pltpu.VMEM((2, PAIR, width // 2), BF),
            dma((2,)),
            dma((2, 2)),
            dma((2,)),
        ]
        + Gather.scratch()
    )
    return (
        [dgp, dup, wg, wu, residual, grads, gain],
        [ANY_SPEC] * 4 + [VMEM_SPEC] * 3,
        outs,
        [VMEM_SPEC, ANY_SPEC, VMEM_SPEC, ANY_SPEC],
        scratch,
        functools.partial(feed_tasks, groups),
    )


def input_tasks(groups, extra_in, extra_out, scratch):
    i_ref, y_ref, rows_in, dr, gain, residual = extra_in
    input_grad, gain_grad, output = extra_out
    bufs, free = scratch[:-1], scratch[-1]
    first = Scatter(i_ref, groups, bufs[:9], bufs[9:])
    last = Scatter(y_ref, groups, bufs[:9], bufs[9:])
    order = list(reversed(range(len(groups))))

    def begin():
        gain_grad[...] = jnp.zeros_like(gain_grad)
        for g in order:
            first.start(g)

    def use(at, total):
        back, more = norm_back_rows(rows_in[at, :].astype(F32), gain[...], total)
        input_grad[at, :] = (dr[at, :] + back).astype(BF)
        gain_grad[...] += more

    def again():
        first.total(order[-1], use)
        for device in neighbours():
            signal(free, device)
        pl.semaphore_wait(free, 2)
        for g in order:
            last.start(g)

    def use_out(at, total):
        output[at, :] = (residual[at, :] + total).astype(BF)

    def finish():
        for g in order:
            last.total(g, use_out)

    return {
        0: begin,
        3: lambda: first.forward(order[0]),
        8: lambda: first.forward(order[-1]),
        9: lambda: first.total(order[0], use),
        11: again,
        15: lambda: last.forward(order[0]),
        20: lambda: last.forward(order[-1]),
        23: finish,
    }, None


def input_extra(groups, i_partial, y_partial, rows_in, dr, gain, residual):
    rows, width = rows_in.shape
    outs = [
        jax.ShapeDtypeStruct((rows, width), BF),
        jax.ShapeDtypeStruct((1, width), F32),
        jax.ShapeDtypeStruct((rows, width), BF),
    ]
    return (
        [i_partial, y_partial, rows_in, dr, gain, residual],
        [ANY_SPEC, ANY_SPEC] + [VMEM_SPEC] * 4,
        outs,
        [VMEM_SPEC] * 3,
        Scatter.scratch(rows, width) + [pltpu.SemaphoreType.REGULAR],
        functools.partial(input_tasks, groups),
    )


class Exchange:
    def __init__(self, dest, sems, by_device):
        self.dest, self.by_device = dest, by_device
        self.send_sem, self.recv_sem, self.own_sem = sems
        self.n_ctx = dest.shape[1]
        self.me, self.rank = lax.axis_index("ctx"), lax.axis_index("tp")

    @staticmethod
    def scratch(units, n_ctx):
        dma = pltpu.SemaphoreType.DMA
        return [dma((units, n_ctx)), dma((units, n_ctx)), dma((units,))]

    def copy(self, source, unit, k):
        other = jnp.bitwise_xor(self.me, k)
        place = other if self.by_device else k
        return remote(
            source.at[unit, place],
            self.dest.at[unit, k],
            self.send_sem.at[unit, k],
            self.recv_sem.at[unit, k],
            (other, self.rank),
        )

    def own(self, source, unit):
        place = self.me if self.by_device else 0
        return pltpu.make_async_copy(source.at[unit, place], self.dest.at[unit, 0], self.own_sem.at[unit])

    def start(self, source, unit):
        for k in reversed(range(1, self.n_ctx)):
            self.copy(source, unit, k).start()
        self.own(source, unit).start()

    def arrived(self, source, unit):
        for k in range(1, self.n_ctx):
            self.copy(source, unit, k).wait_recv()
        self.own(source, unit).wait()

    def sent(self, source, unit):
        for k in range(1, self.n_ctx):
            self.copy(source, unit, k).wait_send()


def greet(n_ctx, tp_too):
    index, rank = lax.axis_index("ctx"), lax.axis_index("tp")
    barrier = pltpu.get_barrier_semaphore()
    for k in range(1, n_ctx):
        signal(barrier, (jnp.bitwise_xor(index, k), rank))
    if tp_too:
        for device in neighbours():
            signal(barrier, device)
    pl.semaphore_wait(barrier, n_ctx - 1 + (2 if tp_too else 0))


def in_turn(count):
    return [count - 1] + list(range(count - 1))


def attend_rows(qs, ks, vs, os, tile):
    length = qs.shape[0]
    factor = -(HD ** (-0.5)) * LOG2E
    shift = math.log(length) * LOG2E
    row_at = lax.broadcasted_iota(jnp.int32, (tile, tile), 0)
    col_at = lax.broadcasted_iota(jnp.int32, (tile, tile), 1)
    for i in range(length // tile):
        query = qs[i * tile : (i + 1) * tile, :]

        def part(j, masked):
            at = pl.ds(pl.multiple_of(j * tile, tile), tile)
            raw = times_transposed(query, ks[at, :])
            prob = 1.0 / (1.0 + jnp.exp2(raw * factor + shift))
            if masked:
                prob = jnp.where(row_at >= col_at, prob, 0.0)
            return dot(prob.astype(BF), vs[at, :])

        total = part(i, True)
        if i > 0:
            total = lax.fori_loop(0, i, lambda j, acc: acc + part(j, False), total)
        os[i * tile : (i + 1) * tile, :] = total.astype(BF)


def forward_kernel(n_ctx, groups, units, tile, *refs):
    x_ref, cot_ref, gain_one, gain_two, wq_ref, wk_ref, wv_ref, wo_ref, cos_ref, sin_ref, valid_ref = refs[:11]
    n1_out, got_out, heads_out, residual, n2_out, cot_out = refs[11:17]
    rows_buf, own_buf, send, got, o_send, o_got, qs, ks, vs, os = refs[17:27]
    rest = refs[27:]
    n_gather, n_exchange = len(Gather.scratch()), len(Exchange.scratch(1, 2))
    n1_sems, rest = rest[:n_gather], rest[n_gather:]
    n2_sems, rest = rest[:n_gather], rest[n_gather:]
    cot_sems, rest = rest[:n_gather], rest[n_gather:]
    x_sems, rest = rest[:n_exchange], rest[n_exchange:]
    o_sems, rest = rest[:n_exchange], rest[n_exchange:]
    (n1_sem, got_sem), rest = rest[:2], rest[2:]
    me, rank = lax.axis_index("ctx"), lax.axis_index("tp")
    odd = lax.rem(rank, 2)
    heads = wq_ref.shape[1] // HD
    per_unit = n_ctx // heads
    unit_rows = per_unit * PAIR

    greet(n_ctx, True)
    gather_one = Gather(own_buf, rows_buf, groups, n1_sems)
    gather_two = Gather(own_buf, n2_out, groups, n2_sems)
    gather_cot = Gather(cot_ref, cot_out, groups, cot_sems)
    scatter = Scatter(rows_buf, groups, rest[:6], rest[6:], loaded=False)
    trade = Exchange(got, x_sems, True)
    trade_back = Exchange(o_got, o_sems, False)
    order = list(reversed(range(len(groups))))
    last_u, mid_u, end_u = in_turn(len(units))

    def halves_of(u):
        return halves_at(odd if units[u][1] else 0)

    def normed(source, gain, at):
        values = source[at, :].astype(F32)
        return (values * inverse_rms(values) * gain[...]).astype(BF)

    for g in order:
        _, rows, own = groups[g]
        at = pl.ds(own, rows)
        own_buf[at, :] = normed(x_ref, gain_one, at)
        gather_one.start(g)

    def query(u, block):
        base, flipped = units[u]
        first, second = halves_of(u)
        at = pl.ds(base + block * PAIR, PAIR)
        rows = rows_buf[at, :]
        table = 1 if flipped else 0
        for which, w_ref in enumerate((wq_ref, wk_ref, wv_ref)):
            product = dot(rows, w_ref[...])
            for head in range(heads):
                part = product[:, head * HD : (head + 1) * HD]
                if which < 2:
                    part = part * cos_ref[table] + pltpu.roll(part, HD // 2, 1) * sin_ref[table]
                else:
                    part = part * valid_ref[at, :]
                part = part.astype(BF)
                send[u, block * heads + head, which, first, :] = part[:BLOCK]
                send[u, block * heads + head, which, second, :] = part[BLOCK:]

    def query_unit(u):
        for block in range(per_unit):
            query(u, block)
        trade.start(send, u)

    store_n1 = pltpu.make_async_copy(rows_buf, n1_out, n1_sem)
    store_got = [pltpu.make_async_copy(got.at[u], got_out.at[u], got_sem.at[u]) for u in range(len(units))]

    gather_one.forward(order[0])
    gather_one.finish(order[0])
    query_unit(last_u)
    gather_one.forward(order[1])
    query_unit(mid_u)
    gather_one.finish(order[1])
    for g in order:
        gather_cot.start(g)
    query_unit(end_u)
    store_n1.start()

    def attend(u):
        trade.arrived(send, u)
        store_got[u].start()
        for k in range(n_ctx):
            front, back = both_places(me, k, n_ctx)
            for which, dest in enumerate((qs, ks, vs)):
                dest[front, :] = got[u, k, which, :BLOCK, :]
                dest[back, :] = got[u, k, which, BLOCK:, :]
        attend_rows(qs, ks, vs, os, tile)
        for k in range(n_ctx):
            front, back = both_places(me, k, n_ctx)
            o_send[u, k, :BLOCK, :] = os[front, :]
            o_send[u, k, BLOCK:, :] = os[back, :]
        trade_back.start(o_send, u)

    def project(u):
        trade_back.arrived(o_send, u)
        base, _ = units[u]
        first, second = halves_of(u)
        for block in range(per_unit):
            at = pl.ds(base + block * PAIR, PAIR)
            low = valid_ref[at, :].astype(BF)
            for head in range(heads):
                place = jnp.bitwise_xor(me, block * heads + head)
                part = jnp.concatenate([o_got[u, place, first, :], o_got[u, place, second, :]], axis=0)
                heads_out[at, head * HD : (head + 1) * HD] = part * low
            rows_buf[at, :] = dot(heads_out[at, :], wo_ref[...]).astype(BF)

    def use(at, total):
        residual[at, :] = x_ref[at, :].astype(F32) + total
        own_buf[at, :] = normed(residual, gain_two, at)

    def finish_group(g):
        scatter.total(g, use)
        gather_two.start(g)

    attend(last_u)
    for g in order:
        gather_one.sent(g)
    store_n1.wait()
    project(last_u)
    scatter.start(order[0], loads=False)
    for g in order:
        gather_cot.forward(g)
    scatter.forward(order[0])
    finish_group(order[0])
    attend(mid_u)
    gather_two.forward(order[0])
    project(mid_u)
    scatter.start(order[1], (0,), loads=False)
    attend(end_u)
    project(end_u)
    scatter.start(order[1], (1, 3, 2), loads=False)
    scatter.forward(order[1])
    finish_group(order[1])
    gather_two.forward(order[1])
    for u in range(len(units)):
        trade.sent(send, u)
        trade_back.sent(o_send, u)
        store_got[u].wait()
    for g in order:
        gather_cot.finish(g)
        gather_two.finish(g)
        gather_two.sent(g)
        gather_cot.sent(g)


def forward_layer(x_own, cot_own, gain_one, gain_two, wq, wk, wv, wo, cos_tab, sin_tab, valid, n_ctx, groups, units):
    rows, depth = x_own.shape
    width = wq.shape[1]
    tokens = valid.shape[0]
    length = 2 * n_ctx * BLOCK
    n_units = len(units)
    vmem = lambda shape, dtype=BF: pltpu.VMEM(shape, dtype)
    outs = [
        jax.ShapeDtypeStruct((tokens, depth), BF),
        jax.ShapeDtypeStruct((n_units, n_ctx, 3, PAIR, HD), BF),
        jax.ShapeDtypeStruct((tokens, width), BF),
        jax.ShapeDtypeStruct((rows, depth), F32),
        jax.ShapeDtypeStruct((tokens, depth), BF),
        jax.ShapeDtypeStruct((tokens, depth), BF),
    ]
    return pl.pallas_call(
        functools.partial(forward_kernel, n_ctx, groups, units, min(512, length)),
        out_shape=outs,
        in_specs=[VMEM_SPEC, ANY_SPEC] + [VMEM_SPEC] * 9,
        out_specs=[ANY_SPEC, ANY_SPEC, VMEM_SPEC, VMEM_SPEC, ANY_SPEC, ANY_SPEC],
        scratch_shapes=[
            vmem((tokens, depth)),
            vmem((rows, depth)),
            vmem((n_units, n_ctx, 3, PAIR, HD)),
            vmem((n_units, n_ctx, 3, PAIR, HD)),
            vmem((n_units, n_ctx, PAIR, HD)),
            vmem((n_units, n_ctx, PAIR, HD)),
        ]
        + [vmem((length, HD))] * 4
        + Gather.scratch() * 3
        + Exchange.scratch(n_units, n_ctx) * 2
        + [pltpu.SemaphoreType.DMA, pltpu.SemaphoreType.DMA((n_units,))]
        + Scatter.scratch(rows, depth, loaded=False),
        compiler_params=pltpu.CompilerParams(vmem_limit_bytes=VMEM_LIMIT, collective_id=3, has_side_effects=True),
        cost_estimate=pl.CostEstimate(
            flops=8 * tokens * depth * width, bytes_accessed=8 * tokens * depth, transcendentals=0
        ),
    )(x_own, cot_own, gain_one, gain_two, wq, wk, wv, wo, cos_tab, sin_tab, valid)


def attend_rows_back(qs, ks, vs, gs, os, dqs, cos_ref, sin_ref, tile):
    length = qs.shape[0]
    scale = HD ** (-0.5)
    factor = -scale * LOG2E
    shift = math.log(length) * LOG2E
    count = length // tile
    key_at = lax.broadcasted_iota(jnp.int32, (tile, tile), 0)
    query_at = lax.broadcasted_iota(jnp.int32, (tile, tile), 1)
    dqs[...] = jnp.zeros_like(dqs)

    def unrotate(values, at):
        return (values * cos_ref[at, :] - pltpu.roll(values, HD // 2, 1) * sin_ref[at, :]).astype(BF)

    for j in range(count):
        own = slice(j * tile, (j + 1) * tile)
        keys = ks[own, :]
        values = vs[own, :]

        def part(i, masked):
            at = pl.ds(pl.multiple_of(i * tile, tile), tile)
            query = qs[at, :]
            grad = gs[at, :]
            raw = times_transposed(keys, query)
            prob = 1.0 / (1.0 + jnp.exp2(raw * factor + shift))
            if masked:
                prob = jnp.where(query_at >= key_at, prob, 0.0)
            prob_grad = times_transposed(values, grad)
            score_grad = (prob_grad * prob * (1.0 - prob)).astype(BF)
            dqs[at, :] += contract_rows(score_grad, keys)
            return dot(score_grad, query), dot(prob.astype(BF), grad)

        total = part(j, True)
        if j + 1 < count:

            def step(i, acc):
                more = part(i, False)
                return acc[0] + more[0], acc[1] + more[1]

            total = lax.fori_loop(j + 1, count, step, total)
        os[1, own, :] = unrotate(total[0] * scale, own)
        os[2, own, :] = total[1].astype(BF)
    for i in range(count):
        at = slice(i * tile, (i + 1) * tile)
        os[0, at, :] = unrotate(dqs[at, :] * scale, at)


def middle_kernel(n_ctx, units, tile, *refs):
    da_ref, got_ref, h_ref, wq_ref, wk_ref, wv_ref, wo_ref, wd_ref, cos_ref, sin_ref, valid_ref = refs[:11]
    grad_ref, partial_out, y_out = refs[11:14]
    rows_buf, got, do_send, do_got, back_send, back_got, h_buf, qs, ks, vs, gs, os, dqs = refs[14:27]
    rest = refs[27:]
    n_exchange = len(Exchange.scratch(1, 2))
    do_sems, back_sems, rest = rest[:n_exchange], rest[n_exchange : 2 * n_exchange], rest[2 * n_exchange :]
    da_sem, got_sem, out_sem, h_sem, y_sem = rest
    me, rank = lax.axis_index("ctx"), lax.axis_index("tp")
    odd = lax.rem(rank, 2)
    heads = wq_ref.shape[1] // HD
    per_unit = n_ctx // heads
    unit_rows = per_unit * PAIR
    count = len(units)
    order = in_turn(count)

    def rows_of(u):
        return pl.ds(units[u][0], unit_rows)

    load_da = [pltpu.make_async_copy(da_ref.at[rows_of(u)], rows_buf.at[rows_of(u)], da_sem.at[u]) for u in range(count)]
    load_got = [pltpu.make_async_copy(got_ref.at[u], got.at[u], got_sem.at[u]) for u in range(count)]
    store = [
        pltpu.make_async_copy(rows_buf.at[rows_of(u)], partial_out.at[rows_of(u)], out_sem.at[u]) for u in range(count)
    ]
    for u in order:
        load_da[u].start()
    for u in order:
        load_got[u].start()
    greet(n_ctx, False)
    trade = Exchange(do_got, do_sems, True)
    trade_back = Exchange(back_got, back_sems, False)

    for u in order:
        load_da[u].wait()
        base, flipped = units[u]
        first, second = halves_at(odd if flipped else 0)
        for block in range(per_unit):
            at = pl.ds(base + block * PAIR, PAIR)
            grad = times_transposed(rows_buf[at, :], wo_ref[...]).astype(BF)
            low = valid_ref[at, :].astype(BF)
            for head in range(heads):
                part = grad[:, head * HD : (head + 1) * HD] * low
                do_send[u, block * heads + head, first, :] = part[:BLOCK]
                do_send[u, block * heads + head, second, :] = part[BLOCK:]
        trade.start(do_send, u)
    for u in order:
        load_got[u].wait()

    def attend(turn, carry):
        u = lax.rem(turn + count - 1, count)
        trade.arrived(do_send, u)
        for k in range(n_ctx):
            front, back = both_places(me, k, n_ctx)
            for which, dest in enumerate((qs, ks, vs)):
                dest[front, :] = got[u, k, which, :BLOCK, :]
                dest[back, :] = got[u, k, which, BLOCK:, :]
            gs[front, :] = do_got[u, k, :BLOCK, :]
            gs[back, :] = do_got[u, k, BLOCK:, :]
        attend_rows_back(qs, ks, vs, gs, os, dqs, cos_ref, sin_ref, tile)
        for k in range(n_ctx):
            front, back = both_places(me, k, n_ctx)
            for which in range(3):
                back_send[u, k, which, :BLOCK, :] = os[which, front, :]
                back_send[u, k, which, BLOCK:, :] = os[which, back, :]
        trade_back.start(back_send, u)
        return carry

    lax.fori_loop(0, count, attend, 0)

    tiles = rows_buf.shape[0] // PAIR

    def tile_rows(tile):
        return pl.ds(pl.multiple_of(tile * PAIR, PAIR), PAIR)

    def load_h(tile):
        slot = lax.rem(tile, 2)
        return pltpu.make_async_copy(h_ref.at[tile_rows(tile)], h_buf.at[slot], h_sem.at[slot])

    load_h(0).start()

    def down(tile, carry):
        @pl.when(tile + 1 < tiles)
        def _():
            load_h(tile + 1).start()

        load_h(tile).wait()
        rows_buf[tile_rows(tile), :] = dot(h_buf[lax.rem(tile, 2)], wd_ref[...]).astype(BF)
        return carry

    lax.fori_loop(0, tiles, down, 0)
    store_y = pltpu.make_async_copy(rows_buf, y_out, y_sem)
    store_y.start()
    store_y.wait()

    for u in order:
        trade_back.arrived(back_send, u)
        base, flipped = units[u]
        first, second = halves_at(odd if flipped else 0)
        for block in range(per_unit):
            at = pl.ds(base + block * PAIR, PAIR)
            low = valid_ref[at, :].astype(BF)
            total = None
            for which, w_ref in enumerate((wq_ref, wk_ref, wv_ref)):
                width = heads * HD
                for head in range(heads):
                    place = jnp.bitwise_xor(me, block * heads + head)
                    part = jnp.concatenate(
                        [back_got[u, place, which, first, :], back_got[u, place, which, second, :]], axis=0
                    )
                    columns = slice(which * width + head * HD, which * width + (head + 1) * HD)
                    grad_ref[at, columns] = part * low if which == 2 else part
                product = times_transposed(grad_ref[at, which * width : (which + 1) * width], w_ref[...])
                total = product if total is None else total + product
            rows_buf[at, :] = total.astype(BF)
        store[u].start()
    for u in order:
        trade.sent(do_send, u)
        trade_back.sent(back_send, u)
        store[u].wait()


def middle_layer(da, got, h, wq, wk, wv, wo, wd, cos_full, sin_full, valid, n_ctx, units):
    tokens, depth = da.shape
    width = wq.shape[1]
    length = 2 * n_ctx * BLOCK
    count = len(units)
    vmem = lambda shape, dtype=BF: pltpu.VMEM(shape, dtype)
    dma = pltpu.SemaphoreType.DMA
    three, one = (count, n_ctx, 3, PAIR, HD), (count, n_ctx, PAIR, HD)
    return pl.pallas_call(
        functools.partial(middle_kernel, n_ctx, units, min(512, length)),
        out_shape=[jax.ShapeDtypeStruct((tokens, 3 * width), BF)] + [jax.ShapeDtypeStruct((tokens, depth), BF)] * 2,
        in_specs=[ANY_SPEC] * 3 + [VMEM_SPEC] * 8,
        out_specs=[VMEM_SPEC] + [ANY_SPEC] * 2,
        scratch_shapes=[vmem((tokens, depth)), vmem(three), vmem(one), vmem(one), vmem(three), vmem(three)]
        + [vmem((2, PAIR, h.shape[1]))]
        + [vmem((length, HD))] * 4
        + [vmem((3, length, HD)), vmem((length, HD), F32)]
        + Exchange.scratch(count, n_ctx) * 2
        + [dma((count,))] * 3
        + [dma((2,)), dma],
        compiler_params=pltpu.CompilerParams(vmem_limit_bytes=VMEM_LIMIT, collective_id=4, has_side_effects=True),
        cost_estimate=pl.CostEstimate(
            flops=8 * tokens * depth * width + 2 * tokens * depth * h.shape[1],
            bytes_accessed=8 * tokens * depth,
            transcendentals=0,
        ),
    )(da, got, h, wq, wk, wv, wo, wd, cos_full, sin_full, valid)


def body(
    tokens,
    counts,
    norm_gain,
    w_query,
    w_key,
    w_value,
    w_output,
    mlp_gain,
    w_gate,
    w_up,
    w_down,
    cotangent,
):
    n_ctx = lax.axis_size("ctx")
    me = lax.axis_index("ctx")
    rank = lax.axis_index("tp")
    odd = rank & 1
    core = me & 1
    length = 2 * BLOCK * n_ctx
    heads = w_query.shape[1] // HD
    gain_one = norm_gain.astype(F32)
    gain_two = mlp_gain.astype(F32)

    inverse = THETA ** (-(jnp.arange(HD // 2, dtype=F32) * (2.0 / HD)))
    angles = jnp.arange(length, dtype=jnp.int32).astype(F32)[:, None] * inverse[None, :]
    cos_half, sin_half = jnp.cos(angles), jnp.sin(angles)
    cos_full = jnp.concatenate([cos_half, cos_half], axis=1)
    sin_full = jnp.concatenate([-sin_half, sin_half], axis=1)

    def own_blocks(table):
        front = lax.dynamic_slice_in_dim(table, me * BLOCK, BLOCK, 0)
        back = lax.dynamic_slice_in_dim(table, (2 * n_ctx - 1 - me) * BLOCK, BLOCK, 0)
        return front, back

    cos_front, cos_back = own_blocks(cos_full)
    sin_front, sin_back = own_blocks(sin_full)
    own_counts = lax.dynamic_index_in_dim(counts, me, 0, keepdims=False)
    offsets = jnp.arange(BLOCK, dtype=jnp.int32)

    def valid_of(sequence_list, half_list):
        held = own_counts[jnp.stack(sequence_list), jnp.stack(half_list)]
        return (offsets[None, :] < held[:, None]).astype(F32).reshape(-1)

    cos_own = jnp.concatenate([cos_front, cos_back])
    sin_own = jnp.concatenate([sin_front, sin_back])
    sequences = counts.shape[1]
    paired = by_four() and sequences == 6 and n_ctx == 2 * heads
    if paired:
        ranks = [rank ^ k for k in range(4)]
        blocks_a = [(3 * (r >> 1) + 2 * (r & 1), jnp.int32(half)) for r in ranks for half in range(2)]
        blocks_b = [(1 + 3 * (r >> 1), r & 1) for r in ranks]
        flat_valid = valid_of(*zip(*(blocks_a + blocks_b)))
        valids = {"b": flat_valid[len(blocks_a) * BLOCK :], "a": flat_valid[: len(blocks_a) * BLOCK]}
        flip_back = lambda own: jnp.where(odd == 1, jnp.roll(own, BLOCK, axis=0), own)
        tables = {
            "b": (jnp.tile(flip_back(cos_own), (2, 1)), jnp.tile(flip_back(sin_own), (2, 1))),
            "a": (jnp.tile(cos_own, (4, 1)), jnp.tile(sin_own, (4, 1))),
        }
        scalars = {"b": jnp.stack([me, odd]).astype(jnp.int32), "a": jnp.stack([me, 0]).astype(jnp.int32)}
        n_pairs = {"b": 2 * heads, "a": 4 * heads}
    else:
        flat_valid = (offsets[None, None, :] < own_counts[:, :, None]).astype(F32).reshape(-1)
        valids = {"a": flat_valid}
        tables = {"a": (jnp.tile(cos_own, (sequences, 1)), jnp.tile(sin_own, (sequences, 1)))}
        scalars = {"a": jnp.stack([me, 0]).astype(jnp.int32)}
        n_pairs = {"a": sequences * heads}
    names = tuple(n_pairs)

    def own_rows(array):
        if not paired:
            return {"a": array}
        return {
            "b": lax.dynamic_slice_in_dim(array, (1 - odd) * PAIR, BLOCK, 0),
            "a": lax.dynamic_slice_in_dim(array, odd * BLOCK, PAIR, 0),
        }

    def whole_rows(array):
        return jnp.where(odd == 1, jnp.roll(array, BLOCK, axis=0), array) if paired else array

    x_own = {name: rows.astype(F32) for name, rows in own_rows(tokens[0]).items()}
    g_own = own_rows(cotangent[0])

    split = by_four()
    rows_of = {name: valids[name].shape[0] for name in names}
    total_rows = sum(rows_of.values())
    first_row = {"a": 0, "b": rows_of["a"]}
    valid_head = {name: jnp.broadcast_to(valids[name][:, None], (rows_of[name], HD)) for name in names}
    valid_wide = {name: jnp.broadcast_to(valids[name][:, None].astype(BF), (rows_of[name], heads * HD)) for name in names}
    near = [k for k in range(n_ctx) if k < 6]
    far = [k for k in range(n_ctx) if k >= 6]
    state = {}

    def fence():
        names_held = list(state)
        values = lax.optimization_barrier([state[name] for name in names_held])
        state.update(zip(names_held, values))

    def only_b(step):
        if "b" in names:
            step("b")

    def norm_one(n):
        state["n1", n] = (x_own[n] * inverse_rms(x_own[n]) * gain_one).astype(BF)

    def gather_a(key):
        def step(n):
            state[key, n] = gather_first(state[key, n])

        return step

    def gather_b(key):
        def step(n):
            state[key, n] = gather_second(state[key, n])

        return step

    def query(n):
        state["n1", n] = gathered(state["n1", n])
        cos_tab, sin_tab = tables[n]
        state["qkv", n] = project_qkv(
            scalars[n], state["n1", n], w_query, w_key, w_value, cos_tab, sin_tab, valid_head[n], n_ctx
        )

    def swap_part(key, places, to):
        def step(n):
            got = dict(state.get((to, n), {}))
            got.update(exchange(state[key, n], places, n_ctx))
            state[to, n] = got
            if len(got) == n_ctx:
                state[to, n] = [got[k] for k in range(n_ctx)]
                del state[key, n]

        return step

    def attend(n):
        state["mixed", n] = attention_forward(scalars[n], state["got", n], n_ctx)

    def project(n):
        heads_out, *parts = project_out(
            scalars[n], state.pop(("back", n)), w_output, valid_wide[n], n_pairs[n], n_ctx, split
        )
        state["heads", n], state["r", n] = heads_out, tuple(parts)

    def scatter_a(key):
        def step(n):
            state[key, n] = scatter_first(state[key, n])

        return step

    def scatter_b(key):
        def step(n):
            state[key, n] = scatter_second(state[key, n])

        return step

    def norm_two(n):
        residual = x_own[n] + scattered(state.pop(("r", n)))
        state["residual", n] = residual
        state["n2", n] = (residual * inverse_rms(residual) * gain_two).astype(BF)

    def core_mlp(n):
        state["n2", n] = gathered(state["n2", n])
        state["cot", n] = gathered(state["cot", n])
        held = state.get("mlp", ())
        state["mlp"] = mlp_core(
            state["n2", n], state["cot", n], w_gate, w_up, w_down, total_rows, first_row[n], held
        )

    def attend_back(n):
        state["dqkv", n] = attention_backward(
            scalars[n], state.pop(("got", n)), state.pop(("gdo", n)), cos_full, sin_full, n_ctx
        )

    def query_back(n):
        dq, dk, dv, *parts = project_in(
            scalars[n], state.pop(("gdqkv", n)), (w_query, w_key, w_value), valid_wide[n], n_pairs[n], n_ctx, False
        )
        state["dq", n], state["dk", n], state["dv", n], state["i", n] = dq, dk, dv, parts[0]

    def joined(key):
        parts = [state[key, n] for n in ("a", "b") if n in names]
        return jnp.concatenate(parts) if len(parts) > 1 else parts[0]

    groups = tuple((first_row[n], rows_of[n] // 4, first_row[n] // 4) for n in ("a", "b") if n in names)

    def own_order(array):
        return jnp.where(odd == 1, jnp.roll(array, -BLOCK, axis=0), array) if paired else array

    own_grads, own_rows_in = own_order(cotangent[0]), own_order(tokens[0])
    if paired:
        units = ((0, False), (2 * PAIR, False), (4 * PAIR, True))
        wide_valid = jnp.broadcast_to(flat_valid[:, None], (total_rows, HD))
        tabs = [jnp.stack([tab, flip_back(tab)]) for tab in (cos_own, sin_own)]
        all_n1, got, heads_out, own_residual, all_n2, all_cot = forward_layer(
            own_rows_in, own_grads, gain_one[None], gain_two[None], w_query, w_key, w_value, w_output,
            *tabs, wide_valid, n_ctx, groups, units,
        )
    else:
        norm_one("a")
        state["cot", "a"] = g_own["a"]
        gather_a("n1")("a")
        query("a")
        swap_part("qkv", range(n_ctx), "got")("a")
        attend("a")
        swap_part("mixed", range(n_ctx), "back")("a")
        project("a")
        scatter_a("r")("a")
        norm_two("a")
        gather_a("n2")("a")
        gather_a("cot")("a")
        all_n1, all_n2, all_cot = state["n1", "a"], gathered(state["n2", "a"]), gathered(state["cot", "a"])
        heads_out, own_residual = state["heads", "a"], state["residual", "a"]
    h, dgp, dup = mlp_core(all_n2, all_cot, w_gate, w_up, w_down, total_rows, 0)
    if paired:
        extra = feed_extra(groups, dgp, dup, w_gate, w_up, own_residual, own_grads, gain_two[None])
        sum_down, sum_gate, sum_up, sum_out, dr, da, gain_two_grad, _ = weight_sums(
            [(h, 0), (all_n2, 1), (all_n2, 2), (heads_out, 3)], [all_cot, dgp, dup], n_ctx, 1, extra, late=(1,)
        )
        dqkv, i_partial, y_partial = middle_layer(
            da, got, h, w_query, w_key, w_value, w_output, w_down, cos_full, sin_full, wide_valid, n_ctx, units
        )
        extra = input_extra(groups, i_partial, y_partial, own_rows_in, dr, gain_one[None], own_residual)
        sum_qkv, input_grad, gain_one_grad, output = weight_sums([(all_n1, 0)], [dqkv], n_ctx, 2, extra)
    else:
        d_partial = (times_transposed(dgp, w_gate) + times_transposed(dup, w_up)).astype(BF)
        y_partial = dot(h, w_down).astype(BF)
        (sum_down,) = weight_sums([(h, 0)], [all_cot], n_ctx, 1)
        sum_gate, sum_up = weight_sums([(all_n2, 0), (all_n2, 1)], [dgp, dup], n_ctx, 2)
        back, gain_two_grad = norm_back_rows(own_residual, gain_two, scattered(scatter_first((d_partial,))))
        dr = own_grads.astype(F32) + back
        da = gathered(gather_first(dr.astype(BF)))
        output = (own_residual + scattered(scatter_first((y_partial,)))).astype(BF)
        state["do", "a"] = heads_back(scalars["a"], da, w_output, valid_wide["a"], n_ctx)
        swap_part("do", range(n_ctx), "gdo")("a")
        attend_back("a")
        swap_part("dqkv", range(n_ctx), "gdqkv")("a")
        query_back("a")
        (sum_out,) = weight_sums([(heads_out, 0)], [da], n_ctx, 3)
        (sum_qkv,) = weight_sums(
            [(all_n1, 0)], [jnp.concatenate([state[key, "a"] for key in ("dq", "dk", "dv")], axis=1)], n_ctx, 4
        )
        back, gain_one_grad = norm_back_rows(x_own["a"], gain_one, scattered(scatter_first((state["i", "a"],))))
        input_grad = (dr + back).astype(BF)
    grad_query, grad_key, grad_value = (part.astype(F32) for part in jnp.split(sum_qkv, 3, axis=1))
    gains = jnp.concatenate([gain_one_grad, gain_two_grad])
    for axis in ("tp", "ctx"):
        size = lax.axis_size(axis)
        for bit in range(size.bit_length() - 1):
            gains = gains + lax.ppermute(gains, axis, [(i, i ^ (1 << bit)) for i in range(size)])
    return (
        whole_rows(output)[None],
        whole_rows(input_grad)[None],
        gains[0],
        grad_query,
        grad_key,
        grad_value,
        sum_out.astype(F32),
        gains[1],
        sum_gate.astype(F32),
        sum_up.astype(F32),
        sum_down.astype(F32),
    )


def solution(mesh):
    placed = (
        P("ctx", "tp", None),
        P(),
        P(),
        P(None, "tp"),
        P(None, "tp"),
        P(None, "tp"),
        P("tp", None),
        P(),
        P(None, "tp"),
        P(None, "tp"),
        P("tp", None),
        P("ctx", "tp", None),
    )
    return jax.shard_map(
        body,
        mesh=mesh,
        in_specs=placed,
        out_specs=(
            P("ctx", "tp", None),
            P("ctx", "tp", None),
            P(),
            P(None, "tp"),
            P(None, "tp"),
            P(None, "tp"),
            P("tp", None),
            P(),
            P(None, "tp"),
            P(None, "tp"),
            P("tp", None),
        ),
        check_vma=False,
    )
```

```python
import functools
import math

import jax
import jax.numpy as jnp
from jax import lax
from jax.experimental import pallas as pl
from jax.experimental.pallas import tpu as pltpu
from jax.sharding import PartitionSpec as P

HD = 128
BLOCK = 128
PAIR = 2 * BLOCK
EPS = 1e-05
THETA = 10000.0
LOG2E = 1.4426950408889634
BF = jnp.bfloat16
F32 = jnp.float32
VMEM_LIMIT = 60 * 1024 * 1024

X_SWAP = [(i, i ^ 1) for i in range(4)]
Y_SWAP = [(i, i ^ 2) for i in range(4)]


def dot(left, right):
    return jnp.dot(left, right, preferred_element_type=F32)


def contract_rows(left, right):
    return lax.dot_general(left, right, (((0,), (0,)), ((), ())), preferred_element_type=F32)


def times_transposed(left, right):
    return lax.dot_general(left, right, (((1,), (1,)), ((), ())), preferred_element_type=F32)


def send_x(values):
    return lax.ppermute(values, "tp", X_SWAP)


def send_y(values):
    return lax.ppermute(values, "tp", Y_SWAP)


def by_four():
    return lax.axis_size("tp") == 4


def gather_first(own):
    if not by_four():
        return (lax.all_gather(own, "tp", axis=0, tiled=True),)
    return own, send_x(own), send_y(own)


def gather_second(held):
    if len(held) == 1:
        return held
    own, from_x, from_y = held
    half = own.shape[0] // 2
    return own, from_x, from_y, send_x(from_y[:half]), send_y(from_x[half:])


def gathered(held):
    return jnp.concatenate(held) if len(held) > 1 else held[0]


def scatter_parts(partial):
    if not by_four():
        return (partial,)
    rows = partial.shape[0] // 4
    half = rows // 2
    at = lambda first: partial[first * half : (first + 1) * half]
    return (
        jnp.concatenate([at(2), at(6)]),
        jnp.concatenate([at(5), at(7)]),
        jnp.concatenate([at(0), at(1), at(4), at(3)]),
    )


def scatter_first(parts):
    if len(parts) == 1:
        return (lax.psum_scatter(parts[0], "tp", scatter_dimension=0, tiled=True),)
    return send_x(parts[0]), send_y(parts[1]), parts[2]


def add_low(left, right):
    return (left.astype(F32) + right.astype(F32)).astype(BF)


def scatter_second(held):
    if len(held) == 1:
        return held
    from_x, from_y, stay = held
    half = from_x.shape[0] // 2
    low_rest = send_y(add_low(stay[2 * half : 3 * half], from_x[half:]))
    high_rest = send_x(add_low(stay[3 * half :], from_y[half:]))
    return from_x, from_y, stay, low_rest, high_rest


def scattered(held):
    if len(held) == 1:
        return held[0].astype(F32)
    from_x, from_y, stay, low_rest, high_rest = (part.astype(F32) for part in held)
    half = low_rest.shape[0]
    low = stay[:half] + from_x[:half] + low_rest
    high = stay[half : 2 * half] + from_y[:half] + high_rest
    return jnp.concatenate([low, high])


def exchange(pieces, places, n_ctx):
    got = {}
    for k in places:
        got[k] = pieces[k] if k == 0 else lax.ppermute(pieces[k], "ctx", [(i, i ^ k) for i in range(n_ctx)])
    return got


def params():
    return pltpu.CompilerParams(vmem_limit_bytes=VMEM_LIMIT)


def whole(shape):
    return pl.BlockSpec(shape, lambda *_: (0,) * len(shape))


def put_partial(refs, first, value, rows):
    if len(refs) == 1:
        refs[0][first : first + value.shape[0], :] = value
        return
    to_x, to_y, stay = refs
    half = rows // 2
    homes = {
        0: (stay, 0), 1: (stay, 1), 2: (to_x, 0), 3: (stay, 3), 4: (stay, 2), 5: (to_y, 0), 6: (to_x, 1), 7: (to_y, 1)
    }
    for part in range(value.shape[0] // half):
        ref, place = homes[first // half + part]
        ref[place * half : (place + 1) * half, :] = value[part * half : (part + 1) * half]


def partial_shapes(rows, width, split):
    if not split:
        return [jax.ShapeDtypeStruct((rows, width), BF)]
    return [jax.ShapeDtypeStruct((rows // 4, width), BF)] * 2 + [jax.ShapeDtypeStruct((rows // 2, width), BF)]


def per_device(pairs, n_ctx):
    return -(-pairs // n_ctx)


def halves_at(swap):
    first = pl.multiple_of(swap * BLOCK, BLOCK)
    second = pl.multiple_of((1 - swap) * BLOCK, BLOCK)
    return pl.ds(first, BLOCK), pl.ds(second, BLOCK)


def qkv_kernel(n_ctx, pairs, scalar_ref, n_ref, wq_ref, wk_ref, wv_ref, cos_ref, sin_ref, valid_ref, *rest):
    out_refs, buffer = rest[:n_ctx], rest[n_ctx]
    rows = n_ref[...]
    first, second = halves_at(scalar_ref[1])
    me = scalar_ref[0]
    cos_tab = cos_ref[...]
    sin_tab = sin_ref[...]
    heads = wq_ref.shape[1] // HD
    step = pl.program_id(0)
    per = out_refs[0].shape[0]
    for pair in range(pairs, per * n_ctx):
        buffer[pair] = jnp.zeros(buffer.shape[1:], BF)
    for which, w_ref in enumerate((wq_ref, wk_ref, wv_ref)):
        product = dot(rows, w_ref[...])
        for head in range(heads):
            part = product[:, head * HD : (head + 1) * HD]
            if which < 2:
                part = part * cos_tab + pltpu.roll(part, HD // 2, 1) * sin_tab
            else:
                part = part * valid_ref[...]
            part = part.astype(BF)
            buffer[step * heads + head, which, first, :] = part[:BLOCK]
            buffer[step * heads + head, which, second, :] = part[BLOCK:]

    @pl.when(step == pl.num_programs(0) - 1)
    def _():
        for k in range(n_ctx):
            source = jnp.bitwise_xor(me, k)
            for p in range(per):
                out_refs[k][p] = buffer[source * per + p]


def project_qkv(scalars, normed, wq, wk, wv, cos_tab, sin_tab, valid, n_ctx):
    rows, depth = normed.shape
    width = wq.shape[1]
    heads = width // HD
    steps = rows // PAIR
    per = per_device(steps * heads, n_ctx)
    row_block = pl.BlockSpec((PAIR, HD), lambda i, s: (i, 0))
    weight = whole((depth, width))
    piece = (per, 3, PAIR, HD)
    return pl.pallas_call(
        functools.partial(qkv_kernel, n_ctx, steps * heads),
        out_shape=[jax.ShapeDtypeStruct(piece, BF)] * n_ctx,
        grid_spec=pltpu.PrefetchScalarGridSpec(
            num_scalar_prefetch=1,
            grid=(steps,),
            in_specs=[
                pl.BlockSpec((PAIR, depth), lambda i, s: (i, 0)),
                weight,
                weight,
                weight,
                row_block,
                row_block,
                row_block,
            ],
            out_specs=[whole(piece)] * n_ctx,
            scratch_shapes=[pltpu.VMEM((per * n_ctx, 3, PAIR, HD), BF)],
        ),
        compiler_params=params(),
        cost_estimate=pl.CostEstimate(
            flops=6 * rows * depth * width, bytes_accessed=rows * depth * 2 + 6 * depth * width, transcendentals=0
        ),
    )(scalars, normed, wq, wk, wv, cos_tab, sin_tab, valid)


def out_kernel(n_ctx, pairs, scalar_ref, *refs):
    piece_refs, (w_ref, valid_ref), (heads_ref, *partial_refs), buffer = (
        refs[:n_ctx],
        refs[n_ctx : n_ctx + 2],
        refs[n_ctx + 2 : -1],
        refs[-1],
    )
    me = scalar_ref[0]
    first, second = halves_at(scalar_ref[1])
    per = piece_refs[0].shape[0]
    heads = w_ref.shape[0] // HD
    for k in range(n_ctx):
        source = jnp.bitwise_xor(me, k)
        for p in range(per):
            buffer[source * per + p] = piece_refs[k][p]
    weight = w_ref[...]
    for sequence in range(pairs // heads):
        at = slice(sequence * PAIR, (sequence + 1) * PAIR)
        rows = jnp.concatenate(
            [
                jnp.concatenate(
                    [buffer[sequence * heads + head, first, :], buffer[sequence * heads + head, second, :]], axis=0
                )
                for head in range(heads)
            ],
            axis=1,
        )
        rows = rows * valid_ref[at, :]
        heads_ref[at, :] = rows
        put_partial(partial_refs, sequence * PAIR, dot(rows, weight).astype(BF), pairs // heads * PAIR // 4)


def project_out(scalars, pieces, weight, valid, pairs, n_ctx, split):
    width, depth = weight.shape
    rows = valid.shape[0]
    per = pieces[0].shape[0]
    shapes = [jax.ShapeDtypeStruct((rows, width), BF)] + partial_shapes(rows, depth, split)
    return pl.pallas_call(
        functools.partial(out_kernel, n_ctx, pairs),
        out_shape=shapes,
        grid_spec=pltpu.PrefetchScalarGridSpec(
            num_scalar_prefetch=1,
            grid=(1,),
            in_specs=[whole(piece.shape) for piece in pieces] + [whole(weight.shape), whole(valid.shape)],
            out_specs=[whole(shape.shape) for shape in shapes],
            scratch_shapes=[pltpu.VMEM((per * n_ctx, PAIR, HD), BF)],
        ),
        compiler_params=params(),
        cost_estimate=pl.CostEstimate(
            flops=2 * rows * depth * width, bytes_accessed=rows * depth * 2 + 2 * depth * width, transcendentals=0
        ),
    )(scalars, *pieces, weight, valid)


def heads_back_kernel(n_ctx, scalar_ref, da_ref, w_ref, valid_ref, *rest):
    out_refs, buffer = rest[:n_ctx], rest[n_ctx]
    me = scalar_ref[0]
    first, second = halves_at(scalar_ref[1])
    per = out_refs[0].shape[0]
    heads = w_ref.shape[0] // HD
    weight = w_ref[...]
    for pair in range(da_ref.shape[0] // PAIR * heads, per * n_ctx):
        buffer[pair] = jnp.zeros(buffer.shape[1:], BF)
    for sequence in range(da_ref.shape[0] // PAIR):
        at = slice(sequence * PAIR, (sequence + 1) * PAIR)
        grad = times_transposed(da_ref[at, :], weight).astype(BF) * valid_ref[at, :]
        for head in range(heads):
            part = grad[:, head * HD : (head + 1) * HD]
            buffer[sequence * heads + head, first, :] = part[:BLOCK]
            buffer[sequence * heads + head, second, :] = part[BLOCK:]
    for k in range(n_ctx):
        source = jnp.bitwise_xor(me, k)
        for p in range(per):
            out_refs[k][p] = buffer[source * per + p]


def heads_back(scalars, da, weight, valid, n_ctx):
    rows, depth = da.shape
    width = weight.shape[0]
    per = per_device(rows // PAIR * (width // HD), n_ctx)
    piece = (per, PAIR, HD)
    return pl.pallas_call(
        functools.partial(heads_back_kernel, n_ctx),
        out_shape=[jax.ShapeDtypeStruct(piece, BF)] * n_ctx,
        grid_spec=pltpu.PrefetchScalarGridSpec(
            num_scalar_prefetch=1,
            grid=(1,),
            in_specs=[whole(da.shape), whole(weight.shape), whole(valid.shape)],
            out_specs=[whole(piece)] * n_ctx,
            scratch_shapes=[pltpu.VMEM((per * n_ctx, PAIR, HD), BF)],
        ),
        compiler_params=params(),
        cost_estimate=pl.CostEstimate(
            flops=2 * rows * depth * width, bytes_accessed=rows * depth * 2 + 2 * depth * width, transcendentals=0
        ),
    )(scalars, da, weight, valid)


def in_kernel(n_ctx, pairs, scalar_ref, *refs):
    piece_refs, weight_refs, valid_ref = refs[:n_ctx], refs[n_ctx : n_ctx + 3], refs[n_ctx + 3]
    grad_refs, partial_refs, buffer = refs[n_ctx + 4 : n_ctx + 7], refs[n_ctx + 7 : -1], refs[-1]
    me = scalar_ref[0]
    first, second = halves_at(scalar_ref[1])
    per = piece_refs[0].shape[0]
    heads = weight_refs[0].shape[1] // HD
    for k in range(n_ctx):
        source = jnp.bitwise_xor(me, k)
        for p in range(per):
            buffer[source * per + p] = piece_refs[k][p]
    for sequence in range(pairs // heads):
        at = slice(sequence * PAIR, (sequence + 1) * PAIR)
        total = None
        for which in range(3):
            rows = jnp.concatenate(
                [
                    jnp.concatenate([buffer[pair, which, first, :], buffer[pair, which, second, :]], axis=0)
                    for pair in range(sequence * heads, (sequence + 1) * heads)
                ],
                axis=1,
            )
            if which == 2:
                rows = rows * valid_ref[at, :]
            grad_refs[which][at, :] = rows
            product = times_transposed(rows, weight_refs[which][...])
            total = product if total is None else total + product
        put_partial(partial_refs, sequence * PAIR, total.astype(BF), pairs // heads * PAIR // 4)


def project_in(scalars, pieces, weights, valid, pairs, n_ctx, split):
    depth, width = weights[0].shape
    rows = valid.shape[0]
    per = pieces[0].shape[0]
    shapes = [jax.ShapeDtypeStruct((rows, width), BF)] * 3 + partial_shapes(rows, depth, split)
    return pl.pallas_call(
        functools.partial(in_kernel, n_ctx, pairs),
        out_shape=shapes,
        grid_spec=pltpu.PrefetchScalarGridSpec(
            num_scalar_prefetch=1,
            grid=(1,),
            in_specs=[whole(piece.shape) for piece in pieces]
            + [whole(weight.shape) for weight in weights]
            + [whole(valid.shape)],
            out_specs=[whole(shape.shape) for shape in shapes],
            scratch_shapes=[pltpu.VMEM((per * n_ctx, 3, PAIR, HD), BF)],
        ),
        compiler_params=params(),
        cost_estimate=pl.CostEstimate(
            flops=6 * rows * depth * width, bytes_accessed=rows * depth * 2 + 6 * depth * width, transcendentals=0
        ),
    )(scalars, *pieces, *weights, valid)


def both_places(me, k, n_ctx):
    source = jnp.bitwise_xor(me, k)
    front = pl.multiple_of(source * BLOCK, BLOCK)
    back = pl.multiple_of((2 * n_ctx - 1 - source) * BLOCK, BLOCK)
    return pl.ds(front, BLOCK), pl.ds(back, BLOCK)


def attention_kernel(n_ctx, tile, scalar_ref, *refs):
    x_refs, o_refs, (qs, ks, vs, os) = refs[:n_ctx], refs[n_ctx : 2 * n_ctx], refs[2 * n_ctx :]
    me = scalar_ref[0]
    length = 2 * n_ctx * BLOCK
    for k in range(n_ctx):
        front, back = both_places(me, k, n_ctx)
        for which, dest in enumerate((qs, ks, vs)):
            dest[front, :] = x_refs[k][0, which, :BLOCK, :]
            dest[back, :] = x_refs[k][0, which, BLOCK:, :]
    factor = -(HD ** (-0.5)) * LOG2E
    shift = math.log(length) * LOG2E
    row_at = lax.broadcasted_iota(jnp.int32, (tile, tile), 0)
    col_at = lax.broadcasted_iota(jnp.int32, (tile, tile), 1)
    for i in range(length // tile):
        query = qs[i * tile : (i + 1) * tile, :]

        def part(j, masked):
            at = pl.ds(pl.multiple_of(j * tile, tile), tile)
            raw = times_transposed(query, ks[at, :])
            prob = 1.0 / (1.0 + jnp.exp2(raw * factor + shift))
            if masked:
                prob = jnp.where(row_at >= col_at, prob, 0.0)
            return dot(prob.astype(BF), vs[at, :])

        total = part(i, True)
        if i > 0:
            total = lax.fori_loop(0, i, lambda j, acc: acc + part(j, False), total)
        os[i * tile : (i + 1) * tile, :] = total.astype(BF)
    for k in range(n_ctx):
        front, back = both_places(me, k, n_ctx)
        o_refs[k][0, :BLOCK, :] = os[front, :]
        o_refs[k][0, BLOCK:, :] = os[back, :]


def attention_forward(scalars, pieces, n_ctx):
    pairs = pieces[0].shape[0]
    length = 2 * n_ctx * BLOCK
    tile = min(512, length)
    return pl.pallas_call(
        functools.partial(attention_kernel, n_ctx, tile),
        out_shape=[jax.ShapeDtypeStruct((pairs, PAIR, HD), BF)] * n_ctx,
        grid_spec=pltpu.PrefetchScalarGridSpec(
            num_scalar_prefetch=1,
            grid=(pairs,),
            in_specs=[pl.BlockSpec((1, 3, PAIR, HD), lambda i, s: (i, 0, 0, 0))] * n_ctx,
            out_specs=[pl.BlockSpec((1, PAIR, HD), lambda i, s: (i, 0, 0))] * n_ctx,
            scratch_shapes=[pltpu.VMEM((length, HD), BF)] * 4,
        ),
        compiler_params=params(),
        cost_estimate=pl.CostEstimate(
            flops=pairs * length * length * HD * 6,
            bytes_accessed=pairs * length * HD * 8,
            transcendentals=pairs * length * length,
        ),
    )(scalars, *pieces)


def attention_back_kernel(n_ctx, tile, scalar_ref, *refs):
    x_refs, g_refs, (cos_ref, sin_ref) = refs[:n_ctx], refs[n_ctx : 2 * n_ctx], refs[2 * n_ctx : 2 * n_ctx + 2]
    out_refs = refs[2 * n_ctx + 2 : 3 * n_ctx + 2]
    qs, ks, vs, gs, os, dqs = refs[3 * n_ctx + 2 :]
    me = scalar_ref[0]
    length = 2 * n_ctx * BLOCK
    for k in range(n_ctx):
        front, back = both_places(me, k, n_ctx)
        for which, dest in enumerate((qs, ks, vs)):
            dest[front, :] = x_refs[k][0, which, :BLOCK, :]
            dest[back, :] = x_refs[k][0, which, BLOCK:, :]
        gs[front, :] = g_refs[k][0, :BLOCK, :]
        gs[back, :] = g_refs[k][0, BLOCK:, :]
    scale = HD ** (-0.5)
    factor = -scale * LOG2E
    shift = math.log(length) * LOG2E
    count = length // tile
    key_at = lax.broadcasted_iota(jnp.int32, (tile, tile), 0)
    query_at = lax.broadcasted_iota(jnp.int32, (tile, tile), 1)
    dqs[...] = jnp.zeros_like(dqs)

    def unrotate(values, at):
        return (values * cos_ref[at, :] - pltpu.roll(values, HD // 2, 1) * sin_ref[at, :]).astype(BF)

    for j in range(count):
        own = slice(j * tile, (j + 1) * tile)
        keys = ks[own, :]
        values = vs[own, :]

        def part(i, masked):
            at = pl.ds(pl.multiple_of(i * tile, tile), tile)
            query = qs[at, :]
            grad = gs[at, :]
            raw = times_transposed(keys, query)
            prob = 1.0 / (1.0 + jnp.exp2(raw * factor + shift))
            if masked:
                prob = jnp.where(query_at >= key_at, prob, 0.0)
            prob_grad = times_transposed(values, grad)
            score_grad = (prob_grad * prob * (1.0 - prob)).astype(BF)
            dqs[at, :] += contract_rows(score_grad, keys)
            return dot(score_grad, query), dot(prob.astype(BF), grad)

        total = part(j, True)
        if j + 1 < count:

            def step(i, acc):
                more = part(i, False)
                return acc[0] + more[0], acc[1] + more[1]

            total = lax.fori_loop(j + 1, count, step, total)
        os[1, own, :] = unrotate(total[0] * scale, own)
        os[2, own, :] = total[1].astype(BF)
    for i in range(count):
        at = slice(i * tile, (i + 1) * tile)
        os[0, at, :] = unrotate(dqs[at, :] * scale, at)
    for k in range(n_ctx):
        front, back = both_places(me, k, n_ctx)
        for which in range(3):
            out_refs[k][0, which, :BLOCK, :] = os[which, front, :]
            out_refs[k][0, which, BLOCK:, :] = os[which, back, :]


def attention_backward(scalars, pieces, grads, cos_tab, sin_tab, n_ctx):
    pairs = pieces[0].shape[0]
    length = 2 * n_ctx * BLOCK
    tile = min(512, length)
    three = pl.BlockSpec((1, 3, PAIR, HD), lambda i, s: (i, 0, 0, 0))
    one = pl.BlockSpec((1, PAIR, HD), lambda i, s: (i, 0, 0))
    return pl.pallas_call(
        functools.partial(attention_back_kernel, n_ctx, tile),
        out_shape=[jax.ShapeDtypeStruct((pairs, 3, PAIR, HD), BF)] * n_ctx,
        grid_spec=pltpu.PrefetchScalarGridSpec(
            num_scalar_prefetch=1,
            grid=(pairs,),
            in_specs=[three] * n_ctx + [one] * n_ctx + [whole((length, HD))] * 2,
            out_specs=[three] * n_ctx,
            scratch_shapes=[pltpu.VMEM((length, HD), BF)] * 4
            + [pltpu.VMEM((3, length, HD), BF), pltpu.VMEM((length, HD), F32)],
        ),
        compiler_params=params(),
        cost_estimate=pl.CostEstimate(
            flops=pairs * length * length * HD * 12,
            bytes_accessed=pairs * length * HD * 14,
            transcendentals=pairs * length * length,
        ),
    )(scalars, *pieces, *grads, cos_tab, sin_tab)


def mlp_kernel(n_ref, g_ref, wg_ref, wu_ref, wd_ref, *rest):
    h_ref, dgp_ref, dup_ref = rest[-3:]
    rows = n_ref[...]
    gate_pre = dot(rows, wg_ref[...])
    up_pre = dot(rows, wu_ref[...])
    hidden_grad = times_transposed(g_ref[...], wd_ref[...])
    gate_sig = 1.0 / (1.0 + jnp.exp2(gate_pre * (-LOG2E)))
    gate_act = gate_pre * gate_sig
    h_ref[...] = (gate_act * up_pre).astype(BF)
    dup_ref[...] = (hidden_grad * gate_act).astype(BF)
    dgp_ref[...] = (hidden_grad * up_pre * (gate_sig * (1.0 + gate_pre * (1.0 - gate_sig)))).astype(BF)


def mlp_core(normed, grads, wg, wu, wd, total, first, held=()):
    rows, depth = normed.shape
    hidden = wg.shape[1]
    row_tile, tile = 512, 512
    skip = first // row_tile
    row_block = pl.BlockSpec((row_tile, depth), lambda j, i: (i, 0))
    out_block = pl.BlockSpec((row_tile, tile), lambda j, i: (i + skip, j))
    out = jax.ShapeDtypeStruct((total, hidden), BF)
    return pl.pallas_call(
        mlp_kernel,
        out_shape=(out, out, out),
        grid=(hidden // tile, rows // row_tile),
        in_specs=[
            row_block,
            row_block,
            pl.BlockSpec((depth, tile), lambda j, i: (0, j)),
            pl.BlockSpec((depth, tile), lambda j, i: (0, j)),
            pl.BlockSpec((tile, depth), lambda j, i: (j, 0)),
        ]
        + [pl.BlockSpec(memory_space=pl.ANY)] * len(held),
        out_specs=(out_block, out_block, out_block),
        input_output_aliases={5 + k: k for k in range(len(held))},
        compiler_params=params(),
        cost_estimate=pl.CostEstimate(
            flops=6 * rows * depth * hidden,
            bytes_accessed=rows * depth * 4 + 6 * depth * hidden + 6 * rows * hidden,
            transcendentals=rows * hidden,
        ),
    )(normed, grads, wg, wu, wd, *held)


def inverse_rms(values):
    return lax.rsqrt(jnp.mean(values * values, axis=-1, keepdims=True) + EPS)


def neighbours():
    index, rank = lax.axis_index("ctx"), lax.axis_index("tp")
    return (index, jnp.bitwise_xor(rank, 1)), (index, jnp.bitwise_xor(rank, 2))


def remote(source, dest, send_sem, recv_sem, device):
    return pltpu.make_async_remote_copy(
        src_ref=source,
        dst_ref=dest,
        send_sem=send_sem,
        recv_sem=recv_sem,
        device_id=device,
        device_id_type=pl.DeviceIdType.MESH,
    )


def signal(sem, device):
    pl.semaphore_signal(sem, inc=1, device_id=device, device_id_type=pl.DeviceIdType.MESH)


class Scatter:
    def __init__(self, partial, groups, bufs, sems, loaded=True):
        self.partial, self.groups, self.loaded = partial, groups, loaded
        self.from_x, self.from_y, self.for_y, self.for_x, self.low, self.high = bufs[:6]
        if loaded:
            self.stay, self.stay_y, self.stay_x = bufs[6:]
        self.first_send, self.first_recv, self.second_send, self.second_recv, self.load_sem = sems
        self.to_x, self.to_y = neighbours()

    @staticmethod
    def scratch(rows, width, loaded=True):
        dma = pltpu.SemaphoreType.DMA
        whole_rows, half_rows = pltpu.VMEM((rows, width), BF), pltpu.VMEM((rows // 2, width), BF)
        bufs = [whole_rows] * 2 + [half_rows] * 4 + ([whole_rows] + [half_rows] * 2 if loaded else [])
        return bufs + [dma((8,)), dma((8,)), dma((4,)), dma((4,)), dma((6,))]

    def piece(self, g, number):
        base, rows, own = self.groups[g]
        half = rows // 2
        if not self.loaded:
            return self.partial[pl.ds(base + number * half, half), :]
        if number < 2:
            return self.stay[pl.ds(own + number * half, half), :]
        return (self.stay_x if number == 3 else self.stay_y)[pl.ds(own // 2, half), :]

    def first_copies(self, g):
        base, rows, own = self.groups[g]
        half = rows // 2
        part = lambda number: self.partial.at[pl.ds(base + number * half, half)]
        at = lambda buf, number: buf.at[pl.ds(own + number * half, half)]
        plan = [
            (part(2), at(self.from_x, 0), self.to_x),
            (part(6), at(self.from_x, 1), self.to_x),
            (part(5), at(self.from_y, 0), self.to_y),
            (part(7), at(self.from_y, 1), self.to_y),
        ]
        return [
            remote(source, dest, self.first_send.at[4 * g + k], self.first_recv.at[4 * g + k], device)
            for k, (source, dest, device) in enumerate(plan)
        ]

    def loads(self, g):
        base, rows, own = self.groups[g]
        half = rows // 2
        copy = lambda number, count, dest, k: pltpu.make_async_copy(
            self.partial.at[pl.ds(base + number * half, count)], dest, self.load_sem.at[3 * g + k]
        )
        return [
            copy(0, rows, self.stay.at[pl.ds(own, rows)], 0),
            copy(4, half, self.stay_y.at[pl.ds(own // 2, half)], 1),
            copy(3, half, self.stay_x.at[pl.ds(own // 2, half)], 2),
        ]

    def second_copies(self, g):
        _, rows, own = self.groups[g]
        at = pl.ds(own // 2, rows // 2)
        return [
            remote(self.for_y.at[at], self.low.at[at], self.second_send.at[2 * g], self.second_recv.at[2 * g], self.to_y),
            remote(
                self.for_x.at[at], self.high.at[at], self.second_send.at[2 * g + 1], self.second_recv.at[2 * g + 1], self.to_x
            ),
        ]

    def start(self, g, which=(1, 3, 0, 2), loads=True):
        copies = self.first_copies(g)
        for k in which:
            copies[k].start()
        if loads:
            for copy in self.loads(g):
                copy.start()

    def forward(self, g):
        _, rows, own = self.groups[g]
        half = rows // 2
        copies = self.first_copies(g)
        copies[1].wait_recv()
        copies[3].wait_recv()
        if self.loaded:
            for copy in self.loads(g):
                copy.wait()
        at = pl.ds(own // 2, half)
        self.for_y[at, :] = add_low(self.piece(g, 4), self.from_x[pl.ds(own + half, half), :])
        self.for_x[at, :] = add_low(self.piece(g, 3), self.from_y[pl.ds(own + half, half), :])
        for copy in self.second_copies(g):
            copy.start()

    def total(self, g, use):
        _, rows, own = self.groups[g]
        half = rows // 2
        copies, seconds = self.first_copies(g), self.second_copies(g)
        copies[0].wait_recv()
        copies[2].wait_recv()
        for copy in copies:
            copy.wait_send()
        for copy in seconds:
            copy.wait()
        first = pl.ds(own, half)
        rest = pl.ds(own // 2, half)
        for side, (got, more) in enumerate(((self.from_x, self.low), (self.from_y, self.high))):
            at = pl.ds(own + side * half, half)
            use(at, self.piece(g, side).astype(F32) + got[first, :].astype(F32) + more[rest, :].astype(F32))


class Gather:
    def __init__(self, own, out, groups, sems, own_at=None, local=True):
        self.own, self.out, self.groups, self.has_local = own, out, groups, local
        self.own_at = own_at if own_at is not None else [group[2] for group in groups]
        self.first_send, self.first_recv, self.second_send, self.second_recv, self.local_sem = sems
        self.to_x, self.to_y = neighbours()

    @staticmethod
    def scratch():
        dma = pltpu.SemaphoreType.DMA
        return [dma((4,)), dma((4,)), dma((4,)), dma((4,)), dma((2,))]

    def first_copies(self, g):
        base, rows, _ = self.groups[g]
        source = self.own.at[pl.ds(self.own_at[g], rows)]
        place = lambda k: self.out.at[pl.ds(base + k * rows, rows)]
        return [
            remote(source, place(1), self.first_send.at[2 * g], self.first_recv.at[2 * g], self.to_x),
            remote(source, place(2), self.first_send.at[2 * g + 1], self.first_recv.at[2 * g + 1], self.to_y),
        ]

    def local(self, g):
        base, rows, _ = self.groups[g]
        return pltpu.make_async_copy(self.own.at[pl.ds(self.own_at[g], rows)], self.out.at[pl.ds(base, rows)], self.local_sem.at[g])

    def second_copies(self, g):
        base, rows, _ = self.groups[g]
        half = rows // 2
        part = lambda number: self.out.at[pl.ds(base + number * half, half)]
        return [
            remote(part(4), part(6), self.second_send.at[2 * g], self.second_recv.at[2 * g], self.to_x),
            remote(part(3), part(7), self.second_send.at[2 * g + 1], self.second_recv.at[2 * g + 1], self.to_y),
        ]

    def start(self, g):
        for copy in self.first_copies(g):
            copy.start()
        if self.has_local:
            self.local(g).start()

    def forward_x(self, g):
        self.first_copies(g)[0].wait_recv()
        self.second_copies(g)[1].start()

    def forward_y(self, g):
        self.first_copies(g)[1].wait_recv()
        self.second_copies(g)[0].start()

    def forward(self, g):
        self.forward_x(g)
        self.forward_y(g)
        if self.has_local:
            self.local(g).wait()

    def finish(self, g):
        for copy in self.second_copies(g):
            copy.wait_recv()

    def sent(self, g):
        for copy in self.first_copies(g) + self.second_copies(g):
            copy.wait_send()


TILE, ROWS = 128, 64
CORE_SLOTS, HOP_SLOTS = 4, 4


class Ring:
    def __init__(self, slots, send_sem, recv_sem, credit, total):
        self.slots, self.send_sem, self.recv_sem, self.credit, self.total = slots, send_sem, recv_sem, credit, total
        self.count = slots.shape[0]

    def copy(self, source, at, send_at, device):
        slot = lax.rem(at, self.count)
        return pltpu.make_async_remote_copy(
            src_ref=source,
            dst_ref=self.slots.at[slot],
            send_sem=self.send_sem.at[send_at],
            recv_sem=self.recv_sem.at[slot],
            device_id=device,
            device_id_type=pl.DeviceIdType.MESH,
        )

    def send(self, source, at, send_at, device):
        @pl.when(at >= self.count)
        def _():
            pl.semaphore_wait(self.credit, 1)

        self.copy(source, at, send_at, device).start()

    def sent(self, source, at, send_at, device):
        self.copy(source, at, send_at, device).wait_send()

    def arrived(self, source, at, send_at, device):
        self.copy(source, at, send_at, device).wait_recv()
        return self.slots.at[lax.rem(at, self.count)]

    def free(self, at, device):
        @pl.when(at + self.count < self.total)
        def _():
            pl.semaphore_signal(self.credit, inc=1, device_id=device, device_id_type=pl.DeviceIdType.MESH)


def sums_kernel(n_ctx, items, n_right, n_extra, tasks, late, *refs):
    n_left = len(items)
    left_refs, right_refs = refs[:n_left], refs[n_left : n_left + n_right]
    extra_in, refs = refs[n_left + n_right : n_left + n_right + n_extra[0]], refs[n_left + n_right + n_extra[0] :]
    out_refs, extra_out, refs = refs[:n_left], refs[n_left : n_left + n_extra[1]], refs[n_left + n_extra[1] :]
    extra_scratch, refs = refs[: n_extra[2]], refs[n_extra[2] :]
    right_refs = list(right_refs) + [extra_out[k] for k in late]
    n_right += len(late)
    (
        left_buf, right_buf, other_buf, ring, core_in, hop_in, hop_mid, hop_out, core_out,
        left_sem, right_sem, core_send, core_recv, in_send, in_recv, mid_send, mid_recv, out_send, out_recv,
        fin_send, fin_recv, store_sem, core_credit, in_credit, mid_credit, out_credit, fin_credit,
    ) = refs
    starts = [0]
    for _, _, chunks in items:
        starts.append(starts[-1] + chunks)
    total = starts[-1]
    n_ring = ring.shape[0]
    chips = n_ctx // 2
    mid = chips // 2
    index = lax.axis_index("ctx")
    rank = lax.axis_index("tp")
    core = lax.rem(index, 2)
    chip = index // 2
    low_side = chip < mid
    place = jnp.where(low_side, chip, chips - 1 - chip)
    toward = jnp.where(low_side, 1, -1)
    partner = (chip * 2 + 1 - core, rank)
    after = ((chip + toward) * 2 + core, rank)
    before = ((chip - toward) * 2 + core, rank)
    is_first = place == 0
    is_last = place == mid - 1
    lag_t = mid
    lag_u = lag_t + 2
    lag_o = lag_u + 2 * (mid - 1)
    lag_f = lag_o + 1
    lag_w = lag_f + 1

    if tasks is not None:
        greet(n_ctx, True)
    else:
        barrier = pltpu.get_barrier_semaphore()
        pl.semaphore_signal(barrier, inc=1, device_id=partner, device_id_type=pl.DeviceIdType.MESH)

        @pl.when(chip > 0)
        def _():
            pl.semaphore_signal(
                barrier, inc=1, device_id=((chip - 1) * 2 + core, rank), device_id_type=pl.DeviceIdType.MESH
            )

        @pl.when(chip < chips - 1)
        def _():
            pl.semaphore_signal(
                barrier, inc=1, device_id=((chip + 1) * 2 + core, rank), device_id_type=pl.DeviceIdType.MESH
            )

        pl.semaphore_wait(barrier, 1 + jnp.where(chip > 0, 1, 0) + jnp.where(chip < chips - 1, 1, 0))

    to_core = Ring(core_in, core_send, core_recv, core_credit, total)
    to_after = Ring(hop_in, in_send, in_recv, in_credit, total)
    across = Ring(hop_mid, mid_send, mid_recv, mid_credit, total)
    to_before = Ring(hop_out, out_send, out_recv, out_credit, total)
    to_final = Ring(core_out, fin_send, fin_recv, fin_credit, total)

    def right_copy(k):
        return pltpu.make_async_copy(right_refs[k], right_buf.at[k % 2], right_sem.at[k % 2])

    right_copy(0).start()

    def for_item(at, action):
        for number in range(n_left):
            @pl.when((at >= starts[number]) & (at < starts[number + 1]))
            def _(number=number):
                action(number, at - starts[number])

    def rows_at(number, chunk, side):
        half = items[number][2] * ROWS
        return pl.multiple_of(side * half + chunk * ROWS, ROWS)

    def left_copy(number, chunk, slot, which):
        side = core if which == 0 else 1 - core
        half = items[number][2] * ROWS
        return pltpu.make_async_copy(
            left_refs[number].at[:, pl.ds(pl.multiple_of(side * half + chunk // 2 * TILE, TILE), TILE)],
            left_buf.at[slot, which],
            left_sem.at[slot, which],
        )

    def load_left(at):
        def action(number, chunk):
            for which in range(2):
                left_copy(number, chunk, lax.rem(at // 2, 2), which).start()

        for_item(at, action)

    load_left(0)
    planned, each = tasks(extra_in, extra_out, extra_scratch) if tasks is not None else ({}, None)
    if 0 in planned:
        planned.pop(0)()
    if n_right > 1:
        right_copy(1).start()
    right_copy(0).wait()

    def step(i, carry):
        def at_lag(lag):
            at = i - lag
            return at, (at >= 0) & (at < total)

        at, now = at_lag(lag_w)

        @pl.when(now)
        def _():
            slot = lax.rem(at, n_ring)
            source = ring.at[slot]

            def action(number, chunk):
                store(number, chunk, at, 0).wait()
                store(number, chunk, at, 1).wait()

            for_item(at, action)
            to_final.sent(source, at, slot, partner)
            to_final.free(at, partner)

            @pl.when(jnp.logical_not(is_first))
            def _():
                to_before.sent(source, at, slot, before)

        at, now = at_lag(lag_o)

        @pl.when(now & jnp.logical_not(is_last))
        def _():
            slot = lax.rem(at, n_ring)
            source = ring.at[slot]
            to_after.sent(source, at, slot, after)
            got = to_before.arrived(source, at, slot, after)
            ring[slot] = got[...]
            to_before.free(at, after)

            @pl.when(jnp.logical_not(is_first))
            def _():
                to_before.send(source, at, slot, before)

        @pl.when(now)
        def _():
            slot = lax.rem(at, n_ring)
            to_final.send(ring.at[slot], at, slot, partner)

        at, now = at_lag(lag_u)

        @pl.when(now & is_last)
        def _():
            slot = lax.rem(at, n_ring)
            source = ring.at[slot]
            across.sent(source, at, slot, after)
            got = across.arrived(source, at, slot, after)
            ring[slot] = add_low(ring[slot], got[...])
            across.free(at, after)

            @pl.when(jnp.logical_not(is_first))
            def _():
                to_before.send(source, at, slot, before)

        at, now = at_lag(lag_t)

        @pl.when(now)
        def _():
            slot = lax.rem(at, n_ring)
            source = ring.at[slot]

            @pl.when(jnp.logical_not(is_first))
            def _():
                got = to_after.arrived(source, at, slot, before)
                ring[slot] = add_low(ring[slot], got[...])
                to_after.free(at, before)

            @pl.when(is_last)
            def _():
                across.send(source, at, slot, after)

            @pl.when(jnp.logical_not(is_first) & jnp.logical_not(is_last))
            def _():
                to_after.send(source, at, slot, after)

        at, now = at_lag(1)

        @pl.when(now)
        def _():
            slot = lax.rem(at, n_ring)
            source = ring.at[slot]
            own = other_buf.at[lax.rem(at, 4)]
            to_core.sent(own, at, lax.rem(at, 4), partner)
            got = to_core.arrived(own, at, lax.rem(at, 4), partner)
            ring[slot] = add_low(ring[slot], got[...])
            to_core.free(at, partner)

            @pl.when(is_first & jnp.logical_not(is_last))
            def _():
                to_after.send(source, at, slot, after)

        at, now = at_lag(lag_f)

        @pl.when(now)
        def _():
            slot = lax.rem(at, n_ring)
            to_final.arrived(ring.at[slot], at, slot, partner)

            def action(number, chunk):
                store(number, chunk, at, 0).start()
                store(number, chunk, at, 1).start()

            for_item(at, action)

        for when, task in planned.items():
            pl.when(i == when)(task)

        if each is not None:
            each(i)

        @pl.when((i + 2 < total) & (lax.rem(i, 2) == 0))
        def _():
            load_left(i + 2)

        @pl.when((i < total) & (lax.rem(i, 2) == 0))
        def _():
            slot = lax.rem(i // 2, 2)

            def action(number, chunk):
                which_right = items[number][1]
                if which_right > 0 and items[number - 1][1] != which_right:

                    @pl.when(chunk == 0)
                    def _():
                        right_copy(which_right).wait()

                if which_right > 0 and which_right + 1 < n_right:

                    @pl.when(chunk == items[number][2] // 2)
                    def _():
                        right_copy(which_right + 1).start()

                for which in range(2):
                    left_copy(number, chunk, slot, which).wait()
                right = right_buf.at[which_right % 2]
                product = contract_rows(left_buf[slot, 1], right[...]).astype(BF)
                for part in range(2):
                    place = lax.rem(i + part, 4)
                    other_buf[place] = product[part * ROWS : (part + 1) * ROWS]
                    to_core.send(other_buf.at[place], i + part, place, partner)
                product = contract_rows(left_buf[slot, 0], right[...]).astype(BF)
                for part in range(2):
                    ring[lax.rem(i + part, n_ring)] = product[part * ROWS : (part + 1) * ROWS]

            for_item(i, action)

        return carry

    def store(number, chunk, at, which):
        source = ring.at[lax.rem(at, n_ring)] if which == 0 else core_out.at[lax.rem(at, CORE_SLOTS)]
        side = core if which == 0 else 1 - core
        return pltpu.make_async_copy(
            source,
            out_refs[number].at[pl.ds(rows_at(number, chunk, side), ROWS), :],
            store_sem.at[which, lax.rem(at, 2)],
        )

    lax.fori_loop(0, total + lag_w, step, 0)


def weight_sums(items, rights, n_ctx, collective_id, extra=None, late=()):
    tokens, width = rights[0].shape
    shapes = [(k, right, left.shape[1] // 2 // ROWS) for k, (left, right) in enumerate(items)]
    mid = n_ctx // 4
    n_ring = mid + 2 + 2 * (mid - 1) + 4
    any_spec = pl.BlockSpec(memory_space=pl.ANY)
    args, arg_specs, outs, out_specs, scratch, tasks = extra if extra is not None else ([], [], [], [], [], None)
    counts = (len(args), len(outs), len(scratch))
    chunk = (ROWS, width)
    dma = pltpu.SemaphoreType.DMA
    return pl.pallas_call(
        functools.partial(sums_kernel, n_ctx, shapes, len(rights), counts, tasks, late),
        out_shape=[jax.ShapeDtypeStruct((left.shape[1], width), BF) for left, _ in items] + outs,
        in_specs=[any_spec] * (len(items) + len(rights)) + arg_specs,
        out_specs=[any_spec] * len(items) + out_specs,
        scratch_shapes=scratch
        + [
            pltpu.VMEM((2, 2, tokens, TILE), BF),
            pltpu.VMEM((min(2, len(rights) + len(late)), tokens, width), BF),
            pltpu.VMEM((4,) + chunk, BF),
            pltpu.VMEM((n_ring,) + chunk, BF),
            pltpu.VMEM((CORE_SLOTS,) + chunk, BF),
            pltpu.VMEM((HOP_SLOTS,) + chunk, BF),
            pltpu.VMEM((HOP_SLOTS,) + chunk, BF),
            pltpu.VMEM((HOP_SLOTS,) + chunk, BF),
            pltpu.VMEM((CORE_SLOTS,) + chunk, BF),
            dma((2, 2)),
            dma((2,)),
            dma((4,)),
            dma((CORE_SLOTS,)),
            dma((n_ring,)),
            dma((HOP_SLOTS,)),
            dma((n_ring,)),
            dma((HOP_SLOTS,)),
            dma((n_ring,)),
            dma((HOP_SLOTS,)),
            dma((n_ring,)),
            dma((CORE_SLOTS,)),
            dma((2, 2)),
        ]
        + [pltpu.SemaphoreType.REGULAR] * 5,
        compiler_params=pltpu.CompilerParams(
            vmem_limit_bytes=VMEM_LIMIT, collective_id=collective_id, has_side_effects=True
        ),
        cost_estimate=pl.CostEstimate(
            flops=sum(2 * left.shape[1] * tokens * width for left, _ in items),
            bytes_accessed=sum(2 * left.shape[1] * (tokens + width) for left, _ in items),
            transcendentals=0,
        ),
    )(*[left for left, _ in items], *rights, *args)


VMEM_SPEC = pl.BlockSpec(memory_space=pltpu.VMEM)
ANY_SPEC = pl.BlockSpec(memory_space=pl.ANY)


def norm_back_rows(values, gain, grad):
    inv = inverse_rms(values)
    unit = values * inv
    scaled = grad * gain
    back = (scaled - unit * jnp.mean(scaled * unit, axis=-1, keepdims=True)) * inv
    return back, jnp.sum(grad * unit, axis=0, keepdims=True)


def feed_tasks(groups, extra_in, extra_out, scratch):
    dgp_ref, dup_ref, wg_ref, wu_ref, residual, grads, gain = extra_in
    dr, da_all, gain_grad, d_ref = extra_out
    n = len(Scatter.scratch(16, 128))
    bufs, rest = scratch[:n], scratch[n:]
    weights, lefts, tile_out, weight_sem, left_sem, out_sem = rest[:6]
    da_own = bufs[0]
    scatter = Scatter(d_ref, groups, bufs[:9], bufs[9:])
    gather = Gather(da_own, da_all, groups, rest[6:])
    order = list(reversed(range(len(groups))))
    rows, columns = lefts.shape[2], weights.shape[1]
    row_tiles = dgp_ref.shape[0] // rows
    tiles = row_tiles * (d_ref.shape[1] // columns)

    def weight_copies(part):
        at = pl.ds(pl.multiple_of(part * columns, columns), columns)
        return [
            pltpu.make_async_copy(ref.at[at], weights.at[k], weight_sem.at[k]) for k, ref in enumerate((wg_ref, wu_ref))
        ]

    def left_copies(tile):
        at = pl.ds(pl.multiple_of(lax.rem(tile, row_tiles) * rows, rows), rows)
        slot = lax.rem(tile, 2)
        return [
            pltpu.make_async_copy(ref.at[at], lefts.at[slot, k], left_sem.at[slot, k])
            for k, ref in enumerate((dgp_ref, dup_ref))
        ]

    def out_copy(tile):
        slot = lax.rem(tile, 2)
        return pltpu.make_async_copy(
            tile_out.at[slot],
            d_ref.at[
                pl.ds(pl.multiple_of(lax.rem(tile, row_tiles) * rows, rows), rows),
                pl.ds(pl.multiple_of(tile // row_tiles * columns, columns), columns),
            ],
            out_sem.at[slot],
        )

    def begin():
        gain_grad[...] = jnp.zeros_like(gain_grad)
        for copy in weight_copies(0) + left_copies(0):
            copy.start()

    def each(i):
        @pl.when(i < tiles)
        def _():
            slot = lax.rem(i, 2)

            @pl.when(i + 1 < tiles)
            def _():
                for copy in left_copies(i + 1):
                    copy.start()

            @pl.when(lax.rem(i, row_tiles) == 0)
            def _():
                @pl.when(i > 0)
                def _():
                    for copy in weight_copies(i // row_tiles):
                        copy.start()

                for copy in weight_copies(i // row_tiles):
                    copy.wait()

            for copy in left_copies(i):
                copy.wait()
            total = times_transposed(lefts[slot, 0], weights[0]) + times_transposed(lefts[slot, 1], weights[1])

            @pl.when(i >= 2)
            def _():
                out_copy(i - 2).wait()

            tile_out[slot] = total.astype(BF)
            out_copy(i).start()

    def start():
        out_copy(tiles - 2).wait()
        out_copy(tiles - 1).wait()
        for g in order:
            scatter.start(g)

    def use(at, total):
        back, more = norm_back_rows(residual[at, :], gain[...], total)
        total_grad = grads[at, :].astype(F32) + back
        dr[at, :] = total_grad
        da_own[at, :] = total_grad.astype(BF)
        gain_grad[...] += more

    def spread(g):
        scatter.total(g, use)
        gather.start(g)

    def finish():
        for g in order:
            gather.finish(g)
            gather.sent(g)

    plan = {
        0: begin,
        tiles: start,
        tiles + 4: lambda: scatter.forward(order[0]),
        tiles + 7: lambda: scatter.forward(order[-1]),
        tiles + 8: lambda: spread(order[0]),
        tiles + 10: lambda: spread(order[-1]),
        tiles + 13: lambda: gather.forward(order[0]),
        tiles + 17: lambda: gather.forward(order[-1]),
        tiles + 23: finish,
    }
    return plan, each


def feed_extra(groups, dgp, dup, wg, wu, residual, grads, gain):
    rows, width = residual.shape
    tokens, hidden = dgp.shape
    dma = pltpu.SemaphoreType.DMA
    outs = [
        jax.ShapeDtypeStruct((rows, width), F32),
        jax.ShapeDtypeStruct((tokens, width), BF),
        jax.ShapeDtypeStruct((1, width), F32),
        jax.ShapeDtypeStruct((tokens, width), BF),
    ]
    scratch = (
        Scatter.scratch(rows, width)
        + [
            pltpu.VMEM((2, width // 2, hidden), BF),
            pltpu.VMEM((2, 2, PAIR, hidden), BF),
            pltpu.VMEM((2, PAIR, width // 2), BF),
            dma((2,)),
            dma((2, 2)),
            dma((2,)),
        ]
        + Gather.scratch()
    )
    return (
        [dgp, dup, wg, wu, residual, grads, gain],
        [ANY_SPEC] * 4 + [VMEM_SPEC] * 3,
        outs,
        [VMEM_SPEC, ANY_SPEC, VMEM_SPEC, ANY_SPEC],
        scratch,
        functools.partial(feed_tasks, groups),
    )


def input_tasks(n_ctx, groups, extra_in, extra_out, scratch):
    i_ref, rows_in, dr, gain, gain_two_grad = extra_in
    input_grad, gain_sums = extra_out
    n = len(Scatter.scratch(16, 128))
    scatter = Scatter(i_ref, groups, scratch[:9], scratch[9:n])
    gains, got_tp, got_ctx, send_tp, recv_tp, send_ctx, recv_ctx = scratch[n:]
    order = list(reversed(range(len(groups))))
    me, rank = lax.axis_index("ctx"), lax.axis_index("tp")

    def tp_hop(k):
        return remote(gains.at[k], got_tp.at[k], send_tp.at[k], recv_tp.at[k], neighbours()[k])

    def ctx_hop(k):
        place = gains.at[2]
        return remote(place, got_ctx.at[k], send_ctx.at[k], recv_ctx.at[k], (jnp.bitwise_xor(me, k), rank))

    def begin():
        gains[0] = jnp.zeros(gains.shape[1:], F32)
        gains[0, 8:9, :] = gain_two_grad[...]
        for g in order:
            scatter.start(g)

    def use(at, total):
        back, more = norm_back_rows(rows_in[at, :].astype(F32), gain[...], total)
        input_grad[at, :] = (dr[at, :] + back).astype(BF)
        gains[0, 0:1, :] += more

    def rest():
        scatter.total(order[-1], use)
        tp_hop(0).start()

    def second():
        tp_hop(0).wait()
        gains[1] = gains[0] + got_tp[0]
        tp_hop(1).start()

    def third():
        tp_hop(1).wait()
        gains[2] = gains[1] + got_tp[1]
        for k in range(1, n_ctx):
            ctx_hop(k).start()

    def finish():
        for k in range(1, n_ctx):
            ctx_hop(k).wait()
        got_ctx[0] = gains[2]
        total = got_ctx[jnp.bitwise_xor(me, 0)]
        for index in range(1, n_ctx):
            total = total + got_ctx[jnp.bitwise_xor(me, index)]
        gain_sums[...] = total

    return {
        0: begin,
        4: lambda: scatter.forward(order[0]),
        9: lambda: scatter.forward(order[-1]),
        10: lambda: scatter.total(order[0], use),
        13: rest,
        15: second,
        17: third,
        20: finish,
    }, None


def input_extra(n_ctx, groups, i_partial, rows_in, dr, gain, gain_two_grad):
    rows, width = rows_in.shape
    dma = pltpu.SemaphoreType.DMA
    outs = [jax.ShapeDtypeStruct((rows, width), BF), jax.ShapeDtypeStruct((16, width), F32)]
    return (
        [i_partial, rows_in, dr, gain, gain_two_grad],
        [ANY_SPEC] + [VMEM_SPEC] * 4,
        outs,
        [VMEM_SPEC] * 2,
        Scatter.scratch(rows, width)
        + [
            pltpu.VMEM((3, 16, width), F32),
            pltpu.VMEM((2, 16, width), F32),
            pltpu.VMEM((n_ctx, 16, width), F32),
            dma((2,)),
            dma((2,)),
            dma((n_ctx,)),
            dma((n_ctx,)),
        ],
        functools.partial(input_tasks, n_ctx, groups),
    )


class Exchange:
    def __init__(self, dest, sems, by_device):
        self.dest, self.by_device = dest, by_device
        self.send_sem, self.recv_sem, self.own_sem = sems
        self.n_ctx = dest.shape[1]
        self.me, self.rank = lax.axis_index("ctx"), lax.axis_index("tp")

    @staticmethod
    def scratch(units, n_ctx):
        dma = pltpu.SemaphoreType.DMA
        return [dma((units, n_ctx)), dma((units, n_ctx)), dma((units,))]

    def copy(self, source, unit, k):
        other = jnp.bitwise_xor(self.me, k)
        place = other if self.by_device else k
        return remote(
            source.at[unit, place],
            self.dest.at[unit, k],
            self.send_sem.at[unit, k],
            self.recv_sem.at[unit, k],
            (other, self.rank),
        )

    def own(self, source, unit):
        place = self.me if self.by_device else 0
        return pltpu.make_async_copy(source.at[unit, place], self.dest.at[unit, 0], self.own_sem.at[unit])

    def start(self, source, unit):
        for k in reversed(range(1, self.n_ctx)):
            self.copy(source, unit, k).start()
        self.own(source, unit).start()

    def start_some(self, source, unit, first, count):
        for k in reversed(range(self.n_ctx)):
            other = jnp.bitwise_xor(self.me, k)

            @pl.when((other >= first) & (other < first + count))
            def _(k=k):
                if k == 0:
                    self.own(source, unit).start()
                else:
                    self.copy(source, unit, k).start()

    def arrived(self, source, unit):
        for k in range(1, self.n_ctx):
            self.copy(source, unit, k).wait_recv()
        self.own(source, unit).wait()

    def sent(self, source, unit):
        for k in range(1, self.n_ctx):
            self.copy(source, unit, k).wait_send()


def greet(n_ctx, tp_too):
    index, rank = lax.axis_index("ctx"), lax.axis_index("tp")
    barrier = pltpu.get_barrier_semaphore()
    for k in range(1, n_ctx):
        signal(barrier, (jnp.bitwise_xor(index, k), rank))
    if tp_too:
        for device in neighbours():
            signal(barrier, device)
    pl.semaphore_wait(barrier, n_ctx - 1 + (2 if tp_too else 0))


def rotation(cos_tab, sin_tab, block_cos, block_sin):
    sign = jnp.where(lax.broadcasted_iota(jnp.int32, cos_tab.shape, 1) < HD // 2, -1.0, 1.0)
    return cos_tab * block_cos - sin_tab * block_sin, (sin_tab * block_cos + cos_tab * block_sin) * sign


def in_turn(count):
    return [count - 1] + list(range(count - 1))


def attend_rows(qs, ks, vs, os, tile):
    length = qs.shape[0]
    factor = -(HD ** (-0.5)) * LOG2E
    shift = math.log(length) * LOG2E
    row_at = lax.broadcasted_iota(jnp.int32, (tile, tile), 0)
    col_at = lax.broadcasted_iota(jnp.int32, (tile, tile), 1)
    for i in range(length // tile):
        query = qs[i * tile : (i + 1) * tile, :]

        def part(j, masked):
            at = pl.ds(pl.multiple_of(j * tile, tile), tile)
            raw = times_transposed(query, ks[at, :])
            prob = 1.0 / (1.0 + jnp.exp2(raw * factor + shift))
            if masked:
                prob = jnp.where(row_at >= col_at, prob, 0.0)
            return dot(prob.astype(BF), vs[at, :])

        total = part(i, True)
        if i > 0:
            total = lax.fori_loop(0, i, lambda j, acc: acc + part(j, False), total)
        os[i * tile : (i + 1) * tile, :] = total.astype(BF)


def forward_kernel(n_ctx, groups, units, tile, *refs):
    tokens_ref, cot_ref, gain_one, gain_two, wq_ref, wk_ref, wv_ref, wo_ref, cos_ref, sin_ref, bcos_ref, bsin_ref, valid_ref = refs[:13]
    n1_out, got_out, heads_out, residual, n2_out, cot_out = refs[13:19]
    x_ref, rows_buf, own_buf, send, got, o_send, o_got, tabs, qs, ks, vs, os = refs[19:31]
    rest = refs[31:]
    n_gather, n_exchange = len(Gather.scratch()), len(Exchange.scratch(1, 2))
    n1_sems, rest = rest[:n_gather], rest[n_gather:]
    n2_sems, rest = rest[:n_gather], rest[n_gather:]
    cot_sems, rest = rest[:n_gather], rest[n_gather:]
    x_sems, rest = rest[:n_exchange], rest[n_exchange:]
    o_sems, rest = rest[:n_exchange], rest[n_exchange:]
    (n1_sem, got_sem, load_sem), rest = rest[:3], rest[3:]
    me, rank = lax.axis_index("ctx"), lax.axis_index("tp")
    odd = lax.rem(rank, 2)
    heads = wq_ref.shape[1] // HD
    per_unit = n_ctx // heads
    own_at = [pl.multiple_of(odd * BLOCK, BLOCK), pl.multiple_of((1 - odd) * PAIR, BLOCK)]

    def load_x(g):
        _, rows, own = groups[g]
        return pltpu.make_async_copy(
            tokens_ref.at[pl.ds(own_at[g], rows)], x_ref.at[pl.ds(own, rows)], load_sem.at[g]
        )

    for g in range(2):
        load_x(g).start()
    greet(n_ctx, True)
    gather_one = Gather(own_buf, rows_buf, groups, n1_sems, local=False)
    gather_two = Gather(own_buf, n2_out, groups, n2_sems)
    gather_cot = Gather(cot_ref, cot_out, groups, cot_sems, own_at=own_at)
    scatter = Scatter(rows_buf, groups, rest[:6], rest[6:], loaded=False)
    trade = Exchange(got, x_sems, True)
    trade_back = Exchange(o_got, o_sems, False)

    def halves_of(u):
        return halves_at(odd if units[u][1] else 0)

    def normed(source, gain, at):
        values = source[at, :].astype(F32)
        return (values * inverse_rms(values) * gain[...]).astype(BF)

    def begin(g):
        base, rows, own = groups[g]
        load_x(g).wait()
        low = normed(x_ref, gain_one, pl.ds(own, rows))
        own_buf[pl.ds(own, rows), :] = low
        gather_one.start(g)
        rows_buf[pl.ds(base, rows), :] = low

    begin(0)
    for half, block in enumerate((me, 2 * n_ctx - 1 - me)):
        cos_part, sin_part = rotation(
            cos_ref[...], sin_ref[...], bcos_ref[pl.ds(block, 1), :], bsin_ref[pl.ds(block, 1), :]
        )
        tabs[0, half * BLOCK : (half + 1) * BLOCK, :] = cos_part
        tabs[1, half * BLOCK : (half + 1) * BLOCK, :] = sin_part

    def query(u, block):
        base, flipped = units[u]
        first, second = halves_of(u)
        at = pl.ds(base + block * PAIR, PAIR)
        rows = rows_buf[at, :]
        for which, w_ref in enumerate((wq_ref, wk_ref, wv_ref)):
            product = dot(rows, w_ref[...])
            for head in range(heads):
                part = product[:, head * HD : (head + 1) * HD]
                pair = block * heads + head
                for half, to in ((0, first), (1, second)):
                    piece = part[half * BLOCK : (half + 1) * BLOCK]
                    if which < 2:
                        piece = piece * tabs[0, to, :] + pltpu.roll(piece, HD // 2, 1) * tabs[1, to, :]
                    else:
                        piece = piece * valid_ref[pl.ds(base + block * PAIR + half * BLOCK, BLOCK), :]
                    send[u, pair, which, to, :] = piece.astype(BF)
        trade.start_some(send, u, block * heads, heads)

    store_n1 = pltpu.make_async_copy(rows_buf, n1_out, n1_sem)
    store_got = [pltpu.make_async_copy(got.at[u], got_out.at[u], got_sem.at[u]) for u in range(len(units))]

    query(0, 0)
    gather_one.forward_x(0)
    gather_one.forward_y(0)
    begin(1)
    query(0, 1)
    query(1, 0)
    gather_one.finish(0)
    query(1, 1)
    gather_one.forward(1)
    gather_one.finish(1)
    for g in range(2):
        gather_cot.start(g)
    query(2, 0)
    query(2, 1)
    store_n1.start()

    def attend(u):
        trade.arrived(send, u)
        store_got[u].start()
        for k in range(n_ctx):
            front, back = both_places(me, k, n_ctx)
            for which, dest in enumerate((qs, ks, vs)):
                dest[front, :] = got[u, k, which, :BLOCK, :]
                dest[back, :] = got[u, k, which, BLOCK:, :]
        attend_rows(qs, ks, vs, os, tile)
        for k in range(n_ctx):
            front, back = both_places(me, k, n_ctx)
            o_send[u, k, :BLOCK, :] = os[front, :]
            o_send[u, k, BLOCK:, :] = os[back, :]
        trade_back.start(o_send, u)

    def project(u):
        trade_back.arrived(o_send, u)
        base, _ = units[u]
        first, second = halves_of(u)
        for block in range(per_unit):
            at = pl.ds(base + block * PAIR, PAIR)
            low = valid_ref[at, :].astype(BF)
            for head in range(heads):
                place = jnp.bitwise_xor(me, block * heads + head)
                part = jnp.concatenate([o_got[u, place, first, :], o_got[u, place, second, :]], axis=0)
                heads_out[at, head * HD : (head + 1) * HD] = part * low
            rows_buf[at, :] = dot(heads_out[at, :], wo_ref[...]).astype(BF)

    def use(at, total):
        residual[at, :] = x_ref[at, :].astype(F32) + total
        own_buf[at, :] = normed(residual, gain_two, at)

    def finish_group(g):
        scatter.total(g, use)
        gather_two.start(g)

    attend(0)
    for g in range(2):
        gather_one.sent(g)
    store_n1.wait()
    attend(1)
    for g in range(2):
        gather_cot.forward(g)
    project(0)
    scatter.start(0, (0,), loads=False)
    project(1)
    scatter.start(0, (1, 3, 2), loads=False)
    attend(2)
    scatter.forward(0)
    project(2)
    scatter.start(1, loads=False)
    finish_group(0)
    scatter.forward(1)
    finish_group(1)
    gather_two.forward(0)
    gather_two.forward(1)
    for u in range(len(units)):
        trade.sent(send, u)
        trade_back.sent(o_send, u)
        store_got[u].wait()
    for g in range(2):
        gather_cot.finish(g)
        gather_two.finish(g)
        gather_two.sent(g)
        gather_cot.sent(g)


def forward_layer(tokens_in, cot_in, gain_one, gain_two, wq, wk, wv, wo, tables, valid, n_ctx, groups, units):
    rows, depth = tokens_in.shape
    width = wq.shape[1]
    tokens = valid.shape[0]
    length = 2 * n_ctx * BLOCK
    n_units = len(units)
    vmem = lambda shape, dtype=BF: pltpu.VMEM(shape, dtype)
    outs = [
        jax.ShapeDtypeStruct((tokens, depth), BF),
        jax.ShapeDtypeStruct((n_units, n_ctx, 3, PAIR, HD), BF),
        jax.ShapeDtypeStruct((tokens, width), BF),
        jax.ShapeDtypeStruct((rows, depth), F32),
        jax.ShapeDtypeStruct((tokens, depth), BF),
        jax.ShapeDtypeStruct((tokens, depth), BF),
    ]
    return pl.pallas_call(
        functools.partial(forward_kernel, n_ctx, groups, units, min(512, length)),
        out_shape=outs,
        in_specs=[ANY_SPEC, ANY_SPEC] + [VMEM_SPEC] * 11,
        out_specs=[ANY_SPEC, ANY_SPEC, VMEM_SPEC, VMEM_SPEC, ANY_SPEC, ANY_SPEC],
        scratch_shapes=[
            vmem((rows, depth)),
            vmem((tokens, depth)),
            vmem((rows, depth)),
            vmem((n_units, n_ctx, 3, PAIR, HD)),
            vmem((n_units, n_ctx, 3, PAIR, HD)),
            vmem((n_units, n_ctx, PAIR, HD)),
            vmem((n_units, n_ctx, PAIR, HD)),
            vmem((2, PAIR, HD), F32),
        ]
        + [vmem((length, HD))] * 4
        + Gather.scratch() * 3
        + Exchange.scratch(n_units, n_ctx) * 2
        + [pltpu.SemaphoreType.DMA, pltpu.SemaphoreType.DMA((n_units,)), pltpu.SemaphoreType.DMA((2,))]
        + Scatter.scratch(rows, depth, loaded=False),
        compiler_params=pltpu.CompilerParams(vmem_limit_bytes=VMEM_LIMIT, collective_id=3, has_side_effects=True),
        cost_estimate=pl.CostEstimate(
            flops=8 * tokens * depth * width, bytes_accessed=8 * tokens * depth, transcendentals=0
        ),
    )(tokens_in, cot_in, gain_one, gain_two, wq, wk, wv, wo, *tables, valid)


def attend_rows_back(qs, ks, vs, gs, os, dqs, cos_ref, sin_ref, tile):
    length = qs.shape[0]
    scale = HD ** (-0.5)
    factor = -scale * LOG2E
    shift = math.log(length) * LOG2E
    count = length // tile
    key_at = lax.broadcasted_iota(jnp.int32, (tile, tile), 0)
    query_at = lax.broadcasted_iota(jnp.int32, (tile, tile), 1)
    dqs[...] = jnp.zeros_like(dqs)

    def unrotate(values, at):
        return (values * cos_ref[at, :] - pltpu.roll(values, HD // 2, 1) * sin_ref[at, :]).astype(BF)

    for j in range(count):
        own = slice(j * tile, (j + 1) * tile)
        keys = ks[own, :]
        values = vs[own, :]

        def part(i, masked):
            at = pl.ds(pl.multiple_of(i * tile, tile), tile)
            query = qs[at, :]
            grad = gs[at, :]
            raw = times_transposed(keys, query)
            prob = 1.0 / (1.0 + jnp.exp2(raw * factor + shift))
            if masked:
                prob = jnp.where(query_at >= key_at, prob, 0.0)
            prob_grad = times_transposed(values, grad)
            score_grad = (prob_grad * prob * (1.0 - prob)).astype(BF)
            dqs[at, :] += contract_rows(score_grad, keys)
            return dot(score_grad, query), dot(prob.astype(BF), grad)

        total = part(j, True)
        if j + 1 < count:

            def step(i, acc):
                more = part(i, False)
                return acc[0] + more[0], acc[1] + more[1]

            total = lax.fori_loop(j + 1, count, step, total)
        os[1, own, :] = unrotate(total[0] * scale, own)
        os[2, own, :] = total[1].astype(BF)
    for i in range(count):
        at = slice(i * tile, (i + 1) * tile)
        os[0, at, :] = unrotate(dqs[at, :] * scale, at)


def middle_kernel(n_ctx, groups, units, tile, *refs):
    da_ref, got_ref, h_ref, residual_ref, wd_ref, wq_ref, wk_ref, wv_ref, wo_ref = refs[:9]
    cos_ref, sin_ref, bcos_ref, bsin_ref, valid_ref = refs[9:14]
    grad_ref, partial_out, output = refs[14:17]
    rows_buf, got, do_send, do_got, back_got, h_buf, wd_buf, res_buf, cos_full, sin_full = refs[17:27]
    qs, ks, vs, gs, os, dqs = refs[27:33]
    rest = refs[33:]
    back_send = got
    n_exchange = len(Exchange.scratch(1, 2))
    do_sems, back_sems, rest = rest[:n_exchange], rest[n_exchange : 2 * n_exchange], rest[2 * n_exchange :]
    (da_sem, got_sem, out_sem, h_sem, wd_sem, res_sem, y_sem), rest = rest[:7], rest[7:]
    me, rank = lax.axis_index("ctx"), lax.axis_index("tp")
    odd = lax.rem(rank, 2)
    heads = wq_ref.shape[1] // HD
    per_unit = n_ctx // heads
    unit_rows = per_unit * PAIR
    count = len(units)
    order = in_turn(count)

    def rows_of(u):
        return pl.ds(units[u][0], unit_rows)

    load_da = [pltpu.make_async_copy(da_ref.at[rows_of(u)], rows_buf.at[rows_of(u)], da_sem.at[u]) for u in range(count)]
    load_got = [pltpu.make_async_copy(got_ref.at[u], got.at[u], got_sem.at[u]) for u in range(count)]
    for u in order:
        load_da[u].start()
    for u in order:
        load_got[u].start()
    first_wd = pltpu.make_async_copy(wd_ref.at[:, pl.ds(0, wd_buf.shape[1])], wd_buf, wd_sem)
    first_wd.start()
    greet(n_ctx, True)
    scatter = Scatter(rows_buf, groups, rest[:6], rest[6:], loaded=False)
    trade = Exchange(do_got, do_sems, True)
    trade_back = Exchange(back_got, back_sems, False)

    for u in order:
        load_da[u].wait()
        base, flipped = units[u]
        first, second = halves_at(odd if flipped else 0)
        for block in range(per_unit):
            at = pl.ds(base + block * PAIR, PAIR)
            grad = times_transposed(rows_buf[at, :], wo_ref[...]).astype(BF)
            low = valid_ref[at, :].astype(BF)
            for head in range(heads):
                part = grad[:, head * HD : (head + 1) * HD] * low
                do_send[u, block * heads + head, first, :] = part[:BLOCK]
                do_send[u, block * heads + head, second, :] = part[BLOCK:]
        trade.start(do_send, u)
    for block in range(2 * n_ctx):
        at = slice(block * BLOCK, (block + 1) * BLOCK)
        cos_full[at, :], sin_full[at, :] = rotation(
            cos_ref[...], sin_ref[...], bcos_ref[block : block + 1, :], bsin_ref[block : block + 1, :]
        )
    for u in order:
        load_got[u].wait()

    def attend(turn, carry):
        u = lax.rem(turn + count - 1, count)
        trade.arrived(do_send, u)
        for k in range(n_ctx):
            front, back = both_places(me, k, n_ctx)
            for which, dest in enumerate((qs, ks, vs)):
                dest[front, :] = got[u, k, which, :BLOCK, :]
                dest[back, :] = got[u, k, which, BLOCK:, :]
            gs[front, :] = do_got[u, k, :BLOCK, :]
            gs[back, :] = do_got[u, k, BLOCK:, :]
        attend_rows_back(qs, ks, vs, gs, os, dqs, cos_full, sin_full, tile)
        for k in range(n_ctx):
            front, back = both_places(me, k, n_ctx)
            for which in range(3):
                back_send[u, k, which, :BLOCK, :] = os[which, front, :]
                back_send[u, k, which, BLOCK:, :] = os[which, back, :]
        trade_back.start(back_send, u)
        return carry

    lax.fori_loop(0, count, attend, 0)

    tiles = rows_buf.shape[0] // PAIR

    def tile_rows(tile):
        return pl.ds(pl.multiple_of(tile * PAIR, PAIR), PAIR)

    def load_h(step):
        slot = lax.rem(step, 2)
        return pltpu.make_async_copy(h_ref.at[tile_rows(lax.rem(step, tiles))], h_buf.at[slot], h_sem.at[slot])

    columns = wd_buf.shape[1]
    parts = rows_buf.shape[1] // columns

    def part_columns(part):
        return pl.ds(pl.multiple_of(part * columns, columns), columns)

    def load_wd(part):
        return pltpu.make_async_copy(wd_ref.at[:, part_columns(part)], wd_buf, wd_sem)

    load_h(0).start()

    def down(step, carry):
        part, tile = step // tiles, lax.rem(step, tiles)

        @pl.when(step + 1 < tiles * parts)
        def _():
            load_h(step + 1).start()

        @pl.when(tile == 0)
        def _():
            @pl.when(part > 0)
            def _():
                load_wd(part).start()

            load_wd(part).wait()

        load_h(step).wait()
        rows_buf[tile_rows(tile), part_columns(part)] = dot(h_buf[lax.rem(step, 2)], wd_buf[...]).astype(BF)
        return carry

    lax.fori_loop(0, tiles * parts, down, 0)
    last_group = len(groups) - 1
    out_rows = rest[0]
    for g in (last_group, 0):
        scatter.start(g, loads=False)

    def use(at, total):
        size = total.shape[0]
        load = pltpu.make_async_copy(residual_ref.at[at], res_buf.at[pl.ds(0, size)], res_sem)
        load.start()
        load.wait()
        low = (res_buf[:size, :] + total).astype(BF)
        out_rows[at, :] = low

    def store(number, first):
        slot = number % 2
        return pltpu.make_async_copy(h_buf.at[slot], partial_out.at[pl.ds(first, PAIR)], out_sem.at[slot])

    stored = []
    for turn, u in enumerate(order):
        trade_back.arrived(back_send, u)
        base, flipped = units[u]
        first, second = halves_at(odd if flipped else 0)
        for block in range(per_unit):
            at = pl.ds(base + block * PAIR, PAIR)
            low = valid_ref[at, :].astype(BF)
            total = None
            for which, w_ref in enumerate((wq_ref, wk_ref, wv_ref)):
                width = heads * HD
                for head in range(heads):
                    place = jnp.bitwise_xor(me, block * heads + head)
                    part = jnp.concatenate(
                        [back_got[u, place, which, first, :], back_got[u, place, which, second, :]], axis=0
                    )
                    columns = slice(which * width + head * HD, which * width + (head + 1) * HD)
                    grad_ref[at, columns] = part * low if which == 2 else part
                product = times_transposed(grad_ref[at, which * width : (which + 1) * width], w_ref[...])
                total = product if total is None else total + product
            number = len(stored)
            if number >= 2:
                stored[number - 2].wait()
            h_buf[number % 2] = total.astype(BF)
            stored.append(store(number, base + block * PAIR))
            stored[-1].start()
        if turn == 0:
            scatter.forward(last_group)
            scatter.forward(0)
        if turn == 1:
            for g in (last_group, 0):
                scatter.total(g, use)
            store_y = pltpu.make_async_copy(out_rows, output, y_sem)
            store_y.start()
    store_y.wait()
    for copy in stored[-2:]:
        copy.wait()
    for u in order:
        trade.sent(do_send, u)
        trade_back.sent(back_send, u)


def middle_layer(da, got, h, residual, wq, wk, wv, wo, wd, tables, valid, n_ctx, groups, units):
    tokens, depth = da.shape
    width = wq.shape[1]
    length = 2 * n_ctx * BLOCK
    count = len(units)
    vmem = lambda shape, dtype=BF: pltpu.VMEM(shape, dtype)
    dma = pltpu.SemaphoreType.DMA
    three, one = (count, n_ctx, 3, PAIR, HD), (count, n_ctx, PAIR, HD)
    most_rows = max(rows for _, rows, _ in groups) // 2
    return pl.pallas_call(
        functools.partial(middle_kernel, n_ctx, groups, units, min(512, length)),
        out_shape=[
            jax.ShapeDtypeStruct((tokens, 3 * width), BF),
            jax.ShapeDtypeStruct((tokens, depth), BF),
            jax.ShapeDtypeStruct(residual.shape, BF),
        ],
        in_specs=[ANY_SPEC] * 5 + [VMEM_SPEC] * 9,
        out_specs=[VMEM_SPEC, ANY_SPEC, ANY_SPEC],
        scratch_shapes=[vmem((tokens, depth)), vmem(three), vmem(one), vmem(one), vmem(three)]
        + [vmem((2, PAIR, depth)), vmem((h.shape[1], depth // 2)), vmem((most_rows, depth), F32)]
        + [vmem((length, HD), F32)] * 2
        + [vmem((length, HD))] * 4
        + [vmem((3, length, HD)), vmem((length, HD), F32)]
        + Exchange.scratch(count, n_ctx) * 2
        + [dma((count,)), dma((count,)), dma((2,)), dma((2,)), dma, dma, dma]
        + Scatter.scratch(residual.shape[0], depth, loaded=False),
        compiler_params=pltpu.CompilerParams(vmem_limit_bytes=VMEM_LIMIT, collective_id=4, has_side_effects=True),
        cost_estimate=pl.CostEstimate(
            flops=8 * tokens * depth * width + 2 * tokens * depth * h.shape[1],
            bytes_accessed=8 * tokens * depth,
            transcendentals=0,
        ),
    )(da, got, h, residual, wd, wq, wk, wv, wo, *tables, valid)


def body(
    tokens,
    counts,
    norm_gain,
    w_query,
    w_key,
    w_value,
    w_output,
    mlp_gain,
    w_gate,
    w_up,
    w_down,
    cotangent,
):
    n_ctx = lax.axis_size("ctx")
    me = lax.axis_index("ctx")
    rank = lax.axis_index("tp")
    odd = rank & 1
    core = me & 1
    length = 2 * BLOCK * n_ctx
    heads = w_query.shape[1] // HD
    gain_one = norm_gain.astype(F32)
    gain_two = mlp_gain.astype(F32)

    inverse = THETA ** (-(jnp.arange(HD // 2, dtype=F32) * (2.0 / HD)))
    angles = jnp.arange(length, dtype=jnp.int32).astype(F32)[:, None] * inverse[None, :]
    cos_half, sin_half = jnp.cos(angles), jnp.sin(angles)
    cos_full = jnp.concatenate([cos_half, cos_half], axis=1)
    sin_full = jnp.concatenate([-sin_half, sin_half], axis=1)

    def own_blocks(table):
        front = lax.dynamic_slice_in_dim(table, me * BLOCK, BLOCK, 0)
        back = lax.dynamic_slice_in_dim(table, (2 * n_ctx - 1 - me) * BLOCK, BLOCK, 0)
        return front, back

    cos_front, cos_back = own_blocks(cos_full)
    sin_front, sin_back = own_blocks(sin_full)
    own_counts = lax.dynamic_index_in_dim(counts, me, 0, keepdims=False)
    offsets = jnp.arange(BLOCK, dtype=jnp.int32)

    def valid_of(sequence_list, half_list):
        held = own_counts[jnp.stack(sequence_list), jnp.stack(half_list)]
        return (offsets[None, :] < held[:, None]).astype(F32).reshape(-1)

    cos_own = jnp.concatenate([cos_front, cos_back])
    sin_own = jnp.concatenate([sin_front, sin_back])
    sequences = counts.shape[1]
    paired = by_four() and sequences == 6 and n_ctx == 2 * heads
    if paired:
        ranks = [rank ^ k for k in range(4)]
        blocks_a = [(3 * (r >> 1) + 2 * (r & 1), jnp.int32(half)) for r in ranks for half in range(2)]
        blocks_b = [(1 + 3 * (r >> 1), r & 1) for r in ranks]
        flat_valid = valid_of(*zip(*(blocks_a + blocks_b)))
        valids = {"b": flat_valid[len(blocks_a) * BLOCK :], "a": flat_valid[: len(blocks_a) * BLOCK]}
        flip_back = lambda own: jnp.where(odd == 1, jnp.roll(own, BLOCK, axis=0), own)
        tables = {
            "b": (jnp.tile(flip_back(cos_own), (2, 1)), jnp.tile(flip_back(sin_own), (2, 1))),
            "a": (jnp.tile(cos_own, (4, 1)), jnp.tile(sin_own, (4, 1))),
        }
        scalars = {"b": jnp.stack([me, odd]).astype(jnp.int32), "a": jnp.stack([me, 0]).astype(jnp.int32)}
        n_pairs = {"b": 2 * heads, "a": 4 * heads}
    else:
        flat_valid = (offsets[None, None, :] < own_counts[:, :, None]).astype(F32).reshape(-1)
        valids = {"a": flat_valid}
        tables = {"a": (jnp.tile(cos_own, (sequences, 1)), jnp.tile(sin_own, (sequences, 1)))}
        scalars = {"a": jnp.stack([me, 0]).astype(jnp.int32)}
        n_pairs = {"a": sequences * heads}
    names = tuple(n_pairs)

    def own_rows(array):
        if not paired:
            return {"a": array}
        return {
            "b": lax.dynamic_slice_in_dim(array, (1 - odd) * PAIR, BLOCK, 0),
            "a": lax.dynamic_slice_in_dim(array, odd * BLOCK, PAIR, 0),
        }

    def whole_rows(array):
        return jnp.where(odd == 1, jnp.roll(array, BLOCK, axis=0), array) if paired else array

    x_own = {name: rows.astype(F32) for name, rows in own_rows(tokens[0]).items()}
    g_own = own_rows(cotangent[0])

    split = by_four()
    rows_of = {name: valids[name].shape[0] for name in names}
    total_rows = sum(rows_of.values())
    first_row = {"a": 0, "b": rows_of["a"]}
    valid_head = {name: jnp.broadcast_to(valids[name][:, None], (rows_of[name], HD)) for name in names}
    valid_wide = {name: jnp.broadcast_to(valids[name][:, None].astype(BF), (rows_of[name], heads * HD)) for name in names}
    near = [k for k in range(n_ctx) if k < 6]
    far = [k for k in range(n_ctx) if k >= 6]
    state = {}

    def fence():
        names_held = list(state)
        values = lax.optimization_barrier([state[name] for name in names_held])
        state.update(zip(names_held, values))

    def only_b(step):
        if "b" in names:
            step("b")

    def norm_one(n):
        state["n1", n] = (x_own[n] * inverse_rms(x_own[n]) * gain_one).astype(BF)

    def gather_a(key):
        def step(n):
            state[key, n] = gather_first(state[key, n])

        return step

    def gather_b(key):
        def step(n):
            state[key, n] = gather_second(state[key, n])

        return step

    def query(n):
        state["n1", n] = gathered(state["n1", n])
        cos_tab, sin_tab = tables[n]
        state["qkv", n] = project_qkv(
            scalars[n], state["n1", n], w_query, w_key, w_value, cos_tab, sin_tab, valid_head[n], n_ctx
        )

    def swap_part(key, places, to):
        def step(n):
            got = dict(state.get((to, n), {}))
            got.update(exchange(state[key, n], places, n_ctx))
            state[to, n] = got
            if len(got) == n_ctx:
                state[to, n] = [got[k] for k in range(n_ctx)]
                del state[key, n]

        return step

    def attend(n):
        state["mixed", n] = attention_forward(scalars[n], state["got", n], n_ctx)

    def project(n):
        heads_out, *parts = project_out(
            scalars[n], state.pop(("back", n)), w_output, valid_wide[n], n_pairs[n], n_ctx, split
        )
        state["heads", n], state["r", n] = heads_out, tuple(parts)

    def scatter_a(key):
        def step(n):
            state[key, n] = scatter_first(state[key, n])

        return step

    def scatter_b(key):
        def step(n):
            state[key, n] = scatter_second(state[key, n])

        return step

    def norm_two(n):
        residual = x_own[n] + scattered(state.pop(("r", n)))
        state["residual", n] = residual
        state["n2", n] = (residual * inverse_rms(residual) * gain_two).astype(BF)

    def core_mlp(n):
        state["n2", n] = gathered(state["n2", n])
        state["cot", n] = gathered(state["cot", n])
        held = state.get("mlp", ())
        state["mlp"] = mlp_core(
            state["n2", n], state["cot", n], w_gate, w_up, w_down, total_rows, first_row[n], held
        )

    def attend_back(n):
        state["dqkv", n] = attention_backward(
            scalars[n], state.pop(("got", n)), state.pop(("gdo", n)), cos_full, sin_full, n_ctx
        )

    def query_back(n):
        dq, dk, dv, *parts = project_in(
            scalars[n], state.pop(("gdqkv", n)), (w_query, w_key, w_value), valid_wide[n], n_pairs[n], n_ctx, False
        )
        state["dq", n], state["dk", n], state["dv", n], state["i", n] = dq, dk, dv, parts[0]

    def joined(key):
        parts = [state[key, n] for n in ("a", "b") if n in names]
        return jnp.concatenate(parts) if len(parts) > 1 else parts[0]

    groups = tuple((first_row[n], rows_of[n] // 4, first_row[n] // 4) for n in ("a", "b") if n in names)

    def own_order(array):
        return jnp.where(odd == 1, jnp.roll(array, -BLOCK, axis=0), array) if paired else array

    own_grads, own_rows_in = own_order(cotangent[0]), own_order(tokens[0])
    if paired:
        units = ((0, False), (2 * PAIR, False), (4 * PAIR, True))
        wide_valid = jnp.broadcast_to(flat_valid[:, None], (total_rows, HD))
        twice = lambda table: jnp.concatenate([table, table], axis=1)
        starts = BLOCK * jnp.arange(2 * n_ctx, dtype=jnp.int32)
        spans = [at.astype(F32)[:, None] * inverse[None, :] for at in (offsets, starts)]
        turns = [twice(part(angle)) for angle in spans for part in (jnp.cos, jnp.sin)]
        all_n1, got, heads_out, own_residual, all_n2, all_cot = forward_layer(
            tokens[0], cotangent[0], gain_one[None], gain_two[None], w_query, w_key, w_value, w_output,
            turns, wide_valid, n_ctx, groups, units,
        )
    else:
        norm_one("a")
        state["cot", "a"] = g_own["a"]
        gather_a("n1")("a")
        query("a")
        swap_part("qkv", range(n_ctx), "got")("a")
        attend("a")
        swap_part("mixed", range(n_ctx), "back")("a")
        project("a")
        scatter_a("r")("a")
        norm_two("a")
        gather_a("n2")("a")
        gather_a("cot")("a")
        all_n1, all_n2, all_cot = state["n1", "a"], gathered(state["n2", "a"]), gathered(state["cot", "a"])
        heads_out, own_residual = state["heads", "a"], state["residual", "a"]
    h, dgp, dup = mlp_core(all_n2, all_cot, w_gate, w_up, w_down, total_rows, 0)
    if paired:
        extra = feed_extra(groups, dgp, dup, w_gate, w_up, own_residual, own_grads, gain_two[None])
        sum_down, sum_gate, sum_up, sum_out, dr, da, gain_two_grad, _ = weight_sums(
            [(h, 0), (all_n2, 1), (all_n2, 2), (heads_out, 3)], [all_cot, dgp, dup], n_ctx, 1, extra, late=(1,)
        )
        dqkv, i_partial, output = middle_layer(
            da, got, h, own_residual, w_query, w_key, w_value, w_output, w_down, turns, wide_valid, n_ctx, groups, units
        )
        extra = input_extra(n_ctx, groups, i_partial, own_rows_in, dr, gain_one[None], gain_two_grad)
        sum_qkv, input_grad, gain_sums = weight_sums([(all_n1, 0)], [dqkv], n_ctx, 2, extra)
        gains = gain_sums[::8]
    else:
        d_partial = (times_transposed(dgp, w_gate) + times_transposed(dup, w_up)).astype(BF)
        y_partial = dot(h, w_down).astype(BF)
        (sum_down,) = weight_sums([(h, 0)], [all_cot], n_ctx, 1)
        sum_gate, sum_up = weight_sums([(all_n2, 0), (all_n2, 1)], [dgp, dup], n_ctx, 2)
        back, gain_two_grad = norm_back_rows(own_residual, gain_two, scattered(scatter_first((d_partial,))))
        dr = own_grads.astype(F32) + back
        da = gathered(gather_first(dr.astype(BF)))
        output = (own_residual + scattered(scatter_first((y_partial,)))).astype(BF)
        state["do", "a"] = heads_back(scalars["a"], da, w_output, valid_wide["a"], n_ctx)
        swap_part("do", range(n_ctx), "gdo")("a")
        attend_back("a")
        swap_part("dqkv", range(n_ctx), "gdqkv")("a")
        query_back("a")
        (sum_out,) = weight_sums([(heads_out, 0)], [da], n_ctx, 3)
        (sum_qkv,) = weight_sums(
            [(all_n1, 0)], [jnp.concatenate([state[key, "a"] for key in ("dq", "dk", "dv")], axis=1)], n_ctx, 4
        )
        back, gain_one_grad = norm_back_rows(x_own["a"], gain_one, scattered(scatter_first((state["i", "a"],))))
        input_grad = (dr + back).astype(BF)
    grad_query, grad_key, grad_value = (part.astype(F32) for part in jnp.split(sum_qkv, 3, axis=1))
    if not paired:
        gains = lax.psum(jnp.concatenate([gain_one_grad, gain_two_grad]), ("ctx", "tp"))
    return (
        whole_rows(output)[None],
        whole_rows(input_grad)[None],
        gains[0],
        grad_query,
        grad_key,
        grad_value,
        sum_out.astype(F32),
        gains[1],
        sum_gate.astype(F32),
        sum_up.astype(F32),
        sum_down.astype(F32),
    )


def solution(mesh):
    placed = (
        P("ctx", "tp", None),
        P(),
        P(),
        P(None, "tp"),
        P(None, "tp"),
        P(None, "tp"),
        P("tp", None),
        P(),
        P(None, "tp"),
        P(None, "tp"),
        P("tp", None),
        P("ctx", "tp", None),
    )
    return jax.shard_map(
        body,
        mesh=mesh,
        in_specs=placed,
        out_specs=(
            P("ctx", "tp", None),
            P("ctx", "tp", None),
            P(),
            P(None, "tp"),
            P(None, "tp"),
            P(None, "tp"),
            P("tp", None),
            P(),
            P(None, "tp"),
            P(None, "tp"),
            P("tp", None),
        ),
        check_vma=False,
    )
```

```python
import functools
import math

import jax
import jax.numpy as jnp
from jax import lax
from jax.experimental import pallas as pl
from jax.experimental.pallas import tpu as pltpu
from jax.sharding import PartitionSpec as P

HD = 128
BLOCK = 128
PAIR = 2 * BLOCK
EPS = 1e-05
THETA = 10000.0
LOG2E = 1.4426950408889634
BF = jnp.bfloat16
F32 = jnp.float32
VMEM_LIMIT = 60 * 1024 * 1024

X_SWAP = [(i, i ^ 1) for i in range(4)]
Y_SWAP = [(i, i ^ 2) for i in range(4)]


def dot(left, right):
    return jnp.dot(left, right, preferred_element_type=F32)


def contract_rows(left, right):
    return lax.dot_general(left, right, (((0,), (0,)), ((), ())), preferred_element_type=F32)


def times_transposed(left, right):
    return lax.dot_general(left, right, (((1,), (1,)), ((), ())), preferred_element_type=F32)


def send_x(values):
    return lax.ppermute(values, "tp", X_SWAP)


def send_y(values):
    return lax.ppermute(values, "tp", Y_SWAP)


def by_four():
    return lax.axis_size("tp") == 4


def gather_first(own):
    if not by_four():
        return (lax.all_gather(own, "tp", axis=0, tiled=True),)
    return own, send_x(own), send_y(own)


def gather_second(held):
    if len(held) == 1:
        return held
    own, from_x, from_y = held
    half = own.shape[0] // 2
    return own, from_x, from_y, send_x(from_y[:half]), send_y(from_x[half:])


def gathered(held):
    return jnp.concatenate(held) if len(held) > 1 else held[0]


def scatter_parts(partial):
    if not by_four():
        return (partial,)
    rows = partial.shape[0] // 4
    half = rows // 2
    at = lambda first: partial[first * half : (first + 1) * half]
    return (
        jnp.concatenate([at(2), at(6)]),
        jnp.concatenate([at(5), at(7)]),
        jnp.concatenate([at(0), at(1), at(4), at(3)]),
    )


def scatter_first(parts):
    if len(parts) == 1:
        return (lax.psum_scatter(parts[0], "tp", scatter_dimension=0, tiled=True),)
    return send_x(parts[0]), send_y(parts[1]), parts[2]


def add_low(left, right):
    return (left.astype(F32) + right.astype(F32)).astype(BF)


def scatter_second(held):
    if len(held) == 1:
        return held
    from_x, from_y, stay = held
    half = from_x.shape[0] // 2
    low_rest = send_y(add_low(stay[2 * half : 3 * half], from_x[half:]))
    high_rest = send_x(add_low(stay[3 * half :], from_y[half:]))
    return from_x, from_y, stay, low_rest, high_rest


def scattered(held):
    if len(held) == 1:
        return held[0].astype(F32)
    from_x, from_y, stay, low_rest, high_rest = (part.astype(F32) for part in held)
    half = low_rest.shape[0]
    low = stay[:half] + from_x[:half] + low_rest
    high = stay[half : 2 * half] + from_y[:half] + high_rest
    return jnp.concatenate([low, high])


def exchange(pieces, places, n_ctx):
    got = {}
    for k in places:
        got[k] = pieces[k] if k == 0 else lax.ppermute(pieces[k], "ctx", [(i, i ^ k) for i in range(n_ctx)])
    return got


def params():
    return pltpu.CompilerParams(vmem_limit_bytes=VMEM_LIMIT)


def whole(shape):
    return pl.BlockSpec(shape, lambda *_: (0,) * len(shape))


def put_partial(refs, first, value, rows):
    if len(refs) == 1:
        refs[0][first : first + value.shape[0], :] = value
        return
    to_x, to_y, stay = refs
    half = rows // 2
    homes = {
        0: (stay, 0), 1: (stay, 1), 2: (to_x, 0), 3: (stay, 3), 4: (stay, 2), 5: (to_y, 0), 6: (to_x, 1), 7: (to_y, 1)
    }
    for part in range(value.shape[0] // half):
        ref, place = homes[first // half + part]
        ref[place * half : (place + 1) * half, :] = value[part * half : (part + 1) * half]


def partial_shapes(rows, width, split):
    if not split:
        return [jax.ShapeDtypeStruct((rows, width), BF)]
    return [jax.ShapeDtypeStruct((rows // 4, width), BF)] * 2 + [jax.ShapeDtypeStruct((rows // 2, width), BF)]


def per_device(pairs, n_ctx):
    return -(-pairs // n_ctx)


def halves_at(swap):
    first = pl.multiple_of(swap * BLOCK, BLOCK)
    second = pl.multiple_of((1 - swap) * BLOCK, BLOCK)
    return pl.ds(first, BLOCK), pl.ds(second, BLOCK)


def qkv_kernel(n_ctx, pairs, scalar_ref, n_ref, wq_ref, wk_ref, wv_ref, cos_ref, sin_ref, valid_ref, *rest):
    out_refs, buffer = rest[:n_ctx], rest[n_ctx]
    rows = n_ref[...]
    first, second = halves_at(scalar_ref[1])
    me = scalar_ref[0]
    cos_tab = cos_ref[...]
    sin_tab = sin_ref[...]
    heads = wq_ref.shape[1] // HD
    step = pl.program_id(0)
    per = out_refs[0].shape[0]
    for pair in range(pairs, per * n_ctx):
        buffer[pair] = jnp.zeros(buffer.shape[1:], BF)
    for which, w_ref in enumerate((wq_ref, wk_ref, wv_ref)):
        product = dot(rows, w_ref[...])
        for head in range(heads):
            part = product[:, head * HD : (head + 1) * HD]
            if which < 2:
                part = part * cos_tab + pltpu.roll(part, HD // 2, 1) * sin_tab
            else:
                part = part * valid_ref[...]
            part = part.astype(BF)
            buffer[step * heads + head, which, first, :] = part[:BLOCK]
            buffer[step * heads + head, which, second, :] = part[BLOCK:]

    @pl.when(step == pl.num_programs(0) - 1)
    def _():
        for k in range(n_ctx):
            source = jnp.bitwise_xor(me, k)
            for p in range(per):
                out_refs[k][p] = buffer[source * per + p]


def project_qkv(scalars, normed, wq, wk, wv, cos_tab, sin_tab, valid, n_ctx):
    rows, depth = normed.shape
    width = wq.shape[1]
    heads = width // HD
    steps = rows // PAIR
    per = per_device(steps * heads, n_ctx)
    row_block = pl.BlockSpec((PAIR, HD), lambda i, s: (i, 0))
    weight = whole((depth, width))
    piece = (per, 3, PAIR, HD)
    return pl.pallas_call(
        functools.partial(qkv_kernel, n_ctx, steps * heads),
        out_shape=[jax.ShapeDtypeStruct(piece, BF)] * n_ctx,
        grid_spec=pltpu.PrefetchScalarGridSpec(
            num_scalar_prefetch=1,
            grid=(steps,),
            in_specs=[
                pl.BlockSpec((PAIR, depth), lambda i, s: (i, 0)),
                weight,
                weight,
                weight,
                row_block,
                row_block,
                row_block,
            ],
            out_specs=[whole(piece)] * n_ctx,
            scratch_shapes=[pltpu.VMEM((per * n_ctx, 3, PAIR, HD), BF)],
        ),
        compiler_params=params(),
        cost_estimate=pl.CostEstimate(
            flops=6 * rows * depth * width, bytes_accessed=rows * depth * 2 + 6 * depth * width, transcendentals=0
        ),
    )(scalars, normed, wq, wk, wv, cos_tab, sin_tab, valid)


def out_kernel(n_ctx, pairs, scalar_ref, *refs):
    piece_refs, (w_ref, valid_ref), (heads_ref, *partial_refs), buffer = (
        refs[:n_ctx],
        refs[n_ctx : n_ctx + 2],
        refs[n_ctx + 2 : -1],
        refs[-1],
    )
    me = scalar_ref[0]
    first, second = halves_at(scalar_ref[1])
    per = piece_refs[0].shape[0]
    heads = w_ref.shape[0] // HD
    for k in range(n_ctx):
        source = jnp.bitwise_xor(me, k)
        for p in range(per):
            buffer[source * per + p] = piece_refs[k][p]
    weight = w_ref[...]
    for sequence in range(pairs // heads):
        at = slice(sequence * PAIR, (sequence + 1) * PAIR)
        rows = jnp.concatenate(
            [
                jnp.concatenate(
                    [buffer[sequence * heads + head, first, :], buffer[sequence * heads + head, second, :]], axis=0
                )
                for head in range(heads)
            ],
            axis=1,
        )
        rows = rows * valid_ref[at, :]
        heads_ref[at, :] = rows
        put_partial(partial_refs, sequence * PAIR, dot(rows, weight).astype(BF), pairs // heads * PAIR // 4)


def project_out(scalars, pieces, weight, valid, pairs, n_ctx, split):
    width, depth = weight.shape
    rows = valid.shape[0]
    per = pieces[0].shape[0]
    shapes = [jax.ShapeDtypeStruct((rows, width), BF)] + partial_shapes(rows, depth, split)
    return pl.pallas_call(
        functools.partial(out_kernel, n_ctx, pairs),
        out_shape=shapes,
        grid_spec=pltpu.PrefetchScalarGridSpec(
            num_scalar_prefetch=1,
            grid=(1,),
            in_specs=[whole(piece.shape) for piece in pieces] + [whole(weight.shape), whole(valid.shape)],
            out_specs=[whole(shape.shape) for shape in shapes],
            scratch_shapes=[pltpu.VMEM((per * n_ctx, PAIR, HD), BF)],
        ),
        compiler_params=params(),
        cost_estimate=pl.CostEstimate(
            flops=2 * rows * depth * width, bytes_accessed=rows * depth * 2 + 2 * depth * width, transcendentals=0
        ),
    )(scalars, *pieces, weight, valid)


def heads_back_kernel(n_ctx, scalar_ref, da_ref, w_ref, valid_ref, *rest):
    out_refs, buffer = rest[:n_ctx], rest[n_ctx]
    me = scalar_ref[0]
    first, second = halves_at(scalar_ref[1])
    per = out_refs[0].shape[0]
    heads = w_ref.shape[0] // HD
    weight = w_ref[...]
    for pair in range(da_ref.shape[0] // PAIR * heads, per * n_ctx):
        buffer[pair] = jnp.zeros(buffer.shape[1:], BF)
    for sequence in range(da_ref.shape[0] // PAIR):
        at = slice(sequence * PAIR, (sequence + 1) * PAIR)
        grad = times_transposed(da_ref[at, :], weight).astype(BF) * valid_ref[at, :]
        for head in range(heads):
            part = grad[:, head * HD : (head + 1) * HD]
            buffer[sequence * heads + head, first, :] = part[:BLOCK]
            buffer[sequence * heads + head, second, :] = part[BLOCK:]
    for k in range(n_ctx):
        source = jnp.bitwise_xor(me, k)
        for p in range(per):
            out_refs[k][p] = buffer[source * per + p]


def heads_back(scalars, da, weight, valid, n_ctx):
    rows, depth = da.shape
    width = weight.shape[0]
    per = per_device(rows // PAIR * (width // HD), n_ctx)
    piece = (per, PAIR, HD)
    return pl.pallas_call(
        functools.partial(heads_back_kernel, n_ctx),
        out_shape=[jax.ShapeDtypeStruct(piece, BF)] * n_ctx,
        grid_spec=pltpu.PrefetchScalarGridSpec(
            num_scalar_prefetch=1,
            grid=(1,),
            in_specs=[whole(da.shape), whole(weight.shape), whole(valid.shape)],
            out_specs=[whole(piece)] * n_ctx,
            scratch_shapes=[pltpu.VMEM((per * n_ctx, PAIR, HD), BF)],
        ),
        compiler_params=params(),
        cost_estimate=pl.CostEstimate(
            flops=2 * rows * depth * width, bytes_accessed=rows * depth * 2 + 2 * depth * width, transcendentals=0
        ),
    )(scalars, da, weight, valid)


def in_kernel(n_ctx, pairs, scalar_ref, *refs):
    piece_refs, weight_refs, valid_ref = refs[:n_ctx], refs[n_ctx : n_ctx + 3], refs[n_ctx + 3]
    grad_refs, partial_refs, buffer = refs[n_ctx + 4 : n_ctx + 7], refs[n_ctx + 7 : -1], refs[-1]
    me = scalar_ref[0]
    first, second = halves_at(scalar_ref[1])
    per = piece_refs[0].shape[0]
    heads = weight_refs[0].shape[1] // HD
    for k in range(n_ctx):
        source = jnp.bitwise_xor(me, k)
        for p in range(per):
            buffer[source * per + p] = piece_refs[k][p]
    for sequence in range(pairs // heads):
        at = slice(sequence * PAIR, (sequence + 1) * PAIR)
        total = None
        for which in range(3):
            rows = jnp.concatenate(
                [
                    jnp.concatenate([buffer[pair, which, first, :], buffer[pair, which, second, :]], axis=0)
                    for pair in range(sequence * heads, (sequence + 1) * heads)
                ],
                axis=1,
            )
            if which == 2:
                rows = rows * valid_ref[at, :]
            grad_refs[which][at, :] = rows
            product = times_transposed(rows, weight_refs[which][...])
            total = product if total is None else total + product
        put_partial(partial_refs, sequence * PAIR, total.astype(BF), pairs // heads * PAIR // 4)


def project_in(scalars, pieces, weights, valid, pairs, n_ctx, split):
    depth, width = weights[0].shape
    rows = valid.shape[0]
    per = pieces[0].shape[0]
    shapes = [jax.ShapeDtypeStruct((rows, width), BF)] * 3 + partial_shapes(rows, depth, split)
    return pl.pallas_call(
        functools.partial(in_kernel, n_ctx, pairs),
        out_shape=shapes,
        grid_spec=pltpu.PrefetchScalarGridSpec(
            num_scalar_prefetch=1,
            grid=(1,),
            in_specs=[whole(piece.shape) for piece in pieces]
            + [whole(weight.shape) for weight in weights]
            + [whole(valid.shape)],
            out_specs=[whole(shape.shape) for shape in shapes],
            scratch_shapes=[pltpu.VMEM((per * n_ctx, 3, PAIR, HD), BF)],
        ),
        compiler_params=params(),
        cost_estimate=pl.CostEstimate(
            flops=6 * rows * depth * width, bytes_accessed=rows * depth * 2 + 6 * depth * width, transcendentals=0
        ),
    )(scalars, *pieces, *weights, valid)


def both_places(me, k, n_ctx):
    source = jnp.bitwise_xor(me, k)
    front = pl.multiple_of(source * BLOCK, BLOCK)
    back = pl.multiple_of((2 * n_ctx - 1 - source) * BLOCK, BLOCK)
    return pl.ds(front, BLOCK), pl.ds(back, BLOCK)


def attention_kernel(n_ctx, tile, scalar_ref, *refs):
    x_refs, o_refs, (qs, ks, vs, os) = refs[:n_ctx], refs[n_ctx : 2 * n_ctx], refs[2 * n_ctx :]
    me = scalar_ref[0]
    length = 2 * n_ctx * BLOCK
    for k in range(n_ctx):
        front, back = both_places(me, k, n_ctx)
        for which, dest in enumerate((qs, ks, vs)):
            dest[front, :] = x_refs[k][0, which, :BLOCK, :]
            dest[back, :] = x_refs[k][0, which, BLOCK:, :]
    factor = -(HD ** (-0.5)) * LOG2E
    shift = math.log(length) * LOG2E
    row_at = lax.broadcasted_iota(jnp.int32, (tile, tile), 0)
    col_at = lax.broadcasted_iota(jnp.int32, (tile, tile), 1)
    for i in range(length // tile):
        query = qs[i * tile : (i + 1) * tile, :]

        def part(j, masked):
            at = pl.ds(pl.multiple_of(j * tile, tile), tile)
            raw = times_transposed(query, ks[at, :])
            prob = 1.0 / (1.0 + jnp.exp2(raw * factor + shift))
            if masked:
                prob = jnp.where(row_at >= col_at, prob, 0.0)
            return dot(prob.astype(BF), vs[at, :])

        total = part(i, True)
        if i > 0:
            total = lax.fori_loop(0, i, lambda j, acc: acc + part(j, False), total)
        os[i * tile : (i + 1) * tile, :] = total.astype(BF)
    for k in range(n_ctx):
        front, back = both_places(me, k, n_ctx)
        o_refs[k][0, :BLOCK, :] = os[front, :]
        o_refs[k][0, BLOCK:, :] = os[back, :]


def attention_forward(scalars, pieces, n_ctx):
    pairs = pieces[0].shape[0]
    length = 2 * n_ctx * BLOCK
    tile = min(512, length)
    return pl.pallas_call(
        functools.partial(attention_kernel, n_ctx, tile),
        out_shape=[jax.ShapeDtypeStruct((pairs, PAIR, HD), BF)] * n_ctx,
        grid_spec=pltpu.PrefetchScalarGridSpec(
            num_scalar_prefetch=1,
            grid=(pairs,),
            in_specs=[pl.BlockSpec((1, 3, PAIR, HD), lambda i, s: (i, 0, 0, 0))] * n_ctx,
            out_specs=[pl.BlockSpec((1, PAIR, HD), lambda i, s: (i, 0, 0))] * n_ctx,
            scratch_shapes=[pltpu.VMEM((length, HD), BF)] * 4,
        ),
        compiler_params=params(),
        cost_estimate=pl.CostEstimate(
            flops=pairs * length * length * HD * 6,
            bytes_accessed=pairs * length * HD * 8,
            transcendentals=pairs * length * length,
        ),
    )(scalars, *pieces)


def attention_back_kernel(n_ctx, tile, scalar_ref, *refs):
    x_refs, g_refs, (cos_ref, sin_ref) = refs[:n_ctx], refs[n_ctx : 2 * n_ctx], refs[2 * n_ctx : 2 * n_ctx + 2]
    out_refs = refs[2 * n_ctx + 2 : 3 * n_ctx + 2]
    qs, ks, vs, gs, os, dqs = refs[3 * n_ctx + 2 :]
    me = scalar_ref[0]
    length = 2 * n_ctx * BLOCK
    for k in range(n_ctx):
        front, back = both_places(me, k, n_ctx)
        for which, dest in enumerate((qs, ks, vs)):
            dest[front, :] = x_refs[k][0, which, :BLOCK, :]
            dest[back, :] = x_refs[k][0, which, BLOCK:, :]
        gs[front, :] = g_refs[k][0, :BLOCK, :]
        gs[back, :] = g_refs[k][0, BLOCK:, :]
    scale = HD ** (-0.5)
    factor = -scale * LOG2E
    shift = math.log(length) * LOG2E
    count = length // tile
    key_at = lax.broadcasted_iota(jnp.int32, (tile, tile), 0)
    query_at = lax.broadcasted_iota(jnp.int32, (tile, tile), 1)
    dqs[...] = jnp.zeros_like(dqs)

    def unrotate(values, at):
        return (values * cos_ref[at, :] - pltpu.roll(values, HD // 2, 1) * sin_ref[at, :]).astype(BF)

    for j in range(count):
        own = slice(j * tile, (j + 1) * tile)
        keys = ks[own, :]
        values = vs[own, :]

        def part(i, masked):
            at = pl.ds(pl.multiple_of(i * tile, tile), tile)
            query = qs[at, :]
            grad = gs[at, :]
            raw = times_transposed(keys, query)
            prob = 1.0 / (1.0 + jnp.exp2(raw * factor + shift))
            if masked:
                prob = jnp.where(query_at >= key_at, prob, 0.0)
            prob_grad = times_transposed(values, grad)
            score_grad = (prob_grad * prob * (1.0 - prob)).astype(BF)
            dqs[at, :] += contract_rows(score_grad, keys)
            return dot(score_grad, query), dot(prob.astype(BF), grad)

        total = part(j, True)
        if j + 1 < count:

            def step(i, acc):
                more = part(i, False)
                return acc[0] + more[0], acc[1] + more[1]

            total = lax.fori_loop(j + 1, count, step, total)
        os[1, own, :] = unrotate(total[0] * scale, own)
        os[2, own, :] = total[1].astype(BF)
    for i in range(count):
        at = slice(i * tile, (i + 1) * tile)
        os[0, at, :] = unrotate(dqs[at, :] * scale, at)
    for k in range(n_ctx):
        front, back = both_places(me, k, n_ctx)
        for which in range(3):
            out_refs[k][0, which, :BLOCK, :] = os[which, front, :]
            out_refs[k][0, which, BLOCK:, :] = os[which, back, :]


def attention_backward(scalars, pieces, grads, cos_tab, sin_tab, n_ctx):
    pairs = pieces[0].shape[0]
    length = 2 * n_ctx * BLOCK
    tile = min(512, length)
    three = pl.BlockSpec((1, 3, PAIR, HD), lambda i, s: (i, 0, 0, 0))
    one = pl.BlockSpec((1, PAIR, HD), lambda i, s: (i, 0, 0))
    return pl.pallas_call(
        functools.partial(attention_back_kernel, n_ctx, tile),
        out_shape=[jax.ShapeDtypeStruct((pairs, 3, PAIR, HD), BF)] * n_ctx,
        grid_spec=pltpu.PrefetchScalarGridSpec(
            num_scalar_prefetch=1,
            grid=(pairs,),
            in_specs=[three] * n_ctx + [one] * n_ctx + [whole((length, HD))] * 2,
            out_specs=[three] * n_ctx,
            scratch_shapes=[pltpu.VMEM((length, HD), BF)] * 4
            + [pltpu.VMEM((3, length, HD), BF), pltpu.VMEM((length, HD), F32)],
        ),
        compiler_params=params(),
        cost_estimate=pl.CostEstimate(
            flops=pairs * length * length * HD * 12,
            bytes_accessed=pairs * length * HD * 14,
            transcendentals=pairs * length * length,
        ),
    )(scalars, *pieces, *grads, cos_tab, sin_tab)


def mlp_kernel(n_ref, g_ref, wg_ref, wu_ref, wd_ref, *rest):
    h_ref, dgp_ref, dup_ref = rest[-3:]
    rows = n_ref[...]
    gate_pre = dot(rows, wg_ref[...])
    up_pre = dot(rows, wu_ref[...])
    hidden_grad = times_transposed(g_ref[...], wd_ref[...])
    h_ref[...], dgp_ref[...], dup_ref[...] = feed_values(gate_pre, up_pre, hidden_grad)


def mlp_core(normed, grads, wg, wu, wd, total, first, held=()):
    rows, depth = normed.shape
    hidden = wg.shape[1]
    row_tile, tile = 512, 512
    skip = first // row_tile
    row_block = pl.BlockSpec((row_tile, depth), lambda j, i: (i, 0))
    out_block = pl.BlockSpec((row_tile, tile), lambda j, i: (i + skip, j))
    out = jax.ShapeDtypeStruct((total, hidden), BF)
    return pl.pallas_call(
        mlp_kernel,
        out_shape=(out, out, out),
        grid=(hidden // tile, rows // row_tile),
        in_specs=[
            row_block,
            row_block,
            pl.BlockSpec((depth, tile), lambda j, i: (0, j)),
            pl.BlockSpec((depth, tile), lambda j, i: (0, j)),
            pl.BlockSpec((tile, depth), lambda j, i: (j, 0)),
        ]
        + [pl.BlockSpec(memory_space=pl.ANY)] * len(held),
        out_specs=(out_block, out_block, out_block),
        input_output_aliases={5 + k: k for k in range(len(held))},
        compiler_params=params(),
        cost_estimate=pl.CostEstimate(
            flops=6 * rows * depth * hidden,
            bytes_accessed=rows * depth * 4 + 6 * depth * hidden + 6 * rows * hidden,
            transcendentals=rows * hidden,
        ),
    )(normed, grads, wg, wu, wd, *held)


def inverse_rms(values):
    return lax.rsqrt(jnp.mean(values * values, axis=-1, keepdims=True) + EPS)


def neighbours():
    index, rank = lax.axis_index("ctx"), lax.axis_index("tp")
    return (index, jnp.bitwise_xor(rank, 1)), (index, jnp.bitwise_xor(rank, 2))


def remote(source, dest, send_sem, recv_sem, device):
    return pltpu.make_async_remote_copy(
        src_ref=source,
        dst_ref=dest,
        send_sem=send_sem,
        recv_sem=recv_sem,
        device_id=device,
        device_id_type=pl.DeviceIdType.MESH,
    )


def signal(sem, device):
    pl.semaphore_signal(sem, inc=1, device_id=device, device_id_type=pl.DeviceIdType.MESH)


class Scatter:
    def __init__(self, partial, groups, bufs, sems, loaded=True):
        self.partial, self.groups, self.loaded = partial, groups, loaded
        self.from_x, self.from_y, self.for_y, self.for_x, self.low, self.high = bufs[:6]
        if loaded:
            self.stay, self.stay_y, self.stay_x = bufs[6:]
        self.first_send, self.first_recv, self.second_send, self.second_recv, self.load_sem = sems
        self.to_x, self.to_y = neighbours()

    @staticmethod
    def scratch(rows, width, loaded=True):
        dma = pltpu.SemaphoreType.DMA
        whole_rows, half_rows = pltpu.VMEM((rows, width), BF), pltpu.VMEM((rows // 2, width), BF)
        bufs = [whole_rows] * 2 + [half_rows] * 4 + ([whole_rows] + [half_rows] * 2 if loaded else [])
        return bufs + [dma((8,)), dma((8,)), dma((4,)), dma((4,)), dma((6,))]

    def piece(self, g, number):
        base, rows, own = self.groups[g]
        half = rows // 2
        if not self.loaded:
            return self.partial[pl.ds(base + number * half, half), :]
        if number < 2:
            return self.stay[pl.ds(own + number * half, half), :]
        return (self.stay_x if number == 3 else self.stay_y)[pl.ds(own // 2, half), :]

    def first_copies(self, g):
        base, rows, own = self.groups[g]
        half = rows // 2
        part = lambda number: self.partial.at[pl.ds(base + number * half, half)]
        at = lambda buf, number: buf.at[pl.ds(own + number * half, half)]
        plan = [
            (part(2), at(self.from_x, 0), self.to_x),
            (part(6), at(self.from_x, 1), self.to_x),
            (part(5), at(self.from_y, 0), self.to_y),
            (part(7), at(self.from_y, 1), self.to_y),
        ]
        return [
            remote(source, dest, self.first_send.at[4 * g + k], self.first_recv.at[4 * g + k], device)
            for k, (source, dest, device) in enumerate(plan)
        ]

    def loads(self, g):
        base, rows, own = self.groups[g]
        half = rows // 2
        copy = lambda number, count, dest, k: pltpu.make_async_copy(
            self.partial.at[pl.ds(base + number * half, count)], dest, self.load_sem.at[3 * g + k]
        )
        return [
            copy(0, rows, self.stay.at[pl.ds(own, rows)], 0),
            copy(4, half, self.stay_y.at[pl.ds(own // 2, half)], 1),
            copy(3, half, self.stay_x.at[pl.ds(own // 2, half)], 2),
        ]

    def second_copies(self, g):
        _, rows, own = self.groups[g]
        at = pl.ds(own // 2, rows // 2)
        return [
            remote(self.for_y.at[at], self.low.at[at], self.second_send.at[2 * g], self.second_recv.at[2 * g], self.to_y),
            remote(
                self.for_x.at[at], self.high.at[at], self.second_send.at[2 * g + 1], self.second_recv.at[2 * g + 1], self.to_x
            ),
        ]

    def start(self, g, which=(1, 3, 0, 2), loads=True):
        copies = self.first_copies(g)
        for k in which:
            copies[k].start()
        if loads:
            for copy in self.loads(g):
                copy.start()

    def forward(self, g):
        _, rows, own = self.groups[g]
        half = rows // 2
        copies = self.first_copies(g)
        copies[1].wait_recv()
        copies[3].wait_recv()
        if self.loaded:
            for copy in self.loads(g):
                copy.wait()
        at = pl.ds(own // 2, half)
        self.for_y[at, :] = add_low(self.piece(g, 4), self.from_x[pl.ds(own + half, half), :])
        self.for_x[at, :] = add_low(self.piece(g, 3), self.from_y[pl.ds(own + half, half), :])
        for copy in self.second_copies(g):
            copy.start()

    def total(self, g, use):
        _, rows, own = self.groups[g]
        half = rows // 2
        copies, seconds = self.first_copies(g), self.second_copies(g)
        copies[0].wait_recv()
        copies[2].wait_recv()
        for copy in copies:
            copy.wait_send()
        for copy in seconds:
            copy.wait()
        first = pl.ds(own, half)
        rest = pl.ds(own // 2, half)
        for side, (got, more) in enumerate(((self.from_x, self.low), (self.from_y, self.high))):
            at = pl.ds(own + side * half, half)
            use(at, self.piece(g, side).astype(F32) + got[first, :].astype(F32) + more[rest, :].astype(F32))


class Gather:
    def __init__(self, own, out, groups, sems, own_at=None, local=True):
        self.own, self.out, self.groups, self.has_local = own, out, groups, local
        self.own_at = own_at if own_at is not None else [group[2] for group in groups]
        self.first_send, self.first_recv, self.second_send, self.second_recv, self.local_sem = sems
        self.to_x, self.to_y = neighbours()

    @staticmethod
    def scratch():
        dma = pltpu.SemaphoreType.DMA
        return [dma((4,)), dma((4,)), dma((4,)), dma((4,)), dma((2,))]

    def first_copies(self, g):
        base, rows, _ = self.groups[g]
        source = self.own.at[pl.ds(self.own_at[g], rows)]
        place = lambda k: self.out.at[pl.ds(base + k * rows, rows)]
        return [
            remote(source, place(1), self.first_send.at[2 * g], self.first_recv.at[2 * g], self.to_x),
            remote(source, place(2), self.first_send.at[2 * g + 1], self.first_recv.at[2 * g + 1], self.to_y),
        ]

    def local(self, g):
        base, rows, _ = self.groups[g]
        return pltpu.make_async_copy(self.own.at[pl.ds(self.own_at[g], rows)], self.out.at[pl.ds(base, rows)], self.local_sem.at[g])

    def second_copies(self, g):
        base, rows, _ = self.groups[g]
        half = rows // 2
        part = lambda number: self.out.at[pl.ds(base + number * half, half)]
        return [
            remote(part(4), part(6), self.second_send.at[2 * g], self.second_recv.at[2 * g], self.to_x),
            remote(part(3), part(7), self.second_send.at[2 * g + 1], self.second_recv.at[2 * g + 1], self.to_y),
        ]

    def start(self, g):
        for copy in self.first_copies(g):
            copy.start()
        if self.has_local:
            self.local(g).start()

    def forward_x(self, g):
        self.first_copies(g)[0].wait_recv()
        self.second_copies(g)[1].start()

    def forward_y(self, g):
        self.first_copies(g)[1].wait_recv()
        self.second_copies(g)[0].start()

    def forward(self, g):
        self.forward_x(g)
        self.forward_y(g)
        if self.has_local:
            self.local(g).wait()

    def finish(self, g):
        for copy in self.second_copies(g):
            copy.wait_recv()

    def sent(self, g):
        for copy in self.first_copies(g) + self.second_copies(g):
            copy.wait_send()


TILE, ROWS = 128, 64
CORE_SLOTS, HOP_SLOTS = 4, 4


class Ring:
    def __init__(self, slots, send_sem, recv_sem, credit, total):
        self.slots, self.send_sem, self.recv_sem, self.credit, self.total = slots, send_sem, recv_sem, credit, total
        self.count = slots.shape[0]

    def copy(self, source, at, send_at, device):
        slot = lax.rem(at, self.count)
        return pltpu.make_async_remote_copy(
            src_ref=source,
            dst_ref=self.slots.at[slot],
            send_sem=self.send_sem.at[send_at],
            recv_sem=self.recv_sem.at[slot],
            device_id=device,
            device_id_type=pl.DeviceIdType.MESH,
        )

    def send(self, source, at, send_at, device):
        @pl.when(at >= self.count)
        def _():
            pl.semaphore_wait(self.credit, 1)

        self.copy(source, at, send_at, device).start()

    def sent(self, source, at, send_at, device):
        self.copy(source, at, send_at, device).wait_send()

    def arrived(self, source, at, send_at, device):
        self.copy(source, at, send_at, device).wait_recv()
        return self.slots.at[lax.rem(at, self.count)]

    def free(self, at, device):
        @pl.when(at + self.count < self.total)
        def _():
            pl.semaphore_signal(self.credit, inc=1, device_id=device, device_id_type=pl.DeviceIdType.MESH)


def sums_kernel(n_ctx, items, n_right, n_extra, tasks, late, *refs):
    n_left = len(items)
    made = items[0][3]
    n_held = n_left - (1 if made else 0)
    left_refs, right_refs = refs[:n_held], refs[n_held : n_held + n_right]
    left_refs = ((None,) if made else ()) + tuple(left_refs)
    refs = refs[n_held + n_right :]
    extra_in, refs = refs[: n_extra[0]], refs[n_extra[0] :]
    out_refs, extra_out, refs = refs[:n_left], refs[n_left : n_left + n_extra[1]], refs[n_left + n_extra[1] :]
    extra_scratch, refs = refs[: n_extra[2]], refs[n_extra[2] :]
    right_refs = list(right_refs) + [extra_out[k] for k in late]
    n_right += len(late)
    (
        left_buf, right_buf, other_buf, ring, core_in, hop_in, hop_mid, hop_out, core_out,
        left_sem, right_sem, core_send, core_recv, in_send, in_recv, mid_send, mid_recv, out_send, out_recv,
        fin_send, fin_recv, store_sem, core_credit, in_credit, mid_credit, out_credit, fin_credit,
    ) = refs
    starts = [0]
    for _, _, chunks, _ in items:
        starts.append(starts[-1] + chunks)
    total = starts[-1]
    n_ring = ring.shape[0]
    chips = n_ctx // 2
    mid = chips // 2
    index = lax.axis_index("ctx")
    rank = lax.axis_index("tp")
    core = lax.rem(index, 2)
    chip = index // 2
    low_side = chip < mid
    place = jnp.where(low_side, chip, chips - 1 - chip)
    toward = jnp.where(low_side, 1, -1)
    partner = (chip * 2 + 1 - core, rank)
    after = ((chip + toward) * 2 + core, rank)
    before = ((chip - toward) * 2 + core, rank)
    is_first = place == 0
    is_last = place == mid - 1
    lag_t = mid
    lag_u = lag_t + 2
    lag_o = lag_u + 2 * (mid - 1)
    lag_f = lag_o + 1
    lag_w = lag_f + 1

    if tasks is not None:
        greet(n_ctx, True)
    else:
        barrier = pltpu.get_barrier_semaphore()
        pl.semaphore_signal(barrier, inc=1, device_id=partner, device_id_type=pl.DeviceIdType.MESH)

        @pl.when(chip > 0)
        def _():
            pl.semaphore_signal(
                barrier, inc=1, device_id=((chip - 1) * 2 + core, rank), device_id_type=pl.DeviceIdType.MESH
            )

        @pl.when(chip < chips - 1)
        def _():
            pl.semaphore_signal(
                barrier, inc=1, device_id=((chip + 1) * 2 + core, rank), device_id_type=pl.DeviceIdType.MESH
            )

        pl.semaphore_wait(barrier, 1 + jnp.where(chip > 0, 1, 0) + jnp.where(chip < chips - 1, 1, 0))

    to_core = Ring(core_in, core_send, core_recv, core_credit, total)
    to_after = Ring(hop_in, in_send, in_recv, in_credit, total)
    across = Ring(hop_mid, mid_send, mid_recv, mid_credit, total)
    to_before = Ring(hop_out, out_send, out_recv, out_credit, total)
    to_final = Ring(core_out, fin_send, fin_recv, fin_credit, total)

    def right_copy(k):
        return pltpu.make_async_copy(right_refs[k], right_buf.at[k % 2], right_sem.at[k % 2])

    right_copy(0).start()

    def for_item(at, action):
        for number in range(n_left):
            @pl.when((at >= starts[number]) & (at < starts[number + 1]))
            def _(number=number):
                action(number, at - starts[number])

    def rows_at(number, chunk, side):
        half = items[number][2] * ROWS
        return pl.multiple_of(side * half + chunk * ROWS, ROWS)

    def left_copy(number, chunk, slot, which):
        side = core if which == 0 else 1 - core
        half = items[number][2] * ROWS
        return pltpu.make_async_copy(
            left_refs[number].at[:, pl.ds(pl.multiple_of(side * half + chunk // 2 * TILE, TILE), TILE)],
            left_buf.at[slot, which],
            left_sem.at[slot, which],
        )

    def load_left(at):
        def action(number, chunk):
            if number == 0 and made:
                maker.load(chunk // 2)
                return
            if number == 1 and made:

                @pl.when(chunk == 0)
                def _():
                    maker.release()

            for which in range(2):
                left_copy(number, chunk, lax.rem(at // 2, 2), which).start()

        for_item(at, action)

    planned, each, maker = tasks(extra_in, extra_out, extra_scratch) if tasks is not None else ({}, None, None)
    if 0 in planned:
        planned.pop(0)()
    if made:
        maker.begin(left_buf, right_buf)
    load_left(0)
    if n_right > 1 and not made:
        right_copy(1).start()
    right_copy(0).wait()

    def step(i, carry):
        def at_lag(lag):
            at = i - lag
            return at, (at >= 0) & (at < total)

        at, now = at_lag(lag_w)

        @pl.when(now)
        def _():
            slot = lax.rem(at, n_ring)
            source = ring.at[slot]

            def action(number, chunk):
                store(number, chunk, at, 0).wait()
                store(number, chunk, at, 1).wait()

            for_item(at, action)
            to_final.sent(source, at, slot, partner)
            to_final.free(at, partner)

            @pl.when(jnp.logical_not(is_first))
            def _():
                to_before.sent(source, at, slot, before)

        at, now = at_lag(lag_o)

        @pl.when(now & jnp.logical_not(is_last))
        def _():
            slot = lax.rem(at, n_ring)
            source = ring.at[slot]
            to_after.sent(source, at, slot, after)
            got = to_before.arrived(source, at, slot, after)
            ring[slot] = got[...]
            to_before.free(at, after)

            @pl.when(jnp.logical_not(is_first))
            def _():
                to_before.send(source, at, slot, before)

        @pl.when(now)
        def _():
            slot = lax.rem(at, n_ring)
            to_final.send(ring.at[slot], at, slot, partner)

        at, now = at_lag(lag_u)

        @pl.when(now & is_last)
        def _():
            slot = lax.rem(at, n_ring)
            source = ring.at[slot]
            across.sent(source, at, slot, after)
            got = across.arrived(source, at, slot, after)
            ring[slot] = add_low(ring[slot], got[...])
            across.free(at, after)

            @pl.when(jnp.logical_not(is_first))
            def _():
                to_before.send(source, at, slot, before)

        at, now = at_lag(lag_t)

        @pl.when(now)
        def _():
            slot = lax.rem(at, n_ring)
            source = ring.at[slot]

            @pl.when(jnp.logical_not(is_first))
            def _():
                got = to_after.arrived(source, at, slot, before)
                ring[slot] = add_low(ring[slot], got[...])
                to_after.free(at, before)

            @pl.when(is_last)
            def _():
                across.send(source, at, slot, after)

            @pl.when(jnp.logical_not(is_first) & jnp.logical_not(is_last))
            def _():
                to_after.send(source, at, slot, after)

        at, now = at_lag(1)

        @pl.when(now)
        def _():
            slot = lax.rem(at, n_ring)
            source = ring.at[slot]
            own = other_buf.at[lax.rem(at, 4)]
            to_core.sent(own, at, lax.rem(at, 4), partner)
            got = to_core.arrived(own, at, lax.rem(at, 4), partner)
            ring[slot] = add_low(ring[slot], got[...])
            to_core.free(at, partner)

            @pl.when(is_first & jnp.logical_not(is_last))
            def _():
                to_after.send(source, at, slot, after)

        at, now = at_lag(lag_f)

        @pl.when(now)
        def _():
            slot = lax.rem(at, n_ring)
            to_final.arrived(ring.at[slot], at, slot, partner)

            def action(number, chunk):
                store(number, chunk, at, 0).start()
                store(number, chunk, at, 1).start()

            for_item(at, action)

        for when, task in planned.items():
            pl.when(i == when)(task)

        if each is not None:
            each(i)

        @pl.when((i + 2 < total) & (lax.rem(i, 2) == 0))
        def _():
            load_left(i + 2)

        @pl.when((i < total) & (lax.rem(i, 2) == 0))
        def _():
            slot = lax.rem(i // 2, 2)

            def action(number, chunk):
                which_right = items[number][1]
                if which_right > 0 and items[number - 1][1] != which_right:

                    @pl.when(chunk == 0)
                    def _():
                        if made and which_right in (1, n_right - 1):
                            right_copy(which_right).start()
                        right_copy(which_right).wait()

                if which_right > 0 and which_right + 1 < n_right - (1 if made else 0):

                    @pl.when(chunk == items[number][2] // 2)
                    def _():
                        right_copy(which_right + 1).start()

                if number == 0 and made:
                    maker.make(chunk // 2)
                else:
                    for which in range(2):
                        left_copy(number, chunk, slot, which).wait()
                right = right_buf.at[which_right % 2]
                product = contract_rows(left_buf[slot, 1], right[...]).astype(BF)
                for part in range(2):
                    place = lax.rem(i + part, 4)
                    other_buf[place] = product[part * ROWS : (part + 1) * ROWS]
                    to_core.send(other_buf.at[place], i + part, place, partner)
                product = contract_rows(left_buf[slot, 0], right[...]).astype(BF)
                for part in range(2):
                    ring[lax.rem(i + part, n_ring)] = product[part * ROWS : (part + 1) * ROWS]

            for_item(i, action)

        return carry

    def store(number, chunk, at, which):
        source = ring.at[lax.rem(at, n_ring)] if which == 0 else core_out.at[lax.rem(at, CORE_SLOTS)]
        side = core if which == 0 else 1 - core
        return pltpu.make_async_copy(
            source,
            out_refs[number].at[pl.ds(rows_at(number, chunk, side), ROWS), :],
            store_sem.at[which, lax.rem(at, 2)],
        )

    lax.fori_loop(0, total + lag_w, step, 0)


def weight_sums(items, rights, n_ctx, collective_id, extra=None, late=(), limit=VMEM_LIMIT):
    tokens, width = rights[0].shape
    columns = [left if isinstance(left, int) else left.shape[1] for left, _ in items]
    held = [left for left, _ in items if not isinstance(left, int)]
    shapes = [
        (k, right, columns[k] // 2 // ROWS, isinstance(left, int)) for k, (left, right) in enumerate(items)
    ]
    mid = n_ctx // 4
    n_ring = mid + 2 + 2 * (mid - 1) + 4
    any_spec = pl.BlockSpec(memory_space=pl.ANY)
    args, arg_specs, outs, out_specs, scratch, tasks = extra if extra is not None else ([], [], [], [], [], None)
    counts = (len(args), len(outs), len(scratch))
    chunk = (ROWS, width)
    dma = pltpu.SemaphoreType.DMA
    return pl.pallas_call(
        functools.partial(sums_kernel, n_ctx, shapes, len(rights), counts, tasks, late),
        out_shape=[jax.ShapeDtypeStruct((count, width), BF) for count in columns] + outs,
        in_specs=[any_spec] * (len(held) + len(rights)) + arg_specs,
        out_specs=[any_spec] * len(items) + out_specs,
        scratch_shapes=scratch
        + [
            pltpu.VMEM((2, 2, tokens, TILE), BF),
            pltpu.VMEM((min(2, len(rights) + len(late)), tokens, width), BF),
            pltpu.VMEM((4,) + chunk, BF),
            pltpu.VMEM((n_ring,) + chunk, BF),
            pltpu.VMEM((CORE_SLOTS,) + chunk, BF),
            pltpu.VMEM((HOP_SLOTS,) + chunk, BF),
            pltpu.VMEM((HOP_SLOTS,) + chunk, BF),
            pltpu.VMEM((HOP_SLOTS,) + chunk, BF),
            pltpu.VMEM((CORE_SLOTS,) + chunk, BF),
            dma((2, 2)),
            dma((2,)),
            dma((4,)),
            dma((CORE_SLOTS,)),
            dma((n_ring,)),
            dma((HOP_SLOTS,)),
            dma((n_ring,)),
            dma((HOP_SLOTS,)),
            dma((n_ring,)),
            dma((HOP_SLOTS,)),
            dma((n_ring,)),
            dma((CORE_SLOTS,)),
            dma((2, 2)),
        ]
        + [pltpu.SemaphoreType.REGULAR] * 5,
        compiler_params=pltpu.CompilerParams(
            vmem_limit_bytes=limit, collective_id=collective_id, has_side_effects=True
        ),
        cost_estimate=pl.CostEstimate(
            flops=sum(2 * count * tokens * width for count in columns),
            bytes_accessed=sum(2 * count * (tokens + width) for count in columns),
            transcendentals=0,
        ),
    )(*held, *rights, *args)


VMEM_SPEC = pl.BlockSpec(memory_space=pltpu.VMEM)
ANY_SPEC = pl.BlockSpec(memory_space=pl.ANY)


def norm_back_rows(values, gain, grad):
    inv = inverse_rms(values)
    unit = values * inv
    scaled = grad * gain
    back = (scaled - unit * jnp.mean(scaled * unit, axis=-1, keepdims=True)) * inv
    return back, jnp.sum(grad * unit, axis=0, keepdims=True)


def own_copies(ref, buf, groups, sem):
    odd = lax.rem(lax.axis_index("tp"), 2)
    starts = [pl.multiple_of(odd * BLOCK, BLOCK), pl.multiple_of((1 - odd) * PAIR, BLOCK)]
    return [
        pltpu.make_async_copy(ref.at[pl.ds(start, rows)], buf.at[pl.ds(own, rows)], sem.at[g])
        for g, (start, (_, rows, own)) in enumerate(zip(starts, groups))
    ]


class Maker:
    def __init__(self, refs, outs, weights, downs, stage, sems):
        self.n2_ref, self.wg_ref, self.wu_ref, self.wd_ref = refs
        self.h_out, self.dgp_out, self.dup_out = outs
        self.weights, self.downs, self.stage = weights, downs, stage
        self.n2_sem, self.weight_sem, self.h_sem, self.grad_sem = sems
        self.core = lax.rem(lax.axis_index("ctx"), 2)
        self.half = self.h_out.shape[1] // 2
        self.tiles = self.half // TILE

    def first(self, tile, which):
        side = self.core if which == 0 else 1 - self.core
        return pl.multiple_of(side * self.half + tile * TILE, TILE)

    def copies(self, tile):
        slot = lax.rem(tile, 2)
        deep = self.weights.shape[1]
        made = []
        for which in range(2):
            at = pl.ds(self.first(tile, which), TILE)
            for kind, ref in enumerate((self.wg_ref, self.wu_ref)):
                to = pl.multiple_of((slot * 2 + kind) * 2 * TILE + which * TILE, TILE)
                for part in range(2):
                    made.append((ref.at[pl.ds(part * deep, deep), at], self.weights.at[part, :, pl.ds(to, TILE)]))
            made.append((self.wd_ref.at[at], self.downs.at[slot, 0, pl.ds(which * TILE, TILE)]))
        return [
            pltpu.make_async_copy(source, dest, self.weight_sem.at[slot, k]) for k, (source, dest) in enumerate(made)
        ]

    def load(self, tile):
        for copy in self.copies(tile):
            copy.start()

    def begin(self, left_buf, right_buf):
        self.left_buf, self.right_buf = left_buf, right_buf
        self.n2_copy().start()

    def n2_copy(self):
        return pltpu.make_async_copy(self.n2_ref, self.right_buf.at[1], self.n2_sem)

    def h_stores(self, tile):
        slot = lax.rem(tile, 2)
        return [
            pltpu.make_async_copy(
                self.left_buf.at[slot, which],
                self.h_out.at[:, pl.ds(self.first(tile, which), TILE)],
                self.h_sem.at[slot, which],
            )
            for which in range(2)
        ]

    def grad_stores(self, tile):
        return [
            pltpu.make_async_copy(
                self.stage.at[kind, which], out.at[:, pl.ds(self.first(tile, which), TILE)], self.grad_sem.at[kind, which]
            )
            for kind, out in enumerate((self.dgp_out, self.dup_out))
            for which in range(2)
        ]

    def make(self, tile):
        slot = lax.rem(tile, 2)
        deep = self.weights.shape[1]

        @pl.when(tile == 0)
        def _():
            self.n2_copy().wait()

        @pl.when(tile > 0)
        def _():
            for copy in self.grad_stores(tile - 1):
                copy.wait()

        @pl.when(tile > 1)
        def _():
            for copy in self.h_stores(tile - 2):
                copy.wait()

        for copy in self.copies(tile):
            copy.wait()
        at_gate = pl.ds(pl.multiple_of(slot * 4 * TILE, TILE), 2 * TILE)
        at_up = pl.ds(pl.multiple_of((slot * 4 + 2) * TILE, TILE), 2 * TILE)
        count = 512

        def rows_step(step, carry):
            rows = pl.ds(pl.multiple_of(step * count, count), count)
            low, high = self.right_buf[1, rows, :deep], self.right_buf[1, rows, deep:]
            gate_pre = dot(low, self.weights[0, :, at_gate]) + dot(high, self.weights[1, :, at_gate])
            up_pre = dot(low, self.weights[0, :, at_up]) + dot(high, self.weights[1, :, at_up])
            hidden_grad = times_transposed(self.right_buf[0, rows, :], self.downs[slot, 0])
            h, dgp, dup = feed_values(gate_pre, up_pre, hidden_grad)
            for which in range(2):
                part = slice(which * TILE, (which + 1) * TILE)
                self.left_buf[slot, which, rows, :] = h[:, part]
                self.stage[0, which, rows, :] = dgp[:, part]
                self.stage[1, which, rows, :] = dup[:, part]
            return carry

        lax.fori_loop(0, self.right_buf.shape[1] // count, rows_step, 0)
        for copy in self.h_stores(tile) + self.grad_stores(tile):
            copy.start()

    def release(self):
        for copy in self.h_stores(self.tiles - 2):
            copy.wait()

    def finish(self):
        for copy in self.h_stores(self.tiles - 1) + self.grad_stores(self.tiles - 1):
            copy.wait()


def feed_values(gate_pre, up_pre, hidden_grad):
    gate_sig = 1.0 / (1.0 + jnp.exp2(gate_pre * (-LOG2E)))
    gate_act = gate_pre * gate_sig
    return (
        (gate_act * up_pre).astype(BF),
        (hidden_grad * up_pre * (gate_sig * (1.0 + gate_pre * (1.0 - gate_sig)))).astype(BF),
        (hidden_grad * gate_act).astype(BF),
    )


def feed_tasks(groups, extra_in, extra_out, scratch):
    n2_ref, wg_ref, wu_ref, wd_ref, residual, cot_ref, gain = extra_in
    dr, da_all, gain_grad, d_ref, h_ref, dgp_ref, dup_ref = extra_out
    n = len(Scatter.scratch(16, 128))
    bufs, rest = scratch[:n], scratch[n:]
    weights, lefts, tile_out, weight_sem, left_sem, out_sem = rest[:6]
    grads, stage, own_sem, n2_sem, make_sem, h_sem, grad_sem = rest[6:13]
    da_own = bufs[0]
    scatter = Scatter(d_ref, groups, bufs[:9], bufs[9:])
    gather = Gather(da_own, da_all, groups, rest[13:])
    maker = Maker(
        (n2_ref, wg_ref, wu_ref, wd_ref),
        (h_ref, dgp_ref, dup_ref),
        weights,
        lefts,
        stage,
        (n2_sem, make_sem, h_sem, grad_sem),
    )
    order = list(reversed(range(len(groups))))
    rows, columns = lefts.shape[2], weights.shape[1]
    row_tiles = dgp_ref.shape[0] // rows
    tiles = row_tiles * (d_ref.shape[1] // columns)
    after = maker.half // ROWS
    shift = after + 1

    def weight_copies(part):
        at = pl.ds(pl.multiple_of(part * columns, columns), columns)
        return [
            pltpu.make_async_copy(ref.at[at], weights.at[k], weight_sem.at[k]) for k, ref in enumerate((wg_ref, wu_ref))
        ]

    def left_copies(tile):
        at = pl.ds(pl.multiple_of(lax.rem(tile, row_tiles) * rows, rows), rows)
        slot = lax.rem(tile, 2)
        return [
            pltpu.make_async_copy(ref.at[at], lefts.at[slot, k], left_sem.at[slot, k])
            for k, ref in enumerate((dgp_ref, dup_ref))
        ]

    def out_copy(tile):
        slot = lax.rem(tile, 2)
        return pltpu.make_async_copy(
            tile_out.at[slot],
            d_ref.at[
                pl.ds(pl.multiple_of(lax.rem(tile, row_tiles) * rows, rows), rows),
                pl.ds(pl.multiple_of(tile // row_tiles * columns, columns), columns),
            ],
            out_sem.at[slot],
        )

    def begin():
        gain_grad[...] = jnp.zeros_like(gain_grad)
        for copy in own_copies(cot_ref, grads, groups, own_sem):
            copy.start()

    def whole_hidden():
        maker.finish()
        for copy in weight_copies(0) + left_copies(0):
            copy.start()

    def each(step):
        i = step - shift

        @pl.when((i >= 0) & (i < tiles))
        def _():
            slot = lax.rem(i, 2)

            @pl.when(i + 1 < tiles)
            def _():
                for copy in left_copies(i + 1):
                    copy.start()

            @pl.when(lax.rem(i, row_tiles) == 0)
            def _():
                @pl.when(i > 0)
                def _():
                    for copy in weight_copies(i // row_tiles):
                        copy.start()

                for copy in weight_copies(i // row_tiles):
                    copy.wait()

            for copy in left_copies(i):
                copy.wait()
            total = times_transposed(lefts[slot, 0], weights[0]) + times_transposed(lefts[slot, 1], weights[1])

            @pl.when(i >= 2)
            def _():
                out_copy(i - 2).wait()

            tile_out[slot] = total.astype(BF)
            out_copy(i).start()

    def start():
        out_copy(tiles - 2).wait()
        out_copy(tiles - 1).wait()
        for copy in own_copies(cot_ref, grads, groups, own_sem):
            copy.wait()
        for g in order:
            scatter.start(g)

    def use(at, total):
        back, more = norm_back_rows(residual[at, :], gain[...], total)
        total_grad = grads[at, :].astype(F32) + back
        dr[at, :] = total_grad
        da_own[at, :] = total_grad.astype(BF)
        gain_grad[...] += more

    def spread(g):
        scatter.total(g, use)
        gather.start(g)

    def finish():
        for g in order:
            gather.finish(g)
            gather.sent(g)

    first = shift + tiles
    plan = {
        0: begin,
        after: whole_hidden,
        first: start,
        first + 3: lambda: scatter.forward(order[0]),
        first + 6: lambda: scatter.forward(order[-1]),
        first + 7: lambda: spread(order[0]),
        first + 9: lambda: spread(order[-1]),
        first + 11: lambda: gather.forward(order[0]),
        first + 15: lambda: gather.forward(order[-1]),
        first + 18: finish,
    }
    return plan, each, maker


def feed_extra(groups, n2, wg, wu, wd, residual, cot, gain):
    rows, width = residual.shape
    tokens, hidden = n2.shape[0], wg.shape[1]
    dma = pltpu.SemaphoreType.DMA
    outs = [
        jax.ShapeDtypeStruct((rows, width), F32),
        jax.ShapeDtypeStruct((tokens, width), BF),
        jax.ShapeDtypeStruct((1, width), F32),
        jax.ShapeDtypeStruct((tokens, width), BF),
    ] + [jax.ShapeDtypeStruct((tokens, hidden), BF)] * 3
    scratch = (
        Scatter.scratch(rows, width)
        + [
            pltpu.VMEM((2, width // 2, hidden), BF),
            pltpu.VMEM((2, 2, PAIR, hidden), BF),
            pltpu.VMEM((2, PAIR, width // 2), BF),
            dma((2,)),
            dma((2, 2)),
            dma((2,)),
            pltpu.VMEM((rows, width), BF),
            pltpu.VMEM((2, 2, tokens, TILE), BF),
            dma((2,)),
            dma,
            dma((2, 10)),
            dma((2, 2)),
            dma((2, 2)),
        ]
        + Gather.scratch()
    )
    return (
        [n2, wg, wu, wd, residual, cot, gain],
        [ANY_SPEC] * 4 + [VMEM_SPEC, ANY_SPEC, VMEM_SPEC],
        outs,
        [VMEM_SPEC, ANY_SPEC, VMEM_SPEC] + [ANY_SPEC] * 4,
        scratch,
        functools.partial(feed_tasks, groups),
    )


def input_tasks(n_ctx, groups, extra_in, extra_out, scratch):
    i_ref, tokens_ref, dr, gain, gain_two_grad = extra_in
    input_grad, gain_sums = extra_out
    n = len(Scatter.scratch(16, 128))
    scatter = Scatter(i_ref, groups, scratch[:9], scratch[9:n])
    gains, got_tp, got_ctx, send_tp, recv_tp, send_ctx, recv_ctx, rows_in, own_sem = scratch[n:]
    order = list(reversed(range(len(groups))))
    me, rank = lax.axis_index("ctx"), lax.axis_index("tp")

    def tp_hop(k):
        return remote(gains.at[k], got_tp.at[k], send_tp.at[k], recv_tp.at[k], neighbours()[k])

    def ctx_hop(k):
        place = gains.at[2]
        return remote(place, got_ctx.at[k], send_ctx.at[k], recv_ctx.at[k], (jnp.bitwise_xor(me, k), rank))

    def begin():
        gains[0] = jnp.zeros(gains.shape[1:], F32)
        gains[0, 8:9, :] = gain_two_grad[...]
        for copy in own_copies(tokens_ref, rows_in, groups, own_sem):
            copy.start()
        for g in order:
            scatter.start(g)
        for copy in own_copies(tokens_ref, rows_in, groups, own_sem):
            copy.wait()

    def use(at, total):
        back, more = norm_back_rows(rows_in[at, :].astype(F32), gain[...], total)
        input_grad[at, :] = (dr[at, :] + back).astype(BF)
        gains[0, 0:1, :] += more

    def rest():
        scatter.total(order[-1], use)
        tp_hop(0).start()

    def second():
        tp_hop(0).wait()
        gains[1] = gains[0] + got_tp[0]
        tp_hop(1).start()

    def third():
        tp_hop(1).wait()
        gains[2] = gains[1] + got_tp[1]
        for k in range(1, n_ctx):
            ctx_hop(k).start()

    def finish():
        for k in range(1, n_ctx):
            ctx_hop(k).wait()
        got_ctx[0] = gains[2]
        total = got_ctx[jnp.bitwise_xor(me, 0)]
        for index in range(1, n_ctx):
            total = total + got_ctx[jnp.bitwise_xor(me, index)]
        gain_sums[...] = total

    return {
        0: begin,
        4: lambda: scatter.forward(order[0]),
        9: lambda: scatter.forward(order[-1]),
        10: lambda: scatter.total(order[0], use),
        13: rest,
        15: second,
        17: third,
        20: finish,
    }, None, None


def input_extra(n_ctx, groups, i_partial, tokens_in, dr, gain, gain_two_grad):
    rows, width = tokens_in.shape
    dma = pltpu.SemaphoreType.DMA
    outs = [jax.ShapeDtypeStruct((rows, width), BF), jax.ShapeDtypeStruct((16, width), F32)]
    return (
        [i_partial, tokens_in, dr, gain, gain_two_grad],
        [ANY_SPEC] * 2 + [VMEM_SPEC] * 3,
        outs,
        [VMEM_SPEC] * 2,
        Scatter.scratch(rows, width)
        + [
            pltpu.VMEM((3, 16, width), F32),
            pltpu.VMEM((2, 16, width), F32),
            pltpu.VMEM((n_ctx, 16, width), F32),
            dma((2,)),
            dma((2,)),
            dma((n_ctx,)),
            dma((n_ctx,)),
            pltpu.VMEM((rows, width), BF),
            dma((2,)),
        ],
        functools.partial(input_tasks, n_ctx, groups),
    )


class Exchange:
    def __init__(self, dest, sems, by_device):
        self.dest, self.by_device = dest, by_device
        self.send_sem, self.recv_sem, self.own_sem = sems
        self.n_ctx = dest.shape[1]
        self.me, self.rank = lax.axis_index("ctx"), lax.axis_index("tp")

    @staticmethod
    def scratch(units, n_ctx):
        dma = pltpu.SemaphoreType.DMA
        return [dma((units, n_ctx)), dma((units, n_ctx)), dma((units,))]

    def copy(self, source, unit, k):
        other = jnp.bitwise_xor(self.me, k)
        place = other if self.by_device else k
        return remote(
            source.at[unit, place],
            self.dest.at[unit, k],
            self.send_sem.at[unit, k],
            self.recv_sem.at[unit, k],
            (other, self.rank),
        )

    def own(self, source, unit):
        place = self.me if self.by_device else 0
        return pltpu.make_async_copy(source.at[unit, place], self.dest.at[unit, 0], self.own_sem.at[unit])

    def start(self, source, unit):
        for k in reversed(range(1, self.n_ctx)):
            self.copy(source, unit, k).start()
        self.own(source, unit).start()

    def start_some(self, source, unit, first, count):
        for k in reversed(range(self.n_ctx)):
            other = jnp.bitwise_xor(self.me, k)

            @pl.when((other >= first) & (other < first + count))
            def _(k=k):
                if k == 0:
                    self.own(source, unit).start()
                else:
                    self.copy(source, unit, k).start()

    def arrived(self, source, unit):
        for k in range(1, self.n_ctx):
            self.copy(source, unit, k).wait_recv()
        self.own(source, unit).wait()

    def sent(self, source, unit):
        for k in range(1, self.n_ctx):
            self.copy(source, unit, k).wait_send()


def greet(n_ctx, tp_too):
    index, rank = lax.axis_index("ctx"), lax.axis_index("tp")
    barrier = pltpu.get_barrier_semaphore()
    for k in range(1, n_ctx):
        signal(barrier, (jnp.bitwise_xor(index, k), rank))
    if tp_too:
        for device in neighbours():
            signal(barrier, device)
    pl.semaphore_wait(barrier, n_ctx - 1 + (2 if tp_too else 0))


def rotation(cos_tab, sin_tab, block_cos, block_sin):
    sign = jnp.where(lax.broadcasted_iota(jnp.int32, cos_tab.shape, 1) < HD // 2, -1.0, 1.0)
    return cos_tab * block_cos - sin_tab * block_sin, (sin_tab * block_cos + cos_tab * block_sin) * sign


def in_turn(count):
    return [count - 1] + list(range(count - 1))


def attend_rows(qs, ks, vs, os, tile):
    length = qs.shape[0]
    factor = -(HD ** (-0.5)) * LOG2E
    shift = math.log(length) * LOG2E
    row_at = lax.broadcasted_iota(jnp.int32, (tile, tile), 0)
    col_at = lax.broadcasted_iota(jnp.int32, (tile, tile), 1)
    for i in range(length // tile):
        query = qs[i * tile : (i + 1) * tile, :]

        def part(j, masked):
            at = pl.ds(pl.multiple_of(j * tile, tile), tile)
            raw = times_transposed(query, ks[at, :])
            prob = 1.0 / (1.0 + jnp.exp2(raw * factor + shift))
            if masked:
                prob = jnp.where(row_at >= col_at, prob, 0.0)
            return dot(prob.astype(BF), vs[at, :])

        total = part(i, True)
        if i > 0:
            total = lax.fori_loop(0, i, lambda j, acc: acc + part(j, False), total)
        os[i * tile : (i + 1) * tile, :] = total.astype(BF)


def forward_kernel(n_ctx, groups, units, tile, *refs):
    tokens_ref, cot_ref, gain_one, gain_two, wq_ref, wk_ref, wv_ref, wo_ref, cos_ref, sin_ref, bcos_ref, bsin_ref, valid_ref = refs[:13]
    n1_out, got_out, heads_out, residual, n2_out, cot_out = refs[13:19]
    x_ref, rows_buf, own_buf, send, got, o_send, o_got, tabs, qs, ks, vs, os = refs[19:31]
    rest = refs[31:]
    n_gather, n_exchange = len(Gather.scratch()), len(Exchange.scratch(1, 2))
    n1_sems, rest = rest[:n_gather], rest[n_gather:]
    n2_sems, rest = rest[:n_gather], rest[n_gather:]
    cot_sems, rest = rest[:n_gather], rest[n_gather:]
    x_sems, rest = rest[:n_exchange], rest[n_exchange:]
    o_sems, rest = rest[:n_exchange], rest[n_exchange:]
    (n1_sem, got_sem, load_sem), rest = rest[:3], rest[3:]
    me, rank = lax.axis_index("ctx"), lax.axis_index("tp")
    odd = lax.rem(rank, 2)
    heads = wq_ref.shape[1] // HD
    per_unit = n_ctx // heads
    own_at = [pl.multiple_of(odd * BLOCK, BLOCK), pl.multiple_of((1 - odd) * PAIR, BLOCK)]

    def load_x(g):
        _, rows, own = groups[g]
        return pltpu.make_async_copy(
            tokens_ref.at[pl.ds(own_at[g], rows)], x_ref.at[pl.ds(own, rows)], load_sem.at[g]
        )

    for g in range(2):
        load_x(g).start()
    greet(n_ctx, True)
    gather_one = Gather(own_buf, rows_buf, groups, n1_sems, local=False)
    gather_two = Gather(own_buf, n2_out, groups, n2_sems)
    gather_cot = Gather(cot_ref, cot_out, groups, cot_sems, own_at=own_at)
    scatter = Scatter(rows_buf, groups, rest[:6], rest[6:], loaded=False)
    trade = Exchange(got, x_sems, True)
    trade_back = Exchange(o_got, o_sems, False)

    def halves_of(u):
        return halves_at(odd if units[u][1] else 0)

    def normed(source, gain, at):
        values = source[at, :].astype(F32)
        return (values * inverse_rms(values) * gain[...]).astype(BF)

    def begin(g):
        base, rows, own = groups[g]
        load_x(g).wait()
        low = normed(x_ref, gain_one, pl.ds(own, rows))
        own_buf[pl.ds(own, rows), :] = low
        gather_one.start(g)
        rows_buf[pl.ds(base, rows), :] = low

    begin(0)
    for half, block in enumerate((me, 2 * n_ctx - 1 - me)):
        cos_part, sin_part = rotation(
            cos_ref[...], sin_ref[...], bcos_ref[pl.ds(block, 1), :], bsin_ref[pl.ds(block, 1), :]
        )
        tabs[0, half * BLOCK : (half + 1) * BLOCK, :] = cos_part
        tabs[1, half * BLOCK : (half + 1) * BLOCK, :] = sin_part

    def query(u, block):
        base, flipped = units[u]
        first, second = halves_of(u)
        at = pl.ds(base + block * PAIR, PAIR)
        rows = rows_buf[at, :]
        for which, w_ref in enumerate((wq_ref, wk_ref, wv_ref)):
            product = dot(rows, w_ref[...])
            for head in range(heads):
                part = product[:, head * HD : (head + 1) * HD]
                pair = block * heads + head
                for half, to in ((0, first), (1, second)):
                    piece = part[half * BLOCK : (half + 1) * BLOCK]
                    if which < 2:
                        piece = piece * tabs[0, to, :] + pltpu.roll(piece, HD // 2, 1) * tabs[1, to, :]
                    else:
                        piece = piece * valid_ref[pl.ds(base + block * PAIR + half * BLOCK, BLOCK), :]
                    send[u, pair, which, to, :] = piece.astype(BF)
        trade.start_some(send, u, block * heads, heads)

    store_n1 = pltpu.make_async_copy(rows_buf, n1_out, n1_sem)
    store_got = [pltpu.make_async_copy(got.at[u], got_out.at[u], got_sem.at[u]) for u in range(len(units))]

    query(0, 0)
    gather_one.forward_x(0)
    gather_one.forward_y(0)
    begin(1)
    query(0, 1)
    query(1, 0)
    gather_one.finish(0)
    query(1, 1)
    gather_one.forward(1)
    gather_one.finish(1)
    for g in range(2):
        gather_cot.start(g)
    query(2, 0)
    query(2, 1)
    store_n1.start()

    def attend(u):
        trade.arrived(send, u)
        store_got[u].start()
        for k in range(n_ctx):
            front, back = both_places(me, k, n_ctx)
            for which, dest in enumerate((qs, ks, vs)):
                dest[front, :] = got[u, k, which, :BLOCK, :]
                dest[back, :] = got[u, k, which, BLOCK:, :]
        attend_rows(qs, ks, vs, os, tile)
        for k in range(n_ctx):
            front, back = both_places(me, k, n_ctx)
            o_send[u, k, :BLOCK, :] = os[front, :]
            o_send[u, k, BLOCK:, :] = os[back, :]
        trade_back.start(o_send, u)

    def project(u):
        trade_back.arrived(o_send, u)
        base, _ = units[u]
        first, second = halves_of(u)
        for block in range(per_unit):
            at = pl.ds(base + block * PAIR, PAIR)
            low = valid_ref[at, :].astype(BF)
            for head in range(heads):
                place = jnp.bitwise_xor(me, block * heads + head)
                part = jnp.concatenate([o_got[u, place, first, :], o_got[u, place, second, :]], axis=0)
                heads_out[at, head * HD : (head + 1) * HD] = part * low
            rows_buf[at, :] = dot(heads_out[at, :], wo_ref[...]).astype(BF)

    def use(at, total):
        residual[at, :] = x_ref[at, :].astype(F32) + total
        own_buf[at, :] = normed(residual, gain_two, at)

    def finish_group(g):
        scatter.total(g, use)
        gather_two.start(g)

    attend(0)
    for g in range(2):
        gather_one.sent(g)
    store_n1.wait()
    attend(1)
    for g in range(2):
        gather_cot.forward(g)
    project(0)
    scatter.start(0, (0,), loads=False)
    project(1)
    scatter.start(0, (1, 3, 2), loads=False)
    attend(2)
    scatter.forward(0)
    project(2)
    scatter.start(1, loads=False)
    finish_group(0)
    scatter.forward(1)
    finish_group(1)
    gather_two.forward(0)
    gather_two.forward(1)
    for u in range(len(units)):
        trade.sent(send, u)
        trade_back.sent(o_send, u)
        store_got[u].wait()
    for g in range(2):
        gather_cot.finish(g)
        gather_two.finish(g)
        gather_two.sent(g)
        gather_cot.sent(g)


def forward_layer(tokens_in, cot_in, gain_one, gain_two, wq, wk, wv, wo, tables, valid, n_ctx, groups, units):
    rows, depth = tokens_in.shape
    width = wq.shape[1]
    tokens = valid.shape[0]
    length = 2 * n_ctx * BLOCK
    n_units = len(units)
    vmem = lambda shape, dtype=BF: pltpu.VMEM(shape, dtype)
    outs = [
        jax.ShapeDtypeStruct((tokens, depth), BF),
        jax.ShapeDtypeStruct((n_units, n_ctx, 3, PAIR, HD), BF),
        jax.ShapeDtypeStruct((tokens, width), BF),
        jax.ShapeDtypeStruct((rows, depth), F32),
        jax.ShapeDtypeStruct((tokens, depth), BF),
        jax.ShapeDtypeStruct((tokens, depth), BF),
    ]
    return pl.pallas_call(
        functools.partial(forward_kernel, n_ctx, groups, units, min(512, length)),
        out_shape=outs,
        in_specs=[ANY_SPEC, ANY_SPEC] + [VMEM_SPEC] * 11,
        out_specs=[ANY_SPEC, ANY_SPEC, VMEM_SPEC, VMEM_SPEC, ANY_SPEC, ANY_SPEC],
        scratch_shapes=[
            vmem((rows, depth)),
            vmem((tokens, depth)),
            vmem((rows, depth)),
            vmem((n_units, n_ctx, 3, PAIR, HD)),
            vmem((n_units, n_ctx, 3, PAIR, HD)),
            vmem((n_units, n_ctx, PAIR, HD)),
            vmem((n_units, n_ctx, PAIR, HD)),
            vmem((2, PAIR, HD), F32),
        ]
        + [vmem((length, HD))] * 4
        + Gather.scratch() * 3
        + Exchange.scratch(n_units, n_ctx) * 2
        + [pltpu.SemaphoreType.DMA, pltpu.SemaphoreType.DMA((n_units,)), pltpu.SemaphoreType.DMA((2,))]
        + Scatter.scratch(rows, depth, loaded=False),
        compiler_params=pltpu.CompilerParams(vmem_limit_bytes=VMEM_LIMIT, collective_id=3, has_side_effects=True),
        cost_estimate=pl.CostEstimate(
            flops=8 * tokens * depth * width, bytes_accessed=8 * tokens * depth, transcendentals=0
        ),
    )(tokens_in, cot_in, gain_one, gain_two, wq, wk, wv, wo, *tables, valid)


def attend_rows_back(qs, ks, vs, gs, os, dqs, cos_ref, sin_ref, tile):
    length = qs.shape[0]
    scale = HD ** (-0.5)
    factor = -scale * LOG2E
    shift = math.log(length) * LOG2E
    count = length // tile
    key_at = lax.broadcasted_iota(jnp.int32, (tile, tile), 0)
    query_at = lax.broadcasted_iota(jnp.int32, (tile, tile), 1)
    dqs[...] = jnp.zeros_like(dqs)

    def unrotate(values, at):
        return (values * cos_ref[at, :] - pltpu.roll(values, HD // 2, 1) * sin_ref[at, :]).astype(BF)

    for j in range(count):
        own = slice(j * tile, (j + 1) * tile)
        keys = ks[own, :]
        values = vs[own, :]

        def part(i, masked):
            at = pl.ds(pl.multiple_of(i * tile, tile), tile)
            query = qs[at, :]
            grad = gs[at, :]
            raw = times_transposed(keys, query)
            prob = 1.0 / (1.0 + jnp.exp2(raw * factor + shift))
            if masked:
                prob = jnp.where(query_at >= key_at, prob, 0.0)
            prob_grad = times_transposed(values, grad)
            score_grad = (prob_grad * prob * (1.0 - prob)).astype(BF)
            dqs[at, :] += contract_rows(score_grad, keys)
            return dot(score_grad, query), dot(prob.astype(BF), grad)

        total = part(j, True)
        if j + 1 < count:

            def step(i, acc):
                more = part(i, False)
                return acc[0] + more[0], acc[1] + more[1]

            total = lax.fori_loop(j + 1, count, step, total)
        os[1, own, :] = unrotate(total[0] * scale, own)
        os[2, own, :] = total[1].astype(BF)
    for i in range(count):
        at = slice(i * tile, (i + 1) * tile)
        os[0, at, :] = unrotate(dqs[at, :] * scale, at)


def middle_kernel(n_ctx, groups, units, tile, *refs):
    da_ref, got_ref, h_ref, residual_ref, wd_ref, wq_ref, wk_ref, wv_ref, wo_ref = refs[:9]
    cos_ref, sin_ref, bcos_ref, bsin_ref, valid_ref = refs[9:14]
    grad_ref, partial_out, output = refs[14:17]
    rows_buf, got, do_send, do_got, back_got, h_buf, wd_buf, res_buf, cos_full, sin_full = refs[17:27]
    qs, ks, vs, gs, os, dqs = refs[27:33]
    rest = refs[33:]
    back_send = got
    n_exchange = len(Exchange.scratch(1, 2))
    do_sems, back_sems, rest = rest[:n_exchange], rest[n_exchange : 2 * n_exchange], rest[2 * n_exchange :]
    (da_sem, got_sem, out_sem, h_sem, wd_sem, res_sem, y_sem), rest = rest[:7], rest[7:]
    me, rank = lax.axis_index("ctx"), lax.axis_index("tp")
    odd = lax.rem(rank, 2)
    heads = wq_ref.shape[1] // HD
    per_unit = n_ctx // heads
    unit_rows = per_unit * PAIR
    count = len(units)
    order = in_turn(count)

    def rows_of(u):
        return pl.ds(units[u][0], unit_rows)

    load_da = [pltpu.make_async_copy(da_ref.at[rows_of(u)], rows_buf.at[rows_of(u)], da_sem.at[u]) for u in range(count)]
    load_got = [pltpu.make_async_copy(got_ref.at[u], got.at[u], got_sem.at[u]) for u in range(count)]
    for u in order:
        load_da[u].start()
    for u in order:
        load_got[u].start()
    first_wd = pltpu.make_async_copy(wd_ref.at[:, pl.ds(0, wd_buf.shape[1])], wd_buf, wd_sem)
    first_wd.start()
    greet(n_ctx, True)
    scatter = Scatter(rows_buf, groups, rest[:6], rest[6:], loaded=False)
    trade = Exchange(do_got, do_sems, True)
    trade_back = Exchange(back_got, back_sems, False)

    for u in order:
        load_da[u].wait()
        base, flipped = units[u]
        first, second = halves_at(odd if flipped else 0)
        for block in range(per_unit):
            at = pl.ds(base + block * PAIR, PAIR)
            grad = times_transposed(rows_buf[at, :], wo_ref[...]).astype(BF)
            low = valid_ref[at, :].astype(BF)
            for head in range(heads):
                part = grad[:, head * HD : (head + 1) * HD] * low
                do_send[u, block * heads + head, first, :] = part[:BLOCK]
                do_send[u, block * heads + head, second, :] = part[BLOCK:]
        trade.start(do_send, u)
    for block in range(2 * n_ctx):
        at = slice(block * BLOCK, (block + 1) * BLOCK)
        cos_full[at, :], sin_full[at, :] = rotation(
            cos_ref[...], sin_ref[...], bcos_ref[block : block + 1, :], bsin_ref[block : block + 1, :]
        )
    for u in order:
        load_got[u].wait()

    def attend(turn, carry):
        u = lax.rem(turn + count - 1, count)
        trade.arrived(do_send, u)
        for k in range(n_ctx):
            front, back = both_places(me, k, n_ctx)
            for which, dest in enumerate((qs, ks, vs)):
                dest[front, :] = got[u, k, which, :BLOCK, :]
                dest[back, :] = got[u, k, which, BLOCK:, :]
            gs[front, :] = do_got[u, k, :BLOCK, :]
            gs[back, :] = do_got[u, k, BLOCK:, :]
        attend_rows_back(qs, ks, vs, gs, os, dqs, cos_full, sin_full, tile)
        for k in range(n_ctx):
            front, back = both_places(me, k, n_ctx)
            for which in range(3):
                back_send[u, k, which, :BLOCK, :] = os[which, front, :]
                back_send[u, k, which, BLOCK:, :] = os[which, back, :]
        trade_back.start(back_send, u)
        return carry

    lax.fori_loop(0, count, attend, 0)

    tiles = rows_buf.shape[0] // PAIR

    def tile_rows(tile):
        return pl.ds(pl.multiple_of(tile * PAIR, PAIR), PAIR)

    def load_h(step):
        slot = lax.rem(step, 2)
        return pltpu.make_async_copy(h_ref.at[tile_rows(lax.rem(step, tiles))], h_buf.at[slot], h_sem.at[slot])

    columns = wd_buf.shape[1]
    parts = rows_buf.shape[1] // columns

    def part_columns(part):
        return pl.ds(pl.multiple_of(part * columns, columns), columns)

    def load_wd(part):
        return pltpu.make_async_copy(wd_ref.at[:, part_columns(part)], wd_buf, wd_sem)

    load_h(0).start()

    def down(step, carry):
        part, tile = step // tiles, lax.rem(step, tiles)

        @pl.when(step + 1 < tiles * parts)
        def _():
            load_h(step + 1).start()

        @pl.when(tile == 0)
        def _():
            @pl.when(part > 0)
            def _():
                load_wd(part).start()

            load_wd(part).wait()

        load_h(step).wait()
        rows_buf[tile_rows(tile), part_columns(part)] = dot(h_buf[lax.rem(step, 2)], wd_buf[...]).astype(BF)
        return carry

    lax.fori_loop(0, tiles * parts, down, 0)
    last_group = len(groups) - 1
    out_rows = rest[0]
    for g in (last_group, 0):
        scatter.start(g, loads=False)

    def use(at, total):
        size = total.shape[0]
        load = pltpu.make_async_copy(residual_ref.at[at], res_buf.at[pl.ds(0, size)], res_sem)
        load.start()
        load.wait()
        low = (res_buf[:size, :] + total).astype(BF)
        out_rows[at, :] = low

    def store(number, first):
        slot = number % 2
        return pltpu.make_async_copy(h_buf.at[slot], partial_out.at[pl.ds(first, PAIR)], out_sem.at[slot])

    stored = []
    for turn, u in enumerate(order):
        trade_back.arrived(back_send, u)
        base, flipped = units[u]
        first, second = halves_at(odd if flipped else 0)
        for block in range(per_unit):
            at = pl.ds(base + block * PAIR, PAIR)
            low = valid_ref[at, :].astype(BF)
            total = None
            for which, w_ref in enumerate((wq_ref, wk_ref, wv_ref)):
                width = heads * HD
                for head in range(heads):
                    place = jnp.bitwise_xor(me, block * heads + head)
                    part = jnp.concatenate(
                        [back_got[u, place, which, first, :], back_got[u, place, which, second, :]], axis=0
                    )
                    columns = slice(which * width + head * HD, which * width + (head + 1) * HD)
                    grad_ref[at, columns] = part * low if which == 2 else part
                product = times_transposed(grad_ref[at, which * width : (which + 1) * width], w_ref[...])
                total = product if total is None else total + product
            number = len(stored)
            if number >= 2:
                stored[number - 2].wait()
            h_buf[number % 2] = total.astype(BF)
            stored.append(store(number, base + block * PAIR))
            stored[-1].start()
        if turn == 0:
            scatter.forward(last_group)
            scatter.forward(0)
        if turn == 1:
            for g in (last_group, 0):
                scatter.total(g, use)
            store_y = pltpu.make_async_copy(out_rows, output, y_sem)
            store_y.start()
    store_y.wait()
    for copy in stored[-2:]:
        copy.wait()
    for u in order:
        trade.sent(do_send, u)
        trade_back.sent(back_send, u)


def middle_layer(da, got, h, residual, wq, wk, wv, wo, wd, tables, valid, n_ctx, groups, units):
    tokens, depth = da.shape
    width = wq.shape[1]
    length = 2 * n_ctx * BLOCK
    count = len(units)
    vmem = lambda shape, dtype=BF: pltpu.VMEM(shape, dtype)
    dma = pltpu.SemaphoreType.DMA
    three, one = (count, n_ctx, 3, PAIR, HD), (count, n_ctx, PAIR, HD)
    most_rows = max(rows for _, rows, _ in groups) // 2
    return pl.pallas_call(
        functools.partial(middle_kernel, n_ctx, groups, units, min(512, length)),
        out_shape=[
            jax.ShapeDtypeStruct((tokens, 3 * width), BF),
            jax.ShapeDtypeStruct((tokens, depth), BF),
            jax.ShapeDtypeStruct(residual.shape, BF),
        ],
        in_specs=[ANY_SPEC] * 5 + [VMEM_SPEC] * 9,
        out_specs=[VMEM_SPEC, ANY_SPEC, ANY_SPEC],
        scratch_shapes=[vmem((tokens, depth)), vmem(three), vmem(one), vmem(one), vmem(three)]
        + [vmem((2, PAIR, depth)), vmem((h.shape[1], depth // 2)), vmem((most_rows, depth), F32)]
        + [vmem((length, HD), F32)] * 2
        + [vmem((length, HD))] * 4
        + [vmem((3, length, HD)), vmem((length, HD), F32)]
        + Exchange.scratch(count, n_ctx) * 2
        + [dma((count,)), dma((count,)), dma((2,)), dma((2,)), dma, dma, dma]
        + Scatter.scratch(residual.shape[0], depth, loaded=False),
        compiler_params=pltpu.CompilerParams(vmem_limit_bytes=VMEM_LIMIT, collective_id=4, has_side_effects=True),
        cost_estimate=pl.CostEstimate(
            flops=8 * tokens * depth * width + 2 * tokens * depth * h.shape[1],
            bytes_accessed=8 * tokens * depth,
            transcendentals=0,
        ),
    )(da, got, h, residual, wd, wq, wk, wv, wo, *tables, valid)


def body(
    tokens,
    counts,
    norm_gain,
    w_query,
    w_key,
    w_value,
    w_output,
    mlp_gain,
    w_gate,
    w_up,
    w_down,
    cotangent,
):
    n_ctx = lax.axis_size("ctx")
    me = lax.axis_index("ctx")
    rank = lax.axis_index("tp")
    odd = rank & 1
    core = me & 1
    length = 2 * BLOCK * n_ctx
    heads = w_query.shape[1] // HD
    gain_one = norm_gain.astype(F32)
    gain_two = mlp_gain.astype(F32)

    inverse = THETA ** (-(jnp.arange(HD // 2, dtype=F32) * (2.0 / HD)))
    angles = jnp.arange(length, dtype=jnp.int32).astype(F32)[:, None] * inverse[None, :]
    cos_half, sin_half = jnp.cos(angles), jnp.sin(angles)
    cos_full = jnp.concatenate([cos_half, cos_half], axis=1)
    sin_full = jnp.concatenate([-sin_half, sin_half], axis=1)

    def own_blocks(table):
        front = lax.dynamic_slice_in_dim(table, me * BLOCK, BLOCK, 0)
        back = lax.dynamic_slice_in_dim(table, (2 * n_ctx - 1 - me) * BLOCK, BLOCK, 0)
        return front, back

    cos_front, cos_back = own_blocks(cos_full)
    sin_front, sin_back = own_blocks(sin_full)
    own_counts = lax.dynamic_index_in_dim(counts, me, 0, keepdims=False)
    offsets = jnp.arange(BLOCK, dtype=jnp.int32)

    def valid_of(sequence_list, half_list):
        held = own_counts[jnp.stack(sequence_list), jnp.stack(half_list)]
        return (offsets[None, :] < held[:, None]).astype(F32).reshape(-1)

    cos_own = jnp.concatenate([cos_front, cos_back])
    sin_own = jnp.concatenate([sin_front, sin_back])
    sequences = counts.shape[1]
    paired = by_four() and sequences == 6 and n_ctx == 2 * heads
    if paired:
        ranks = [rank ^ k for k in range(4)]
        blocks_a = [(3 * (r >> 1) + 2 * (r & 1), jnp.int32(half)) for r in ranks for half in range(2)]
        blocks_b = [(1 + 3 * (r >> 1), r & 1) for r in ranks]
        flat_valid = valid_of(*zip(*(blocks_a + blocks_b)))
        valids = {"b": flat_valid[len(blocks_a) * BLOCK :], "a": flat_valid[: len(blocks_a) * BLOCK]}
        flip_back = lambda own: jnp.where(odd == 1, jnp.roll(own, BLOCK, axis=0), own)
        tables = {
            "b": (jnp.tile(flip_back(cos_own), (2, 1)), jnp.tile(flip_back(sin_own), (2, 1))),
            "a": (jnp.tile(cos_own, (4, 1)), jnp.tile(sin_own, (4, 1))),
        }
        scalars = {"b": jnp.stack([me, odd]).astype(jnp.int32), "a": jnp.stack([me, 0]).astype(jnp.int32)}
        n_pairs = {"b": 2 * heads, "a": 4 * heads}
    else:
        flat_valid = (offsets[None, None, :] < own_counts[:, :, None]).astype(F32).reshape(-1)
        valids = {"a": flat_valid}
        tables = {"a": (jnp.tile(cos_own, (sequences, 1)), jnp.tile(sin_own, (sequences, 1)))}
        scalars = {"a": jnp.stack([me, 0]).astype(jnp.int32)}
        n_pairs = {"a": sequences * heads}
    names = tuple(n_pairs)

    def own_rows(array):
        if not paired:
            return {"a": array}
        return {
            "b": lax.dynamic_slice_in_dim(array, (1 - odd) * PAIR, BLOCK, 0),
            "a": lax.dynamic_slice_in_dim(array, odd * BLOCK, PAIR, 0),
        }

    def whole_rows(array):
        return jnp.where(odd == 1, jnp.roll(array, BLOCK, axis=0), array) if paired else array

    x_own = {name: rows.astype(F32) for name, rows in own_rows(tokens[0]).items()}
    g_own = own_rows(cotangent[0])

    split = by_four()
    rows_of = {name: valids[name].shape[0] for name in names}
    total_rows = sum(rows_of.values())
    first_row = {"a": 0, "b": rows_of["a"]}
    valid_head = {name: jnp.broadcast_to(valids[name][:, None], (rows_of[name], HD)) for name in names}
    valid_wide = {name: jnp.broadcast_to(valids[name][:, None].astype(BF), (rows_of[name], heads * HD)) for name in names}
    near = [k for k in range(n_ctx) if k < 6]
    far = [k for k in range(n_ctx) if k >= 6]
    state = {}

    def fence():
        names_held = list(state)
        values = lax.optimization_barrier([state[name] for name in names_held])
        state.update(zip(names_held, values))

    def only_b(step):
        if "b" in names:
            step("b")

    def norm_one(n):
        state["n1", n] = (x_own[n] * inverse_rms(x_own[n]) * gain_one).astype(BF)

    def gather_a(key):
        def step(n):
            state[key, n] = gather_first(state[key, n])

        return step

    def gather_b(key):
        def step(n):
            state[key, n] = gather_second(state[key, n])

        return step

    def query(n):
        state["n1", n] = gathered(state["n1", n])
        cos_tab, sin_tab = tables[n]
        state["qkv", n] = project_qkv(
            scalars[n], state["n1", n], w_query, w_key, w_value, cos_tab, sin_tab, valid_head[n], n_ctx
        )

    def swap_part(key, places, to):
        def step(n):
            got = dict(state.get((to, n), {}))
            got.update(exchange(state[key, n], places, n_ctx))
            state[to, n] = got
            if len(got) == n_ctx:
                state[to, n] = [got[k] for k in range(n_ctx)]
                del state[key, n]

        return step

    def attend(n):
        state["mixed", n] = attention_forward(scalars[n], state["got", n], n_ctx)

    def project(n):
        heads_out, *parts = project_out(
            scalars[n], state.pop(("back", n)), w_output, valid_wide[n], n_pairs[n], n_ctx, split
        )
        state["heads", n], state["r", n] = heads_out, tuple(parts)

    def scatter_a(key):
        def step(n):
            state[key, n] = scatter_first(state[key, n])

        return step

    def scatter_b(key):
        def step(n):
            state[key, n] = scatter_second(state[key, n])

        return step

    def norm_two(n):
        residual = x_own[n] + scattered(state.pop(("r", n)))
        state["residual", n] = residual
        state["n2", n] = (residual * inverse_rms(residual) * gain_two).astype(BF)

    def core_mlp(n):
        state["n2", n] = gathered(state["n2", n])
        state["cot", n] = gathered(state["cot", n])
        held = state.get("mlp", ())
        state["mlp"] = mlp_core(
            state["n2", n], state["cot", n], w_gate, w_up, w_down, total_rows, first_row[n], held
        )

    def attend_back(n):
        state["dqkv", n] = attention_backward(
            scalars[n], state.pop(("got", n)), state.pop(("gdo", n)), cos_full, sin_full, n_ctx
        )

    def query_back(n):
        dq, dk, dv, *parts = project_in(
            scalars[n], state.pop(("gdqkv", n)), (w_query, w_key, w_value), valid_wide[n], n_pairs[n], n_ctx, False
        )
        state["dq", n], state["dk", n], state["dv", n], state["i", n] = dq, dk, dv, parts[0]

    def joined(key):
        parts = [state[key, n] for n in ("a", "b") if n in names]
        return jnp.concatenate(parts) if len(parts) > 1 else parts[0]

    groups = tuple((first_row[n], rows_of[n] // 4, first_row[n] // 4) for n in ("a", "b") if n in names)

    if paired:
        units = ((0, False), (2 * PAIR, False), (4 * PAIR, True))
        wide_valid = jnp.broadcast_to(flat_valid[:, None], (total_rows, HD))
        twice = lambda table: jnp.concatenate([table, table], axis=1)
        starts = BLOCK * jnp.arange(2 * n_ctx, dtype=jnp.int32)
        spans = [at.astype(F32)[:, None] * inverse[None, :] for at in (offsets, starts)]
        turns = [twice(part(angle)) for angle in spans for part in (jnp.cos, jnp.sin)]
        all_n1, got, heads_out, own_residual, all_n2, all_cot = forward_layer(
            tokens[0], cotangent[0], gain_one[None], gain_two[None], w_query, w_key, w_value, w_output,
            turns, wide_valid, n_ctx, groups, units,
        )
    else:
        norm_one("a")
        state["cot", "a"] = g_own["a"]
        gather_a("n1")("a")
        query("a")
        swap_part("qkv", range(n_ctx), "got")("a")
        attend("a")
        swap_part("mixed", range(n_ctx), "back")("a")
        project("a")
        scatter_a("r")("a")
        norm_two("a")
        gather_a("n2")("a")
        gather_a("cot")("a")
        all_n1, all_n2, all_cot = state["n1", "a"], gathered(state["n2", "a"]), gathered(state["cot", "a"])
        heads_out, own_residual = state["heads", "a"], state["residual", "a"]
    if paired:
        extra = feed_extra(groups, all_n2, w_gate, w_up, w_down, own_residual, cotangent[0], gain_two[None])
        sum_down, sum_gate, sum_up, sum_out, dr, da, gain_two_grad, _, h, _, _ = weight_sums(
            [(w_down.shape[0], 0), (all_n2, 1), (all_n2, 2), (heads_out, 3)],
            [all_cot], n_ctx, 1, extra, late=(5, 6, 1), limit=62 * 1024 * 1024,
        )
        dqkv, i_partial, output = middle_layer(
            da, got, h, own_residual, w_query, w_key, w_value, w_output, w_down, turns, wide_valid, n_ctx, groups, units
        )
        extra = input_extra(n_ctx, groups, i_partial, tokens[0], dr, gain_one[None], gain_two_grad)
        sum_qkv, input_grad, gain_sums = weight_sums(
            [(all_n1, 0)], [dqkv], n_ctx, 2, extra, limit=36 * 1024 * 1024
        )
        gains = gain_sums[::8]
    else:
        own_grads = cotangent[0]
        h, dgp, dup = mlp_core(all_n2, all_cot, w_gate, w_up, w_down, total_rows, 0)
        d_partial = (times_transposed(dgp, w_gate) + times_transposed(dup, w_up)).astype(BF)
        y_partial = dot(h, w_down).astype(BF)
        (sum_down,) = weight_sums([(h, 0)], [all_cot], n_ctx, 1)
        sum_gate, sum_up = weight_sums([(all_n2, 0), (all_n2, 1)], [dgp, dup], n_ctx, 2)
        back, gain_two_grad = norm_back_rows(own_residual, gain_two, scattered(scatter_first((d_partial,))))
        dr = own_grads.astype(F32) + back
        da = gathered(gather_first(dr.astype(BF)))
        output = (own_residual + scattered(scatter_first((y_partial,)))).astype(BF)
        state["do", "a"] = heads_back(scalars["a"], da, w_output, valid_wide["a"], n_ctx)
        swap_part("do", range(n_ctx), "gdo")("a")
        attend_back("a")
        swap_part("dqkv", range(n_ctx), "gdqkv")("a")
        query_back("a")
        (sum_out,) = weight_sums([(heads_out, 0)], [da], n_ctx, 3)
        (sum_qkv,) = weight_sums(
            [(all_n1, 0)], [jnp.concatenate([state[key, "a"] for key in ("dq", "dk", "dv")], axis=1)], n_ctx, 4
        )
        back, gain_one_grad = norm_back_rows(x_own["a"], gain_one, scattered(scatter_first((state["i", "a"],))))
        input_grad = (dr + back).astype(BF)
    grad_query, grad_key, grad_value = (part.astype(F32) for part in jnp.split(sum_qkv, 3, axis=1))
    if not paired:
        gains = lax.psum(jnp.concatenate([gain_one_grad, gain_two_grad]), ("ctx", "tp"))
    return (
        whole_rows(output)[None],
        whole_rows(input_grad)[None],
        gains[0],
        grad_query,
        grad_key,
        grad_value,
        sum_out.astype(F32),
        gains[1],
        sum_gate.astype(F32),
        sum_up.astype(F32),
        sum_down.astype(F32),
    )


def solution(mesh):
    placed = (
        P("ctx", "tp", None),
        P(),
        P(),
        P(None, "tp"),
        P(None, "tp"),
        P(None, "tp"),
        P("tp", None),
        P(),
        P(None, "tp"),
        P(None, "tp"),
        P("tp", None),
        P("ctx", "tp", None),
    )
    return jax.shard_map(
        body,
        mesh=mesh,
        in_specs=placed,
        out_specs=(
            P("ctx", "tp", None),
            P("ctx", "tp", None),
            P(),
            P(None, "tp"),
            P(None, "tp"),
            P(None, "tp"),
            P("tp", None),
            P(),
            P(None, "tp"),
            P(None, "tp"),
            P("tp", None),
        ),
        check_vma=False,
    )
```

```python
import functools
import math

import jax
import jax.numpy as jnp
from jax import lax
from jax.experimental import pallas as pl
from jax.experimental.pallas import tpu as pltpu
from jax.sharding import PartitionSpec as P

HD = 128
BLOCK = 128
PAIR = 2 * BLOCK
EPS = 1e-05
THETA = 10000.0
LOG2E = 1.4426950408889634
BF = jnp.bfloat16
F32 = jnp.float32
VMEM_LIMIT = 60 * 1024 * 1024

X_SWAP = [(i, i ^ 1) for i in range(4)]
Y_SWAP = [(i, i ^ 2) for i in range(4)]


def dot(left, right):
    return jnp.dot(left, right, preferred_element_type=F32)


def contract_rows(left, right):
    return lax.dot_general(left, right, (((0,), (0,)), ((), ())), preferred_element_type=F32)


def times_transposed(left, right):
    return lax.dot_general(left, right, (((1,), (1,)), ((), ())), preferred_element_type=F32)


def send_x(values):
    return lax.ppermute(values, "tp", X_SWAP)


def send_y(values):
    return lax.ppermute(values, "tp", Y_SWAP)


def by_four():
    return lax.axis_size("tp") == 4


def gather_first(own):
    if not by_four():
        return (lax.all_gather(own, "tp", axis=0, tiled=True),)
    return own, send_x(own), send_y(own)


def gather_second(held):
    if len(held) == 1:
        return held
    own, from_x, from_y = held
    half = own.shape[0] // 2
    return own, from_x, from_y, send_x(from_y[:half]), send_y(from_x[half:])


def gathered(held):
    return jnp.concatenate(held) if len(held) > 1 else held[0]


def scatter_parts(partial):
    if not by_four():
        return (partial,)
    rows = partial.shape[0] // 4
    half = rows // 2
    at = lambda first: partial[first * half : (first + 1) * half]
    return (
        jnp.concatenate([at(2), at(6)]),
        jnp.concatenate([at(5), at(7)]),
        jnp.concatenate([at(0), at(1), at(4), at(3)]),
    )


def scatter_first(parts):
    if len(parts) == 1:
        return (lax.psum_scatter(parts[0], "tp", scatter_dimension=0, tiled=True),)
    return send_x(parts[0]), send_y(parts[1]), parts[2]


def add_low(left, right):
    return (left.astype(F32) + right.astype(F32)).astype(BF)


def scatter_second(held):
    if len(held) == 1:
        return held
    from_x, from_y, stay = held
    half = from_x.shape[0] // 2
    low_rest = send_y(add_low(stay[2 * half : 3 * half], from_x[half:]))
    high_rest = send_x(add_low(stay[3 * half :], from_y[half:]))
    return from_x, from_y, stay, low_rest, high_rest


def scattered(held):
    if len(held) == 1:
        return held[0].astype(F32)
    from_x, from_y, stay, low_rest, high_rest = (part.astype(F32) for part in held)
    half = low_rest.shape[0]
    low = stay[:half] + from_x[:half] + low_rest
    high = stay[half : 2 * half] + from_y[:half] + high_rest
    return jnp.concatenate([low, high])


def exchange(pieces, places, n_ctx):
    got = {}
    for k in places:
        got[k] = pieces[k] if k == 0 else lax.ppermute(pieces[k], "ctx", [(i, i ^ k) for i in range(n_ctx)])
    return got


def params():
    return pltpu.CompilerParams(vmem_limit_bytes=VMEM_LIMIT)


def whole(shape):
    return pl.BlockSpec(shape, lambda *_: (0,) * len(shape))


def put_partial(refs, first, value, rows):
    if len(refs) == 1:
        refs[0][first : first + value.shape[0], :] = value
        return
    to_x, to_y, stay = refs
    half = rows // 2
    homes = {
        0: (stay, 0), 1: (stay, 1), 2: (to_x, 0), 3: (stay, 3), 4: (stay, 2), 5: (to_y, 0), 6: (to_x, 1), 7: (to_y, 1)
    }
    for part in range(value.shape[0] // half):
        ref, place = homes[first // half + part]
        ref[place * half : (place + 1) * half, :] = value[part * half : (part + 1) * half]


def partial_shapes(rows, width, split):
    if not split:
        return [jax.ShapeDtypeStruct((rows, width), BF)]
    return [jax.ShapeDtypeStruct((rows // 4, width), BF)] * 2 + [jax.ShapeDtypeStruct((rows // 2, width), BF)]


def per_device(pairs, n_ctx):
    return -(-pairs // n_ctx)


def halves_at(swap):
    first = pl.multiple_of(swap * BLOCK, BLOCK)
    second = pl.multiple_of((1 - swap) * BLOCK, BLOCK)
    return pl.ds(first, BLOCK), pl.ds(second, BLOCK)


def qkv_kernel(n_ctx, pairs, scalar_ref, n_ref, wq_ref, wk_ref, wv_ref, cos_ref, sin_ref, valid_ref, *rest):
    out_refs, buffer = rest[:n_ctx], rest[n_ctx]
    rows = n_ref[...]
    first, second = halves_at(scalar_ref[1])
    me = scalar_ref[0]
    cos_tab = cos_ref[...]
    sin_tab = sin_ref[...]
    heads = wq_ref.shape[1] // HD
    step = pl.program_id(0)
    per = out_refs[0].shape[0]
    for pair in range(pairs, per * n_ctx):
        buffer[pair] = jnp.zeros(buffer.shape[1:], BF)
    for which, w_ref in enumerate((wq_ref, wk_ref, wv_ref)):
        product = dot(rows, w_ref[...])
        for head in range(heads):
            part = product[:, head * HD : (head + 1) * HD]
            if which < 2:
                part = part * cos_tab + pltpu.roll(part, HD // 2, 1) * sin_tab
            else:
                part = part * valid_ref[...]
            part = part.astype(BF)
            buffer[step * heads + head, which, first, :] = part[:BLOCK]
            buffer[step * heads + head, which, second, :] = part[BLOCK:]

    @pl.when(step == pl.num_programs(0) - 1)
    def _():
        for k in range(n_ctx):
            source = jnp.bitwise_xor(me, k)
            for p in range(per):
                out_refs[k][p] = buffer[source * per + p]


def project_qkv(scalars, normed, wq, wk, wv, cos_tab, sin_tab, valid, n_ctx):
    rows, depth = normed.shape
    width = wq.shape[1]
    heads = width // HD
    steps = rows // PAIR
    per = per_device(steps * heads, n_ctx)
    row_block = pl.BlockSpec((PAIR, HD), lambda i, s: (i, 0))
    weight = whole((depth, width))
    piece = (per, 3, PAIR, HD)
    return pl.pallas_call(
        functools.partial(qkv_kernel, n_ctx, steps * heads),
        out_shape=[jax.ShapeDtypeStruct(piece, BF)] * n_ctx,
        grid_spec=pltpu.PrefetchScalarGridSpec(
            num_scalar_prefetch=1,
            grid=(steps,),
            in_specs=[
                pl.BlockSpec((PAIR, depth), lambda i, s: (i, 0)),
                weight,
                weight,
                weight,
                row_block,
                row_block,
                row_block,
            ],
            out_specs=[whole(piece)] * n_ctx,
            scratch_shapes=[pltpu.VMEM((per * n_ctx, 3, PAIR, HD), BF)],
        ),
        compiler_params=params(),
        cost_estimate=pl.CostEstimate(
            flops=6 * rows * depth * width, bytes_accessed=rows * depth * 2 + 6 * depth * width, transcendentals=0
        ),
    )(scalars, normed, wq, wk, wv, cos_tab, sin_tab, valid)


def out_kernel(n_ctx, pairs, scalar_ref, *refs):
    piece_refs, (w_ref, valid_ref), (heads_ref, *partial_refs), buffer = (
        refs[:n_ctx],
        refs[n_ctx : n_ctx + 2],
        refs[n_ctx + 2 : -1],
        refs[-1],
    )
    me = scalar_ref[0]
    first, second = halves_at(scalar_ref[1])
    per = piece_refs[0].shape[0]
    heads = w_ref.shape[0] // HD
    for k in range(n_ctx):
        source = jnp.bitwise_xor(me, k)
        for p in range(per):
            buffer[source * per + p] = piece_refs[k][p]
    weight = w_ref[...]
    for sequence in range(pairs // heads):
        at = slice(sequence * PAIR, (sequence + 1) * PAIR)
        rows = jnp.concatenate(
            [
                jnp.concatenate(
                    [buffer[sequence * heads + head, first, :], buffer[sequence * heads + head, second, :]], axis=0
                )
                for head in range(heads)
            ],
            axis=1,
        )
        rows = rows * valid_ref[at, :]
        heads_ref[at, :] = rows
        put_partial(partial_refs, sequence * PAIR, dot(rows, weight).astype(BF), pairs // heads * PAIR // 4)


def project_out(scalars, pieces, weight, valid, pairs, n_ctx, split):
    width, depth = weight.shape
    rows = valid.shape[0]
    per = pieces[0].shape[0]
    shapes = [jax.ShapeDtypeStruct((rows, width), BF)] + partial_shapes(rows, depth, split)
    return pl.pallas_call(
        functools.partial(out_kernel, n_ctx, pairs),
        out_shape=shapes,
        grid_spec=pltpu.PrefetchScalarGridSpec(
            num_scalar_prefetch=1,
            grid=(1,),
            in_specs=[whole(piece.shape) for piece in pieces] + [whole(weight.shape), whole(valid.shape)],
            out_specs=[whole(shape.shape) for shape in shapes],
            scratch_shapes=[pltpu.VMEM((per * n_ctx, PAIR, HD), BF)],
        ),
        compiler_params=params(),
        cost_estimate=pl.CostEstimate(
            flops=2 * rows * depth * width, bytes_accessed=rows * depth * 2 + 2 * depth * width, transcendentals=0
        ),
    )(scalars, *pieces, weight, valid)


def heads_back_kernel(n_ctx, scalar_ref, da_ref, w_ref, valid_ref, *rest):
    out_refs, buffer = rest[:n_ctx], rest[n_ctx]
    me = scalar_ref[0]
    first, second = halves_at(scalar_ref[1])
    per = out_refs[0].shape[0]
    heads = w_ref.shape[0] // HD
    weight = w_ref[...]
    for pair in range(da_ref.shape[0] // PAIR * heads, per * n_ctx):
        buffer[pair] = jnp.zeros(buffer.shape[1:], BF)
    for sequence in range(da_ref.shape[0] // PAIR):
        at = slice(sequence * PAIR, (sequence + 1) * PAIR)
        grad = times_transposed(da_ref[at, :], weight).astype(BF) * valid_ref[at, :]
        for head in range(heads):
            part = grad[:, head * HD : (head + 1) * HD]
            buffer[sequence * heads + head, first, :] = part[:BLOCK]
            buffer[sequence * heads + head, second, :] = part[BLOCK:]
    for k in range(n_ctx):
        source = jnp.bitwise_xor(me, k)
        for p in range(per):
            out_refs[k][p] = buffer[source * per + p]


def heads_back(scalars, da, weight, valid, n_ctx):
    rows, depth = da.shape
    width = weight.shape[0]
    per = per_device(rows // PAIR * (width // HD), n_ctx)
    piece = (per, PAIR, HD)
    return pl.pallas_call(
        functools.partial(heads_back_kernel, n_ctx),
        out_shape=[jax.ShapeDtypeStruct(piece, BF)] * n_ctx,
        grid_spec=pltpu.PrefetchScalarGridSpec(
            num_scalar_prefetch=1,
            grid=(1,),
            in_specs=[whole(da.shape), whole(weight.shape), whole(valid.shape)],
            out_specs=[whole(piece)] * n_ctx,
            scratch_shapes=[pltpu.VMEM((per * n_ctx, PAIR, HD), BF)],
        ),
        compiler_params=params(),
        cost_estimate=pl.CostEstimate(
            flops=2 * rows * depth * width, bytes_accessed=rows * depth * 2 + 2 * depth * width, transcendentals=0
        ),
    )(scalars, da, weight, valid)


def in_kernel(n_ctx, pairs, scalar_ref, *refs):
    piece_refs, weight_refs, valid_ref = refs[:n_ctx], refs[n_ctx : n_ctx + 3], refs[n_ctx + 3]
    grad_refs, partial_refs, buffer = refs[n_ctx + 4 : n_ctx + 7], refs[n_ctx + 7 : -1], refs[-1]
    me = scalar_ref[0]
    first, second = halves_at(scalar_ref[1])
    per = piece_refs[0].shape[0]
    heads = weight_refs[0].shape[1] // HD
    for k in range(n_ctx):
        source = jnp.bitwise_xor(me, k)
        for p in range(per):
            buffer[source * per + p] = piece_refs[k][p]
    for sequence in range(pairs // heads):
        at = slice(sequence * PAIR, (sequence + 1) * PAIR)
        total = None
        for which in range(3):
            rows = jnp.concatenate(
                [
                    jnp.concatenate([buffer[pair, which, first, :], buffer[pair, which, second, :]], axis=0)
                    for pair in range(sequence * heads, (sequence + 1) * heads)
                ],
                axis=1,
            )
            if which == 2:
                rows = rows * valid_ref[at, :]
            grad_refs[which][at, :] = rows
            product = times_transposed(rows, weight_refs[which][...])
            total = product if total is None else total + product
        put_partial(partial_refs, sequence * PAIR, total.astype(BF), pairs // heads * PAIR // 4)


def project_in(scalars, pieces, weights, valid, pairs, n_ctx, split):
    depth, width = weights[0].shape
    rows = valid.shape[0]
    per = pieces[0].shape[0]
    shapes = [jax.ShapeDtypeStruct((rows, width), BF)] * 3 + partial_shapes(rows, depth, split)
    return pl.pallas_call(
        functools.partial(in_kernel, n_ctx, pairs),
        out_shape=shapes,
        grid_spec=pltpu.PrefetchScalarGridSpec(
            num_scalar_prefetch=1,
            grid=(1,),
            in_specs=[whole(piece.shape) for piece in pieces]
            + [whole(weight.shape) for weight in weights]
            + [whole(valid.shape)],
            out_specs=[whole(shape.shape) for shape in shapes],
            scratch_shapes=[pltpu.VMEM((per * n_ctx, 3, PAIR, HD), BF)],
        ),
        compiler_params=params(),
        cost_estimate=pl.CostEstimate(
            flops=6 * rows * depth * width, bytes_accessed=rows * depth * 2 + 6 * depth * width, transcendentals=0
        ),
    )(scalars, *pieces, *weights, valid)


def both_places(me, k, n_ctx):
    source = jnp.bitwise_xor(me, k)
    front = pl.multiple_of(source * BLOCK, BLOCK)
    back = pl.multiple_of((2 * n_ctx - 1 - source) * BLOCK, BLOCK)
    return pl.ds(front, BLOCK), pl.ds(back, BLOCK)


def attention_kernel(n_ctx, tile, scalar_ref, *refs):
    x_refs, o_refs, (qs, ks, vs, os) = refs[:n_ctx], refs[n_ctx : 2 * n_ctx], refs[2 * n_ctx :]
    me = scalar_ref[0]
    length = 2 * n_ctx * BLOCK
    for k in range(n_ctx):
        front, back = both_places(me, k, n_ctx)
        for which, dest in enumerate((qs, ks, vs)):
            dest[front, :] = x_refs[k][0, which, :BLOCK, :]
            dest[back, :] = x_refs[k][0, which, BLOCK:, :]
    factor = -(HD ** (-0.5)) * LOG2E
    shift = math.log(length) * LOG2E
    row_at = lax.broadcasted_iota(jnp.int32, (tile, tile), 0)
    col_at = lax.broadcasted_iota(jnp.int32, (tile, tile), 1)
    for i in range(length // tile):
        query = qs[i * tile : (i + 1) * tile, :]

        def part(j, masked):
            at = pl.ds(pl.multiple_of(j * tile, tile), tile)
            raw = times_transposed(query, ks[at, :])
            prob = 1.0 / (1.0 + jnp.exp2(raw * factor + shift))
            if masked:
                prob = jnp.where(row_at >= col_at, prob, 0.0)
            return dot(prob.astype(BF), vs[at, :])

        total = part(i, True)
        if i > 0:
            total = lax.fori_loop(0, i, lambda j, acc: acc + part(j, False), total)
        os[i * tile : (i + 1) * tile, :] = total.astype(BF)
    for k in range(n_ctx):
        front, back = both_places(me, k, n_ctx)
        o_refs[k][0, :BLOCK, :] = os[front, :]
        o_refs[k][0, BLOCK:, :] = os[back, :]


def attention_forward(scalars, pieces, n_ctx):
    pairs = pieces[0].shape[0]
    length = 2 * n_ctx * BLOCK
    tile = min(512, length)
    return pl.pallas_call(
        functools.partial(attention_kernel, n_ctx, tile),
        out_shape=[jax.ShapeDtypeStruct((pairs, PAIR, HD), BF)] * n_ctx,
        grid_spec=pltpu.PrefetchScalarGridSpec(
            num_scalar_prefetch=1,
            grid=(pairs,),
            in_specs=[pl.BlockSpec((1, 3, PAIR, HD), lambda i, s: (i, 0, 0, 0))] * n_ctx,
            out_specs=[pl.BlockSpec((1, PAIR, HD), lambda i, s: (i, 0, 0))] * n_ctx,
            scratch_shapes=[pltpu.VMEM((length, HD), BF)] * 4,
        ),
        compiler_params=params(),
        cost_estimate=pl.CostEstimate(
            flops=pairs * length * length * HD * 6,
            bytes_accessed=pairs * length * HD * 8,
            transcendentals=pairs * length * length,
        ),
    )(scalars, *pieces)


def attention_back_kernel(n_ctx, tile, scalar_ref, *refs):
    x_refs, g_refs, (cos_ref, sin_ref) = refs[:n_ctx], refs[n_ctx : 2 * n_ctx], refs[2 * n_ctx : 2 * n_ctx + 2]
    out_refs = refs[2 * n_ctx + 2 : 3 * n_ctx + 2]
    qs, ks, vs, gs, os, dqs = refs[3 * n_ctx + 2 :]
    me = scalar_ref[0]
    length = 2 * n_ctx * BLOCK
    for k in range(n_ctx):
        front, back = both_places(me, k, n_ctx)
        for which, dest in enumerate((qs, ks, vs)):
            dest[front, :] = x_refs[k][0, which, :BLOCK, :]
            dest[back, :] = x_refs[k][0, which, BLOCK:, :]
        gs[front, :] = g_refs[k][0, :BLOCK, :]
        gs[back, :] = g_refs[k][0, BLOCK:, :]
    scale = HD ** (-0.5)
    factor = -scale * LOG2E
    shift = math.log(length) * LOG2E
    count = length // tile
    key_at = lax.broadcasted_iota(jnp.int32, (tile, tile), 0)
    query_at = lax.broadcasted_iota(jnp.int32, (tile, tile), 1)
    dqs[...] = jnp.zeros_like(dqs)

    def unrotate(values, at):
        return (values * cos_ref[at, :] - pltpu.roll(values, HD // 2, 1) * sin_ref[at, :]).astype(BF)

    for j in range(count):
        own = slice(j * tile, (j + 1) * tile)
        keys = ks[own, :]
        values = vs[own, :]

        def part(i, masked):
            at = pl.ds(pl.multiple_of(i * tile, tile), tile)
            query = qs[at, :]
            grad = gs[at, :]
            raw = times_transposed(keys, query)
            prob = 1.0 / (1.0 + jnp.exp2(raw * factor + shift))
            if masked:
                prob = jnp.where(query_at >= key_at, prob, 0.0)
            prob_grad = times_transposed(values, grad)
            score_grad = (prob_grad * prob * (1.0 - prob)).astype(BF)
            dqs[at, :] += contract_rows(score_grad, keys)
            return dot(score_grad, query), dot(prob.astype(BF), grad)

        total = part(j, True)
        if j + 1 < count:

            def step(i, acc):
                more = part(i, False)
                return acc[0] + more[0], acc[1] + more[1]

            total = lax.fori_loop(j + 1, count, step, total)
        os[1, own, :] = unrotate(total[0] * scale, own)
        os[2, own, :] = total[1].astype(BF)
    for i in range(count):
        at = slice(i * tile, (i + 1) * tile)
        os[0, at, :] = unrotate(dqs[at, :] * scale, at)
    for k in range(n_ctx):
        front, back = both_places(me, k, n_ctx)
        for which in range(3):
            out_refs[k][0, which, :BLOCK, :] = os[which, front, :]
            out_refs[k][0, which, BLOCK:, :] = os[which, back, :]


def attention_backward(scalars, pieces, grads, cos_tab, sin_tab, n_ctx):
    pairs = pieces[0].shape[0]
    length = 2 * n_ctx * BLOCK
    tile = min(512, length)
    three = pl.BlockSpec((1, 3, PAIR, HD), lambda i, s: (i, 0, 0, 0))
    one = pl.BlockSpec((1, PAIR, HD), lambda i, s: (i, 0, 0))
    return pl.pallas_call(
        functools.partial(attention_back_kernel, n_ctx, tile),
        out_shape=[jax.ShapeDtypeStruct((pairs, 3, PAIR, HD), BF)] * n_ctx,
        grid_spec=pltpu.PrefetchScalarGridSpec(
            num_scalar_prefetch=1,
            grid=(pairs,),
            in_specs=[three] * n_ctx + [one] * n_ctx + [whole((length, HD))] * 2,
            out_specs=[three] * n_ctx,
            scratch_shapes=[pltpu.VMEM((length, HD), BF)] * 4
            + [pltpu.VMEM((3, length, HD), BF), pltpu.VMEM((length, HD), F32)],
        ),
        compiler_params=params(),
        cost_estimate=pl.CostEstimate(
            flops=pairs * length * length * HD * 12,
            bytes_accessed=pairs * length * HD * 14,
            transcendentals=pairs * length * length,
        ),
    )(scalars, *pieces, *grads, cos_tab, sin_tab)


def mlp_kernel(n_ref, g_ref, wg_ref, wu_ref, wd_ref, *rest):
    h_ref, dgp_ref, dup_ref = rest[-3:]
    rows = n_ref[...]
    gate_pre = dot(rows, wg_ref[...])
    up_pre = dot(rows, wu_ref[...])
    hidden_grad = times_transposed(g_ref[...], wd_ref[...])
    h_ref[...], dgp_ref[...], dup_ref[...] = feed_values(gate_pre, up_pre, hidden_grad)


def mlp_core(normed, grads, wg, wu, wd, total, first, held=()):
    rows, depth = normed.shape
    hidden = wg.shape[1]
    row_tile, tile = 512, 512
    skip = first // row_tile
    row_block = pl.BlockSpec((row_tile, depth), lambda j, i: (i, 0))
    out_block = pl.BlockSpec((row_tile, tile), lambda j, i: (i + skip, j))
    out = jax.ShapeDtypeStruct((total, hidden), BF)
    return pl.pallas_call(
        mlp_kernel,
        out_shape=(out, out, out),
        grid=(hidden // tile, rows // row_tile),
        in_specs=[
            row_block,
            row_block,
            pl.BlockSpec((depth, tile), lambda j, i: (0, j)),
            pl.BlockSpec((depth, tile), lambda j, i: (0, j)),
            pl.BlockSpec((tile, depth), lambda j, i: (j, 0)),
        ]
        + [pl.BlockSpec(memory_space=pl.ANY)] * len(held),
        out_specs=(out_block, out_block, out_block),
        input_output_aliases={5 + k: k for k in range(len(held))},
        compiler_params=params(),
        cost_estimate=pl.CostEstimate(
            flops=6 * rows * depth * hidden,
            bytes_accessed=rows * depth * 4 + 6 * depth * hidden + 6 * rows * hidden,
            transcendentals=rows * hidden,
        ),
    )(normed, grads, wg, wu, wd, *held)


def inverse_rms(values):
    return lax.rsqrt(jnp.mean(values * values, axis=-1, keepdims=True) + EPS)


def neighbours():
    index, rank = lax.axis_index("ctx"), lax.axis_index("tp")
    return (index, jnp.bitwise_xor(rank, 1)), (index, jnp.bitwise_xor(rank, 2))


def remote(source, dest, send_sem, recv_sem, device):
    return pltpu.make_async_remote_copy(
        src_ref=source,
        dst_ref=dest,
        send_sem=send_sem,
        recv_sem=recv_sem,
        device_id=device,
        device_id_type=pl.DeviceIdType.MESH,
    )


def signal(sem, device):
    pl.semaphore_signal(sem, inc=1, device_id=device, device_id_type=pl.DeviceIdType.MESH)


class Scatter:
    def __init__(self, partial, groups, bufs, sems, loaded=True):
        self.partial, self.groups, self.loaded = partial, groups, loaded
        self.from_x, self.from_y, self.for_y, self.for_x, self.low, self.high = bufs[:6]
        if loaded:
            self.stay, self.stay_y, self.stay_x = bufs[6:]
        self.first_send, self.first_recv, self.second_send, self.second_recv, self.load_sem = sems
        self.to_x, self.to_y = neighbours()

    @staticmethod
    def scratch(rows, width, loaded=True):
        dma = pltpu.SemaphoreType.DMA
        whole_rows, half_rows = pltpu.VMEM((rows, width), BF), pltpu.VMEM((rows // 2, width), BF)
        bufs = [whole_rows] * 2 + [half_rows] * 4 + ([whole_rows] + [half_rows] * 2 if loaded else [])
        return bufs + [dma((8,)), dma((8,)), dma((4,)), dma((4,)), dma((6,))]

    def piece(self, g, number):
        base, rows, own = self.groups[g]
        half = rows // 2
        if not self.loaded:
            return self.partial[pl.ds(base + number * half, half), :]
        if number < 2:
            return self.stay[pl.ds(own + number * half, half), :]
        return (self.stay_x if number == 3 else self.stay_y)[pl.ds(own // 2, half), :]

    def first_copies(self, g):
        base, rows, own = self.groups[g]
        half = rows // 2
        part = lambda number: self.partial.at[pl.ds(base + number * half, half)]
        at = lambda buf, number: buf.at[pl.ds(own + number * half, half)]
        plan = [
            (part(2), at(self.from_x, 0), self.to_x),
            (part(6), at(self.from_x, 1), self.to_x),
            (part(5), at(self.from_y, 0), self.to_y),
            (part(7), at(self.from_y, 1), self.to_y),
        ]
        return [
            remote(source, dest, self.first_send.at[4 * g + k], self.first_recv.at[4 * g + k], device)
            for k, (source, dest, device) in enumerate(plan)
        ]

    def loads(self, g):
        base, rows, own = self.groups[g]
        half = rows // 2
        copy = lambda number, count, dest, k: pltpu.make_async_copy(
            self.partial.at[pl.ds(base + number * half, count)], dest, self.load_sem.at[3 * g + k]
        )
        return [
            copy(0, rows, self.stay.at[pl.ds(own, rows)], 0),
            copy(4, half, self.stay_y.at[pl.ds(own // 2, half)], 1),
            copy(3, half, self.stay_x.at[pl.ds(own // 2, half)], 2),
        ]

    def second_copies(self, g):
        _, rows, own = self.groups[g]
        at = pl.ds(own // 2, rows // 2)
        return [
            remote(self.for_y.at[at], self.low.at[at], self.second_send.at[2 * g], self.second_recv.at[2 * g], self.to_y),
            remote(
                self.for_x.at[at], self.high.at[at], self.second_send.at[2 * g + 1], self.second_recv.at[2 * g + 1], self.to_x
            ),
        ]

    def start(self, g, which=(1, 3, 0, 2), loads=True):
        copies = self.first_copies(g)
        for k in which:
            copies[k].start()
        if loads:
            for copy in self.loads(g):
                copy.start()

    def forward(self, g):
        _, rows, own = self.groups[g]
        half = rows // 2
        copies = self.first_copies(g)
        copies[1].wait_recv()
        copies[3].wait_recv()
        if self.loaded:
            for copy in self.loads(g):
                copy.wait()
        at = pl.ds(own // 2, half)
        self.for_y[at, :] = add_low(self.piece(g, 4), self.from_x[pl.ds(own + half, half), :])
        self.for_x[at, :] = add_low(self.piece(g, 3), self.from_y[pl.ds(own + half, half), :])
        for copy in self.second_copies(g):
            copy.start()

    def total(self, g, use):
        _, rows, own = self.groups[g]
        half = rows // 2
        copies, seconds = self.first_copies(g), self.second_copies(g)
        copies[0].wait_recv()
        copies[2].wait_recv()
        for copy in copies:
            copy.wait_send()
        for copy in seconds:
            copy.wait()
        first = pl.ds(own, half)
        rest = pl.ds(own // 2, half)
        for side, (got, more) in enumerate(((self.from_x, self.low), (self.from_y, self.high))):
            at = pl.ds(own + side * half, half)
            use(at, self.piece(g, side).astype(F32) + got[first, :].astype(F32) + more[rest, :].astype(F32))


class Gather:
    def __init__(self, own, out, groups, sems, own_at=None, local=True):
        self.own, self.out, self.groups, self.has_local = own, out, groups, local
        self.own_at = own_at if own_at is not None else [group[2] for group in groups]
        self.first_send, self.first_recv, self.second_send, self.second_recv, self.local_sem = sems
        self.to_x, self.to_y = neighbours()

    @staticmethod
    def scratch():
        dma = pltpu.SemaphoreType.DMA
        return [dma((4,)), dma((4,)), dma((4,)), dma((4,)), dma((2,))]

    def first_copies(self, g):
        base, rows, _ = self.groups[g]
        source = self.own.at[pl.ds(self.own_at[g], rows)]
        place = lambda k: self.out.at[pl.ds(base + k * rows, rows)]
        return [
            remote(source, place(1), self.first_send.at[2 * g], self.first_recv.at[2 * g], self.to_x),
            remote(source, place(2), self.first_send.at[2 * g + 1], self.first_recv.at[2 * g + 1], self.to_y),
        ]

    def local(self, g):
        base, rows, _ = self.groups[g]
        return pltpu.make_async_copy(self.own.at[pl.ds(self.own_at[g], rows)], self.out.at[pl.ds(base, rows)], self.local_sem.at[g])

    def second_copies(self, g):
        base, rows, _ = self.groups[g]
        half = rows // 2
        part = lambda number: self.out.at[pl.ds(base + number * half, half)]
        return [
            remote(part(4), part(6), self.second_send.at[2 * g], self.second_recv.at[2 * g], self.to_x),
            remote(part(3), part(7), self.second_send.at[2 * g + 1], self.second_recv.at[2 * g + 1], self.to_y),
        ]

    def start(self, g):
        for copy in self.first_copies(g):
            copy.start()
        if self.has_local:
            self.local(g).start()

    def forward_x(self, g):
        self.first_copies(g)[0].wait_recv()
        self.second_copies(g)[1].start()

    def forward_y(self, g):
        self.first_copies(g)[1].wait_recv()
        self.second_copies(g)[0].start()

    def forward(self, g):
        self.forward_x(g)
        self.forward_y(g)
        if self.has_local:
            self.local(g).wait()

    def finish(self, g):
        for copy in self.second_copies(g):
            copy.wait_recv()

    def sent(self, g):
        for copy in self.first_copies(g) + self.second_copies(g):
            copy.wait_send()


TILE, ROWS = 128, 64
CORE_SLOTS, HOP_SLOTS = 4, 4


class Ring:
    def __init__(self, slots, send_sem, recv_sem, credit, total):
        self.slots, self.send_sem, self.recv_sem, self.credit, self.total = slots, send_sem, recv_sem, credit, total
        self.count = slots.shape[0]

    def copy(self, source, at, send_at, device):
        slot = lax.rem(at, self.count)
        return pltpu.make_async_remote_copy(
            src_ref=source,
            dst_ref=self.slots.at[slot],
            send_sem=self.send_sem.at[send_at],
            recv_sem=self.recv_sem.at[slot],
            device_id=device,
            device_id_type=pl.DeviceIdType.MESH,
        )

    def send(self, source, at, send_at, device):
        @pl.when(at >= self.count)
        def _():
            pl.semaphore_wait(self.credit, 1)

        self.copy(source, at, send_at, device).start()

    def sent(self, source, at, send_at, device):
        self.copy(source, at, send_at, device).wait_send()

    def arrived(self, source, at, send_at, device):
        self.copy(source, at, send_at, device).wait_recv()
        return self.slots.at[lax.rem(at, self.count)]

    def free(self, at, device):
        @pl.when(at + self.count < self.total)
        def _():
            pl.semaphore_signal(self.credit, inc=1, device_id=device, device_id_type=pl.DeviceIdType.MESH)


def sums_kernel(n_ctx, items, n_right, n_extra, tasks, late, *refs):
    n_left = len(items)
    made = items[0][3]
    n_held = n_left - (1 if made else 0)
    left_refs, right_refs = refs[:n_held], refs[n_held : n_held + n_right]
    left_refs = ((None,) if made else ()) + tuple(left_refs)
    refs = refs[n_held + n_right :]
    extra_in, refs = refs[: n_extra[0]], refs[n_extra[0] :]
    out_refs, extra_out, refs = refs[:n_left], refs[n_left : n_left + n_extra[1]], refs[n_left + n_extra[1] :]
    extra_scratch, refs = refs[: n_extra[2]], refs[n_extra[2] :]
    right_refs = list(right_refs) + [extra_out[k] for k in late]
    n_right += len(late)
    (
        left_buf, right_buf, other_buf, ring, core_in, hop_in, hop_mid, hop_out, core_out,
        left_sem, right_sem, core_send, core_recv, in_send, in_recv, mid_send, mid_recv, out_send, out_recv,
        fin_send, fin_recv, store_sem, core_credit, in_credit, mid_credit, out_credit, fin_credit,
    ) = refs
    starts = [0]
    for _, _, chunks, _ in items:
        starts.append(starts[-1] + chunks)
    total = starts[-1]
    n_ring = ring.shape[0]
    chips = n_ctx // 2
    mid = chips // 2
    index = lax.axis_index("ctx")
    rank = lax.axis_index("tp")
    core = lax.rem(index, 2)
    chip = index // 2
    low_side = chip < mid
    place = jnp.where(low_side, chip, chips - 1 - chip)
    toward = jnp.where(low_side, 1, -1)
    partner = (chip * 2 + 1 - core, rank)
    after = ((chip + toward) * 2 + core, rank)
    before = ((chip - toward) * 2 + core, rank)
    is_first = place == 0
    is_last = place == mid - 1
    lag_t = mid
    lag_u = lag_t + 2
    lag_o = lag_u + 2 * (mid - 1)
    lag_f = lag_o + 1
    lag_w = lag_f + 1

    to_core = Ring(core_in, core_send, core_recv, core_credit, total)
    to_after = Ring(hop_in, in_send, in_recv, in_credit, total)
    across = Ring(hop_mid, mid_send, mid_recv, mid_credit, total)
    to_before = Ring(hop_out, out_send, out_recv, out_credit, total)
    to_final = Ring(core_out, fin_send, fin_recv, fin_credit, total)

    def right_copy(k):
        return pltpu.make_async_copy(right_refs[k], right_buf.at[k % 2], right_sem.at[k % 2])

    right_copy(0).start()

    def for_item(at, action):
        for number in range(n_left):
            @pl.when((at >= starts[number]) & (at < starts[number + 1]))
            def _(number=number):
                action(number, at - starts[number])

    def rows_at(number, chunk, side):
        half = items[number][2] * ROWS
        return pl.multiple_of(side * half + chunk * ROWS, ROWS)

    def left_copy(number, chunk, slot, which):
        side = core if which == 0 else 1 - core
        half = items[number][2] * ROWS
        return pltpu.make_async_copy(
            left_refs[number].at[:, pl.ds(pl.multiple_of(side * half + chunk // 2 * TILE, TILE), TILE)],
            left_buf.at[slot, :, pl.ds(which * TILE, TILE)],
            left_sem.at[slot, which],
        )

    def load_left(at):
        def action(number, chunk):
            if number == 0 and made:
                maker.load(chunk // 2)
                return
            if number == 1 and made:

                @pl.when(chunk == 0)
                def _():
                    maker.release()

            for which in range(2):
                left_copy(number, chunk, lax.rem(at // 2, 2), which).start()

        for_item(at, action)

    planned, each, maker = tasks(extra_in, extra_out, extra_scratch) if tasks is not None else ({}, None, None)
    if made:
        maker.begin(left_buf, right_buf)
    load_left(0)
    if n_right > 1 and not made:
        right_copy(1).start()
    if tasks is not None:
        greet(n_ctx, True)
    else:
        barrier = pltpu.get_barrier_semaphore()
        pl.semaphore_signal(barrier, inc=1, device_id=partner, device_id_type=pl.DeviceIdType.MESH)

        @pl.when(chip > 0)
        def _():
            pl.semaphore_signal(
                barrier, inc=1, device_id=((chip - 1) * 2 + core, rank), device_id_type=pl.DeviceIdType.MESH
            )

        @pl.when(chip < chips - 1)
        def _():
            pl.semaphore_signal(
                barrier, inc=1, device_id=((chip + 1) * 2 + core, rank), device_id_type=pl.DeviceIdType.MESH
            )

        pl.semaphore_wait(barrier, 1 + jnp.where(chip > 0, 1, 0) + jnp.where(chip < chips - 1, 1, 0))
    if 0 in planned:
        planned.pop(0)()
    right_copy(0).wait()

    def step(i, carry):
        def at_lag(lag):
            at = i - lag
            return at, (at >= 0) & (at < total)

        at, now = at_lag(lag_w)

        @pl.when(now)
        def _():
            slot = lax.rem(at, n_ring)
            source = ring.at[slot]

            def action(number, chunk):
                store(number, chunk, at, 0).wait()
                store(number, chunk, at, 1).wait()

            for_item(at, action)
            to_final.sent(source, at, slot, partner)
            to_final.free(at, partner)

            @pl.when(jnp.logical_not(is_first))
            def _():
                to_before.sent(source, at, slot, before)

        at, now = at_lag(lag_o)

        @pl.when(now & jnp.logical_not(is_last))
        def _():
            slot = lax.rem(at, n_ring)
            source = ring.at[slot]
            to_after.sent(source, at, slot, after)
            got = to_before.arrived(source, at, slot, after)
            ring[slot] = got[...]
            to_before.free(at, after)

            @pl.when(jnp.logical_not(is_first))
            def _():
                to_before.send(source, at, slot, before)

        @pl.when(now)
        def _():
            slot = lax.rem(at, n_ring)
            to_final.send(ring.at[slot], at, slot, partner)

        at, now = at_lag(lag_u)

        @pl.when(now & is_last)
        def _():
            slot = lax.rem(at, n_ring)
            source = ring.at[slot]
            across.sent(source, at, slot, after)
            got = across.arrived(source, at, slot, after)
            ring[slot] = add_low(ring[slot], got[...])
            across.free(at, after)

            @pl.when(jnp.logical_not(is_first))
            def _():
                to_before.send(source, at, slot, before)

        at, now = at_lag(lag_t)

        @pl.when(now)
        def _():
            slot = lax.rem(at, n_ring)
            source = ring.at[slot]

            @pl.when(jnp.logical_not(is_first))
            def _():
                got = to_after.arrived(source, at, slot, before)
                ring[slot] = add_low(ring[slot], got[...])
                to_after.free(at, before)

            @pl.when(is_last)
            def _():
                across.send(source, at, slot, after)

            @pl.when(jnp.logical_not(is_first) & jnp.logical_not(is_last))
            def _():
                to_after.send(source, at, slot, after)

        at, now = at_lag(1)

        @pl.when(now)
        def _():
            slot = lax.rem(at, n_ring)
            source = ring.at[slot]
            own = other_buf.at[lax.rem(at, 4)]
            to_core.sent(own, at, lax.rem(at, 4), partner)
            got = to_core.arrived(own, at, lax.rem(at, 4), partner)
            ring[slot] = add_low(ring[slot], got[...])
            to_core.free(at, partner)

            @pl.when(is_first & jnp.logical_not(is_last))
            def _():
                to_after.send(source, at, slot, after)

        at, now = at_lag(lag_f)

        @pl.when(now)
        def _():
            slot = lax.rem(at, n_ring)
            to_final.arrived(ring.at[slot], at, slot, partner)

            def action(number, chunk):
                store(number, chunk, at, 0).start()
                store(number, chunk, at, 1).start()

            for_item(at, action)

        for when, task in planned.items():
            pl.when(i == when)(task)

        if each is not None:
            each(i)

        @pl.when((i + 2 < total) & (lax.rem(i, 2) == 0))
        def _():
            load_left(i + 2)

        @pl.when((i < total) & (lax.rem(i, 2) == 0))
        def _():
            slot = lax.rem(i // 2, 2)

            def action(number, chunk):
                which_right = items[number][1]
                if which_right > 0 and items[number - 1][1] != which_right:

                    @pl.when(chunk == 0)
                    def _():
                        if made and which_right in (1, n_right - 1):
                            right_copy(which_right).start()
                        right_copy(which_right).wait()

                if which_right > 0 and which_right + 1 < n_right - (1 if made else 0):

                    @pl.when(chunk == items[number][2] // 2)
                    def _():
                        right_copy(which_right + 1).start()

                if number == 0 and made:
                    maker.make(chunk // 2)
                else:
                    for which in range(2):
                        left_copy(number, chunk, slot, which).wait()
                right = right_buf.at[which_right % 2]
                product = contract_rows(left_buf[slot], right[...]).astype(BF)
                for part in range(2):
                    place = lax.rem(i + part, 4)
                    other_buf[place] = product[TILE + part * ROWS : TILE + (part + 1) * ROWS]
                    to_core.send(other_buf.at[place], i + part, place, partner)
                    ring[lax.rem(i + part, n_ring)] = product[part * ROWS : (part + 1) * ROWS]

            for_item(i, action)

        return carry

    def store(number, chunk, at, which):
        source = ring.at[lax.rem(at, n_ring)] if which == 0 else core_out.at[lax.rem(at, CORE_SLOTS)]
        side = core if which == 0 else 1 - core
        return pltpu.make_async_copy(
            source,
            out_refs[number].at[pl.ds(rows_at(number, chunk, side), ROWS), :],
            store_sem.at[which, lax.rem(at, 2)],
        )

    lax.fori_loop(0, total + lag_w, step, 0)


def weight_sums(items, rights, n_ctx, collective_id, extra=None, late=(), limit=VMEM_LIMIT):
    tokens, width = rights[0].shape
    columns = [left if isinstance(left, int) else left.shape[1] for left, _ in items]
    held = [left for left, _ in items if not isinstance(left, int)]
    shapes = [
        (k, right, columns[k] // 2 // ROWS, isinstance(left, int)) for k, (left, right) in enumerate(items)
    ]
    mid = n_ctx // 4
    n_ring = mid + 2 + 2 * (mid - 1) + 4
    any_spec = pl.BlockSpec(memory_space=pl.ANY)
    args, arg_specs, outs, out_specs, scratch, tasks = extra if extra is not None else ([], [], [], [], [], None)
    counts = (len(args), len(outs), len(scratch))
    chunk = (ROWS, width)
    dma = pltpu.SemaphoreType.DMA
    return pl.pallas_call(
        functools.partial(sums_kernel, n_ctx, shapes, len(rights), counts, tasks, late),
        out_shape=[jax.ShapeDtypeStruct((count, width), BF) for count in columns] + outs,
        in_specs=[any_spec] * (len(held) + len(rights)) + arg_specs,
        out_specs=[any_spec] * len(items) + out_specs,
        scratch_shapes=scratch
        + [
            pltpu.VMEM((2, tokens, 2 * TILE), BF),
            pltpu.VMEM((min(2, len(rights) + len(late)), tokens, width), BF),
            pltpu.VMEM((4,) + chunk, BF),
            pltpu.VMEM((n_ring,) + chunk, BF),
            pltpu.VMEM((CORE_SLOTS,) + chunk, BF),
            pltpu.VMEM((HOP_SLOTS,) + chunk, BF),
            pltpu.VMEM((HOP_SLOTS,) + chunk, BF),
            pltpu.VMEM((HOP_SLOTS,) + chunk, BF),
            pltpu.VMEM((CORE_SLOTS,) + chunk, BF),
            dma((2, 2)),
            dma((2,)),
            dma((4,)),
            dma((CORE_SLOTS,)),
            dma((n_ring,)),
            dma((HOP_SLOTS,)),
            dma((n_ring,)),
            dma((HOP_SLOTS,)),
            dma((n_ring,)),
            dma((HOP_SLOTS,)),
            dma((n_ring,)),
            dma((CORE_SLOTS,)),
            dma((2, 2)),
        ]
        + [pltpu.SemaphoreType.REGULAR] * 5,
        compiler_params=pltpu.CompilerParams(
            vmem_limit_bytes=limit, collective_id=collective_id, has_side_effects=True
        ),
        cost_estimate=pl.CostEstimate(
            flops=sum(2 * count * tokens * width for count in columns),
            bytes_accessed=sum(2 * count * (tokens + width) for count in columns),
            transcendentals=0,
        ),
    )(*held, *rights, *args)


VMEM_SPEC = pl.BlockSpec(memory_space=pltpu.VMEM)
ANY_SPEC = pl.BlockSpec(memory_space=pl.ANY)


def norm_back_rows(values, gain, grad):
    inv = inverse_rms(values)
    unit = values * inv
    scaled = grad * gain
    back = (scaled - unit * jnp.mean(scaled * unit, axis=-1, keepdims=True)) * inv
    return back, jnp.sum(grad * unit, axis=0, keepdims=True)


def own_copies(ref, buf, groups, sem):
    odd = lax.rem(lax.axis_index("tp"), 2)
    starts = [pl.multiple_of(odd * BLOCK, BLOCK), pl.multiple_of((1 - odd) * PAIR, BLOCK)]
    return [
        pltpu.make_async_copy(ref.at[pl.ds(start, rows)], buf.at[pl.ds(own, rows)], sem.at[g])
        for g, (start, (_, rows, own)) in enumerate(zip(starts, groups))
    ]


class Maker:
    def __init__(self, refs, outs, weights, downs, stage, sems):
        self.n2_ref, self.wg_ref, self.wu_ref, self.wd_ref = refs
        self.h_out, self.dgp_out, self.dup_out = outs
        self.weights, self.downs, self.stage = weights, downs, stage
        self.n2_sem, self.weight_sem, self.h_sem, self.grad_sem = sems
        self.core = lax.rem(lax.axis_index("ctx"), 2)
        self.half = self.h_out.shape[1] // 2
        self.tiles = self.half // TILE

    def first(self, tile, which):
        side = self.core if which == 0 else 1 - self.core
        return pl.multiple_of(side * self.half + tile * TILE, TILE)

    def copies(self, tile):
        slot = lax.rem(tile, 2)
        deep = self.weights.shape[1]
        made = []
        for which in range(2):
            at = pl.ds(self.first(tile, which), TILE)
            for kind, ref in enumerate((self.wg_ref, self.wu_ref)):
                to = pl.multiple_of((slot * 2 + kind) * 2 * TILE + which * TILE, TILE)
                for part in range(2):
                    made.append((ref.at[pl.ds(part * deep, deep), at], self.weights.at[part, :, pl.ds(to, TILE)]))
            made.append((self.wd_ref.at[at], self.downs.at[slot, 0, pl.ds(which * TILE, TILE)]))
        return [
            pltpu.make_async_copy(source, dest, self.weight_sem.at[slot, k]) for k, (source, dest) in enumerate(made)
        ]

    def load(self, tile):
        for copy in self.copies(tile):
            copy.start()

    def begin(self, left_buf, right_buf):
        self.left_buf, self.right_buf = left_buf, right_buf
        self.n2_copy().start()

    def n2_copy(self):
        return pltpu.make_async_copy(self.n2_ref, self.right_buf.at[1], self.n2_sem)

    def h_stores(self, tile):
        slot = lax.rem(tile, 2)
        return [
            pltpu.make_async_copy(
                self.left_buf.at[slot, :, pl.ds(which * TILE, TILE)],
                self.h_out.at[:, pl.ds(self.first(tile, which), TILE)],
                self.h_sem.at[slot, which],
            )
            for which in range(2)
        ]

    def grad_stores(self, tile):
        return [
            pltpu.make_async_copy(
                self.stage.at[kind, :, pl.ds(which * TILE, TILE)],
                out.at[:, pl.ds(self.first(tile, which), TILE)],
                self.grad_sem.at[kind, which],
            )
            for kind, out in enumerate((self.dgp_out, self.dup_out))
            for which in range(2)
        ]

    def make(self, tile):
        slot = lax.rem(tile, 2)
        deep = self.weights.shape[1]

        @pl.when(tile == 0)
        def _():
            self.n2_copy().wait()

        @pl.when(tile > 0)
        def _():
            for copy in self.grad_stores(tile - 1):
                copy.wait()

        @pl.when(tile > 1)
        def _():
            for copy in self.h_stores(tile - 2):
                copy.wait()

        for copy in self.copies(tile):
            copy.wait()
        at_gate = pl.ds(pl.multiple_of(slot * 4 * TILE, TILE), 2 * TILE)
        at_up = pl.ds(pl.multiple_of((slot * 4 + 2) * TILE, TILE), 2 * TILE)
        count = 512

        def rows_step(step, carry):
            rows = pl.ds(pl.multiple_of(step * count, count), count)
            low, high = self.right_buf[1, rows, :deep], self.right_buf[1, rows, deep:]
            gate_pre = dot(low, self.weights[0, :, at_gate]) + dot(high, self.weights[1, :, at_gate])
            up_pre = dot(low, self.weights[0, :, at_up]) + dot(high, self.weights[1, :, at_up])
            hidden_grad = times_transposed(self.right_buf[0, rows, :], self.downs[slot, 0])
            h, dgp, dup = feed_values(gate_pre, up_pre, hidden_grad)
            self.left_buf[slot, rows, :] = h
            self.stage[0, rows, :] = dgp
            self.stage[1, rows, :] = dup
            return carry

        lax.fori_loop(0, self.right_buf.shape[1] // count, rows_step, 0)
        for copy in self.h_stores(tile) + self.grad_stores(tile):
            copy.start()

    def release(self):
        for copy in self.h_stores(self.tiles - 2):
            copy.wait()

    def finish(self):
        for copy in self.h_stores(self.tiles - 1) + self.grad_stores(self.tiles - 1):
            copy.wait()


def feed_values(gate_pre, up_pre, hidden_grad):
    gate_sig = 1.0 / (1.0 + jnp.exp2(gate_pre * (-LOG2E)))
    gate_act = gate_pre * gate_sig
    return (
        (gate_act * up_pre).astype(BF),
        (hidden_grad * up_pre * (gate_sig * (1.0 + gate_pre * (1.0 - gate_sig)))).astype(BF),
        (hidden_grad * gate_act).astype(BF),
    )


def feed_tasks(groups, extra_in, extra_out, scratch):
    n2_ref, wg_ref, wu_ref, wd_ref, residual, cot_ref, gain = extra_in
    dr, da_all, gain_grad, d_ref, h_ref, dgp_ref, dup_ref = extra_out
    n = len(Scatter.scratch(16, 128))
    bufs, rest = scratch[:n], scratch[n:]
    weights, lefts, tile_out, weight_sem, left_sem, out_sem = rest[:6]
    grads, stage, own_sem, n2_sem, make_sem, h_sem, grad_sem = rest[6:13]
    da_own = bufs[0]
    scatter = Scatter(d_ref, groups, bufs[:9], bufs[9:])
    gather = Gather(da_own, da_all, groups, rest[13:])
    maker = Maker(
        (n2_ref, wg_ref, wu_ref, wd_ref),
        (h_ref, dgp_ref, dup_ref),
        weights,
        lefts,
        stage,
        (n2_sem, make_sem, h_sem, grad_sem),
    )
    order = list(reversed(range(len(groups))))
    rows, columns = lefts.shape[2], weights.shape[1]
    row_tiles = dgp_ref.shape[0] // rows
    tiles = row_tiles * (d_ref.shape[1] // columns)
    after = maker.half // ROWS
    shift = after + 1

    def weight_copies(part):
        at = pl.ds(pl.multiple_of(part * columns, columns), columns)
        return [
            pltpu.make_async_copy(ref.at[at], weights.at[k], weight_sem.at[k]) for k, ref in enumerate((wg_ref, wu_ref))
        ]

    def left_copies(tile):
        at = pl.ds(pl.multiple_of(lax.rem(tile, row_tiles) * rows, rows), rows)
        slot = lax.rem(tile, 2)
        return [
            pltpu.make_async_copy(ref.at[at], lefts.at[slot, k], left_sem.at[slot, k])
            for k, ref in enumerate((dgp_ref, dup_ref))
        ]

    def out_copy(tile):
        slot = lax.rem(tile, 2)
        return pltpu.make_async_copy(
            tile_out.at[slot],
            d_ref.at[
                pl.ds(pl.multiple_of(lax.rem(tile, row_tiles) * rows, rows), rows),
                pl.ds(pl.multiple_of(tile // row_tiles * columns, columns), columns),
            ],
            out_sem.at[slot],
        )

    def begin():
        gain_grad[...] = jnp.zeros_like(gain_grad)
        for copy in own_copies(cot_ref, grads, groups, own_sem):
            copy.start()

    def whole_hidden():
        maker.finish()
        for copy in weight_copies(0) + left_copies(0):
            copy.start()

    def each(step):
        i = step - shift

        @pl.when((i >= 0) & (i < tiles))
        def _():
            slot = lax.rem(i, 2)

            @pl.when(i + 1 < tiles)
            def _():
                for copy in left_copies(i + 1):
                    copy.start()

            @pl.when(lax.rem(i, row_tiles) == 0)
            def _():
                @pl.when(i > 0)
                def _():
                    for copy in weight_copies(i // row_tiles):
                        copy.start()

                for copy in weight_copies(i // row_tiles):
                    copy.wait()

            for copy in left_copies(i):
                copy.wait()
            total = times_transposed(lefts[slot, 0], weights[0]) + times_transposed(lefts[slot, 1], weights[1])

            @pl.when(i >= 2)
            def _():
                out_copy(i - 2).wait()

            tile_out[slot] = total.astype(BF)
            out_copy(i).start()

    def start():
        out_copy(tiles - 2).wait()
        out_copy(tiles - 1).wait()
        for copy in own_copies(cot_ref, grads, groups, own_sem):
            copy.wait()
        for g in order:
            scatter.start(g)

    def use(at, total):
        back, more = norm_back_rows(residual[at, :], gain[...], total)
        total_grad = grads[at, :].astype(F32) + back
        dr[at, :] = total_grad
        da_own[at, :] = total_grad.astype(BF)
        gain_grad[...] += more

    def spread(g):
        scatter.total(g, use)
        gather.start(g)

    def finish():
        for g in order:
            gather.finish(g)
            gather.sent(g)

    first = shift + tiles
    plan = {
        0: begin,
        after: whole_hidden,
        first: start,
        first + 3: lambda: scatter.forward(order[0]),
        first + 6: lambda: scatter.forward(order[-1]),
        first + 7: lambda: spread(order[0]),
        first + 9: lambda: spread(order[-1]),
        first + 11: lambda: gather.forward(order[0]),
        first + 15: lambda: gather.forward(order[-1]),
        first + 18: finish,
    }
    return plan, each, maker


def feed_extra(groups, n2, wg, wu, wd, residual, cot, gain):
    rows, width = residual.shape
    tokens, hidden = n2.shape[0], wg.shape[1]
    dma = pltpu.SemaphoreType.DMA
    outs = [
        jax.ShapeDtypeStruct((rows, width), F32),
        jax.ShapeDtypeStruct((tokens, width), BF),
        jax.ShapeDtypeStruct((1, width), F32),
        jax.ShapeDtypeStruct((tokens, width), BF),
    ] + [jax.ShapeDtypeStruct((tokens, hidden), BF)] * 3
    scratch = (
        Scatter.scratch(rows, width)
        + [
            pltpu.VMEM((2, width // 2, hidden), BF),
            pltpu.VMEM((2, 2, PAIR, hidden), BF),
            pltpu.VMEM((2, PAIR, width // 2), BF),
            dma((2,)),
            dma((2, 2)),
            dma((2,)),
            pltpu.VMEM((rows, width), BF),
            pltpu.VMEM((2, tokens, 2 * TILE), BF),
            dma((2,)),
            dma,
            dma((2, 10)),
            dma((2, 2)),
            dma((2, 2)),
        ]
        + Gather.scratch()
    )
    return (
        [n2, wg, wu, wd, residual, cot, gain],
        [ANY_SPEC] * 4 + [VMEM_SPEC, ANY_SPEC, VMEM_SPEC],
        outs,
        [VMEM_SPEC, ANY_SPEC, VMEM_SPEC] + [ANY_SPEC] * 4,
        scratch,
        functools.partial(feed_tasks, groups),
    )


def input_tasks(n_ctx, groups, extra_in, extra_out, scratch):
    i_ref, tokens_ref, dr, gain, gain_two_grad = extra_in
    input_grad, gain_sums = extra_out
    n = len(Scatter.scratch(16, 128))
    scatter = Scatter(i_ref, groups, scratch[:9], scratch[9:n])
    gains, got_tp, got_ctx, send_tp, recv_tp, send_ctx, recv_ctx, rows_in, own_sem = scratch[n:]
    order = list(reversed(range(len(groups))))
    me, rank = lax.axis_index("ctx"), lax.axis_index("tp")

    def tp_hop(k):
        return remote(gains.at[k], got_tp.at[k], send_tp.at[k], recv_tp.at[k], neighbours()[k])

    def ctx_hop(k):
        place = gains.at[2]
        return remote(place, got_ctx.at[k], send_ctx.at[k], recv_ctx.at[k], (jnp.bitwise_xor(me, k), rank))

    def begin():
        gains[0] = jnp.zeros(gains.shape[1:], F32)
        gains[0, 8:9, :] = gain_two_grad[...]
        for copy in own_copies(tokens_ref, rows_in, groups, own_sem):
            copy.start()
        for g in order:
            scatter.start(g)
        for copy in own_copies(tokens_ref, rows_in, groups, own_sem):
            copy.wait()

    def use(at, total):
        back, more = norm_back_rows(rows_in[at, :].astype(F32), gain[...], total)
        input_grad[at, :] = (dr[at, :] + back).astype(BF)
        gains[0, 0:1, :] += more

    def rest():
        scatter.total(order[-1], use)
        tp_hop(0).start()

    def second():
        tp_hop(0).wait()
        gains[1] = gains[0] + got_tp[0]
        tp_hop(1).start()

    def third():
        tp_hop(1).wait()
        gains[2] = gains[1] + got_tp[1]
        for k in range(1, n_ctx):
            ctx_hop(k).start()

    def finish():
        for k in range(1, n_ctx):
            ctx_hop(k).wait()
        got_ctx[0] = gains[2]
        total = got_ctx[jnp.bitwise_xor(me, 0)]
        for index in range(1, n_ctx):
            total = total + got_ctx[jnp.bitwise_xor(me, index)]
        gain_sums[...] = total

    return {
        0: begin,
        4: lambda: scatter.forward(order[0]),
        9: lambda: scatter.forward(order[-1]),
        10: lambda: scatter.total(order[0], use),
        13: rest,
        15: second,
        17: third,
        20: finish,
    }, None, None


def input_extra(n_ctx, groups, i_partial, tokens_in, dr, gain, gain_two_grad):
    rows, width = tokens_in.shape
    dma = pltpu.SemaphoreType.DMA
    outs = [jax.ShapeDtypeStruct((rows, width), BF), jax.ShapeDtypeStruct((16, width), F32)]
    return (
        [i_partial, tokens_in, dr, gain, gain_two_grad],
        [ANY_SPEC] * 2 + [VMEM_SPEC] * 3,
        outs,
        [VMEM_SPEC] * 2,
        Scatter.scratch(rows, width)
        + [
            pltpu.VMEM((3, 16, width), F32),
            pltpu.VMEM((2, 16, width), F32),
            pltpu.VMEM((n_ctx, 16, width), F32),
            dma((2,)),
            dma((2,)),
            dma((n_ctx,)),
            dma((n_ctx,)),
            pltpu.VMEM((rows, width), BF),
            dma((2,)),
        ],
        functools.partial(input_tasks, n_ctx, groups),
    )


def cast_kernel(out_in, gate_in, up_in, down_in, qkv_in, out_ref, gate_ref, up_ref, down_ref, *qkv_refs):
    for source, dest in ((out_in, out_ref), (gate_in, gate_ref), (up_in, up_ref), (down_in, down_ref)):
        dest[...] = source[...].astype(F32)
    width = qkv_refs[0].shape[1]
    for k, dest in enumerate(qkv_refs):
        dest[...] = qkv_in[:, k * width : (k + 1) * width].astype(F32)


def cast_sums(*sums):
    steps = 16
    block = lambda array: pl.BlockSpec((array.shape[0] // steps, array.shape[1]), lambda i: (i, 0))
    outs = [jax.ShapeDtypeStruct(array.shape, F32) for array in sums[:-1]]
    outs += [jax.ShapeDtypeStruct((sums[-1].shape[0], sums[-1].shape[1] // 3), F32)] * 3
    return pl.pallas_call(
        cast_kernel,
        out_shape=outs,
        grid=(steps,),
        in_specs=[block(array) for array in sums],
        out_specs=[block(array) for array in outs],
        compiler_params=params(),
        cost_estimate=pl.CostEstimate(
            flops=0, bytes_accessed=sum(6 * array.shape[0] * array.shape[1] for array in sums), transcendentals=0
        ),
    )(*sums)


class Exchange:
    def __init__(self, dest, sems, by_device):
        self.dest, self.by_device = dest, by_device
        self.send_sem, self.recv_sem, self.own_sem = sems
        self.n_ctx = dest.shape[1]
        self.me, self.rank = lax.axis_index("ctx"), lax.axis_index("tp")

    @staticmethod
    def scratch(units, n_ctx):
        dma = pltpu.SemaphoreType.DMA
        return [dma((units, n_ctx)), dma((units, n_ctx)), dma((units,))]

    def copy(self, source, unit, k):
        other = jnp.bitwise_xor(self.me, k)
        place = other if self.by_device else k
        return remote(
            source.at[unit, place],
            self.dest.at[unit, k],
            self.send_sem.at[unit, k],
            self.recv_sem.at[unit, k],
            (other, self.rank),
        )

    def own(self, source, unit):
        place = self.me if self.by_device else 0
        return pltpu.make_async_copy(source.at[unit, place], self.dest.at[unit, 0], self.own_sem.at[unit])

    def start(self, source, unit):
        for k in reversed(range(1, self.n_ctx)):
            self.copy(source, unit, k).start()
        self.own(source, unit).start()

    def start_some(self, source, unit, first, count):
        for k in reversed(range(self.n_ctx)):
            other = jnp.bitwise_xor(self.me, k)

            @pl.when((other >= first) & (other < first + count))
            def _(k=k):
                if k == 0:
                    self.own(source, unit).start()
                else:
                    self.copy(source, unit, k).start()

    def arrived(self, source, unit):
        for k in range(1, self.n_ctx):
            self.copy(source, unit, k).wait_recv()
        self.own(source, unit).wait()

    def sent(self, source, unit):
        for k in range(1, self.n_ctx):
            self.copy(source, unit, k).wait_send()


def greet(n_ctx, tp_too):
    index, rank = lax.axis_index("ctx"), lax.axis_index("tp")
    barrier = pltpu.get_barrier_semaphore()
    for k in range(1, n_ctx):
        signal(barrier, (jnp.bitwise_xor(index, k), rank))
    if tp_too:
        for device in neighbours():
            signal(barrier, device)
    pl.semaphore_wait(barrier, n_ctx - 1 + (2 if tp_too else 0))


def rotation(cos_tab, sin_tab, block_cos, block_sin):
    sign = jnp.where(lax.broadcasted_iota(jnp.int32, cos_tab.shape, 1) < HD // 2, -1.0, 1.0)
    return cos_tab * block_cos - sin_tab * block_sin, (sin_tab * block_cos + cos_tab * block_sin) * sign


def in_turn(count):
    return [count - 1] + list(range(count - 1))


def attend_rows(qs, ks, vs, os, tile):
    length = qs.shape[0]
    factor = -(HD ** (-0.5)) * LOG2E
    shift = math.log(length) * LOG2E
    row_at = lax.broadcasted_iota(jnp.int32, (tile, tile), 0)
    col_at = lax.broadcasted_iota(jnp.int32, (tile, tile), 1)
    for i in range(length // tile):
        query = qs[i * tile : (i + 1) * tile, :]

        def part(j, masked):
            at = pl.ds(pl.multiple_of(j * tile, tile), tile)
            raw = times_transposed(query, ks[at, :])
            prob = 1.0 / (1.0 + jnp.exp2(raw * factor + shift))
            if masked:
                prob = jnp.where(row_at >= col_at, prob, 0.0)
            return dot(prob.astype(BF), vs[at, :])

        total = part(i, True)
        if i > 0:
            total = lax.fori_loop(0, i, lambda j, acc: acc + part(j, False), total)
        os[i * tile : (i + 1) * tile, :] = total.astype(BF)


def forward_kernel(n_ctx, groups, units, tile, *refs):
    tokens_ref, cot_ref, gain_one, gain_two, wq_ref, wk_ref, wv_ref, wo_ref, cos_ref, sin_ref, bcos_ref, bsin_ref, valid_ref = refs[:13]
    n1_out, got_out, heads_out, residual, n2_out, cot_out = refs[13:19]
    x_ref, rows_buf, own_buf, send, got, o_send, o_got, tabs, qs, ks, vs, os = refs[19:31]
    rest = refs[31:]
    n_gather, n_exchange = len(Gather.scratch()), len(Exchange.scratch(1, 2))
    n1_sems, rest = rest[:n_gather], rest[n_gather:]
    n2_sems, rest = rest[:n_gather], rest[n_gather:]
    cot_sems, rest = rest[:n_gather], rest[n_gather:]
    x_sems, rest = rest[:n_exchange], rest[n_exchange:]
    o_sems, rest = rest[:n_exchange], rest[n_exchange:]
    (n1_sem, got_sem, load_sem), rest = rest[:3], rest[3:]
    me, rank = lax.axis_index("ctx"), lax.axis_index("tp")
    odd = lax.rem(rank, 2)
    heads = wq_ref.shape[1] // HD
    per_unit = n_ctx // heads
    own_at = [pl.multiple_of(odd * BLOCK, BLOCK), pl.multiple_of((1 - odd) * PAIR, BLOCK)]

    def load_x(g):
        _, rows, own = groups[g]
        return pltpu.make_async_copy(
            tokens_ref.at[pl.ds(own_at[g], rows)], x_ref.at[pl.ds(own, rows)], load_sem.at[g]
        )

    for g in range(2):
        load_x(g).start()
    greet(n_ctx, True)
    gather_one = Gather(own_buf, rows_buf, groups, n1_sems, local=False)
    gather_two = Gather(own_buf, n2_out, groups, n2_sems)
    gather_cot = Gather(cot_ref, cot_out, groups, cot_sems, own_at=own_at)
    scatter = Scatter(rows_buf, groups, rest[:6], rest[6:], loaded=False)
    trade = Exchange(got, x_sems, True)
    trade_back = Exchange(o_got, o_sems, False)

    def halves_of(u):
        return halves_at(odd if units[u][1] else 0)

    def normed(source, gain, at):
        values = source[at, :].astype(F32)
        return (values * inverse_rms(values) * gain[...]).astype(BF)

    def begin(g):
        base, rows, own = groups[g]
        load_x(g).wait()
        low = normed(x_ref, gain_one, pl.ds(own, rows))
        own_buf[pl.ds(own, rows), :] = low
        gather_one.start(g)
        rows_buf[pl.ds(base, rows), :] = low

    begin(0)
    for half, block in enumerate((me, 2 * n_ctx - 1 - me)):
        cos_part, sin_part = rotation(
            cos_ref[...], sin_ref[...], bcos_ref[pl.ds(block, 1), :], bsin_ref[pl.ds(block, 1), :]
        )
        tabs[0, half * BLOCK : (half + 1) * BLOCK, :] = cos_part
        tabs[1, half * BLOCK : (half + 1) * BLOCK, :] = sin_part

    def query(u, block):
        base, flipped = units[u]
        first, second = halves_of(u)
        at = pl.ds(base + block * PAIR, PAIR)
        rows = rows_buf[at, :]
        for which, w_ref in enumerate((wq_ref, wk_ref, wv_ref)):
            product = dot(rows, w_ref[...])
            for head in range(heads):
                part = product[:, head * HD : (head + 1) * HD]
                pair = block * heads + head
                for half, to in ((0, first), (1, second)):
                    piece = part[half * BLOCK : (half + 1) * BLOCK]
                    if which < 2:
                        piece = piece * tabs[0, to, :] + pltpu.roll(piece, HD // 2, 1) * tabs[1, to, :]
                    else:
                        piece = piece * valid_ref[pl.ds(base + block * PAIR + half * BLOCK, BLOCK), :]
                    send[u, pair, which, to, :] = piece.astype(BF)
        trade.start_some(send, u, block * heads, heads)

    store_n1 = pltpu.make_async_copy(rows_buf, n1_out, n1_sem)
    store_got = [pltpu.make_async_copy(got.at[u], got_out.at[u], got_sem.at[u]) for u in range(len(units))]

    query(0, 0)
    gather_one.forward_x(0)
    gather_one.forward_y(0)
    begin(1)
    query(0, 1)
    query(1, 0)
    gather_one.finish(0)
    query(1, 1)
    gather_one.forward(1)
    gather_one.finish(1)
    for g in range(2):
        gather_cot.start(g)
    query(2, 0)
    query(2, 1)
    store_n1.start()

    def attend(u):
        trade.arrived(send, u)
        store_got[u].start()
        for k in range(n_ctx):
            front, back = both_places(me, k, n_ctx)
            for which, dest in enumerate((qs, ks, vs)):
                dest[front, :] = got[u, k, which, :BLOCK, :]
                dest[back, :] = got[u, k, which, BLOCK:, :]
        attend_rows(qs, ks, vs, os, tile)
        for k in range(n_ctx):
            front, back = both_places(me, k, n_ctx)
            o_send[u, k, :BLOCK, :] = os[front, :]
            o_send[u, k, BLOCK:, :] = os[back, :]
        trade_back.start(o_send, u)

    def project(u):
        trade_back.arrived(o_send, u)
        base, _ = units[u]
        first, second = halves_of(u)
        for block in range(per_unit):
            at = pl.ds(base + block * PAIR, PAIR)
            low = valid_ref[at, :].astype(BF)
            for head in range(heads):
                place = jnp.bitwise_xor(me, block * heads + head)
                part = jnp.concatenate([o_got[u, place, first, :], o_got[u, place, second, :]], axis=0)
                heads_out[at, head * HD : (head + 1) * HD] = part * low
            rows_buf[at, :] = dot(heads_out[at, :], wo_ref[...]).astype(BF)

    def use(at, total):
        residual[at, :] = x_ref[at, :].astype(F32) + total
        own_buf[at, :] = normed(residual, gain_two, at)

    def finish_group(g):
        scatter.total(g, use)
        gather_two.start(g)

    attend(0)
    for g in range(2):
        gather_one.sent(g)
    store_n1.wait()
    attend(1)
    for g in range(2):
        gather_cot.forward(g)
    project(0)
    scatter.start(0, (0,), loads=False)
    project(1)
    scatter.start(0, (1, 3, 2), loads=False)
    attend(2)
    scatter.forward(0)
    project(2)
    scatter.start(1, loads=False)
    finish_group(0)
    scatter.forward(1)
    finish_group(1)
    gather_two.forward(0)
    gather_two.forward(1)
    for u in range(len(units)):
        trade.sent(send, u)
        trade_back.sent(o_send, u)
        store_got[u].wait()
    for g in range(2):
        gather_cot.finish(g)
        gather_two.finish(g)
        gather_two.sent(g)
        gather_cot.sent(g)


def forward_layer(tokens_in, cot_in, gain_one, gain_two, wq, wk, wv, wo, tables, valid, n_ctx, groups, units):
    rows, depth = tokens_in.shape
    width = wq.shape[1]
    tokens = valid.shape[0]
    length = 2 * n_ctx * BLOCK
    n_units = len(units)
    vmem = lambda shape, dtype=BF: pltpu.VMEM(shape, dtype)
    outs = [
        jax.ShapeDtypeStruct((tokens, depth), BF),
        jax.ShapeDtypeStruct((n_units, n_ctx, 3, PAIR, HD), BF),
        jax.ShapeDtypeStruct((tokens, width), BF),
        jax.ShapeDtypeStruct((rows, depth), F32),
        jax.ShapeDtypeStruct((tokens, depth), BF),
        jax.ShapeDtypeStruct((tokens, depth), BF),
    ]
    return pl.pallas_call(
        functools.partial(forward_kernel, n_ctx, groups, units, min(512, length)),
        out_shape=outs,
        in_specs=[ANY_SPEC, ANY_SPEC] + [VMEM_SPEC] * 11,
        out_specs=[ANY_SPEC, ANY_SPEC, VMEM_SPEC, VMEM_SPEC, ANY_SPEC, ANY_SPEC],
        scratch_shapes=[
            vmem((rows, depth)),
            vmem((tokens, depth)),
            vmem((rows, depth)),
            vmem((n_units, n_ctx, 3, PAIR, HD)),
            vmem((n_units, n_ctx, 3, PAIR, HD)),
            vmem((n_units, n_ctx, PAIR, HD)),
            vmem((n_units, n_ctx, PAIR, HD)),
            vmem((2, PAIR, HD), F32),
        ]
        + [vmem((length, HD))] * 4
        + Gather.scratch() * 3
        + Exchange.scratch(n_units, n_ctx) * 2
        + [pltpu.SemaphoreType.DMA, pltpu.SemaphoreType.DMA((n_units,)), pltpu.SemaphoreType.DMA((2,))]
        + Scatter.scratch(rows, depth, loaded=False),
        compiler_params=pltpu.CompilerParams(vmem_limit_bytes=VMEM_LIMIT, collective_id=3, has_side_effects=True),
        cost_estimate=pl.CostEstimate(
            flops=8 * tokens * depth * width, bytes_accessed=8 * tokens * depth, transcendentals=0
        ),
    )(tokens_in, cot_in, gain_one, gain_two, wq, wk, wv, wo, *tables, valid)


def attend_rows_back(qs, ks, vs, gs, os, dqs, cos_ref, sin_ref, tile):
    length = qs.shape[0]
    scale = HD ** (-0.5)
    factor = -scale * LOG2E
    shift = math.log(length) * LOG2E
    count = length // tile
    key_at = lax.broadcasted_iota(jnp.int32, (tile, tile), 0)
    query_at = lax.broadcasted_iota(jnp.int32, (tile, tile), 1)
    dqs[...] = jnp.zeros_like(dqs)

    def unrotate(values, at):
        return (values * cos_ref[at, :] - pltpu.roll(values, HD // 2, 1) * sin_ref[at, :]).astype(BF)

    for j in range(count):
        own = slice(j * tile, (j + 1) * tile)
        keys = ks[own, :]
        values = vs[own, :]

        def part(i, masked):
            at = pl.ds(pl.multiple_of(i * tile, tile), tile)
            query = qs[at, :]
            grad = gs[at, :]
            raw = times_transposed(keys, query)
            prob = 1.0 / (1.0 + jnp.exp2(raw * factor + shift))
            if masked:
                prob = jnp.where(query_at >= key_at, prob, 0.0)
            prob_grad = times_transposed(values, grad)
            score_grad = (prob_grad * prob * (1.0 - prob)).astype(BF)
            dqs[at, :] += contract_rows(score_grad, keys)
            return dot(score_grad, query), dot(prob.astype(BF), grad)

        total = part(j, True)
        if j + 1 < count:

            def step(i, acc):
                more = part(i, False)
                return acc[0] + more[0], acc[1] + more[1]

            total = lax.fori_loop(j + 1, count, step, total)
        os[1, own, :] = unrotate(total[0] * scale, own)
        os[2, own, :] = total[1].astype(BF)
    for i in range(count):
        at = slice(i * tile, (i + 1) * tile)
        os[0, at, :] = unrotate(dqs[at, :] * scale, at)


def middle_kernel(n_ctx, groups, units, tile, *refs):
    da_ref, got_ref, h_ref, residual_ref, wd_ref, wq_ref, wk_ref, wv_ref, wo_ref = refs[:9]
    cos_ref, sin_ref, bcos_ref, bsin_ref, valid_ref = refs[9:14]
    grad_ref, partial_out, output = refs[14:17]
    rows_buf, got, do_send, do_got, back_got, h_buf, wd_buf, res_buf, cos_full, sin_full = refs[17:27]
    qs, ks, vs, gs, os, dqs = refs[27:33]
    rest = refs[33:]
    back_send = got
    n_exchange = len(Exchange.scratch(1, 2))
    do_sems, back_sems, rest = rest[:n_exchange], rest[n_exchange : 2 * n_exchange], rest[2 * n_exchange :]
    (da_sem, got_sem, out_sem, h_sem, wd_sem, res_sem, y_sem), rest = rest[:7], rest[7:]
    me, rank = lax.axis_index("ctx"), lax.axis_index("tp")
    odd = lax.rem(rank, 2)
    heads = wq_ref.shape[1] // HD
    per_unit = n_ctx // heads
    unit_rows = per_unit * PAIR
    count = len(units)
    order = in_turn(count)

    def rows_of(u):
        return pl.ds(units[u][0], unit_rows)

    load_da = [pltpu.make_async_copy(da_ref.at[rows_of(u)], rows_buf.at[rows_of(u)], da_sem.at[u]) for u in range(count)]
    load_got = [pltpu.make_async_copy(got_ref.at[u], got.at[u], got_sem.at[u]) for u in range(count)]
    for u in order:
        load_da[u].start()
    for u in order:
        load_got[u].start()
    first_wd = pltpu.make_async_copy(wd_ref.at[:, pl.ds(0, wd_buf.shape[1])], wd_buf, wd_sem)
    first_wd.start()
    greet(n_ctx, True)
    scatter = Scatter(rows_buf, groups, rest[:6], rest[6:], loaded=False)
    trade = Exchange(do_got, do_sems, True)
    trade_back = Exchange(back_got, back_sems, False)

    for u in order:
        load_da[u].wait()
        base, flipped = units[u]
        first, second = halves_at(odd if flipped else 0)
        for block in range(per_unit):
            at = pl.ds(base + block * PAIR, PAIR)
            grad = times_transposed(rows_buf[at, :], wo_ref[...]).astype(BF)
            low = valid_ref[at, :].astype(BF)
            for head in range(heads):
                part = grad[:, head * HD : (head + 1) * HD] * low
                do_send[u, block * heads + head, first, :] = part[:BLOCK]
                do_send[u, block * heads + head, second, :] = part[BLOCK:]
        trade.start(do_send, u)
    for block in range(2 * n_ctx):
        at = slice(block * BLOCK, (block + 1) * BLOCK)
        cos_full[at, :], sin_full[at, :] = rotation(
            cos_ref[...], sin_ref[...], bcos_ref[block : block + 1, :], bsin_ref[block : block + 1, :]
        )
    for u in order:
        load_got[u].wait()

    def attend(turn, carry):
        u = lax.rem(turn + count - 1, count)
        trade.arrived(do_send, u)
        for k in range(n_ctx):
            front, back = both_places(me, k, n_ctx)
            for which, dest in enumerate((qs, ks, vs)):
                dest[front, :] = got[u, k, which, :BLOCK, :]
                dest[back, :] = got[u, k, which, BLOCK:, :]
            gs[front, :] = do_got[u, k, :BLOCK, :]
            gs[back, :] = do_got[u, k, BLOCK:, :]
        attend_rows_back(qs, ks, vs, gs, os, dqs, cos_full, sin_full, tile)
        for k in range(n_ctx):
            front, back = both_places(me, k, n_ctx)
            for which in range(3):
                back_send[u, k, which, :BLOCK, :] = os[which, front, :]
                back_send[u, k, which, BLOCK:, :] = os[which, back, :]
        trade_back.start(back_send, u)
        return carry

    lax.fori_loop(0, count, attend, 0)

    tiles = rows_buf.shape[0] // PAIR

    def tile_rows(tile):
        return pl.ds(pl.multiple_of(tile * PAIR, PAIR), PAIR)

    def load_h(step):
        slot = lax.rem(step, 2)
        return pltpu.make_async_copy(h_ref.at[tile_rows(lax.rem(step, tiles))], h_buf.at[slot], h_sem.at[slot])

    columns = wd_buf.shape[1]
    parts = rows_buf.shape[1] // columns

    def part_columns(part):
        return pl.ds(pl.multiple_of(part * columns, columns), columns)

    def load_wd(part):
        return pltpu.make_async_copy(wd_ref.at[:, part_columns(part)], wd_buf, wd_sem)

    load_h(0).start()

    def down(step, carry):
        part, tile = step // tiles, lax.rem(step, tiles)

        @pl.when(step + 1 < tiles * parts)
        def _():
            load_h(step + 1).start()

        @pl.when(tile == 0)
        def _():
            @pl.when(part > 0)
            def _():
                load_wd(part).start()

            load_wd(part).wait()

        load_h(step).wait()
        rows_buf[tile_rows(tile), part_columns(part)] = dot(h_buf[lax.rem(step, 2)], wd_buf[...]).astype(BF)
        return carry

    lax.fori_loop(0, tiles * parts, down, 0)
    last_group = len(groups) - 1
    out_rows = rest[0]
    for g in (last_group, 0):
        scatter.start(g, loads=False)

    def use(at, total):
        size = total.shape[0]
        load = pltpu.make_async_copy(residual_ref.at[at], res_buf.at[pl.ds(0, size)], res_sem)
        load.start()
        load.wait()
        low = (res_buf[:size, :] + total).astype(BF)
        out_rows[at, :] = low

    def store(number, first):
        slot = number % 2
        return pltpu.make_async_copy(h_buf.at[slot], partial_out.at[pl.ds(first, PAIR)], out_sem.at[slot])

    stored = []
    for turn, u in enumerate(order):
        trade_back.arrived(back_send, u)
        base, flipped = units[u]
        first, second = halves_at(odd if flipped else 0)
        for block in range(per_unit):
            at = pl.ds(base + block * PAIR, PAIR)
            low = valid_ref[at, :].astype(BF)
            total = None
            for which, w_ref in enumerate((wq_ref, wk_ref, wv_ref)):
                width = heads * HD
                for head in range(heads):
                    place = jnp.bitwise_xor(me, block * heads + head)
                    part = jnp.concatenate(
                        [back_got[u, place, which, first, :], back_got[u, place, which, second, :]], axis=0
                    )
                    columns = slice(which * width + head * HD, which * width + (head + 1) * HD)
                    grad_ref[at, columns] = part * low if which == 2 else part
                product = times_transposed(grad_ref[at, which * width : (which + 1) * width], w_ref[...])
                total = product if total is None else total + product
            number = len(stored)
            if number >= 2:
                stored[number - 2].wait()
            h_buf[number % 2] = total.astype(BF)
            stored.append(store(number, base + block * PAIR))
            stored[-1].start()
        if turn == 0:
            scatter.forward(last_group)
            scatter.forward(0)
        if turn == 1:
            for g in (last_group, 0):
                scatter.total(g, use)
            store_y = pltpu.make_async_copy(out_rows, output, y_sem)
            store_y.start()
    store_y.wait()
    for copy in stored[-2:]:
        copy.wait()
    for u in order:
        trade.sent(do_send, u)
        trade_back.sent(back_send, u)


def middle_layer(da, got, h, residual, wq, wk, wv, wo, wd, tables, valid, n_ctx, groups, units):
    tokens, depth = da.shape
    width = wq.shape[1]
    length = 2 * n_ctx * BLOCK
    count = len(units)
    vmem = lambda shape, dtype=BF: pltpu.VMEM(shape, dtype)
    dma = pltpu.SemaphoreType.DMA
    three, one = (count, n_ctx, 3, PAIR, HD), (count, n_ctx, PAIR, HD)
    most_rows = max(rows for _, rows, _ in groups) // 2
    return pl.pallas_call(
        functools.partial(middle_kernel, n_ctx, groups, units, min(512, length)),
        out_shape=[
            jax.ShapeDtypeStruct((tokens, 3 * width), BF),
            jax.ShapeDtypeStruct((tokens, depth), BF),
            jax.ShapeDtypeStruct(residual.shape, BF),
        ],
        in_specs=[ANY_SPEC] * 5 + [VMEM_SPEC] * 9,
        out_specs=[VMEM_SPEC, ANY_SPEC, ANY_SPEC],
        scratch_shapes=[vmem((tokens, depth)), vmem(three), vmem(one), vmem(one), vmem(three)]
        + [vmem((2, PAIR, depth)), vmem((h.shape[1], depth // 2)), vmem((most_rows, depth), F32)]
        + [vmem((length, HD), F32)] * 2
        + [vmem((length, HD))] * 4
        + [vmem((3, length, HD)), vmem((length, HD), F32)]
        + Exchange.scratch(count, n_ctx) * 2
        + [dma((count,)), dma((count,)), dma((2,)), dma((2,)), dma, dma, dma]
        + Scatter.scratch(residual.shape[0], depth, loaded=False),
        compiler_params=pltpu.CompilerParams(vmem_limit_bytes=VMEM_LIMIT, collective_id=4, has_side_effects=True),
        cost_estimate=pl.CostEstimate(
            flops=8 * tokens * depth * width + 2 * tokens * depth * h.shape[1],
            bytes_accessed=8 * tokens * depth,
            transcendentals=0,
        ),
    )(da, got, h, residual, wd, wq, wk, wv, wo, *tables, valid)


def body(
    tokens,
    counts,
    norm_gain,
    w_query,
    w_key,
    w_value,
    w_output,
    mlp_gain,
    w_gate,
    w_up,
    w_down,
    cotangent,
):
    n_ctx = lax.axis_size("ctx")
    me = lax.axis_index("ctx")
    rank = lax.axis_index("tp")
    odd = rank & 1
    core = me & 1
    length = 2 * BLOCK * n_ctx
    heads = w_query.shape[1] // HD
    gain_one = norm_gain.astype(F32)
    gain_two = mlp_gain.astype(F32)

    inverse = THETA ** (-(jnp.arange(HD // 2, dtype=F32) * (2.0 / HD)))
    angles = jnp.arange(length, dtype=jnp.int32).astype(F32)[:, None] * inverse[None, :]
    cos_half, sin_half = jnp.cos(angles), jnp.sin(angles)
    cos_full = jnp.concatenate([cos_half, cos_half], axis=1)
    sin_full = jnp.concatenate([-sin_half, sin_half], axis=1)

    def own_blocks(table):
        front = lax.dynamic_slice_in_dim(table, me * BLOCK, BLOCK, 0)
        back = lax.dynamic_slice_in_dim(table, (2 * n_ctx - 1 - me) * BLOCK, BLOCK, 0)
        return front, back

    cos_front, cos_back = own_blocks(cos_full)
    sin_front, sin_back = own_blocks(sin_full)
    own_counts = lax.dynamic_index_in_dim(counts, me, 0, keepdims=False)
    offsets = jnp.arange(BLOCK, dtype=jnp.int32)

    def valid_of(sequence_list, half_list):
        held = own_counts[jnp.stack(sequence_list), jnp.stack(half_list)]
        return (offsets[None, :] < held[:, None]).astype(F32).reshape(-1)

    cos_own = jnp.concatenate([cos_front, cos_back])
    sin_own = jnp.concatenate([sin_front, sin_back])
    sequences = counts.shape[1]
    paired = by_four() and sequences == 6 and n_ctx == 2 * heads
    if paired:
        ranks = [rank ^ k for k in range(4)]
        blocks_a = [(3 * (r >> 1) + 2 * (r & 1), jnp.int32(half)) for r in ranks for half in range(2)]
        blocks_b = [(1 + 3 * (r >> 1), r & 1) for r in ranks]
        flat_valid = valid_of(*zip(*(blocks_a + blocks_b)))
        valids = {"b": flat_valid[len(blocks_a) * BLOCK :], "a": flat_valid[: len(blocks_a) * BLOCK]}
        flip_back = lambda own: jnp.where(odd == 1, jnp.roll(own, BLOCK, axis=0), own)
        tables = {
            "b": (jnp.tile(flip_back(cos_own), (2, 1)), jnp.tile(flip_back(sin_own), (2, 1))),
            "a": (jnp.tile(cos_own, (4, 1)), jnp.tile(sin_own, (4, 1))),
        }
        scalars = {"b": jnp.stack([me, odd]).astype(jnp.int32), "a": jnp.stack([me, 0]).astype(jnp.int32)}
        n_pairs = {"b": 2 * heads, "a": 4 * heads}
    else:
        flat_valid = (offsets[None, None, :] < own_counts[:, :, None]).astype(F32).reshape(-1)
        valids = {"a": flat_valid}
        tables = {"a": (jnp.tile(cos_own, (sequences, 1)), jnp.tile(sin_own, (sequences, 1)))}
        scalars = {"a": jnp.stack([me, 0]).astype(jnp.int32)}
        n_pairs = {"a": sequences * heads}
    names = tuple(n_pairs)

    def own_rows(array):
        if not paired:
            return {"a": array}
        return {
            "b": lax.dynamic_slice_in_dim(array, (1 - odd) * PAIR, BLOCK, 0),
            "a": lax.dynamic_slice_in_dim(array, odd * BLOCK, PAIR, 0),
        }

    def whole_rows(array):
        return jnp.where(odd == 1, jnp.roll(array, BLOCK, axis=0), array) if paired else array

    x_own = {name: rows.astype(F32) for name, rows in own_rows(tokens[0]).items()}
    g_own = own_rows(cotangent[0])

    split = by_four()
    rows_of = {name: valids[name].shape[0] for name in names}
    total_rows = sum(rows_of.values())
    first_row = {"a": 0, "b": rows_of["a"]}
    valid_head = {name: jnp.broadcast_to(valids[name][:, None], (rows_of[name], HD)) for name in names}
    valid_wide = {name: jnp.broadcast_to(valids[name][:, None].astype(BF), (rows_of[name], heads * HD)) for name in names}
    near = [k for k in range(n_ctx) if k < 6]
    far = [k for k in range(n_ctx) if k >= 6]
    state = {}

    def fence():
        names_held = list(state)
        values = lax.optimization_barrier([state[name] for name in names_held])
        state.update(zip(names_held, values))

    def only_b(step):
        if "b" in names:
            step("b")

    def norm_one(n):
        state["n1", n] = (x_own[n] * inverse_rms(x_own[n]) * gain_one).astype(BF)

    def gather_a(key):
        def step(n):
            state[key, n] = gather_first(state[key, n])

        return step

    def gather_b(key):
        def step(n):
            state[key, n] = gather_second(state[key, n])

        return step

    def query(n):
        state["n1", n] = gathered(state["n1", n])
        cos_tab, sin_tab = tables[n]
        state["qkv", n] = project_qkv(
            scalars[n], state["n1", n], w_query, w_key, w_value, cos_tab, sin_tab, valid_head[n], n_ctx
        )

    def swap_part(key, places, to):
        def step(n):
            got = dict(state.get((to, n), {}))
            got.update(exchange(state[key, n], places, n_ctx))
            state[to, n] = got
            if len(got) == n_ctx:
                state[to, n] = [got[k] for k in range(n_ctx)]
                del state[key, n]

        return step

    def attend(n):
        state["mixed", n] = attention_forward(scalars[n], state["got", n], n_ctx)

    def project(n):
        heads_out, *parts = project_out(
            scalars[n], state.pop(("back", n)), w_output, valid_wide[n], n_pairs[n], n_ctx, split
        )
        state["heads", n], state["r", n] = heads_out, tuple(parts)

    def scatter_a(key):
        def step(n):
            state[key, n] = scatter_first(state[key, n])

        return step

    def scatter_b(key):
        def step(n):
            state[key, n] = scatter_second(state[key, n])

        return step

    def norm_two(n):
        residual = x_own[n] + scattered(state.pop(("r", n)))
        state["residual", n] = residual
        state["n2", n] = (residual * inverse_rms(residual) * gain_two).astype(BF)

    def core_mlp(n):
        state["n2", n] = gathered(state["n2", n])
        state["cot", n] = gathered(state["cot", n])
        held = state.get("mlp", ())
        state["mlp"] = mlp_core(
            state["n2", n], state["cot", n], w_gate, w_up, w_down, total_rows, first_row[n], held
        )

    def attend_back(n):
        state["dqkv", n] = attention_backward(
            scalars[n], state.pop(("got", n)), state.pop(("gdo", n)), cos_full, sin_full, n_ctx
        )

    def query_back(n):
        dq, dk, dv, *parts = project_in(
            scalars[n], state.pop(("gdqkv", n)), (w_query, w_key, w_value), valid_wide[n], n_pairs[n], n_ctx, False
        )
        state["dq", n], state["dk", n], state["dv", n], state["i", n] = dq, dk, dv, parts[0]

    def joined(key):
        parts = [state[key, n] for n in ("a", "b") if n in names]
        return jnp.concatenate(parts) if len(parts) > 1 else parts[0]

    groups = tuple((first_row[n], rows_of[n] // 4, first_row[n] // 4) for n in ("a", "b") if n in names)

    if paired:
        units = ((0, False), (2 * PAIR, False), (4 * PAIR, True))
        wide_valid = jnp.broadcast_to(flat_valid[:, None], (total_rows, HD))
        twice = lambda table: jnp.concatenate([table, table], axis=1)
        starts = BLOCK * jnp.arange(2 * n_ctx, dtype=jnp.int32)
        spans = [at.astype(F32)[:, None] * inverse[None, :] for at in (offsets, starts)]
        turns = [twice(part(angle)) for angle in spans for part in (jnp.cos, jnp.sin)]
        all_n1, got, heads_out, own_residual, all_n2, all_cot = forward_layer(
            tokens[0], cotangent[0], gain_one[None], gain_two[None], w_query, w_key, w_value, w_output,
            turns, wide_valid, n_ctx, groups, units,
        )
    else:
        norm_one("a")
        state["cot", "a"] = g_own["a"]
        gather_a("n1")("a")
        query("a")
        swap_part("qkv", range(n_ctx), "got")("a")
        attend("a")
        swap_part("mixed", range(n_ctx), "back")("a")
        project("a")
        scatter_a("r")("a")
        norm_two("a")
        gather_a("n2")("a")
        gather_a("cot")("a")
        all_n1, all_n2, all_cot = state["n1", "a"], gathered(state["n2", "a"]), gathered(state["cot", "a"])
        heads_out, own_residual = state["heads", "a"], state["residual", "a"]
    if paired:
        extra = feed_extra(groups, all_n2, w_gate, w_up, w_down, own_residual, cotangent[0], gain_two[None])
        sum_down, sum_gate, sum_up, sum_out, dr, da, gain_two_grad, _, h, _, _ = weight_sums(
            [(w_down.shape[0], 0), (all_n2, 1), (all_n2, 2), (heads_out, 3)],
            [all_cot], n_ctx, 1, extra, late=(5, 6, 1), limit=62 * 1024 * 1024,
        )
        dqkv, i_partial, output = middle_layer(
            da, got, h, own_residual, w_query, w_key, w_value, w_output, w_down, turns, wide_valid, n_ctx, groups, units
        )
        extra = input_extra(n_ctx, groups, i_partial, tokens[0], dr, gain_one[None], gain_two_grad)
        sum_qkv, input_grad, gain_sums = weight_sums(
            [(all_n1, 0)], [dqkv], n_ctx, 2, extra
        )
        gains = gain_sums[::8]
    else:
        own_grads = cotangent[0]
        h, dgp, dup = mlp_core(all_n2, all_cot, w_gate, w_up, w_down, total_rows, 0)
        d_partial = (times_transposed(dgp, w_gate) + times_transposed(dup, w_up)).astype(BF)
        y_partial = dot(h, w_down).astype(BF)
        (sum_down,) = weight_sums([(h, 0)], [all_cot], n_ctx, 1)
        sum_gate, sum_up = weight_sums([(all_n2, 0), (all_n2, 1)], [dgp, dup], n_ctx, 2)
        back, gain_two_grad = norm_back_rows(own_residual, gain_two, scattered(scatter_first((d_partial,))))
        dr = own_grads.astype(F32) + back
        da = gathered(gather_first(dr.astype(BF)))
        output = (own_residual + scattered(scatter_first((y_partial,)))).astype(BF)
        state["do", "a"] = heads_back(scalars["a"], da, w_output, valid_wide["a"], n_ctx)
        swap_part("do", range(n_ctx), "gdo")("a")
        attend_back("a")
        swap_part("dqkv", range(n_ctx), "gdqkv")("a")
        query_back("a")
        (sum_out,) = weight_sums([(heads_out, 0)], [da], n_ctx, 3)
        (sum_qkv,) = weight_sums(
            [(all_n1, 0)], [jnp.concatenate([state[key, "a"] for key in ("dq", "dk", "dv")], axis=1)], n_ctx, 4
        )
        back, gain_one_grad = norm_back_rows(x_own["a"], gain_one, scattered(scatter_first((state["i", "a"],))))
        input_grad = (dr + back).astype(BF)
    grad_out, grad_gate, grad_up, grad_down, grad_query, grad_key, grad_value = cast_sums(
        sum_out, sum_gate, sum_up, sum_down, sum_qkv
    )
    if not paired:
        gains = lax.psum(jnp.concatenate([gain_one_grad, gain_two_grad]), ("ctx", "tp"))
    return (
        whole_rows(output)[None],
        whole_rows(input_grad)[None],
        gains[0],
        grad_query,
        grad_key,
        grad_value,
        grad_out,
        gains[1],
        grad_gate,
        grad_up,
        grad_down,
    )


def solution(mesh):
    placed = (
        P("ctx", "tp", None),
        P(),
        P(),
        P(None, "tp"),
        P(None, "tp"),
        P(None, "tp"),
        P("tp", None),
        P(),
        P(None, "tp"),
        P(None, "tp"),
        P("tp", None),
        P("ctx", "tp", None),
    )
    return jax.shard_map(
        body,
        mesh=mesh,
        in_specs=placed,
        out_specs=(
            P("ctx", "tp", None),
            P("ctx", "tp", None),
            P(),
            P(None, "tp"),
            P(None, "tp"),
            P(None, "tp"),
            P("tp", None),
            P(),
            P(None, "tp"),
            P(None, "tp"),
            P("tp", None),
        ),
        check_vma=False,
    )
```

```python
import functools
import math

import jax
import jax.numpy as jnp
from jax import lax
from jax.experimental import pallas as pl
from jax.experimental.pallas import tpu as pltpu
from jax.sharding import PartitionSpec as P

HD = 128
BLOCK = 128
PAIR = 2 * BLOCK
EPS = 1e-05
THETA = 10000.0
LOG2E = 1.4426950408889634
BF = jnp.bfloat16
F32 = jnp.float32
VMEM_LIMIT = 60 * 1024 * 1024

X_SWAP = [(i, i ^ 1) for i in range(4)]
Y_SWAP = [(i, i ^ 2) for i in range(4)]


def dot(left, right):
    return jnp.dot(left, right, preferred_element_type=F32)


def contract_rows(left, right):
    return lax.dot_general(left, right, (((0,), (0,)), ((), ())), preferred_element_type=F32)


def times_transposed(left, right):
    return lax.dot_general(left, right, (((1,), (1,)), ((), ())), preferred_element_type=F32)


def send_x(values):
    return lax.ppermute(values, "tp", X_SWAP)


def send_y(values):
    return lax.ppermute(values, "tp", Y_SWAP)


def by_four():
    return lax.axis_size("tp") == 4


def gather_first(own):
    if not by_four():
        return (lax.all_gather(own, "tp", axis=0, tiled=True),)
    return own, send_x(own), send_y(own)


def gather_second(held):
    if len(held) == 1:
        return held
    own, from_x, from_y = held
    half = own.shape[0] // 2
    return own, from_x, from_y, send_x(from_y[:half]), send_y(from_x[half:])


def gathered(held):
    return jnp.concatenate(held) if len(held) > 1 else held[0]


def scatter_parts(partial):
    if not by_four():
        return (partial,)
    rows = partial.shape[0] // 4
    half = rows // 2
    at = lambda first: partial[first * half : (first + 1) * half]
    return (
        jnp.concatenate([at(2), at(6)]),
        jnp.concatenate([at(5), at(7)]),
        jnp.concatenate([at(0), at(1), at(4), at(3)]),
    )


def scatter_first(parts):
    if len(parts) == 1:
        return (lax.psum_scatter(parts[0], "tp", scatter_dimension=0, tiled=True),)
    return send_x(parts[0]), send_y(parts[1]), parts[2]


def add_low(left, right):
    return (left.astype(F32) + right.astype(F32)).astype(BF)


def scatter_second(held):
    if len(held) == 1:
        return held
    from_x, from_y, stay = held
    half = from_x.shape[0] // 2
    low_rest = send_y(add_low(stay[2 * half : 3 * half], from_x[half:]))
    high_rest = send_x(add_low(stay[3 * half :], from_y[half:]))
    return from_x, from_y, stay, low_rest, high_rest


def scattered(held):
    if len(held) == 1:
        return held[0].astype(F32)
    from_x, from_y, stay, low_rest, high_rest = (part.astype(F32) for part in held)
    half = low_rest.shape[0]
    low = stay[:half] + from_x[:half] + low_rest
    high = stay[half : 2 * half] + from_y[:half] + high_rest
    return jnp.concatenate([low, high])


def exchange(pieces, places, n_ctx):
    got = {}
    for k in places:
        got[k] = pieces[k] if k == 0 else lax.ppermute(pieces[k], "ctx", [(i, i ^ k) for i in range(n_ctx)])
    return got


def params():
    return pltpu.CompilerParams(vmem_limit_bytes=VMEM_LIMIT)


def whole(shape):
    return pl.BlockSpec(shape, lambda *_: (0,) * len(shape))


def put_partial(refs, first, value, rows):
    if len(refs) == 1:
        refs[0][first : first + value.shape[0], :] = value
        return
    to_x, to_y, stay = refs
    half = rows // 2
    homes = {
        0: (stay, 0), 1: (stay, 1), 2: (to_x, 0), 3: (stay, 3), 4: (stay, 2), 5: (to_y, 0), 6: (to_x, 1), 7: (to_y, 1)
    }
    for part in range(value.shape[0] // half):
        ref, place = homes[first // half + part]
        ref[place * half : (place + 1) * half, :] = value[part * half : (part + 1) * half]


def partial_shapes(rows, width, split):
    if not split:
        return [jax.ShapeDtypeStruct((rows, width), BF)]
    return [jax.ShapeDtypeStruct((rows // 4, width), BF)] * 2 + [jax.ShapeDtypeStruct((rows // 2, width), BF)]


def per_device(pairs, n_ctx):
    return -(-pairs // n_ctx)


def halves_at(swap):
    first = pl.multiple_of(swap * BLOCK, BLOCK)
    second = pl.multiple_of((1 - swap) * BLOCK, BLOCK)
    return pl.ds(first, BLOCK), pl.ds(second, BLOCK)


def qkv_kernel(n_ctx, pairs, scalar_ref, n_ref, wq_ref, wk_ref, wv_ref, cos_ref, sin_ref, valid_ref, *rest):
    out_refs, buffer = rest[:n_ctx], rest[n_ctx]
    rows = n_ref[...]
    first, second = halves_at(scalar_ref[1])
    me = scalar_ref[0]
    cos_tab = cos_ref[...]
    sin_tab = sin_ref[...]
    heads = wq_ref.shape[1] // HD
    step = pl.program_id(0)
    per = out_refs[0].shape[0]
    for pair in range(pairs, per * n_ctx):
        buffer[pair] = jnp.zeros(buffer.shape[1:], BF)
    for which, w_ref in enumerate((wq_ref, wk_ref, wv_ref)):
        product = dot(rows, w_ref[...])
        for head in range(heads):
            part = product[:, head * HD : (head + 1) * HD]
            if which < 2:
                part = part * cos_tab + pltpu.roll(part, HD // 2, 1) * sin_tab
            else:
                part = part * valid_ref[...]
            part = part.astype(BF)
            buffer[step * heads + head, which, first, :] = part[:BLOCK]
            buffer[step * heads + head, which, second, :] = part[BLOCK:]

    @pl.when(step == pl.num_programs(0) - 1)
    def _():
        for k in range(n_ctx):
            source = jnp.bitwise_xor(me, k)
            for p in range(per):
                out_refs[k][p] = buffer[source * per + p]


def project_qkv(scalars, normed, wq, wk, wv, cos_tab, sin_tab, valid, n_ctx):
    rows, depth = normed.shape
    width = wq.shape[1]
    heads = width // HD
    steps = rows // PAIR
    per = per_device(steps * heads, n_ctx)
    row_block = pl.BlockSpec((PAIR, HD), lambda i, s: (i, 0))
    weight = whole((depth, width))
    piece = (per, 3, PAIR, HD)
    return pl.pallas_call(
        functools.partial(qkv_kernel, n_ctx, steps * heads),
        out_shape=[jax.ShapeDtypeStruct(piece, BF)] * n_ctx,
        grid_spec=pltpu.PrefetchScalarGridSpec(
            num_scalar_prefetch=1,
            grid=(steps,),
            in_specs=[
                pl.BlockSpec((PAIR, depth), lambda i, s: (i, 0)),
                weight,
                weight,
                weight,
                row_block,
                row_block,
                row_block,
            ],
            out_specs=[whole(piece)] * n_ctx,
            scratch_shapes=[pltpu.VMEM((per * n_ctx, 3, PAIR, HD), BF)],
        ),
        compiler_params=params(),
        cost_estimate=pl.CostEstimate(
            flops=6 * rows * depth * width, bytes_accessed=rows * depth * 2 + 6 * depth * width, transcendentals=0
        ),
    )(scalars, normed, wq, wk, wv, cos_tab, sin_tab, valid)


def out_kernel(n_ctx, pairs, scalar_ref, *refs):
    piece_refs, (w_ref, valid_ref), (heads_ref, *partial_refs), buffer = (
        refs[:n_ctx],
        refs[n_ctx : n_ctx + 2],
        refs[n_ctx + 2 : -1],
        refs[-1],
    )
    me = scalar_ref[0]
    first, second = halves_at(scalar_ref[1])
    per = piece_refs[0].shape[0]
    heads = w_ref.shape[0] // HD
    for k in range(n_ctx):
        source = jnp.bitwise_xor(me, k)
        for p in range(per):
            buffer[source * per + p] = piece_refs[k][p]
    weight = w_ref[...]
    for sequence in range(pairs // heads):
        at = slice(sequence * PAIR, (sequence + 1) * PAIR)
        rows = jnp.concatenate(
            [
                jnp.concatenate(
                    [buffer[sequence * heads + head, first, :], buffer[sequence * heads + head, second, :]], axis=0
                )
                for head in range(heads)
            ],
            axis=1,
        )
        rows = rows * valid_ref[at, :]
        heads_ref[at, :] = rows
        put_partial(partial_refs, sequence * PAIR, dot(rows, weight).astype(BF), pairs // heads * PAIR // 4)


def project_out(scalars, pieces, weight, valid, pairs, n_ctx, split):
    width, depth = weight.shape
    rows = valid.shape[0]
    per = pieces[0].shape[0]
    shapes = [jax.ShapeDtypeStruct((rows, width), BF)] + partial_shapes(rows, depth, split)
    return pl.pallas_call(
        functools.partial(out_kernel, n_ctx, pairs),
        out_shape=shapes,
        grid_spec=pltpu.PrefetchScalarGridSpec(
            num_scalar_prefetch=1,
            grid=(1,),
            in_specs=[whole(piece.shape) for piece in pieces] + [whole(weight.shape), whole(valid.shape)],
            out_specs=[whole(shape.shape) for shape in shapes],
            scratch_shapes=[pltpu.VMEM((per * n_ctx, PAIR, HD), BF)],
        ),
        compiler_params=params(),
        cost_estimate=pl.CostEstimate(
            flops=2 * rows * depth * width, bytes_accessed=rows * depth * 2 + 2 * depth * width, transcendentals=0
        ),
    )(scalars, *pieces, weight, valid)


def heads_back_kernel(n_ctx, scalar_ref, da_ref, w_ref, valid_ref, *rest):
    out_refs, buffer = rest[:n_ctx], rest[n_ctx]
    me = scalar_ref[0]
    first, second = halves_at(scalar_ref[1])
    per = out_refs[0].shape[0]
    heads = w_ref.shape[0] // HD
    weight = w_ref[...]
    for pair in range(da_ref.shape[0] // PAIR * heads, per * n_ctx):
        buffer[pair] = jnp.zeros(buffer.shape[1:], BF)
    for sequence in range(da_ref.shape[0] // PAIR):
        at = slice(sequence * PAIR, (sequence + 1) * PAIR)
        grad = times_transposed(da_ref[at, :], weight).astype(BF) * valid_ref[at, :]
        for head in range(heads):
            part = grad[:, head * HD : (head + 1) * HD]
            buffer[sequence * heads + head, first, :] = part[:BLOCK]
            buffer[sequence * heads + head, second, :] = part[BLOCK:]
    for k in range(n_ctx):
        source = jnp.bitwise_xor(me, k)
        for p in range(per):
            out_refs[k][p] = buffer[source * per + p]


def heads_back(scalars, da, weight, valid, n_ctx):
    rows, depth = da.shape
    width = weight.shape[0]
    per = per_device(rows // PAIR * (width // HD), n_ctx)
    piece = (per, PAIR, HD)
    return pl.pallas_call(
        functools.partial(heads_back_kernel, n_ctx),
        out_shape=[jax.ShapeDtypeStruct(piece, BF)] * n_ctx,
        grid_spec=pltpu.PrefetchScalarGridSpec(
            num_scalar_prefetch=1,
            grid=(1,),
            in_specs=[whole(da.shape), whole(weight.shape), whole(valid.shape)],
            out_specs=[whole(piece)] * n_ctx,
            scratch_shapes=[pltpu.VMEM((per * n_ctx, PAIR, HD), BF)],
        ),
        compiler_params=params(),
        cost_estimate=pl.CostEstimate(
            flops=2 * rows * depth * width, bytes_accessed=rows * depth * 2 + 2 * depth * width, transcendentals=0
        ),
    )(scalars, da, weight, valid)


def in_kernel(n_ctx, pairs, scalar_ref, *refs):
    piece_refs, weight_refs, valid_ref = refs[:n_ctx], refs[n_ctx : n_ctx + 3], refs[n_ctx + 3]
    grad_refs, partial_refs, buffer = refs[n_ctx + 4 : n_ctx + 7], refs[n_ctx + 7 : -1], refs[-1]
    me = scalar_ref[0]
    first, second = halves_at(scalar_ref[1])
    per = piece_refs[0].shape[0]
    heads = weight_refs[0].shape[1] // HD
    for k in range(n_ctx):
        source = jnp.bitwise_xor(me, k)
        for p in range(per):
            buffer[source * per + p] = piece_refs[k][p]
    for sequence in range(pairs // heads):
        at = slice(sequence * PAIR, (sequence + 1) * PAIR)
        total = None
        for which in range(3):
            rows = jnp.concatenate(
                [
                    jnp.concatenate([buffer[pair, which, first, :], buffer[pair, which, second, :]], axis=0)
                    for pair in range(sequence * heads, (sequence + 1) * heads)
                ],
                axis=1,
            )
            if which == 2:
                rows = rows * valid_ref[at, :]
            grad_refs[which][at, :] = rows
            product = times_transposed(rows, weight_refs[which][...])
            total = product if total is None else total + product
        put_partial(partial_refs, sequence * PAIR, total.astype(BF), pairs // heads * PAIR // 4)


def project_in(scalars, pieces, weights, valid, pairs, n_ctx, split):
    depth, width = weights[0].shape
    rows = valid.shape[0]
    per = pieces[0].shape[0]
    shapes = [jax.ShapeDtypeStruct((rows, width), BF)] * 3 + partial_shapes(rows, depth, split)
    return pl.pallas_call(
        functools.partial(in_kernel, n_ctx, pairs),
        out_shape=shapes,
        grid_spec=pltpu.PrefetchScalarGridSpec(
            num_scalar_prefetch=1,
            grid=(1,),
            in_specs=[whole(piece.shape) for piece in pieces]
            + [whole(weight.shape) for weight in weights]
            + [whole(valid.shape)],
            out_specs=[whole(shape.shape) for shape in shapes],
            scratch_shapes=[pltpu.VMEM((per * n_ctx, 3, PAIR, HD), BF)],
        ),
        compiler_params=params(),
        cost_estimate=pl.CostEstimate(
            flops=6 * rows * depth * width, bytes_accessed=rows * depth * 2 + 6 * depth * width, transcendentals=0
        ),
    )(scalars, *pieces, *weights, valid)


def both_places(me, k, n_ctx):
    source = jnp.bitwise_xor(me, k)
    front = pl.multiple_of(source * BLOCK, BLOCK)
    back = pl.multiple_of((2 * n_ctx - 1 - source) * BLOCK, BLOCK)
    return pl.ds(front, BLOCK), pl.ds(back, BLOCK)


def attention_kernel(n_ctx, tile, scalar_ref, *refs):
    x_refs, o_refs, (qs, ks, vs, os) = refs[:n_ctx], refs[n_ctx : 2 * n_ctx], refs[2 * n_ctx :]
    me = scalar_ref[0]
    length = 2 * n_ctx * BLOCK
    for k in range(n_ctx):
        front, back = both_places(me, k, n_ctx)
        for which, dest in enumerate((qs, ks, vs)):
            dest[front, :] = x_refs[k][0, which, :BLOCK, :]
            dest[back, :] = x_refs[k][0, which, BLOCK:, :]
    factor = -(HD ** (-0.5)) * LOG2E
    shift = math.log(length) * LOG2E
    row_at = lax.broadcasted_iota(jnp.int32, (tile, tile), 0)
    col_at = lax.broadcasted_iota(jnp.int32, (tile, tile), 1)
    for i in range(length // tile):
        query = qs[i * tile : (i + 1) * tile, :]

        def part(j, masked):
            at = pl.ds(pl.multiple_of(j * tile, tile), tile)
            raw = times_transposed(query, ks[at, :])
            prob = 1.0 / (1.0 + jnp.exp2(raw * factor + shift))
            if masked:
                prob = jnp.where(row_at >= col_at, prob, 0.0)
            return dot(prob.astype(BF), vs[at, :])

        total = part(i, True)
        if i > 0:
            total = lax.fori_loop(0, i, lambda j, acc: acc + part(j, False), total)
        os[i * tile : (i + 1) * tile, :] = total.astype(BF)
    for k in range(n_ctx):
        front, back = both_places(me, k, n_ctx)
        o_refs[k][0, :BLOCK, :] = os[front, :]
        o_refs[k][0, BLOCK:, :] = os[back, :]


def attention_forward(scalars, pieces, n_ctx):
    pairs = pieces[0].shape[0]
    length = 2 * n_ctx * BLOCK
    tile = min(512, length)
    return pl.pallas_call(
        functools.partial(attention_kernel, n_ctx, tile),
        out_shape=[jax.ShapeDtypeStruct((pairs, PAIR, HD), BF)] * n_ctx,
        grid_spec=pltpu.PrefetchScalarGridSpec(
            num_scalar_prefetch=1,
            grid=(pairs,),
            in_specs=[pl.BlockSpec((1, 3, PAIR, HD), lambda i, s: (i, 0, 0, 0))] * n_ctx,
            out_specs=[pl.BlockSpec((1, PAIR, HD), lambda i, s: (i, 0, 0))] * n_ctx,
            scratch_shapes=[pltpu.VMEM((length, HD), BF)] * 4,
        ),
        compiler_params=params(),
        cost_estimate=pl.CostEstimate(
            flops=pairs * length * length * HD * 6,
            bytes_accessed=pairs * length * HD * 8,
            transcendentals=pairs * length * length,
        ),
    )(scalars, *pieces)


def attention_back_kernel(n_ctx, tile, scalar_ref, *refs):
    x_refs, g_refs, (cos_ref, sin_ref) = refs[:n_ctx], refs[n_ctx : 2 * n_ctx], refs[2 * n_ctx : 2 * n_ctx + 2]
    out_refs = refs[2 * n_ctx + 2 : 3 * n_ctx + 2]
    qs, ks, vs, gs, os, dqs = refs[3 * n_ctx + 2 :]
    me = scalar_ref[0]
    length = 2 * n_ctx * BLOCK
    for k in range(n_ctx):
        front, back = both_places(me, k, n_ctx)
        for which, dest in enumerate((qs, ks, vs)):
            dest[front, :] = x_refs[k][0, which, :BLOCK, :]
            dest[back, :] = x_refs[k][0, which, BLOCK:, :]
        gs[front, :] = g_refs[k][0, :BLOCK, :]
        gs[back, :] = g_refs[k][0, BLOCK:, :]
    scale = HD ** (-0.5)
    factor = -scale * LOG2E
    shift = math.log(length) * LOG2E
    count = length // tile
    key_at = lax.broadcasted_iota(jnp.int32, (tile, tile), 0)
    query_at = lax.broadcasted_iota(jnp.int32, (tile, tile), 1)
    dqs[...] = jnp.zeros_like(dqs)

    def unrotate(values, at):
        return (values * cos_ref[at, :] - pltpu.roll(values, HD // 2, 1) * sin_ref[at, :]).astype(BF)

    for j in range(count):
        own = slice(j * tile, (j + 1) * tile)
        keys = ks[own, :]
        values = vs[own, :]

        def part(i, masked):
            at = pl.ds(pl.multiple_of(i * tile, tile), tile)
            query = qs[at, :]
            grad = gs[at, :]
            raw = times_transposed(keys, query)
            prob = 1.0 / (1.0 + jnp.exp2(raw * factor + shift))
            if masked:
                prob = jnp.where(query_at >= key_at, prob, 0.0)
            prob_grad = times_transposed(values, grad)
            score_grad = (prob_grad * prob * (1.0 - prob)).astype(BF)
            dqs[at, :] += contract_rows(score_grad, keys)
            return dot(score_grad, query), dot(prob.astype(BF), grad)

        total = part(j, True)
        if j + 1 < count:

            def step(i, acc):
                more = part(i, False)
                return acc[0] + more[0], acc[1] + more[1]

            total = lax.fori_loop(j + 1, count, step, total)
        os[1, own, :] = unrotate(total[0] * scale, own)
        os[2, own, :] = total[1].astype(BF)
    for i in range(count):
        at = slice(i * tile, (i + 1) * tile)
        os[0, at, :] = unrotate(dqs[at, :] * scale, at)
    for k in range(n_ctx):
        front, back = both_places(me, k, n_ctx)
        for which in range(3):
            out_refs[k][0, which, :BLOCK, :] = os[which, front, :]
            out_refs[k][0, which, BLOCK:, :] = os[which, back, :]


def attention_backward(scalars, pieces, grads, cos_tab, sin_tab, n_ctx):
    pairs = pieces[0].shape[0]
    length = 2 * n_ctx * BLOCK
    tile = min(512, length)
    three = pl.BlockSpec((1, 3, PAIR, HD), lambda i, s: (i, 0, 0, 0))
    one = pl.BlockSpec((1, PAIR, HD), lambda i, s: (i, 0, 0))
    return pl.pallas_call(
        functools.partial(attention_back_kernel, n_ctx, tile),
        out_shape=[jax.ShapeDtypeStruct((pairs, 3, PAIR, HD), BF)] * n_ctx,
        grid_spec=pltpu.PrefetchScalarGridSpec(
            num_scalar_prefetch=1,
            grid=(pairs,),
            in_specs=[three] * n_ctx + [one] * n_ctx + [whole((length, HD))] * 2,
            out_specs=[three] * n_ctx,
            scratch_shapes=[pltpu.VMEM((length, HD), BF)] * 4
            + [pltpu.VMEM((3, length, HD), BF), pltpu.VMEM((length, HD), F32)],
        ),
        compiler_params=params(),
        cost_estimate=pl.CostEstimate(
            flops=pairs * length * length * HD * 12,
            bytes_accessed=pairs * length * HD * 14,
            transcendentals=pairs * length * length,
        ),
    )(scalars, *pieces, *grads, cos_tab, sin_tab)


def mlp_kernel(n_ref, g_ref, wg_ref, wu_ref, wd_ref, *rest):
    h_ref, dgp_ref, dup_ref = rest[-3:]
    rows = n_ref[...]
    gate_pre = dot(rows, wg_ref[...])
    up_pre = dot(rows, wu_ref[...])
    hidden_grad = times_transposed(g_ref[...], wd_ref[...])
    h_ref[...], dgp_ref[...], dup_ref[...] = feed_values(gate_pre, up_pre, hidden_grad)


def mlp_core(normed, grads, wg, wu, wd, total, first, held=()):
    rows, depth = normed.shape
    hidden = wg.shape[1]
    row_tile, tile = 512, 512
    skip = first // row_tile
    row_block = pl.BlockSpec((row_tile, depth), lambda j, i: (i, 0))
    out_block = pl.BlockSpec((row_tile, tile), lambda j, i: (i + skip, j))
    out = jax.ShapeDtypeStruct((total, hidden), BF)
    return pl.pallas_call(
        mlp_kernel,
        out_shape=(out, out, out),
        grid=(hidden // tile, rows // row_tile),
        in_specs=[
            row_block,
            row_block,
            pl.BlockSpec((depth, tile), lambda j, i: (0, j)),
            pl.BlockSpec((depth, tile), lambda j, i: (0, j)),
            pl.BlockSpec((tile, depth), lambda j, i: (j, 0)),
        ]
        + [pl.BlockSpec(memory_space=pl.ANY)] * len(held),
        out_specs=(out_block, out_block, out_block),
        input_output_aliases={5 + k: k for k in range(len(held))},
        compiler_params=params(),
        cost_estimate=pl.CostEstimate(
            flops=6 * rows * depth * hidden,
            bytes_accessed=rows * depth * 4 + 6 * depth * hidden + 6 * rows * hidden,
            transcendentals=rows * hidden,
        ),
    )(normed, grads, wg, wu, wd, *held)


def inverse_rms(values):
    return lax.rsqrt(jnp.mean(values * values, axis=-1, keepdims=True) + EPS)


def neighbours():
    index, rank = lax.axis_index("ctx"), lax.axis_index("tp")
    return (index, jnp.bitwise_xor(rank, 1)), (index, jnp.bitwise_xor(rank, 2))


def remote(source, dest, send_sem, recv_sem, device):
    return pltpu.make_async_remote_copy(
        src_ref=source,
        dst_ref=dest,
        send_sem=send_sem,
        recv_sem=recv_sem,
        device_id=device,
        device_id_type=pl.DeviceIdType.MESH,
    )


def signal(sem, device):
    pl.semaphore_signal(sem, inc=1, device_id=device, device_id_type=pl.DeviceIdType.MESH)


class Scatter:
    def __init__(self, partial, groups, bufs, sems, loaded=True):
        self.partial, self.groups, self.loaded = partial, groups, loaded
        self.from_x, self.from_y, self.for_y, self.for_x, self.low, self.high = bufs[:6]
        if loaded:
            self.stay, self.stay_y, self.stay_x = bufs[6:]
        self.first_send, self.first_recv, self.second_send, self.second_recv, self.load_sem = sems
        self.to_x, self.to_y = neighbours()

    @staticmethod
    def scratch(rows, width, loaded=True):
        dma = pltpu.SemaphoreType.DMA
        whole_rows, half_rows = pltpu.VMEM((rows, width), BF), pltpu.VMEM((rows // 2, width), BF)
        bufs = [whole_rows] * 2 + [half_rows] * 4 + ([whole_rows] + [half_rows] * 2 if loaded else [])
        return bufs + [dma((8,)), dma((8,)), dma((4,)), dma((4,)), dma((6,))]

    def piece(self, g, number):
        base, rows, own = self.groups[g]
        half = rows // 2
        if not self.loaded:
            return self.partial[pl.ds(base + number * half, half), :]
        if number < 2:
            return self.stay[pl.ds(own + number * half, half), :]
        return (self.stay_x if number == 3 else self.stay_y)[pl.ds(own // 2, half), :]

    def first_copies(self, g):
        base, rows, own = self.groups[g]
        half = rows // 2
        part = lambda number: self.partial.at[pl.ds(base + number * half, half)]
        at = lambda buf, number: buf.at[pl.ds(own + number * half, half)]
        plan = [
            (part(2), at(self.from_x, 0), self.to_x),
            (part(6), at(self.from_x, 1), self.to_x),
            (part(5), at(self.from_y, 0), self.to_y),
            (part(7), at(self.from_y, 1), self.to_y),
        ]
        return [
            remote(source, dest, self.first_send.at[4 * g + k], self.first_recv.at[4 * g + k], device)
            for k, (source, dest, device) in enumerate(plan)
        ]

    def loads(self, g):
        base, rows, own = self.groups[g]
        half = rows // 2
        copy = lambda number, count, dest, k: pltpu.make_async_copy(
            self.partial.at[pl.ds(base + number * half, count)], dest, self.load_sem.at[3 * g + k]
        )
        return [
            copy(0, rows, self.stay.at[pl.ds(own, rows)], 0),
            copy(4, half, self.stay_y.at[pl.ds(own // 2, half)], 1),
            copy(3, half, self.stay_x.at[pl.ds(own // 2, half)], 2),
        ]

    def second_copies(self, g):
        _, rows, own = self.groups[g]
        at = pl.ds(own // 2, rows // 2)
        return [
            remote(self.for_y.at[at], self.low.at[at], self.second_send.at[2 * g], self.second_recv.at[2 * g], self.to_y),
            remote(
                self.for_x.at[at], self.high.at[at], self.second_send.at[2 * g + 1], self.second_recv.at[2 * g + 1], self.to_x
            ),
        ]

    def start(self, g, which=(1, 3, 0, 2), loads=True):
        copies = self.first_copies(g)
        for k in which:
            copies[k].start()
        if loads:
            for copy in self.loads(g):
                copy.start()

    def forward(self, g):
        _, rows, own = self.groups[g]
        half = rows // 2
        copies = self.first_copies(g)
        copies[1].wait_recv()
        copies[3].wait_recv()
        if self.loaded:
            for copy in self.loads(g):
                copy.wait()
        at = pl.ds(own // 2, half)
        self.for_y[at, :] = add_low(self.piece(g, 4), self.from_x[pl.ds(own + half, half), :])
        self.for_x[at, :] = add_low(self.piece(g, 3), self.from_y[pl.ds(own + half, half), :])
        for copy in self.second_copies(g):
            copy.start()

    def total(self, g, use):
        _, rows, own = self.groups[g]
        half = rows // 2
        copies, seconds = self.first_copies(g), self.second_copies(g)
        copies[0].wait_recv()
        copies[2].wait_recv()
        for copy in copies:
            copy.wait_send()
        for copy in seconds:
            copy.wait()
        first = pl.ds(own, half)
        rest = pl.ds(own // 2, half)
        for side, (got, more) in enumerate(((self.from_x, self.low), (self.from_y, self.high))):
            at = pl.ds(own + side * half, half)
            use(at, self.piece(g, side).astype(F32) + got[first, :].astype(F32) + more[rest, :].astype(F32))


class Gather:
    def __init__(self, own, out, groups, sems, own_at=None, local=True):
        self.own, self.out, self.groups, self.has_local = own, out, groups, local
        self.own_at = own_at if own_at is not None else [group[2] for group in groups]
        self.first_send, self.first_recv, self.second_send, self.second_recv, self.local_sem = sems
        self.to_x, self.to_y = neighbours()

    @staticmethod
    def scratch():
        dma = pltpu.SemaphoreType.DMA
        return [dma((4,)), dma((4,)), dma((4,)), dma((4,)), dma((2,))]

    def first_copies(self, g):
        base, rows, _ = self.groups[g]
        source = self.own.at[pl.ds(self.own_at[g], rows)]
        place = lambda k: self.out.at[pl.ds(base + k * rows, rows)]
        return [
            remote(source, place(1), self.first_send.at[2 * g], self.first_recv.at[2 * g], self.to_x),
            remote(source, place(2), self.first_send.at[2 * g + 1], self.first_recv.at[2 * g + 1], self.to_y),
        ]

    def local(self, g):
        base, rows, _ = self.groups[g]
        return pltpu.make_async_copy(self.own.at[pl.ds(self.own_at[g], rows)], self.out.at[pl.ds(base, rows)], self.local_sem.at[g])

    def second_copies(self, g):
        base, rows, _ = self.groups[g]
        half = rows // 2
        part = lambda number: self.out.at[pl.ds(base + number * half, half)]
        return [
            remote(part(4), part(6), self.second_send.at[2 * g], self.second_recv.at[2 * g], self.to_x),
            remote(part(3), part(7), self.second_send.at[2 * g + 1], self.second_recv.at[2 * g + 1], self.to_y),
        ]

    def start(self, g):
        for copy in self.first_copies(g):
            copy.start()
        if self.has_local:
            self.local(g).start()

    def forward_x(self, g):
        self.first_copies(g)[0].wait_recv()
        self.second_copies(g)[1].start()

    def forward_y(self, g):
        self.first_copies(g)[1].wait_recv()
        self.second_copies(g)[0].start()

    def forward(self, g):
        self.forward_x(g)
        self.forward_y(g)
        if self.has_local:
            self.local(g).wait()

    def finish(self, g):
        for copy in self.second_copies(g):
            copy.wait_recv()

    def sent(self, g):
        for copy in self.first_copies(g) + self.second_copies(g):
            copy.wait_send()


TILE, ROWS = 128, 64
CORE_SLOTS, HOP_SLOTS = 4, 4


class Ring:
    def __init__(self, slots, send_sem, recv_sem, credit, total):
        self.slots, self.send_sem, self.recv_sem, self.credit, self.total = slots, send_sem, recv_sem, credit, total
        self.count = slots.shape[0]

    def copy(self, source, at, send_at, device):
        slot = lax.rem(at, self.count)
        return pltpu.make_async_remote_copy(
            src_ref=source,
            dst_ref=self.slots.at[slot],
            send_sem=self.send_sem.at[send_at],
            recv_sem=self.recv_sem.at[slot],
            device_id=device,
            device_id_type=pl.DeviceIdType.MESH,
        )

    def send(self, source, at, send_at, device):
        @pl.when(at >= self.count)
        def _():
            pl.semaphore_wait(self.credit, 1)

        self.copy(source, at, send_at, device).start()

    def sent(self, source, at, send_at, device):
        self.copy(source, at, send_at, device).wait_send()

    def arrived(self, source, at, send_at, device):
        self.copy(source, at, send_at, device).wait_recv()
        return self.slots.at[lax.rem(at, self.count)]

    def free(self, at, device):
        @pl.when(at + self.count < self.total)
        def _():
            pl.semaphore_signal(self.credit, inc=1, device_id=device, device_id_type=pl.DeviceIdType.MESH)


def sums_kernel(n_ctx, items, n_right, n_extra, tasks, late, *refs):
    n_left = len(items)
    made = items[0][3]
    n_held = n_left - (1 if made else 0)
    left_refs, right_refs = refs[:n_held], refs[n_held : n_held + n_right]
    left_refs = ((None,) if made else ()) + tuple(left_refs)
    refs = refs[n_held + n_right :]
    extra_in, refs = refs[: n_extra[0]], refs[n_extra[0] :]
    out_refs, extra_out, refs = refs[:n_left], refs[n_left : n_left + n_extra[1]], refs[n_left + n_extra[1] :]
    extra_scratch, refs = refs[: n_extra[2]], refs[n_extra[2] :]
    right_refs = list(right_refs) + [extra_out[k] for k in late]
    n_right += len(late)
    (
        left_buf, right_buf, other_buf, ring, core_in, hop_in, hop_mid, hop_out, core_out,
        left_sem, right_sem, core_send, core_recv, in_send, in_recv, mid_send, mid_recv, out_send, out_recv,
        fin_send, fin_recv, store_sem, core_credit, in_credit, mid_credit, out_credit, fin_credit,
    ) = refs
    starts = [0]
    for _, _, chunks, _ in items:
        starts.append(starts[-1] + chunks)
    total = starts[-1]
    n_ring = ring.shape[0]
    chips = n_ctx // 2
    mid = chips // 2
    index = lax.axis_index("ctx")
    rank = lax.axis_index("tp")
    core = lax.rem(index, 2)
    chip = index // 2
    low_side = chip < mid
    place = jnp.where(low_side, chip, chips - 1 - chip)
    toward = jnp.where(low_side, 1, -1)
    partner = (chip * 2 + 1 - core, rank)
    after = ((chip + toward) * 2 + core, rank)
    before = ((chip - toward) * 2 + core, rank)
    is_first = place == 0
    is_last = place == mid - 1
    lag_t = mid
    lag_u = lag_t + 2
    lag_o = lag_u + 2 * (mid - 1)
    lag_f = lag_o + 1
    lag_w = lag_f + 1

    to_core = Ring(core_in, core_send, core_recv, core_credit, total)
    to_after = Ring(hop_in, in_send, in_recv, in_credit, total)
    across = Ring(hop_mid, mid_send, mid_recv, mid_credit, total)
    to_before = Ring(hop_out, out_send, out_recv, out_credit, total)
    to_final = Ring(core_out, fin_send, fin_recv, fin_credit, total)

    def right_copy(k):
        return pltpu.make_async_copy(right_refs[k], right_buf.at[k % 2], right_sem.at[k % 2])

    right_copy(0).start()

    def for_item(at, action):
        for number in range(n_left):
            @pl.when((at >= starts[number]) & (at < starts[number + 1]))
            def _(number=number):
                action(number, at - starts[number])

    def rows_at(number, chunk, side):
        half = items[number][2] * ROWS
        return pl.multiple_of(side * half + chunk * ROWS, ROWS)

    def left_copy(number, chunk, slot, which):
        side = core if which == 0 else 1 - core
        half = items[number][2] * ROWS
        return pltpu.make_async_copy(
            left_refs[number].at[:, pl.ds(pl.multiple_of(side * half + chunk // 2 * TILE, TILE), TILE)],
            left_buf.at[slot, :, pl.ds(which * TILE, TILE)],
            left_sem.at[slot, which],
        )

    def load_left(at):
        def action(number, chunk):
            if number == 0 and made:
                maker.load(chunk // 2)
                return
            if number == 1 and made:

                @pl.when(chunk == 0)
                def _():
                    maker.release()

            for which in range(2):
                left_copy(number, chunk, lax.rem(at // 2, 2), which).start()

        for_item(at, action)

    planned, each, maker = tasks(extra_in, extra_out, extra_scratch) if tasks is not None else ({}, None, None)
    if made:
        maker.begin(left_buf, right_buf)
    load_left(0)
    if n_right > 1 and not made:
        right_copy(1).start()
    if tasks is not None:
        greet(n_ctx, True)
    else:
        barrier = pltpu.get_barrier_semaphore()
        pl.semaphore_signal(barrier, inc=1, device_id=partner, device_id_type=pl.DeviceIdType.MESH)

        @pl.when(chip > 0)
        def _():
            pl.semaphore_signal(
                barrier, inc=1, device_id=((chip - 1) * 2 + core, rank), device_id_type=pl.DeviceIdType.MESH
            )

        @pl.when(chip < chips - 1)
        def _():
            pl.semaphore_signal(
                barrier, inc=1, device_id=((chip + 1) * 2 + core, rank), device_id_type=pl.DeviceIdType.MESH
            )

        pl.semaphore_wait(barrier, 1 + jnp.where(chip > 0, 1, 0) + jnp.where(chip < chips - 1, 1, 0))
    if 0 in planned:
        planned.pop(0)()
    right_copy(0).wait()

    def step(i, carry):
        def at_lag(lag):
            at = i - lag
            return at, (at >= 0) & (at < total)

        at, now = at_lag(lag_w)

        @pl.when(now)
        def _():
            slot = lax.rem(at, n_ring)
            source = ring.at[slot]

            def action(number, chunk):
                store(number, chunk, at, 0).wait()
                store(number, chunk, at, 1).wait()

            for_item(at, action)
            to_final.sent(source, at, slot, partner)
            to_final.free(at, partner)

            @pl.when(jnp.logical_not(is_first))
            def _():
                to_before.sent(source, at, slot, before)

        at, now = at_lag(lag_o)

        @pl.when(now & jnp.logical_not(is_last))
        def _():
            slot = lax.rem(at, n_ring)
            source = ring.at[slot]
            to_after.sent(source, at, slot, after)
            got = to_before.arrived(source, at, slot, after)
            ring[slot] = got[...]
            to_before.free(at, after)

            @pl.when(jnp.logical_not(is_first))
            def _():
                to_before.send(source, at, slot, before)

        @pl.when(now)
        def _():
            slot = lax.rem(at, n_ring)
            to_final.send(ring.at[slot], at, slot, partner)

        at, now = at_lag(lag_u)

        @pl.when(now & is_last)
        def _():
            slot = lax.rem(at, n_ring)
            source = ring.at[slot]
            across.sent(source, at, slot, after)
            got = across.arrived(source, at, slot, after)
            ring[slot] = add_low(ring[slot], got[...])
            across.free(at, after)

            @pl.when(jnp.logical_not(is_first))
            def _():
                to_before.send(source, at, slot, before)

        at, now = at_lag(lag_t)

        @pl.when(now)
        def _():
            slot = lax.rem(at, n_ring)
            source = ring.at[slot]

            @pl.when(jnp.logical_not(is_first))
            def _():
                got = to_after.arrived(source, at, slot, before)
                ring[slot] = add_low(ring[slot], got[...])
                to_after.free(at, before)

            @pl.when(is_last)
            def _():
                across.send(source, at, slot, after)

            @pl.when(jnp.logical_not(is_first) & jnp.logical_not(is_last))
            def _():
                to_after.send(source, at, slot, after)

        at, now = at_lag(1)

        @pl.when(now)
        def _():
            slot = lax.rem(at, n_ring)
            source = ring.at[slot]
            own = other_buf.at[lax.rem(at, 4)]
            to_core.sent(own, at, lax.rem(at, 4), partner)
            got = to_core.arrived(own, at, lax.rem(at, 4), partner)
            ring[slot] = add_low(ring[slot], got[...])
            to_core.free(at, partner)

            @pl.when(is_first & jnp.logical_not(is_last))
            def _():
                to_after.send(source, at, slot, after)

        at, now = at_lag(lag_f)

        @pl.when(now)
        def _():
            slot = lax.rem(at, n_ring)
            to_final.arrived(ring.at[slot], at, slot, partner)

            def action(number, chunk):
                store(number, chunk, at, 0).start()
                store(number, chunk, at, 1).start()

            for_item(at, action)

        for when, task in planned.items():
            pl.when(i == when)(task)

        if each is not None:
            each(i)

        @pl.when((i + 2 < total) & (lax.rem(i, 2) == 0))
        def _():
            load_left(i + 2)

        @pl.when((i < total) & (lax.rem(i, 2) == 0))
        def _():
            slot = lax.rem(i // 2, 2)

            def action(number, chunk):
                which_right = items[number][1]
                if which_right > 0 and items[number - 1][1] != which_right:

                    @pl.when(chunk == 0)
                    def _():
                        if made and which_right in (1, n_right - 1):
                            right_copy(which_right).start()
                        right_copy(which_right).wait()

                if which_right > 0 and which_right + 1 < n_right - (1 if made else 0):

                    @pl.when(chunk == items[number][2] // 2)
                    def _():
                        right_copy(which_right + 1).start()

                if number == 0 and made:
                    maker.make(chunk // 2)
                else:
                    for which in range(2):
                        left_copy(number, chunk, slot, which).wait()
                right = right_buf.at[which_right % 2]
                product = contract_rows(left_buf[slot], right[...]).astype(BF)
                for part in range(2):
                    place = lax.rem(i + part, 4)
                    other_buf[place] = product[TILE + part * ROWS : TILE + (part + 1) * ROWS]
                    to_core.send(other_buf.at[place], i + part, place, partner)
                    ring[lax.rem(i + part, n_ring)] = product[part * ROWS : (part + 1) * ROWS]

            for_item(i, action)

        return carry

    def store(number, chunk, at, which):
        source = ring.at[lax.rem(at, n_ring)] if which == 0 else core_out.at[lax.rem(at, CORE_SLOTS)]
        side = core if which == 0 else 1 - core
        return pltpu.make_async_copy(
            source,
            out_refs[number].at[pl.ds(rows_at(number, chunk, side), ROWS), :],
            store_sem.at[which, lax.rem(at, 2)],
        )

    lax.fori_loop(0, total + lag_w, step, 0)


def weight_sums(items, rights, n_ctx, collective_id, extra=None, late=(), limit=VMEM_LIMIT):
    tokens, width = rights[0].shape
    columns = [left if isinstance(left, int) else left.shape[1] for left, _ in items]
    held = [left for left, _ in items if not isinstance(left, int)]
    shapes = [
        (k, right, columns[k] // 2 // ROWS, isinstance(left, int)) for k, (left, right) in enumerate(items)
    ]
    mid = n_ctx // 4
    n_ring = mid + 2 + 2 * (mid - 1) + 4
    any_spec = pl.BlockSpec(memory_space=pl.ANY)
    args, arg_specs, outs, out_specs, scratch, tasks = extra if extra is not None else ([], [], [], [], [], None)
    counts = (len(args), len(outs), len(scratch))
    chunk = (ROWS, width)
    dma = pltpu.SemaphoreType.DMA
    return pl.pallas_call(
        functools.partial(sums_kernel, n_ctx, shapes, len(rights), counts, tasks, late),
        out_shape=[jax.ShapeDtypeStruct((count, width), BF) for count in columns] + outs,
        in_specs=[any_spec] * (len(held) + len(rights)) + arg_specs,
        out_specs=[any_spec] * len(items) + out_specs,
        scratch_shapes=scratch
        + [
            pltpu.VMEM((2, tokens, 2 * TILE), BF),
            pltpu.VMEM((min(2, len(rights) + len(late)), tokens, width), BF),
            pltpu.VMEM((4,) + chunk, BF),
            pltpu.VMEM((n_ring,) + chunk, BF),
            pltpu.VMEM((CORE_SLOTS,) + chunk, BF),
            pltpu.VMEM((HOP_SLOTS,) + chunk, BF),
            pltpu.VMEM((HOP_SLOTS,) + chunk, BF),
            pltpu.VMEM((HOP_SLOTS,) + chunk, BF),
            pltpu.VMEM((CORE_SLOTS,) + chunk, BF),
            dma((2, 2)),
            dma((2,)),
            dma((4,)),
            dma((CORE_SLOTS,)),
            dma((n_ring,)),
            dma((HOP_SLOTS,)),
            dma((n_ring,)),
            dma((HOP_SLOTS,)),
            dma((n_ring,)),
            dma((HOP_SLOTS,)),
            dma((n_ring,)),
            dma((CORE_SLOTS,)),
            dma((2, 2)),
        ]
        + [pltpu.SemaphoreType.REGULAR] * 5,
        compiler_params=pltpu.CompilerParams(
            vmem_limit_bytes=limit, collective_id=collective_id, has_side_effects=True
        ),
        cost_estimate=pl.CostEstimate(
            flops=sum(2 * count * tokens * width for count in columns),
            bytes_accessed=sum(2 * count * (tokens + width) for count in columns),
            transcendentals=0,
        ),
    )(*held, *rights, *args)


VMEM_SPEC = pl.BlockSpec(memory_space=pltpu.VMEM)
ANY_SPEC = pl.BlockSpec(memory_space=pl.ANY)


def norm_back_rows(values, gain, grad):
    inv = inverse_rms(values)
    unit = values * inv
    scaled = grad * gain
    back = (scaled - unit * jnp.mean(scaled * unit, axis=-1, keepdims=True)) * inv
    return back, jnp.sum(grad * unit, axis=0, keepdims=True)


def own_copies(ref, buf, groups, sem):
    odd = lax.rem(lax.axis_index("tp"), 2)
    starts = [pl.multiple_of(odd * BLOCK, BLOCK), pl.multiple_of((1 - odd) * PAIR, BLOCK)]
    return [
        pltpu.make_async_copy(ref.at[pl.ds(start, rows)], buf.at[pl.ds(own, rows)], sem.at[g])
        for g, (start, (_, rows, own)) in enumerate(zip(starts, groups))
    ]


class Maker:
    def __init__(self, refs, outs, weights, downs, stage, sems):
        self.n2_ref, self.wg_ref, self.wu_ref, self.wd_ref = refs
        self.h_out, self.dgp_out, self.dup_out = outs
        self.weights, self.downs, self.stage = weights, downs, stage
        self.n2_sem, self.weight_sem, self.h_sem, self.grad_sem = sems
        self.core = lax.rem(lax.axis_index("ctx"), 2)
        self.half = self.h_out.shape[1] // 2
        self.tiles = self.half // TILE

    def first(self, tile, which):
        side = self.core if which == 0 else 1 - self.core
        return pl.multiple_of(side * self.half + tile * TILE, TILE)

    def copies(self, tile):
        slot = lax.rem(tile, 2)
        deep = self.weights.shape[1]
        made = []
        for which in range(2):
            at = pl.ds(self.first(tile, which), TILE)
            for kind, ref in enumerate((self.wg_ref, self.wu_ref)):
                to = pl.multiple_of((slot * 2 + kind) * 2 * TILE + which * TILE, TILE)
                for part in range(2):
                    made.append((ref.at[pl.ds(part * deep, deep), at], self.weights.at[part, :, pl.ds(to, TILE)]))
            made.append((self.wd_ref.at[at], self.downs.at[slot, 0, pl.ds(which * TILE, TILE)]))
        return [
            pltpu.make_async_copy(source, dest, self.weight_sem.at[slot, k]) for k, (source, dest) in enumerate(made)
        ]

    def load(self, tile):
        for copy in self.copies(tile):
            copy.start()

    def begin(self, left_buf, right_buf):
        self.left_buf, self.right_buf = left_buf, right_buf
        self.n2_copy().start()

    def n2_copy(self):
        return pltpu.make_async_copy(self.n2_ref, self.right_buf.at[1], self.n2_sem)

    def h_stores(self, tile):
        slot = lax.rem(tile, 2)
        return [
            pltpu.make_async_copy(
                self.left_buf.at[slot, :, pl.ds(which * TILE, TILE)],
                self.h_out.at[:, pl.ds(self.first(tile, which), TILE)],
                self.h_sem.at[slot, which],
            )
            for which in range(2)
        ]

    def grad_stores(self, tile):
        return [
            pltpu.make_async_copy(
                self.stage.at[kind, :, pl.ds(which * TILE, TILE)],
                out.at[:, pl.ds(self.first(tile, which), TILE)],
                self.grad_sem.at[kind, which],
            )
            for kind, out in enumerate((self.dgp_out, self.dup_out))
            for which in range(2)
        ]

    def make(self, tile):
        slot = lax.rem(tile, 2)
        deep = self.weights.shape[1]

        @pl.when(tile == 0)
        def _():
            self.n2_copy().wait()

        @pl.when(tile > 0)
        def _():
            for copy in self.grad_stores(tile - 1):
                copy.wait()

        @pl.when(tile > 1)
        def _():
            for copy in self.h_stores(tile - 2):
                copy.wait()

        for copy in self.copies(tile):
            copy.wait()
        at_gate = pl.ds(pl.multiple_of(slot * 4 * TILE, TILE), 2 * TILE)
        at_up = pl.ds(pl.multiple_of((slot * 4 + 2) * TILE, TILE), 2 * TILE)
        count = 512

        def rows_step(step, carry):
            rows = pl.ds(pl.multiple_of(step * count, count), count)
            low, high = self.right_buf[1, rows, :deep], self.right_buf[1, rows, deep:]
            gate_pre = dot(low, self.weights[0, :, at_gate]) + dot(high, self.weights[1, :, at_gate])
            up_pre = dot(low, self.weights[0, :, at_up]) + dot(high, self.weights[1, :, at_up])
            hidden_grad = times_transposed(self.right_buf[0, rows, :], self.downs[slot, 0])
            h, dgp, dup = feed_values(gate_pre, up_pre, hidden_grad)
            self.left_buf[slot, rows, :] = h
            self.stage[0, rows, :] = dgp
            self.stage[1, rows, :] = dup
            return carry

        lax.fori_loop(0, self.right_buf.shape[1] // count, rows_step, 0)
        for copy in self.h_stores(tile) + self.grad_stores(tile):
            copy.start()

    def release(self):
        for copy in self.h_stores(self.tiles - 2):
            copy.wait()

    def finish(self):
        for copy in self.h_stores(self.tiles - 1) + self.grad_stores(self.tiles - 1):
            copy.wait()


def feed_values(gate_pre, up_pre, hidden_grad):
    gate_sig = 1.0 / (1.0 + jnp.exp2(gate_pre * (-LOG2E)))
    gate_act = gate_pre * gate_sig
    return (
        (gate_act * up_pre).astype(BF),
        (hidden_grad * up_pre * (gate_sig * (1.0 + gate_pre * (1.0 - gate_sig)))).astype(BF),
        (hidden_grad * gate_act).astype(BF),
    )


def feed_tasks(groups, extra_in, extra_out, scratch):
    n2_ref, wg_ref, wu_ref, wd_ref, residual, cot_ref, gain = extra_in
    dr, da_all, gain_grad, d_ref, h_ref, dgp_ref, dup_ref = extra_out
    n = len(Scatter.scratch(16, 128))
    bufs, rest = scratch[:n], scratch[n:]
    weights, lefts, tile_out, weight_sem, left_sem, out_sem = rest[:6]
    grads, stage, own_sem, n2_sem, make_sem, h_sem, grad_sem = rest[6:13]
    da_own = bufs[0]
    scatter = Scatter(d_ref, groups, bufs[:9], bufs[9:])
    gather = Gather(da_own, da_all, groups, rest[13:])
    maker = Maker(
        (n2_ref, wg_ref, wu_ref, wd_ref),
        (h_ref, dgp_ref, dup_ref),
        weights,
        lefts,
        stage,
        (n2_sem, make_sem, h_sem, grad_sem),
    )
    order = list(reversed(range(len(groups))))
    rows, columns = lefts.shape[2], weights.shape[1]
    row_tiles = dgp_ref.shape[0] // rows
    tiles = row_tiles * (d_ref.shape[1] // columns)
    after = maker.half // ROWS
    shift = after + 1

    def weight_copies(part):
        at = pl.ds(pl.multiple_of(part * columns, columns), columns)
        return [
            pltpu.make_async_copy(ref.at[at], weights.at[k], weight_sem.at[k]) for k, ref in enumerate((wg_ref, wu_ref))
        ]

    def left_copies(tile):
        at = pl.ds(pl.multiple_of(lax.rem(tile, row_tiles) * rows, rows), rows)
        slot = lax.rem(tile, 2)
        return [
            pltpu.make_async_copy(ref.at[at], lefts.at[slot, k], left_sem.at[slot, k])
            for k, ref in enumerate((dgp_ref, dup_ref))
        ]

    def out_copy(tile):
        slot = lax.rem(tile, 2)
        return pltpu.make_async_copy(
            tile_out.at[slot],
            d_ref.at[
                pl.ds(pl.multiple_of(lax.rem(tile, row_tiles) * rows, rows), rows),
                pl.ds(pl.multiple_of(tile // row_tiles * columns, columns), columns),
            ],
            out_sem.at[slot],
        )

    def begin():
        gain_grad[...] = jnp.zeros_like(gain_grad)
        for copy in own_copies(cot_ref, grads, groups, own_sem):
            copy.start()

    def whole_hidden():
        maker.finish()
        for copy in weight_copies(0) + left_copies(0):
            copy.start()

    def each(step):
        i = step - shift

        @pl.when((i >= 0) & (i < tiles))
        def _():
            slot = lax.rem(i, 2)

            @pl.when(i + 1 < tiles)
            def _():
                for copy in left_copies(i + 1):
                    copy.start()

            @pl.when(lax.rem(i, row_tiles) == 0)
            def _():
                @pl.when(i > 0)
                def _():
                    for copy in weight_copies(i // row_tiles):
                        copy.start()

                for copy in weight_copies(i // row_tiles):
                    copy.wait()

            for copy in left_copies(i):
                copy.wait()
            total = times_transposed(lefts[slot, 0], weights[0]) + times_transposed(lefts[slot, 1], weights[1])

            @pl.when(i >= 2)
            def _():
                out_copy(i - 2).wait()

            tile_out[slot] = total.astype(BF)
            out_copy(i).start()

    def start():
        out_copy(tiles - 2).wait()
        out_copy(tiles - 1).wait()
        for copy in own_copies(cot_ref, grads, groups, own_sem):
            copy.wait()
        for g in order:
            scatter.start(g)

    def use(at, total):
        back, more = norm_back_rows(residual[at, :], gain[...].astype(F32), total)
        total_grad = grads[at, :].astype(F32) + back
        dr[at, :] = total_grad
        da_own[at, :] = total_grad.astype(BF)
        gain_grad[...] += more

    def spread(g):
        scatter.total(g, use)
        gather.start(g)

    def finish():
        for g in order:
            gather.finish(g)
            gather.sent(g)

    first = shift + tiles
    plan = {
        0: begin,
        after: whole_hidden,
        first: start,
        first + 3: lambda: scatter.forward(order[0]),
        first + 6: lambda: scatter.forward(order[-1]),
        first + 7: lambda: spread(order[0]),
        first + 9: lambda: spread(order[-1]),
        first + 11: lambda: gather.forward(order[0]),
        first + 15: lambda: gather.forward(order[-1]),
        first + 18: finish,
    }
    return plan, each, maker


def feed_extra(groups, n2, wg, wu, wd, residual, cot, gain):
    rows, width = residual.shape
    tokens, hidden = n2.shape[0], wg.shape[1]
    dma = pltpu.SemaphoreType.DMA
    outs = [
        jax.ShapeDtypeStruct((rows, width), F32),
        jax.ShapeDtypeStruct((tokens, width), BF),
        jax.ShapeDtypeStruct((1, width), F32),
        jax.ShapeDtypeStruct((tokens, width), BF),
    ] + [jax.ShapeDtypeStruct((tokens, hidden), BF)] * 3
    scratch = (
        Scatter.scratch(rows, width)
        + [
            pltpu.VMEM((2, width // 2, hidden), BF),
            pltpu.VMEM((2, 2, PAIR, hidden), BF),
            pltpu.VMEM((2, PAIR, width // 2), BF),
            dma((2,)),
            dma((2, 2)),
            dma((2,)),
            pltpu.VMEM((rows, width), BF),
            pltpu.VMEM((2, tokens, 2 * TILE), BF),
            dma((2,)),
            dma,
            dma((2, 10)),
            dma((2, 2)),
            dma((2, 2)),
        ]
        + Gather.scratch()
    )
    return (
        [n2, wg, wu, wd, residual, cot, gain],
        [ANY_SPEC] * 4 + [VMEM_SPEC, ANY_SPEC, VMEM_SPEC],
        outs,
        [VMEM_SPEC, ANY_SPEC, VMEM_SPEC] + [ANY_SPEC] * 4,
        scratch,
        functools.partial(feed_tasks, groups),
    )


def input_tasks(n_ctx, groups, extra_in, extra_out, scratch):
    i_ref, tokens_ref, dr, gain, gain_two_grad = extra_in
    input_grad, gain_sums = extra_out
    n = len(Scatter.scratch(16, 128))
    scatter = Scatter(i_ref, groups, scratch[:9], scratch[9:n])
    gains, got_tp, got_ctx, send_tp, recv_tp, send_ctx, recv_ctx, rows_in, own_sem = scratch[n:]
    order = list(reversed(range(len(groups))))
    me, rank = lax.axis_index("ctx"), lax.axis_index("tp")

    def tp_hop(k):
        return remote(gains.at[k], got_tp.at[k], send_tp.at[k], recv_tp.at[k], neighbours()[k])

    def ctx_hop(k):
        place = gains.at[2]
        return remote(place, got_ctx.at[k], send_ctx.at[k], recv_ctx.at[k], (jnp.bitwise_xor(me, k), rank))

    def begin():
        gains[0] = jnp.zeros(gains.shape[1:], F32)
        gains[0, 8:9, :] = gain_two_grad[...]
        for copy in own_copies(tokens_ref, rows_in, groups, own_sem):
            copy.start()
        for g in order:
            scatter.start(g)

    def forward_first():
        for copy in own_copies(tokens_ref, rows_in, groups, own_sem):
            copy.wait()
        scatter.forward(order[0])

    def use(at, total):
        back, more = norm_back_rows(rows_in[at, :].astype(F32), gain[...].astype(F32), total)
        input_grad[at, :] = (dr[at, :] + back).astype(BF)
        gains[0, 0:1, :] += more

    def rest():
        scatter.total(order[-1], use)
        tp_hop(0).start()

    def second():
        tp_hop(0).wait()
        gains[1] = gains[0] + got_tp[0]
        tp_hop(1).start()

    def third():
        tp_hop(1).wait()
        gains[2] = gains[1] + got_tp[1]
        for k in range(1, n_ctx):
            ctx_hop(k).start()

    def finish():
        for k in range(1, n_ctx):
            ctx_hop(k).wait()
        got_ctx[0] = gains[2]
        total = got_ctx[jnp.bitwise_xor(me, 0)]
        for index in range(1, n_ctx):
            total = total + got_ctx[jnp.bitwise_xor(me, index)]
        gain_sums[...] = total

    return {
        0: begin,
        4: forward_first,
        9: lambda: scatter.forward(order[-1]),
        10: lambda: scatter.total(order[0], use),
        13: rest,
        15: second,
        17: third,
        20: finish,
    }, None, None


def input_extra(n_ctx, groups, i_partial, tokens_in, dr, gain, gain_two_grad):
    rows, width = tokens_in.shape
    dma = pltpu.SemaphoreType.DMA
    outs = [jax.ShapeDtypeStruct((rows, width), BF), jax.ShapeDtypeStruct((16, width), F32)]
    return (
        [i_partial, tokens_in, dr, gain, gain_two_grad],
        [ANY_SPEC] * 2 + [VMEM_SPEC] * 3,
        outs,
        [VMEM_SPEC] * 2,
        Scatter.scratch(rows, width)
        + [
            pltpu.VMEM((3, 16, width), F32),
            pltpu.VMEM((2, 16, width), F32),
            pltpu.VMEM((n_ctx, 16, width), F32),
            dma((2,)),
            dma((2,)),
            dma((n_ctx,)),
            dma((n_ctx,)),
            pltpu.VMEM((rows, width), BF),
            dma((2,)),
        ],
        functools.partial(input_tasks, n_ctx, groups),
    )


def cast_kernel(groups, *refs):
    out_in, gate_in, up_in, down_in, qkv_in = refs[:5]
    n_more = 3 if groups else 0
    more_in, refs = refs[5 : 5 + n_more], refs[5 + n_more :]
    for source, dest in zip((out_in, gate_in, up_in, down_in), refs[:4]):
        dest[...] = source[...].astype(F32)
    width = refs[4].shape[1]
    for k, dest in enumerate(refs[4:7]):
        dest[...] = qkv_in[:, k * width : (k + 1) * width].astype(F32)
    if not groups:
        return
    row_outs, gain_outs, sem = refs[7:9], refs[9:11], refs[11]
    gains = more_in[2]
    gain_outs[0][...] = gains[0:1, :]
    gain_outs[1][...] = gains[8:9, :]
    odd = lax.rem(lax.axis_index("tp"), 2)
    starts = (pl.multiple_of(odd * BLOCK, BLOCK), pl.multiple_of((1 - odd) * PAIR, BLOCK))

    def copies():
        return [
            pltpu.make_async_copy(source.at[pl.ds(own, rows)], dest.at[pl.ds(start, rows)], sem.at[k, g])
            for k, (source, dest) in enumerate(zip(more_in[:2], row_outs))
            for g, (start, (_, rows, own)) in enumerate(zip(starts, groups))
        ]

    @pl.when(pl.program_id(0) == 0)
    def _():
        for copy in copies():
            copy.start()

    @pl.when(pl.program_id(0) == pl.num_programs(0) - 1)
    def _():
        for copy in copies():
            copy.wait()


def cast_sums(sums, groups=(), rows=(), gains=None):
    steps = 16
    block = lambda array: pl.BlockSpec((array.shape[0] // steps, array.shape[1]), lambda i: (i, 0))
    outs = [jax.ShapeDtypeStruct(array.shape, F32) for array in sums[:-1]]
    outs += [jax.ShapeDtypeStruct((sums[-1].shape[0], sums[-1].shape[1] // 3), F32)] * 3
    in_specs, out_specs, scratch = [block(array) for array in sums], [block(array) for array in outs], []
    args = list(sums)
    if groups:
        args += list(rows) + [gains]
        in_specs += [ANY_SPEC, ANY_SPEC, whole(gains.shape)]
        outs += [jax.ShapeDtypeStruct(array.shape, array.dtype) for array in rows]
        outs += [jax.ShapeDtypeStruct((1, gains.shape[1]), F32)] * 2
        out_specs += [ANY_SPEC, ANY_SPEC] + [whole((1, gains.shape[1]))] * 2
        scratch = [pltpu.SemaphoreType.DMA((2, len(groups)))]
    return pl.pallas_call(
        functools.partial(cast_kernel, groups),
        out_shape=outs,
        grid=(steps,),
        in_specs=in_specs,
        out_specs=out_specs,
        scratch_shapes=scratch,
        compiler_params=params(),
        cost_estimate=pl.CostEstimate(
            flops=0, bytes_accessed=sum(6 * array.shape[0] * array.shape[1] for array in sums), transcendentals=0
        ),
    )(*args)


class Exchange:
    def __init__(self, dest, sems, by_device):
        self.dest, self.by_device = dest, by_device
        self.send_sem, self.recv_sem, self.own_sem = sems
        self.n_ctx = dest.shape[1]
        self.me, self.rank = lax.axis_index("ctx"), lax.axis_index("tp")

    @staticmethod
    def scratch(units, n_ctx):
        dma = pltpu.SemaphoreType.DMA
        return [dma((units, n_ctx)), dma((units, n_ctx)), dma((units,))]

    def copy(self, source, unit, k):
        other = jnp.bitwise_xor(self.me, k)
        place = other if self.by_device else k
        return remote(
            source.at[unit, place],
            self.dest.at[unit, k],
            self.send_sem.at[unit, k],
            self.recv_sem.at[unit, k],
            (other, self.rank),
        )

    def own(self, source, unit):
        place = self.me if self.by_device else 0
        return pltpu.make_async_copy(source.at[unit, place], self.dest.at[unit, 0], self.own_sem.at[unit])

    def start(self, source, unit):
        for k in reversed(range(1, self.n_ctx)):
            self.copy(source, unit, k).start()
        self.own(source, unit).start()

    def start_some(self, source, unit, first, count):
        for k in reversed(range(self.n_ctx)):
            other = jnp.bitwise_xor(self.me, k)

            @pl.when((other >= first) & (other < first + count))
            def _(k=k):
                if k == 0:
                    self.own(source, unit).start()
                else:
                    self.copy(source, unit, k).start()

    def arrived(self, source, unit):
        for k in range(1, self.n_ctx):
            self.copy(source, unit, k).wait_recv()
        self.own(source, unit).wait()

    def sent(self, source, unit):
        for k in range(1, self.n_ctx):
            self.copy(source, unit, k).wait_send()


def greet(n_ctx, tp_too):
    index, rank = lax.axis_index("ctx"), lax.axis_index("tp")
    barrier = pltpu.get_barrier_semaphore()
    for k in range(1, n_ctx):
        signal(barrier, (jnp.bitwise_xor(index, k), rank))
    if tp_too:
        for device in neighbours():
            signal(barrier, device)
    pl.semaphore_wait(barrier, n_ctx - 1 + (2 if tp_too else 0))


def rotation(cos_tab, sin_tab, block_cos, block_sin):
    sign = jnp.where(lax.broadcasted_iota(jnp.int32, cos_tab.shape, 1) < HD // 2, -1.0, 1.0)
    return cos_tab * block_cos - sin_tab * block_sin, (sin_tab * block_cos + cos_tab * block_sin) * sign


def in_turn(count):
    return [count - 1] + list(range(count - 1))


def attend_rows(qs, ks, vs, os, tile):
    length = qs.shape[0]
    factor = -(HD ** (-0.5)) * LOG2E
    shift = math.log(length) * LOG2E
    row_at = lax.broadcasted_iota(jnp.int32, (tile, tile), 0)
    col_at = lax.broadcasted_iota(jnp.int32, (tile, tile), 1)
    for i in range(length // tile):
        query = qs[i * tile : (i + 1) * tile, :]

        def part(j, masked):
            at = pl.ds(pl.multiple_of(j * tile, tile), tile)
            raw = times_transposed(query, ks[at, :])
            prob = 1.0 / (1.0 + jnp.exp2(raw * factor + shift))
            if masked:
                prob = jnp.where(row_at >= col_at, prob, 0.0)
            return dot(prob.astype(BF), vs[at, :])

        total = part(i, True)
        if i > 0:
            total = lax.fori_loop(0, i, lambda j, acc: acc + part(j, False), total)
        os[i * tile : (i + 1) * tile, :] = total.astype(BF)


def forward_kernel(n_ctx, groups, units, tile, *refs):
    tokens_ref, cot_ref, wq_in, wk_in, wv_in, wo_in, gain_one, gain_two = refs[:8]
    cos_ref, sin_ref, bcos_ref, bsin_ref, valid_ref = refs[8:13]
    n1_out, got_out, heads_out, residual, n2_out, cot_out = refs[13:19]
    x_ref, rows_buf, own_buf, send, got, o_send, o_got, tabs, qs, ks, vs, os = refs[19:31]
    (wq_ref, wk_ref, wv_ref, wo_ref, weight_sem), rest = refs[31:36], refs[36:]
    n_gather, n_exchange = len(Gather.scratch()), len(Exchange.scratch(1, 2))
    n1_sems, rest = rest[:n_gather], rest[n_gather:]
    n2_sems, rest = rest[:n_gather], rest[n_gather:]
    cot_sems, rest = rest[:n_gather], rest[n_gather:]
    x_sems, rest = rest[:n_exchange], rest[n_exchange:]
    o_sems, rest = rest[:n_exchange], rest[n_exchange:]
    (n1_sem, got_sem, load_sem), rest = rest[:3], rest[3:]
    me, rank = lax.axis_index("ctx"), lax.axis_index("tp")
    odd = lax.rem(rank, 2)
    heads = wq_ref.shape[1] // HD
    per_unit = n_ctx // heads
    own_at = [pl.multiple_of(odd * BLOCK, BLOCK), pl.multiple_of((1 - odd) * PAIR, BLOCK)]

    def load_x(g):
        _, rows, own = groups[g]
        return pltpu.make_async_copy(
            tokens_ref.at[pl.ds(own_at[g], rows)], x_ref.at[pl.ds(own, rows)], load_sem.at[g]
        )

    load_weights = [
        pltpu.make_async_copy(source, dest, weight_sem.at[k])
        for k, (source, dest) in enumerate(((wq_in, wq_ref), (wk_in, wk_ref), (wv_in, wv_ref), (wo_in, wo_ref)))
    ]
    for g in range(2):
        load_x(g).start()
    for copy in load_weights:
        copy.start()
    greet(n_ctx, True)
    gather_one = Gather(own_buf, rows_buf, groups, n1_sems, local=False)
    gather_two = Gather(own_buf, n2_out, groups, n2_sems)
    gather_cot = Gather(cot_ref, cot_out, groups, cot_sems, own_at=own_at)
    scatter = Scatter(rows_buf, groups, rest[:6], rest[6:], loaded=False)
    trade = Exchange(got, x_sems, True)
    trade_back = Exchange(o_got, o_sems, False)

    def halves_of(u):
        return halves_at(odd if units[u][1] else 0)

    def normed(source, gain, at):
        values = source[at, :].astype(F32)
        return (values * inverse_rms(values) * gain[...].astype(F32)).astype(BF)

    def begin(g):
        base, rows, own = groups[g]
        load_x(g).wait()
        low = normed(x_ref, gain_one, pl.ds(own, rows))
        own_buf[pl.ds(own, rows), :] = low
        gather_one.start(g)
        rows_buf[pl.ds(base, rows), :] = low

    begin(0)
    for half, block in enumerate((me, 2 * n_ctx - 1 - me)):
        cos_part, sin_part = rotation(
            cos_ref[...], sin_ref[...], bcos_ref[pl.ds(block, 1), :], bsin_ref[pl.ds(block, 1), :]
        )
        tabs[0, half * BLOCK : (half + 1) * BLOCK, :] = cos_part
        tabs[1, half * BLOCK : (half + 1) * BLOCK, :] = sin_part

    def query(u, block):
        base, flipped = units[u]
        first, second = halves_of(u)
        at = pl.ds(base + block * PAIR, PAIR)
        rows = rows_buf[at, :]
        for which, w_ref in enumerate((wq_ref, wk_ref, wv_ref)):
            product = dot(rows, w_ref[...])
            for head in range(heads):
                part = product[:, head * HD : (head + 1) * HD]
                pair = block * heads + head
                for half, to in ((0, first), (1, second)):
                    piece = part[half * BLOCK : (half + 1) * BLOCK]
                    if which < 2:
                        piece = piece * tabs[0, to, :] + pltpu.roll(piece, HD // 2, 1) * tabs[1, to, :]
                    else:
                        piece = piece * valid_ref[pl.ds(base + block * PAIR + half * BLOCK, BLOCK), :]
                    send[u, pair, which, to, :] = piece.astype(BF)
        trade.start_some(send, u, block * heads, heads)

    store_n1 = pltpu.make_async_copy(rows_buf, n1_out, n1_sem)
    store_got = [pltpu.make_async_copy(got.at[u], got_out.at[u], got_sem.at[u]) for u in range(len(units))]

    for copy in load_weights:
        copy.wait()
    query(0, 0)
    gather_one.forward_x(0)
    gather_one.forward_y(0)
    begin(1)
    query(0, 1)
    query(1, 0)
    gather_one.finish(0)
    query(1, 1)
    gather_one.forward(1)
    gather_one.finish(1)
    for g in range(2):
        gather_cot.start(g)
    query(2, 0)
    query(2, 1)
    store_n1.start()

    def attend(u):
        trade.arrived(send, u)
        store_got[u].start()
        for k in range(n_ctx):
            front, back = both_places(me, k, n_ctx)
            for which, dest in enumerate((qs, ks, vs)):
                dest[front, :] = got[u, k, which, :BLOCK, :]
                dest[back, :] = got[u, k, which, BLOCK:, :]
        attend_rows(qs, ks, vs, os, tile)
        for k in range(n_ctx):
            front, back = both_places(me, k, n_ctx)
            o_send[u, k, :BLOCK, :] = os[front, :]
            o_send[u, k, BLOCK:, :] = os[back, :]
        trade_back.start(o_send, u)

    def project(u):
        trade_back.arrived(o_send, u)
        base, _ = units[u]
        first, second = halves_of(u)
        for block in range(per_unit):
            at = pl.ds(base + block * PAIR, PAIR)
            low = valid_ref[at, :].astype(BF)
            for head in range(heads):
                place = jnp.bitwise_xor(me, block * heads + head)
                part = jnp.concatenate([o_got[u, place, first, :], o_got[u, place, second, :]], axis=0)
                heads_out[at, head * HD : (head + 1) * HD] = part * low
            rows_buf[at, :] = dot(heads_out[at, :], wo_ref[...]).astype(BF)

    def use(at, total):
        residual[at, :] = x_ref[at, :].astype(F32) + total
        own_buf[at, :] = normed(residual, gain_two, at)

    def finish_group(g):
        scatter.total(g, use)
        gather_two.start(g)

    attend(0)
    for g in range(2):
        gather_one.sent(g)
    store_n1.wait()
    attend(1)
    for g in range(2):
        gather_cot.forward(g)
    project(0)
    scatter.start(0, (0,), loads=False)
    project(1)
    scatter.start(0, (1, 3, 2), loads=False)
    attend(2)
    scatter.forward(0)
    project(2)
    scatter.start(1, loads=False)
    finish_group(0)
    scatter.forward(1)
    finish_group(1)
    gather_two.forward(0)
    gather_two.forward(1)
    for u in range(len(units)):
        trade.sent(send, u)
        trade_back.sent(o_send, u)
        store_got[u].wait()
    for g in range(2):
        gather_cot.finish(g)
        gather_two.finish(g)
        gather_two.sent(g)
        gather_cot.sent(g)


def forward_layer(tokens_in, cot_in, gain_one, gain_two, wq, wk, wv, wo, tables, valid, n_ctx, groups, units):
    rows, depth = tokens_in.shape
    width = wq.shape[1]
    tokens = valid.shape[0]
    length = 2 * n_ctx * BLOCK
    n_units = len(units)
    vmem = lambda shape, dtype=BF: pltpu.VMEM(shape, dtype)
    outs = [
        jax.ShapeDtypeStruct((tokens, depth), BF),
        jax.ShapeDtypeStruct((n_units, n_ctx, 3, PAIR, HD), BF),
        jax.ShapeDtypeStruct((tokens, width), BF),
        jax.ShapeDtypeStruct((rows, depth), F32),
        jax.ShapeDtypeStruct((tokens, depth), BF),
        jax.ShapeDtypeStruct((tokens, depth), BF),
    ]
    return pl.pallas_call(
        functools.partial(forward_kernel, n_ctx, groups, units, min(512, length)),
        out_shape=outs,
        in_specs=[ANY_SPEC] * 6 + [VMEM_SPEC] * 7,
        out_specs=[ANY_SPEC, ANY_SPEC, VMEM_SPEC, VMEM_SPEC, ANY_SPEC, ANY_SPEC],
        scratch_shapes=[
            vmem((rows, depth)),
            vmem((tokens, depth)),
            vmem((rows, depth)),
            vmem((n_units, n_ctx, 3, PAIR, HD)),
            vmem((n_units, n_ctx, 3, PAIR, HD)),
            vmem((n_units, n_ctx, PAIR, HD)),
            vmem((n_units, n_ctx, PAIR, HD)),
            vmem((2, PAIR, HD), F32),
        ]
        + [vmem((length, HD))] * 4
        + [vmem(wq.shape)] * 3
        + [vmem(wo.shape), pltpu.SemaphoreType.DMA((4,))]
        + Gather.scratch() * 3
        + Exchange.scratch(n_units, n_ctx) * 2
        + [pltpu.SemaphoreType.DMA, pltpu.SemaphoreType.DMA((n_units,)), pltpu.SemaphoreType.DMA((2,))]
        + Scatter.scratch(rows, depth, loaded=False),
        compiler_params=pltpu.CompilerParams(vmem_limit_bytes=VMEM_LIMIT, collective_id=3, has_side_effects=True),
        cost_estimate=pl.CostEstimate(
            flops=8 * tokens * depth * width, bytes_accessed=8 * tokens * depth, transcendentals=0
        ),
    )(tokens_in, cot_in, wq, wk, wv, wo, gain_one, gain_two, *tables, valid)


def attend_rows_back(qs, ks, vs, gs, os, dqs, cos_ref, sin_ref, tile):
    length = qs.shape[0]
    scale = HD ** (-0.5)
    factor = -scale * LOG2E
    shift = math.log(length) * LOG2E
    count = length // tile
    key_at = lax.broadcasted_iota(jnp.int32, (tile, tile), 0)
    query_at = lax.broadcasted_iota(jnp.int32, (tile, tile), 1)
    dqs[...] = jnp.zeros_like(dqs)

    def unrotate(values, at):
        return (values * cos_ref[at, :] - pltpu.roll(values, HD // 2, 1) * sin_ref[at, :]).astype(BF)

    for j in range(count):
        own = slice(j * tile, (j + 1) * tile)
        keys = ks[own, :]
        values = vs[own, :]

        def part(i, masked):
            at = pl.ds(pl.multiple_of(i * tile, tile), tile)
            query = qs[at, :]
            grad = gs[at, :]
            raw = times_transposed(keys, query)
            prob = 1.0 / (1.0 + jnp.exp2(raw * factor + shift))
            if masked:
                prob = jnp.where(query_at >= key_at, prob, 0.0)
            prob_grad = times_transposed(values, grad)
            score_grad = (prob_grad * prob * (1.0 - prob)).astype(BF)
            dqs[at, :] += contract_rows(score_grad, keys)
            return dot(score_grad, query), dot(prob.astype(BF), grad)

        total = part(j, True)
        if j + 1 < count:

            def step(i, acc):
                more = part(i, False)
                return acc[0] + more[0], acc[1] + more[1]

            total = lax.fori_loop(j + 1, count, step, total)
        os[1, own, :] = unrotate(total[0] * scale, own)
        os[2, own, :] = total[1].astype(BF)
    for i in range(count):
        at = slice(i * tile, (i + 1) * tile)
        os[0, at, :] = unrotate(dqs[at, :] * scale, at)


def middle_kernel(n_ctx, groups, units, tile, *refs):
    da_ref, got_ref, h_ref, residual_ref, wd_ref, wq_in, wk_in, wv_in, wo_in = refs[:9]
    cos_ref, sin_ref, bcos_ref, bsin_ref, valid_ref = refs[9:14]
    grad_ref, partial_out, output = refs[14:17]
    rows_buf, got, do_send, do_got, back_got, h_buf, wd_buf, res_buf, cos_full, sin_full = refs[17:27]
    qs, ks, vs, gs, os, dqs = refs[27:33]
    (wq_ref, wk_ref, wv_ref, wo_ref, weight_sem), rest = refs[33:38], refs[38:]
    load_weights = [
        pltpu.make_async_copy(source, dest, weight_sem.at[k])
        for k, (source, dest) in enumerate(((wo_in, wo_ref), (wq_in, wq_ref), (wk_in, wk_ref), (wv_in, wv_ref)))
    ]
    load_weights[0].start()
    back_send = got
    n_exchange = len(Exchange.scratch(1, 2))
    do_sems, back_sems, rest = rest[:n_exchange], rest[n_exchange : 2 * n_exchange], rest[2 * n_exchange :]
    (da_sem, got_sem, out_sem, h_sem, wd_sem, res_sem, y_sem), rest = rest[:7], rest[7:]
    me, rank = lax.axis_index("ctx"), lax.axis_index("tp")
    odd = lax.rem(rank, 2)
    heads = wq_ref.shape[1] // HD
    per_unit = n_ctx // heads
    unit_rows = per_unit * PAIR
    count = len(units)
    order = in_turn(count)

    def rows_of(u):
        return pl.ds(units[u][0], unit_rows)

    load_da = [pltpu.make_async_copy(da_ref.at[rows_of(u)], rows_buf.at[rows_of(u)], da_sem.at[u]) for u in range(count)]
    load_got = [pltpu.make_async_copy(got_ref.at[u], got.at[u], got_sem.at[u]) for u in range(count)]
    for u in order:
        load_da[u].start()
    for u in order:
        load_got[u].start()
    first_wd = pltpu.make_async_copy(wd_ref.at[:, pl.ds(0, wd_buf.shape[1])], wd_buf, wd_sem)
    first_wd.start()
    for copy in load_weights[1:]:
        copy.start()
    greet(n_ctx, True)
    scatter = Scatter(rows_buf, groups, rest[:6], rest[6:], loaded=False)
    trade = Exchange(do_got, do_sems, True)
    trade_back = Exchange(back_got, back_sems, False)

    load_weights[0].wait()
    for u in order:
        load_da[u].wait()
        base, flipped = units[u]
        first, second = halves_at(odd if flipped else 0)
        for block in range(per_unit):
            at = pl.ds(base + block * PAIR, PAIR)
            grad = times_transposed(rows_buf[at, :], wo_ref[...]).astype(BF)
            low = valid_ref[at, :].astype(BF)
            for head in range(heads):
                part = grad[:, head * HD : (head + 1) * HD] * low
                do_send[u, block * heads + head, first, :] = part[:BLOCK]
                do_send[u, block * heads + head, second, :] = part[BLOCK:]
        trade.start(do_send, u)
    for block in range(2 * n_ctx):
        at = slice(block * BLOCK, (block + 1) * BLOCK)
        cos_full[at, :], sin_full[at, :] = rotation(
            cos_ref[...], sin_ref[...], bcos_ref[block : block + 1, :], bsin_ref[block : block + 1, :]
        )
    for copy in load_weights[1:]:
        copy.wait()
    for u in order:
        load_got[u].wait()

    def attend(turn, carry):
        u = lax.rem(turn + count - 1, count)
        trade.arrived(do_send, u)
        for k in range(n_ctx):
            front, back = both_places(me, k, n_ctx)
            for which, dest in enumerate((qs, ks, vs)):
                dest[front, :] = got[u, k, which, :BLOCK, :]
                dest[back, :] = got[u, k, which, BLOCK:, :]
            gs[front, :] = do_got[u, k, :BLOCK, :]
            gs[back, :] = do_got[u, k, BLOCK:, :]
        attend_rows_back(qs, ks, vs, gs, os, dqs, cos_full, sin_full, tile)
        for k in range(n_ctx):
            front, back = both_places(me, k, n_ctx)
            for which in range(3):
                back_send[u, k, which, :BLOCK, :] = os[which, front, :]
                back_send[u, k, which, BLOCK:, :] = os[which, back, :]
        trade_back.start(back_send, u)
        return carry

    lax.fori_loop(0, count, attend, 0)

    tiles = rows_buf.shape[0] // PAIR

    def tile_rows(tile):
        return pl.ds(pl.multiple_of(tile * PAIR, PAIR), PAIR)

    def load_h(step):
        slot = lax.rem(step, 2)
        return pltpu.make_async_copy(h_ref.at[tile_rows(lax.rem(step, tiles))], h_buf.at[slot], h_sem.at[slot])

    columns = wd_buf.shape[1]
    parts = rows_buf.shape[1] // columns

    def part_columns(part):
        return pl.ds(pl.multiple_of(part * columns, columns), columns)

    def load_wd(part):
        return pltpu.make_async_copy(wd_ref.at[:, part_columns(part)], wd_buf, wd_sem)

    load_h(0).start()

    def down(step, carry):
        part, tile = step // tiles, lax.rem(step, tiles)

        @pl.when(step + 1 < tiles * parts)
        def _():
            load_h(step + 1).start()

        @pl.when(tile == 0)
        def _():
            @pl.when(part > 0)
            def _():
                load_wd(part).start()

            load_wd(part).wait()

        load_h(step).wait()
        rows_buf[tile_rows(tile), part_columns(part)] = dot(h_buf[lax.rem(step, 2)], wd_buf[...]).astype(BF)
        return carry

    lax.fori_loop(0, tiles * parts, down, 0)
    last_group = len(groups) - 1
    out_rows = rest[0]
    for g in (last_group, 0):
        scatter.start(g, loads=False)

    def use(at, total):
        size = total.shape[0]
        load = pltpu.make_async_copy(residual_ref.at[at], res_buf.at[pl.ds(0, size)], res_sem)
        load.start()
        load.wait()
        low = (res_buf[:size, :] + total).astype(BF)
        out_rows[at, :] = low

    def store(number, first):
        slot = number % 2
        return pltpu.make_async_copy(h_buf.at[slot], partial_out.at[pl.ds(first, PAIR)], out_sem.at[slot])

    stored = []
    for turn, u in enumerate(order):
        trade_back.arrived(back_send, u)
        base, flipped = units[u]
        first, second = halves_at(odd if flipped else 0)
        for block in range(per_unit):
            at = pl.ds(base + block * PAIR, PAIR)
            low = valid_ref[at, :].astype(BF)
            total = None
            for which, w_ref in enumerate((wq_ref, wk_ref, wv_ref)):
                width = heads * HD
                for head in range(heads):
                    place = jnp.bitwise_xor(me, block * heads + head)
                    part = jnp.concatenate(
                        [back_got[u, place, which, first, :], back_got[u, place, which, second, :]], axis=0
                    )
                    columns = slice(which * width + head * HD, which * width + (head + 1) * HD)
                    grad_ref[at, columns] = part * low if which == 2 else part
                product = times_transposed(grad_ref[at, which * width : (which + 1) * width], w_ref[...])
                total = product if total is None else total + product
            number = len(stored)
            if number >= 2:
                stored[number - 2].wait()
            h_buf[number % 2] = total.astype(BF)
            stored.append(store(number, base + block * PAIR))
            stored[-1].start()
        if turn == 0:
            scatter.forward(last_group)
            scatter.forward(0)
        if turn == 1:
            for g in (last_group, 0):
                scatter.total(g, use)
            store_y = pltpu.make_async_copy(out_rows, output, y_sem)
            store_y.start()
    store_y.wait()
    for copy in stored[-2:]:
        copy.wait()
    for u in order:
        trade.sent(do_send, u)
        trade_back.sent(back_send, u)


def middle_layer(da, got, h, residual, wq, wk, wv, wo, wd, tables, valid, n_ctx, groups, units):
    tokens, depth = da.shape
    width = wq.shape[1]
    length = 2 * n_ctx * BLOCK
    count = len(units)
    vmem = lambda shape, dtype=BF: pltpu.VMEM(shape, dtype)
    dma = pltpu.SemaphoreType.DMA
    three, one = (count, n_ctx, 3, PAIR, HD), (count, n_ctx, PAIR, HD)
    most_rows = max(rows for _, rows, _ in groups) // 2
    return pl.pallas_call(
        functools.partial(middle_kernel, n_ctx, groups, units, min(512, length)),
        out_shape=[
            jax.ShapeDtypeStruct((tokens, 3 * width), BF),
            jax.ShapeDtypeStruct((tokens, depth), BF),
            jax.ShapeDtypeStruct(residual.shape, BF),
        ],
        in_specs=[ANY_SPEC] * 9 + [VMEM_SPEC] * 5,
        out_specs=[VMEM_SPEC, ANY_SPEC, ANY_SPEC],
        scratch_shapes=[vmem((tokens, depth)), vmem(three), vmem(one), vmem(one), vmem(three)]
        + [vmem((2, PAIR, depth)), vmem((h.shape[1], depth // 2)), vmem((most_rows, depth), F32)]
        + [vmem((length, HD), F32)] * 2
        + [vmem((length, HD))] * 4
        + [vmem((3, length, HD)), vmem((length, HD), F32)]
        + [vmem(wq.shape)] * 3
        + [vmem(wo.shape), dma((4,))]
        + Exchange.scratch(count, n_ctx) * 2
        + [dma((count,)), dma((count,)), dma((2,)), dma((2,)), dma, dma, dma]
        + Scatter.scratch(residual.shape[0], depth, loaded=False),
        compiler_params=pltpu.CompilerParams(vmem_limit_bytes=VMEM_LIMIT, collective_id=4, has_side_effects=True),
        cost_estimate=pl.CostEstimate(
            flops=8 * tokens * depth * width + 2 * tokens * depth * h.shape[1],
            bytes_accessed=8 * tokens * depth,
            transcendentals=0,
        ),
    )(da, got, h, residual, wd, wq, wk, wv, wo, *tables, valid)


def body(
    tokens,
    counts,
    norm_gain,
    w_query,
    w_key,
    w_value,
    w_output,
    mlp_gain,
    w_gate,
    w_up,
    w_down,
    cotangent,
):
    n_ctx = lax.axis_size("ctx")
    me = lax.axis_index("ctx")
    rank = lax.axis_index("tp")
    odd = rank & 1
    core = me & 1
    length = 2 * BLOCK * n_ctx
    heads = w_query.shape[1] // HD
    gain_one = norm_gain.astype(F32)
    gain_two = mlp_gain.astype(F32)

    inverse = THETA ** (-(jnp.arange(HD // 2, dtype=F32) * (2.0 / HD)))
    angles = jnp.arange(length, dtype=jnp.int32).astype(F32)[:, None] * inverse[None, :]
    cos_half, sin_half = jnp.cos(angles), jnp.sin(angles)
    cos_full = jnp.concatenate([cos_half, cos_half], axis=1)
    sin_full = jnp.concatenate([-sin_half, sin_half], axis=1)

    def own_blocks(table):
        front = lax.dynamic_slice_in_dim(table, me * BLOCK, BLOCK, 0)
        back = lax.dynamic_slice_in_dim(table, (2 * n_ctx - 1 - me) * BLOCK, BLOCK, 0)
        return front, back

    cos_front, cos_back = own_blocks(cos_full)
    sin_front, sin_back = own_blocks(sin_full)
    own_counts = lax.dynamic_index_in_dim(counts, me, 0, keepdims=False)
    offsets = jnp.arange(BLOCK, dtype=jnp.int32)

    def valid_of(sequence_list, half_list):
        held = own_counts[jnp.stack(sequence_list), jnp.stack(half_list)]
        return (offsets[None, :] < held[:, None]).astype(F32).reshape(-1)

    cos_own = jnp.concatenate([cos_front, cos_back])
    sin_own = jnp.concatenate([sin_front, sin_back])
    sequences = counts.shape[1]
    paired = by_four() and sequences == 6 and n_ctx == 2 * heads
    if paired:
        ranks = [rank ^ k for k in range(4)]
        blocks_a = [(3 * (r >> 1) + 2 * (r & 1), jnp.int32(half)) for r in ranks for half in range(2)]
        blocks_b = [(1 + 3 * (r >> 1), r & 1) for r in ranks]
        flat_valid = valid_of(*zip(*(blocks_a + blocks_b)))
        valids = {"b": flat_valid[len(blocks_a) * BLOCK :], "a": flat_valid[: len(blocks_a) * BLOCK]}
        flip_back = lambda own: jnp.where(odd == 1, jnp.roll(own, BLOCK, axis=0), own)
        tables = {
            "b": (jnp.tile(flip_back(cos_own), (2, 1)), jnp.tile(flip_back(sin_own), (2, 1))),
            "a": (jnp.tile(cos_own, (4, 1)), jnp.tile(sin_own, (4, 1))),
        }
        scalars = {"b": jnp.stack([me, odd]).astype(jnp.int32), "a": jnp.stack([me, 0]).astype(jnp.int32)}
        n_pairs = {"b": 2 * heads, "a": 4 * heads}
    else:
        flat_valid = (offsets[None, None, :] < own_counts[:, :, None]).astype(F32).reshape(-1)
        valids = {"a": flat_valid}
        tables = {"a": (jnp.tile(cos_own, (sequences, 1)), jnp.tile(sin_own, (sequences, 1)))}
        scalars = {"a": jnp.stack([me, 0]).astype(jnp.int32)}
        n_pairs = {"a": sequences * heads}
    names = tuple(n_pairs)

    def own_rows(array):
        if not paired:
            return {"a": array}
        return {
            "b": lax.dynamic_slice_in_dim(array, (1 - odd) * PAIR, BLOCK, 0),
            "a": lax.dynamic_slice_in_dim(array, odd * BLOCK, PAIR, 0),
        }

    x_own = {name: rows.astype(F32) for name, rows in own_rows(tokens[0]).items()}
    g_own = own_rows(cotangent[0])

    split = by_four()
    rows_of = {name: valids[name].shape[0] for name in names}
    total_rows = sum(rows_of.values())
    first_row = {"a": 0, "b": rows_of["a"]}
    valid_head = {name: jnp.broadcast_to(valids[name][:, None], (rows_of[name], HD)) for name in names}
    valid_wide = {name: jnp.broadcast_to(valids[name][:, None].astype(BF), (rows_of[name], heads * HD)) for name in names}
    near = [k for k in range(n_ctx) if k < 6]
    far = [k for k in range(n_ctx) if k >= 6]
    state = {}

    def fence():
        names_held = list(state)
        values = lax.optimization_barrier([state[name] for name in names_held])
        state.update(zip(names_held, values))

    def only_b(step):
        if "b" in names:
            step("b")

    def norm_one(n):
        state["n1", n] = (x_own[n] * inverse_rms(x_own[n]) * gain_one).astype(BF)

    def gather_a(key):
        def step(n):
            state[key, n] = gather_first(state[key, n])

        return step

    def gather_b(key):
        def step(n):
            state[key, n] = gather_second(state[key, n])

        return step

    def query(n):
        state["n1", n] = gathered(state["n1", n])
        cos_tab, sin_tab = tables[n]
        state["qkv", n] = project_qkv(
            scalars[n], state["n1", n], w_query, w_key, w_value, cos_tab, sin_tab, valid_head[n], n_ctx
        )

    def swap_part(key, places, to):
        def step(n):
            got = dict(state.get((to, n), {}))
            got.update(exchange(state[key, n], places, n_ctx))
            state[to, n] = got
            if len(got) == n_ctx:
                state[to, n] = [got[k] for k in range(n_ctx)]
                del state[key, n]

        return step

    def attend(n):
        state["mixed", n] = attention_forward(scalars[n], state["got", n], n_ctx)

    def project(n):
        heads_out, *parts = project_out(
            scalars[n], state.pop(("back", n)), w_output, valid_wide[n], n_pairs[n], n_ctx, split
        )
        state["heads", n], state["r", n] = heads_out, tuple(parts)

    def scatter_a(key):
        def step(n):
            state[key, n] = scatter_first(state[key, n])

        return step

    def scatter_b(key):
        def step(n):
            state[key, n] = scatter_second(state[key, n])

        return step

    def norm_two(n):
        residual = x_own[n] + scattered(state.pop(("r", n)))
        state["residual", n] = residual
        state["n2", n] = (residual * inverse_rms(residual) * gain_two).astype(BF)

    def core_mlp(n):
        state["n2", n] = gathered(state["n2", n])
        state["cot", n] = gathered(state["cot", n])
        held = state.get("mlp", ())
        state["mlp"] = mlp_core(
            state["n2", n], state["cot", n], w_gate, w_up, w_down, total_rows, first_row[n], held
        )

    def attend_back(n):
        state["dqkv", n] = attention_backward(
            scalars[n], state.pop(("got", n)), state.pop(("gdo", n)), cos_full, sin_full, n_ctx
        )

    def query_back(n):
        dq, dk, dv, *parts = project_in(
            scalars[n], state.pop(("gdqkv", n)), (w_query, w_key, w_value), valid_wide[n], n_pairs[n], n_ctx, False
        )
        state["dq", n], state["dk", n], state["dv", n], state["i", n] = dq, dk, dv, parts[0]

    def joined(key):
        parts = [state[key, n] for n in ("a", "b") if n in names]
        return jnp.concatenate(parts) if len(parts) > 1 else parts[0]

    groups = tuple((first_row[n], rows_of[n] // 4, first_row[n] // 4) for n in ("a", "b") if n in names)

    if paired:
        units = ((0, False), (2 * PAIR, False), (4 * PAIR, True))
        wide_valid = jnp.broadcast_to(flat_valid[:, None], (total_rows, HD))
        twice = lambda table: jnp.concatenate([table, table], axis=1)
        starts = BLOCK * jnp.arange(2 * n_ctx, dtype=jnp.int32)
        spans = [at.astype(F32)[:, None] * inverse[None, :] for at in (offsets, starts)]
        turns = [twice(part(angle)) for angle in spans for part in (jnp.cos, jnp.sin)]
        all_n1, got, heads_out, own_residual, all_n2, all_cot = forward_layer(
            tokens[0], cotangent[0], norm_gain[None], mlp_gain[None], w_query, w_key, w_value, w_output,
            turns, wide_valid, n_ctx, groups, units,
        )
    else:
        norm_one("a")
        state["cot", "a"] = g_own["a"]
        gather_a("n1")("a")
        query("a")
        swap_part("qkv", range(n_ctx), "got")("a")
        attend("a")
        swap_part("mixed", range(n_ctx), "back")("a")
        project("a")
        scatter_a("r")("a")
        norm_two("a")
        gather_a("n2")("a")
        gather_a("cot")("a")
        all_n1, all_n2, all_cot = state["n1", "a"], gathered(state["n2", "a"]), gathered(state["cot", "a"])
        heads_out, own_residual = state["heads", "a"], state["residual", "a"]
    if paired:
        extra = feed_extra(groups, all_n2, w_gate, w_up, w_down, own_residual, cotangent[0], mlp_gain[None])
        sum_down, sum_gate, sum_up, sum_out, dr, da, gain_two_grad, _, h, _, _ = weight_sums(
            [(w_down.shape[0], 0), (all_n2, 1), (all_n2, 2), (heads_out, 3)],
            [all_cot], n_ctx, 1, extra, late=(5, 6, 1), limit=62 * 1024 * 1024,
        )
        dqkv, i_partial, output = middle_layer(
            da, got, h, own_residual, w_query, w_key, w_value, w_output, w_down, turns, wide_valid, n_ctx, groups, units
        )
        extra = input_extra(n_ctx, groups, i_partial, tokens[0], dr, norm_gain[None], gain_two_grad)
        sum_qkv, input_grad, gain_sums = weight_sums(
            [(all_n1, 0)], [dqkv], n_ctx, 2, extra
        )
    else:
        own_grads = cotangent[0]
        h, dgp, dup = mlp_core(all_n2, all_cot, w_gate, w_up, w_down, total_rows, 0)
        d_partial = (times_transposed(dgp, w_gate) + times_transposed(dup, w_up)).astype(BF)
        y_partial = dot(h, w_down).astype(BF)
        (sum_down,) = weight_sums([(h, 0)], [all_cot], n_ctx, 1)
        sum_gate, sum_up = weight_sums([(all_n2, 0), (all_n2, 1)], [dgp, dup], n_ctx, 2)
        back, gain_two_grad = norm_back_rows(own_residual, gain_two, scattered(scatter_first((d_partial,))))
        dr = own_grads.astype(F32) + back
        da = gathered(gather_first(dr.astype(BF)))
        output = (own_residual + scattered(scatter_first((y_partial,)))).astype(BF)
        state["do", "a"] = heads_back(scalars["a"], da, w_output, valid_wide["a"], n_ctx)
        swap_part("do", range(n_ctx), "gdo")("a")
        attend_back("a")
        swap_part("dqkv", range(n_ctx), "gdqkv")("a")
        query_back("a")
        (sum_out,) = weight_sums([(heads_out, 0)], [da], n_ctx, 3)
        (sum_qkv,) = weight_sums(
            [(all_n1, 0)], [jnp.concatenate([state[key, "a"] for key in ("dq", "dk", "dv")], axis=1)], n_ctx, 4
        )
        back, gain_one_grad = norm_back_rows(x_own["a"], gain_one, scattered(scatter_first((state["i", "a"],))))
        input_grad = (dr + back).astype(BF)
    sums = (sum_out, sum_gate, sum_up, sum_down, sum_qkv)
    if paired:
        *grads, output, input_grad, grad_norm_gain, grad_mlp_gain = cast_sums(sums, groups, (output, input_grad), gain_sums)
        gains = grad_norm_gain[0], grad_mlp_gain[0]
    else:
        grads = cast_sums(sums)
        gains = lax.psum(jnp.concatenate([gain_one_grad, gain_two_grad]), ("ctx", "tp"))
    grad_out, grad_gate, grad_up, grad_down, grad_query, grad_key, grad_value = grads
    return (
        output[None],
        input_grad[None],
        gains[0],
        grad_query,
        grad_key,
        grad_value,
        grad_out,
        gains[1],
        grad_gate,
        grad_up,
        grad_down,
    )


def solution(mesh):
    placed = (
        P("ctx", "tp", None),
        P(),
        P(),
        P(None, "tp"),
        P(None, "tp"),
        P(None, "tp"),
        P("tp", None),
        P(),
        P(None, "tp"),
        P(None, "tp"),
        P("tp", None),
        P("ctx", "tp", None),
    )
    return jax.shard_map(
        body,
        mesh=mesh,
        in_specs=placed,
        out_specs=(
            P("ctx", "tp", None),
            P("ctx", "tp", None),
            P(),
            P(None, "tp"),
            P(None, "tp"),
            P(None, "tp"),
            P("tp", None),
            P(),
            P(None, "tp"),
            P(None, "tp"),
            P("tp", None),
        ),
        check_vma=False,
    )
```

```python
import functools
import math

import jax
import jax.numpy as jnp
from jax import lax
from jax.experimental import pallas as pl
from jax.experimental.pallas import tpu as pltpu
from jax.sharding import PartitionSpec as P

HD = 128
BLOCK = 128
PAIR = 2 * BLOCK
EPS = 1e-05
THETA = 10000.0
LOG2E = 1.4426950408889634
BF = jnp.bfloat16
F32 = jnp.float32
VMEM_LIMIT = 60 * 1024 * 1024

X_SWAP = [(i, i ^ 1) for i in range(4)]
Y_SWAP = [(i, i ^ 2) for i in range(4)]


def dot(left, right):
    return jnp.dot(left, right, preferred_element_type=F32)


def contract_rows(left, right):
    return lax.dot_general(left, right, (((0,), (0,)), ((), ())), preferred_element_type=F32)


def times_transposed(left, right):
    return lax.dot_general(left, right, (((1,), (1,)), ((), ())), preferred_element_type=F32)


def send_x(values):
    return lax.ppermute(values, "tp", X_SWAP)


def send_y(values):
    return lax.ppermute(values, "tp", Y_SWAP)


def by_four():
    return lax.axis_size("tp") == 4


def gather_first(own):
    if not by_four():
        return (lax.all_gather(own, "tp", axis=0, tiled=True),)
    return own, send_x(own), send_y(own)


def gather_second(held):
    if len(held) == 1:
        return held
    own, from_x, from_y = held
    half = own.shape[0] // 2
    return own, from_x, from_y, send_x(from_y[:half]), send_y(from_x[half:])


def gathered(held):
    return jnp.concatenate(held) if len(held) > 1 else held[0]


def scatter_parts(partial):
    if not by_four():
        return (partial,)
    rows = partial.shape[0] // 4
    half = rows // 2
    at = lambda first: partial[first * half : (first + 1) * half]
    return (
        jnp.concatenate([at(2), at(6)]),
        jnp.concatenate([at(5), at(7)]),
        jnp.concatenate([at(0), at(1), at(4), at(3)]),
    )


def scatter_first(parts):
    if len(parts) == 1:
        return (lax.psum_scatter(parts[0], "tp", scatter_dimension=0, tiled=True),)
    return send_x(parts[0]), send_y(parts[1]), parts[2]


def add_low(left, right):
    return (left.astype(F32) + right.astype(F32)).astype(BF)


def scatter_second(held):
    if len(held) == 1:
        return held
    from_x, from_y, stay = held
    half = from_x.shape[0] // 2
    low_rest = send_y(add_low(stay[2 * half : 3 * half], from_x[half:]))
    high_rest = send_x(add_low(stay[3 * half :], from_y[half:]))
    return from_x, from_y, stay, low_rest, high_rest


def scattered(held):
    if len(held) == 1:
        return held[0].astype(F32)
    from_x, from_y, stay, low_rest, high_rest = (part.astype(F32) for part in held)
    half = low_rest.shape[0]
    low = stay[:half] + from_x[:half] + low_rest
    high = stay[half : 2 * half] + from_y[:half] + high_rest
    return jnp.concatenate([low, high])


def exchange(pieces, places, n_ctx):
    got = {}
    for k in places:
        got[k] = pieces[k] if k == 0 else lax.ppermute(pieces[k], "ctx", [(i, i ^ k) for i in range(n_ctx)])
    return got


def params():
    return pltpu.CompilerParams(vmem_limit_bytes=VMEM_LIMIT)


def whole(shape):
    return pl.BlockSpec(shape, lambda *_: (0,) * len(shape))


def put_partial(refs, first, value, rows):
    if len(refs) == 1:
        refs[0][first : first + value.shape[0], :] = value
        return
    to_x, to_y, stay = refs
    half = rows // 2
    homes = {
        0: (stay, 0), 1: (stay, 1), 2: (to_x, 0), 3: (stay, 3), 4: (stay, 2), 5: (to_y, 0), 6: (to_x, 1), 7: (to_y, 1)
    }
    for part in range(value.shape[0] // half):
        ref, place = homes[first // half + part]
        ref[place * half : (place + 1) * half, :] = value[part * half : (part + 1) * half]


def partial_shapes(rows, width, split):
    if not split:
        return [jax.ShapeDtypeStruct((rows, width), BF)]
    return [jax.ShapeDtypeStruct((rows // 4, width), BF)] * 2 + [jax.ShapeDtypeStruct((rows // 2, width), BF)]


def per_device(pairs, n_ctx):
    return -(-pairs // n_ctx)


def halves_at(swap):
    first = pl.multiple_of(swap * BLOCK, BLOCK)
    second = pl.multiple_of((1 - swap) * BLOCK, BLOCK)
    return pl.ds(first, BLOCK), pl.ds(second, BLOCK)


def qkv_kernel(n_ctx, pairs, scalar_ref, n_ref, wq_ref, wk_ref, wv_ref, cos_ref, sin_ref, valid_ref, *rest):
    out_refs, buffer = rest[:n_ctx], rest[n_ctx]
    rows = n_ref[...]
    first, second = halves_at(scalar_ref[1])
    me = scalar_ref[0]
    cos_tab = cos_ref[...]
    sin_tab = sin_ref[...]
    heads = wq_ref.shape[1] // HD
    step = pl.program_id(0)
    per = out_refs[0].shape[0]
    for pair in range(pairs, per * n_ctx):
        buffer[pair] = jnp.zeros(buffer.shape[1:], BF)
    for which, w_ref in enumerate((wq_ref, wk_ref, wv_ref)):
        product = dot(rows, w_ref[...])
        for head in range(heads):
            part = product[:, head * HD : (head + 1) * HD]
            if which < 2:
                part = part * cos_tab + pltpu.roll(part, HD // 2, 1) * sin_tab
            else:
                part = part * valid_ref[...]
            part = part.astype(BF)
            buffer[step * heads + head, which, first, :] = part[:BLOCK]
            buffer[step * heads + head, which, second, :] = part[BLOCK:]

    @pl.when(step == pl.num_programs(0) - 1)
    def _():
        for k in range(n_ctx):
            source = jnp.bitwise_xor(me, k)
            for p in range(per):
                out_refs[k][p] = buffer[source * per + p]


def project_qkv(scalars, normed, wq, wk, wv, cos_tab, sin_tab, valid, n_ctx):
    rows, depth = normed.shape
    width = wq.shape[1]
    heads = width // HD
    steps = rows // PAIR
    per = per_device(steps * heads, n_ctx)
    row_block = pl.BlockSpec((PAIR, HD), lambda i, s: (i, 0))
    weight = whole((depth, width))
    piece = (per, 3, PAIR, HD)
    return pl.pallas_call(
        functools.partial(qkv_kernel, n_ctx, steps * heads),
        out_shape=[jax.ShapeDtypeStruct(piece, BF)] * n_ctx,
        grid_spec=pltpu.PrefetchScalarGridSpec(
            num_scalar_prefetch=1,
            grid=(steps,),
            in_specs=[
                pl.BlockSpec((PAIR, depth), lambda i, s: (i, 0)),
                weight,
                weight,
                weight,
                row_block,
                row_block,
                row_block,
            ],
            out_specs=[whole(piece)] * n_ctx,
            scratch_shapes=[pltpu.VMEM((per * n_ctx, 3, PAIR, HD), BF)],
        ),
        compiler_params=params(),
        cost_estimate=pl.CostEstimate(
            flops=6 * rows * depth * width, bytes_accessed=rows * depth * 2 + 6 * depth * width, transcendentals=0
        ),
    )(scalars, normed, wq, wk, wv, cos_tab, sin_tab, valid)


def out_kernel(n_ctx, pairs, scalar_ref, *refs):
    piece_refs, (w_ref, valid_ref), (heads_ref, *partial_refs), buffer = (
        refs[:n_ctx],
        refs[n_ctx : n_ctx + 2],
        refs[n_ctx + 2 : -1],
        refs[-1],
    )
    me = scalar_ref[0]
    first, second = halves_at(scalar_ref[1])
    per = piece_refs[0].shape[0]
    heads = w_ref.shape[0] // HD
    for k in range(n_ctx):
        source = jnp.bitwise_xor(me, k)
        for p in range(per):
            buffer[source * per + p] = piece_refs[k][p]
    weight = w_ref[...]
    for sequence in range(pairs // heads):
        at = slice(sequence * PAIR, (sequence + 1) * PAIR)
        rows = jnp.concatenate(
            [
                jnp.concatenate(
                    [buffer[sequence * heads + head, first, :], buffer[sequence * heads + head, second, :]], axis=0
                )
                for head in range(heads)
            ],
            axis=1,
        )
        rows = rows * valid_ref[at, :]
        heads_ref[at, :] = rows
        put_partial(partial_refs, sequence * PAIR, dot(rows, weight).astype(BF), pairs // heads * PAIR // 4)


def project_out(scalars, pieces, weight, valid, pairs, n_ctx, split):
    width, depth = weight.shape
    rows = valid.shape[0]
    per = pieces[0].shape[0]
    shapes = [jax.ShapeDtypeStruct((rows, width), BF)] + partial_shapes(rows, depth, split)
    return pl.pallas_call(
        functools.partial(out_kernel, n_ctx, pairs),
        out_shape=shapes,
        grid_spec=pltpu.PrefetchScalarGridSpec(
            num_scalar_prefetch=1,
            grid=(1,),
            in_specs=[whole(piece.shape) for piece in pieces] + [whole(weight.shape), whole(valid.shape)],
            out_specs=[whole(shape.shape) for shape in shapes],
            scratch_shapes=[pltpu.VMEM((per * n_ctx, PAIR, HD), BF)],
        ),
        compiler_params=params(),
        cost_estimate=pl.CostEstimate(
            flops=2 * rows * depth * width, bytes_accessed=rows * depth * 2 + 2 * depth * width, transcendentals=0
        ),
    )(scalars, *pieces, weight, valid)


def heads_back_kernel(n_ctx, scalar_ref, da_ref, w_ref, valid_ref, *rest):
    out_refs, buffer = rest[:n_ctx], rest[n_ctx]
    me = scalar_ref[0]
    first, second = halves_at(scalar_ref[1])
    per = out_refs[0].shape[0]
    heads = w_ref.shape[0] // HD
    weight = w_ref[...]
    for pair in range(da_ref.shape[0] // PAIR * heads, per * n_ctx):
        buffer[pair] = jnp.zeros(buffer.shape[1:], BF)
    for sequence in range(da_ref.shape[0] // PAIR):
        at = slice(sequence * PAIR, (sequence + 1) * PAIR)
        grad = times_transposed(da_ref[at, :], weight).astype(BF) * valid_ref[at, :]
        for head in range(heads):
            part = grad[:, head * HD : (head + 1) * HD]
            buffer[sequence * heads + head, first, :] = part[:BLOCK]
            buffer[sequence * heads + head, second, :] = part[BLOCK:]
    for k in range(n_ctx):
        source = jnp.bitwise_xor(me, k)
        for p in range(per):
            out_refs[k][p] = buffer[source * per + p]


def heads_back(scalars, da, weight, valid, n_ctx):
    rows, depth = da.shape
    width = weight.shape[0]
    per = per_device(rows // PAIR * (width // HD), n_ctx)
    piece = (per, PAIR, HD)
    return pl.pallas_call(
        functools.partial(heads_back_kernel, n_ctx),
        out_shape=[jax.ShapeDtypeStruct(piece, BF)] * n_ctx,
        grid_spec=pltpu.PrefetchScalarGridSpec(
            num_scalar_prefetch=1,
            grid=(1,),
            in_specs=[whole(da.shape), whole(weight.shape), whole(valid.shape)],
            out_specs=[whole(piece)] * n_ctx,
            scratch_shapes=[pltpu.VMEM((per * n_ctx, PAIR, HD), BF)],
        ),
        compiler_params=params(),
        cost_estimate=pl.CostEstimate(
            flops=2 * rows * depth * width, bytes_accessed=rows * depth * 2 + 2 * depth * width, transcendentals=0
        ),
    )(scalars, da, weight, valid)


def in_kernel(n_ctx, pairs, scalar_ref, *refs):
    piece_refs, weight_refs, valid_ref = refs[:n_ctx], refs[n_ctx : n_ctx + 3], refs[n_ctx + 3]
    grad_refs, partial_refs, buffer = refs[n_ctx + 4 : n_ctx + 7], refs[n_ctx + 7 : -1], refs[-1]
    me = scalar_ref[0]
    first, second = halves_at(scalar_ref[1])
    per = piece_refs[0].shape[0]
    heads = weight_refs[0].shape[1] // HD
    for k in range(n_ctx):
        source = jnp.bitwise_xor(me, k)
        for p in range(per):
            buffer[source * per + p] = piece_refs[k][p]
    for sequence in range(pairs // heads):
        at = slice(sequence * PAIR, (sequence + 1) * PAIR)
        total = None
        for which in range(3):
            rows = jnp.concatenate(
                [
                    jnp.concatenate([buffer[pair, which, first, :], buffer[pair, which, second, :]], axis=0)
                    for pair in range(sequence * heads, (sequence + 1) * heads)
                ],
                axis=1,
            )
            if which == 2:
                rows = rows * valid_ref[at, :]
            grad_refs[which][at, :] = rows
            product = times_transposed(rows, weight_refs[which][...])
            total = product if total is None else total + product
        put_partial(partial_refs, sequence * PAIR, total.astype(BF), pairs // heads * PAIR // 4)


def project_in(scalars, pieces, weights, valid, pairs, n_ctx, split):
    depth, width = weights[0].shape
    rows = valid.shape[0]
    per = pieces[0].shape[0]
    shapes = [jax.ShapeDtypeStruct((rows, width), BF)] * 3 + partial_shapes(rows, depth, split)
    return pl.pallas_call(
        functools.partial(in_kernel, n_ctx, pairs),
        out_shape=shapes,
        grid_spec=pltpu.PrefetchScalarGridSpec(
            num_scalar_prefetch=1,
            grid=(1,),
            in_specs=[whole(piece.shape) for piece in pieces]
            + [whole(weight.shape) for weight in weights]
            + [whole(valid.shape)],
            out_specs=[whole(shape.shape) for shape in shapes],
            scratch_shapes=[pltpu.VMEM((per * n_ctx, 3, PAIR, HD), BF)],
        ),
        compiler_params=params(),
        cost_estimate=pl.CostEstimate(
            flops=6 * rows * depth * width, bytes_accessed=rows * depth * 2 + 6 * depth * width, transcendentals=0
        ),
    )(scalars, *pieces, *weights, valid)


def both_places(me, k, n_ctx):
    source = jnp.bitwise_xor(me, k)
    front = pl.multiple_of(source * BLOCK, BLOCK)
    back = pl.multiple_of((2 * n_ctx - 1 - source) * BLOCK, BLOCK)
    return pl.ds(front, BLOCK), pl.ds(back, BLOCK)


def attention_kernel(n_ctx, tile, scalar_ref, *refs):
    x_refs, o_refs, (qs, ks, vs, os) = refs[:n_ctx], refs[n_ctx : 2 * n_ctx], refs[2 * n_ctx :]
    me = scalar_ref[0]
    length = 2 * n_ctx * BLOCK
    for k in range(n_ctx):
        front, back = both_places(me, k, n_ctx)
        for which, dest in enumerate((qs, ks, vs)):
            dest[front, :] = x_refs[k][0, which, :BLOCK, :]
            dest[back, :] = x_refs[k][0, which, BLOCK:, :]
    factor = -(HD ** (-0.5)) * LOG2E
    shift = math.log(length) * LOG2E
    row_at = lax.broadcasted_iota(jnp.int32, (tile, tile), 0)
    col_at = lax.broadcasted_iota(jnp.int32, (tile, tile), 1)
    for i in range(length // tile):
        query = qs[i * tile : (i + 1) * tile, :]

        def part(j, masked):
            at = pl.ds(pl.multiple_of(j * tile, tile), tile)
            raw = times_transposed(query, ks[at, :])
            prob = 1.0 / (1.0 + jnp.exp2(raw * factor + shift))
            if masked:
                prob = jnp.where(row_at >= col_at, prob, 0.0)
            return dot(prob.astype(BF), vs[at, :])

        total = part(i, True)
        if i > 0:
            total = lax.fori_loop(0, i, lambda j, acc: acc + part(j, False), total)
        os[i * tile : (i + 1) * tile, :] = total.astype(BF)
    for k in range(n_ctx):
        front, back = both_places(me, k, n_ctx)
        o_refs[k][0, :BLOCK, :] = os[front, :]
        o_refs[k][0, BLOCK:, :] = os[back, :]


def attention_forward(scalars, pieces, n_ctx):
    pairs = pieces[0].shape[0]
    length = 2 * n_ctx * BLOCK
    tile = min(512, length)
    return pl.pallas_call(
        functools.partial(attention_kernel, n_ctx, tile),
        out_shape=[jax.ShapeDtypeStruct((pairs, PAIR, HD), BF)] * n_ctx,
        grid_spec=pltpu.PrefetchScalarGridSpec(
            num_scalar_prefetch=1,
            grid=(pairs,),
            in_specs=[pl.BlockSpec((1, 3, PAIR, HD), lambda i, s: (i, 0, 0, 0))] * n_ctx,
            out_specs=[pl.BlockSpec((1, PAIR, HD), lambda i, s: (i, 0, 0))] * n_ctx,
            scratch_shapes=[pltpu.VMEM((length, HD), BF)] * 4,
        ),
        compiler_params=params(),
        cost_estimate=pl.CostEstimate(
            flops=pairs * length * length * HD * 6,
            bytes_accessed=pairs * length * HD * 8,
            transcendentals=pairs * length * length,
        ),
    )(scalars, *pieces)


def attention_back_kernel(n_ctx, tile, scalar_ref, *refs):
    x_refs, g_refs, (cos_ref, sin_ref) = refs[:n_ctx], refs[n_ctx : 2 * n_ctx], refs[2 * n_ctx : 2 * n_ctx + 2]
    out_refs = refs[2 * n_ctx + 2 : 3 * n_ctx + 2]
    qs, ks, vs, gs, os, dqs = refs[3 * n_ctx + 2 :]
    me = scalar_ref[0]
    length = 2 * n_ctx * BLOCK
    for k in range(n_ctx):
        front, back = both_places(me, k, n_ctx)
        for which, dest in enumerate((qs, ks, vs)):
            dest[front, :] = x_refs[k][0, which, :BLOCK, :]
            dest[back, :] = x_refs[k][0, which, BLOCK:, :]
        gs[front, :] = g_refs[k][0, :BLOCK, :]
        gs[back, :] = g_refs[k][0, BLOCK:, :]
    scale = HD ** (-0.5)
    factor = -scale * LOG2E
    shift = math.log(length) * LOG2E
    count = length // tile
    key_at = lax.broadcasted_iota(jnp.int32, (tile, tile), 0)
    query_at = lax.broadcasted_iota(jnp.int32, (tile, tile), 1)
    dqs[...] = jnp.zeros_like(dqs)

    def unrotate(values, at):
        return (values * cos_ref[at, :] - pltpu.roll(values, HD // 2, 1) * sin_ref[at, :]).astype(BF)

    for j in range(count):
        own = slice(j * tile, (j + 1) * tile)
        keys = ks[own, :]
        values = vs[own, :]

        def part(i, masked):
            at = pl.ds(pl.multiple_of(i * tile, tile), tile)
            query = qs[at, :]
            grad = gs[at, :]
            raw = times_transposed(keys, query)
            prob = 1.0 / (1.0 + jnp.exp2(raw * factor + shift))
            if masked:
                prob = jnp.where(query_at >= key_at, prob, 0.0)
            prob_grad = times_transposed(values, grad)
            score_grad = (prob_grad * prob * (1.0 - prob)).astype(BF)
            dqs[at, :] += contract_rows(score_grad, keys)
            return dot(score_grad, query), dot(prob.astype(BF), grad)

        total = part(j, True)
        if j + 1 < count:

            def step(i, acc):
                more = part(i, False)
                return acc[0] + more[0], acc[1] + more[1]

            total = lax.fori_loop(j + 1, count, step, total)
        os[1, own, :] = unrotate(total[0] * scale, own)
        os[2, own, :] = total[1].astype(BF)
    for i in range(count):
        at = slice(i * tile, (i + 1) * tile)
        os[0, at, :] = unrotate(dqs[at, :] * scale, at)
    for k in range(n_ctx):
        front, back = both_places(me, k, n_ctx)
        for which in range(3):
            out_refs[k][0, which, :BLOCK, :] = os[which, front, :]
            out_refs[k][0, which, BLOCK:, :] = os[which, back, :]


def attention_backward(scalars, pieces, grads, cos_tab, sin_tab, n_ctx):
    pairs = pieces[0].shape[0]
    length = 2 * n_ctx * BLOCK
    tile = min(512, length)
    three = pl.BlockSpec((1, 3, PAIR, HD), lambda i, s: (i, 0, 0, 0))
    one = pl.BlockSpec((1, PAIR, HD), lambda i, s: (i, 0, 0))
    return pl.pallas_call(
        functools.partial(attention_back_kernel, n_ctx, tile),
        out_shape=[jax.ShapeDtypeStruct((pairs, 3, PAIR, HD), BF)] * n_ctx,
        grid_spec=pltpu.PrefetchScalarGridSpec(
            num_scalar_prefetch=1,
            grid=(pairs,),
            in_specs=[three] * n_ctx + [one] * n_ctx + [whole((length, HD))] * 2,
            out_specs=[three] * n_ctx,
            scratch_shapes=[pltpu.VMEM((length, HD), BF)] * 4
            + [pltpu.VMEM((3, length, HD), BF), pltpu.VMEM((length, HD), F32)],
        ),
        compiler_params=params(),
        cost_estimate=pl.CostEstimate(
            flops=pairs * length * length * HD * 12,
            bytes_accessed=pairs * length * HD * 14,
            transcendentals=pairs * length * length,
        ),
    )(scalars, *pieces, *grads, cos_tab, sin_tab)


def mlp_kernel(n_ref, g_ref, wg_ref, wu_ref, wd_ref, *rest):
    h_ref, dgp_ref, dup_ref = rest[-3:]
    rows = n_ref[...]
    gate_pre = dot(rows, wg_ref[...])
    up_pre = dot(rows, wu_ref[...])
    hidden_grad = times_transposed(g_ref[...], wd_ref[...])
    h_ref[...], dgp_ref[...], dup_ref[...] = feed_values(gate_pre, up_pre, hidden_grad)


def mlp_core(normed, grads, wg, wu, wd, total, first, held=()):
    rows, depth = normed.shape
    hidden = wg.shape[1]
    row_tile, tile = 512, 512
    skip = first // row_tile
    row_block = pl.BlockSpec((row_tile, depth), lambda j, i: (i, 0))
    out_block = pl.BlockSpec((row_tile, tile), lambda j, i: (i + skip, j))
    out = jax.ShapeDtypeStruct((total, hidden), BF)
    return pl.pallas_call(
        mlp_kernel,
        out_shape=(out, out, out),
        grid=(hidden // tile, rows // row_tile),
        in_specs=[
            row_block,
            row_block,
            pl.BlockSpec((depth, tile), lambda j, i: (0, j)),
            pl.BlockSpec((depth, tile), lambda j, i: (0, j)),
            pl.BlockSpec((tile, depth), lambda j, i: (j, 0)),
        ]
        + [pl.BlockSpec(memory_space=pl.ANY)] * len(held),
        out_specs=(out_block, out_block, out_block),
        input_output_aliases={5 + k: k for k in range(len(held))},
        compiler_params=params(),
        cost_estimate=pl.CostEstimate(
            flops=6 * rows * depth * hidden,
            bytes_accessed=rows * depth * 4 + 6 * depth * hidden + 6 * rows * hidden,
            transcendentals=rows * hidden,
        ),
    )(normed, grads, wg, wu, wd, *held)


def inverse_rms(values):
    return lax.rsqrt(jnp.mean(values * values, axis=-1, keepdims=True) + EPS)


def neighbours():
    index, rank = lax.axis_index("ctx"), lax.axis_index("tp")
    return (index, jnp.bitwise_xor(rank, 1)), (index, jnp.bitwise_xor(rank, 2))


def remote(source, dest, send_sem, recv_sem, device):
    return pltpu.make_async_remote_copy(
        src_ref=source,
        dst_ref=dest,
        send_sem=send_sem,
        recv_sem=recv_sem,
        device_id=device,
        device_id_type=pl.DeviceIdType.MESH,
    )


def signal(sem, device):
    pl.semaphore_signal(sem, inc=1, device_id=device, device_id_type=pl.DeviceIdType.MESH)


class Scatter:
    def __init__(self, partial, groups, bufs, sems, loaded=True):
        self.partial, self.groups, self.loaded = partial, groups, loaded
        self.from_x, self.from_y, self.for_y, self.for_x, self.low, self.high = bufs[:6]
        if loaded:
            self.stay, self.stay_y, self.stay_x = bufs[6:]
        self.first_send, self.first_recv, self.second_send, self.second_recv, self.load_sem = sems
        self.to_x, self.to_y = neighbours()

    @staticmethod
    def scratch(rows, width, loaded=True):
        dma = pltpu.SemaphoreType.DMA
        whole_rows, half_rows = pltpu.VMEM((rows, width), BF), pltpu.VMEM((rows // 2, width), BF)
        bufs = [whole_rows] * 2 + [half_rows] * 4 + ([whole_rows] + [half_rows] * 2 if loaded else [])
        return bufs + [dma((8,)), dma((8,)), dma((4,)), dma((4,)), dma((6,))]

    def piece(self, g, number):
        base, rows, own = self.groups[g]
        half = rows // 2
        if not self.loaded:
            return self.partial[pl.ds(base + number * half, half), :]
        if number < 2:
            return self.stay[pl.ds(own + number * half, half), :]
        return (self.stay_x if number == 3 else self.stay_y)[pl.ds(own // 2, half), :]

    def first_copies(self, g):
        base, rows, own = self.groups[g]
        half = rows // 2
        part = lambda number: self.partial.at[pl.ds(base + number * half, half)]
        at = lambda buf, number: buf.at[pl.ds(own + number * half, half)]
        plan = [
            (part(2), at(self.from_x, 0), self.to_x),
            (part(6), at(self.from_x, 1), self.to_x),
            (part(5), at(self.from_y, 0), self.to_y),
            (part(7), at(self.from_y, 1), self.to_y),
        ]
        return [
            remote(source, dest, self.first_send.at[4 * g + k], self.first_recv.at[4 * g + k], device)
            for k, (source, dest, device) in enumerate(plan)
        ]

    def loads(self, g):
        base, rows, own = self.groups[g]
        half = rows // 2
        copy = lambda number, count, dest, k: pltpu.make_async_copy(
            self.partial.at[pl.ds(base + number * half, count)], dest, self.load_sem.at[3 * g + k]
        )
        return [
            copy(0, rows, self.stay.at[pl.ds(own, rows)], 0),
            copy(4, half, self.stay_y.at[pl.ds(own // 2, half)], 1),
            copy(3, half, self.stay_x.at[pl.ds(own // 2, half)], 2),
        ]

    def second_copies(self, g):
        _, rows, own = self.groups[g]
        at = pl.ds(own // 2, rows // 2)
        return [
            remote(self.for_y.at[at], self.low.at[at], self.second_send.at[2 * g], self.second_recv.at[2 * g], self.to_y),
            remote(
                self.for_x.at[at], self.high.at[at], self.second_send.at[2 * g + 1], self.second_recv.at[2 * g + 1], self.to_x
            ),
        ]

    def start(self, g, which=(1, 3, 0, 2), loads=True):
        copies = self.first_copies(g)
        for k in which:
            copies[k].start()
        if loads:
            for copy in self.loads(g):
                copy.start()

    def forward(self, g):
        _, rows, own = self.groups[g]
        half = rows // 2
        copies = self.first_copies(g)
        copies[1].wait_recv()
        copies[3].wait_recv()
        if self.loaded:
            for copy in self.loads(g):
                copy.wait()
        at = pl.ds(own // 2, half)
        self.for_y[at, :] = add_low(self.piece(g, 4), self.from_x[pl.ds(own + half, half), :])
        self.for_x[at, :] = add_low(self.piece(g, 3), self.from_y[pl.ds(own + half, half), :])
        for copy in self.second_copies(g):
            copy.start()

    def total(self, g, use):
        _, rows, own = self.groups[g]
        half = rows // 2
        copies, seconds = self.first_copies(g), self.second_copies(g)
        copies[0].wait_recv()
        copies[2].wait_recv()
        for copy in copies:
            copy.wait_send()
        for copy in seconds:
            copy.wait()
        first = pl.ds(own, half)
        rest = pl.ds(own // 2, half)
        for side, (got, more) in enumerate(((self.from_x, self.low), (self.from_y, self.high))):
            at = pl.ds(own + side * half, half)
            use(at, self.piece(g, side).astype(F32) + got[first, :].astype(F32) + more[rest, :].astype(F32))


class Gather:
    def __init__(self, own, out, groups, sems, local=True, via=None):
        self.own, self.out, self.groups, self.has_local, self.via = own, out, groups, local, via
        self.first_send, self.first_recv, self.second_send, self.second_recv, self.local_sem, self.via_sem = sems
        self.to_x, self.to_y = neighbours()

    @staticmethod
    def scratch():
        dma = pltpu.SemaphoreType.DMA
        return [dma((4,)), dma((4,)), dma((4,)), dma((4,)), dma((2,)), dma((4,))]

    def first_copies(self, g):
        base, rows, own = self.groups[g]
        source = self.own.at[pl.ds(own, rows)]
        place = lambda k: self.out.at[pl.ds(base + k * rows, rows)]
        return [
            remote(source, place(1), self.first_send.at[2 * g], self.first_recv.at[2 * g], self.to_x),
            remote(source, place(2), self.first_send.at[2 * g + 1], self.first_recv.at[2 * g + 1], self.to_y),
        ]

    def local(self, g):
        base, rows, own = self.groups[g]
        return pltpu.make_async_copy(self.own.at[pl.ds(own, rows)], self.out.at[pl.ds(base, rows)], self.local_sem.at[g])

    def second_copies(self, g):
        base, rows, own = self.groups[g]
        half = rows // 2
        part = lambda number: self.out.at[pl.ds(base + number * half, half)]
        if self.via is None:
            low, high = part(4), part(3)
        else:
            low, high = (self.via.at[pl.ds(own + k * half, half)] for k in range(2))
        return [
            remote(low, part(6), self.second_send.at[2 * g], self.second_recv.at[2 * g], self.to_x),
            remote(high, part(7), self.second_send.at[2 * g + 1], self.second_recv.at[2 * g + 1], self.to_y),
        ]

    def pass_on(self, g, which):
        if self.via is not None:
            base, rows, own = self.groups[g]
            half = rows // 2
            load = pltpu.make_async_copy(
                self.out.at[pl.ds(base + (4 - which) * half, half)],
                self.via.at[pl.ds(own + which * half, half)],
                self.via_sem.at[2 * g + which],
            )
            load.start()
            load.wait()
        self.second_copies(g)[which].start()

    def start(self, g):
        for copy in self.first_copies(g):
            copy.start()
        if self.has_local:
            self.local(g).start()

    def forward_x(self, g):
        self.first_copies(g)[0].wait_recv()
        self.pass_on(g, 1)

    def forward_y(self, g):
        self.first_copies(g)[1].wait_recv()
        self.pass_on(g, 0)

    def forward(self, g):
        self.forward_x(g)
        self.forward_y(g)
        if self.has_local:
            self.local(g).wait()

    def finish(self, g):
        for copy in self.second_copies(g):
            copy.wait_recv()

    def sent(self, g):
        for copy in self.first_copies(g) + self.second_copies(g):
            copy.wait_send()


TILE, ROWS = 128, 64
CORE_SLOTS, HOP_SLOTS = 4, 4


class Ring:
    def __init__(self, slots, send_sem, recv_sem, credit, total):
        self.slots, self.send_sem, self.recv_sem, self.credit, self.total = slots, send_sem, recv_sem, credit, total
        self.count = slots.shape[0]

    def copy(self, source, at, send_at, device):
        slot = lax.rem(at, self.count)
        return pltpu.make_async_remote_copy(
            src_ref=source,
            dst_ref=self.slots.at[slot],
            send_sem=self.send_sem.at[send_at],
            recv_sem=self.recv_sem.at[slot],
            device_id=device,
            device_id_type=pl.DeviceIdType.MESH,
        )

    def send(self, source, at, send_at, device):
        @pl.when(at >= self.count)
        def _():
            pl.semaphore_wait(self.credit, 1)

        self.copy(source, at, send_at, device).start()

    def sent(self, source, at, send_at, device):
        self.copy(source, at, send_at, device).wait_send()

    def arrived(self, source, at, send_at, device):
        self.copy(source, at, send_at, device).wait_recv()
        return self.slots.at[lax.rem(at, self.count)]

    def free(self, at, device):
        @pl.when(at + self.count < self.total)
        def _():
            pl.semaphore_signal(self.credit, inc=1, device_id=device, device_id_type=pl.DeviceIdType.MESH)


def sums_kernel(n_ctx, items, n_right, n_extra, tasks, late, *refs):
    n_left = len(items)
    made = items[0][3]
    n_held = n_left - (1 if made else 0)
    left_refs, right_refs = refs[:n_held], refs[n_held : n_held + n_right]
    left_refs = ((None,) if made else ()) + tuple(left_refs)
    refs = refs[n_held + n_right :]
    extra_in, refs = refs[: n_extra[0]], refs[n_extra[0] :]
    out_refs, extra_out, refs = refs[:n_left], refs[n_left : n_left + n_extra[1]], refs[n_left + n_extra[1] :]
    extra_scratch, refs = refs[: n_extra[2]], refs[n_extra[2] :]
    right_refs = list(right_refs) + [extra_out[k] for k in late]
    n_right += len(late)
    (
        left_buf, right_buf, other_buf, ring, core_in, hop_in, hop_mid, hop_out, core_out,
        left_sem, right_sem, core_send, core_recv, in_send, in_recv, mid_send, mid_recv, out_send, out_recv,
        fin_send, fin_recv, store_sem, core_credit, in_credit, mid_credit, out_credit, fin_credit,
    ) = refs
    starts = [0]
    for _, _, chunks, _ in items:
        starts.append(starts[-1] + chunks)
    total = starts[-1]
    n_ring = ring.shape[0]
    chips = n_ctx // 2
    mid = chips // 2
    index = lax.axis_index("ctx")
    rank = lax.axis_index("tp")
    core = lax.rem(index, 2)
    chip = index // 2
    low_side = chip < mid
    place = jnp.where(low_side, chip, chips - 1 - chip)
    toward = jnp.where(low_side, 1, -1)
    partner = (chip * 2 + 1 - core, rank)
    after = ((chip + toward) * 2 + core, rank)
    before = ((chip - toward) * 2 + core, rank)
    is_first = place == 0
    is_last = place == mid - 1
    lag_t = mid
    lag_u = lag_t + 2
    lag_o = lag_u + 2 * (mid - 1)
    lag_f = lag_o + 1
    lag_w = lag_f + 1

    to_core = Ring(core_in, core_send, core_recv, core_credit, total)
    to_after = Ring(hop_in, in_send, in_recv, in_credit, total)
    across = Ring(hop_mid, mid_send, mid_recv, mid_credit, total)
    to_before = Ring(hop_out, out_send, out_recv, out_credit, total)
    to_final = Ring(core_out, fin_send, fin_recv, fin_credit, total)

    def right_copy(k):
        return pltpu.make_async_copy(right_refs[k], right_buf.at[k % 2], right_sem.at[k % 2])

    right_copy(0).start()

    def for_item(at, action):
        for number in range(n_left):
            @pl.when((at >= starts[number]) & (at < starts[number + 1]))
            def _(number=number):
                action(number, at - starts[number])

    def rows_at(number, chunk, side):
        half = items[number][2] * ROWS
        return pl.multiple_of(side * half + chunk * ROWS, ROWS)

    def left_copy(number, chunk, slot, which):
        side = core if which == 0 else 1 - core
        half = items[number][2] * ROWS
        return pltpu.make_async_copy(
            left_refs[number].at[:, pl.ds(pl.multiple_of(side * half + chunk // 2 * TILE, TILE), TILE)],
            left_buf.at[slot, :, pl.ds(which * TILE, TILE)],
            left_sem.at[slot, which],
        )

    def load_left(at):
        def action(number, chunk):
            if number == 0 and made:
                maker.load(chunk // 2)
                return
            if number == 1 and made:

                @pl.when(chunk == 0)
                def _():
                    maker.release()

            for which in range(2):
                left_copy(number, chunk, lax.rem(at // 2, 2), which).start()

        for_item(at, action)

    planned, each, maker = tasks(extra_in, extra_out, extra_scratch) if tasks is not None else ({}, None, None)
    if made:
        maker.begin(left_buf, right_buf)
    load_left(0)
    if n_right > 1 and not made:
        right_copy(1).start()
    if tasks is not None:
        greet(n_ctx, True)
    else:
        barrier = pltpu.get_barrier_semaphore()
        pl.semaphore_signal(barrier, inc=1, device_id=partner, device_id_type=pl.DeviceIdType.MESH)

        @pl.when(chip > 0)
        def _():
            pl.semaphore_signal(
                barrier, inc=1, device_id=((chip - 1) * 2 + core, rank), device_id_type=pl.DeviceIdType.MESH
            )

        @pl.when(chip < chips - 1)
        def _():
            pl.semaphore_signal(
                barrier, inc=1, device_id=((chip + 1) * 2 + core, rank), device_id_type=pl.DeviceIdType.MESH
            )

        pl.semaphore_wait(barrier, 1 + jnp.where(chip > 0, 1, 0) + jnp.where(chip < chips - 1, 1, 0))
    if 0 in planned:
        planned.pop(0)()
    right_copy(0).wait()

    def step(i, carry):
        def at_lag(lag):
            at = i - lag
            return at, (at >= 0) & (at < total)

        at, now = at_lag(lag_w)

        @pl.when(now)
        def _():
            slot = lax.rem(at, n_ring)
            source = ring.at[slot]

            def action(number, chunk):
                store(number, chunk, at, 0).wait()
                store(number, chunk, at, 1).wait()

            for_item(at, action)
            to_final.sent(source, at, slot, partner)
            to_final.free(at, partner)

            @pl.when(jnp.logical_not(is_first))
            def _():
                to_before.sent(source, at, slot, before)

        at, now = at_lag(lag_o)

        @pl.when(now & jnp.logical_not(is_last))
        def _():
            slot = lax.rem(at, n_ring)
            source = ring.at[slot]
            to_after.sent(source, at, slot, after)
            got = to_before.arrived(source, at, slot, after)
            ring[slot] = got[...]
            to_before.free(at, after)

            @pl.when(jnp.logical_not(is_first))
            def _():
                to_before.send(source, at, slot, before)

        @pl.when(now)
        def _():
            slot = lax.rem(at, n_ring)
            to_final.send(ring.at[slot], at, slot, partner)

        at, now = at_lag(lag_u)

        @pl.when(now & is_last)
        def _():
            slot = lax.rem(at, n_ring)
            source = ring.at[slot]
            across.sent(source, at, slot, after)
            got = across.arrived(source, at, slot, after)
            ring[slot] = add_low(ring[slot], got[...])
            across.free(at, after)

            @pl.when(jnp.logical_not(is_first))
            def _():
                to_before.send(source, at, slot, before)

        at, now = at_lag(lag_t)

        @pl.when(now)
        def _():
            slot = lax.rem(at, n_ring)
            source = ring.at[slot]

            @pl.when(jnp.logical_not(is_first))
            def _():
                got = to_after.arrived(source, at, slot, before)
                ring[slot] = add_low(ring[slot], got[...])
                to_after.free(at, before)

            @pl.when(is_last)
            def _():
                across.send(source, at, slot, after)

            @pl.when(jnp.logical_not(is_first) & jnp.logical_not(is_last))
            def _():
                to_after.send(source, at, slot, after)

        at, now = at_lag(1)

        @pl.when(now)
        def _():
            slot = lax.rem(at, n_ring)
            source = ring.at[slot]
            own = other_buf.at[lax.rem(at, 4)]
            to_core.sent(own, at, lax.rem(at, 4), partner)
            got = to_core.arrived(own, at, lax.rem(at, 4), partner)
            ring[slot] = add_low(ring[slot], got[...])
            to_core.free(at, partner)

            @pl.when(is_first & jnp.logical_not(is_last))
            def _():
                to_after.send(source, at, slot, after)

        at, now = at_lag(lag_f)

        @pl.when(now)
        def _():
            slot = lax.rem(at, n_ring)
            to_final.arrived(ring.at[slot], at, slot, partner)

            def action(number, chunk):
                store(number, chunk, at, 0).start()
                store(number, chunk, at, 1).start()

            for_item(at, action)

        for when, task in planned.items():
            pl.when(i == when)(task)

        if each is not None:
            each(i)

        @pl.when((i + 2 < total) & (lax.rem(i, 2) == 0))
        def _():
            load_left(i + 2)

        @pl.when((i < total) & (lax.rem(i, 2) == 0))
        def _():
            slot = lax.rem(i // 2, 2)

            def action(number, chunk):
                which_right = items[number][1]
                if which_right > 0 and items[number - 1][1] != which_right:

                    @pl.when(chunk == 0)
                    def _():
                        if made and which_right in (1, n_right - 1):
                            right_copy(which_right).start()
                        right_copy(which_right).wait()

                if which_right > 0 and which_right + 1 < n_right - (1 if made else 0):

                    @pl.when(chunk == items[number][2] // 2)
                    def _():
                        right_copy(which_right + 1).start()

                if number == 0 and made:
                    maker.make(chunk // 2)
                else:
                    for which in range(2):
                        left_copy(number, chunk, slot, which).wait()
                right = right_buf.at[which_right % 2]
                product = contract_rows(left_buf[slot], right[...]).astype(BF)
                for part in range(2):
                    place = lax.rem(i + part, 4)
                    other_buf[place] = product[TILE + part * ROWS : TILE + (part + 1) * ROWS]
                    to_core.send(other_buf.at[place], i + part, place, partner)
                    ring[lax.rem(i + part, n_ring)] = product[part * ROWS : (part + 1) * ROWS]

            for_item(i, action)

        return carry

    def store(number, chunk, at, which):
        source = ring.at[lax.rem(at, n_ring)] if which == 0 else core_out.at[lax.rem(at, CORE_SLOTS)]
        side = core if which == 0 else 1 - core
        return pltpu.make_async_copy(
            source,
            out_refs[number].at[pl.ds(rows_at(number, chunk, side), ROWS), :],
            store_sem.at[which, lax.rem(at, 2)],
        )

    lax.fori_loop(0, total + lag_w, step, 0)


def weight_sums(items, rights, n_ctx, collective_id, extra=None, late=(), limit=VMEM_LIMIT):
    tokens, width = rights[0].shape
    columns = [left if isinstance(left, int) else left.shape[1] for left, _ in items]
    held = [left for left, _ in items if not isinstance(left, int)]
    shapes = [
        (k, right, columns[k] // 2 // ROWS, isinstance(left, int)) for k, (left, right) in enumerate(items)
    ]
    mid = n_ctx // 4
    n_ring = mid + 2 + 2 * (mid - 1) + 4
    any_spec = pl.BlockSpec(memory_space=pl.ANY)
    args, arg_specs, outs, out_specs, scratch, tasks = extra if extra is not None else ([], [], [], [], [], None)
    counts = (len(args), len(outs), len(scratch))
    chunk = (ROWS, width)
    dma = pltpu.SemaphoreType.DMA
    return pl.pallas_call(
        functools.partial(sums_kernel, n_ctx, shapes, len(rights), counts, tasks, late),
        out_shape=[jax.ShapeDtypeStruct((count, width), BF) for count in columns] + outs,
        in_specs=[any_spec] * (len(held) + len(rights)) + arg_specs,
        out_specs=[any_spec] * len(items) + out_specs,
        scratch_shapes=scratch
        + [
            pltpu.VMEM((2, tokens, 2 * TILE), BF),
            pltpu.VMEM((min(2, len(rights) + len(late)), tokens, width), BF),
            pltpu.VMEM((4,) + chunk, BF),
            pltpu.VMEM((n_ring,) + chunk, BF),
            pltpu.VMEM((CORE_SLOTS,) + chunk, BF),
            pltpu.VMEM((HOP_SLOTS,) + chunk, BF),
            pltpu.VMEM((HOP_SLOTS,) + chunk, BF),
            pltpu.VMEM((HOP_SLOTS,) + chunk, BF),
            pltpu.VMEM((CORE_SLOTS,) + chunk, BF),
            dma((2, 2)),
            dma((2,)),
            dma((4,)),
            dma((CORE_SLOTS,)),
            dma((n_ring,)),
            dma((HOP_SLOTS,)),
            dma((n_ring,)),
            dma((HOP_SLOTS,)),
            dma((n_ring,)),
            dma((HOP_SLOTS,)),
            dma((n_ring,)),
            dma((CORE_SLOTS,)),
            dma((2, 2)),
        ]
        + [pltpu.SemaphoreType.REGULAR] * 5,
        compiler_params=pltpu.CompilerParams(
            vmem_limit_bytes=limit, collective_id=collective_id, has_side_effects=True
        ),
        cost_estimate=pl.CostEstimate(
            flops=sum(2 * count * tokens * width for count in columns),
            bytes_accessed=sum(2 * count * (tokens + width) for count in columns),
            transcendentals=0,
        ),
    )(*held, *rights, *args)


VMEM_SPEC = pl.BlockSpec(memory_space=pltpu.VMEM)
ANY_SPEC = pl.BlockSpec(memory_space=pl.ANY)


def norm_back_rows(values, gain, grad):
    inv = inverse_rms(values)
    unit = values * inv
    scaled = grad * gain
    back = (scaled - unit * jnp.mean(scaled * unit, axis=-1, keepdims=True)) * inv
    return back, jnp.sum(grad * unit, axis=0, keepdims=True)


def own_copies(ref, buf, groups, sem):
    odd = lax.rem(lax.axis_index("tp"), 2)
    starts = [pl.multiple_of(odd * BLOCK, BLOCK), pl.multiple_of((1 - odd) * PAIR, BLOCK)]
    return [
        pltpu.make_async_copy(ref.at[pl.ds(start, rows)], buf.at[pl.ds(own, rows)], sem.at[g])
        for g, (start, (_, rows, own)) in enumerate(zip(starts, groups))
    ]


class Maker:
    def __init__(self, refs, outs, weights, downs, stage, sems):
        self.n2_ref, self.wg_ref, self.wu_ref, self.wd_ref = refs
        self.h_out, self.dgp_out, self.dup_out = outs
        self.weights, self.downs, self.stage = weights, downs, stage
        self.n2_sem, self.weight_sem, self.h_sem, self.grad_sem = sems
        self.core = lax.rem(lax.axis_index("ctx"), 2)
        self.half = self.h_out.shape[1] // 2
        self.tiles = self.half // TILE

    def first(self, tile, which):
        side = self.core if which == 0 else 1 - self.core
        return pl.multiple_of(side * self.half + tile * TILE, TILE)

    def copies(self, tile):
        slot = lax.rem(tile, 2)
        deep = self.weights.shape[1]
        made = []
        for which in range(2):
            at = pl.ds(self.first(tile, which), TILE)
            for kind, ref in enumerate((self.wg_ref, self.wu_ref)):
                to = pl.multiple_of((slot * 2 + kind) * 2 * TILE + which * TILE, TILE)
                for part in range(2):
                    made.append((ref.at[pl.ds(part * deep, deep), at], self.weights.at[part, :, pl.ds(to, TILE)]))
            made.append((self.wd_ref.at[at], self.downs.at[slot, 0, pl.ds(which * TILE, TILE)]))
        return [
            pltpu.make_async_copy(source, dest, self.weight_sem.at[slot, k]) for k, (source, dest) in enumerate(made)
        ]

    def load(self, tile):
        for copy in self.copies(tile):
            copy.start()

    def begin(self, left_buf, right_buf):
        self.left_buf, self.right_buf = left_buf, right_buf
        self.n2_copy().start()

    def n2_copy(self):
        return pltpu.make_async_copy(self.n2_ref, self.right_buf.at[1], self.n2_sem)

    def h_stores(self, tile):
        slot = lax.rem(tile, 2)
        return [
            pltpu.make_async_copy(
                self.left_buf.at[slot, :, pl.ds(which * TILE, TILE)],
                self.h_out.at[:, pl.ds(self.first(tile, which), TILE)],
                self.h_sem.at[slot, which],
            )
            for which in range(2)
        ]

    def grad_stores(self, tile):
        return [
            pltpu.make_async_copy(
                self.stage.at[kind, :, pl.ds(which * TILE, TILE)],
                out.at[:, pl.ds(self.first(tile, which), TILE)],
                self.grad_sem.at[kind, which],
            )
            for kind, out in enumerate((self.dgp_out, self.dup_out))
            for which in range(2)
        ]

    def make(self, tile):
        slot = lax.rem(tile, 2)
        deep = self.weights.shape[1]

        @pl.when(tile == 0)
        def _():
            self.n2_copy().wait()

        @pl.when(tile > 0)
        def _():
            for copy in self.grad_stores(tile - 1):
                copy.wait()

        @pl.when(tile > 1)
        def _():
            for copy in self.h_stores(tile - 2):
                copy.wait()

        for copy in self.copies(tile):
            copy.wait()
        at_gate = pl.ds(pl.multiple_of(slot * 4 * TILE, TILE), 2 * TILE)
        at_up = pl.ds(pl.multiple_of((slot * 4 + 2) * TILE, TILE), 2 * TILE)
        count = 512

        def rows_step(step, carry):
            rows = pl.ds(pl.multiple_of(step * count, count), count)
            low, high = self.right_buf[1, rows, :deep], self.right_buf[1, rows, deep:]
            gate_pre = dot(low, self.weights[0, :, at_gate]) + dot(high, self.weights[1, :, at_gate])
            up_pre = dot(low, self.weights[0, :, at_up]) + dot(high, self.weights[1, :, at_up])
            hidden_grad = times_transposed(self.right_buf[0, rows, :], self.downs[slot, 0])
            h, dgp, dup = feed_values(gate_pre, up_pre, hidden_grad)
            self.left_buf[slot, rows, :] = h
            self.stage[0, rows, :] = dgp
            self.stage[1, rows, :] = dup
            return carry

        lax.fori_loop(0, self.right_buf.shape[1] // count, rows_step, 0)
        for copy in self.h_stores(tile) + self.grad_stores(tile):
            copy.start()

    def release(self):
        for copy in self.h_stores(self.tiles - 2):
            copy.wait()

    def finish(self):
        for copy in self.h_stores(self.tiles - 1) + self.grad_stores(self.tiles - 1):
            copy.wait()


def feed_values(gate_pre, up_pre, hidden_grad):
    gate_sig = 1.0 / (1.0 + jnp.exp2(gate_pre * (-LOG2E)))
    gate_act = gate_pre * gate_sig
    return (
        (gate_act * up_pre).astype(BF),
        (hidden_grad * up_pre * (gate_sig * (1.0 + gate_pre * (1.0 - gate_sig)))).astype(BF),
        (hidden_grad * gate_act).astype(BF),
    )


def feed_tasks(groups, extra_in, extra_out, scratch):
    n2_ref, wg_ref, wu_ref, wd_ref, residual, cot_ref, gain = extra_in
    dr, da_all, gain_grad, d_ref, h_ref, dgp_ref, dup_ref = extra_out
    n = len(Scatter.scratch(16, 128))
    bufs, rest = scratch[:n], scratch[n:]
    weights, lefts, tile_out, weight_sem, left_sem, out_sem = rest[:6]
    grads, stage, own_sem, n2_sem, make_sem, h_sem, grad_sem = rest[6:13]
    da_own = bufs[0]
    scatter = Scatter(d_ref, groups, bufs[:9], bufs[9:])
    gather = Gather(da_own, da_all, groups, rest[13:], via=bufs[1])
    maker = Maker(
        (n2_ref, wg_ref, wu_ref, wd_ref),
        (h_ref, dgp_ref, dup_ref),
        weights,
        lefts,
        stage,
        (n2_sem, make_sem, h_sem, grad_sem),
    )
    order = list(reversed(range(len(groups))))
    rows, columns = lefts.shape[2], weights.shape[1]
    row_tiles = dgp_ref.shape[0] // rows
    tiles = row_tiles * (d_ref.shape[1] // columns)
    after = maker.half // ROWS
    shift = after + 1

    def weight_copies(part):
        at = pl.ds(pl.multiple_of(part * columns, columns), columns)
        return [
            pltpu.make_async_copy(ref.at[at], weights.at[k], weight_sem.at[k]) for k, ref in enumerate((wg_ref, wu_ref))
        ]

    def left_copies(tile):
        at = pl.ds(pl.multiple_of(lax.rem(tile, row_tiles) * rows, rows), rows)
        slot = lax.rem(tile, 2)
        return [
            pltpu.make_async_copy(ref.at[at], lefts.at[slot, k], left_sem.at[slot, k])
            for k, ref in enumerate((dgp_ref, dup_ref))
        ]

    def out_copy(tile):
        slot = lax.rem(tile, 2)
        return pltpu.make_async_copy(
            tile_out.at[slot],
            d_ref.at[
                pl.ds(pl.multiple_of(lax.rem(tile, row_tiles) * rows, rows), rows),
                pl.ds(pl.multiple_of(tile // row_tiles * columns, columns), columns),
            ],
            out_sem.at[slot],
        )

    def begin():
        gain_grad[...] = jnp.zeros_like(gain_grad)
        for copy in own_copies(cot_ref, grads, groups, own_sem):
            copy.start()

    def whole_hidden():
        maker.finish()
        for copy in weight_copies(0) + left_copies(0):
            copy.start()

    def each(step):
        i = step - shift

        @pl.when((i >= 0) & (i < tiles))
        def _():
            slot = lax.rem(i, 2)

            @pl.when(i + 1 < tiles)
            def _():
                for copy in left_copies(i + 1):
                    copy.start()

            @pl.when(lax.rem(i, row_tiles) == 0)
            def _():
                @pl.when(i > 0)
                def _():
                    for copy in weight_copies(i // row_tiles):
                        copy.start()

                for copy in weight_copies(i // row_tiles):
                    copy.wait()

            for copy in left_copies(i):
                copy.wait()
            total = times_transposed(lefts[slot, 0], weights[0]) + times_transposed(lefts[slot, 1], weights[1])

            @pl.when(i >= 2)
            def _():
                out_copy(i - 2).wait()

            tile_out[slot] = total.astype(BF)
            out_copy(i).start()

    def start():
        out_copy(tiles - 2).wait()
        out_copy(tiles - 1).wait()
        for copy in own_copies(cot_ref, grads, groups, own_sem):
            copy.wait()
        for g in order:
            scatter.start(g)

    def use(at, total):
        back, more = norm_back_rows(residual[at, :], gain[...].astype(F32), total)
        total_grad = grads[at, :].astype(F32) + back
        dr[at, :] = total_grad
        da_own[at, :] = total_grad.astype(BF)
        gain_grad[...] += more

    def spread(g):
        scatter.total(g, use)
        gather.start(g)

    def finish():
        for g in order:
            gather.finish(g)
            gather.sent(g)

    first = shift + tiles
    plan = {
        0: begin,
        after: whole_hidden,
        first: start,
        first + 3: lambda: scatter.forward(order[0]),
        first + 6: lambda: scatter.forward(order[-1]),
        first + 7: lambda: spread(order[0]),
        first + 9: lambda: spread(order[-1]),
        first + 11: lambda: gather.forward(order[0]),
        first + 15: lambda: gather.forward(order[-1]),
        first + 18: finish,
    }
    return plan, each, maker


def feed_extra(groups, n2, wg, wu, wd, residual, cot, gain):
    rows, width = residual.shape
    tokens, hidden = n2.shape[0], wg.shape[1]
    dma = pltpu.SemaphoreType.DMA
    outs = [
        jax.ShapeDtypeStruct((rows, width), F32),
        jax.ShapeDtypeStruct((tokens, width), BF),
        jax.ShapeDtypeStruct((1, width), F32),
        jax.ShapeDtypeStruct((tokens, width), BF),
    ] + [jax.ShapeDtypeStruct((tokens, hidden), BF)] * 3
    scratch = (
        Scatter.scratch(rows, width)
        + [
            pltpu.VMEM((2, width // 2, hidden), BF),
            pltpu.VMEM((2, 2, PAIR, hidden), BF),
            pltpu.VMEM((2, PAIR, width // 2), BF),
            dma((2,)),
            dma((2, 2)),
            dma((2,)),
            pltpu.VMEM((rows, width), BF),
            pltpu.VMEM((2, tokens, 2 * TILE), BF),
            dma((2,)),
            dma,
            dma((2, 10)),
            dma((2, 2)),
            dma((2, 2)),
        ]
        + Gather.scratch()
    )
    return (
        [n2, wg, wu, wd, residual, cot, gain],
        [ANY_SPEC] * 4 + [VMEM_SPEC, ANY_SPEC, VMEM_SPEC],
        outs,
        [VMEM_SPEC, ANY_SPEC, VMEM_SPEC] + [ANY_SPEC] * 4,
        scratch,
        functools.partial(feed_tasks, groups),
    )


def input_tasks(n_ctx, groups, extra_in, extra_out, scratch):
    i_ref, tokens_ref, dr, gain, gain_two_grad = extra_in
    input_grad, gain_sums = extra_out
    n = len(Scatter.scratch(16, 128))
    scatter = Scatter(i_ref, groups, scratch[:9], scratch[9:n])
    gains, got_tp, got_ctx, send_tp, recv_tp, send_ctx, recv_ctx, rows_in, own_sem = scratch[n:]
    order = list(reversed(range(len(groups))))
    me, rank = lax.axis_index("ctx"), lax.axis_index("tp")

    def tp_hop(k):
        return remote(gains.at[k], got_tp.at[k], send_tp.at[k], recv_tp.at[k], neighbours()[k])

    def ctx_hop(k):
        place = gains.at[2]
        return remote(place, got_ctx.at[k], send_ctx.at[k], recv_ctx.at[k], (jnp.bitwise_xor(me, k), rank))

    def begin():
        gains[0] = jnp.zeros(gains.shape[1:], F32)
        gains[0, 8:9, :] = gain_two_grad[...]
        for copy in own_copies(tokens_ref, rows_in, groups, own_sem):
            copy.start()
        for g in order:
            scatter.start(g)

    def forward_first():
        for copy in own_copies(tokens_ref, rows_in, groups, own_sem):
            copy.wait()
        scatter.forward(order[0])

    def use(at, total):
        back, more = norm_back_rows(rows_in[at, :].astype(F32), gain[...].astype(F32), total)
        input_grad[at, :] = (dr[at, :] + back).astype(BF)
        gains[0, 0:1, :] += more

    def rest():
        scatter.total(order[-1], use)
        tp_hop(0).start()

    def second():
        tp_hop(0).wait()
        gains[1] = gains[0] + got_tp[0]
        tp_hop(1).start()

    def third():
        tp_hop(1).wait()
        gains[2] = gains[1] + got_tp[1]
        for k in range(1, n_ctx):
            ctx_hop(k).start()

    def finish():
        for k in range(1, n_ctx):
            ctx_hop(k).wait()
        got_ctx[0] = gains[2]
        total = got_ctx[jnp.bitwise_xor(me, 0)]
        for index in range(1, n_ctx):
            total = total + got_ctx[jnp.bitwise_xor(me, index)]
        gain_sums[...] = total

    return {
        0: begin,
        4: forward_first,
        9: lambda: scatter.forward(order[-1]),
        10: lambda: scatter.total(order[0], use),
        13: rest,
        15: second,
        17: third,
        20: finish,
    }, None, None


def input_extra(n_ctx, groups, i_partial, tokens_in, dr, gain, gain_two_grad):
    rows, width = tokens_in.shape
    dma = pltpu.SemaphoreType.DMA
    outs = [jax.ShapeDtypeStruct((rows, width), BF), jax.ShapeDtypeStruct((16, width), F32)]
    return (
        [i_partial, tokens_in, dr, gain, gain_two_grad],
        [ANY_SPEC] * 2 + [VMEM_SPEC] * 3,
        outs,
        [VMEM_SPEC] * 2,
        Scatter.scratch(rows, width)
        + [
            pltpu.VMEM((3, 16, width), F32),
            pltpu.VMEM((2, 16, width), F32),
            pltpu.VMEM((n_ctx, 16, width), F32),
            dma((2,)),
            dma((2,)),
            dma((n_ctx,)),
            dma((n_ctx,)),
            pltpu.VMEM((rows, width), BF),
            dma((2,)),
        ],
        functools.partial(input_tasks, n_ctx, groups),
    )


def cast_kernel(groups, *refs):
    out_in, gate_in, up_in, down_in, qkv_in = refs[:5]
    n_more = 3 if groups else 0
    more_in, refs = refs[5 : 5 + n_more], refs[5 + n_more :]
    for source, dest in zip((out_in, gate_in, up_in, down_in), refs[:4]):
        dest[...] = source[...].astype(F32)
    width = refs[4].shape[1]
    for k, dest in enumerate(refs[4:7]):
        dest[...] = qkv_in[:, k * width : (k + 1) * width].astype(F32)
    if not groups:
        return
    row_outs, gain_outs = refs[7:9], refs[9:11]
    gains = more_in[2]
    odd = lax.rem(lax.axis_index("tp"), 2)
    starts = (pl.multiple_of(odd * BLOCK, BLOCK), pl.multiple_of((1 - odd) * PAIR, BLOCK))

    @pl.when(pl.program_id(0) == 0)
    def _():
        gain_outs[0][...] = gains[0:1, :]
        gain_outs[1][...] = gains[8:9, :]
        for source, dest in zip(more_in[:2], row_outs):
            for start, (_, rows, own) in zip(starts, groups):
                dest[pl.ds(start, rows), :] = source[pl.ds(own, rows), :]


def cast_sums(sums, groups=(), rows=(), gains=None):
    steps = 16
    block = lambda array: pl.BlockSpec((array.shape[0] // steps, array.shape[1]), lambda i: (i, 0))
    outs = [jax.ShapeDtypeStruct(array.shape, F32) for array in sums[:-1]]
    outs += [jax.ShapeDtypeStruct((sums[-1].shape[0], sums[-1].shape[1] // 3), F32)] * 3
    in_specs, out_specs = [block(array) for array in sums], [block(array) for array in outs]
    args = list(sums)
    if groups:
        args += list(rows) + [gains]
        in_specs += [whole(array.shape) for array in (*rows, gains)]
        outs += [jax.ShapeDtypeStruct(array.shape, array.dtype) for array in rows]
        outs += [jax.ShapeDtypeStruct((1, gains.shape[1]), F32)] * 2
        out_specs += [whole(array.shape) for array in rows] + [whole((1, gains.shape[1]))] * 2
    return pl.pallas_call(
        functools.partial(cast_kernel, groups),
        out_shape=outs,
        grid=(steps,),
        in_specs=in_specs,
        out_specs=out_specs,
        compiler_params=params(),
        cost_estimate=pl.CostEstimate(
            flops=0, bytes_accessed=sum(6 * array.shape[0] * array.shape[1] for array in sums), transcendentals=0
        ),
    )(*args)


class Exchange:
    def __init__(self, dest, sems, by_device):
        self.dest, self.by_device = dest, by_device
        self.send_sem, self.recv_sem, self.own_sem = sems
        self.n_ctx = dest.shape[1]
        self.me, self.rank = lax.axis_index("ctx"), lax.axis_index("tp")

    @staticmethod
    def scratch(units, n_ctx):
        dma = pltpu.SemaphoreType.DMA
        return [dma((units, n_ctx)), dma((units, n_ctx)), dma((units,))]

    def copy(self, source, unit, k):
        other = jnp.bitwise_xor(self.me, k)
        place = other if self.by_device else k
        return remote(
            source.at[unit, place],
            self.dest.at[unit, k],
            self.send_sem.at[unit, k],
            self.recv_sem.at[unit, k],
            (other, self.rank),
        )

    def own(self, source, unit):
        place = self.me if self.by_device else 0
        return pltpu.make_async_copy(source.at[unit, place], self.dest.at[unit, 0], self.own_sem.at[unit])

    def start(self, source, unit):
        for k in reversed(range(1, self.n_ctx)):
            self.copy(source, unit, k).start()
        self.own(source, unit).start()

    def start_some(self, source, unit, first, count):
        for k in reversed(range(self.n_ctx)):
            other = jnp.bitwise_xor(self.me, k)

            @pl.when((other >= first) & (other < first + count))
            def _(k=k):
                if k == 0:
                    self.own(source, unit).start()
                else:
                    self.copy(source, unit, k).start()

    def arrived(self, source, unit):
        for k in range(1, self.n_ctx):
            self.copy(source, unit, k).wait_recv()
        self.own(source, unit).wait()

    def sent(self, source, unit):
        for k in range(1, self.n_ctx):
            self.copy(source, unit, k).wait_send()


def greet(n_ctx, tp_too):
    index, rank = lax.axis_index("ctx"), lax.axis_index("tp")
    barrier = pltpu.get_barrier_semaphore()
    for k in range(1, n_ctx):
        signal(barrier, (jnp.bitwise_xor(index, k), rank))
    if tp_too:
        for device in neighbours():
            signal(barrier, device)
    pl.semaphore_wait(barrier, n_ctx - 1 + (2 if tp_too else 0))


def rotation(cos_tab, sin_tab, block_cos, block_sin):
    sign = jnp.where(lax.broadcasted_iota(jnp.int32, cos_tab.shape, 1) < HD // 2, -1.0, 1.0)
    return cos_tab * block_cos - sin_tab * block_sin, (sin_tab * block_cos + cos_tab * block_sin) * sign


def in_turn(count):
    return [count - 1] + list(range(count - 1))


def attend_rows(qs, ks, vs, os, tile):
    length = qs.shape[0]
    factor = -(HD ** (-0.5)) * LOG2E
    shift = math.log(length) * LOG2E
    row_at = lax.broadcasted_iota(jnp.int32, (tile, tile), 0)
    col_at = lax.broadcasted_iota(jnp.int32, (tile, tile), 1)
    for i in range(length // tile):
        query = qs[i * tile : (i + 1) * tile, :]

        def part(j, masked):
            at = pl.ds(pl.multiple_of(j * tile, tile), tile)
            raw = times_transposed(query, ks[at, :])
            prob = 1.0 / (1.0 + jnp.exp2(raw * factor + shift))
            if masked:
                prob = jnp.where(row_at >= col_at, prob, 0.0)
            return dot(prob.astype(BF), vs[at, :])

        total = part(i, True)
        if i > 0:
            total = lax.fori_loop(0, i, lambda j, acc: acc + part(j, False), total)
        os[i * tile : (i + 1) * tile, :] = total.astype(BF)


def forward_kernel(n_ctx, groups, units, tile, *refs):
    tokens_ref, cot_ref, wq_in, wk_in, wv_in, wo_in, gain_one, gain_two = refs[:8]
    cos_ref, sin_ref, bcos_ref, bsin_ref, valid_ref = refs[8:13]
    n1_out, got_out, heads_out, residual, n2_out, cot_out = refs[13:19]
    x_ref, rows_buf, own_buf, send, got, o_send, o_got, tabs, qs, ks, vs, os = refs[19:31]
    (wq_ref, wk_ref, wv_ref, wo_ref, weight_sem, cot_buf, cot_via, cot_sem), rest = refs[31:39], refs[39:]
    n_gather, n_exchange = len(Gather.scratch()), len(Exchange.scratch(1, 2))
    n1_sems, rest = rest[:n_gather], rest[n_gather:]
    n2_sems, rest = rest[:n_gather], rest[n_gather:]
    cot_sems, rest = rest[:n_gather], rest[n_gather:]
    x_sems, rest = rest[:n_exchange], rest[n_exchange:]
    o_sems, rest = rest[:n_exchange], rest[n_exchange:]
    (n1_sem, got_sem, load_sem), rest = rest[:3], rest[3:]
    me, rank = lax.axis_index("ctx"), lax.axis_index("tp")
    odd = lax.rem(rank, 2)
    heads = wq_ref.shape[1] // HD
    per_unit = n_ctx // heads
    own_at = [pl.multiple_of(odd * BLOCK, BLOCK), pl.multiple_of((1 - odd) * PAIR, BLOCK)]

    def load_x(g):
        _, rows, own = groups[g]
        return pltpu.make_async_copy(
            tokens_ref.at[pl.ds(own_at[g], rows)], x_ref.at[pl.ds(own, rows)], load_sem.at[g]
        )

    load_weights = [
        pltpu.make_async_copy(source, dest, weight_sem.at[k])
        for k, (source, dest) in enumerate(((wq_in, wq_ref), (wk_in, wk_ref), (wv_in, wv_ref), (wo_in, wo_ref)))
    ]
    for g in range(2):
        load_x(g).start()
    for copy in load_weights + own_copies(cot_ref, cot_buf, groups, cot_sem):
        copy.start()
    greet(n_ctx, True)
    gather_one = Gather(own_buf, rows_buf, groups, n1_sems, local=False)
    scatter = Scatter(rows_buf, groups, rest[:6], rest[6:], loaded=False)
    gather_two = Gather(own_buf, n2_out, groups, n2_sems, via=scatter.from_y)
    gather_cot = Gather(cot_buf, cot_out, groups, cot_sems, via=cot_via)
    trade = Exchange(got, x_sems, True)
    trade_back = Exchange(o_got, o_sems, False)

    def halves_of(u):
        return halves_at(odd if units[u][1] else 0)

    def normed(source, gain, at):
        values = source[at, :].astype(F32)
        return (values * inverse_rms(values) * gain[...].astype(F32)).astype(BF)

    def begin(g):
        base, rows, own = groups[g]
        load_x(g).wait()
        low = normed(x_ref, gain_one, pl.ds(own, rows))
        own_buf[pl.ds(own, rows), :] = low
        gather_one.start(g)
        rows_buf[pl.ds(base, rows), :] = low

    begin(0)
    for half, block in enumerate((me, 2 * n_ctx - 1 - me)):
        cos_part, sin_part = rotation(
            cos_ref[...], sin_ref[...], bcos_ref[pl.ds(block, 1), :], bsin_ref[pl.ds(block, 1), :]
        )
        tabs[0, half * BLOCK : (half + 1) * BLOCK, :] = cos_part
        tabs[1, half * BLOCK : (half + 1) * BLOCK, :] = sin_part

    def query(u, block):
        base, flipped = units[u]
        first, second = halves_of(u)
        at = pl.ds(base + block * PAIR, PAIR)
        rows = rows_buf[at, :]
        for which, w_ref in enumerate((wq_ref, wk_ref, wv_ref)):
            product = dot(rows, w_ref[...])
            for head in range(heads):
                part = product[:, head * HD : (head + 1) * HD]
                pair = block * heads + head
                for half, to in ((0, first), (1, second)):
                    piece = part[half * BLOCK : (half + 1) * BLOCK]
                    if which < 2:
                        piece = piece * tabs[0, to, :] + pltpu.roll(piece, HD // 2, 1) * tabs[1, to, :]
                    else:
                        piece = piece * valid_ref[pl.ds(base + block * PAIR + half * BLOCK, BLOCK), :]
                    send[u, pair, which, to, :] = piece.astype(BF)
        trade.start_some(send, u, block * heads, heads)

    store_n1 = pltpu.make_async_copy(rows_buf, n1_out, n1_sem)
    store_got = [pltpu.make_async_copy(got.at[u], got_out.at[u], got_sem.at[u]) for u in range(len(units))]

    for copy in load_weights:
        copy.wait()
    query(0, 0)
    gather_one.forward_x(0)
    gather_one.forward_y(0)
    begin(1)
    query(0, 1)
    query(1, 0)
    gather_one.finish(0)
    query(1, 1)
    gather_one.forward(1)
    gather_one.finish(1)
    for copy in own_copies(cot_ref, cot_buf, groups, cot_sem):
        copy.wait()
    for g in range(2):
        gather_cot.start(g)
    query(2, 0)
    query(2, 1)
    store_n1.start()

    def attend(u):
        trade.arrived(send, u)
        store_got[u].start()
        for k in range(n_ctx):
            front, back = both_places(me, k, n_ctx)
            for which, dest in enumerate((qs, ks, vs)):
                dest[front, :] = got[u, k, which, :BLOCK, :]
                dest[back, :] = got[u, k, which, BLOCK:, :]
        attend_rows(qs, ks, vs, os, tile)
        for k in range(n_ctx):
            front, back = both_places(me, k, n_ctx)
            o_send[u, k, :BLOCK, :] = os[front, :]
            o_send[u, k, BLOCK:, :] = os[back, :]
        trade_back.start(o_send, u)

    def project(u):
        trade_back.arrived(o_send, u)
        base, _ = units[u]
        first, second = halves_of(u)
        for block in range(per_unit):
            at = pl.ds(base + block * PAIR, PAIR)
            low = valid_ref[at, :].astype(BF)
            for head in range(heads):
                place = jnp.bitwise_xor(me, block * heads + head)
                part = jnp.concatenate([o_got[u, place, first, :], o_got[u, place, second, :]], axis=0)
                heads_out[at, head * HD : (head + 1) * HD] = part * low
            rows_buf[at, :] = dot(heads_out[at, :], wo_ref[...]).astype(BF)

    def use(at, total):
        residual[at, :] = x_ref[at, :].astype(F32) + total
        own_buf[at, :] = normed(residual, gain_two, at)

    def finish_group(g):
        scatter.total(g, use)
        gather_two.start(g)

    attend(0)
    for g in range(2):
        gather_one.sent(g)
    store_n1.wait()
    attend(1)
    for g in range(2):
        gather_cot.forward(g)
    project(0)
    scatter.start(0, (0,), loads=False)
    project(1)
    scatter.start(0, (1, 3, 2), loads=False)
    attend(2)
    scatter.forward(0)
    project(2)
    scatter.start(1, loads=False)
    finish_group(0)
    scatter.forward(1)
    finish_group(1)
    gather_two.forward(0)
    gather_two.forward(1)
    for u in range(len(units)):
        trade.sent(send, u)
        trade_back.sent(o_send, u)
        store_got[u].wait()
    for g in range(2):
        gather_cot.finish(g)
        gather_two.finish(g)
        gather_two.sent(g)
        gather_cot.sent(g)


def forward_layer(tokens_in, cot_in, gain_one, gain_two, wq, wk, wv, wo, tables, valid, n_ctx, groups, units):
    rows, depth = tokens_in.shape
    width = wq.shape[1]
    tokens = valid.shape[0]
    length = 2 * n_ctx * BLOCK
    n_units = len(units)
    vmem = lambda shape, dtype=BF: pltpu.VMEM(shape, dtype)
    outs = [
        jax.ShapeDtypeStruct((tokens, depth), BF),
        jax.ShapeDtypeStruct((n_units, n_ctx, 3, PAIR, HD), BF),
        jax.ShapeDtypeStruct((tokens, width), BF),
        jax.ShapeDtypeStruct((rows, depth), F32),
        jax.ShapeDtypeStruct((tokens, depth), BF),
        jax.ShapeDtypeStruct((tokens, depth), BF),
    ]
    return pl.pallas_call(
        functools.partial(forward_kernel, n_ctx, groups, units, min(512, length)),
        out_shape=outs,
        in_specs=[ANY_SPEC] * 6 + [VMEM_SPEC] * 7,
        out_specs=[ANY_SPEC, ANY_SPEC, VMEM_SPEC, VMEM_SPEC, ANY_SPEC, ANY_SPEC],
        scratch_shapes=[
            vmem((rows, depth)),
            vmem((tokens, depth)),
            vmem((rows, depth)),
            vmem((n_units, n_ctx, 3, PAIR, HD)),
            vmem((n_units, n_ctx, 3, PAIR, HD)),
            vmem((n_units, n_ctx, PAIR, HD)),
            vmem((n_units, n_ctx, PAIR, HD)),
            vmem((2, PAIR, HD), F32),
        ]
        + [vmem((length, HD))] * 4
        + [vmem(wq.shape)] * 3
        + [vmem(wo.shape), pltpu.SemaphoreType.DMA((4,))]
        + [vmem((rows, depth)), vmem((rows, depth)), pltpu.SemaphoreType.DMA((2,))]
        + Gather.scratch() * 3
        + Exchange.scratch(n_units, n_ctx) * 2
        + [pltpu.SemaphoreType.DMA, pltpu.SemaphoreType.DMA((n_units,)), pltpu.SemaphoreType.DMA((2,))]
        + Scatter.scratch(rows, depth, loaded=False),
        compiler_params=pltpu.CompilerParams(vmem_limit_bytes=VMEM_LIMIT, collective_id=3, has_side_effects=True),
        cost_estimate=pl.CostEstimate(
            flops=8 * tokens * depth * width, bytes_accessed=8 * tokens * depth, transcendentals=0
        ),
    )(tokens_in, cot_in, wq, wk, wv, wo, gain_one, gain_two, *tables, valid)


def attend_rows_back(qs, ks, vs, gs, os, dqs, cos_ref, sin_ref, tile):
    length = qs.shape[0]
    scale = HD ** (-0.5)
    factor = -scale * LOG2E
    shift = math.log(length) * LOG2E
    count = length // tile
    key_at = lax.broadcasted_iota(jnp.int32, (tile, tile), 0)
    query_at = lax.broadcasted_iota(jnp.int32, (tile, tile), 1)
    dqs[...] = jnp.zeros_like(dqs)

    def unrotate(values, at):
        return (values * cos_ref[at, :] - pltpu.roll(values, HD // 2, 1) * sin_ref[at, :]).astype(BF)

    for j in range(count):
        own = slice(j * tile, (j + 1) * tile)
        keys = ks[own, :]
        values = vs[own, :]

        def part(i, masked):
            at = pl.ds(pl.multiple_of(i * tile, tile), tile)
            query = qs[at, :]
            grad = gs[at, :]
            raw = times_transposed(keys, query)
            prob = 1.0 / (1.0 + jnp.exp2(raw * factor + shift))
            if masked:
                prob = jnp.where(query_at >= key_at, prob, 0.0)
            prob_grad = times_transposed(values, grad)
            score_grad = (prob_grad * prob * (1.0 - prob)).astype(BF)
            dqs[at, :] += contract_rows(score_grad, keys)
            return dot(score_grad, query), dot(prob.astype(BF), grad)

        total = part(j, True)
        if j + 1 < count:

            def step(i, acc):
                more = part(i, False)
                return acc[0] + more[0], acc[1] + more[1]

            total = lax.fori_loop(j + 1, count, step, total)
        os[1, own, :] = unrotate(total[0] * scale, own)
        os[2, own, :] = total[1].astype(BF)
    for i in range(count):
        at = slice(i * tile, (i + 1) * tile)
        os[0, at, :] = unrotate(dqs[at, :] * scale, at)


def middle_kernel(n_ctx, groups, units, tile, *refs):
    da_ref, got_ref, h_ref, residual_ref, wd_ref, wq_in, wk_in, wv_in, wo_in = refs[:9]
    cos_ref, sin_ref, bcos_ref, bsin_ref, valid_ref = refs[9:14]
    grad_ref, partial_out, output = refs[14:17]
    rows_buf, got, do_send, do_got, back_got, h_buf, wd_buf, res_buf, cos_full, sin_full = refs[17:27]
    qs, ks, vs, gs, os, dqs = refs[27:33]
    (wq_ref, wk_ref, wv_ref, wo_ref, weight_sem), rest = refs[33:38], refs[38:]
    load_weights = [
        pltpu.make_async_copy(source, dest, weight_sem.at[k])
        for k, (source, dest) in enumerate(((wo_in, wo_ref), (wq_in, wq_ref), (wk_in, wk_ref), (wv_in, wv_ref)))
    ]
    load_weights[0].start()
    back_send = got
    n_exchange = len(Exchange.scratch(1, 2))
    do_sems, back_sems, rest = rest[:n_exchange], rest[n_exchange : 2 * n_exchange], rest[2 * n_exchange :]
    (da_sem, got_sem, out_sem, h_sem, wd_sem, res_sem, y_sem), rest = rest[:7], rest[7:]
    me, rank = lax.axis_index("ctx"), lax.axis_index("tp")
    odd = lax.rem(rank, 2)
    heads = wq_ref.shape[1] // HD
    per_unit = n_ctx // heads
    unit_rows = per_unit * PAIR
    count = len(units)
    order = in_turn(count)

    def rows_of(u):
        return pl.ds(units[u][0], unit_rows)

    load_da = [pltpu.make_async_copy(da_ref.at[rows_of(u)], rows_buf.at[rows_of(u)], da_sem.at[u]) for u in range(count)]
    load_got = [pltpu.make_async_copy(got_ref.at[u], got.at[u], got_sem.at[u]) for u in range(count)]
    for u in order:
        load_da[u].start()
    for u in order:
        load_got[u].start()
    first_wd = pltpu.make_async_copy(wd_ref.at[:, pl.ds(0, wd_buf.shape[1])], wd_buf, wd_sem)
    first_wd.start()
    for copy in load_weights[1:]:
        copy.start()
    greet(n_ctx, True)
    scatter = Scatter(rows_buf, groups, rest[:6], rest[6:], loaded=False)
    trade = Exchange(do_got, do_sems, True)
    trade_back = Exchange(back_got, back_sems, False)

    load_weights[0].wait()
    for u in order:
        load_da[u].wait()
        base, flipped = units[u]
        first, second = halves_at(odd if flipped else 0)
        for block in range(per_unit):
            at = pl.ds(base + block * PAIR, PAIR)
            grad = times_transposed(rows_buf[at, :], wo_ref[...]).astype(BF)
            low = valid_ref[at, :].astype(BF)
            for head in range(heads):
                part = grad[:, head * HD : (head + 1) * HD] * low
                do_send[u, block * heads + head, first, :] = part[:BLOCK]
                do_send[u, block * heads + head, second, :] = part[BLOCK:]
        trade.start(do_send, u)
    for block in range(2 * n_ctx):
        at = slice(block * BLOCK, (block + 1) * BLOCK)
        cos_full[at, :], sin_full[at, :] = rotation(
            cos_ref[...], sin_ref[...], bcos_ref[block : block + 1, :], bsin_ref[block : block + 1, :]
        )
    for copy in load_weights[1:]:
        copy.wait()
    for u in order:
        load_got[u].wait()

    def attend(turn, carry):
        u = lax.rem(turn + count - 1, count)
        trade.arrived(do_send, u)
        for k in range(n_ctx):
            front, back = both_places(me, k, n_ctx)
            for which, dest in enumerate((qs, ks, vs)):
                dest[front, :] = got[u, k, which, :BLOCK, :]
                dest[back, :] = got[u, k, which, BLOCK:, :]
            gs[front, :] = do_got[u, k, :BLOCK, :]
            gs[back, :] = do_got[u, k, BLOCK:, :]
        attend_rows_back(qs, ks, vs, gs, os, dqs, cos_full, sin_full, tile)
        for k in range(n_ctx):
            front, back = both_places(me, k, n_ctx)
            for which in range(3):
                back_send[u, k, which, :BLOCK, :] = os[which, front, :]
                back_send[u, k, which, BLOCK:, :] = os[which, back, :]
        trade_back.start(back_send, u)
        return carry

    lax.fori_loop(0, count, attend, 0)

    tiles = rows_buf.shape[0] // PAIR

    def tile_rows(tile):
        return pl.ds(pl.multiple_of(tile * PAIR, PAIR), PAIR)

    def load_h(step):
        slot = lax.rem(step, 2)
        return pltpu.make_async_copy(h_ref.at[tile_rows(lax.rem(step, tiles))], h_buf.at[slot], h_sem.at[slot])

    columns = wd_buf.shape[1]
    parts = rows_buf.shape[1] // columns

    def part_columns(part):
        return pl.ds(pl.multiple_of(part * columns, columns), columns)

    def load_wd(part):
        return pltpu.make_async_copy(wd_ref.at[:, part_columns(part)], wd_buf, wd_sem)

    load_h(0).start()

    def down(step, carry):
        part, tile = step // tiles, lax.rem(step, tiles)

        @pl.when(step + 1 < tiles * parts)
        def _():
            load_h(step + 1).start()

        @pl.when(tile == 0)
        def _():
            @pl.when(part > 0)
            def _():
                load_wd(part).start()

            load_wd(part).wait()

        load_h(step).wait()
        rows_buf[tile_rows(tile), part_columns(part)] = dot(h_buf[lax.rem(step, 2)], wd_buf[...]).astype(BF)
        return carry

    lax.fori_loop(0, tiles * parts, down, 0)
    last_group = len(groups) - 1
    out_rows = rest[0]
    for g in (last_group, 0):
        scatter.start(g, loads=False)

    def use(at, total):
        size = total.shape[0]
        load = pltpu.make_async_copy(residual_ref.at[at], res_buf.at[pl.ds(0, size)], res_sem)
        load.start()
        load.wait()
        low = (res_buf[:size, :] + total).astype(BF)
        out_rows[at, :] = low

    def store(number, first):
        slot = number % 2
        return pltpu.make_async_copy(h_buf.at[slot], partial_out.at[pl.ds(first, PAIR)], out_sem.at[slot])

    stored = []
    for turn, u in enumerate(order):
        trade_back.arrived(back_send, u)
        base, flipped = units[u]
        first, second = halves_at(odd if flipped else 0)
        for block in range(per_unit):
            at = pl.ds(base + block * PAIR, PAIR)
            low = valid_ref[at, :].astype(BF)
            total = None
            for which, w_ref in enumerate((wq_ref, wk_ref, wv_ref)):
                width = heads * HD
                for head in range(heads):
                    place = jnp.bitwise_xor(me, block * heads + head)
                    part = jnp.concatenate(
                        [back_got[u, place, which, first, :], back_got[u, place, which, second, :]], axis=0
                    )
                    columns = slice(which * width + head * HD, which * width + (head + 1) * HD)
                    grad_ref[at, columns] = part * low if which == 2 else part
                product = times_transposed(grad_ref[at, which * width : (which + 1) * width], w_ref[...])
                total = product if total is None else total + product
            number = len(stored)
            if number >= 2:
                stored[number - 2].wait()
            h_buf[number % 2] = total.astype(BF)
            stored.append(store(number, base + block * PAIR))
            stored[-1].start()
        if turn == 0:
            scatter.forward(last_group)
            scatter.forward(0)
        if turn == 1:
            for g in (last_group, 0):
                scatter.total(g, use)
            store_y = pltpu.make_async_copy(out_rows, output, y_sem)
            store_y.start()
    store_y.wait()
    for copy in stored[-2:]:
        copy.wait()
    for u in order:
        trade.sent(do_send, u)
        trade_back.sent(back_send, u)


def middle_layer(da, got, h, residual, wq, wk, wv, wo, wd, tables, valid, n_ctx, groups, units):
    tokens, depth = da.shape
    width = wq.shape[1]
    length = 2 * n_ctx * BLOCK
    count = len(units)
    vmem = lambda shape, dtype=BF: pltpu.VMEM(shape, dtype)
    dma = pltpu.SemaphoreType.DMA
    three, one = (count, n_ctx, 3, PAIR, HD), (count, n_ctx, PAIR, HD)
    most_rows = max(rows for _, rows, _ in groups) // 2
    return pl.pallas_call(
        functools.partial(middle_kernel, n_ctx, groups, units, min(512, length)),
        out_shape=[
            jax.ShapeDtypeStruct((tokens, 3 * width), BF),
            jax.ShapeDtypeStruct((tokens, depth), BF),
            jax.ShapeDtypeStruct(residual.shape, BF),
        ],
        in_specs=[ANY_SPEC] * 9 + [VMEM_SPEC] * 5,
        out_specs=[VMEM_SPEC, ANY_SPEC, ANY_SPEC],
        scratch_shapes=[vmem((tokens, depth)), vmem(three), vmem(one), vmem(one), vmem(three)]
        + [vmem((2, PAIR, depth)), vmem((h.shape[1], depth // 2)), vmem((most_rows, depth), F32)]
        + [vmem((length, HD), F32)] * 2
        + [vmem((length, HD))] * 4
        + [vmem((3, length, HD)), vmem((length, HD), F32)]
        + [vmem(wq.shape)] * 3
        + [vmem(wo.shape), dma((4,))]
        + Exchange.scratch(count, n_ctx) * 2
        + [dma((count,)), dma((count,)), dma((2,)), dma((2,)), dma, dma, dma]
        + Scatter.scratch(residual.shape[0], depth, loaded=False),
        compiler_params=pltpu.CompilerParams(vmem_limit_bytes=VMEM_LIMIT, collective_id=4, has_side_effects=True),
        cost_estimate=pl.CostEstimate(
            flops=8 * tokens * depth * width + 2 * tokens * depth * h.shape[1],
            bytes_accessed=8 * tokens * depth,
            transcendentals=0,
        ),
    )(da, got, h, residual, wd, wq, wk, wv, wo, *tables, valid)


def body(
    tokens,
    counts,
    norm_gain,
    w_query,
    w_key,
    w_value,
    w_output,
    mlp_gain,
    w_gate,
    w_up,
    w_down,
    cotangent,
):
    n_ctx = lax.axis_size("ctx")
    me = lax.axis_index("ctx")
    rank = lax.axis_index("tp")
    odd = rank & 1
    core = me & 1
    length = 2 * BLOCK * n_ctx
    heads = w_query.shape[1] // HD
    gain_one = norm_gain.astype(F32)
    gain_two = mlp_gain.astype(F32)

    inverse = THETA ** (-(jnp.arange(HD // 2, dtype=F32) * (2.0 / HD)))
    angles = jnp.arange(length, dtype=jnp.int32).astype(F32)[:, None] * inverse[None, :]
    cos_half, sin_half = jnp.cos(angles), jnp.sin(angles)
    cos_full = jnp.concatenate([cos_half, cos_half], axis=1)
    sin_full = jnp.concatenate([-sin_half, sin_half], axis=1)

    def own_blocks(table):
        front = lax.dynamic_slice_in_dim(table, me * BLOCK, BLOCK, 0)
        back = lax.dynamic_slice_in_dim(table, (2 * n_ctx - 1 - me) * BLOCK, BLOCK, 0)
        return front, back

    cos_front, cos_back = own_blocks(cos_full)
    sin_front, sin_back = own_blocks(sin_full)
    own_counts = lax.dynamic_index_in_dim(counts, me, 0, keepdims=False)
    offsets = jnp.arange(BLOCK, dtype=jnp.int32)

    def valid_of(sequence_list, half_list):
        held = own_counts[jnp.stack(sequence_list), jnp.stack(half_list)]
        return (offsets[None, :] < held[:, None]).astype(F32).reshape(-1)

    cos_own = jnp.concatenate([cos_front, cos_back])
    sin_own = jnp.concatenate([sin_front, sin_back])
    sequences = counts.shape[1]
    paired = by_four() and sequences == 6 and n_ctx == 2 * heads
    if paired:
        ranks = [rank ^ k for k in range(4)]
        blocks_a = [(3 * (r >> 1) + 2 * (r & 1), jnp.int32(half)) for r in ranks for half in range(2)]
        blocks_b = [(1 + 3 * (r >> 1), r & 1) for r in ranks]
        flat_valid = valid_of(*zip(*(blocks_a + blocks_b)))
        valids = {"b": flat_valid[len(blocks_a) * BLOCK :], "a": flat_valid[: len(blocks_a) * BLOCK]}
        flip_back = lambda own: jnp.where(odd == 1, jnp.roll(own, BLOCK, axis=0), own)
        tables = {
            "b": (jnp.tile(flip_back(cos_own), (2, 1)), jnp.tile(flip_back(sin_own), (2, 1))),
            "a": (jnp.tile(cos_own, (4, 1)), jnp.tile(sin_own, (4, 1))),
        }
        scalars = {"b": jnp.stack([me, odd]).astype(jnp.int32), "a": jnp.stack([me, 0]).astype(jnp.int32)}
        n_pairs = {"b": 2 * heads, "a": 4 * heads}
    else:
        flat_valid = (offsets[None, None, :] < own_counts[:, :, None]).astype(F32).reshape(-1)
        valids = {"a": flat_valid}
        tables = {"a": (jnp.tile(cos_own, (sequences, 1)), jnp.tile(sin_own, (sequences, 1)))}
        scalars = {"a": jnp.stack([me, 0]).astype(jnp.int32)}
        n_pairs = {"a": sequences * heads}
    names = tuple(n_pairs)

    def own_rows(array):
        if not paired:
            return {"a": array}
        return {
            "b": lax.dynamic_slice_in_dim(array, (1 - odd) * PAIR, BLOCK, 0),
            "a": lax.dynamic_slice_in_dim(array, odd * BLOCK, PAIR, 0),
        }

    x_own = {name: rows.astype(F32) for name, rows in own_rows(tokens[0]).items()}
    g_own = own_rows(cotangent[0])

    split = by_four()
    rows_of = {name: valids[name].shape[0] for name in names}
    total_rows = sum(rows_of.values())
    first_row = {"a": 0, "b": rows_of["a"]}
    valid_head = {name: jnp.broadcast_to(valids[name][:, None], (rows_of[name], HD)) for name in names}
    valid_wide = {name: jnp.broadcast_to(valids[name][:, None].astype(BF), (rows_of[name], heads * HD)) for name in names}
    near = [k for k in range(n_ctx) if k < 6]
    far = [k for k in range(n_ctx) if k >= 6]
    state = {}

    def fence():
        names_held = list(state)
        values = lax.optimization_barrier([state[name] for name in names_held])
        state.update(zip(names_held, values))

    def only_b(step):
        if "b" in names:
            step("b")

    def norm_one(n):
        state["n1", n] = (x_own[n] * inverse_rms(x_own[n]) * gain_one).astype(BF)

    def gather_a(key):
        def step(n):
            state[key, n] = gather_first(state[key, n])

        return step

    def gather_b(key):
        def step(n):
            state[key, n] = gather_second(state[key, n])

        return step

    def query(n):
        state["n1", n] = gathered(state["n1", n])
        cos_tab, sin_tab = tables[n]
        state["qkv", n] = project_qkv(
            scalars[n], state["n1", n], w_query, w_key, w_value, cos_tab, sin_tab, valid_head[n], n_ctx
        )

    def swap_part(key, places, to):
        def step(n):
            got = dict(state.get((to, n), {}))
            got.update(exchange(state[key, n], places, n_ctx))
            state[to, n] = got
            if len(got) == n_ctx:
                state[to, n] = [got[k] for k in range(n_ctx)]
                del state[key, n]

        return step

    def attend(n):
        state["mixed", n] = attention_forward(scalars[n], state["got", n], n_ctx)

    def project(n):
        heads_out, *parts = project_out(
            scalars[n], state.pop(("back", n)), w_output, valid_wide[n], n_pairs[n], n_ctx, split
        )
        state["heads", n], state["r", n] = heads_out, tuple(parts)

    def scatter_a(key):
        def step(n):
            state[key, n] = scatter_first(state[key, n])

        return step

    def scatter_b(key):
        def step(n):
            state[key, n] = scatter_second(state[key, n])

        return step

    def norm_two(n):
        residual = x_own[n] + scattered(state.pop(("r", n)))
        state["residual", n] = residual
        state["n2", n] = (residual * inverse_rms(residual) * gain_two).astype(BF)

    def core_mlp(n):
        state["n2", n] = gathered(state["n2", n])
        state["cot", n] = gathered(state["cot", n])
        held = state.get("mlp", ())
        state["mlp"] = mlp_core(
            state["n2", n], state["cot", n], w_gate, w_up, w_down, total_rows, first_row[n], held
        )

    def attend_back(n):
        state["dqkv", n] = attention_backward(
            scalars[n], state.pop(("got", n)), state.pop(("gdo", n)), cos_full, sin_full, n_ctx
        )

    def query_back(n):
        dq, dk, dv, *parts = project_in(
            scalars[n], state.pop(("gdqkv", n)), (w_query, w_key, w_value), valid_wide[n], n_pairs[n], n_ctx, False
        )
        state["dq", n], state["dk", n], state["dv", n], state["i", n] = dq, dk, dv, parts[0]

    def joined(key):
        parts = [state[key, n] for n in ("a", "b") if n in names]
        return jnp.concatenate(parts) if len(parts) > 1 else parts[0]

    groups = tuple((first_row[n], rows_of[n] // 4, first_row[n] // 4) for n in ("a", "b") if n in names)

    if paired:
        units = ((0, False), (2 * PAIR, False), (4 * PAIR, True))
        wide_valid = jnp.broadcast_to(flat_valid[:, None], (total_rows, HD))
        twice = lambda table: jnp.concatenate([table, table], axis=1)
        starts = BLOCK * jnp.arange(2 * n_ctx, dtype=jnp.int32)
        spans = [at.astype(F32)[:, None] * inverse[None, :] for at in (offsets, starts)]
        turns = [twice(part(angle)) for angle in spans for part in (jnp.cos, jnp.sin)]
        all_n1, got, heads_out, own_residual, all_n2, all_cot = forward_layer(
            tokens[0], cotangent[0], norm_gain[None], mlp_gain[None], w_query, w_key, w_value, w_output,
            turns, wide_valid, n_ctx, groups, units,
        )
    else:
        norm_one("a")
        state["cot", "a"] = g_own["a"]
        gather_a("n1")("a")
        query("a")
        swap_part("qkv", range(n_ctx), "got")("a")
        attend("a")
        swap_part("mixed", range(n_ctx), "back")("a")
        project("a")
        scatter_a("r")("a")
        norm_two("a")
        gather_a("n2")("a")
        gather_a("cot")("a")
        all_n1, all_n2, all_cot = state["n1", "a"], gathered(state["n2", "a"]), gathered(state["cot", "a"])
        heads_out, own_residual = state["heads", "a"], state["residual", "a"]
    if paired:
        extra = feed_extra(groups, all_n2, w_gate, w_up, w_down, own_residual, cotangent[0], mlp_gain[None])
        sum_down, sum_gate, sum_up, sum_out, dr, da, gain_two_grad, _, h, _, _ = weight_sums(
            [(w_down.shape[0], 0), (all_n2, 1), (all_n2, 2), (heads_out, 3)],
            [all_cot], n_ctx, 1, extra, late=(5, 6, 1), limit=62 * 1024 * 1024,
        )
        dqkv, i_partial, output = middle_layer(
            da, got, h, own_residual, w_query, w_key, w_value, w_output, w_down, turns, wide_valid, n_ctx, groups, units
        )
        extra = input_extra(n_ctx, groups, i_partial, tokens[0], dr, norm_gain[None], gain_two_grad)
        sum_qkv, input_grad, gain_sums = weight_sums(
            [(all_n1, 0)], [dqkv], n_ctx, 2, extra
        )
    else:
        own_grads = cotangent[0]
        h, dgp, dup = mlp_core(all_n2, all_cot, w_gate, w_up, w_down, total_rows, 0)
        d_partial = (times_transposed(dgp, w_gate) + times_transposed(dup, w_up)).astype(BF)
        y_partial = dot(h, w_down).astype(BF)
        (sum_down,) = weight_sums([(h, 0)], [all_cot], n_ctx, 1)
        sum_gate, sum_up = weight_sums([(all_n2, 0), (all_n2, 1)], [dgp, dup], n_ctx, 2)
        back, gain_two_grad = norm_back_rows(own_residual, gain_two, scattered(scatter_first((d_partial,))))
        dr = own_grads.astype(F32) + back
        da = gathered(gather_first(dr.astype(BF)))
        output = (own_residual + scattered(scatter_first((y_partial,)))).astype(BF)
        state["do", "a"] = heads_back(scalars["a"], da, w_output, valid_wide["a"], n_ctx)
        swap_part("do", range(n_ctx), "gdo")("a")
        attend_back("a")
        swap_part("dqkv", range(n_ctx), "gdqkv")("a")
        query_back("a")
        (sum_out,) = weight_sums([(heads_out, 0)], [da], n_ctx, 3)
        (sum_qkv,) = weight_sums(
            [(all_n1, 0)], [jnp.concatenate([state[key, "a"] for key in ("dq", "dk", "dv")], axis=1)], n_ctx, 4
        )
        back, gain_one_grad = norm_back_rows(x_own["a"], gain_one, scattered(scatter_first((state["i", "a"],))))
        input_grad = (dr + back).astype(BF)
    sums = (sum_out, sum_gate, sum_up, sum_down, sum_qkv)
    if paired:
        *grads, output, input_grad, grad_norm_gain, grad_mlp_gain = cast_sums(sums, groups, (output, input_grad), gain_sums)
        gains = grad_norm_gain[0], grad_mlp_gain[0]
    else:
        grads = cast_sums(sums)
        gains = lax.psum(jnp.concatenate([gain_one_grad, gain_two_grad]), ("ctx", "tp"))
    grad_out, grad_gate, grad_up, grad_down, grad_query, grad_key, grad_value = grads
    return (
        output[None],
        input_grad[None],
        gains[0],
        grad_query,
        grad_key,
        grad_value,
        grad_out,
        gains[1],
        grad_gate,
        grad_up,
        grad_down,
    )


def solution(mesh):
    placed = (
        P("ctx", "tp", None),
        P(),
        P(),
        P(None, "tp"),
        P(None, "tp"),
        P(None, "tp"),
        P("tp", None),
        P(),
        P(None, "tp"),
        P(None, "tp"),
        P("tp", None),
        P("ctx", "tp", None),
    )
    return jax.shard_map(
        body,
        mesh=mesh,
        in_specs=placed,
        out_specs=(
            P("ctx", "tp", None),
            P("ctx", "tp", None),
            P(),
            P(None, "tp"),
            P(None, "tp"),
            P(None, "tp"),
            P("tp", None),
            P(),
            P(None, "tp"),
            P(None, "tp"),
            P("tp", None),
        ),
        check_vma=False,
    )
```

```python
import functools
import math

import jax
import jax.numpy as jnp
from jax import lax
from jax.experimental import pallas as pl
from jax.experimental.pallas import tpu as pltpu
from jax.sharding import PartitionSpec as P

HD = 128
BLOCK = 128
PAIR = 2 * BLOCK
EPS = 1e-05
THETA = 10000.0
LOG2E = 1.4426950408889634
BF = jnp.bfloat16
F32 = jnp.float32
VMEM_LIMIT = 60 * 1024 * 1024

X_SWAP = [(i, i ^ 1) for i in range(4)]
Y_SWAP = [(i, i ^ 2) for i in range(4)]


def dot(left, right):
    return jnp.dot(left, right, preferred_element_type=F32)


def contract_rows(left, right):
    return lax.dot_general(left, right, (((0,), (0,)), ((), ())), preferred_element_type=F32)


def times_transposed(left, right):
    return lax.dot_general(left, right, (((1,), (1,)), ((), ())), preferred_element_type=F32)


def send_x(values):
    return lax.ppermute(values, "tp", X_SWAP)


def send_y(values):
    return lax.ppermute(values, "tp", Y_SWAP)


def by_four():
    return lax.axis_size("tp") == 4


def gather_first(own):
    if not by_four():
        return (lax.all_gather(own, "tp", axis=0, tiled=True),)
    return own, send_x(own), send_y(own)


def gather_second(held):
    if len(held) == 1:
        return held
    own, from_x, from_y = held
    half = own.shape[0] // 2
    return own, from_x, from_y, send_x(from_y[:half]), send_y(from_x[half:])


def gathered(held):
    return jnp.concatenate(held) if len(held) > 1 else held[0]


def scatter_parts(partial):
    if not by_four():
        return (partial,)
    rows = partial.shape[0] // 4
    half = rows // 2
    at = lambda first: partial[first * half : (first + 1) * half]
    return (
        jnp.concatenate([at(2), at(6)]),
        jnp.concatenate([at(5), at(7)]),
        jnp.concatenate([at(0), at(1), at(4), at(3)]),
    )


def scatter_first(parts):
    if len(parts) == 1:
        return (lax.psum_scatter(parts[0], "tp", scatter_dimension=0, tiled=True),)
    return send_x(parts[0]), send_y(parts[1]), parts[2]


def add_low(left, right):
    return (left.astype(F32) + right.astype(F32)).astype(BF)


def scatter_second(held):
    if len(held) == 1:
        return held
    from_x, from_y, stay = held
    half = from_x.shape[0] // 2
    low_rest = send_y(add_low(stay[2 * half : 3 * half], from_x[half:]))
    high_rest = send_x(add_low(stay[3 * half :], from_y[half:]))
    return from_x, from_y, stay, low_rest, high_rest


def scattered(held):
    if len(held) == 1:
        return held[0].astype(F32)
    from_x, from_y, stay, low_rest, high_rest = (part.astype(F32) for part in held)
    half = low_rest.shape[0]
    low = stay[:half] + from_x[:half] + low_rest
    high = stay[half : 2 * half] + from_y[:half] + high_rest
    return jnp.concatenate([low, high])


def exchange(pieces, places, n_ctx):
    got = {}
    for k in places:
        got[k] = pieces[k] if k == 0 else lax.ppermute(pieces[k], "ctx", [(i, i ^ k) for i in range(n_ctx)])
    return got


def params():
    return pltpu.CompilerParams(vmem_limit_bytes=VMEM_LIMIT)


def whole(shape):
    return pl.BlockSpec(shape, lambda *_: (0,) * len(shape))


def put_partial(refs, first, value, rows):
    if len(refs) == 1:
        refs[0][first : first + value.shape[0], :] = value
        return
    to_x, to_y, stay = refs
    half = rows // 2
    homes = {
        0: (stay, 0), 1: (stay, 1), 2: (to_x, 0), 3: (stay, 3), 4: (stay, 2), 5: (to_y, 0), 6: (to_x, 1), 7: (to_y, 1)
    }
    for part in range(value.shape[0] // half):
        ref, place = homes[first // half + part]
        ref[place * half : (place + 1) * half, :] = value[part * half : (part + 1) * half]


def partial_shapes(rows, width, split):
    if not split:
        return [jax.ShapeDtypeStruct((rows, width), BF)]
    return [jax.ShapeDtypeStruct((rows // 4, width), BF)] * 2 + [jax.ShapeDtypeStruct((rows // 2, width), BF)]


def per_device(pairs, n_ctx):
    return -(-pairs // n_ctx)


def halves_at(swap):
    first = pl.multiple_of(swap * BLOCK, BLOCK)
    second = pl.multiple_of((1 - swap) * BLOCK, BLOCK)
    return pl.ds(first, BLOCK), pl.ds(second, BLOCK)


def qkv_kernel(n_ctx, pairs, scalar_ref, n_ref, wq_ref, wk_ref, wv_ref, cos_ref, sin_ref, valid_ref, *rest):
    out_refs, buffer = rest[:n_ctx], rest[n_ctx]
    rows = n_ref[...]
    first, second = halves_at(scalar_ref[1])
    me = scalar_ref[0]
    cos_tab = cos_ref[...]
    sin_tab = sin_ref[...]
    heads = wq_ref.shape[1] // HD
    step = pl.program_id(0)
    per = out_refs[0].shape[0]
    for pair in range(pairs, per * n_ctx):
        buffer[pair] = jnp.zeros(buffer.shape[1:], BF)
    for which, w_ref in enumerate((wq_ref, wk_ref, wv_ref)):
        product = dot(rows, w_ref[...])
        for head in range(heads):
            part = product[:, head * HD : (head + 1) * HD]
            if which < 2:
                part = part * cos_tab + pltpu.roll(part, HD // 2, 1) * sin_tab
            else:
                part = part * valid_ref[...]
            part = part.astype(BF)
            buffer[step * heads + head, which, first, :] = part[:BLOCK]
            buffer[step * heads + head, which, second, :] = part[BLOCK:]

    @pl.when(step == pl.num_programs(0) - 1)
    def _():
        for k in range(n_ctx):
            source = jnp.bitwise_xor(me, k)
            for p in range(per):
                out_refs[k][p] = buffer[source * per + p]


def project_qkv(scalars, normed, wq, wk, wv, cos_tab, sin_tab, valid, n_ctx):
    rows, depth = normed.shape
    width = wq.shape[1]
    heads = width // HD
    steps = rows // PAIR
    per = per_device(steps * heads, n_ctx)
    row_block = pl.BlockSpec((PAIR, HD), lambda i, s: (i, 0))
    weight = whole((depth, width))
    piece = (per, 3, PAIR, HD)
    return pl.pallas_call(
        functools.partial(qkv_kernel, n_ctx, steps * heads),
        out_shape=[jax.ShapeDtypeStruct(piece, BF)] * n_ctx,
        grid_spec=pltpu.PrefetchScalarGridSpec(
            num_scalar_prefetch=1,
            grid=(steps,),
            in_specs=[
                pl.BlockSpec((PAIR, depth), lambda i, s: (i, 0)),
                weight,
                weight,
                weight,
                row_block,
                row_block,
                row_block,
            ],
            out_specs=[whole(piece)] * n_ctx,
            scratch_shapes=[pltpu.VMEM((per * n_ctx, 3, PAIR, HD), BF)],
        ),
        compiler_params=params(),
        cost_estimate=pl.CostEstimate(
            flops=6 * rows * depth * width, bytes_accessed=rows * depth * 2 + 6 * depth * width, transcendentals=0
        ),
    )(scalars, normed, wq, wk, wv, cos_tab, sin_tab, valid)


def out_kernel(n_ctx, pairs, scalar_ref, *refs):
    piece_refs, (w_ref, valid_ref), (heads_ref, *partial_refs), buffer = (
        refs[:n_ctx],
        refs[n_ctx : n_ctx + 2],
        refs[n_ctx + 2 : -1],
        refs[-1],
    )
    me = scalar_ref[0]
    first, second = halves_at(scalar_ref[1])
    per = piece_refs[0].shape[0]
    heads = w_ref.shape[0] // HD
    for k in range(n_ctx):
        source = jnp.bitwise_xor(me, k)
        for p in range(per):
            buffer[source * per + p] = piece_refs[k][p]
    weight = w_ref[...]
    for sequence in range(pairs // heads):
        at = slice(sequence * PAIR, (sequence + 1) * PAIR)
        rows = jnp.concatenate(
            [
                jnp.concatenate(
                    [buffer[sequence * heads + head, first, :], buffer[sequence * heads + head, second, :]], axis=0
                )
                for head in range(heads)
            ],
            axis=1,
        )
        rows = rows * valid_ref[at, :]
        heads_ref[at, :] = rows
        put_partial(partial_refs, sequence * PAIR, dot(rows, weight).astype(BF), pairs // heads * PAIR // 4)


def project_out(scalars, pieces, weight, valid, pairs, n_ctx, split):
    width, depth = weight.shape
    rows = valid.shape[0]
    per = pieces[0].shape[0]
    shapes = [jax.ShapeDtypeStruct((rows, width), BF)] + partial_shapes(rows, depth, split)
    return pl.pallas_call(
        functools.partial(out_kernel, n_ctx, pairs),
        out_shape=shapes,
        grid_spec=pltpu.PrefetchScalarGridSpec(
            num_scalar_prefetch=1,
            grid=(1,),
            in_specs=[whole(piece.shape) for piece in pieces] + [whole(weight.shape), whole(valid.shape)],
            out_specs=[whole(shape.shape) for shape in shapes],
            scratch_shapes=[pltpu.VMEM((per * n_ctx, PAIR, HD), BF)],
        ),
        compiler_params=params(),
        cost_estimate=pl.CostEstimate(
            flops=2 * rows * depth * width, bytes_accessed=rows * depth * 2 + 2 * depth * width, transcendentals=0
        ),
    )(scalars, *pieces, weight, valid)


def heads_back_kernel(n_ctx, scalar_ref, da_ref, w_ref, valid_ref, *rest):
    out_refs, buffer = rest[:n_ctx], rest[n_ctx]
    me = scalar_ref[0]
    first, second = halves_at(scalar_ref[1])
    per = out_refs[0].shape[0]
    heads = w_ref.shape[0] // HD
    weight = w_ref[...]
    for pair in range(da_ref.shape[0] // PAIR * heads, per * n_ctx):
        buffer[pair] = jnp.zeros(buffer.shape[1:], BF)
    for sequence in range(da_ref.shape[0] // PAIR):
        at = slice(sequence * PAIR, (sequence + 1) * PAIR)
        grad = times_transposed(da_ref[at, :], weight).astype(BF) * valid_ref[at, :]
        for head in range(heads):
            part = grad[:, head * HD : (head + 1) * HD]
            buffer[sequence * heads + head, first, :] = part[:BLOCK]
            buffer[sequence * heads + head, second, :] = part[BLOCK:]
    for k in range(n_ctx):
        source = jnp.bitwise_xor(me, k)
        for p in range(per):
            out_refs[k][p] = buffer[source * per + p]


def heads_back(scalars, da, weight, valid, n_ctx):
    rows, depth = da.shape
    width = weight.shape[0]
    per = per_device(rows // PAIR * (width // HD), n_ctx)
    piece = (per, PAIR, HD)
    return pl.pallas_call(
        functools.partial(heads_back_kernel, n_ctx),
        out_shape=[jax.ShapeDtypeStruct(piece, BF)] * n_ctx,
        grid_spec=pltpu.PrefetchScalarGridSpec(
            num_scalar_prefetch=1,
            grid=(1,),
            in_specs=[whole(da.shape), whole(weight.shape), whole(valid.shape)],
            out_specs=[whole(piece)] * n_ctx,
            scratch_shapes=[pltpu.VMEM((per * n_ctx, PAIR, HD), BF)],
        ),
        compiler_params=params(),
        cost_estimate=pl.CostEstimate(
            flops=2 * rows * depth * width, bytes_accessed=rows * depth * 2 + 2 * depth * width, transcendentals=0
        ),
    )(scalars, da, weight, valid)


def in_kernel(n_ctx, pairs, scalar_ref, *refs):
    piece_refs, weight_refs, valid_ref = refs[:n_ctx], refs[n_ctx : n_ctx + 3], refs[n_ctx + 3]
    grad_refs, partial_refs, buffer = refs[n_ctx + 4 : n_ctx + 7], refs[n_ctx + 7 : -1], refs[-1]
    me = scalar_ref[0]
    first, second = halves_at(scalar_ref[1])
    per = piece_refs[0].shape[0]
    heads = weight_refs[0].shape[1] // HD
    for k in range(n_ctx):
        source = jnp.bitwise_xor(me, k)
        for p in range(per):
            buffer[source * per + p] = piece_refs[k][p]
    for sequence in range(pairs // heads):
        at = slice(sequence * PAIR, (sequence + 1) * PAIR)
        total = None
        for which in range(3):
            rows = jnp.concatenate(
                [
                    jnp.concatenate([buffer[pair, which, first, :], buffer[pair, which, second, :]], axis=0)
                    for pair in range(sequence * heads, (sequence + 1) * heads)
                ],
                axis=1,
            )
            if which == 2:
                rows = rows * valid_ref[at, :]
            grad_refs[which][at, :] = rows
            product = times_transposed(rows, weight_refs[which][...])
            total = product if total is None else total + product
        put_partial(partial_refs, sequence * PAIR, total.astype(BF), pairs // heads * PAIR // 4)


def project_in(scalars, pieces, weights, valid, pairs, n_ctx, split):
    depth, width = weights[0].shape
    rows = valid.shape[0]
    per = pieces[0].shape[0]
    shapes = [jax.ShapeDtypeStruct((rows, width), BF)] * 3 + partial_shapes(rows, depth, split)
    return pl.pallas_call(
        functools.partial(in_kernel, n_ctx, pairs),
        out_shape=shapes,
        grid_spec=pltpu.PrefetchScalarGridSpec(
            num_scalar_prefetch=1,
            grid=(1,),
            in_specs=[whole(piece.shape) for piece in pieces]
            + [whole(weight.shape) for weight in weights]
            + [whole(valid.shape)],
            out_specs=[whole(shape.shape) for shape in shapes],
            scratch_shapes=[pltpu.VMEM((per * n_ctx, 3, PAIR, HD), BF)],
        ),
        compiler_params=params(),
        cost_estimate=pl.CostEstimate(
            flops=6 * rows * depth * width, bytes_accessed=rows * depth * 2 + 6 * depth * width, transcendentals=0
        ),
    )(scalars, *pieces, *weights, valid)


def both_places(me, k, n_ctx):
    source = jnp.bitwise_xor(me, k)
    front = pl.multiple_of(source * BLOCK, BLOCK)
    back = pl.multiple_of((2 * n_ctx - 1 - source) * BLOCK, BLOCK)
    return pl.ds(front, BLOCK), pl.ds(back, BLOCK)


def attention_kernel(n_ctx, tile, scalar_ref, *refs):
    x_refs, o_refs, (qs, ks, vs, os) = refs[:n_ctx], refs[n_ctx : 2 * n_ctx], refs[2 * n_ctx :]
    me = scalar_ref[0]
    length = 2 * n_ctx * BLOCK
    for k in range(n_ctx):
        front, back = both_places(me, k, n_ctx)
        for which, dest in enumerate((qs, ks, vs)):
            dest[front, :] = x_refs[k][0, which, :BLOCK, :]
            dest[back, :] = x_refs[k][0, which, BLOCK:, :]
    factor = -(HD ** (-0.5)) * LOG2E
    shift = math.log(length) * LOG2E
    row_at = lax.broadcasted_iota(jnp.int32, (tile, tile), 0)
    col_at = lax.broadcasted_iota(jnp.int32, (tile, tile), 1)
    for i in range(length // tile):
        query = qs[i * tile : (i + 1) * tile, :]

        def part(j, masked):
            at = pl.ds(pl.multiple_of(j * tile, tile), tile)
            raw = times_transposed(query, ks[at, :])
            prob = 1.0 / (1.0 + jnp.exp2(raw * factor + shift))
            if masked:
                prob = jnp.where(row_at >= col_at, prob, 0.0)
            return dot(prob.astype(BF), vs[at, :])

        total = part(i, True)
        if i > 0:
            total = lax.fori_loop(0, i, lambda j, acc: acc + part(j, False), total)
        os[i * tile : (i + 1) * tile, :] = total.astype(BF)
    for k in range(n_ctx):
        front, back = both_places(me, k, n_ctx)
        o_refs[k][0, :BLOCK, :] = os[front, :]
        o_refs[k][0, BLOCK:, :] = os[back, :]


def attention_forward(scalars, pieces, n_ctx):
    pairs = pieces[0].shape[0]
    length = 2 * n_ctx * BLOCK
    tile = min(512, length)
    return pl.pallas_call(
        functools.partial(attention_kernel, n_ctx, tile),
        out_shape=[jax.ShapeDtypeStruct((pairs, PAIR, HD), BF)] * n_ctx,
        grid_spec=pltpu.PrefetchScalarGridSpec(
            num_scalar_prefetch=1,
            grid=(pairs,),
            in_specs=[pl.BlockSpec((1, 3, PAIR, HD), lambda i, s: (i, 0, 0, 0))] * n_ctx,
            out_specs=[pl.BlockSpec((1, PAIR, HD), lambda i, s: (i, 0, 0))] * n_ctx,
            scratch_shapes=[pltpu.VMEM((length, HD), BF)] * 4,
        ),
        compiler_params=params(),
        cost_estimate=pl.CostEstimate(
            flops=pairs * length * length * HD * 6,
            bytes_accessed=pairs * length * HD * 8,
            transcendentals=pairs * length * length,
        ),
    )(scalars, *pieces)


def attention_back_kernel(n_ctx, tile, scalar_ref, *refs):
    x_refs, g_refs, (cos_ref, sin_ref) = refs[:n_ctx], refs[n_ctx : 2 * n_ctx], refs[2 * n_ctx : 2 * n_ctx + 2]
    out_refs = refs[2 * n_ctx + 2 : 3 * n_ctx + 2]
    qs, ks, vs, gs, os, dqs = refs[3 * n_ctx + 2 :]
    me = scalar_ref[0]
    length = 2 * n_ctx * BLOCK
    for k in range(n_ctx):
        front, back = both_places(me, k, n_ctx)
        for which, dest in enumerate((qs, ks, vs)):
            dest[front, :] = x_refs[k][0, which, :BLOCK, :]
            dest[back, :] = x_refs[k][0, which, BLOCK:, :]
        gs[front, :] = g_refs[k][0, :BLOCK, :]
        gs[back, :] = g_refs[k][0, BLOCK:, :]
    scale = HD ** (-0.5)
    factor = -scale * LOG2E
    shift = math.log(length) * LOG2E
    count = length // tile
    key_at = lax.broadcasted_iota(jnp.int32, (tile, tile), 0)
    query_at = lax.broadcasted_iota(jnp.int32, (tile, tile), 1)
    dqs[...] = jnp.zeros_like(dqs)

    def unrotate(values, at):
        return (values * cos_ref[at, :] - pltpu.roll(values, HD // 2, 1) * sin_ref[at, :]).astype(BF)

    for j in range(count):
        own = slice(j * tile, (j + 1) * tile)
        keys = ks[own, :]
        values = vs[own, :]

        def part(i, masked):
            at = pl.ds(pl.multiple_of(i * tile, tile), tile)
            query = qs[at, :]
            grad = gs[at, :]
            raw = times_transposed(keys, query)
            prob = 1.0 / (1.0 + jnp.exp2(raw * factor + shift))
            if masked:
                prob = jnp.where(query_at >= key_at, prob, 0.0)
            prob_grad = times_transposed(values, grad)
            score_grad = (prob_grad * prob * (1.0 - prob)).astype(BF)
            dqs[at, :] += contract_rows(score_grad, keys)
            return dot(score_grad, query), dot(prob.astype(BF), grad)

        total = part(j, True)
        if j + 1 < count:

            def step(i, acc):
                more = part(i, False)
                return acc[0] + more[0], acc[1] + more[1]

            total = lax.fori_loop(j + 1, count, step, total)
        os[1, own, :] = unrotate(total[0] * scale, own)
        os[2, own, :] = total[1].astype(BF)
    for i in range(count):
        at = slice(i * tile, (i + 1) * tile)
        os[0, at, :] = unrotate(dqs[at, :] * scale, at)
    for k in range(n_ctx):
        front, back = both_places(me, k, n_ctx)
        for which in range(3):
            out_refs[k][0, which, :BLOCK, :] = os[which, front, :]
            out_refs[k][0, which, BLOCK:, :] = os[which, back, :]


def attention_backward(scalars, pieces, grads, cos_tab, sin_tab, n_ctx):
    pairs = pieces[0].shape[0]
    length = 2 * n_ctx * BLOCK
    tile = min(512, length)
    three = pl.BlockSpec((1, 3, PAIR, HD), lambda i, s: (i, 0, 0, 0))
    one = pl.BlockSpec((1, PAIR, HD), lambda i, s: (i, 0, 0))
    return pl.pallas_call(
        functools.partial(attention_back_kernel, n_ctx, tile),
        out_shape=[jax.ShapeDtypeStruct((pairs, 3, PAIR, HD), BF)] * n_ctx,
        grid_spec=pltpu.PrefetchScalarGridSpec(
            num_scalar_prefetch=1,
            grid=(pairs,),
            in_specs=[three] * n_ctx + [one] * n_ctx + [whole((length, HD))] * 2,
            out_specs=[three] * n_ctx,
            scratch_shapes=[pltpu.VMEM((length, HD), BF)] * 4
            + [pltpu.VMEM((3, length, HD), BF), pltpu.VMEM((length, HD), F32)],
        ),
        compiler_params=params(),
        cost_estimate=pl.CostEstimate(
            flops=pairs * length * length * HD * 12,
            bytes_accessed=pairs * length * HD * 14,
            transcendentals=pairs * length * length,
        ),
    )(scalars, *pieces, *grads, cos_tab, sin_tab)


def mlp_kernel(n_ref, g_ref, wg_ref, wu_ref, wd_ref, *rest):
    h_ref, dgp_ref, dup_ref = rest[-3:]
    rows = n_ref[...]
    gate_pre = dot(rows, wg_ref[...])
    up_pre = dot(rows, wu_ref[...])
    hidden_grad = times_transposed(g_ref[...], wd_ref[...])
    h_ref[...], dgp_ref[...], dup_ref[...] = feed_values(gate_pre, up_pre, hidden_grad)


def mlp_core(normed, grads, wg, wu, wd, total, first, held=()):
    rows, depth = normed.shape
    hidden = wg.shape[1]
    row_tile, tile = 512, 512
    skip = first // row_tile
    row_block = pl.BlockSpec((row_tile, depth), lambda j, i: (i, 0))
    out_block = pl.BlockSpec((row_tile, tile), lambda j, i: (i + skip, j))
    out = jax.ShapeDtypeStruct((total, hidden), BF)
    return pl.pallas_call(
        mlp_kernel,
        out_shape=(out, out, out),
        grid=(hidden // tile, rows // row_tile),
        in_specs=[
            row_block,
            row_block,
            pl.BlockSpec((depth, tile), lambda j, i: (0, j)),
            pl.BlockSpec((depth, tile), lambda j, i: (0, j)),
            pl.BlockSpec((tile, depth), lambda j, i: (j, 0)),
        ]
        + [pl.BlockSpec(memory_space=pl.ANY)] * len(held),
        out_specs=(out_block, out_block, out_block),
        input_output_aliases={5 + k: k for k in range(len(held))},
        compiler_params=params(),
        cost_estimate=pl.CostEstimate(
            flops=6 * rows * depth * hidden,
            bytes_accessed=rows * depth * 4 + 6 * depth * hidden + 6 * rows * hidden,
            transcendentals=rows * hidden,
        ),
    )(normed, grads, wg, wu, wd, *held)


def inverse_rms(values):
    return lax.rsqrt(jnp.mean(values * values, axis=-1, keepdims=True) + EPS)


def neighbours():
    index, rank = lax.axis_index("ctx"), lax.axis_index("tp")
    return (index, jnp.bitwise_xor(rank, 1)), (index, jnp.bitwise_xor(rank, 2))


def remote(source, dest, send_sem, recv_sem, device):
    return pltpu.make_async_remote_copy(
        src_ref=source,
        dst_ref=dest,
        send_sem=send_sem,
        recv_sem=recv_sem,
        device_id=device,
        device_id_type=pl.DeviceIdType.MESH,
    )


def signal(sem, device):
    pl.semaphore_signal(sem, inc=1, device_id=device, device_id_type=pl.DeviceIdType.MESH)


class Scatter:
    def __init__(self, partial, groups, bufs, sems, loaded=True):
        self.partial, self.groups, self.loaded = partial, groups, loaded
        self.from_x, self.from_y, self.for_y, self.for_x, self.low, self.high = bufs[:6]
        if loaded:
            self.stay, self.stay_y, self.stay_x = bufs[6:]
        self.first_send, self.first_recv, self.second_send, self.second_recv, self.load_sem = sems
        self.to_x, self.to_y = neighbours()

    @staticmethod
    def scratch(rows, width, loaded=True):
        dma = pltpu.SemaphoreType.DMA
        whole_rows, half_rows = pltpu.VMEM((rows, width), BF), pltpu.VMEM((rows // 2, width), BF)
        bufs = [whole_rows] * 2 + [half_rows] * 4 + ([whole_rows] + [half_rows] * 2 if loaded else [])
        return bufs + [dma((8,)), dma((8,)), dma((4,)), dma((4,)), dma((6,))]

    def piece(self, g, number):
        base, rows, own = self.groups[g]
        half = rows // 2
        if not self.loaded:
            return self.partial[pl.ds(base + number * half, half), :]
        if number < 2:
            return self.stay[pl.ds(own + number * half, half), :]
        return (self.stay_x if number == 3 else self.stay_y)[pl.ds(own // 2, half), :]

    def first_copies(self, g):
        base, rows, own = self.groups[g]
        half = rows // 2
        part = lambda number: self.partial.at[pl.ds(base + number * half, half)]
        at = lambda buf, number: buf.at[pl.ds(own + number * half, half)]
        plan = [
            (part(2), at(self.from_x, 0), self.to_x),
            (part(6), at(self.from_x, 1), self.to_x),
            (part(5), at(self.from_y, 0), self.to_y),
            (part(7), at(self.from_y, 1), self.to_y),
        ]
        return [
            remote(source, dest, self.first_send.at[4 * g + k], self.first_recv.at[4 * g + k], device)
            for k, (source, dest, device) in enumerate(plan)
        ]

    def loads(self, g):
        base, rows, own = self.groups[g]
        half = rows // 2
        copy = lambda number, count, dest, k: pltpu.make_async_copy(
            self.partial.at[pl.ds(base + number * half, count)], dest, self.load_sem.at[3 * g + k]
        )
        return [
            copy(0, rows, self.stay.at[pl.ds(own, rows)], 0),
            copy(4, half, self.stay_y.at[pl.ds(own // 2, half)], 1),
            copy(3, half, self.stay_x.at[pl.ds(own // 2, half)], 2),
        ]

    def second_copies(self, g):
        _, rows, own = self.groups[g]
        at = pl.ds(own // 2, rows // 2)
        return [
            remote(self.for_y.at[at], self.low.at[at], self.second_send.at[2 * g], self.second_recv.at[2 * g], self.to_y),
            remote(
                self.for_x.at[at], self.high.at[at], self.second_send.at[2 * g + 1], self.second_recv.at[2 * g + 1], self.to_x
            ),
        ]

    def start(self, g, which=(1, 3, 0, 2), loads=True):
        copies = self.first_copies(g)
        for k in which:
            copies[k].start()
        if loads:
            for copy in self.loads(g):
                copy.start()

    def forward(self, g):
        _, rows, own = self.groups[g]
        half = rows // 2
        copies = self.first_copies(g)
        copies[1].wait_recv()
        copies[3].wait_recv()
        if self.loaded:
            for copy in self.loads(g):
                copy.wait()
        at = pl.ds(own // 2, half)
        self.for_y[at, :] = add_low(self.piece(g, 4), self.from_x[pl.ds(own + half, half), :])
        self.for_x[at, :] = add_low(self.piece(g, 3), self.from_y[pl.ds(own + half, half), :])
        for copy in self.second_copies(g):
            copy.start()

    def total(self, g, use):
        _, rows, own = self.groups[g]
        half = rows // 2
        copies, seconds = self.first_copies(g), self.second_copies(g)
        copies[0].wait_recv()
        copies[2].wait_recv()
        for copy in copies:
            copy.wait_send()
        for copy in seconds:
            copy.wait()
        first = pl.ds(own, half)
        rest = pl.ds(own // 2, half)
        for side, (got, more) in enumerate(((self.from_x, self.low), (self.from_y, self.high))):
            at = pl.ds(own + side * half, half)
            use(at, self.piece(g, side).astype(F32) + got[first, :].astype(F32) + more[rest, :].astype(F32))


class Gather:
    def __init__(self, own, out, groups, sems, local=True, via=None):
        self.own, self.out, self.groups, self.has_local, self.via = own, out, groups, local, via
        self.first_send, self.first_recv, self.second_send, self.second_recv, self.local_sem, self.via_sem = sems
        self.to_x, self.to_y = neighbours()

    @staticmethod
    def scratch():
        dma = pltpu.SemaphoreType.DMA
        return [dma((4,)), dma((4,)), dma((4,)), dma((4,)), dma((2,)), dma((4,))]

    def first_copies(self, g):
        base, rows, own = self.groups[g]
        source = self.own.at[pl.ds(own, rows)]
        place = lambda k: self.out.at[pl.ds(base + k * rows, rows)]
        return [
            remote(source, place(1), self.first_send.at[2 * g], self.first_recv.at[2 * g], self.to_x),
            remote(source, place(2), self.first_send.at[2 * g + 1], self.first_recv.at[2 * g + 1], self.to_y),
        ]

    def local(self, g):
        base, rows, own = self.groups[g]
        return pltpu.make_async_copy(self.own.at[pl.ds(own, rows)], self.out.at[pl.ds(base, rows)], self.local_sem.at[g])

    def second_copies(self, g):
        base, rows, own = self.groups[g]
        half = rows // 2
        part = lambda number: self.out.at[pl.ds(base + number * half, half)]
        if self.via is None:
            low, high = part(4), part(3)
        else:
            low, high = (self.via.at[pl.ds(own + k * half, half)] for k in range(2))
        return [
            remote(low, part(6), self.second_send.at[2 * g], self.second_recv.at[2 * g], self.to_x),
            remote(high, part(7), self.second_send.at[2 * g + 1], self.second_recv.at[2 * g + 1], self.to_y),
        ]

    def pass_on(self, g, which):
        if self.via is not None:
            base, rows, own = self.groups[g]
            half = rows // 2
            load = pltpu.make_async_copy(
                self.out.at[pl.ds(base + (4 - which) * half, half)],
                self.via.at[pl.ds(own + which * half, half)],
                self.via_sem.at[2 * g + which],
            )
            load.start()
            load.wait()
        self.second_copies(g)[which].start()

    def start(self, g):
        for copy in self.first_copies(g):
            copy.start()
        if self.has_local:
            self.local(g).start()

    def forward_x(self, g):
        self.first_copies(g)[0].wait_recv()
        self.pass_on(g, 1)

    def forward_y(self, g):
        self.first_copies(g)[1].wait_recv()
        self.pass_on(g, 0)

    def forward(self, g):
        self.forward_x(g)
        self.forward_y(g)
        if self.has_local:
            self.local(g).wait()

    def finish(self, g):
        for copy in self.second_copies(g):
            copy.wait_recv()

    def sent(self, g):
        for copy in self.first_copies(g) + self.second_copies(g):
            copy.wait_send()


TILE, ROWS = 128, 64
CORE_SLOTS, HOP_SLOTS = 4, 4


class Ring:
    def __init__(self, slots, send_sem, recv_sem, credit, total):
        self.slots, self.send_sem, self.recv_sem, self.credit, self.total = slots, send_sem, recv_sem, credit, total
        self.count = slots.shape[0]

    def copy(self, source, at, send_at, device):
        slot = lax.rem(at, self.count)
        return pltpu.make_async_remote_copy(
            src_ref=source,
            dst_ref=self.slots.at[slot],
            send_sem=self.send_sem.at[send_at],
            recv_sem=self.recv_sem.at[slot],
            device_id=device,
            device_id_type=pl.DeviceIdType.MESH,
        )

    def send(self, source, at, send_at, device):
        @pl.when(at >= self.count)
        def _():
            pl.semaphore_wait(self.credit, 1)

        self.copy(source, at, send_at, device).start()

    def sent(self, source, at, send_at, device):
        self.copy(source, at, send_at, device).wait_send()

    def arrived(self, source, at, send_at, device):
        self.copy(source, at, send_at, device).wait_recv()
        return self.slots.at[lax.rem(at, self.count)]

    def free(self, at, device):
        @pl.when(at + self.count < self.total)
        def _():
            pl.semaphore_signal(self.credit, inc=1, device_id=device, device_id_type=pl.DeviceIdType.MESH)


def sums_kernel(n_ctx, items, n_right, n_extra, tasks, late, *refs):
    n_left = len(items)
    made = items[0][3]
    n_held = n_left - (1 if made else 0)
    left_refs, right_refs = refs[:n_held], refs[n_held : n_held + n_right]
    left_refs = ((None,) if made else ()) + tuple(left_refs)
    refs = refs[n_held + n_right :]
    extra_in, refs = refs[: n_extra[0]], refs[n_extra[0] :]
    out_refs, extra_out, refs = refs[:n_left], refs[n_left : n_left + n_extra[1]], refs[n_left + n_extra[1] :]
    extra_scratch, refs = refs[: n_extra[2]], refs[n_extra[2] :]
    right_refs = list(right_refs) + [extra_out[k] for k in late]
    n_right += len(late)
    (
        left_buf, right_buf, other_buf, ring, core_in, hop_in, hop_mid, hop_out, core_out,
        left_sem, right_sem, core_send, core_recv, in_send, in_recv, mid_send, mid_recv, out_send, out_recv,
        fin_send, fin_recv, store_sem, core_credit, in_credit, mid_credit, out_credit, fin_credit,
    ) = refs
    starts = [0]
    for _, _, chunks, _ in items:
        starts.append(starts[-1] + chunks)
    total = starts[-1]
    n_ring = ring.shape[0]
    chips = n_ctx // 2
    mid = chips // 2
    index = lax.axis_index("ctx")
    rank = lax.axis_index("tp")
    core = lax.rem(index, 2)
    chip = index // 2
    low_side = chip < mid
    place = jnp.where(low_side, chip, chips - 1 - chip)
    toward = jnp.where(low_side, 1, -1)
    partner = (chip * 2 + 1 - core, rank)
    after = ((chip + toward) * 2 + core, rank)
    before = ((chip - toward) * 2 + core, rank)
    is_first = place == 0
    is_last = place == mid - 1
    lag_t = mid + 1
    lag_u = lag_t + 2
    lag_o = lag_u + 2 * (mid - 1)
    lag_f = lag_o + 2
    lag_w = lag_f + 1

    to_core = Ring(core_in, core_send, core_recv, core_credit, total)
    to_after = Ring(hop_in, in_send, in_recv, in_credit, total)
    across = Ring(hop_mid, mid_send, mid_recv, mid_credit, total)
    to_before = Ring(hop_out, out_send, out_recv, out_credit, total)
    to_final = Ring(core_out, fin_send, fin_recv, fin_credit, total)

    def right_copy(k):
        return pltpu.make_async_copy(right_refs[k], right_buf.at[k % 2], right_sem.at[k % 2])

    right_copy(0).start()

    def for_item(at, action):
        for number in range(n_left):
            @pl.when((at >= starts[number]) & (at < starts[number + 1]))
            def _(number=number):
                action(number, at - starts[number])

    def rows_at(number, chunk, side):
        half = items[number][2] * ROWS
        return pl.multiple_of(side * half + chunk * ROWS, ROWS)

    def left_copy(number, chunk, slot, which):
        side = core if which == 0 else 1 - core
        half = items[number][2] * ROWS
        return pltpu.make_async_copy(
            left_refs[number].at[:, pl.ds(pl.multiple_of(side * half + chunk // 2 * TILE, TILE), TILE)],
            left_buf.at[slot, :, pl.ds(which * TILE, TILE)],
            left_sem.at[slot, which],
        )

    def load_left(at):
        def action(number, chunk):
            if number == 0 and made:
                maker.load(chunk // 2)
                return
            if number == 1 and made:

                @pl.when(chunk == 0)
                def _():
                    maker.release()

            for which in range(2):
                left_copy(number, chunk, lax.rem(at // 2, 2), which).start()

        for_item(at, action)

    planned, each, maker = tasks(extra_in, extra_out, extra_scratch) if tasks is not None else ({}, None, None)
    if made:
        maker.begin(left_buf, right_buf)
    load_left(0)
    if n_right > 1 and not made:
        right_copy(1).start()
    if tasks is not None:
        greet(n_ctx, True)
    else:
        barrier = pltpu.get_barrier_semaphore()
        pl.semaphore_signal(barrier, inc=1, device_id=partner, device_id_type=pl.DeviceIdType.MESH)

        @pl.when(chip > 0)
        def _():
            pl.semaphore_signal(
                barrier, inc=1, device_id=((chip - 1) * 2 + core, rank), device_id_type=pl.DeviceIdType.MESH
            )

        @pl.when(chip < chips - 1)
        def _():
            pl.semaphore_signal(
                barrier, inc=1, device_id=((chip + 1) * 2 + core, rank), device_id_type=pl.DeviceIdType.MESH
            )

        pl.semaphore_wait(barrier, 1 + jnp.where(chip > 0, 1, 0) + jnp.where(chip < chips - 1, 1, 0))
    if 0 in planned:
        planned.pop(0)()
    right_copy(0).wait()

    def step(i, carry):
        def at_lag(lag):
            at = i - lag
            return at, (at >= 0) & (at < total)

        at, now = at_lag(lag_w)

        @pl.when(now)
        def _():
            slot = lax.rem(at, n_ring)
            source = ring.at[slot]

            def action(number, chunk):
                store(number, chunk, at, 0).wait()
                store(number, chunk, at, 1).wait()

            for_item(at, action)
            to_final.sent(source, at, slot, partner)
            to_final.free(at, partner)

            @pl.when(jnp.logical_not(is_first))
            def _():
                to_before.sent(source, at, slot, before)

        at, now = at_lag(lag_o)

        @pl.when(now & jnp.logical_not(is_last))
        def _():
            slot = lax.rem(at, n_ring)
            source = ring.at[slot]
            to_after.sent(source, at, slot, after)
            got = to_before.arrived(source, at, slot, after)
            ring[slot] = got[...]
            to_before.free(at, after)

            @pl.when(jnp.logical_not(is_first))
            def _():
                to_before.send(source, at, slot, before)

        @pl.when(now)
        def _():
            slot = lax.rem(at, n_ring)
            to_final.send(ring.at[slot], at, slot, partner)

        at, now = at_lag(lag_u)

        @pl.when(now & is_last)
        def _():
            slot = lax.rem(at, n_ring)
            source = ring.at[slot]
            across.sent(source, at, slot, after)
            got = across.arrived(source, at, slot, after)
            ring[slot] = add_low(ring[slot], got[...])
            across.free(at, after)

            @pl.when(jnp.logical_not(is_first))
            def _():
                to_before.send(source, at, slot, before)

        at, now = at_lag(lag_t)

        @pl.when(now)
        def _():
            slot = lax.rem(at, n_ring)
            source = ring.at[slot]

            @pl.when(jnp.logical_not(is_first))
            def _():
                got = to_after.arrived(source, at, slot, before)
                ring[slot] = add_low(ring[slot], got[...])
                to_after.free(at, before)

            @pl.when(is_last)
            def _():
                across.send(source, at, slot, after)

            @pl.when(jnp.logical_not(is_first) & jnp.logical_not(is_last))
            def _():
                to_after.send(source, at, slot, after)

        at, now = at_lag(1)

        @pl.when(now)
        def _():
            slot = lax.rem(at, n_ring)
            source = ring.at[slot]
            own = other_buf.at[lax.rem(at, 4)]
            to_core.sent(own, at, lax.rem(at, 4), partner)
            got = to_core.arrived(own, at, lax.rem(at, 4), partner)
            ring[slot] = add_low(ring[slot], got[...])
            to_core.free(at, partner)

            @pl.when(is_first & jnp.logical_not(is_last))
            def _():
                to_after.send(source, at, slot, after)

        at, now = at_lag(lag_f)

        @pl.when(now)
        def _():
            slot = lax.rem(at, n_ring)
            to_final.arrived(ring.at[slot], at, slot, partner)

            def action(number, chunk):
                store(number, chunk, at, 0).start()
                store(number, chunk, at, 1).start()

            for_item(at, action)

        for when, task in planned.items():
            pl.when(i == when)(task)

        if each is not None:
            each(i)

        @pl.when((i + 2 < total) & (lax.rem(i, 2) == 0))
        def _():
            load_left(i + 2)

        @pl.when((i < total) & (lax.rem(i, 2) == 0))
        def _():
            slot = lax.rem(i // 2, 2)

            def action(number, chunk):
                which_right = items[number][1]
                if which_right > 0 and items[number - 1][1] != which_right:

                    @pl.when(chunk == 0)
                    def _():
                        if made and which_right in (1, n_right - 1):
                            right_copy(which_right).start()
                        right_copy(which_right).wait()

                if which_right > 0 and which_right + 1 < n_right - (1 if made else 0):

                    @pl.when(chunk == items[number][2] // 2)
                    def _():
                        right_copy(which_right + 1).start()

                if number == 0 and made:
                    maker.make(chunk // 2)
                else:
                    for which in range(2):
                        left_copy(number, chunk, slot, which).wait()
                right = right_buf.at[which_right % 2]
                product = contract_rows(left_buf[slot], right[...]).astype(BF)
                for part in range(2):
                    place = lax.rem(i + part, 4)
                    other_buf[place] = product[TILE + part * ROWS : TILE + (part + 1) * ROWS]
                    to_core.send(other_buf.at[place], i + part, place, partner)
                    ring[lax.rem(i + part, n_ring)] = product[part * ROWS : (part + 1) * ROWS]

            for_item(i, action)

        return carry

    def store(number, chunk, at, which):
        source = ring.at[lax.rem(at, n_ring)] if which == 0 else core_out.at[lax.rem(at, CORE_SLOTS)]
        side = core if which == 0 else 1 - core
        return pltpu.make_async_copy(
            source,
            out_refs[number].at[pl.ds(rows_at(number, chunk, side), ROWS), :],
            store_sem.at[which, lax.rem(at, 2)],
        )

    lax.fori_loop(0, total + lag_w, step, 0)


def weight_sums(items, rights, n_ctx, collective_id, extra=None, late=(), limit=VMEM_LIMIT):
    tokens, width = rights[0].shape
    columns = [left if isinstance(left, int) else left.shape[1] for left, _ in items]
    held = [left for left, _ in items if not isinstance(left, int)]
    shapes = [
        (k, right, columns[k] // 2 // ROWS, isinstance(left, int)) for k, (left, right) in enumerate(items)
    ]
    mid = n_ctx // 4
    n_ring = mid + 3 + 2 * (mid - 1) + 5
    any_spec = pl.BlockSpec(memory_space=pl.ANY)
    args, arg_specs, outs, out_specs, scratch, tasks = extra if extra is not None else ([], [], [], [], [], None)
    counts = (len(args), len(outs), len(scratch))
    chunk = (ROWS, width)
    dma = pltpu.SemaphoreType.DMA
    return pl.pallas_call(
        functools.partial(sums_kernel, n_ctx, shapes, len(rights), counts, tasks, late),
        out_shape=[jax.ShapeDtypeStruct((count, width), BF) for count in columns] + outs,
        in_specs=[any_spec] * (len(held) + len(rights)) + arg_specs,
        out_specs=[any_spec] * len(items) + out_specs,
        scratch_shapes=scratch
        + [
            pltpu.VMEM((2, tokens, 2 * TILE), BF),
            pltpu.VMEM((min(2, len(rights) + len(late)), tokens, width), BF),
            pltpu.VMEM((4,) + chunk, BF),
            pltpu.VMEM((n_ring,) + chunk, BF),
            pltpu.VMEM((CORE_SLOTS,) + chunk, BF),
            pltpu.VMEM((HOP_SLOTS,) + chunk, BF),
            pltpu.VMEM((HOP_SLOTS,) + chunk, BF),
            pltpu.VMEM((HOP_SLOTS,) + chunk, BF),
            pltpu.VMEM((CORE_SLOTS,) + chunk, BF),
            dma((2, 2)),
            dma((2,)),
            dma((4,)),
            dma((CORE_SLOTS,)),
            dma((n_ring,)),
            dma((HOP_SLOTS,)),
            dma((n_ring,)),
            dma((HOP_SLOTS,)),
            dma((n_ring,)),
            dma((HOP_SLOTS,)),
            dma((n_ring,)),
            dma((CORE_SLOTS,)),
            dma((2, 2)),
        ]
        + [pltpu.SemaphoreType.REGULAR] * 5,
        compiler_params=pltpu.CompilerParams(
            vmem_limit_bytes=limit, collective_id=collective_id, has_side_effects=True
        ),
        cost_estimate=pl.CostEstimate(
            flops=sum(2 * count * tokens * width for count in columns),
            bytes_accessed=sum(2 * count * (tokens + width) for count in columns),
            transcendentals=0,
        ),
    )(*held, *rights, *args)


VMEM_SPEC = pl.BlockSpec(memory_space=pltpu.VMEM)
ANY_SPEC = pl.BlockSpec(memory_space=pl.ANY)


def norm_back_rows(values, gain, grad):
    inv = inverse_rms(values)
    unit = values * inv
    scaled = grad * gain
    back = (scaled - unit * jnp.mean(scaled * unit, axis=-1, keepdims=True)) * inv
    return back, jnp.sum(grad * unit, axis=0, keepdims=True)


def own_copies(ref, buf, groups, sem):
    odd = lax.rem(lax.axis_index("tp"), 2)
    starts = [pl.multiple_of(odd * BLOCK, BLOCK), pl.multiple_of((1 - odd) * PAIR, BLOCK)]
    return [
        pltpu.make_async_copy(ref.at[pl.ds(start, rows)], buf.at[pl.ds(own, rows)], sem.at[g])
        for g, (start, (_, rows, own)) in enumerate(zip(starts, groups))
    ]


class Maker:
    def __init__(self, refs, outs, weights, downs, stage, sems):
        self.n2_ref, self.wg_ref, self.wu_ref, self.wd_ref = refs
        self.h_out, self.dgp_out, self.dup_out = outs
        self.weights, self.downs, self.stage = weights, downs, stage
        self.n2_sem, self.weight_sem, self.h_sem, self.grad_sem = sems
        self.core = lax.rem(lax.axis_index("ctx"), 2)
        self.half = self.h_out.shape[1] // 2
        self.tiles = self.half // TILE

    def first(self, tile, which):
        side = self.core if which == 0 else 1 - self.core
        return pl.multiple_of(side * self.half + tile * TILE, TILE)

    def copies(self, tile):
        slot = lax.rem(tile, 2)
        deep = self.weights.shape[1]
        made = []
        for which in range(2):
            at = pl.ds(self.first(tile, which), TILE)
            for kind, ref in enumerate((self.wg_ref, self.wu_ref)):
                to = pl.multiple_of((slot * 2 + kind) * 2 * TILE + which * TILE, TILE)
                for part in range(2):
                    made.append((ref.at[pl.ds(part * deep, deep), at], self.weights.at[part, :, pl.ds(to, TILE)]))
            made.append((self.wd_ref.at[at], self.downs.at[slot, 0, pl.ds(which * TILE, TILE)]))
        return [
            pltpu.make_async_copy(source, dest, self.weight_sem.at[slot, k]) for k, (source, dest) in enumerate(made)
        ]

    def load(self, tile):
        for copy in self.copies(tile):
            copy.start()

    def begin(self, left_buf, right_buf):
        self.left_buf, self.right_buf = left_buf, right_buf
        self.n2_copy().start()

    def n2_copy(self):
        return pltpu.make_async_copy(self.n2_ref, self.right_buf.at[1], self.n2_sem)

    def h_stores(self, tile):
        slot = lax.rem(tile, 2)
        return [
            pltpu.make_async_copy(
                self.left_buf.at[slot, :, pl.ds(which * TILE, TILE)],
                self.h_out.at[:, pl.ds(self.first(tile, which), TILE)],
                self.h_sem.at[slot, which],
            )
            for which in range(2)
        ]

    def grad_stores(self, tile):
        return [
            pltpu.make_async_copy(
                self.stage.at[kind, :, pl.ds(which * TILE, TILE)],
                out.at[:, pl.ds(self.first(tile, which), TILE)],
                self.grad_sem.at[kind, which],
            )
            for kind, out in enumerate((self.dgp_out, self.dup_out))
            for which in range(2)
        ]

    def make(self, tile):
        slot = lax.rem(tile, 2)
        deep = self.weights.shape[1]

        @pl.when(tile == 0)
        def _():
            self.n2_copy().wait()

        @pl.when(tile > 0)
        def _():
            for copy in self.grad_stores(tile - 1):
                copy.wait()

        @pl.when(tile > 1)
        def _():
            for copy in self.h_stores(tile - 2):
                copy.wait()

        for copy in self.copies(tile):
            copy.wait()
        at_gate = pl.ds(pl.multiple_of(slot * 4 * TILE, TILE), 2 * TILE)
        at_up = pl.ds(pl.multiple_of((slot * 4 + 2) * TILE, TILE), 2 * TILE)
        count = 512

        def rows_step(step, carry):
            rows = pl.ds(pl.multiple_of(step * count, count), count)
            low, high = self.right_buf[1, rows, :deep], self.right_buf[1, rows, deep:]
            gate_pre = dot(low, self.weights[0, :, at_gate]) + dot(high, self.weights[1, :, at_gate])
            up_pre = dot(low, self.weights[0, :, at_up]) + dot(high, self.weights[1, :, at_up])
            hidden_grad = times_transposed(self.right_buf[0, rows, :], self.downs[slot, 0])
            h, dgp, dup = feed_values(gate_pre, up_pre, hidden_grad)
            self.left_buf[slot, rows, :] = h
            self.stage[0, rows, :] = dgp
            self.stage[1, rows, :] = dup
            return carry

        lax.fori_loop(0, self.right_buf.shape[1] // count, rows_step, 0)
        for copy in self.h_stores(tile) + self.grad_stores(tile):
            copy.start()

    def release(self):
        for copy in self.h_stores(self.tiles - 2):
            copy.wait()

    def finish(self):
        for copy in self.h_stores(self.tiles - 1) + self.grad_stores(self.tiles - 1):
            copy.wait()


def feed_values(gate_pre, up_pre, hidden_grad):
    gate_sig = 1.0 / (1.0 + jnp.exp2(gate_pre * (-LOG2E)))
    gate_act = gate_pre * gate_sig
    return (
        (gate_act * up_pre).astype(BF),
        (hidden_grad * up_pre * (gate_sig * (1.0 + gate_pre * (1.0 - gate_sig)))).astype(BF),
        (hidden_grad * gate_act).astype(BF),
    )


def feed_tasks(groups, extra_in, extra_out, scratch):
    n2_ref, wg_ref, wu_ref, wd_ref, residual, cot_ref, gain = extra_in
    dr, da_all, gain_grad, d_ref, h_ref, dgp_ref, dup_ref = extra_out
    n = len(Scatter.scratch(16, 128))
    bufs, rest = scratch[:n], scratch[n:]
    weights, lefts, tile_out, weight_sem, left_sem, out_sem = rest[:6]
    grads, stage, own_sem, n2_sem, make_sem, h_sem, grad_sem = rest[6:13]
    da_own = bufs[0]
    scatter = Scatter(d_ref, groups, bufs[:9], bufs[9:])
    gather = Gather(da_own, da_all, groups, rest[13:], via=bufs[1])
    maker = Maker(
        (n2_ref, wg_ref, wu_ref, wd_ref),
        (h_ref, dgp_ref, dup_ref),
        weights,
        lefts,
        stage,
        (n2_sem, make_sem, h_sem, grad_sem),
    )
    order = list(reversed(range(len(groups))))
    rows, columns = lefts.shape[2], weights.shape[1]
    row_tiles = dgp_ref.shape[0] // rows
    tiles = row_tiles * (d_ref.shape[1] // columns)
    after = maker.half // ROWS
    shift = after + 1

    def weight_copies(part):
        at = pl.ds(pl.multiple_of(part * columns, columns), columns)
        return [
            pltpu.make_async_copy(ref.at[at], weights.at[k], weight_sem.at[k]) for k, ref in enumerate((wg_ref, wu_ref))
        ]

    def left_copies(tile):
        at = pl.ds(pl.multiple_of(lax.rem(tile, row_tiles) * rows, rows), rows)
        slot = lax.rem(tile, 2)
        return [
            pltpu.make_async_copy(ref.at[at], lefts.at[slot, k], left_sem.at[slot, k])
            for k, ref in enumerate((dgp_ref, dup_ref))
        ]

    def out_copy(tile):
        slot = lax.rem(tile, 2)
        return pltpu.make_async_copy(
            tile_out.at[slot],
            d_ref.at[
                pl.ds(pl.multiple_of(lax.rem(tile, row_tiles) * rows, rows), rows),
                pl.ds(pl.multiple_of(tile // row_tiles * columns, columns), columns),
            ],
            out_sem.at[slot],
        )

    def begin():
        gain_grad[...] = jnp.zeros_like(gain_grad)
        for copy in own_copies(cot_ref, grads, groups, own_sem):
            copy.start()

    def whole_hidden():
        maker.finish()
        for copy in weight_copies(0) + left_copies(0):
            copy.start()

    def each(step):
        i = step - shift

        @pl.when((i >= 0) & (i < tiles))
        def _():
            slot = lax.rem(i, 2)

            @pl.when(i + 1 < tiles)
            def _():
                for copy in left_copies(i + 1):
                    copy.start()

            @pl.when(lax.rem(i, row_tiles) == 0)
            def _():
                @pl.when(i > 0)
                def _():
                    for copy in weight_copies(i // row_tiles):
                        copy.start()

                for copy in weight_copies(i // row_tiles):
                    copy.wait()

            for copy in left_copies(i):
                copy.wait()
            total = times_transposed(lefts[slot, 0], weights[0]) + times_transposed(lefts[slot, 1], weights[1])

            @pl.when(i >= 2)
            def _():
                out_copy(i - 2).wait()

            tile_out[slot] = total.astype(BF)
            out_copy(i).start()

    def start():
        out_copy(tiles - 2).wait()
        out_copy(tiles - 1).wait()
        for copy in own_copies(cot_ref, grads, groups, own_sem):
            copy.wait()
        for g in order:
            scatter.start(g)

    def use(at, total):
        back, more = norm_back_rows(residual[at, :], gain[...].astype(F32), total)
        total_grad = grads[at, :].astype(F32) + back
        dr[at, :] = total_grad
        da_own[at, :] = total_grad.astype(BF)
        gain_grad[...] += more

    def spread(g):
        scatter.total(g, use)
        gather.start(g)

    def finish():
        for g in order:
            gather.finish(g)
            gather.sent(g)

    first = shift + tiles
    plan = {
        0: begin,
        after: whole_hidden,
        first: start,
        first + 3: lambda: scatter.forward(order[0]),
        first + 6: lambda: scatter.forward(order[-1]),
        first + 7: lambda: spread(order[0]),
        first + 9: lambda: spread(order[-1]),
        first + 11: lambda: gather.forward(order[0]),
        first + 15: lambda: gather.forward(order[-1]),
        first + 18: finish,
    }
    return plan, each, maker


def feed_extra(groups, n2, wg, wu, wd, residual, cot, gain):
    rows, width = residual.shape
    tokens, hidden = n2.shape[0], wg.shape[1]
    dma = pltpu.SemaphoreType.DMA
    outs = [
        jax.ShapeDtypeStruct((rows, width), F32),
        jax.ShapeDtypeStruct((tokens, width), BF),
        jax.ShapeDtypeStruct((1, width), F32),
        jax.ShapeDtypeStruct((tokens, width), BF),
    ] + [jax.ShapeDtypeStruct((tokens, hidden), BF)] * 3
    scratch = (
        Scatter.scratch(rows, width)
        + [
            pltpu.VMEM((2, width // 2, hidden), BF),
            pltpu.VMEM((2, 2, PAIR, hidden), BF),
            pltpu.VMEM((2, PAIR, width // 2), BF),
            dma((2,)),
            dma((2, 2)),
            dma((2,)),
            pltpu.VMEM((rows, width), BF),
            pltpu.VMEM((2, tokens, 2 * TILE), BF),
            dma((2,)),
            dma,
            dma((2, 10)),
            dma((2, 2)),
            dma((2, 2)),
        ]
        + Gather.scratch()
    )
    return (
        [n2, wg, wu, wd, residual, cot, gain],
        [ANY_SPEC] * 4 + [VMEM_SPEC, ANY_SPEC, VMEM_SPEC],
        outs,
        [VMEM_SPEC, ANY_SPEC, VMEM_SPEC] + [ANY_SPEC] * 4,
        scratch,
        functools.partial(feed_tasks, groups),
    )


def input_tasks(n_ctx, groups, extra_in, extra_out, scratch):
    i_ref, tokens_ref, dr, gain, gain_two_grad = extra_in
    input_grad, gain_sums = extra_out
    n = len(Scatter.scratch(16, 128))
    scatter = Scatter(i_ref, groups, scratch[:9], scratch[9:n])
    gains, got_tp, got_ctx, send_tp, recv_tp, send_ctx, recv_ctx, rows_in, own_sem = scratch[n:]
    order = list(reversed(range(len(groups))))
    me, rank = lax.axis_index("ctx"), lax.axis_index("tp")

    def tp_hop(k):
        return remote(gains.at[k], got_tp.at[k], send_tp.at[k], recv_tp.at[k], neighbours()[k])

    def ctx_hop(k):
        place = gains.at[2]
        return remote(place, got_ctx.at[k], send_ctx.at[k], recv_ctx.at[k], (jnp.bitwise_xor(me, k), rank))

    def begin():
        gains[0] = jnp.zeros(gains.shape[1:], F32)
        gains[0, 8:9, :] = gain_two_grad[...]
        for copy in own_copies(tokens_ref, rows_in, groups, own_sem):
            copy.start()
        for g in order:
            scatter.start(g)

    def forward_first():
        for copy in own_copies(tokens_ref, rows_in, groups, own_sem):
            copy.wait()
        scatter.forward(order[0])

    def use(at, total):
        back, more = norm_back_rows(rows_in[at, :].astype(F32), gain[...].astype(F32), total)
        input_grad[at, :] = (dr[at, :] + back).astype(BF)
        gains[0, 0:1, :] += more

    def rest():
        scatter.total(order[-1], use)
        tp_hop(0).start()

    def second():
        tp_hop(0).wait()
        gains[1] = gains[0] + got_tp[0]
        tp_hop(1).start()

    def third():
        tp_hop(1).wait()
        gains[2] = gains[1] + got_tp[1]
        for k in range(1, n_ctx):
            ctx_hop(k).start()

    def finish():
        for k in range(1, n_ctx):
            ctx_hop(k).wait()
        got_ctx[0] = gains[2]
        total = got_ctx[jnp.bitwise_xor(me, 0)]
        for index in range(1, n_ctx):
            total = total + got_ctx[jnp.bitwise_xor(me, index)]
        gain_sums[...] = total

    return {
        0: begin,
        4: forward_first,
        9: lambda: scatter.forward(order[-1]),
        10: lambda: scatter.total(order[0], use),
        13: rest,
        15: second,
        17: third,
        20: finish,
    }, None, None


def input_extra(n_ctx, groups, i_partial, tokens_in, dr, gain, gain_two_grad):
    rows, width = tokens_in.shape
    dma = pltpu.SemaphoreType.DMA
    outs = [jax.ShapeDtypeStruct((rows, width), BF), jax.ShapeDtypeStruct((16, width), F32)]
    return (
        [i_partial, tokens_in, dr, gain, gain_two_grad],
        [ANY_SPEC] * 2 + [VMEM_SPEC] * 3,
        outs,
        [VMEM_SPEC] * 2,
        Scatter.scratch(rows, width)
        + [
            pltpu.VMEM((3, 16, width), F32),
            pltpu.VMEM((2, 16, width), F32),
            pltpu.VMEM((n_ctx, 16, width), F32),
            dma((2,)),
            dma((2,)),
            dma((n_ctx,)),
            dma((n_ctx,)),
            pltpu.VMEM((rows, width), BF),
            dma((2,)),
        ],
        functools.partial(input_tasks, n_ctx, groups),
    )


def cast_kernel(groups, *refs):
    out_in, gate_in, up_in, down_in, qkv_in = refs[:5]
    n_more = 3 if groups else 0
    more_in, refs = refs[5 : 5 + n_more], refs[5 + n_more :]
    for source, dest in zip((out_in, gate_in, up_in, down_in), refs[:4]):
        dest[...] = source[...].astype(F32)
    width = refs[4].shape[1]
    for k, dest in enumerate(refs[4:7]):
        dest[...] = qkv_in[:, k * width : (k + 1) * width].astype(F32)
    if not groups:
        return
    row_outs, gain_outs = refs[7:9], refs[9:11]
    gains = more_in[2]
    odd = lax.rem(lax.axis_index("tp"), 2)
    starts = (pl.multiple_of(odd * BLOCK, BLOCK), pl.multiple_of((1 - odd) * PAIR, BLOCK))

    @pl.when(pl.program_id(0) == 0)
    def _():
        gain_outs[0][...] = gains[0:1, :]
        gain_outs[1][...] = gains[8:9, :]
        for source, dest in zip(more_in[:2], row_outs):
            for start, (_, rows, own) in zip(starts, groups):
                dest[pl.ds(start, rows), :] = source[pl.ds(own, rows), :]


def cast_sums(sums, groups=(), rows=(), gains=None):
    steps = 8
    block = lambda array: pl.BlockSpec((array.shape[0] // steps, array.shape[1]), lambda i: (i, 0))
    outs = [jax.ShapeDtypeStruct(array.shape, F32) for array in sums[:-1]]
    outs += [jax.ShapeDtypeStruct((sums[-1].shape[0], sums[-1].shape[1] // 3), F32)] * 3
    in_specs, out_specs = [block(array) for array in sums], [block(array) for array in outs]
    args = list(sums)
    if groups:
        args += list(rows) + [gains]
        in_specs += [whole(array.shape) for array in (*rows, gains)]
        outs += [jax.ShapeDtypeStruct(array.shape, array.dtype) for array in rows]
        outs += [jax.ShapeDtypeStruct((1, gains.shape[1]), F32)] * 2
        out_specs += [whole(array.shape) for array in rows] + [whole((1, gains.shape[1]))] * 2
    return pl.pallas_call(
        functools.partial(cast_kernel, groups),
        out_shape=outs,
        grid=(steps,),
        in_specs=in_specs,
        out_specs=out_specs,
        compiler_params=params(),
        cost_estimate=pl.CostEstimate(
            flops=0, bytes_accessed=sum(6 * array.shape[0] * array.shape[1] for array in sums), transcendentals=0
        ),
    )(*args)


class Exchange:
    def __init__(self, dest, sems, by_device):
        self.dest, self.by_device = dest, by_device
        self.send_sem, self.recv_sem, self.own_sem = sems
        self.n_ctx = dest.shape[1]
        self.me, self.rank = lax.axis_index("ctx"), lax.axis_index("tp")

    @staticmethod
    def scratch(units, n_ctx):
        dma = pltpu.SemaphoreType.DMA
        return [dma((units, n_ctx)), dma((units, n_ctx)), dma((units,))]

    def copy(self, source, unit, k):
        other = jnp.bitwise_xor(self.me, k)
        place = other if self.by_device else k
        return remote(
            source.at[unit, place],
            self.dest.at[unit, k],
            self.send_sem.at[unit, k],
            self.recv_sem.at[unit, k],
            (other, self.rank),
        )

    def own(self, source, unit):
        place = self.me if self.by_device else 0
        return pltpu.make_async_copy(source.at[unit, place], self.dest.at[unit, 0], self.own_sem.at[unit])

    def start(self, source, unit):
        for k in reversed(range(1, self.n_ctx)):
            self.copy(source, unit, k).start()
        self.own(source, unit).start()

    def start_some(self, source, unit, first, count):
        for k in reversed(range(self.n_ctx)):
            other = jnp.bitwise_xor(self.me, k)

            @pl.when((other >= first) & (other < first + count))
            def _(k=k):
                if k == 0:
                    self.own(source, unit).start()
                else:
                    self.copy(source, unit, k).start()

    def arrived(self, source, unit):
        for k in range(1, self.n_ctx):
            self.copy(source, unit, k).wait_recv()
        self.own(source, unit).wait()

    def sent(self, source, unit):
        for k in range(1, self.n_ctx):
            self.copy(source, unit, k).wait_send()


def greet(n_ctx, tp_too):
    index, rank = lax.axis_index("ctx"), lax.axis_index("tp")
    barrier = pltpu.get_barrier_semaphore()
    for k in range(1, n_ctx):
        signal(barrier, (jnp.bitwise_xor(index, k), rank))
    if tp_too:
        for device in neighbours():
            signal(barrier, device)
    pl.semaphore_wait(barrier, n_ctx - 1 + (2 if tp_too else 0))


def rotation(cos_tab, sin_tab, block_cos, block_sin):
    sign = jnp.where(lax.broadcasted_iota(jnp.int32, cos_tab.shape, 1) < HD // 2, -1.0, 1.0)
    return cos_tab * block_cos - sin_tab * block_sin, (sin_tab * block_cos + cos_tab * block_sin) * sign


def in_turn(count):
    return [count - 1] + list(range(count - 1))


def attend_rows(qs, ks, vs, os, tile):
    length = qs.shape[0]
    factor = -(HD ** (-0.5)) * LOG2E
    shift = math.log(length) * LOG2E
    row_at = lax.broadcasted_iota(jnp.int32, (tile, tile), 0)
    col_at = lax.broadcasted_iota(jnp.int32, (tile, tile), 1)
    for i in range(length // tile):
        query = qs[i * tile : (i + 1) * tile, :]

        def part(j, masked):
            at = pl.ds(pl.multiple_of(j * tile, tile), tile)
            raw = times_transposed(query, ks[at, :])
            prob = 1.0 / (1.0 + jnp.exp2(raw * factor + shift))
            if masked:
                prob = jnp.where(row_at >= col_at, prob, 0.0)
            return dot(prob.astype(BF), vs[at, :])

        total = part(i, True)
        if i > 0:
            total = lax.fori_loop(0, i, lambda j, acc: acc + part(j, False), total)
        os[i * tile : (i + 1) * tile, :] = total.astype(BF)


def forward_kernel(n_ctx, groups, units, tile, *refs):
    tokens_ref, cot_ref, wq_in, wk_in, wv_in, wo_in, gain_one, gain_two = refs[:8]
    cos_ref, sin_ref, bcos_ref, bsin_ref, valid_ref = refs[8:13]
    n1_out, got_out, heads_out, residual, n2_out, cot_out = refs[13:19]
    x_ref, rows_buf, own_buf, send, got, o_send, o_got, tabs, qs, ks, vs, os = refs[19:31]
    (wq_ref, wk_ref, wv_ref, wo_ref, weight_sem, cot_buf, cot_via, cot_sem), rest = refs[31:39], refs[39:]
    n_gather, n_exchange = len(Gather.scratch()), len(Exchange.scratch(1, 2))
    n1_sems, rest = rest[:n_gather], rest[n_gather:]
    n2_sems, rest = rest[:n_gather], rest[n_gather:]
    cot_sems, rest = rest[:n_gather], rest[n_gather:]
    x_sems, rest = rest[:n_exchange], rest[n_exchange:]
    o_sems, rest = rest[:n_exchange], rest[n_exchange:]
    (n1_sem, got_sem, load_sem), rest = rest[:3], rest[3:]
    me, rank = lax.axis_index("ctx"), lax.axis_index("tp")
    odd = lax.rem(rank, 2)
    heads = wq_ref.shape[1] // HD
    per_unit = n_ctx // heads
    own_at = [pl.multiple_of(odd * BLOCK, BLOCK), pl.multiple_of((1 - odd) * PAIR, BLOCK)]

    def load_x(g):
        _, rows, own = groups[g]
        return pltpu.make_async_copy(
            tokens_ref.at[pl.ds(own_at[g], rows)], x_ref.at[pl.ds(own, rows)], load_sem.at[g]
        )

    load_weights = [
        pltpu.make_async_copy(source, dest, weight_sem.at[k])
        for k, (source, dest) in enumerate(((wq_in, wq_ref), (wk_in, wk_ref), (wv_in, wv_ref), (wo_in, wo_ref)))
    ]
    for g in range(2):
        load_x(g).start()
    for copy in load_weights + own_copies(cot_ref, cot_buf, groups, cot_sem):
        copy.start()
    greet(n_ctx, True)
    gather_one = Gather(own_buf, rows_buf, groups, n1_sems, local=False)
    scatter = Scatter(rows_buf, groups, rest[:6], rest[6:], loaded=False)
    gather_two = Gather(own_buf, n2_out, groups, n2_sems, via=scatter.from_y)
    gather_cot = Gather(cot_buf, cot_out, groups, cot_sems, via=cot_via)
    trade = Exchange(got, x_sems, True)
    trade_back = Exchange(o_got, o_sems, False)

    def halves_of(u):
        return halves_at(odd if units[u][1] else 0)

    def normed(source, gain, at):
        values = source[at, :].astype(F32)
        return (values * inverse_rms(values) * gain[...].astype(F32)).astype(BF)

    def begin(g):
        base, rows, own = groups[g]
        load_x(g).wait()
        low = normed(x_ref, gain_one, pl.ds(own, rows))
        own_buf[pl.ds(own, rows), :] = low
        gather_one.start(g)
        rows_buf[pl.ds(base, rows), :] = low

    begin(0)
    for half, block in enumerate((me, 2 * n_ctx - 1 - me)):
        cos_part, sin_part = rotation(
            cos_ref[...], sin_ref[...], bcos_ref[pl.ds(block, 1), :], bsin_ref[pl.ds(block, 1), :]
        )
        tabs[0, half * BLOCK : (half + 1) * BLOCK, :] = cos_part
        tabs[1, half * BLOCK : (half + 1) * BLOCK, :] = sin_part

    def query(u, block):
        base, flipped = units[u]
        first, second = halves_of(u)
        at = pl.ds(base + block * PAIR, PAIR)
        rows = rows_buf[at, :]
        for which, w_ref in enumerate((wq_ref, wk_ref, wv_ref)):
            product = dot(rows, w_ref[...])
            for head in range(heads):
                part = product[:, head * HD : (head + 1) * HD]
                pair = block * heads + head
                for half, to in ((0, first), (1, second)):
                    piece = part[half * BLOCK : (half + 1) * BLOCK]
                    if which < 2:
                        piece = piece * tabs[0, to, :] + pltpu.roll(piece, HD // 2, 1) * tabs[1, to, :]
                    else:
                        piece = piece * valid_ref[pl.ds(base + block * PAIR + half * BLOCK, BLOCK), :]
                    send[u, pair, which, to, :] = piece.astype(BF)
        trade.start_some(send, u, block * heads, heads)

    store_n1 = pltpu.make_async_copy(rows_buf, n1_out, n1_sem)
    store_got = [pltpu.make_async_copy(got.at[u], got_out.at[u], got_sem.at[u]) for u in range(len(units))]

    for copy in load_weights:
        copy.wait()
    query(0, 0)
    gather_one.forward_x(0)
    gather_one.forward_y(0)
    begin(1)
    query(0, 1)
    query(1, 0)
    gather_one.finish(0)
    query(1, 1)
    gather_one.forward(1)
    gather_one.finish(1)
    for copy in own_copies(cot_ref, cot_buf, groups, cot_sem):
        copy.wait()
    for g in range(2):
        gather_cot.start(g)
    query(2, 0)
    query(2, 1)
    store_n1.start()

    def attend(u):
        trade.arrived(send, u)
        store_got[u].start()
        for k in range(n_ctx):
            front, back = both_places(me, k, n_ctx)
            for which, dest in enumerate((qs, ks, vs)):
                dest[front, :] = got[u, k, which, :BLOCK, :]
                dest[back, :] = got[u, k, which, BLOCK:, :]
        attend_rows(qs, ks, vs, os, tile)
        for k in range(n_ctx):
            front, back = both_places(me, k, n_ctx)
            o_send[u, k, :BLOCK, :] = os[front, :]
            o_send[u, k, BLOCK:, :] = os[back, :]
        trade_back.start(o_send, u)

    def project(u):
        trade_back.arrived(o_send, u)
        base, _ = units[u]
        first, second = halves_of(u)
        for block in range(per_unit):
            at = pl.ds(base + block * PAIR, PAIR)
            low = valid_ref[at, :].astype(BF)
            for head in range(heads):
                place = jnp.bitwise_xor(me, block * heads + head)
                part = jnp.concatenate([o_got[u, place, first, :], o_got[u, place, second, :]], axis=0)
                heads_out[at, head * HD : (head + 1) * HD] = part * low
            rows_buf[at, :] = dot(heads_out[at, :], wo_ref[...]).astype(BF)

    def use(at, total):
        residual[at, :] = x_ref[at, :].astype(F32) + total
        own_buf[at, :] = normed(residual, gain_two, at)

    def finish_group(g):
        scatter.total(g, use)
        gather_two.start(g)

    attend(0)
    for g in range(2):
        gather_one.sent(g)
    store_n1.wait()
    attend(1)
    for g in range(2):
        gather_cot.forward(g)
    project(0)
    scatter.start(0, (0,), loads=False)
    project(1)
    scatter.start(0, (1, 3, 2), loads=False)
    attend(2)
    scatter.forward(0)
    project(2)
    scatter.start(1, loads=False)
    finish_group(0)
    scatter.forward(1)
    finish_group(1)
    gather_two.forward(0)
    gather_two.forward(1)
    for u in range(len(units)):
        trade.sent(send, u)
        trade_back.sent(o_send, u)
        store_got[u].wait()
    for g in range(2):
        gather_cot.finish(g)
        gather_two.finish(g)
        gather_two.sent(g)
        gather_cot.sent(g)


def forward_layer(tokens_in, cot_in, gain_one, gain_two, wq, wk, wv, wo, tables, valid, n_ctx, groups, units):
    rows, depth = tokens_in.shape
    width = wq.shape[1]
    tokens = valid.shape[0]
    length = 2 * n_ctx * BLOCK
    n_units = len(units)
    vmem = lambda shape, dtype=BF: pltpu.VMEM(shape, dtype)
    outs = [
        jax.ShapeDtypeStruct((tokens, depth), BF),
        jax.ShapeDtypeStruct((n_units, n_ctx, 3, PAIR, HD), BF),
        jax.ShapeDtypeStruct((tokens, width), BF),
        jax.ShapeDtypeStruct((rows, depth), F32),
        jax.ShapeDtypeStruct((tokens, depth), BF),
        jax.ShapeDtypeStruct((tokens, depth), BF),
    ]
    return pl.pallas_call(
        functools.partial(forward_kernel, n_ctx, groups, units, min(512, length)),
        out_shape=outs,
        in_specs=[ANY_SPEC] * 6 + [VMEM_SPEC] * 7,
        out_specs=[ANY_SPEC, ANY_SPEC, VMEM_SPEC, VMEM_SPEC, ANY_SPEC, ANY_SPEC],
        scratch_shapes=[
            vmem((rows, depth)),
            vmem((tokens, depth)),
            vmem((rows, depth)),
            vmem((n_units, n_ctx, 3, PAIR, HD)),
            vmem((n_units, n_ctx, 3, PAIR, HD)),
            vmem((n_units, n_ctx, PAIR, HD)),
            vmem((n_units, n_ctx, PAIR, HD)),
            vmem((2, PAIR, HD), F32),
        ]
        + [vmem((length, HD))] * 4
        + [vmem(wq.shape)] * 3
        + [vmem(wo.shape), pltpu.SemaphoreType.DMA((4,))]
        + [vmem((rows, depth)), vmem((rows, depth)), pltpu.SemaphoreType.DMA((2,))]
        + Gather.scratch() * 3
        + Exchange.scratch(n_units, n_ctx) * 2
        + [pltpu.SemaphoreType.DMA, pltpu.SemaphoreType.DMA((n_units,)), pltpu.SemaphoreType.DMA((2,))]
        + Scatter.scratch(rows, depth, loaded=False),
        compiler_params=pltpu.CompilerParams(vmem_limit_bytes=VMEM_LIMIT, collective_id=3, has_side_effects=True),
        cost_estimate=pl.CostEstimate(
            flops=8 * tokens * depth * width, bytes_accessed=8 * tokens * depth, transcendentals=0
        ),
    )(tokens_in, cot_in, wq, wk, wv, wo, gain_one, gain_two, *tables, valid)


def attend_rows_back(qs, ks, vs, gs, os, dqs, cos_ref, sin_ref, tile):
    length = qs.shape[0]
    scale = HD ** (-0.5)
    factor = -scale * LOG2E
    shift = math.log(length) * LOG2E
    count = length // tile
    key_at = lax.broadcasted_iota(jnp.int32, (tile, tile), 0)
    query_at = lax.broadcasted_iota(jnp.int32, (tile, tile), 1)
    dqs[...] = jnp.zeros_like(dqs)

    def unrotate(values, at):
        return (values * cos_ref[at, :] - pltpu.roll(values, HD // 2, 1) * sin_ref[at, :]).astype(BF)

    for j in range(count):
        own = slice(j * tile, (j + 1) * tile)
        keys = ks[own, :]
        values = vs[own, :]

        def part(i, masked):
            at = pl.ds(pl.multiple_of(i * tile, tile), tile)
            query = qs[at, :]
            grad = gs[at, :]
            raw = times_transposed(keys, query)
            prob = 1.0 / (1.0 + jnp.exp2(raw * factor + shift))
            if masked:
                prob = jnp.where(query_at >= key_at, prob, 0.0)
            prob_grad = times_transposed(values, grad)
            score_grad = (prob_grad * prob * (1.0 - prob)).astype(BF)
            dqs[at, :] += contract_rows(score_grad, keys)
            return dot(score_grad, query), dot(prob.astype(BF), grad)

        total = part(j, True)
        if j + 1 < count:

            def step(i, acc):
                more = part(i, False)
                return acc[0] + more[0], acc[1] + more[1]

            total = lax.fori_loop(j + 1, count, step, total)
        os[1, own, :] = unrotate(total[0] * scale, own)
        os[2, own, :] = total[1].astype(BF)
    for i in range(count):
        at = slice(i * tile, (i + 1) * tile)
        os[0, at, :] = unrotate(dqs[at, :] * scale, at)


def middle_kernel(n_ctx, groups, units, tile, *refs):
    da_ref, got_ref, h_ref, residual_ref, wd_ref, wq_in, wk_in, wv_in, wo_in = refs[:9]
    cos_ref, sin_ref, bcos_ref, bsin_ref, valid_ref = refs[9:14]
    grad_ref, partial_out, output = refs[14:17]
    rows_buf, got, do_send, do_got, back_got, h_buf, wd_buf, res_buf, cos_full, sin_full = refs[17:27]
    qs, ks, vs, gs, os, dqs = refs[27:33]
    (wq_ref, wk_ref, wv_ref, wo_ref, weight_sem), rest = refs[33:38], refs[38:]
    load_weights = [
        pltpu.make_async_copy(source, dest, weight_sem.at[k])
        for k, (source, dest) in enumerate(((wo_in, wo_ref), (wq_in, wq_ref), (wk_in, wk_ref), (wv_in, wv_ref)))
    ]
    load_weights[0].start()
    back_send = got
    n_exchange = len(Exchange.scratch(1, 2))
    do_sems, back_sems, rest = rest[:n_exchange], rest[n_exchange : 2 * n_exchange], rest[2 * n_exchange :]
    (da_sem, got_sem, out_sem, h_sem, wd_sem, res_sem, y_sem), rest = rest[:7], rest[7:]
    me, rank = lax.axis_index("ctx"), lax.axis_index("tp")
    odd = lax.rem(rank, 2)
    heads = wq_ref.shape[1] // HD
    per_unit = n_ctx // heads
    unit_rows = per_unit * PAIR
    count = len(units)
    order = in_turn(count)

    def rows_of(u):
        return pl.ds(units[u][0], unit_rows)

    load_da = [pltpu.make_async_copy(da_ref.at[rows_of(u)], rows_buf.at[rows_of(u)], da_sem.at[u]) for u in range(count)]
    load_got = [pltpu.make_async_copy(got_ref.at[u], got.at[u], got_sem.at[u]) for u in range(count)]
    for u in order:
        load_da[u].start()
    for u in order:
        load_got[u].start()
    first_wd = pltpu.make_async_copy(wd_ref.at[:, pl.ds(0, wd_buf.shape[1])], wd_buf, wd_sem)
    first_wd.start()
    for copy in load_weights[1:]:
        copy.start()
    greet(n_ctx, True)
    scatter = Scatter(rows_buf, groups, rest[:6], rest[6:], loaded=False)
    trade = Exchange(do_got, do_sems, True)
    trade_back = Exchange(back_got, back_sems, False)

    load_weights[0].wait()
    for u in order:
        load_da[u].wait()
        base, flipped = units[u]
        first, second = halves_at(odd if flipped else 0)
        for block in range(per_unit):
            at = pl.ds(base + block * PAIR, PAIR)
            grad = times_transposed(rows_buf[at, :], wo_ref[...]).astype(BF)
            low = valid_ref[at, :].astype(BF)
            for head in range(heads):
                part = grad[:, head * HD : (head + 1) * HD] * low
                do_send[u, block * heads + head, first, :] = part[:BLOCK]
                do_send[u, block * heads + head, second, :] = part[BLOCK:]
        trade.start(do_send, u)
    for block in range(2 * n_ctx):
        at = slice(block * BLOCK, (block + 1) * BLOCK)
        cos_full[at, :], sin_full[at, :] = rotation(
            cos_ref[...], sin_ref[...], bcos_ref[block : block + 1, :], bsin_ref[block : block + 1, :]
        )
    for copy in load_weights[1:]:
        copy.wait()
    for u in order:
        load_got[u].wait()

    def attend(turn, carry):
        u = lax.rem(turn + count - 1, count)
        trade.arrived(do_send, u)
        for k in range(n_ctx):
            front, back = both_places(me, k, n_ctx)
            for which, dest in enumerate((qs, ks, vs)):
                dest[front, :] = got[u, k, which, :BLOCK, :]
                dest[back, :] = got[u, k, which, BLOCK:, :]
            gs[front, :] = do_got[u, k, :BLOCK, :]
            gs[back, :] = do_got[u, k, BLOCK:, :]
        attend_rows_back(qs, ks, vs, gs, os, dqs, cos_full, sin_full, tile)
        for k in range(n_ctx):
            front, back = both_places(me, k, n_ctx)
            for which in range(3):
                back_send[u, k, which, :BLOCK, :] = os[which, front, :]
                back_send[u, k, which, BLOCK:, :] = os[which, back, :]
        trade_back.start(back_send, u)
        return carry

    lax.fori_loop(0, count, attend, 0)

    tiles = rows_buf.shape[0] // PAIR

    def tile_rows(tile):
        return pl.ds(pl.multiple_of(tile * PAIR, PAIR), PAIR)

    def load_h(step):
        slot = lax.rem(step, 2)
        return pltpu.make_async_copy(h_ref.at[tile_rows(lax.rem(step, tiles))], h_buf.at[slot], h_sem.at[slot])

    columns = wd_buf.shape[1]
    parts = rows_buf.shape[1] // columns

    def part_columns(part):
        return pl.ds(pl.multiple_of(part * columns, columns), columns)

    def load_wd(part):
        return pltpu.make_async_copy(wd_ref.at[:, part_columns(part)], wd_buf, wd_sem)

    load_h(0).start()

    def down(step, carry):
        part, tile = step // tiles, lax.rem(step, tiles)

        @pl.when(step + 1 < tiles * parts)
        def _():
            load_h(step + 1).start()

        @pl.when(tile == 0)
        def _():
            @pl.when(part > 0)
            def _():
                load_wd(part).start()

            load_wd(part).wait()

        load_h(step).wait()
        rows_buf[tile_rows(tile), part_columns(part)] = dot(h_buf[lax.rem(step, 2)], wd_buf[...]).astype(BF)
        return carry

    lax.fori_loop(0, tiles * parts, down, 0)
    last_group = len(groups) - 1
    out_rows = rest[0]
    for g in (last_group, 0):
        scatter.start(g, loads=False)

    def use(at, total):
        size = total.shape[0]
        load = pltpu.make_async_copy(residual_ref.at[at], res_buf.at[pl.ds(0, size)], res_sem)
        load.start()
        load.wait()
        low = (res_buf[:size, :] + total).astype(BF)
        out_rows[at, :] = low

    def store(number, first):
        slot = number % 2
        return pltpu.make_async_copy(h_buf.at[slot], partial_out.at[pl.ds(first, PAIR)], out_sem.at[slot])

    stored = []
    for turn, u in enumerate(order):
        trade_back.arrived(back_send, u)
        base, flipped = units[u]
        first, second = halves_at(odd if flipped else 0)
        for block in range(per_unit):
            at = pl.ds(base + block * PAIR, PAIR)
            low = valid_ref[at, :].astype(BF)
            total = None
            for which, w_ref in enumerate((wq_ref, wk_ref, wv_ref)):
                width = heads * HD
                for head in range(heads):
                    place = jnp.bitwise_xor(me, block * heads + head)
                    part = jnp.concatenate(
                        [back_got[u, place, which, first, :], back_got[u, place, which, second, :]], axis=0
                    )
                    columns = slice(which * width + head * HD, which * width + (head + 1) * HD)
                    grad_ref[at, columns] = part * low if which == 2 else part
                product = times_transposed(grad_ref[at, which * width : (which + 1) * width], w_ref[...])
                total = product if total is None else total + product
            number = len(stored)
            if number >= 2:
                stored[number - 2].wait()
            h_buf[number % 2] = total.astype(BF)
            stored.append(store(number, base + block * PAIR))
            stored[-1].start()
        if turn == 0:
            scatter.forward(last_group)
            scatter.forward(0)
        if turn == 1:
            for g in (last_group, 0):
                scatter.total(g, use)
            store_y = pltpu.make_async_copy(out_rows, output, y_sem)
            store_y.start()
    store_y.wait()
    for copy in stored[-2:]:
        copy.wait()
    for u in order:
        trade.sent(do_send, u)
        trade_back.sent(back_send, u)


def middle_layer(da, got, h, residual, wq, wk, wv, wo, wd, tables, valid, n_ctx, groups, units):
    tokens, depth = da.shape
    width = wq.shape[1]
    length = 2 * n_ctx * BLOCK
    count = len(units)
    vmem = lambda shape, dtype=BF: pltpu.VMEM(shape, dtype)
    dma = pltpu.SemaphoreType.DMA
    three, one = (count, n_ctx, 3, PAIR, HD), (count, n_ctx, PAIR, HD)
    most_rows = max(rows for _, rows, _ in groups) // 2
    return pl.pallas_call(
        functools.partial(middle_kernel, n_ctx, groups, units, min(512, length)),
        out_shape=[
            jax.ShapeDtypeStruct((tokens, 3 * width), BF),
            jax.ShapeDtypeStruct((tokens, depth), BF),
            jax.ShapeDtypeStruct(residual.shape, BF),
        ],
        in_specs=[ANY_SPEC] * 9 + [VMEM_SPEC] * 5,
        out_specs=[VMEM_SPEC, ANY_SPEC, ANY_SPEC],
        scratch_shapes=[vmem((tokens, depth)), vmem(three), vmem(one), vmem(one), vmem(three)]
        + [vmem((2, PAIR, depth)), vmem((h.shape[1], depth // 2)), vmem((most_rows, depth), F32)]
        + [vmem((length, HD), F32)] * 2
        + [vmem((length, HD))] * 4
        + [vmem((3, length, HD)), vmem((length, HD), F32)]
        + [vmem(wq.shape)] * 3
        + [vmem(wo.shape), dma((4,))]
        + Exchange.scratch(count, n_ctx) * 2
        + [dma((count,)), dma((count,)), dma((2,)), dma((2,)), dma, dma, dma]
        + Scatter.scratch(residual.shape[0], depth, loaded=False),
        compiler_params=pltpu.CompilerParams(vmem_limit_bytes=VMEM_LIMIT, collective_id=4, has_side_effects=True),
        cost_estimate=pl.CostEstimate(
            flops=8 * tokens * depth * width + 2 * tokens * depth * h.shape[1],
            bytes_accessed=8 * tokens * depth,
            transcendentals=0,
        ),
    )(da, got, h, residual, wd, wq, wk, wv, wo, *tables, valid)


def body(
    tokens,
    counts,
    norm_gain,
    w_query,
    w_key,
    w_value,
    w_output,
    mlp_gain,
    w_gate,
    w_up,
    w_down,
    cotangent,
):
    n_ctx = lax.axis_size("ctx")
    me = lax.axis_index("ctx")
    rank = lax.axis_index("tp")
    odd = rank & 1
    core = me & 1
    length = 2 * BLOCK * n_ctx
    heads = w_query.shape[1] // HD
    gain_one = norm_gain.astype(F32)
    gain_two = mlp_gain.astype(F32)

    inverse = THETA ** (-(jnp.arange(HD // 2, dtype=F32) * (2.0 / HD)))
    angles = jnp.arange(length, dtype=jnp.int32).astype(F32)[:, None] * inverse[None, :]
    cos_half, sin_half = jnp.cos(angles), jnp.sin(angles)
    cos_full = jnp.concatenate([cos_half, cos_half], axis=1)
    sin_full = jnp.concatenate([-sin_half, sin_half], axis=1)

    def own_blocks(table):
        front = lax.dynamic_slice_in_dim(table, me * BLOCK, BLOCK, 0)
        back = lax.dynamic_slice_in_dim(table, (2 * n_ctx - 1 - me) * BLOCK, BLOCK, 0)
        return front, back

    cos_front, cos_back = own_blocks(cos_full)
    sin_front, sin_back = own_blocks(sin_full)
    own_counts = lax.dynamic_index_in_dim(counts, me, 0, keepdims=False)
    offsets = jnp.arange(BLOCK, dtype=jnp.int32)

    def valid_of(sequence_list, half_list):
        held = own_counts[jnp.stack(sequence_list), jnp.stack(half_list)]
        return (offsets[None, :] < held[:, None]).astype(F32).reshape(-1)

    cos_own = jnp.concatenate([cos_front, cos_back])
    sin_own = jnp.concatenate([sin_front, sin_back])
    sequences = counts.shape[1]
    paired = by_four() and sequences == 6 and n_ctx == 2 * heads
    if paired:
        ranks = [rank ^ k for k in range(4)]
        blocks_a = [(3 * (r >> 1) + 2 * (r & 1), jnp.int32(half)) for r in ranks for half in range(2)]
        blocks_b = [(1 + 3 * (r >> 1), r & 1) for r in ranks]
        flat_valid = valid_of(*zip(*(blocks_a + blocks_b)))
        valids = {"b": flat_valid[len(blocks_a) * BLOCK :], "a": flat_valid[: len(blocks_a) * BLOCK]}
        flip_back = lambda own: jnp.where(odd == 1, jnp.roll(own, BLOCK, axis=0), own)
        tables = {
            "b": (jnp.tile(flip_back(cos_own), (2, 1)), jnp.tile(flip_back(sin_own), (2, 1))),
            "a": (jnp.tile(cos_own, (4, 1)), jnp.tile(sin_own, (4, 1))),
        }
        scalars = {"b": jnp.stack([me, odd]).astype(jnp.int32), "a": jnp.stack([me, 0]).astype(jnp.int32)}
        n_pairs = {"b": 2 * heads, "a": 4 * heads}
    else:
        flat_valid = (offsets[None, None, :] < own_counts[:, :, None]).astype(F32).reshape(-1)
        valids = {"a": flat_valid}
        tables = {"a": (jnp.tile(cos_own, (sequences, 1)), jnp.tile(sin_own, (sequences, 1)))}
        scalars = {"a": jnp.stack([me, 0]).astype(jnp.int32)}
        n_pairs = {"a": sequences * heads}
    names = tuple(n_pairs)

    def own_rows(array):
        if not paired:
            return {"a": array}
        return {
            "b": lax.dynamic_slice_in_dim(array, (1 - odd) * PAIR, BLOCK, 0),
            "a": lax.dynamic_slice_in_dim(array, odd * BLOCK, PAIR, 0),
        }

    x_own = {name: rows.astype(F32) for name, rows in own_rows(tokens[0]).items()}
    g_own = own_rows(cotangent[0])

    split = by_four()
    rows_of = {name: valids[name].shape[0] for name in names}
    total_rows = sum(rows_of.values())
    first_row = {"a": 0, "b": rows_of["a"]}
    valid_head = {name: jnp.broadcast_to(valids[name][:, None], (rows_of[name], HD)) for name in names}
    valid_wide = {name: jnp.broadcast_to(valids[name][:, None].astype(BF), (rows_of[name], heads * HD)) for name in names}
    near = [k for k in range(n_ctx) if k < 6]
    far = [k for k in range(n_ctx) if k >= 6]
    state = {}

    def fence():
        names_held = list(state)
        values = lax.optimization_barrier([state[name] for name in names_held])
        state.update(zip(names_held, values))

    def only_b(step):
        if "b" in names:
            step("b")

    def norm_one(n):
        state["n1", n] = (x_own[n] * inverse_rms(x_own[n]) * gain_one).astype(BF)

    def gather_a(key):
        def step(n):
            state[key, n] = gather_first(state[key, n])

        return step

    def gather_b(key):
        def step(n):
            state[key, n] = gather_second(state[key, n])

        return step

    def query(n):
        state["n1", n] = gathered(state["n1", n])
        cos_tab, sin_tab = tables[n]
        state["qkv", n] = project_qkv(
            scalars[n], state["n1", n], w_query, w_key, w_value, cos_tab, sin_tab, valid_head[n], n_ctx
        )

    def swap_part(key, places, to):
        def step(n):
            got = dict(state.get((to, n), {}))
            got.update(exchange(state[key, n], places, n_ctx))
            state[to, n] = got
            if len(got) == n_ctx:
                state[to, n] = [got[k] for k in range(n_ctx)]
                del state[key, n]

        return step

    def attend(n):
        state["mixed", n] = attention_forward(scalars[n], state["got", n], n_ctx)

    def project(n):
        heads_out, *parts = project_out(
            scalars[n], state.pop(("back", n)), w_output, valid_wide[n], n_pairs[n], n_ctx, split
        )
        state["heads", n], state["r", n] = heads_out, tuple(parts)

    def scatter_a(key):
        def step(n):
            state[key, n] = scatter_first(state[key, n])

        return step

    def scatter_b(key):
        def step(n):
            state[key, n] = scatter_second(state[key, n])

        return step

    def norm_two(n):
        residual = x_own[n] + scattered(state.pop(("r", n)))
        state["residual", n] = residual
        state["n2", n] = (residual * inverse_rms(residual) * gain_two).astype(BF)

    def core_mlp(n):
        state["n2", n] = gathered(state["n2", n])
        state["cot", n] = gathered(state["cot", n])
        held = state.get("mlp", ())
        state["mlp"] = mlp_core(
            state["n2", n], state["cot", n], w_gate, w_up, w_down, total_rows, first_row[n], held
        )

    def attend_back(n):
        state["dqkv", n] = attention_backward(
            scalars[n], state.pop(("got", n)), state.pop(("gdo", n)), cos_full, sin_full, n_ctx
        )

    def query_back(n):
        dq, dk, dv, *parts = project_in(
            scalars[n], state.pop(("gdqkv", n)), (w_query, w_key, w_value), valid_wide[n], n_pairs[n], n_ctx, False
        )
        state["dq", n], state["dk", n], state["dv", n], state["i", n] = dq, dk, dv, parts[0]

    def joined(key):
        parts = [state[key, n] for n in ("a", "b") if n in names]
        return jnp.concatenate(parts) if len(parts) > 1 else parts[0]

    groups = tuple((first_row[n], rows_of[n] // 4, first_row[n] // 4) for n in ("a", "b") if n in names)

    if paired:
        units = ((0, False), (2 * PAIR, False), (4 * PAIR, True))
        wide_valid = jnp.broadcast_to(flat_valid[:, None], (total_rows, HD))
        twice = lambda table: jnp.concatenate([table, table], axis=1)
        starts = BLOCK * jnp.arange(2 * n_ctx, dtype=jnp.int32)
        spans = [at.astype(F32)[:, None] * inverse[None, :] for at in (offsets, starts)]
        turns = [twice(part(angle)) for angle in spans for part in (jnp.cos, jnp.sin)]
        all_n1, got, heads_out, own_residual, all_n2, all_cot = forward_layer(
            tokens[0], cotangent[0], norm_gain[None], mlp_gain[None], w_query, w_key, w_value, w_output,
            turns, wide_valid, n_ctx, groups, units,
        )
    else:
        norm_one("a")
        state["cot", "a"] = g_own["a"]
        gather_a("n1")("a")
        query("a")
        swap_part("qkv", range(n_ctx), "got")("a")
        attend("a")
        swap_part("mixed", range(n_ctx), "back")("a")
        project("a")
        scatter_a("r")("a")
        norm_two("a")
        gather_a("n2")("a")
        gather_a("cot")("a")
        all_n1, all_n2, all_cot = state["n1", "a"], gathered(state["n2", "a"]), gathered(state["cot", "a"])
        heads_out, own_residual = state["heads", "a"], state["residual", "a"]
    if paired:
        extra = feed_extra(groups, all_n2, w_gate, w_up, w_down, own_residual, cotangent[0], mlp_gain[None])
        sum_down, sum_gate, sum_up, sum_out, dr, da, gain_two_grad, _, h, _, _ = weight_sums(
            [(w_down.shape[0], 0), (all_n2, 1), (all_n2, 2), (heads_out, 3)],
            [all_cot], n_ctx, 1, extra, late=(5, 6, 1), limit=62 * 1024 * 1024,
        )
        dqkv, i_partial, output = middle_layer(
            da, got, h, own_residual, w_query, w_key, w_value, w_output, w_down, turns, wide_valid, n_ctx, groups, units
        )
        extra = input_extra(n_ctx, groups, i_partial, tokens[0], dr, norm_gain[None], gain_two_grad)
        sum_qkv, input_grad, gain_sums = weight_sums(
            [(all_n1, 0)], [dqkv], n_ctx, 2, extra
        )
    else:
        own_grads = cotangent[0]
        h, dgp, dup = mlp_core(all_n2, all_cot, w_gate, w_up, w_down, total_rows, 0)
        d_partial = (times_transposed(dgp, w_gate) + times_transposed(dup, w_up)).astype(BF)
        y_partial = dot(h, w_down).astype(BF)
        (sum_down,) = weight_sums([(h, 0)], [all_cot], n_ctx, 1)
        sum_gate, sum_up = weight_sums([(all_n2, 0), (all_n2, 1)], [dgp, dup], n_ctx, 2)
        back, gain_two_grad = norm_back_rows(own_residual, gain_two, scattered(scatter_first((d_partial,))))
        dr = own_grads.astype(F32) + back
        da = gathered(gather_first(dr.astype(BF)))
        output = (own_residual + scattered(scatter_first((y_partial,)))).astype(BF)
        state["do", "a"] = heads_back(scalars["a"], da, w_output, valid_wide["a"], n_ctx)
        swap_part("do", range(n_ctx), "gdo")("a")
        attend_back("a")
        swap_part("dqkv", range(n_ctx), "gdqkv")("a")
        query_back("a")
        (sum_out,) = weight_sums([(heads_out, 0)], [da], n_ctx, 3)
        (sum_qkv,) = weight_sums(
            [(all_n1, 0)], [jnp.concatenate([state[key, "a"] for key in ("dq", "dk", "dv")], axis=1)], n_ctx, 4
        )
        back, gain_one_grad = norm_back_rows(x_own["a"], gain_one, scattered(scatter_first((state["i", "a"],))))
        input_grad = (dr + back).astype(BF)
    sums = (sum_out, sum_gate, sum_up, sum_down, sum_qkv)
    if paired:
        *grads, output, input_grad, grad_norm_gain, grad_mlp_gain = cast_sums(sums, groups, (output, input_grad), gain_sums)
        gains = grad_norm_gain[0], grad_mlp_gain[0]
    else:
        grads = cast_sums(sums)
        gains = lax.psum(jnp.concatenate([gain_one_grad, gain_two_grad]), ("ctx", "tp"))
    grad_out, grad_gate, grad_up, grad_down, grad_query, grad_key, grad_value = grads
    return (
        output[None],
        input_grad[None],
        gains[0],
        grad_query,
        grad_key,
        grad_value,
        grad_out,
        gains[1],
        grad_gate,
        grad_up,
        grad_down,
    )


def solution(mesh):
    placed = (
        P("ctx", "tp", None),
        P(),
        P(),
        P(None, "tp"),
        P(None, "tp"),
        P(None, "tp"),
        P("tp", None),
        P(),
        P(None, "tp"),
        P(None, "tp"),
        P("tp", None),
        P("ctx", "tp", None),
    )
    return jax.shard_map(
        body,
        mesh=mesh,
        in_specs=placed,
        out_specs=(
            P("ctx", "tp", None),
            P("ctx", "tp", None),
            P(),
            P(None, "tp"),
            P(None, "tp"),
            P(None, "tp"),
            P("tp", None),
            P(),
            P(None, "tp"),
            P(None, "tp"),
            P("tp", None),
        ),
        check_vma=False,
    )
```

```python
import functools
import math

import jax
import jax.numpy as jnp
from jax import lax
from jax.experimental import pallas as pl
from jax.experimental.pallas import tpu as pltpu
from jax.sharding import PartitionSpec as P

HD = 128
BLOCK = 128
PAIR = 2 * BLOCK
EPS = 1e-05
THETA = 10000.0
LOG2E = 1.4426950408889634
BF = jnp.bfloat16
F32 = jnp.float32
VMEM_LIMIT = 60 * 1024 * 1024

X_SWAP = [(i, i ^ 1) for i in range(4)]
Y_SWAP = [(i, i ^ 2) for i in range(4)]


def dot(left, right):
    return jnp.dot(left, right, preferred_element_type=F32)


def contract_rows(left, right):
    return lax.dot_general(left, right, (((0,), (0,)), ((), ())), preferred_element_type=F32)


def times_transposed(left, right):
    return lax.dot_general(left, right, (((1,), (1,)), ((), ())), preferred_element_type=F32)


def send_x(values):
    return lax.ppermute(values, "tp", X_SWAP)


def send_y(values):
    return lax.ppermute(values, "tp", Y_SWAP)


def by_four():
    return lax.axis_size("tp") == 4


def gather_first(own):
    if not by_four():
        return (lax.all_gather(own, "tp", axis=0, tiled=True),)
    return own, send_x(own), send_y(own)


def gather_second(held):
    if len(held) == 1:
        return held
    own, from_x, from_y = held
    half = own.shape[0] // 2
    return own, from_x, from_y, send_x(from_y[:half]), send_y(from_x[half:])


def gathered(held):
    return jnp.concatenate(held) if len(held) > 1 else held[0]


def scatter_parts(partial):
    if not by_four():
        return (partial,)
    rows = partial.shape[0] // 4
    half = rows // 2
    at = lambda first: partial[first * half : (first + 1) * half]
    return (
        jnp.concatenate([at(2), at(6)]),
        jnp.concatenate([at(5), at(7)]),
        jnp.concatenate([at(0), at(1), at(4), at(3)]),
    )


def scatter_first(parts):
    if len(parts) == 1:
        return (lax.psum_scatter(parts[0], "tp", scatter_dimension=0, tiled=True),)
    return send_x(parts[0]), send_y(parts[1]), parts[2]


def add_low(left, right):
    return (left.astype(F32) + right.astype(F32)).astype(BF)


def scatter_second(held):
    if len(held) == 1:
        return held
    from_x, from_y, stay = held
    half = from_x.shape[0] // 2
    low_rest = send_y(add_low(stay[2 * half : 3 * half], from_x[half:]))
    high_rest = send_x(add_low(stay[3 * half :], from_y[half:]))
    return from_x, from_y, stay, low_rest, high_rest


def scattered(held):
    if len(held) == 1:
        return held[0].astype(F32)
    from_x, from_y, stay, low_rest, high_rest = (part.astype(F32) for part in held)
    half = low_rest.shape[0]
    low = stay[:half] + from_x[:half] + low_rest
    high = stay[half : 2 * half] + from_y[:half] + high_rest
    return jnp.concatenate([low, high])


def exchange(pieces, places, n_ctx):
    got = {}
    for k in places:
        got[k] = pieces[k] if k == 0 else lax.ppermute(pieces[k], "ctx", [(i, i ^ k) for i in range(n_ctx)])
    return got


def params():
    return pltpu.CompilerParams(vmem_limit_bytes=VMEM_LIMIT)


def whole(shape):
    return pl.BlockSpec(shape, lambda *_: (0,) * len(shape))


def put_partial(refs, first, value, rows):
    if len(refs) == 1:
        refs[0][first : first + value.shape[0], :] = value
        return
    to_x, to_y, stay = refs
    half = rows // 2
    homes = {
        0: (stay, 0), 1: (stay, 1), 2: (to_x, 0), 3: (stay, 3), 4: (stay, 2), 5: (to_y, 0), 6: (to_x, 1), 7: (to_y, 1)
    }
    for part in range(value.shape[0] // half):
        ref, place = homes[first // half + part]
        ref[place * half : (place + 1) * half, :] = value[part * half : (part + 1) * half]


def partial_shapes(rows, width, split):
    if not split:
        return [jax.ShapeDtypeStruct((rows, width), BF)]
    return [jax.ShapeDtypeStruct((rows // 4, width), BF)] * 2 + [jax.ShapeDtypeStruct((rows // 2, width), BF)]


def per_device(pairs, n_ctx):
    return -(-pairs // n_ctx)


def halves_at(swap):
    first = pl.multiple_of(swap * BLOCK, BLOCK)
    second = pl.multiple_of((1 - swap) * BLOCK, BLOCK)
    return pl.ds(first, BLOCK), pl.ds(second, BLOCK)


def qkv_kernel(n_ctx, pairs, scalar_ref, n_ref, wq_ref, wk_ref, wv_ref, cos_ref, sin_ref, valid_ref, *rest):
    out_refs, buffer = rest[:n_ctx], rest[n_ctx]
    rows = n_ref[...]
    first, second = halves_at(scalar_ref[1])
    me = scalar_ref[0]
    cos_tab = cos_ref[...]
    sin_tab = sin_ref[...]
    heads = wq_ref.shape[1] // HD
    step = pl.program_id(0)
    per = out_refs[0].shape[0]
    for pair in range(pairs, per * n_ctx):
        buffer[pair] = jnp.zeros(buffer.shape[1:], BF)
    for which, w_ref in enumerate((wq_ref, wk_ref, wv_ref)):
        product = dot(rows, w_ref[...])
        for head in range(heads):
            part = product[:, head * HD : (head + 1) * HD]
            if which < 2:
                part = part * cos_tab + pltpu.roll(part, HD // 2, 1) * sin_tab
            else:
                part = part * valid_ref[...]
            part = part.astype(BF)
            buffer[step * heads + head, which, first, :] = part[:BLOCK]
            buffer[step * heads + head, which, second, :] = part[BLOCK:]

    @pl.when(step == pl.num_programs(0) - 1)
    def _():
        for k in range(n_ctx):
            source = jnp.bitwise_xor(me, k)
            for p in range(per):
                out_refs[k][p] = buffer[source * per + p]


def project_qkv(scalars, normed, wq, wk, wv, cos_tab, sin_tab, valid, n_ctx):
    rows, depth = normed.shape
    width = wq.shape[1]
    heads = width // HD
    steps = rows // PAIR
    per = per_device(steps * heads, n_ctx)
    row_block = pl.BlockSpec((PAIR, HD), lambda i, s: (i, 0))
    weight = whole((depth, width))
    piece = (per, 3, PAIR, HD)
    return pl.pallas_call(
        functools.partial(qkv_kernel, n_ctx, steps * heads),
        out_shape=[jax.ShapeDtypeStruct(piece, BF)] * n_ctx,
        grid_spec=pltpu.PrefetchScalarGridSpec(
            num_scalar_prefetch=1,
            grid=(steps,),
            in_specs=[
                pl.BlockSpec((PAIR, depth), lambda i, s: (i, 0)),
                weight,
                weight,
                weight,
                row_block,
                row_block,
                row_block,
            ],
            out_specs=[whole(piece)] * n_ctx,
            scratch_shapes=[pltpu.VMEM((per * n_ctx, 3, PAIR, HD), BF)],
        ),
        compiler_params=params(),
        cost_estimate=pl.CostEstimate(
            flops=6 * rows * depth * width, bytes_accessed=rows * depth * 2 + 6 * depth * width, transcendentals=0
        ),
    )(scalars, normed, wq, wk, wv, cos_tab, sin_tab, valid)


def out_kernel(n_ctx, pairs, scalar_ref, *refs):
    piece_refs, (w_ref, valid_ref), (heads_ref, *partial_refs), buffer = (
        refs[:n_ctx],
        refs[n_ctx : n_ctx + 2],
        refs[n_ctx + 2 : -1],
        refs[-1],
    )
    me = scalar_ref[0]
    first, second = halves_at(scalar_ref[1])
    per = piece_refs[0].shape[0]
    heads = w_ref.shape[0] // HD
    for k in range(n_ctx):
        source = jnp.bitwise_xor(me, k)
        for p in range(per):
            buffer[source * per + p] = piece_refs[k][p]
    weight = w_ref[...]
    for sequence in range(pairs // heads):
        at = slice(sequence * PAIR, (sequence + 1) * PAIR)
        rows = jnp.concatenate(
            [
                jnp.concatenate(
                    [buffer[sequence * heads + head, first, :], buffer[sequence * heads + head, second, :]], axis=0
                )
                for head in range(heads)
            ],
            axis=1,
        )
        rows = rows * valid_ref[at, :]
        heads_ref[at, :] = rows
        put_partial(partial_refs, sequence * PAIR, dot(rows, weight).astype(BF), pairs // heads * PAIR // 4)


def project_out(scalars, pieces, weight, valid, pairs, n_ctx, split):
    width, depth = weight.shape
    rows = valid.shape[0]
    per = pieces[0].shape[0]
    shapes = [jax.ShapeDtypeStruct((rows, width), BF)] + partial_shapes(rows, depth, split)
    return pl.pallas_call(
        functools.partial(out_kernel, n_ctx, pairs),
        out_shape=shapes,
        grid_spec=pltpu.PrefetchScalarGridSpec(
            num_scalar_prefetch=1,
            grid=(1,),
            in_specs=[whole(piece.shape) for piece in pieces] + [whole(weight.shape), whole(valid.shape)],
            out_specs=[whole(shape.shape) for shape in shapes],
            scratch_shapes=[pltpu.VMEM((per * n_ctx, PAIR, HD), BF)],
        ),
        compiler_params=params(),
        cost_estimate=pl.CostEstimate(
            flops=2 * rows * depth * width, bytes_accessed=rows * depth * 2 + 2 * depth * width, transcendentals=0
        ),
    )(scalars, *pieces, weight, valid)


def heads_back_kernel(n_ctx, scalar_ref, da_ref, w_ref, valid_ref, *rest):
    out_refs, buffer = rest[:n_ctx], rest[n_ctx]
    me = scalar_ref[0]
    first, second = halves_at(scalar_ref[1])
    per = out_refs[0].shape[0]
    heads = w_ref.shape[0] // HD
    weight = w_ref[...]
    for pair in range(da_ref.shape[0] // PAIR * heads, per * n_ctx):
        buffer[pair] = jnp.zeros(buffer.shape[1:], BF)
    for sequence in range(da_ref.shape[0] // PAIR):
        at = slice(sequence * PAIR, (sequence + 1) * PAIR)
        grad = times_transposed(da_ref[at, :], weight).astype(BF) * valid_ref[at, :]
        for head in range(heads):
            part = grad[:, head * HD : (head + 1) * HD]
            buffer[sequence * heads + head, first, :] = part[:BLOCK]
            buffer[sequence * heads + head, second, :] = part[BLOCK:]
    for k in range(n_ctx):
        source = jnp.bitwise_xor(me, k)
        for p in range(per):
            out_refs[k][p] = buffer[source * per + p]


def heads_back(scalars, da, weight, valid, n_ctx):
    rows, depth = da.shape
    width = weight.shape[0]
    per = per_device(rows // PAIR * (width // HD), n_ctx)
    piece = (per, PAIR, HD)
    return pl.pallas_call(
        functools.partial(heads_back_kernel, n_ctx),
        out_shape=[jax.ShapeDtypeStruct(piece, BF)] * n_ctx,
        grid_spec=pltpu.PrefetchScalarGridSpec(
            num_scalar_prefetch=1,
            grid=(1,),
            in_specs=[whole(da.shape), whole(weight.shape), whole(valid.shape)],
            out_specs=[whole(piece)] * n_ctx,
            scratch_shapes=[pltpu.VMEM((per * n_ctx, PAIR, HD), BF)],
        ),
        compiler_params=params(),
        cost_estimate=pl.CostEstimate(
            flops=2 * rows * depth * width, bytes_accessed=rows * depth * 2 + 2 * depth * width, transcendentals=0
        ),
    )(scalars, da, weight, valid)


def in_kernel(n_ctx, pairs, scalar_ref, *refs):
    piece_refs, weight_refs, valid_ref = refs[:n_ctx], refs[n_ctx : n_ctx + 3], refs[n_ctx + 3]
    grad_refs, partial_refs, buffer = refs[n_ctx + 4 : n_ctx + 7], refs[n_ctx + 7 : -1], refs[-1]
    me = scalar_ref[0]
    first, second = halves_at(scalar_ref[1])
    per = piece_refs[0].shape[0]
    heads = weight_refs[0].shape[1] // HD
    for k in range(n_ctx):
        source = jnp.bitwise_xor(me, k)
        for p in range(per):
            buffer[source * per + p] = piece_refs[k][p]
    for sequence in range(pairs // heads):
        at = slice(sequence * PAIR, (sequence + 1) * PAIR)
        total = None
        for which in range(3):
            rows = jnp.concatenate(
                [
                    jnp.concatenate([buffer[pair, which, first, :], buffer[pair, which, second, :]], axis=0)
                    for pair in range(sequence * heads, (sequence + 1) * heads)
                ],
                axis=1,
            )
            if which == 2:
                rows = rows * valid_ref[at, :]
            grad_refs[which][at, :] = rows
            product = times_transposed(rows, weight_refs[which][...])
            total = product if total is None else total + product
        put_partial(partial_refs, sequence * PAIR, total.astype(BF), pairs // heads * PAIR // 4)


def project_in(scalars, pieces, weights, valid, pairs, n_ctx, split):
    depth, width = weights[0].shape
    rows = valid.shape[0]
    per = pieces[0].shape[0]
    shapes = [jax.ShapeDtypeStruct((rows, width), BF)] * 3 + partial_shapes(rows, depth, split)
    return pl.pallas_call(
        functools.partial(in_kernel, n_ctx, pairs),
        out_shape=shapes,
        grid_spec=pltpu.PrefetchScalarGridSpec(
            num_scalar_prefetch=1,
            grid=(1,),
            in_specs=[whole(piece.shape) for piece in pieces]
            + [whole(weight.shape) for weight in weights]
            + [whole(valid.shape)],
            out_specs=[whole(shape.shape) for shape in shapes],
            scratch_shapes=[pltpu.VMEM((per * n_ctx, 3, PAIR, HD), BF)],
        ),
        compiler_params=params(),
        cost_estimate=pl.CostEstimate(
            flops=6 * rows * depth * width, bytes_accessed=rows * depth * 2 + 6 * depth * width, transcendentals=0
        ),
    )(scalars, *pieces, *weights, valid)


def both_places(me, k, n_ctx):
    source = jnp.bitwise_xor(me, k)
    front = pl.multiple_of(source * BLOCK, BLOCK)
    back = pl.multiple_of((2 * n_ctx - 1 - source) * BLOCK, BLOCK)
    return pl.ds(front, BLOCK), pl.ds(back, BLOCK)


def attention_kernel(n_ctx, tile, scalar_ref, *refs):
    x_refs, o_refs, (qs, ks, vs, os) = refs[:n_ctx], refs[n_ctx : 2 * n_ctx], refs[2 * n_ctx :]
    me = scalar_ref[0]
    length = 2 * n_ctx * BLOCK
    for k in range(n_ctx):
        front, back = both_places(me, k, n_ctx)
        for which, dest in enumerate((qs, ks, vs)):
            dest[front, :] = x_refs[k][0, which, :BLOCK, :]
            dest[back, :] = x_refs[k][0, which, BLOCK:, :]
    factor = -(HD ** (-0.5)) * LOG2E
    shift = math.log(length) * LOG2E
    row_at = lax.broadcasted_iota(jnp.int32, (tile, tile), 0)
    col_at = lax.broadcasted_iota(jnp.int32, (tile, tile), 1)
    for i in range(length // tile):
        query = qs[i * tile : (i + 1) * tile, :]

        def part(j, masked):
            at = pl.ds(pl.multiple_of(j * tile, tile), tile)
            raw = times_transposed(query, ks[at, :])
            prob = 1.0 / (1.0 + jnp.exp2(raw * factor + shift))
            if masked:
                prob = jnp.where(row_at >= col_at, prob, 0.0)
            return dot(prob.astype(BF), vs[at, :])

        total = part(i, True)
        if i > 0:
            total = lax.fori_loop(0, i, lambda j, acc: acc + part(j, False), total)
        os[i * tile : (i + 1) * tile, :] = total.astype(BF)
    for k in range(n_ctx):
        front, back = both_places(me, k, n_ctx)
        o_refs[k][0, :BLOCK, :] = os[front, :]
        o_refs[k][0, BLOCK:, :] = os[back, :]


def attention_forward(scalars, pieces, n_ctx):
    pairs = pieces[0].shape[0]
    length = 2 * n_ctx * BLOCK
    tile = min(512, length)
    return pl.pallas_call(
        functools.partial(attention_kernel, n_ctx, tile),
        out_shape=[jax.ShapeDtypeStruct((pairs, PAIR, HD), BF)] * n_ctx,
        grid_spec=pltpu.PrefetchScalarGridSpec(
            num_scalar_prefetch=1,
            grid=(pairs,),
            in_specs=[pl.BlockSpec((1, 3, PAIR, HD), lambda i, s: (i, 0, 0, 0))] * n_ctx,
            out_specs=[pl.BlockSpec((1, PAIR, HD), lambda i, s: (i, 0, 0))] * n_ctx,
            scratch_shapes=[pltpu.VMEM((length, HD), BF)] * 4,
        ),
        compiler_params=params(),
        cost_estimate=pl.CostEstimate(
            flops=pairs * length * length * HD * 6,
            bytes_accessed=pairs * length * HD * 8,
            transcendentals=pairs * length * length,
        ),
    )(scalars, *pieces)


def attention_back_kernel(n_ctx, tile, scalar_ref, *refs):
    x_refs, g_refs, (cos_ref, sin_ref) = refs[:n_ctx], refs[n_ctx : 2 * n_ctx], refs[2 * n_ctx : 2 * n_ctx + 2]
    out_refs = refs[2 * n_ctx + 2 : 3 * n_ctx + 2]
    qs, ks, vs, gs, os, dqs = refs[3 * n_ctx + 2 :]
    me = scalar_ref[0]
    length = 2 * n_ctx * BLOCK
    for k in range(n_ctx):
        front, back = both_places(me, k, n_ctx)
        for which, dest in enumerate((qs, ks, vs)):
            dest[front, :] = x_refs[k][0, which, :BLOCK, :]
            dest[back, :] = x_refs[k][0, which, BLOCK:, :]
        gs[front, :] = g_refs[k][0, :BLOCK, :]
        gs[back, :] = g_refs[k][0, BLOCK:, :]
    scale = HD ** (-0.5)
    factor = -scale * LOG2E
    shift = math.log(length) * LOG2E
    count = length // tile
    key_at = lax.broadcasted_iota(jnp.int32, (tile, tile), 0)
    query_at = lax.broadcasted_iota(jnp.int32, (tile, tile), 1)
    dqs[...] = jnp.zeros_like(dqs)

    def unrotate(values, at):
        return (values * cos_ref[at, :] - pltpu.roll(values, HD // 2, 1) * sin_ref[at, :]).astype(BF)

    for j in range(count):
        own = slice(j * tile, (j + 1) * tile)
        keys = ks[own, :]
        values = vs[own, :]

        def part(i, masked):
            at = pl.ds(pl.multiple_of(i * tile, tile), tile)
            query = qs[at, :]
            grad = gs[at, :]
            raw = times_transposed(keys, query)
            prob = 1.0 / (1.0 + jnp.exp2(raw * factor + shift))
            if masked:
                prob = jnp.where(query_at >= key_at, prob, 0.0)
            prob_grad = times_transposed(values, grad)
            score_grad = (prob_grad * prob * (1.0 - prob)).astype(BF)
            dqs[at, :] += contract_rows(score_grad, keys)
            return dot(score_grad, query), dot(prob.astype(BF), grad)

        total = part(j, True)
        if j + 1 < count:

            def step(i, acc):
                more = part(i, False)
                return acc[0] + more[0], acc[1] + more[1]

            total = lax.fori_loop(j + 1, count, step, total)
        os[1, own, :] = unrotate(total[0] * scale, own)
        os[2, own, :] = total[1].astype(BF)
    for i in range(count):
        at = slice(i * tile, (i + 1) * tile)
        os[0, at, :] = unrotate(dqs[at, :] * scale, at)
    for k in range(n_ctx):
        front, back = both_places(me, k, n_ctx)
        for which in range(3):
            out_refs[k][0, which, :BLOCK, :] = os[which, front, :]
            out_refs[k][0, which, BLOCK:, :] = os[which, back, :]


def attention_backward(scalars, pieces, grads, cos_tab, sin_tab, n_ctx):
    pairs = pieces[0].shape[0]
    length = 2 * n_ctx * BLOCK
    tile = min(512, length)
    three = pl.BlockSpec((1, 3, PAIR, HD), lambda i, s: (i, 0, 0, 0))
    one = pl.BlockSpec((1, PAIR, HD), lambda i, s: (i, 0, 0))
    return pl.pallas_call(
        functools.partial(attention_back_kernel, n_ctx, tile),
        out_shape=[jax.ShapeDtypeStruct((pairs, 3, PAIR, HD), BF)] * n_ctx,
        grid_spec=pltpu.PrefetchScalarGridSpec(
            num_scalar_prefetch=1,
            grid=(pairs,),
            in_specs=[three] * n_ctx + [one] * n_ctx + [whole((length, HD))] * 2,
            out_specs=[three] * n_ctx,
            scratch_shapes=[pltpu.VMEM((length, HD), BF)] * 4
            + [pltpu.VMEM((3, length, HD), BF), pltpu.VMEM((length, HD), F32)],
        ),
        compiler_params=params(),
        cost_estimate=pl.CostEstimate(
            flops=pairs * length * length * HD * 12,
            bytes_accessed=pairs * length * HD * 14,
            transcendentals=pairs * length * length,
        ),
    )(scalars, *pieces, *grads, cos_tab, sin_tab)


def mlp_kernel(n_ref, g_ref, wg_ref, wu_ref, wd_ref, *rest):
    h_ref, dgp_ref, dup_ref = rest[-3:]
    rows = n_ref[...]
    gate_pre = dot(rows, wg_ref[...])
    up_pre = dot(rows, wu_ref[...])
    hidden_grad = times_transposed(g_ref[...], wd_ref[...])
    h_ref[...], dgp_ref[...], dup_ref[...] = feed_values(gate_pre, up_pre, hidden_grad)


def mlp_core(normed, grads, wg, wu, wd, total, first, held=()):
    rows, depth = normed.shape
    hidden = wg.shape[1]
    row_tile, tile = 512, 512
    skip = first // row_tile
    row_block = pl.BlockSpec((row_tile, depth), lambda j, i: (i, 0))
    out_block = pl.BlockSpec((row_tile, tile), lambda j, i: (i + skip, j))
    out = jax.ShapeDtypeStruct((total, hidden), BF)
    return pl.pallas_call(
        mlp_kernel,
        out_shape=(out, out, out),
        grid=(hidden // tile, rows // row_tile),
        in_specs=[
            row_block,
            row_block,
            pl.BlockSpec((depth, tile), lambda j, i: (0, j)),
            pl.BlockSpec((depth, tile), lambda j, i: (0, j)),
            pl.BlockSpec((tile, depth), lambda j, i: (j, 0)),
        ]
        + [pl.BlockSpec(memory_space=pl.ANY)] * len(held),
        out_specs=(out_block, out_block, out_block),
        input_output_aliases={5 + k: k for k in range(len(held))},
        compiler_params=params(),
        cost_estimate=pl.CostEstimate(
            flops=6 * rows * depth * hidden,
            bytes_accessed=rows * depth * 4 + 6 * depth * hidden + 6 * rows * hidden,
            transcendentals=rows * hidden,
        ),
    )(normed, grads, wg, wu, wd, *held)


def inverse_rms(values):
    return lax.rsqrt(jnp.mean(values * values, axis=-1, keepdims=True) + EPS)


def neighbours():
    index, rank = lax.axis_index("ctx"), lax.axis_index("tp")
    return (index, jnp.bitwise_xor(rank, 1)), (index, jnp.bitwise_xor(rank, 2))


def remote(source, dest, send_sem, recv_sem, device):
    return pltpu.make_async_remote_copy(
        src_ref=source,
        dst_ref=dest,
        send_sem=send_sem,
        recv_sem=recv_sem,
        device_id=device,
        device_id_type=pl.DeviceIdType.MESH,
    )


def signal(sem, device):
    pl.semaphore_signal(sem, inc=1, device_id=device, device_id_type=pl.DeviceIdType.MESH)


class Scatter:
    def __init__(self, partial, groups, bufs, sems, loaded=True):
        self.partial, self.groups, self.loaded = partial, groups, loaded
        self.from_x, self.from_y, self.for_y, self.for_x, self.low, self.high = bufs[:6]
        if loaded:
            self.stay, self.stay_y, self.stay_x = bufs[6:]
        self.first_send, self.first_recv, self.second_send, self.second_recv, self.load_sem = sems
        self.to_x, self.to_y = neighbours()

    @staticmethod
    def scratch(rows, width, loaded=True):
        dma = pltpu.SemaphoreType.DMA
        whole_rows, half_rows = pltpu.VMEM((rows, width), BF), pltpu.VMEM((rows // 2, width), BF)
        bufs = [whole_rows] * 2 + [half_rows] * 4 + ([whole_rows] + [half_rows] * 2 if loaded else [])
        return bufs + [dma((8,)), dma((8,)), dma((4,)), dma((4,)), dma((6,))]

    def piece(self, g, number):
        base, rows, own = self.groups[g]
        half = rows // 2
        if not self.loaded:
            return self.partial[pl.ds(base + number * half, half), :]
        if number < 2:
            return self.stay[pl.ds(own + number * half, half), :]
        return (self.stay_x if number == 3 else self.stay_y)[pl.ds(own // 2, half), :]

    def first_copies(self, g):
        base, rows, own = self.groups[g]
        half = rows // 2
        part = lambda number: self.partial.at[pl.ds(base + number * half, half)]
        at = lambda buf, number: buf.at[pl.ds(own + number * half, half)]
        plan = [
            (part(2), at(self.from_x, 0), self.to_x),
            (part(6), at(self.from_x, 1), self.to_x),
            (part(5), at(self.from_y, 0), self.to_y),
            (part(7), at(self.from_y, 1), self.to_y),
        ]
        return [
            remote(source, dest, self.first_send.at[4 * g + k], self.first_recv.at[4 * g + k], device)
            for k, (source, dest, device) in enumerate(plan)
        ]

    def loads(self, g):
        base, rows, own = self.groups[g]
        half = rows // 2
        copy = lambda number, count, dest, k: pltpu.make_async_copy(
            self.partial.at[pl.ds(base + number * half, count)], dest, self.load_sem.at[3 * g + k]
        )
        return [
            copy(0, rows, self.stay.at[pl.ds(own, rows)], 0),
            copy(4, half, self.stay_y.at[pl.ds(own // 2, half)], 1),
            copy(3, half, self.stay_x.at[pl.ds(own // 2, half)], 2),
        ]

    def second_copies(self, g):
        _, rows, own = self.groups[g]
        at = pl.ds(own // 2, rows // 2)
        return [
            remote(self.for_y.at[at], self.low.at[at], self.second_send.at[2 * g], self.second_recv.at[2 * g], self.to_y),
            remote(
                self.for_x.at[at], self.high.at[at], self.second_send.at[2 * g + 1], self.second_recv.at[2 * g + 1], self.to_x
            ),
        ]

    def start(self, g, which=(1, 3, 0, 2), loads=True):
        copies = self.first_copies(g)
        for k in which:
            copies[k].start()
        if loads:
            for copy in self.loads(g):
                copy.start()

    def forward(self, g):
        _, rows, own = self.groups[g]
        half = rows // 2
        copies = self.first_copies(g)
        copies[1].wait_recv()
        copies[3].wait_recv()
        if self.loaded:
            for copy in self.loads(g):
                copy.wait()
        at = pl.ds(own // 2, half)
        self.for_y[at, :] = add_low(self.piece(g, 4), self.from_x[pl.ds(own + half, half), :])
        self.for_x[at, :] = add_low(self.piece(g, 3), self.from_y[pl.ds(own + half, half), :])
        for copy in self.second_copies(g):
            copy.start()

    def total(self, g, use):
        _, rows, own = self.groups[g]
        half = rows // 2
        copies, seconds = self.first_copies(g), self.second_copies(g)
        copies[0].wait_recv()
        copies[2].wait_recv()
        for copy in copies:
            copy.wait_send()
        for copy in seconds:
            copy.wait()
        first = pl.ds(own, half)
        rest = pl.ds(own // 2, half)
        for side, (got, more) in enumerate(((self.from_x, self.low), (self.from_y, self.high))):
            at = pl.ds(own + side * half, half)
            use(at, self.piece(g, side).astype(F32) + got[first, :].astype(F32) + more[rest, :].astype(F32))


class Gather:
    def __init__(self, own, out, groups, sems, local=True, via=None):
        self.own, self.out, self.groups, self.has_local, self.via = own, out, groups, local, via
        self.first_send, self.first_recv, self.second_send, self.second_recv, self.local_sem, self.via_sem = sems
        self.to_x, self.to_y = neighbours()

    @staticmethod
    def scratch():
        dma = pltpu.SemaphoreType.DMA
        return [dma((4,)), dma((4,)), dma((4,)), dma((4,)), dma((2,)), dma((4,))]

    def first_copies(self, g):
        base, rows, own = self.groups[g]
        source = self.own.at[pl.ds(own, rows)]
        place = lambda k: self.out.at[pl.ds(base + k * rows, rows)]
        return [
            remote(source, place(1), self.first_send.at[2 * g], self.first_recv.at[2 * g], self.to_x),
            remote(source, place(2), self.first_send.at[2 * g + 1], self.first_recv.at[2 * g + 1], self.to_y),
        ]

    def local(self, g):
        base, rows, own = self.groups[g]
        return pltpu.make_async_copy(self.own.at[pl.ds(own, rows)], self.out.at[pl.ds(base, rows)], self.local_sem.at[g])

    def second_copies(self, g):
        base, rows, own = self.groups[g]
        half = rows // 2
        part = lambda number: self.out.at[pl.ds(base + number * half, half)]
        if self.via is None:
            low, high = part(4), part(3)
        else:
            low, high = (self.via.at[pl.ds(own + k * half, half)] for k in range(2))
        return [
            remote(low, part(6), self.second_send.at[2 * g], self.second_recv.at[2 * g], self.to_x),
            remote(high, part(7), self.second_send.at[2 * g + 1], self.second_recv.at[2 * g + 1], self.to_y),
        ]

    def pass_on(self, g, which):
        if self.via is not None:
            base, rows, own = self.groups[g]
            half = rows // 2
            load = pltpu.make_async_copy(
                self.out.at[pl.ds(base + (4 - which) * half, half)],
                self.via.at[pl.ds(own + which * half, half)],
                self.via_sem.at[2 * g + which],
            )
            load.start()
            load.wait()
        self.second_copies(g)[which].start()

    def start(self, g):
        for copy in self.first_copies(g):
            copy.start()
        if self.has_local:
            self.local(g).start()

    def forward_x(self, g):
        self.first_copies(g)[0].wait_recv()
        self.pass_on(g, 1)

    def forward_y(self, g):
        self.first_copies(g)[1].wait_recv()
        self.pass_on(g, 0)

    def forward(self, g):
        self.forward_x(g)
        self.forward_y(g)
        if self.has_local:
            self.local(g).wait()

    def finish(self, g):
        for copy in self.second_copies(g):
            copy.wait_recv()

    def sent(self, g):
        for copy in self.first_copies(g) + self.second_copies(g):
            copy.wait_send()


TILE, ROWS = 128, 64
CORE_SLOTS, HOP_SLOTS = 4, 4


class Ring:
    def __init__(self, slots, send_sem, recv_sem, credit, total):
        self.slots, self.send_sem, self.recv_sem, self.credit, self.total = slots, send_sem, recv_sem, credit, total
        self.count = slots.shape[0]

    def copy(self, source, at, send_at, device):
        slot = lax.rem(at, self.count)
        return pltpu.make_async_remote_copy(
            src_ref=source,
            dst_ref=self.slots.at[slot],
            send_sem=self.send_sem.at[send_at],
            recv_sem=self.recv_sem.at[slot],
            device_id=device,
            device_id_type=pl.DeviceIdType.MESH,
        )

    def send(self, source, at, send_at, device):
        @pl.when(at >= self.count)
        def _():
            pl.semaphore_wait(self.credit, 1)

        self.copy(source, at, send_at, device).start()

    def sent(self, source, at, send_at, device):
        self.copy(source, at, send_at, device).wait_send()

    def arrived(self, source, at, send_at, device):
        self.copy(source, at, send_at, device).wait_recv()
        return self.slots.at[lax.rem(at, self.count)]

    def free(self, at, device):
        @pl.when(at + self.count < self.total)
        def _():
            pl.semaphore_signal(self.credit, inc=1, device_id=device, device_id_type=pl.DeviceIdType.MESH)


def lags(mid, spare):
    more = 1 if spare else 0
    lag_t = mid + 2 * more
    lag_o = lag_t + 2 + 2 * (mid - 1)
    lag_f = lag_o + 1 + more
    return 1 + more, lag_t, lag_t + 2, lag_o, lag_f, lag_f + 1


def sums_kernel(n_ctx, items, n_right, n_extra, tasks, late, *refs):
    n_left = len(items)
    made = items[0][3]
    n_held = n_left - (1 if made else 0)
    left_refs, right_refs = refs[:n_held], refs[n_held : n_held + n_right]
    left_refs = ((None,) if made else ()) + tuple(left_refs)
    refs = refs[n_held + n_right :]
    extra_in, refs = refs[: n_extra[0]], refs[n_extra[0] :]
    out_refs, extra_out, refs = refs[:n_left], refs[n_left : n_left + n_extra[1]], refs[n_left + n_extra[1] :]
    extra_scratch, refs = refs[: n_extra[2]], refs[n_extra[2] :]
    right_refs = list(right_refs) + [extra_out[k] for k in late]
    n_right += len(late)
    (
        left_buf, right_buf, other_buf, ring, core_in, hop_in, hop_mid, hop_out, core_out,
        left_sem, right_sem, core_send, core_recv, in_send, in_recv, mid_send, mid_recv, out_send, out_recv,
        fin_send, fin_recv, store_sem, core_credit, in_credit, mid_credit, out_credit, fin_credit,
    ) = refs
    starts = [0]
    for _, _, chunks, _ in items:
        starts.append(starts[-1] + chunks)
    total = starts[-1]
    n_ring = ring.shape[0]
    chips = n_ctx // 2
    mid = chips // 2
    index = lax.axis_index("ctx")
    rank = lax.axis_index("tp")
    core = lax.rem(index, 2)
    chip = index // 2
    low_side = chip < mid
    place = jnp.where(low_side, chip, chips - 1 - chip)
    toward = jnp.where(low_side, 1, -1)
    partner = (chip * 2 + 1 - core, rank)
    after = ((chip + toward) * 2 + core, rank)
    before = ((chip - toward) * 2 + core, rank)
    is_first = place == 0
    is_last = place == mid - 1
    lag_a, lag_t, lag_u, lag_o, lag_f, lag_w = lags(mid, made)

    to_core = Ring(core_in, core_send, core_recv, core_credit, total)
    to_after = Ring(hop_in, in_send, in_recv, in_credit, total)
    across = Ring(hop_mid, mid_send, mid_recv, mid_credit, total)
    to_before = Ring(hop_out, out_send, out_recv, out_credit, total)
    to_final = Ring(core_out, fin_send, fin_recv, fin_credit, total)

    def right_copy(k):
        return pltpu.make_async_copy(right_refs[k], right_buf.at[k % 2], right_sem.at[k % 2])

    right_copy(0).start()

    def for_item(at, action):
        for number in range(n_left):
            @pl.when((at >= starts[number]) & (at < starts[number + 1]))
            def _(number=number):
                action(number, at - starts[number])

    def rows_at(number, chunk, side):
        half = items[number][2] * ROWS
        return pl.multiple_of(side * half + chunk * ROWS, ROWS)

    def left_copy(number, chunk, slot, which):
        side = core if which == 0 else 1 - core
        half = items[number][2] * ROWS
        return pltpu.make_async_copy(
            left_refs[number].at[:, pl.ds(pl.multiple_of(side * half + chunk // 2 * TILE, TILE), TILE)],
            left_buf.at[slot, :, pl.ds(which * TILE, TILE)],
            left_sem.at[slot, which],
        )

    def load_left(at):
        def action(number, chunk):
            if number == 0 and made:
                maker.load(chunk // 2)
                return
            if number == 1 and made:

                @pl.when(chunk == 0)
                def _():
                    maker.release()

            for which in range(2):
                left_copy(number, chunk, lax.rem(at // 2, 2), which).start()

        for_item(at, action)

    planned, each, maker = tasks(extra_in, extra_out, extra_scratch) if tasks is not None else ({}, None, None)
    if made:
        maker.begin(left_buf, right_buf)
    load_left(0)
    if n_right > 1 and not made:
        right_copy(1).start()
    if tasks is not None:
        greet(n_ctx, True)
    else:
        barrier = pltpu.get_barrier_semaphore()
        pl.semaphore_signal(barrier, inc=1, device_id=partner, device_id_type=pl.DeviceIdType.MESH)

        @pl.when(chip > 0)
        def _():
            pl.semaphore_signal(
                barrier, inc=1, device_id=((chip - 1) * 2 + core, rank), device_id_type=pl.DeviceIdType.MESH
            )

        @pl.when(chip < chips - 1)
        def _():
            pl.semaphore_signal(
                barrier, inc=1, device_id=((chip + 1) * 2 + core, rank), device_id_type=pl.DeviceIdType.MESH
            )

        pl.semaphore_wait(barrier, 1 + jnp.where(chip > 0, 1, 0) + jnp.where(chip < chips - 1, 1, 0))
    if 0 in planned:
        planned.pop(0)()
    right_copy(0).wait()

    def step(i, carry):
        def at_lag(lag):
            at = i - lag
            return at, (at >= 0) & (at < total)

        at, now = at_lag(lag_w)

        @pl.when(now)
        def _():
            slot = lax.rem(at, n_ring)
            source = ring.at[slot]

            def action(number, chunk):
                store(number, chunk, at, 0).wait()
                store(number, chunk, at, 1).wait()

            for_item(at, action)
            to_final.sent(source, at, slot, partner)
            to_final.free(at, partner)

            @pl.when(jnp.logical_not(is_first))
            def _():
                to_before.sent(source, at, slot, before)

        at, now = at_lag(lag_o)

        @pl.when(now & jnp.logical_not(is_last))
        def _():
            slot = lax.rem(at, n_ring)
            source = ring.at[slot]
            to_after.sent(source, at, slot, after)
            got = to_before.arrived(source, at, slot, after)
            ring[slot] = got[...]
            to_before.free(at, after)

            @pl.when(jnp.logical_not(is_first))
            def _():
                to_before.send(source, at, slot, before)

        @pl.when(now)
        def _():
            slot = lax.rem(at, n_ring)
            to_final.send(ring.at[slot], at, slot, partner)

        at, now = at_lag(lag_u)

        @pl.when(now & is_last)
        def _():
            slot = lax.rem(at, n_ring)
            source = ring.at[slot]
            across.sent(source, at, slot, after)
            got = across.arrived(source, at, slot, after)
            ring[slot] = add_low(ring[slot], got[...])
            across.free(at, after)

            @pl.when(jnp.logical_not(is_first))
            def _():
                to_before.send(source, at, slot, before)

        at, now = at_lag(lag_t)

        @pl.when(now)
        def _():
            slot = lax.rem(at, n_ring)
            source = ring.at[slot]

            @pl.when(jnp.logical_not(is_first))
            def _():
                got = to_after.arrived(source, at, slot, before)
                ring[slot] = add_low(ring[slot], got[...])
                to_after.free(at, before)

            @pl.when(is_last)
            def _():
                across.send(source, at, slot, after)

            @pl.when(jnp.logical_not(is_first) & jnp.logical_not(is_last))
            def _():
                to_after.send(source, at, slot, after)

        at, now = at_lag(lag_a)

        @pl.when(now)
        def _():
            slot = lax.rem(at, n_ring)
            source = ring.at[slot]
            own = other_buf.at[lax.rem(at, 4)]
            to_core.sent(own, at, lax.rem(at, 4), partner)
            got = to_core.arrived(own, at, lax.rem(at, 4), partner)
            ring[slot] = add_low(ring[slot], got[...])
            to_core.free(at, partner)

            @pl.when(is_first & jnp.logical_not(is_last))
            def _():
                to_after.send(source, at, slot, after)

        at, now = at_lag(lag_f)

        @pl.when(now)
        def _():
            slot = lax.rem(at, n_ring)
            to_final.arrived(ring.at[slot], at, slot, partner)

            def action(number, chunk):
                store(number, chunk, at, 0).start()
                store(number, chunk, at, 1).start()

            for_item(at, action)

        for when, task in planned.items():
            pl.when(i == when)(task)

        if each is not None:
            each(i)

        @pl.when((i + 2 < total) & (lax.rem(i, 2) == 0))
        def _():
            load_left(i + 2)

        @pl.when((i < total) & (lax.rem(i, 2) == 0))
        def _():
            slot = lax.rem(i // 2, 2)

            def action(number, chunk):
                which_right = items[number][1]
                if which_right > 0 and items[number - 1][1] != which_right:

                    @pl.when(chunk == 0)
                    def _():
                        if made and which_right in (1, n_right - 1):
                            right_copy(which_right).start()
                        right_copy(which_right).wait()

                if which_right > 0 and which_right + 1 < n_right - (1 if made else 0):

                    @pl.when(chunk == items[number][2] // 2)
                    def _():
                        right_copy(which_right + 1).start()

                if number == 0 and made:
                    maker.make(chunk // 2)
                else:
                    for which in range(2):
                        left_copy(number, chunk, slot, which).wait()
                right = right_buf.at[which_right % 2]
                product = contract_rows(left_buf[slot], right[...]).astype(BF)
                for part in range(2):
                    place = lax.rem(i + part, 4)
                    other_buf[place] = product[TILE + part * ROWS : TILE + (part + 1) * ROWS]
                    to_core.send(other_buf.at[place], i + part, place, partner)
                    ring[lax.rem(i + part, n_ring)] = product[part * ROWS : (part + 1) * ROWS]

            for_item(i, action)

        return carry

    def store(number, chunk, at, which):
        source = ring.at[lax.rem(at, n_ring)] if which == 0 else core_out.at[lax.rem(at, CORE_SLOTS)]
        side = core if which == 0 else 1 - core
        return pltpu.make_async_copy(
            source,
            out_refs[number].at[pl.ds(rows_at(number, chunk, side), ROWS), :],
            store_sem.at[which, lax.rem(at, 2)],
        )

    lax.fori_loop(0, total + lag_w, step, 0)


def weight_sums(items, rights, n_ctx, collective_id, extra=None, late=(), limit=VMEM_LIMIT):
    tokens, width = rights[0].shape
    columns = [left if isinstance(left, int) else left.shape[1] for left, _ in items]
    held = [left for left, _ in items if not isinstance(left, int)]
    shapes = [
        (k, right, columns[k] // 2 // ROWS, isinstance(left, int)) for k, (left, right) in enumerate(items)
    ]
    mid = n_ctx // 4
    n_ring = lags(mid, shapes[0][3])[-1] + 2
    any_spec = pl.BlockSpec(memory_space=pl.ANY)
    args, arg_specs, outs, out_specs, scratch, tasks = extra if extra is not None else ([], [], [], [], [], None)
    counts = (len(args), len(outs), len(scratch))
    chunk = (ROWS, width)
    dma = pltpu.SemaphoreType.DMA
    return pl.pallas_call(
        functools.partial(sums_kernel, n_ctx, shapes, len(rights), counts, tasks, late),
        out_shape=[jax.ShapeDtypeStruct((count, width), BF) for count in columns] + outs,
        in_specs=[any_spec] * (len(held) + len(rights)) + arg_specs,
        out_specs=[any_spec] * len(items) + out_specs,
        scratch_shapes=scratch
        + [
            pltpu.VMEM((2, tokens, 2 * TILE), BF),
            pltpu.VMEM((min(2, len(rights) + len(late)), tokens, width), BF),
            pltpu.VMEM((4,) + chunk, BF),
            pltpu.VMEM((n_ring,) + chunk, BF),
            pltpu.VMEM((CORE_SLOTS,) + chunk, BF),
            pltpu.VMEM((HOP_SLOTS,) + chunk, BF),
            pltpu.VMEM((HOP_SLOTS,) + chunk, BF),
            pltpu.VMEM((HOP_SLOTS,) + chunk, BF),
            pltpu.VMEM((CORE_SLOTS,) + chunk, BF),
            dma((2, 2)),
            dma((2,)),
            dma((4,)),
            dma((CORE_SLOTS,)),
            dma((n_ring,)),
            dma((HOP_SLOTS,)),
            dma((n_ring,)),
            dma((HOP_SLOTS,)),
            dma((n_ring,)),
            dma((HOP_SLOTS,)),
            dma((n_ring,)),
            dma((CORE_SLOTS,)),
            dma((2, 2)),
        ]
        + [pltpu.SemaphoreType.REGULAR] * 5,
        compiler_params=pltpu.CompilerParams(
            vmem_limit_bytes=limit, collective_id=collective_id, has_side_effects=True
        ),
        cost_estimate=pl.CostEstimate(
            flops=sum(2 * count * tokens * width for count in columns),
            bytes_accessed=sum(2 * count * (tokens + width) for count in columns),
            transcendentals=0,
        ),
    )(*held, *rights, *args)


VMEM_SPEC = pl.BlockSpec(memory_space=pltpu.VMEM)
ANY_SPEC = pl.BlockSpec(memory_space=pl.ANY)


def norm_back_rows(values, gain, grad):
    inv = inverse_rms(values)
    unit = values * inv
    scaled = grad * gain
    back = (scaled - unit * jnp.mean(scaled * unit, axis=-1, keepdims=True)) * inv
    return back, jnp.sum(grad * unit, axis=0, keepdims=True)


def own_copies(ref, buf, groups, sem):
    odd = lax.rem(lax.axis_index("tp"), 2)
    starts = [pl.multiple_of(odd * BLOCK, BLOCK), pl.multiple_of((1 - odd) * PAIR, BLOCK)]
    return [
        pltpu.make_async_copy(ref.at[pl.ds(start, rows)], buf.at[pl.ds(own, rows)], sem.at[g])
        for g, (start, (_, rows, own)) in enumerate(zip(starts, groups))
    ]


class Maker:
    def __init__(self, refs, outs, weights, downs, stage, sems):
        self.n2_ref, self.wg_ref, self.wu_ref, self.wd_ref = refs
        self.h_out, self.dgp_out, self.dup_out = outs
        self.weights, self.downs, self.stage = weights, downs, stage
        self.n2_sem, self.weight_sem, self.h_sem, self.grad_sem = sems
        self.core = lax.rem(lax.axis_index("ctx"), 2)
        self.half = self.h_out.shape[1] // 2
        self.tiles = self.half // TILE

    def first(self, tile, which):
        side = self.core if which == 0 else 1 - self.core
        return pl.multiple_of(side * self.half + tile * TILE, TILE)

    def copies(self, tile):
        slot = lax.rem(tile, 2)
        deep = self.weights.shape[1]
        made = []
        for which in range(2):
            at = pl.ds(self.first(tile, which), TILE)
            for kind, ref in enumerate((self.wg_ref, self.wu_ref)):
                to = pl.multiple_of((slot * 2 + kind) * 2 * TILE + which * TILE, TILE)
                for part in range(2):
                    made.append((ref.at[pl.ds(part * deep, deep), at], self.weights.at[part, :, pl.ds(to, TILE)]))
            made.append((self.wd_ref.at[at], self.downs.at[slot, 0, pl.ds(which * TILE, TILE)]))
        return [
            pltpu.make_async_copy(source, dest, self.weight_sem.at[slot, k]) for k, (source, dest) in enumerate(made)
        ]

    def load(self, tile):
        for copy in self.copies(tile):
            copy.start()

    def begin(self, left_buf, right_buf):
        self.left_buf, self.right_buf = left_buf, right_buf
        self.n2_copy().start()

    def n2_copy(self):
        return pltpu.make_async_copy(self.n2_ref, self.right_buf.at[1], self.n2_sem)

    def h_stores(self, tile):
        slot = lax.rem(tile, 2)
        return [
            pltpu.make_async_copy(
                self.left_buf.at[slot, :, pl.ds(which * TILE, TILE)],
                self.h_out.at[:, pl.ds(self.first(tile, which), TILE)],
                self.h_sem.at[slot, which],
            )
            for which in range(2)
        ]

    def grad_stores(self, tile):
        return [
            pltpu.make_async_copy(
                self.stage.at[kind, :, pl.ds(which * TILE, TILE)],
                out.at[:, pl.ds(self.first(tile, which), TILE)],
                self.grad_sem.at[kind, which],
            )
            for kind, out in enumerate((self.dgp_out, self.dup_out))
            for which in range(2)
        ]

    def make(self, tile):
        slot = lax.rem(tile, 2)
        deep = self.weights.shape[1]

        @pl.when(tile == 0)
        def _():
            self.n2_copy().wait()

        @pl.when(tile > 0)
        def _():
            for copy in self.grad_stores(tile - 1):
                copy.wait()

        @pl.when(tile > 1)
        def _():
            for copy in self.h_stores(tile - 2):
                copy.wait()

        for copy in self.copies(tile):
            copy.wait()
        at_gate = pl.ds(pl.multiple_of(slot * 4 * TILE, TILE), 2 * TILE)
        at_up = pl.ds(pl.multiple_of((slot * 4 + 2) * TILE, TILE), 2 * TILE)
        count = 512

        def rows_step(step, carry):
            rows = pl.ds(pl.multiple_of(step * count, count), count)
            low, high = self.right_buf[1, rows, :deep], self.right_buf[1, rows, deep:]
            gate_pre = dot(low, self.weights[0, :, at_gate]) + dot(high, self.weights[1, :, at_gate])
            up_pre = dot(low, self.weights[0, :, at_up]) + dot(high, self.weights[1, :, at_up])
            hidden_grad = times_transposed(self.right_buf[0, rows, :], self.downs[slot, 0])
            h, dgp, dup = feed_values(gate_pre, up_pre, hidden_grad)
            self.left_buf[slot, rows, :] = h
            self.stage[0, rows, :] = dgp
            self.stage[1, rows, :] = dup
            return carry

        lax.fori_loop(0, self.right_buf.shape[1] // count, rows_step, 0)
        for copy in self.h_stores(tile) + self.grad_stores(tile):
            copy.start()

    def release(self):
        for copy in self.h_stores(self.tiles - 2):
            copy.wait()

    def finish(self):
        for copy in self.h_stores(self.tiles - 1) + self.grad_stores(self.tiles - 1):
            copy.wait()


def feed_values(gate_pre, up_pre, hidden_grad):
    gate_sig = 1.0 / (1.0 + jnp.exp2(gate_pre * (-LOG2E)))
    gate_act = gate_pre * gate_sig
    return (
        (gate_act * up_pre).astype(BF),
        (hidden_grad * up_pre * (gate_sig * (1.0 + gate_pre * (1.0 - gate_sig)))).astype(BF),
        (hidden_grad * gate_act).astype(BF),
    )


def feed_tasks(groups, extra_in, extra_out, scratch):
    n2_ref, wg_ref, wu_ref, wd_ref, residual, cot_ref, gain = extra_in
    dr, da_all, gain_grad, d_ref, h_ref, dgp_ref, dup_ref = extra_out
    n = len(Scatter.scratch(16, 128))
    bufs, rest = scratch[:n], scratch[n:]
    weights, lefts, tile_out, weight_sem, left_sem, out_sem = rest[:6]
    grads, stage, own_sem, n2_sem, make_sem, h_sem, grad_sem = rest[6:13]
    da_own = bufs[0]
    scatter = Scatter(d_ref, groups, bufs[:9], bufs[9:])
    gather = Gather(da_own, da_all, groups, rest[13:], via=bufs[1])
    maker = Maker(
        (n2_ref, wg_ref, wu_ref, wd_ref),
        (h_ref, dgp_ref, dup_ref),
        weights,
        lefts,
        stage,
        (n2_sem, make_sem, h_sem, grad_sem),
    )
    order = list(reversed(range(len(groups))))
    rows, columns = lefts.shape[2], weights.shape[1]
    row_tiles = dgp_ref.shape[0] // rows
    tiles = row_tiles * (d_ref.shape[1] // columns)
    after = maker.half // ROWS
    shift = after + 1

    def weight_copies(part):
        at = pl.ds(pl.multiple_of(part * columns, columns), columns)
        return [
            pltpu.make_async_copy(ref.at[at], weights.at[k], weight_sem.at[k]) for k, ref in enumerate((wg_ref, wu_ref))
        ]

    def left_copies(tile):
        at = pl.ds(pl.multiple_of(lax.rem(tile, row_tiles) * rows, rows), rows)
        slot = lax.rem(tile, 2)
        return [
            pltpu.make_async_copy(ref.at[at], lefts.at[slot, k], left_sem.at[slot, k])
            for k, ref in enumerate((dgp_ref, dup_ref))
        ]

    def out_copy(tile):
        slot = lax.rem(tile, 2)
        return pltpu.make_async_copy(
            tile_out.at[slot],
            d_ref.at[
                pl.ds(pl.multiple_of(lax.rem(tile, row_tiles) * rows, rows), rows),
                pl.ds(pl.multiple_of(tile // row_tiles * columns, columns), columns),
            ],
            out_sem.at[slot],
        )

    def begin():
        gain_grad[...] = jnp.zeros_like(gain_grad)
        for copy in own_copies(cot_ref, grads, groups, own_sem):
            copy.start()

    def whole_hidden():
        maker.finish()
        for copy in weight_copies(0) + left_copies(0):
            copy.start()

    def each(step):
        i = step - shift

        @pl.when((i >= 0) & (i < tiles))
        def _():
            slot = lax.rem(i, 2)

            @pl.when(i + 1 < tiles)
            def _():
                for copy in left_copies(i + 1):
                    copy.start()

            @pl.when(lax.rem(i, row_tiles) == 0)
            def _():
                @pl.when(i > 0)
                def _():
                    for copy in weight_copies(i // row_tiles):
                        copy.start()

                for copy in weight_copies(i // row_tiles):
                    copy.wait()

            for copy in left_copies(i):
                copy.wait()
            total = times_transposed(lefts[slot, 0], weights[0]) + times_transposed(lefts[slot, 1], weights[1])

            @pl.when(i >= 2)
            def _():
                out_copy(i - 2).wait()

            tile_out[slot] = total.astype(BF)
            out_copy(i).start()

    def start():
        out_copy(tiles - 2).wait()
        out_copy(tiles - 1).wait()
        for copy in own_copies(cot_ref, grads, groups, own_sem):
            copy.wait()
        for g in order:
            scatter.start(g)

    def use(at, total):
        back, more = norm_back_rows(residual[at, :], gain[...].astype(F32), total)
        total_grad = grads[at, :].astype(F32) + back
        dr[at, :] = total_grad
        da_own[at, :] = total_grad.astype(BF)
        gain_grad[...] += more

    def spread(g):
        scatter.total(g, use)
        gather.start(g)

    def finish():
        for g in order:
            gather.finish(g)
            gather.sent(g)

    first = shift + tiles
    plan = {
        0: begin,
        after: whole_hidden,
        first: start,
        first + 3: lambda: scatter.forward(order[0]),
        first + 6: lambda: scatter.forward(order[-1]),
        first + 7: lambda: spread(order[0]),
        first + 9: lambda: spread(order[-1]),
        first + 11: lambda: gather.forward(order[0]),
        first + 15: lambda: gather.forward(order[-1]),
        first + 18: finish,
    }
    return plan, each, maker


def feed_extra(groups, n2, wg, wu, wd, residual, cot, gain):
    rows, width = residual.shape
    tokens, hidden = n2.shape[0], wg.shape[1]
    dma = pltpu.SemaphoreType.DMA
    outs = [
        jax.ShapeDtypeStruct((rows, width), F32),
        jax.ShapeDtypeStruct((tokens, width), BF),
        jax.ShapeDtypeStruct((1, width), F32),
        jax.ShapeDtypeStruct((tokens, width), BF),
    ] + [jax.ShapeDtypeStruct((tokens, hidden), BF)] * 3
    scratch = (
        Scatter.scratch(rows, width)
        + [
            pltpu.VMEM((2, width // 2, hidden), BF),
            pltpu.VMEM((2, 2, PAIR, hidden), BF),
            pltpu.VMEM((2, PAIR, width // 2), BF),
            dma((2,)),
            dma((2, 2)),
            dma((2,)),
            pltpu.VMEM((rows, width), BF),
            pltpu.VMEM((2, tokens, 2 * TILE), BF),
            dma((2,)),
            dma,
            dma((2, 10)),
            dma((2, 2)),
            dma((2, 2)),
        ]
        + Gather.scratch()
    )
    return (
        [n2, wg, wu, wd, residual, cot, gain],
        [ANY_SPEC] * 4 + [VMEM_SPEC, ANY_SPEC, VMEM_SPEC],
        outs,
        [VMEM_SPEC, ANY_SPEC, VMEM_SPEC] + [ANY_SPEC] * 4,
        scratch,
        functools.partial(feed_tasks, groups),
    )


def input_tasks(n_ctx, groups, extra_in, extra_out, scratch):
    i_ref, tokens_ref, dr, gain, gain_two_grad = extra_in
    input_grad, gain_sums = extra_out
    n = len(Scatter.scratch(16, 128))
    scatter = Scatter(i_ref, groups, scratch[:9], scratch[9:n])
    gains, got_tp, got_ctx, send_tp, recv_tp, send_ctx, recv_ctx, rows_in, own_sem = scratch[n:]
    order = list(reversed(range(len(groups))))
    me, rank = lax.axis_index("ctx"), lax.axis_index("tp")

    def tp_hop(k):
        return remote(gains.at[k], got_tp.at[k], send_tp.at[k], recv_tp.at[k], neighbours()[k])

    def ctx_hop(k):
        place = gains.at[2]
        return remote(place, got_ctx.at[k], send_ctx.at[k], recv_ctx.at[k], (jnp.bitwise_xor(me, k), rank))

    def begin():
        gains[0] = jnp.zeros(gains.shape[1:], F32)
        gains[0, 8:9, :] = gain_two_grad[...]
        for copy in own_copies(tokens_ref, rows_in, groups, own_sem):
            copy.start()
        for g in order:
            scatter.start(g)

    def forward_first():
        for copy in own_copies(tokens_ref, rows_in, groups, own_sem):
            copy.wait()
        scatter.forward(order[0])

    def use(at, total):
        back, more = norm_back_rows(rows_in[at, :].astype(F32), gain[...].astype(F32), total)
        input_grad[at, :] = (dr[at, :] + back).astype(BF)
        gains[0, 0:1, :] += more

    def rest():
        scatter.total(order[-1], use)
        tp_hop(0).start()

    def second():
        tp_hop(0).wait()
        gains[1] = gains[0] + got_tp[0]
        tp_hop(1).start()

    def third():
        tp_hop(1).wait()
        gains[2] = gains[1] + got_tp[1]
        for k in range(1, n_ctx):
            ctx_hop(k).start()

    def finish():
        for k in range(1, n_ctx):
            ctx_hop(k).wait()
        got_ctx[0] = gains[2]
        total = got_ctx[jnp.bitwise_xor(me, 0)]
        for index in range(1, n_ctx):
            total = total + got_ctx[jnp.bitwise_xor(me, index)]
        gain_sums[...] = total

    return {
        0: begin,
        4: forward_first,
        9: lambda: scatter.forward(order[-1]),
        10: lambda: scatter.total(order[0], use),
        13: rest,
        15: second,
        17: third,
        20: finish,
    }, None, None


def input_extra(n_ctx, groups, i_partial, tokens_in, dr, gain, gain_two_grad):
    rows, width = tokens_in.shape
    dma = pltpu.SemaphoreType.DMA
    outs = [jax.ShapeDtypeStruct((rows, width), BF), jax.ShapeDtypeStruct((16, width), F32)]
    return (
        [i_partial, tokens_in, dr, gain, gain_two_grad],
        [ANY_SPEC] * 2 + [VMEM_SPEC] * 3,
        outs,
        [VMEM_SPEC] * 2,
        Scatter.scratch(rows, width)
        + [
            pltpu.VMEM((3, 16, width), F32),
            pltpu.VMEM((2, 16, width), F32),
            pltpu.VMEM((n_ctx, 16, width), F32),
            dma((2,)),
            dma((2,)),
            dma((n_ctx,)),
            dma((n_ctx,)),
            pltpu.VMEM((rows, width), BF),
            dma((2,)),
        ],
        functools.partial(input_tasks, n_ctx, groups),
    )


def cast_kernel(groups, *refs):
    out_in, gate_in, up_in, down_in, qkv_in = refs[:5]
    n_more = 3 if groups else 0
    more_in, refs = refs[5 : 5 + n_more], refs[5 + n_more :]
    for source, dest in zip((out_in, gate_in, up_in, down_in), refs[:4]):
        dest[...] = source[...].astype(F32)
    width = refs[4].shape[1]
    for k, dest in enumerate(refs[4:7]):
        dest[...] = qkv_in[:, k * width : (k + 1) * width].astype(F32)
    if not groups:
        return
    row_outs, gain_outs = refs[7:9], refs[9:11]
    gains = more_in[2]
    odd = lax.rem(lax.axis_index("tp"), 2)
    starts = (pl.multiple_of(odd * BLOCK, BLOCK), pl.multiple_of((1 - odd) * PAIR, BLOCK))

    @pl.when(pl.program_id(0) == 0)
    def _():
        gain_outs[0][...] = gains[0:1, :]
        gain_outs[1][...] = gains[8:9, :]
        for source, dest in zip(more_in[:2], row_outs):
            for start, (_, rows, own) in zip(starts, groups):
                dest[pl.ds(start, rows), :] = source[pl.ds(own, rows), :]


def cast_sums(sums, groups=(), rows=(), gains=None):
    steps = 8
    block = lambda array: pl.BlockSpec((array.shape[0] // steps, array.shape[1]), lambda i: (i, 0))
    outs = [jax.ShapeDtypeStruct(array.shape, F32) for array in sums[:-1]]
    outs += [jax.ShapeDtypeStruct((sums[-1].shape[0], sums[-1].shape[1] // 3), F32)] * 3
    in_specs, out_specs = [block(array) for array in sums], [block(array) for array in outs]
    args = list(sums)
    if groups:
        args += list(rows) + [gains]
        in_specs += [whole(array.shape) for array in (*rows, gains)]
        outs += [jax.ShapeDtypeStruct(array.shape, array.dtype) for array in rows]
        outs += [jax.ShapeDtypeStruct((1, gains.shape[1]), F32)] * 2
        out_specs += [whole(array.shape) for array in rows] + [whole((1, gains.shape[1]))] * 2
    return pl.pallas_call(
        functools.partial(cast_kernel, groups),
        out_shape=outs,
        grid=(steps,),
        in_specs=in_specs,
        out_specs=out_specs,
        compiler_params=params(),
        cost_estimate=pl.CostEstimate(
            flops=0, bytes_accessed=sum(6 * array.shape[0] * array.shape[1] for array in sums), transcendentals=0
        ),
    )(*args)


class Exchange:
    def __init__(self, dest, sems, by_device):
        self.dest, self.by_device = dest, by_device
        self.send_sem, self.recv_sem, self.own_sem = sems
        self.n_ctx = dest.shape[1]
        self.me, self.rank = lax.axis_index("ctx"), lax.axis_index("tp")

    @staticmethod
    def scratch(units, n_ctx):
        dma = pltpu.SemaphoreType.DMA
        return [dma((units, n_ctx)), dma((units, n_ctx)), dma((units,))]

    def copy(self, source, unit, k):
        other = jnp.bitwise_xor(self.me, k)
        place = other if self.by_device else k
        return remote(
            source.at[unit, place],
            self.dest.at[unit, k],
            self.send_sem.at[unit, k],
            self.recv_sem.at[unit, k],
            (other, self.rank),
        )

    def own(self, source, unit):
        place = self.me if self.by_device else 0
        return pltpu.make_async_copy(source.at[unit, place], self.dest.at[unit, 0], self.own_sem.at[unit])

    def start(self, source, unit):
        for k in reversed(range(1, self.n_ctx)):
            self.copy(source, unit, k).start()
        self.own(source, unit).start()

    def start_some(self, source, unit, first, count):
        for k in reversed(range(self.n_ctx)):
            other = jnp.bitwise_xor(self.me, k)

            @pl.when((other >= first) & (other < first + count))
            def _(k=k):
                if k == 0:
                    self.own(source, unit).start()
                else:
                    self.copy(source, unit, k).start()

    def arrived(self, source, unit):
        for k in range(1, self.n_ctx):
            self.copy(source, unit, k).wait_recv()
        self.own(source, unit).wait()

    def sent(self, source, unit):
        for k in range(1, self.n_ctx):
            self.copy(source, unit, k).wait_send()


def greet(n_ctx, tp_too):
    index, rank = lax.axis_index("ctx"), lax.axis_index("tp")
    barrier = pltpu.get_barrier_semaphore()
    for k in range(1, n_ctx):
        signal(barrier, (jnp.bitwise_xor(index, k), rank))
    if tp_too:
        for device in neighbours():
            signal(barrier, device)
    pl.semaphore_wait(barrier, n_ctx - 1 + (2 if tp_too else 0))


def rotation(cos_tab, sin_tab, block_cos, block_sin):
    sign = jnp.where(lax.broadcasted_iota(jnp.int32, cos_tab.shape, 1) < HD // 2, -1.0, 1.0)
    return cos_tab * block_cos - sin_tab * block_sin, (sin_tab * block_cos + cos_tab * block_sin) * sign


def in_turn(count):
    return [count - 1] + list(range(count - 1))


def attend_rows(qs, ks, vs, os, tile):
    length = qs.shape[0]
    factor = -(HD ** (-0.5)) * LOG2E
    shift = math.log(length) * LOG2E
    row_at = lax.broadcasted_iota(jnp.int32, (tile, tile), 0)
    col_at = lax.broadcasted_iota(jnp.int32, (tile, tile), 1)
    for i in range(length // tile):
        query = qs[i * tile : (i + 1) * tile, :]

        def part(j, masked):
            at = pl.ds(pl.multiple_of(j * tile, tile), tile)
            raw = times_transposed(query, ks[at, :])
            prob = 1.0 / (1.0 + jnp.exp2(raw * factor + shift))
            if masked:
                prob = jnp.where(row_at >= col_at, prob, 0.0)
            return dot(prob.astype(BF), vs[at, :])

        total = part(i, True)
        if i > 0:
            total = lax.fori_loop(0, i, lambda j, acc: acc + part(j, False), total)
        os[i * tile : (i + 1) * tile, :] = total.astype(BF)


def forward_kernel(n_ctx, groups, units, tile, *refs):
    tokens_ref, cot_ref, wq_in, wk_in, wv_in, wo_in, gain_one, gain_two = refs[:8]
    cos_ref, sin_ref, bcos_ref, bsin_ref, valid_ref = refs[8:13]
    n1_out, got_out, heads_out, residual, n2_out, cot_out = refs[13:19]
    x_ref, rows_buf, own_buf, send, got, o_send, o_got, tabs, qs, ks, vs, os = refs[19:31]
    (wq_ref, wk_ref, wv_ref, wo_ref, weight_sem, cot_buf, cot_via, cot_sem), rest = refs[31:39], refs[39:]
    n_gather, n_exchange = len(Gather.scratch()), len(Exchange.scratch(1, 2))
    n1_sems, rest = rest[:n_gather], rest[n_gather:]
    n2_sems, rest = rest[:n_gather], rest[n_gather:]
    cot_sems, rest = rest[:n_gather], rest[n_gather:]
    x_sems, rest = rest[:n_exchange], rest[n_exchange:]
    o_sems, rest = rest[:n_exchange], rest[n_exchange:]
    (n1_sem, got_sem, load_sem), rest = rest[:3], rest[3:]
    me, rank = lax.axis_index("ctx"), lax.axis_index("tp")
    odd = lax.rem(rank, 2)
    heads = wq_ref.shape[1] // HD
    per_unit = n_ctx // heads
    own_at = [pl.multiple_of(odd * BLOCK, BLOCK), pl.multiple_of((1 - odd) * PAIR, BLOCK)]

    def load_x(g):
        _, rows, own = groups[g]
        return pltpu.make_async_copy(
            tokens_ref.at[pl.ds(own_at[g], rows)], x_ref.at[pl.ds(own, rows)], load_sem.at[g]
        )

    load_weights = [
        pltpu.make_async_copy(source, dest, weight_sem.at[k])
        for k, (source, dest) in enumerate(((wq_in, wq_ref), (wk_in, wk_ref), (wv_in, wv_ref), (wo_in, wo_ref)))
    ]
    for g in range(2):
        load_x(g).start()
    for copy in load_weights + own_copies(cot_ref, cot_buf, groups, cot_sem):
        copy.start()
    greet(n_ctx, True)
    gather_one = Gather(own_buf, rows_buf, groups, n1_sems, local=False)
    scatter = Scatter(rows_buf, groups, rest[:6], rest[6:], loaded=False)
    gather_two = Gather(own_buf, n2_out, groups, n2_sems, via=scatter.from_y)
    gather_cot = Gather(cot_buf, cot_out, groups, cot_sems, via=cot_via)
    trade = Exchange(got, x_sems, True)
    trade_back = Exchange(o_got, o_sems, False)

    def halves_of(u):
        return halves_at(odd if units[u][1] else 0)

    def normed(source, gain, at):
        values = source[at, :].astype(F32)
        return (values * inverse_rms(values) * gain[...].astype(F32)).astype(BF)

    def begin(g):
        base, rows, own = groups[g]
        load_x(g).wait()
        low = normed(x_ref, gain_one, pl.ds(own, rows))
        own_buf[pl.ds(own, rows), :] = low
        gather_one.start(g)
        rows_buf[pl.ds(base, rows), :] = low

    begin(0)
    for half, block in enumerate((me, 2 * n_ctx - 1 - me)):
        cos_part, sin_part = rotation(
            cos_ref[...], sin_ref[...], bcos_ref[pl.ds(block, 1), :], bsin_ref[pl.ds(block, 1), :]
        )
        tabs[0, half * BLOCK : (half + 1) * BLOCK, :] = cos_part
        tabs[1, half * BLOCK : (half + 1) * BLOCK, :] = sin_part

    def query(u, block):
        base, flipped = units[u]
        first, second = halves_of(u)
        at = pl.ds(base + block * PAIR, PAIR)
        rows = rows_buf[at, :]
        for which, w_ref in enumerate((wq_ref, wk_ref, wv_ref)):
            product = dot(rows, w_ref[...])
            for head in range(heads):
                part = product[:, head * HD : (head + 1) * HD]
                pair = block * heads + head
                for half, to in ((0, first), (1, second)):
                    piece = part[half * BLOCK : (half + 1) * BLOCK]
                    if which < 2:
                        piece = piece * tabs[0, to, :] + pltpu.roll(piece, HD // 2, 1) * tabs[1, to, :]
                    else:
                        piece = piece * valid_ref[pl.ds(base + block * PAIR + half * BLOCK, BLOCK), :]
                    send[u, pair, which, to, :] = piece.astype(BF)
        trade.start_some(send, u, block * heads, heads)

    store_n1 = pltpu.make_async_copy(rows_buf, n1_out, n1_sem)
    store_got = [pltpu.make_async_copy(got.at[u], got_out.at[u], got_sem.at[u]) for u in range(len(units))]

    for copy in load_weights:
        copy.wait()
    query(0, 0)
    gather_one.forward_x(0)
    gather_one.forward_y(0)
    begin(1)
    query(0, 1)
    query(1, 0)
    gather_one.finish(0)
    query(1, 1)
    gather_one.forward(1)
    gather_one.finish(1)
    for copy in own_copies(cot_ref, cot_buf, groups, cot_sem):
        copy.wait()
    for g in range(2):
        gather_cot.start(g)
    query(2, 0)
    query(2, 1)
    store_n1.start()

    def attend(u):
        trade.arrived(send, u)
        store_got[u].start()
        for k in range(n_ctx):
            front, back = both_places(me, k, n_ctx)
            for which, dest in enumerate((qs, ks, vs)):
                dest[front, :] = got[u, k, which, :BLOCK, :]
                dest[back, :] = got[u, k, which, BLOCK:, :]
        attend_rows(qs, ks, vs, os, tile)
        for k in range(n_ctx):
            front, back = both_places(me, k, n_ctx)
            o_send[u, k, :BLOCK, :] = os[front, :]
            o_send[u, k, BLOCK:, :] = os[back, :]
        trade_back.start(o_send, u)

    def project(u):
        trade_back.arrived(o_send, u)
        base, _ = units[u]
        first, second = halves_of(u)
        for block in range(per_unit):
            at = pl.ds(base + block * PAIR, PAIR)
            low = valid_ref[at, :].astype(BF)
            for head in range(heads):
                place = jnp.bitwise_xor(me, block * heads + head)
                part = jnp.concatenate([o_got[u, place, first, :], o_got[u, place, second, :]], axis=0)
                heads_out[at, head * HD : (head + 1) * HD] = part * low
            rows_buf[at, :] = dot(heads_out[at, :], wo_ref[...]).astype(BF)

    def use(at, total):
        residual[at, :] = x_ref[at, :].astype(F32) + total
        own_buf[at, :] = normed(residual, gain_two, at)

    def finish_group(g):
        scatter.total(g, use)
        gather_two.start(g)

    attend(0)
    for g in range(2):
        gather_one.sent(g)
    store_n1.wait()
    attend(1)
    for g in range(2):
        gather_cot.forward(g)
    project(0)
    scatter.start(0, (0,), loads=False)
    project(1)
    scatter.start(0, (1, 3, 2), loads=False)
    attend(2)
    scatter.forward(0)
    project(2)
    scatter.start(1, loads=False)
    finish_group(0)
    scatter.forward(1)
    finish_group(1)
    gather_two.forward(0)
    gather_two.forward(1)
    for u in range(len(units)):
        trade.sent(send, u)
        trade_back.sent(o_send, u)
        store_got[u].wait()
    for g in range(2):
        gather_cot.finish(g)
        gather_two.finish(g)
        gather_two.sent(g)
        gather_cot.sent(g)


def forward_layer(tokens_in, cot_in, gain_one, gain_two, wq, wk, wv, wo, tables, valid, n_ctx, groups, units):
    rows, depth = tokens_in.shape
    width = wq.shape[1]
    tokens = valid.shape[0]
    length = 2 * n_ctx * BLOCK
    n_units = len(units)
    vmem = lambda shape, dtype=BF: pltpu.VMEM(shape, dtype)
    outs = [
        jax.ShapeDtypeStruct((tokens, depth), BF),
        jax.ShapeDtypeStruct((n_units, n_ctx, 3, PAIR, HD), BF),
        jax.ShapeDtypeStruct((tokens, width), BF),
        jax.ShapeDtypeStruct((rows, depth), F32),
        jax.ShapeDtypeStruct((tokens, depth), BF),
        jax.ShapeDtypeStruct((tokens, depth), BF),
    ]
    return pl.pallas_call(
        functools.partial(forward_kernel, n_ctx, groups, units, min(512, length)),
        out_shape=outs,
        in_specs=[ANY_SPEC] * 6 + [VMEM_SPEC] * 7,
        out_specs=[ANY_SPEC, ANY_SPEC, VMEM_SPEC, VMEM_SPEC, ANY_SPEC, ANY_SPEC],
        scratch_shapes=[
            vmem((rows, depth)),
            vmem((tokens, depth)),
            vmem((rows, depth)),
            vmem((n_units, n_ctx, 3, PAIR, HD)),
            vmem((n_units, n_ctx, 3, PAIR, HD)),
            vmem((n_units, n_ctx, PAIR, HD)),
            vmem((n_units, n_ctx, PAIR, HD)),
            vmem((2, PAIR, HD), F32),
        ]
        + [vmem((length, HD))] * 4
        + [vmem(wq.shape)] * 3
        + [vmem(wo.shape), pltpu.SemaphoreType.DMA((4,))]
        + [vmem((rows, depth)), vmem((rows, depth)), pltpu.SemaphoreType.DMA((2,))]
        + Gather.scratch() * 3
        + Exchange.scratch(n_units, n_ctx) * 2
        + [pltpu.SemaphoreType.DMA, pltpu.SemaphoreType.DMA((n_units,)), pltpu.SemaphoreType.DMA((2,))]
        + Scatter.scratch(rows, depth, loaded=False),
        compiler_params=pltpu.CompilerParams(vmem_limit_bytes=VMEM_LIMIT, collective_id=3, has_side_effects=True),
        cost_estimate=pl.CostEstimate(
            flops=8 * tokens * depth * width, bytes_accessed=8 * tokens * depth, transcendentals=0
        ),
    )(tokens_in, cot_in, wq, wk, wv, wo, gain_one, gain_two, *tables, valid)


def attend_rows_back(qs, ks, vs, gs, os, dqs, cos_ref, sin_ref, tile):
    length = qs.shape[0]
    scale = HD ** (-0.5)
    factor = -scale * LOG2E
    shift = math.log(length) * LOG2E
    count = length // tile
    key_at = lax.broadcasted_iota(jnp.int32, (tile, tile), 0)
    query_at = lax.broadcasted_iota(jnp.int32, (tile, tile), 1)
    dqs[...] = jnp.zeros_like(dqs)

    def unrotate(values, at):
        return (values * cos_ref[at, :] - pltpu.roll(values, HD // 2, 1) * sin_ref[at, :]).astype(BF)

    for j in range(count):
        own = slice(j * tile, (j + 1) * tile)
        keys = ks[own, :]
        values = vs[own, :]

        def part(i, masked):
            at = pl.ds(pl.multiple_of(i * tile, tile), tile)
            query = qs[at, :]
            grad = gs[at, :]
            raw = times_transposed(keys, query)
            prob = 1.0 / (1.0 + jnp.exp2(raw * factor + shift))
            if masked:
                prob = jnp.where(query_at >= key_at, prob, 0.0)
            prob_grad = times_transposed(values, grad)
            score_grad = (prob_grad * prob * (1.0 - prob)).astype(BF)
            dqs[at, :] += contract_rows(score_grad, keys)
            return dot(score_grad, query), dot(prob.astype(BF), grad)

        total = part(j, True)
        if j + 1 < count:

            def step(i, acc):
                more = part(i, False)
                return acc[0] + more[0], acc[1] + more[1]

            total = lax.fori_loop(j + 1, count, step, total)
        os[1, own, :] = unrotate(total[0] * scale, own)
        os[2, own, :] = total[1].astype(BF)
    for i in range(count):
        at = slice(i * tile, (i + 1) * tile)
        os[0, at, :] = unrotate(dqs[at, :] * scale, at)


def middle_kernel(n_ctx, groups, units, tile, *refs):
    da_ref, got_ref, h_ref, residual_ref, wd_ref, wq_in, wk_in, wv_in, wo_in = refs[:9]
    cos_ref, sin_ref, bcos_ref, bsin_ref, valid_ref = refs[9:14]
    grad_ref, partial_out, output = refs[14:17]
    rows_buf, got, do_send, do_got, back_got, h_buf, wd_buf, res_buf, cos_full, sin_full = refs[17:27]
    qs, ks, vs, gs, os, dqs = refs[27:33]
    (wq_ref, wk_ref, wv_ref, wo_ref, weight_sem), rest = refs[33:38], refs[38:]
    load_weights = [
        pltpu.make_async_copy(source, dest, weight_sem.at[k])
        for k, (source, dest) in enumerate(((wo_in, wo_ref), (wq_in, wq_ref), (wk_in, wk_ref), (wv_in, wv_ref)))
    ]
    load_weights[0].start()
    back_send = got
    n_exchange = len(Exchange.scratch(1, 2))
    do_sems, back_sems, rest = rest[:n_exchange], rest[n_exchange : 2 * n_exchange], rest[2 * n_exchange :]
    (da_sem, got_sem, out_sem, h_sem, wd_sem, res_sem, y_sem), rest = rest[:7], rest[7:]
    me, rank = lax.axis_index("ctx"), lax.axis_index("tp")
    odd = lax.rem(rank, 2)
    heads = wq_ref.shape[1] // HD
    per_unit = n_ctx // heads
    unit_rows = per_unit * PAIR
    count = len(units)
    order = in_turn(count)

    def rows_of(u):
        return pl.ds(units[u][0], unit_rows)

    load_da = [pltpu.make_async_copy(da_ref.at[rows_of(u)], rows_buf.at[rows_of(u)], da_sem.at[u]) for u in range(count)]
    load_got = [pltpu.make_async_copy(got_ref.at[u], got.at[u], got_sem.at[u]) for u in range(count)]
    for u in order:
        load_da[u].start()
    for u in order:
        load_got[u].start()
    first_wd = pltpu.make_async_copy(wd_ref.at[:, pl.ds(0, wd_buf.shape[1])], wd_buf, wd_sem)
    first_wd.start()
    for copy in load_weights[1:]:
        copy.start()
    greet(n_ctx, True)
    scatter = Scatter(rows_buf, groups, rest[:6], rest[6:], loaded=False)
    trade = Exchange(do_got, do_sems, True)
    trade_back = Exchange(back_got, back_sems, False)

    load_weights[0].wait()
    for u in order:
        load_da[u].wait()
        base, flipped = units[u]
        first, second = halves_at(odd if flipped else 0)
        for block in range(per_unit):
            at = pl.ds(base + block * PAIR, PAIR)
            grad = times_transposed(rows_buf[at, :], wo_ref[...]).astype(BF)
            low = valid_ref[at, :].astype(BF)
            for head in range(heads):
                part = grad[:, head * HD : (head + 1) * HD] * low
                do_send[u, block * heads + head, first, :] = part[:BLOCK]
                do_send[u, block * heads + head, second, :] = part[BLOCK:]
        trade.start(do_send, u)
    for block in range(2 * n_ctx):
        at = slice(block * BLOCK, (block + 1) * BLOCK)
        cos_full[at, :], sin_full[at, :] = rotation(
            cos_ref[...], sin_ref[...], bcos_ref[block : block + 1, :], bsin_ref[block : block + 1, :]
        )
    for copy in load_weights[1:]:
        copy.wait()
    for u in order:
        load_got[u].wait()

    def attend(turn, carry):
        u = lax.rem(turn + count - 1, count)
        trade.arrived(do_send, u)
        for k in range(n_ctx):
            front, back = both_places(me, k, n_ctx)
            for which, dest in enumerate((qs, ks, vs)):
                dest[front, :] = got[u, k, which, :BLOCK, :]
                dest[back, :] = got[u, k, which, BLOCK:, :]
            gs[front, :] = do_got[u, k, :BLOCK, :]
            gs[back, :] = do_got[u, k, BLOCK:, :]
        attend_rows_back(qs, ks, vs, gs, os, dqs, cos_full, sin_full, tile)
        for k in range(n_ctx):
            front, back = both_places(me, k, n_ctx)
            for which in range(3):
                back_send[u, k, which, :BLOCK, :] = os[which, front, :]
                back_send[u, k, which, BLOCK:, :] = os[which, back, :]
        trade_back.start(back_send, u)
        return carry

    lax.fori_loop(0, count, attend, 0)

    tiles = rows_buf.shape[0] // PAIR

    def tile_rows(tile):
        return pl.ds(pl.multiple_of(tile * PAIR, PAIR), PAIR)

    def load_h(step):
        slot = lax.rem(step, 2)
        return pltpu.make_async_copy(h_ref.at[tile_rows(lax.rem(step, tiles))], h_buf.at[slot], h_sem.at[slot])

    columns = wd_buf.shape[1]
    parts = rows_buf.shape[1] // columns

    def part_columns(part):
        return pl.ds(pl.multiple_of(part * columns, columns), columns)

    def load_wd(part):
        return pltpu.make_async_copy(wd_ref.at[:, part_columns(part)], wd_buf, wd_sem)

    load_h(0).start()

    def down(step, carry):
        part, tile = step // tiles, lax.rem(step, tiles)

        @pl.when(step + 1 < tiles * parts)
        def _():
            load_h(step + 1).start()

        @pl.when(tile == 0)
        def _():
            @pl.when(part > 0)
            def _():
                load_wd(part).start()

            load_wd(part).wait()

        load_h(step).wait()
        rows_buf[tile_rows(tile), part_columns(part)] = dot(h_buf[lax.rem(step, 2)], wd_buf[...]).astype(BF)
        return carry

    lax.fori_loop(0, tiles * parts, down, 0)
    last_group = len(groups) - 1
    out_rows = rest[0]
    for g in (last_group, 0):
        scatter.start(g, loads=False)

    def use(at, total):
        size = total.shape[0]
        load = pltpu.make_async_copy(residual_ref.at[at], res_buf.at[pl.ds(0, size)], res_sem)
        load.start()
        load.wait()
        low = (res_buf[:size, :] + total).astype(BF)
        out_rows[at, :] = low

    def store(number, first):
        slot = number % 2
        return pltpu.make_async_copy(h_buf.at[slot], partial_out.at[pl.ds(first, PAIR)], out_sem.at[slot])

    stored = []
    for turn, u in enumerate(order):
        trade_back.arrived(back_send, u)
        base, flipped = units[u]
        first, second = halves_at(odd if flipped else 0)
        for block in range(per_unit):
            at = pl.ds(base + block * PAIR, PAIR)
            low = valid_ref[at, :].astype(BF)
            total = None
            for which, w_ref in enumerate((wq_ref, wk_ref, wv_ref)):
                width = heads * HD
                for head in range(heads):
                    place = jnp.bitwise_xor(me, block * heads + head)
                    part = jnp.concatenate(
                        [back_got[u, place, which, first, :], back_got[u, place, which, second, :]], axis=0
                    )
                    columns = slice(which * width + head * HD, which * width + (head + 1) * HD)
                    grad_ref[at, columns] = part * low if which == 2 else part
                product = times_transposed(grad_ref[at, which * width : (which + 1) * width], w_ref[...])
                total = product if total is None else total + product
            number = len(stored)
            if number >= 2:
                stored[number - 2].wait()
            h_buf[number % 2] = total.astype(BF)
            stored.append(store(number, base + block * PAIR))
            stored[-1].start()
        if turn == 0:
            scatter.forward(last_group)
            scatter.forward(0)
        if turn == 1:
            for g in (last_group, 0):
                scatter.total(g, use)
            store_y = pltpu.make_async_copy(out_rows, output, y_sem)
            store_y.start()
    store_y.wait()
    for copy in stored[-2:]:
        copy.wait()
    for u in order:
        trade.sent(do_send, u)
        trade_back.sent(back_send, u)


def middle_layer(da, got, h, residual, wq, wk, wv, wo, wd, tables, valid, n_ctx, groups, units):
    tokens, depth = da.shape
    width = wq.shape[1]
    length = 2 * n_ctx * BLOCK
    count = len(units)
    vmem = lambda shape, dtype=BF: pltpu.VMEM(shape, dtype)
    dma = pltpu.SemaphoreType.DMA
    three, one = (count, n_ctx, 3, PAIR, HD), (count, n_ctx, PAIR, HD)
    most_rows = max(rows for _, rows, _ in groups) // 2
    return pl.pallas_call(
        functools.partial(middle_kernel, n_ctx, groups, units, min(512, length)),
        out_shape=[
            jax.ShapeDtypeStruct((tokens, 3 * width), BF),
            jax.ShapeDtypeStruct((tokens, depth), BF),
            jax.ShapeDtypeStruct(residual.shape, BF),
        ],
        in_specs=[ANY_SPEC] * 9 + [VMEM_SPEC] * 5,
        out_specs=[VMEM_SPEC, ANY_SPEC, ANY_SPEC],
        scratch_shapes=[vmem((tokens, depth)), vmem(three), vmem(one), vmem(one), vmem(three)]
        + [vmem((2, PAIR, depth)), vmem((h.shape[1], depth // 2)), vmem((most_rows, depth), F32)]
        + [vmem((length, HD), F32)] * 2
        + [vmem((length, HD))] * 4
        + [vmem((3, length, HD)), vmem((length, HD), F32)]
        + [vmem(wq.shape)] * 3
        + [vmem(wo.shape), dma((4,))]
        + Exchange.scratch(count, n_ctx) * 2
        + [dma((count,)), dma((count,)), dma((2,)), dma((2,)), dma, dma, dma]
        + Scatter.scratch(residual.shape[0], depth, loaded=False),
        compiler_params=pltpu.CompilerParams(vmem_limit_bytes=VMEM_LIMIT, collective_id=4, has_side_effects=True),
        cost_estimate=pl.CostEstimate(
            flops=8 * tokens * depth * width + 2 * tokens * depth * h.shape[1],
            bytes_accessed=8 * tokens * depth,
            transcendentals=0,
        ),
    )(da, got, h, residual, wd, wq, wk, wv, wo, *tables, valid)


def body(
    tokens,
    counts,
    norm_gain,
    w_query,
    w_key,
    w_value,
    w_output,
    mlp_gain,
    w_gate,
    w_up,
    w_down,
    cotangent,
):
    n_ctx = lax.axis_size("ctx")
    me = lax.axis_index("ctx")
    rank = lax.axis_index("tp")
    odd = rank & 1
    core = me & 1
    length = 2 * BLOCK * n_ctx
    heads = w_query.shape[1] // HD
    gain_one = norm_gain.astype(F32)
    gain_two = mlp_gain.astype(F32)

    inverse = THETA ** (-(jnp.arange(HD // 2, dtype=F32) * (2.0 / HD)))
    angles = jnp.arange(length, dtype=jnp.int32).astype(F32)[:, None] * inverse[None, :]
    cos_half, sin_half = jnp.cos(angles), jnp.sin(angles)
    cos_full = jnp.concatenate([cos_half, cos_half], axis=1)
    sin_full = jnp.concatenate([-sin_half, sin_half], axis=1)

    def own_blocks(table):
        front = lax.dynamic_slice_in_dim(table, me * BLOCK, BLOCK, 0)
        back = lax.dynamic_slice_in_dim(table, (2 * n_ctx - 1 - me) * BLOCK, BLOCK, 0)
        return front, back

    cos_front, cos_back = own_blocks(cos_full)
    sin_front, sin_back = own_blocks(sin_full)
    own_counts = lax.dynamic_index_in_dim(counts, me, 0, keepdims=False)
    offsets = jnp.arange(BLOCK, dtype=jnp.int32)

    def valid_of(sequence_list, half_list):
        held = own_counts[jnp.stack(sequence_list), jnp.stack(half_list)]
        return (offsets[None, :] < held[:, None]).astype(F32).reshape(-1)

    cos_own = jnp.concatenate([cos_front, cos_back])
    sin_own = jnp.concatenate([sin_front, sin_back])
    sequences = counts.shape[1]
    paired = by_four() and sequences == 6 and n_ctx == 2 * heads
    if paired:
        ranks = [rank ^ k for k in range(4)]
        blocks_a = [(3 * (r >> 1) + 2 * (r & 1), jnp.int32(half)) for r in ranks for half in range(2)]
        blocks_b = [(1 + 3 * (r >> 1), r & 1) for r in ranks]
        flat_valid = valid_of(*zip(*(blocks_a + blocks_b)))
        valids = {"b": flat_valid[len(blocks_a) * BLOCK :], "a": flat_valid[: len(blocks_a) * BLOCK]}
        flip_back = lambda own: jnp.where(odd == 1, jnp.roll(own, BLOCK, axis=0), own)
        tables = {
            "b": (jnp.tile(flip_back(cos_own), (2, 1)), jnp.tile(flip_back(sin_own), (2, 1))),
            "a": (jnp.tile(cos_own, (4, 1)), jnp.tile(sin_own, (4, 1))),
        }
        scalars = {"b": jnp.stack([me, odd]).astype(jnp.int32), "a": jnp.stack([me, 0]).astype(jnp.int32)}
        n_pairs = {"b": 2 * heads, "a": 4 * heads}
    else:
        flat_valid = (offsets[None, None, :] < own_counts[:, :, None]).astype(F32).reshape(-1)
        valids = {"a": flat_valid}
        tables = {"a": (jnp.tile(cos_own, (sequences, 1)), jnp.tile(sin_own, (sequences, 1)))}
        scalars = {"a": jnp.stack([me, 0]).astype(jnp.int32)}
        n_pairs = {"a": sequences * heads}
    names = tuple(n_pairs)

    def own_rows(array):
        if not paired:
            return {"a": array}
        return {
            "b": lax.dynamic_slice_in_dim(array, (1 - odd) * PAIR, BLOCK, 0),
            "a": lax.dynamic_slice_in_dim(array, odd * BLOCK, PAIR, 0),
        }

    x_own = {name: rows.astype(F32) for name, rows in own_rows(tokens[0]).items()}
    g_own = own_rows(cotangent[0])

    split = by_four()
    rows_of = {name: valids[name].shape[0] for name in names}
    total_rows = sum(rows_of.values())
    first_row = {"a": 0, "b": rows_of["a"]}
    valid_head = {name: jnp.broadcast_to(valids[name][:, None], (rows_of[name], HD)) for name in names}
    valid_wide = {name: jnp.broadcast_to(valids[name][:, None].astype(BF), (rows_of[name], heads * HD)) for name in names}
    near = [k for k in range(n_ctx) if k < 6]
    far = [k for k in range(n_ctx) if k >= 6]
    state = {}

    def fence():
        names_held = list(state)
        values = lax.optimization_barrier([state[name] for name in names_held])
        state.update(zip(names_held, values))

    def only_b(step):
        if "b" in names:
            step("b")

    def norm_one(n):
        state["n1", n] = (x_own[n] * inverse_rms(x_own[n]) * gain_one).astype(BF)

    def gather_a(key):
        def step(n):
            state[key, n] = gather_first(state[key, n])

        return step

    def gather_b(key):
        def step(n):
            state[key, n] = gather_second(state[key, n])

        return step

    def query(n):
        state["n1", n] = gathered(state["n1", n])
        cos_tab, sin_tab = tables[n]
        state["qkv", n] = project_qkv(
            scalars[n], state["n1", n], w_query, w_key, w_value, cos_tab, sin_tab, valid_head[n], n_ctx
        )

    def swap_part(key, places, to):
        def step(n):
            got = dict(state.get((to, n), {}))
            got.update(exchange(state[key, n], places, n_ctx))
            state[to, n] = got
            if len(got) == n_ctx:
                state[to, n] = [got[k] for k in range(n_ctx)]
                del state[key, n]

        return step

    def attend(n):
        state["mixed", n] = attention_forward(scalars[n], state["got", n], n_ctx)

    def project(n):
        heads_out, *parts = project_out(
            scalars[n], state.pop(("back", n)), w_output, valid_wide[n], n_pairs[n], n_ctx, split
        )
        state["heads", n], state["r", n] = heads_out, tuple(parts)

    def scatter_a(key):
        def step(n):
            state[key, n] = scatter_first(state[key, n])

        return step

    def scatter_b(key):
        def step(n):
            state[key, n] = scatter_second(state[key, n])

        return step

    def norm_two(n):
        residual = x_own[n] + scattered(state.pop(("r", n)))
        state["residual", n] = residual
        state["n2", n] = (residual * inverse_rms(residual) * gain_two).astype(BF)

    def core_mlp(n):
        state["n2", n] = gathered(state["n2", n])
        state["cot", n] = gathered(state["cot", n])
        held = state.get("mlp", ())
        state["mlp"] = mlp_core(
            state["n2", n], state["cot", n], w_gate, w_up, w_down, total_rows, first_row[n], held
        )

    def attend_back(n):
        state["dqkv", n] = attention_backward(
            scalars[n], state.pop(("got", n)), state.pop(("gdo", n)), cos_full, sin_full, n_ctx
        )

    def query_back(n):
        dq, dk, dv, *parts = project_in(
            scalars[n], state.pop(("gdqkv", n)), (w_query, w_key, w_value), valid_wide[n], n_pairs[n], n_ctx, False
        )
        state["dq", n], state["dk", n], state["dv", n], state["i", n] = dq, dk, dv, parts[0]

    def joined(key):
        parts = [state[key, n] for n in ("a", "b") if n in names]
        return jnp.concatenate(parts) if len(parts) > 1 else parts[0]

    groups = tuple((first_row[n], rows_of[n] // 4, first_row[n] // 4) for n in ("a", "b") if n in names)

    if paired:
        units = ((0, False), (2 * PAIR, False), (4 * PAIR, True))
        wide_valid = jnp.broadcast_to(flat_valid[:, None], (total_rows, HD))
        twice = lambda table: jnp.concatenate([table, table], axis=1)
        starts = BLOCK * jnp.arange(2 * n_ctx, dtype=jnp.int32)
        spans = [at.astype(F32)[:, None] * inverse[None, :] for at in (offsets, starts)]
        turns = [twice(part(angle)) for angle in spans for part in (jnp.cos, jnp.sin)]
        all_n1, got, heads_out, own_residual, all_n2, all_cot = forward_layer(
            tokens[0], cotangent[0], norm_gain[None], mlp_gain[None], w_query, w_key, w_value, w_output,
            turns, wide_valid, n_ctx, groups, units,
        )
    else:
        norm_one("a")
        state["cot", "a"] = g_own["a"]
        gather_a("n1")("a")
        query("a")
        swap_part("qkv", range(n_ctx), "got")("a")
        attend("a")
        swap_part("mixed", range(n_ctx), "back")("a")
        project("a")
        scatter_a("r")("a")
        norm_two("a")
        gather_a("n2")("a")
        gather_a("cot")("a")
        all_n1, all_n2, all_cot = state["n1", "a"], gathered(state["n2", "a"]), gathered(state["cot", "a"])
        heads_out, own_residual = state["heads", "a"], state["residual", "a"]
    if paired:
        extra = feed_extra(groups, all_n2, w_gate, w_up, w_down, own_residual, cotangent[0], mlp_gain[None])
        sum_down, sum_gate, sum_up, sum_out, dr, da, gain_two_grad, _, h, _, _ = weight_sums(
            [(w_down.shape[0], 0), (all_n2, 1), (all_n2, 2), (heads_out, 3)],
            [all_cot], n_ctx, 1, extra, late=(5, 6, 1), limit=62 * 1024 * 1024,
        )
        dqkv, i_partial, output = middle_layer(
            da, got, h, own_residual, w_query, w_key, w_value, w_output, w_down, turns, wide_valid, n_ctx, groups, units
        )
        extra = input_extra(n_ctx, groups, i_partial, tokens[0], dr, norm_gain[None], gain_two_grad)
        sum_qkv, input_grad, gain_sums = weight_sums(
            [(all_n1, 0)], [dqkv], n_ctx, 2, extra
        )
    else:
        own_grads = cotangent[0]
        h, dgp, dup = mlp_core(all_n2, all_cot, w_gate, w_up, w_down, total_rows, 0)
        d_partial = (times_transposed(dgp, w_gate) + times_transposed(dup, w_up)).astype(BF)
        y_partial = dot(h, w_down).astype(BF)
        (sum_down,) = weight_sums([(h, 0)], [all_cot], n_ctx, 1)
        sum_gate, sum_up = weight_sums([(all_n2, 0), (all_n2, 1)], [dgp, dup], n_ctx, 2)
        back, gain_two_grad = norm_back_rows(own_residual, gain_two, scattered(scatter_first((d_partial,))))
        dr = own_grads.astype(F32) + back
        da = gathered(gather_first(dr.astype(BF)))
        output = (own_residual + scattered(scatter_first((y_partial,)))).astype(BF)
        state["do", "a"] = heads_back(scalars["a"], da, w_output, valid_wide["a"], n_ctx)
        swap_part("do", range(n_ctx), "gdo")("a")
        attend_back("a")
        swap_part("dqkv", range(n_ctx), "gdqkv")("a")
        query_back("a")
        (sum_out,) = weight_sums([(heads_out, 0)], [da], n_ctx, 3)
        (sum_qkv,) = weight_sums(
            [(all_n1, 0)], [jnp.concatenate([state[key, "a"] for key in ("dq", "dk", "dv")], axis=1)], n_ctx, 4
        )
        back, gain_one_grad = norm_back_rows(x_own["a"], gain_one, scattered(scatter_first((state["i", "a"],))))
        input_grad = (dr + back).astype(BF)
    sums = (sum_out, sum_gate, sum_up, sum_down, sum_qkv)
    if paired:
        *grads, output, input_grad, grad_norm_gain, grad_mlp_gain = cast_sums(sums, groups, (output, input_grad), gain_sums)
        gains = grad_norm_gain[0], grad_mlp_gain[0]
    else:
        grads = cast_sums(sums)
        gains = lax.psum(jnp.concatenate([gain_one_grad, gain_two_grad]), ("ctx", "tp"))
    grad_out, grad_gate, grad_up, grad_down, grad_query, grad_key, grad_value = grads
    return (
        output[None],
        input_grad[None],
        gains[0],
        grad_query,
        grad_key,
        grad_value,
        grad_out,
        gains[1],
        grad_gate,
        grad_up,
        grad_down,
    )


def solution(mesh):
    placed = (
        P("ctx", "tp", None),
        P(),
        P(),
        P(None, "tp"),
        P(None, "tp"),
        P(None, "tp"),
        P("tp", None),
        P(),
        P(None, "tp"),
        P(None, "tp"),
        P("tp", None),
        P("ctx", "tp", None),
    )
    return jax.shard_map(
        body,
        mesh=mesh,
        in_specs=placed,
        out_specs=(
            P("ctx", "tp", None),
            P("ctx", "tp", None),
            P(),
            P(None, "tp"),
            P(None, "tp"),
            P(None, "tp"),
            P("tp", None),
            P(),
            P(None, "tp"),
            P(None, "tp"),
            P("tp", None),
        ),
        check_vma=False,
    )
```
